32 devices in a mesh: clips: 4 (over z), ha: 4 (over y, x), wa: 2 (over core).
Axes of the slice: x: 2, y: 2, z: 4, core: 2. Of those that a mesh axis runs over, the one named last changes fastest.
Arguments:
- slow_input: bfloat16 [12, 8, 8, 8, 1024], P('clips', None, 'ha', 'wa'), may hold values from -6 to 6
- fast_input: bfloat16 [12, 32, 8, 8, 128], P('clips', None, 'ha', 'wa'), may hold values from -6 to 6
- slow_cotangent: bfloat16 [12, 8, 8, 8, 1024], P('clips', None, 'ha', 'wa'), may hold values from -6 to 6
- fast_cotangent: bfloat16 [12, 32, 8, 8, 128], P('clips', None, 'ha', 'wa'), may hold values from -6 to 6
- clip_counts: int32 [4], P('clips'), may hold values from 1 to 3, as said below
- lateral_weight: bfloat16 [5, 128, 256], P(None, ('ha', 'wa')), may hold values from -0.25 to 0.25
- slow_reduce_one: bfloat16 [3, 1280, 256], P(None, ('ha', 'wa')), may hold values from -0.09375 to 0.09375
- slow_spatial_one: bfloat16 [3, 3, 256, 256], P(None, None, ('ha', 'wa')), may hold values from -0.125 to 0.125
- slow_expand_one: bfloat16 [256, 1024], P(('ha', 'wa')), may hold values from -0.375 to 0.375
- slow_shortcut_one: bfloat16 [1280, 1024], P(('ha', 'wa')), may hold values from -0.15625 to 0.15625
- fast_reduce_one: bfloat16 [3, 128, 32], P(None, ('ha', 'wa')), may hold values from -0.3125 to 0.3125
- fast_spatial_one: bfloat16 [3, 3, 32, 32], P(None, None, ('ha', 'wa')), may hold values from -0.375 to 0.375
- fast_expand_one: bfloat16 [32, 128], P(('ha', 'wa')), may hold values from -1 to 1
- slow_reduce_two: bfloat16 [3, 1024, 256], P(None, ('ha', 'wa')), may hold values from -0.109375 to 0.109375
- slow_spatial_two: bfloat16 [3, 3, 256, 256], P(None, None, ('ha', 'wa')), may hold values from -0.125 to 0.125
- slow_expand_two: bfloat16 [256, 1024], P(('ha', 'wa')), may hold values from -0.375 to 0.375
- fast_reduce_two: bfloat16 [3, 128, 32], P(None, ('ha', 'wa')), may hold values from -0.3125 to 0.3125
- fast_spatial_two: bfloat16 [3, 3, 32, 32], P(None, None, ('ha', 'wa')), may hold values from -0.375 to 0.375
- fast_expand_two: bfloat16 [32, 128], P(('ha', 'wa')), may hold values from -1 to 1
- slow_norms_one: float32 [2, 2560], replicated, may hold values from -0.75 to 0.75
- fast_norms_one: float32 [2, 192], replicated, may hold values from -0.75 to 0.75
- slow_norms_two: float32 [2, 1536], replicated, may hold values from -0.75 to 0.75
- fast_norms_two: float32 [2, 192], replicated, may hold values from -0.75 to 0.75
Outputs:
- slow_output: bfloat16 [12, 8, 8, 8, 1024], P('clips', None, 'ha', 'wa')
- fast_output: bfloat16 [12, 32, 8, 8, 128], P('clips', None, 'ha', 'wa')
- grad_slow_input: float32 [12, 8, 8, 8, 1024], P('clips', None, 'ha', 'wa')
- grad_fast_input: float32 [12, 32, 8, 8, 128], P('clips', None, 'ha', 'wa')
- grad_lateral_weight: float32 [5, 128, 256], P(None, ('ha', 'wa'))
- grad_slow_reduce_one: float32 [3, 1280, 256], P(None, ('ha', 'wa'))
- grad_slow_spatial_one: float32 [3, 3, 256, 256], P(None, None, ('ha', 'wa'))
- grad_slow_expand_one: float32 [256, 1024], P(('ha', 'wa'))
- grad_slow_shortcut_one: float32 [1280, 1024], P(('ha', 'wa'))
- grad_fast_reduce_one: float32 [3, 128, 32], P(None, ('ha', 'wa'))
- grad_fast_spatial_one: float32 [3, 3, 32, 32], P(None, None, ('ha', 'wa'))
- grad_fast_expand_one: float32 [32, 128], P(('ha', 'wa'))
- grad_slow_reduce_two: float32 [3, 1024, 256], P(None, ('ha', 'wa'))
- grad_slow_spatial_two: float32 [3, 3, 256, 256], P(None, None, ('ha', 'wa'))
- grad_slow_expand_two: float32 [256, 1024], P(('ha', 'wa'))
- grad_fast_reduce_two: float32 [3, 128, 32], P(None, ('ha', 'wa'))
- grad_fast_spatial_two: float32 [3, 3, 32, 32], P(None, None, ('ha', 'wa'))
- grad_fast_expand_two: float32 [32, 128], P(('ha', 'wa'))
- grad_slow_norms_one: float32 [2, 2560], replicated
- grad_fast_norms_one: float32 [2, 192], replicated
- grad_slow_norms_two: float32 [2, 1536], replicated
- grad_fast_norms_two: float32 [2, 192], replicated
The draws below stay inside these ranges and needn't reach their ends.
Inputs may be any that keep to these rules, and one draw needn't show every extreme that they name: Each group has 3 clip slots, and clip_counts[g] of them, from slot 0, hold clips; some group is full.
All inputs are finite; a program needn't handle non-finite values.
Results may differ from the reference program's by a relative error of at most 0.023.
Values may be sent and summed in bfloat16 or wider, within the bound.
No kernel may reach another device: no remote copies, remote signals or barrier semaphores. Data moves between devices by JAX's collectives and lax.ppermute only.
A program may use at most 128 MiB of HBM per device.

```python
import jax
import jax.numpy as jnp
from jax import lax

DSLOW = 1024
DSB = 256
DFAST = 128
DFB = 32
DLAT = 256
TS = 8
TF = 32
CAP = 3
CLIPS = 12
H = 8
W = 8
N_CLIPS = 4


def draw_clip_counts(key, part):
    key = jax.random.fold_in(key, 11)
    first_key, second_key, full_key = jax.random.split(key, 3)
    first = jax.random.randint(first_key, (N_CLIPS,), 0, CAP, dtype=jnp.int32)
    second = jax.random.randint(second_key, (N_CLIPS,), 0, CAP, dtype=jnp.int32)
    counts = 1 + jnp.maximum(first, second)
    full_group = jax.random.randint(full_key, (), 0, N_CLIPS, dtype=jnp.int32)
    groups = jnp.arange(N_CLIPS, dtype=jnp.int32)
    return jnp.where(groups == full_group, jnp.int32(CAP), counts).astype(jnp.int32)


def level_of(rng, shape, cuts, smallest, largest):
    def one(axis_at, parts):
        heights = jax.random.uniform(jax.random.fold_in(jax.random.fold_in(rng, 6), axis_at), (parts,), jnp.float32, smallest / len(cuts), largest / len(cuts))
        return jnp.repeat(jnp.exp(heights), shape[axis_at] // parts).reshape((-1,) + (1,) * (len(shape) - axis_at - 1))

    loudness = one(*cuts[0])
    for cut in cuts[1:]:
        loudness = loudness * one(*cut)
    return loudness


def centred(own_key, dims, deviation, most, cuts=(), kind=jnp.bfloat16):
    result = jax.random.normal(own_key, dims, jnp.float32) * deviation
    if len(cuts) > 0:
        result = level_of(own_key, dims, cuts, -0.22, 0.18) * result
    return jnp.clip(result, min=-most, max=most).astype(kind)


def setup_inputs(seed: int = 0) -> dict:
    key_list = jax.random.split(jax.random.key(seed), 24)
    slow_input = centred(key_list[0], (CLIPS, TS, H, W, DSLOW), 1.0, 6.0, ((0, 4), (2, 4), (3, 2)))
    fast_input = centred(key_list[1], (CLIPS, TF, H, W, DFAST), 1.0, 6.0, ((0, 4), (2, 4), (3, 2)))
    slow_cotangent = centred(key_list[2], (CLIPS, TS, H, W, DSLOW), 1.0, 6.0, ((0, 4), (2, 4), (3, 2)))
    fast_cotangent = centred(key_list[3], (CLIPS, TF, H, W, DFAST), 1.0, 6.0, ((0, 4), (2, 4), (3, 2)))
    clip_counts = draw_clip_counts(jax.random.fold_in(key_list[23], 71), 0)
    lateral_weight = centred(key_list[5], (5, DFAST, DLAT), (5 * DFAST) ** -0.5, 0.25, ((1, 8),))
    slow_reduce_one = centred(key_list[6], (3, DSLOW + DLAT, DSB), (3 * (DSLOW + DLAT)) ** -0.5, 0.09375, ((1, 8),))
    slow_spatial_one = centred(key_list[7], (3, 3, DSB, DSB), (9 * DSB) ** -0.5, 0.125, ((2, 8),))
    slow_expand_one = centred(key_list[8], (DSB, DSLOW), DSB ** -0.5, 0.375, ((0, 8),))
    slow_shortcut_one = centred(key_list[9], (DSLOW + DLAT, DSLOW), (DSLOW + DLAT) ** -0.5, 0.15625, ((0, 8),))
    fast_reduce_one = centred(key_list[10], (3, DFAST, DFB), (3 * DFAST) ** -0.5, 0.3125, ((1, 8),))
    fast_spatial_one = centred(key_list[11], (3, 3, DFB, DFB), (9 * DFB) ** -0.5, 0.375, ((2, 8),))
    fast_expand_one = centred(key_list[12], (DFB, DFAST), DFB ** -0.5, 1.0, ((0, 8),))
    slow_reduce_two = centred(key_list[13], (3, DSLOW, DSB), (3 * DSLOW) ** -0.5, 0.109375, ((1, 8),))
    slow_spatial_two = centred(key_list[14], (3, 3, DSB, DSB), (9 * DSB) ** -0.5, 0.125, ((2, 8),))
    slow_expand_two = centred(key_list[15], (DSB, DSLOW), DSB ** -0.5, 0.375, ((0, 8),))
    fast_reduce_two = centred(key_list[16], (3, DFAST, DFB), (3 * DFAST) ** -0.5, 0.3125, ((1, 8),))
    fast_spatial_two = centred(key_list[17], (3, 3, DFB, DFB), (9 * DFB) ** -0.5, 0.375, ((2, 8),))
    fast_expand_two = centred(key_list[18], (DFB, DFAST), DFB ** -0.5, 1.0, ((0, 8),))
    slow_norms_one = centred(key_list[19], (2, 2 * DSB + 2 * DSLOW), 0.25, 0.75, (), jnp.float32)
    fast_norms_one = centred(key_list[20], (2, 2 * DFB + DFAST), 0.25, 0.75, (), jnp.float32)
    slow_norms_two = centred(key_list[21], (2, 2 * DSB + DSLOW), 0.25, 0.75, (), jnp.float32)
    fast_norms_two = centred(key_list[22], (2, 2 * DFB + DFAST), 0.25, 0.75, (), jnp.float32)
    return {"slow_input": slow_input, "fast_input": fast_input, "slow_cotangent": slow_cotangent, "fast_cotangent": fast_cotangent, "clip_counts": clip_counts, "lateral_weight": lateral_weight, "slow_reduce_one": slow_reduce_one, "slow_spatial_one": slow_spatial_one, "slow_expand_one": slow_expand_one, "slow_shortcut_one": slow_shortcut_one, "fast_reduce_one": fast_reduce_one, "fast_spatial_one": fast_spatial_one, "fast_expand_one": fast_expand_one, "slow_reduce_two": slow_reduce_two, "slow_spatial_two": slow_spatial_two, "slow_expand_two": slow_expand_two, "fast_reduce_two": fast_reduce_two, "fast_spatial_two": fast_spatial_two, "fast_expand_two": fast_expand_two, "slow_norms_one": slow_norms_one, "fast_norms_one": fast_norms_one, "slow_norms_two": slow_norms_two, "fast_norms_two": fast_norms_two}


@jax.custom_vjp
def low(v):
    return lax.optimization_barrier(v.astype(jnp.bfloat16)).astype(jnp.float32)

@jax.custom_vjp
def low_back(v):
    return v

def low_keep(v):
    return (low(v), None)

def low_pass(kept, grad):
    return (grad,)

def back_keep(v):
    return (v, None)

def back_low(kept, grad):
    return (low(grad),)
low.defvjp(low_keep, low_pass)
low_back.defvjp(back_keep, back_low)
epsilon = 1e-05

def convolve(signal, kernel, stride, padding):
    return lax.conv_general_dilated(signal, kernel, window_strides=stride, padding=padding, dimension_numbers=('NDHWC', 'DHWIO', 'NDHWC'), precision=lax.Precision.HIGHEST)

def temporal(signal, weight):
    return convolve(signal, weight[:, None, None], (1, 1, 1), ((1, 1), (0, 0), (0, 0)))

def spatial(signal, weight):
    return convolve(signal, weight[None], (1, 1, 1), ((0, 0), (1, 1), (1, 1)))

def pointwise(signal, weight):
    return convolve(signal, weight[None, None, None], (1, 1, 1), ((0, 0), (0, 0), (0, 0)))

def lateral(signal, weight):
    return convolve(signal, weight[:, None, None], (4, 1, 1), ((2, 2), (0, 0), (0, 0)))

def normalize(signal, params, valid_mask):
    counted = jnp.sum(valid_mask) * (signal.shape[1] * signal.shape[2] * signal.shape[3])
    average = lax.optimization_barrier(jnp.sum(valid_mask * signal, axis=(0, 1, 2, 3))) / counted
    spread = lax.optimization_barrier(jnp.sum(valid_mask * jnp.square(signal - average), axis=(0, 1, 2, 3))) / counted
    return (1.0 + params[0]) * (signal - average) * lax.rsqrt(spread + epsilon) + params[1]

def branch(inputs, reduce_weight, spatial_weight, expand_weight, params, valid_mask):
    reduce_end = reduce_weight.shape[-1]
    spatial_end = reduce_end + spatial_weight.shape[-1]
    expand_end = spatial_end + expand_weight.shape[-1]
    reduced = low_back(temporal(inputs, reduce_weight))
    hidden = low(jax.nn.silu(normalize(reduced, params[:, :reduce_end], valid_mask)))
    mixed = low_back(spatial(hidden, spatial_weight))
    hidden = low(jax.nn.silu(normalize(mixed, params[:, reduce_end:spatial_end], valid_mask)))
    expanded = low_back(pointwise(hidden, expand_weight))
    return normalize(expanded, params[:, spatial_end:expand_end], valid_mask)

def layer_one(slow_signal, fast_signal, weights, slow_params, fast_params, valid_mask):
    fast_low = low(fast_signal)
    united = low_back(lateral(fast_low, weights[0]))
    joined = low(jnp.concatenate([slow_signal, united], axis=-1))
    slow_branch = branch(joined, weights[1], weights[2], weights[3], slow_params, valid_mask)
    shortcut = low_back(pointwise(joined, weights[4]))
    offset = slow_params.shape[1] - weights[4].shape[1]
    slow_result = jax.nn.silu(slow_branch + normalize(shortcut, slow_params[:, offset:], valid_mask))
    fast_branch = branch(fast_low, weights[5], weights[6], weights[7], fast_params, valid_mask)
    fast_result = jax.nn.silu(fast_branch + fast_signal)
    return (slow_result, fast_result)

def layer_two(slow_signal, fast_signal, weights, slow_params, fast_params, valid_mask):
    slow_branch = branch(low(slow_signal), weights[0], weights[1], weights[2], slow_params, valid_mask)
    fast_branch = branch(low(fast_signal), weights[3], weights[4], weights[5], fast_params, valid_mask)
    return (jax.nn.silu(slow_branch + slow_signal), jax.nn.silu(fast_branch + fast_signal))

def reference(slow_input, fast_input, slow_cotangent, fast_cotangent, clip_counts, lateral_weight, slow_reduce_one, slow_spatial_one, slow_expand_one, slow_shortcut_one, fast_reduce_one, fast_spatial_one, fast_expand_one, slow_reduce_two, slow_spatial_two, slow_expand_two, fast_reduce_two, fast_spatial_two, fast_expand_two, slow_norms_one, fast_norms_one, slow_norms_two, fast_norms_two):
    positions = jnp.arange(CLIPS, dtype=jnp.int32) % CAP
    per_clip = jnp.repeat(clip_counts, CAP)
    valid_mask = (positions < per_clip).astype(jnp.float32).reshape(CLIPS, 1, 1, 1, 1)
    weights = (lateral_weight, slow_reduce_one, slow_spatial_one, slow_expand_one, slow_shortcut_one, fast_reduce_one, fast_spatial_one, fast_expand_one, slow_reduce_two, slow_spatial_two, slow_expand_two, fast_reduce_two, fast_spatial_two, fast_expand_two)
    weights = tuple((weight.astype(jnp.float32) for weight in weights))
    norms = (slow_norms_one, fast_norms_one, slow_norms_two, fast_norms_two)

    def first_layer(slow_signal, fast_signal, layer_weights, slow_params, fast_params):
        return layer_one(slow_signal, fast_signal, layer_weights, slow_params, fast_params, valid_mask)

    def second_layer(slow_signal, fast_signal, layer_weights, slow_params, fast_params):
        return layer_two(slow_signal, fast_signal, layer_weights, slow_params, fast_params, valid_mask)
    first_saved = jax.checkpoint(first_layer)
    second_saved = jax.checkpoint(second_layer)

    def forward(slow_signal, fast_signal, all_weights, all_norms):
        slow_hidden, fast_hidden = first_saved(slow_signal, fast_signal, all_weights[:8], all_norms[0], all_norms[1])
        slow_result, fast_result = second_saved(slow_hidden, fast_hidden, all_weights[8:], all_norms[2], all_norms[3])
        return (valid_mask * slow_result, valid_mask * fast_result)
    outputs, pullback = jax.vjp(forward, slow_input.astype(jnp.float32), fast_input.astype(jnp.float32), weights, norms)
    grads = pullback((slow_cotangent.astype(jnp.float32), fast_cotangent.astype(jnp.float32)))
    weight_grads = grads[2]
    norm_grads = grads[3]
    return (outputs[0].astype(jnp.bfloat16), outputs[1].astype(jnp.bfloat16), grads[0], grads[1], weight_grads[0], weight_grads[1], weight_grads[2], weight_grads[3], weight_grads[4], weight_grads[5], weight_grads[6], weight_grads[7], weight_grads[8], weight_grads[9], weight_grads[10], weight_grads[11], weight_grads[12], weight_grads[13], norm_grads[0], norm_grads[1], norm_grads[2], norm_grads[3])
```

```python
import jax
import jax.numpy as jnp
from jax import lax
from jax.sharding import PartitionSpec as P

epsilon = 1e-05


def with_halo(shard, sides, width):
    for axis, dim in sides:
        count, length = (lax.axis_size(axis), shard.shape[dim])
        up = [(i, (i + 1) % count) for i in range(count - 1)]
        down = [(j, i) for i, j in up]
        last = lax.slice_in_dim(shard, length - width, length, axis=dim)
        leading = lax.slice_in_dim(shard, 0, width, axis=dim)
        before = lax.ppermute(last, axis, up)
        after = lax.ppermute(leading, axis, down)
        shard = jnp.concatenate([before, shard, after], axis=dim)
    return shard


def silu_slope(signal):
    sigma = jax.nn.sigmoid(signal)
    return sigma * (1.0 + signal * (1.0 - sigma))


def matmul(left, right):
    return jnp.dot(left, right, preferred_element_type=jnp.float32)


def outer_product(left, right):
    return lax.dot_general(
        left, right, (((0,), (0,)), ((), ())), preferred_element_type=jnp.float32
    )


def times_transposed(left, right):
    return lax.dot_general(
        left, right, (((1,), (1,)), ((), ())), preferred_element_type=jnp.float32
    )


def flatten_rows(signal):
    return signal.reshape(-1, signal.shape[-1])


def unflatten(rows_value, layout):
    return rows_value.reshape(layout[:4] + (rows_value.shape[-1],))


AXES = ("clips", "ha", "wa")


def pack(vectors):
    flat = jnp.concatenate([vector.reshape(-1) for vector in vectors])
    short = -flat.shape[0] % 1024
    return jnp.pad(flat, (0, short)).reshape(-1, 128)


def all_sums(vectors):
    gathered = lax.all_gather(pack(vectors), AXES, axis=0)
    flat = jnp.sum(gathered, axis=0).reshape(-1)
    result = []
    at = 0
    for vector in vectors:
        result.append(flat[at : at + vector.size].reshape(vector.shape))
        at += vector.size
    return result


def norm_sums(signal, valid_mask):
    masked = signal * valid_mask
    return [jnp.sum(masked, axis=(0, 1, 2, 3)), jnp.sum(masked * signal, axis=(0, 1, 2, 3))]


def norm_apply(signal, params, sums, counted):
    average = sums[0] / counted
    inverse_std = lax.rsqrt(sums[1] / counted - average * average + epsilon)
    normal = (signal - average) * inverse_std
    return ((1.0 + params[0]) * normal + params[1], (normal, inverse_std, counted))


def back_sums(gradient, saved, valid_mask):
    masked = gradient * valid_mask
    return [jnp.sum(masked, axis=(0, 1, 2, 3)), jnp.sum(masked * saved[0], axis=(0, 1, 2, 3))]


def back_apply(gradient, params, saved, sums, valid_mask):
    normal, inverse_std, counted = saved
    totals, crossed = sums
    result = (
        (1.0 + params[0])
        * inverse_std
        * (gradient - valid_mask * (totals + normal * crossed) / counted)
    )
    return (result.astype(jnp.bfloat16), jnp.stack([crossed, totals]))


def time_patches(signal):
    length = signal.shape[1]
    padded = jnp.pad(signal, ((0, 0), (1, 1), (0, 0), (0, 0), (0, 0)))
    return jnp.concatenate([padded[:, step : step + length] for step in range(3)], axis=-1)


def time_back(gradient):
    length = gradient.shape[1]
    pieces = jnp.split(gradient, 3, axis=-1)
    result = None
    for step in range(3):
        shifted = jnp.pad(pieces[step], ((0, 0), (step, 2 - step), (0, 0), (0, 0), (0, 0)))
        result = shifted if result is None else result + shifted
    return result[:, 1 : 1 + length]


def space_patches(haloed, height, width, flipped):
    pieces = []
    for row_step in range(3):
        for col_step in range(3):
            row_start = 2 - row_step if flipped else row_step
            col_start = 2 - col_step if flipped else col_step
            pieces.append(
                haloed[:, :, row_start : row_start + height, col_start : col_start + width]
            )
    return jnp.concatenate(pieces, axis=-1)


def lateral_patches(signal):
    slow_len = signal.shape[1] // 4
    padded = jnp.pad(signal, ((0, 0), (2, 2), (0, 0), (0, 0), (0, 0)))
    grouped = padded.reshape((signal.shape[0], slow_len + 1, 4) + signal.shape[2:])
    pieces = [grouped[:, 0:slow_len, step] for step in range(4)] + [grouped[:, 1 : slow_len + 1, 0]]
    return jnp.concatenate(pieces, axis=-1)


def lateral_back(gradient):
    slow_len = gradient.shape[1]
    pieces = jnp.split(gradient, 5, axis=-1)
    tail_pad = ((0, 0), (0, 1), (0, 0), (0, 0), (0, 0))
    phases = [
        jnp.pad(pieces[0], tail_pad) + jnp.pad(pieces[4], ((0, 0), (1, 0), (0, 0), (0, 0), (0, 0)))
    ]
    phases = phases + [jnp.pad(pieces[step], tail_pad) for step in range(1, 4)]
    stacked = jnp.stack(phases, axis=2)
    merged = stacked.reshape((gradient.shape[0], 4 * slow_len + 4) + stacked.shape[3:])
    return merged[:, 2 : 2 + 4 * slow_len]


def spatial_halo(signal):
    return with_halo(signal, (("ha", 2), ("wa", 3)), 1)


def layer_forward(slow_in, fast_in, slow_w, fast_w, slow_p, fast_p, mask, counts, shortcut):
    slow_cnt, fast_cnt = counts
    sp, fp = time_patches(slow_in), time_patches(fast_in)
    ls, lf = slow_in.shape, fast_in.shape
    za_s = unflatten(matmul(flatten_rows(sp), slow_w[0].reshape(-1, slow_w[0].shape[-1])), ls)
    za_f = unflatten(matmul(flatten_rows(fp), fast_w[0].reshape(-1, fast_w[0].shape[-1])), lf)
    vectors = norm_sums(za_s, mask) + norm_sums(za_f, mask)
    if shortcut is not None:
        vectors = vectors + norm_sums(shortcut, mask)
    sums = all_sums(vectors)
    rs, rf = za_s.shape[-1], za_f.shape[-1]
    un_s, sv1s = norm_apply(za_s, slow_p[:, :rs], sums[0:2], slow_cnt)
    un_f, sv1f = norm_apply(za_f, fast_p[:, :rf], sums[2:4], fast_cnt)
    short = None
    if shortcut is not None:
        offset = slow_p.shape[1] - shortcut.shape[-1]
        short = norm_apply(shortcut, slow_p[:, offset:], sums[4:6], slow_cnt)
    ha_s, ha_f = [jax.nn.silu(v).astype(jnp.bfloat16) for v in (un_s, un_f)]
    ps = space_patches(spatial_halo(ha_s), ls[2], ls[3], False)
    pf = space_patches(spatial_halo(ha_f), lf[2], lf[3], False)
    zb_s = unflatten(matmul(flatten_rows(ps), slow_w[1].reshape(-1, slow_w[1].shape[-1])), ls)
    zb_f = unflatten(matmul(flatten_rows(pf), fast_w[1].reshape(-1, fast_w[1].shape[-1])), lf)
    sums = all_sums(norm_sums(zb_s, mask) + norm_sums(zb_f, mask))
    es, ef = rs + zb_s.shape[-1], rf + zb_f.shape[-1]
    um_s, sv2s = norm_apply(zb_s, slow_p[:, rs:es], sums[0:2], slow_cnt)
    um_f, sv2f = norm_apply(zb_f, fast_p[:, rf:ef], sums[2:4], fast_cnt)
    hb_s, hb_f = [jax.nn.silu(v).astype(jnp.bfloat16) for v in (um_s, um_f)]
    zc_s = unflatten(matmul(flatten_rows(hb_s), slow_w[2]), ls)
    zc_f = unflatten(matmul(flatten_rows(hb_f), fast_w[2]), lf)
    sums = all_sums(norm_sums(zc_s, mask) + norm_sums(zc_f, mask))
    xs, xf = es + zc_s.shape[-1], ef + zc_f.shape[-1]
    out_s, sv3s = norm_apply(zc_s, slow_p[:, es:xs], sums[0:2], slow_cnt)
    out_f, sv3f = norm_apply(zc_f, fast_p[:, ef:xf], sums[2:4], fast_cnt)
    saved_s = (sp, un_s, sv1s, ps, um_s, sv2s, hb_s, sv3s)
    saved_f = (fp, un_f, sv1f, pf, um_f, sv2f, hb_f, sv3f)
    return out_s, out_f, short, saved_s, saved_f


def layer_backward(g_s, g_f, slow_w, fast_w, slow_p, fast_p, saved_s, saved_f, mask, short):
    sp, un_s, sv1s, ps, um_s, sv2s, hb_s, sv3s = saved_s
    fp, un_f, sv1f, pf, um_f, sv2f, hb_f, sv3f = saved_f
    ls, lf = g_s.shape, g_f.shape
    rs, rf = un_s.shape[-1], un_f.shape[-1]
    es, ef = rs + um_s.shape[-1], rf + um_f.shape[-1]
    xs, xf = es + g_s.shape[-1], ef + g_f.shape[-1]
    vectors = back_sums(g_s, sv3s, mask) + back_sums(g_f, sv3f, mask)
    if short is not None:
        vectors = vectors + back_sums(g_s, short, mask)[1:]
    sums = all_sums(vectors)
    gz_s, par3s = back_apply(g_s, slow_p[:, es:xs], sv3s, sums[0:2], mask)
    gz_f, par3f = back_apply(g_f, fast_p[:, ef:xf], sv3f, sums[2:4], mask)
    short_back = None
    if short is not None:
        short_back = back_apply(g_s, slow_p[:, xs:], short, (sums[0], sums[4]), mask)
    gw3s = outer_product(flatten_rows(hb_s), flatten_rows(gz_s))
    gw3f = outer_product(flatten_rows(hb_f), flatten_rows(gz_f))
    g_s = unflatten(times_transposed(flatten_rows(gz_s), slow_w[2]), ls) * silu_slope(um_s)
    g_f = unflatten(times_transposed(flatten_rows(gz_f), fast_w[2]), lf) * silu_slope(um_f)
    sums = all_sums(back_sums(g_s, sv2s, mask) + back_sums(g_f, sv2f, mask))
    gz_s, par2s = back_apply(g_s, slow_p[:, rs:es], sv2s, sums[0:2], mask)
    gz_f, par2f = back_apply(g_f, fast_p[:, rf:ef], sv2f, sums[2:4], mask)
    gw2s = outer_product(flatten_rows(ps), flatten_rows(gz_s)).reshape(slow_w[1].shape)
    gw2f = outer_product(flatten_rows(pf), flatten_rows(gz_f)).reshape(fast_w[1].shape)
    bs = space_patches(spatial_halo(gz_s), ls[2], ls[3], True)
    bf = space_patches(spatial_halo(gz_f), lf[2], lf[3], True)
    flip_s = jnp.transpose(slow_w[1], (0, 1, 3, 2)).reshape(-1, slow_w[1].shape[2])
    flip_f = jnp.transpose(fast_w[1], (0, 1, 3, 2)).reshape(-1, fast_w[1].shape[2])
    g_s = unflatten(matmul(flatten_rows(bs), flip_s), ls) * silu_slope(un_s)
    g_f = unflatten(matmul(flatten_rows(bf), flip_f), lf) * silu_slope(un_f)
    sums = all_sums(back_sums(g_s, sv1s, mask) + back_sums(g_f, sv1f, mask))
    gz_s, par1s = back_apply(g_s, slow_p[:, :rs], sv1s, sums[0:2], mask)
    gz_f, par1f = back_apply(g_f, fast_p[:, :rf], sv1f, sums[2:4], mask)
    gw1s = outer_product(flatten_rows(sp), flatten_rows(gz_s)).reshape(slow_w[0].shape)
    gw1f = outer_product(flatten_rows(fp), flatten_rows(gz_f)).reshape(fast_w[0].shape)
    in_s = time_back(
        unflatten(times_transposed(flatten_rows(gz_s), slow_w[0].reshape(-1, rs)), ls)
    )
    in_f = time_back(
        unflatten(times_transposed(flatten_rows(gz_f), fast_w[0].reshape(-1, rf)), lf)
    )
    params_s = jnp.concatenate([par1s, par2s, par3s], axis=1)
    params_f = jnp.concatenate([par1f, par2f, par3f], axis=1)
    return in_s, in_f, (gw1s, gw2s, gw3s), (gw1f, gw2f, gw3f), params_s, params_f, short_back


TILE = ("ha", "wa")


def gather_weights(shards, dims):
    rows = [shard.reshape(-1) for shard in shards]
    flat = jnp.concatenate(rows)
    short = -flat.shape[0] % 4096
    packed = jnp.pad(flat, (0, short)).reshape(-1, 256)
    gathered = lax.all_gather(packed, TILE, axis=0)
    count = gathered.shape[0]
    flat = gathered.reshape(count, -1)
    result = []
    at = 0
    for shard, dim in zip(shards, dims):
        part = flat[:, at : at + shard.size].reshape((count,) + shard.shape)
        at += shard.size
        part = jnp.moveaxis(part, 0, dim)
        full = shard.shape[:dim] + (count * shard.shape[dim],) + shard.shape[dim + 1 :]
        result.append(part.reshape(full))
    return result


def reduce_grads(grads, dims, count):
    parts = []
    shapes = []
    for grad, dim in zip(grads, dims):
        low = grad.astype(jnp.bfloat16)
        depth = low.shape[dim] // count
        split = low.reshape(low.shape[:dim] + (count, depth) + low.shape[dim + 1 :])
        split = jnp.moveaxis(split, dim, 0)
        shapes.append(split.shape[1:])
        parts.append(split.reshape(count, -1))
    flat = jnp.concatenate(parts, axis=1)
    short = -flat.shape[1] % 4096
    packed = jnp.pad(flat, ((0, 0), (0, short))).reshape(count, -1, 256)
    summed = lax.psum_scatter(packed, TILE, scatter_dimension=0, tiled=False)
    total = lax.psum(summed, "clips").reshape(-1)
    result = []
    at = 0
    for shape in shapes:
        size = 1
        for length in shape:
            size *= length
        result.append(total[at : at + size].reshape(shape).astype(jnp.float32))
        at += size
    return result


def on_device(
    slow_input,
    fast_input,
    slow_cotangent,
    fast_cotangent,
    clip_counts,
    lateral_weight,
    slow_reduce_one,
    slow_spatial_one,
    slow_expand_one,
    slow_shortcut_one,
    fast_reduce_one,
    fast_spatial_one,
    fast_expand_one,
    slow_reduce_two,
    slow_spatial_two,
    slow_expand_two,
    fast_reduce_two,
    fast_spatial_two,
    fast_expand_two,
    slow_norms_one,
    fast_norms_one,
    slow_norms_two,
    fast_norms_two,
):
    count = lax.axis_size("ha") * lax.axis_size("wa")
    lateral_full, reduce_one = gather_weights((lateral_weight, slow_reduce_one), (1, 1))
    rest = gather_weights(
        (
            slow_spatial_one,
            slow_expand_one,
            slow_shortcut_one,
            fast_reduce_one,
            fast_spatial_one,
            fast_expand_one,
        ),
        (2, 0, 0, 1, 2, 0),
    )
    two = gather_weights(
        (
            slow_reduce_two,
            slow_spatial_two,
            slow_expand_two,
            fast_reduce_two,
            fast_spatial_two,
            fast_expand_two,
        ),
        (1, 2, 0, 1, 2, 0),
    )
    slow_w1 = (reduce_one, rest[0], rest[1])
    shortcut_w = rest[2]
    fast_w1 = tuple(rest[3:6])
    slow_w2, fast_w2 = tuple(two[:3]), tuple(two[3:])
    capacity = slow_input.shape[0]
    mask = (
        (jnp.arange(capacity, dtype=jnp.int32) < clip_counts[0])
        .astype(jnp.float32)
        .reshape(capacity, 1, 1, 1, 1)
    )
    slow_layout = slow_input.shape
    slow_width = slow_input.shape[-1]
    clips_held = jnp.sum(lax.all_gather(clip_counts, "clips", axis=0)).astype(jnp.float32)
    spread = lax.axis_size("ha") * lax.axis_size("wa")
    slow_cnt = clips_held * (slow_layout[1] * slow_layout[2] * slow_layout[3] * spread)
    fast_layout = fast_input.shape
    fast_cnt = clips_held * (fast_layout[1] * fast_layout[2] * fast_layout[3] * spread)
    counts = (slow_cnt, fast_cnt)
    lateral_width = lateral_full.shape[-1]
    patches_lateral = lateral_patches(fast_input)
    united = unflatten(
        matmul(flatten_rows(patches_lateral), lateral_full.reshape(-1, lateral_width)), slow_layout
    )
    joined = jnp.concatenate([slow_input, united.astype(jnp.bfloat16)], axis=-1)
    shortcut = unflatten(matmul(flatten_rows(joined), shortcut_w), slow_layout)
    one_s, one_f, short, saved_s1, saved_f1 = layer_forward(
        joined, fast_input, slow_w1, fast_w1, slow_norms_one, fast_norms_one, mask, counts, shortcut
    )
    slow_sum_one = one_s + short[0]
    slow_hidden = jax.nn.silu(slow_sum_one)
    fast_sum_one = one_f + fast_input.astype(jnp.float32)
    fast_hidden = jax.nn.silu(fast_sum_one)
    two_s, two_f, _, saved_s2, saved_f2 = layer_forward(
        slow_hidden.astype(jnp.bfloat16),
        fast_hidden.astype(jnp.bfloat16),
        slow_w2,
        fast_w2,
        slow_norms_two,
        fast_norms_two,
        mask,
        counts,
        None,
    )
    slow_sum_two = two_s + slow_hidden
    fast_sum_two = two_f + fast_hidden
    slow_output = (mask * jax.nn.silu(slow_sum_two)).astype(jnp.bfloat16)
    fast_output = (mask * jax.nn.silu(fast_sum_two)).astype(jnp.bfloat16)
    slow_pre_two = slow_cotangent.astype(jnp.float32) * mask * silu_slope(slow_sum_two)
    fast_pre_two = fast_cotangent.astype(jnp.float32) * mask * silu_slope(fast_sum_two)
    in_s2, in_f2, gws2, gwf2, grad_slow_norms_two, grad_fast_norms_two, _ = layer_backward(
        slow_pre_two,
        fast_pre_two,
        slow_w2,
        fast_w2,
        slow_norms_two,
        fast_norms_two,
        saved_s2,
        saved_f2,
        mask,
        None,
    )
    summed_two = reduce_grads(gws2 + gwf2, (1, 2, 0, 1, 2, 0), count)
    slow_pre_one = (in_s2 + slow_pre_two) * silu_slope(slow_sum_one)
    fast_pre_one = (in_f2 + fast_pre_two) * silu_slope(fast_sum_one)
    in_s1, in_f1, gws1, gwf1, params_s1, grad_fast_norms_one, short_back = layer_backward(
        slow_pre_one,
        fast_pre_one,
        slow_w1,
        fast_w1,
        slow_norms_one,
        fast_norms_one,
        saved_s1,
        saved_f1,
        mask,
        short[1],
    )
    shortcut_low, shortcut_params = short_back
    grad_shortcut = outer_product(flatten_rows(joined), flatten_rows(shortcut_low))
    joined_grad = in_s1 + unflatten(
        times_transposed(flatten_rows(shortcut_low), shortcut_w), slow_layout
    )
    grad_slow_input = joined_grad[..., :slow_width]
    united_low = joined_grad[..., slow_width:].astype(jnp.bfloat16)
    grad_lateral = outer_product(flatten_rows(patches_lateral), flatten_rows(united_low)).reshape(
        lateral_full.shape
    )
    lateral_patch_grad = unflatten(
        times_transposed(flatten_rows(united_low), lateral_full.reshape(-1, lateral_width)),
        slow_layout,
    )
    grad_fast_input = in_f1 + fast_pre_one + lateral_back(lateral_patch_grad)
    early = reduce_grads((gws1[1], gws1[2], grad_shortcut), (2, 0, 0), count)
    late = reduce_grads((grad_lateral, gws1[0]) + gwf1, (1, 1, 1, 2, 0), count)
    summed = (
        late[0],
        late[1],
        early[0],
        early[1],
        early[2],
        late[2],
        late[3],
        late[4],
    ) + tuple(summed_two)
    grad_slow_norms_one = jnp.concatenate([params_s1, shortcut_params], axis=1)
    return (
        slow_output,
        fast_output,
        grad_slow_input,
        grad_fast_input,
        summed[0],
        summed[1],
        summed[2],
        summed[3],
        summed[4],
        summed[5],
        summed[6],
        summed[7],
        summed[8],
        summed[9],
        summed[10],
        summed[11],
        summed[12],
        summed[13],
        grad_slow_norms_one,
        grad_fast_norms_one,
        grad_slow_norms_two,
        grad_fast_norms_two,
    )


def solution(mesh):
    in_specs = (
        P("clips", None, "ha", "wa", None),
        P("clips", None, "ha", "wa", None),
        P("clips", None, "ha", "wa", None),
        P("clips", None, "ha", "wa", None),
        P("clips"),
        P(None, ("ha", "wa"), None),
        P(None, ("ha", "wa"), None),
        P(None, None, ("ha", "wa"), None),
        P(("ha", "wa"), None),
        P(("ha", "wa"), None),
        P(None, ("ha", "wa"), None),
        P(None, None, ("ha", "wa"), None),
        P(("ha", "wa"), None),
        P(None, ("ha", "wa"), None),
        P(None, None, ("ha", "wa"), None),
        P(("ha", "wa"), None),
        P(None, ("ha", "wa"), None),
        P(None, None, ("ha", "wa"), None),
        P(("ha", "wa"), None),
        P(),
        P(),
        P(),
        P(),
    )
    out_specs = (
        P("clips", None, "ha", "wa", None),
        P("clips", None, "ha", "wa", None),
        P("clips", None, "ha", "wa", None),
        P("clips", None, "ha", "wa", None),
        P(None, ("ha", "wa"), None),
        P(None, ("ha", "wa"), None),
        P(None, None, ("ha", "wa"), None),
        P(("ha", "wa"), None),
        P(("ha", "wa"), None),
        P(None, ("ha", "wa"), None),
        P(None, None, ("ha", "wa"), None),
        P(("ha", "wa"), None),
        P(None, ("ha", "wa"), None),
        P(None, None, ("ha", "wa"), None),
        P(("ha", "wa"), None),
        P(None, ("ha", "wa"), None),
        P(None, None, ("ha", "wa"), None),
        P(("ha", "wa"), None),
        P(),
        P(),
        P(),
        P(),
    )
    return jax.shard_map(
        on_device, mesh=mesh, in_specs=in_specs, out_specs=out_specs, check_vma=False
    )
```

```python
import jax
import jax.numpy as jnp
from jax import lax
from jax.sharding import PartitionSpec as P

epsilon = 1e-05


def with_halo(shard, sides, width):
    for axis, dim in sides:
        count, length = (lax.axis_size(axis), shard.shape[dim])
        up = [(i, (i + 1) % count) for i in range(count - 1)]
        down = [(j, i) for i, j in up]
        last = lax.slice_in_dim(shard, length - width, length, axis=dim)
        leading = lax.slice_in_dim(shard, 0, width, axis=dim)
        before = lax.ppermute(last, axis, up)
        after = lax.ppermute(leading, axis, down)
        shard = jnp.concatenate([before, shard, after], axis=dim)
    return shard


def silu_slope(signal):
    sigma = jax.nn.sigmoid(signal)
    return sigma * (1.0 + signal * (1.0 - sigma))


def matmul(left, right):
    return jnp.dot(left, right, preferred_element_type=jnp.float32)


def outer_product(left, right):
    return lax.dot_general(
        left, right, (((0,), (0,)), ((), ())), preferred_element_type=jnp.float32
    )


def times_transposed(left, right):
    return lax.dot_general(
        left, right, (((1,), (1,)), ((), ())), preferred_element_type=jnp.float32
    )


def flatten_rows(signal):
    return signal.reshape(-1, signal.shape[-1])


def unflatten(rows_value, layout):
    return rows_value.reshape(layout[:4] + (rows_value.shape[-1],))


AXES = ("clips", "ha", "wa")


def pack(vectors):
    flat = jnp.concatenate([vector.reshape(-1) for vector in vectors])
    short = -flat.shape[0] % 1024
    return jnp.pad(flat, (0, short)).reshape(-1, 128)


def tiers(packed):
    inner = jnp.sum(lax.all_gather(packed, ("ha", "wa"), axis=0), axis=0)
    return jnp.sum(lax.all_gather(inner, "clips", axis=0), axis=0)


def outer_first(packed):
    inner = jnp.sum(lax.all_gather(packed, "clips", axis=0), axis=0)
    return jnp.sum(lax.all_gather(inner, ("ha", "wa"), axis=0), axis=0)


def exchange(packed):
    count = lax.axis_size("clips") * lax.axis_size("ha") * lax.axis_size("wa")
    copies = jnp.broadcast_to(packed[None], (count,) + packed.shape)
    return jnp.sum(lax.all_to_all(copies, AXES, 0, 0), axis=0)


def others(packed, axes):
    count = 1
    for axis in axes:
        count *= lax.axis_size(axis)
    total = packed
    for step in range(1, count):
        total = total + lax.ppermute(packed, axes, [(i, (i + step) % count) for i in range(count)])
    return total


def permutes(packed):
    for axes in (("wa",), ("ha",), ("clips",)):
        packed = others(packed, axes)
    return packed


def all_sums(vectors, form):
    flat = form(pack(vectors)).reshape(-1)
    result = []
    at = 0
    for vector in vectors:
        result.append(flat[at : at + vector.size].reshape(vector.shape))
        at += vector.size
    return result


def norm_sums(signal, valid_mask):
    masked = signal * valid_mask
    return [jnp.sum(masked, axis=(0, 1, 2, 3)), jnp.sum(masked * signal, axis=(0, 1, 2, 3))]


def norm_apply(signal, params, sums, counted):
    average = sums[0] / counted
    inverse_std = lax.rsqrt(sums[1] / counted - average * average + epsilon)
    normal = (signal - average) * inverse_std
    return ((1.0 + params[0]) * normal + params[1], (normal, inverse_std, counted))


def back_sums(gradient, saved, valid_mask):
    masked = gradient * valid_mask
    return [jnp.sum(masked, axis=(0, 1, 2, 3)), jnp.sum(masked * saved[0], axis=(0, 1, 2, 3))]


def back_apply(gradient, params, saved, sums, valid_mask):
    normal, inverse_std, counted = saved
    totals, crossed = sums
    result = (
        (1.0 + params[0])
        * inverse_std
        * (gradient - valid_mask * (totals + normal * crossed) / counted)
    )
    return (result.astype(jnp.bfloat16), jnp.stack([crossed, totals]))


def time_patches(signal):
    length = signal.shape[1]
    padded = jnp.pad(signal, ((0, 0), (1, 1), (0, 0), (0, 0), (0, 0)))
    return jnp.concatenate([padded[:, step : step + length] for step in range(3)], axis=-1)


def time_back(gradient):
    length = gradient.shape[1]
    pieces = jnp.split(gradient, 3, axis=-1)
    result = None
    for step in range(3):
        shifted = jnp.pad(pieces[step], ((0, 0), (step, 2 - step), (0, 0), (0, 0), (0, 0)))
        result = shifted if result is None else result + shifted
    return result[:, 1 : 1 + length]


def space_patches(haloed, height, width, flipped):
    pieces = []
    for row_step in range(3):
        for col_step in range(3):
            row_start = 2 - row_step if flipped else row_step
            col_start = 2 - col_step if flipped else col_step
            pieces.append(
                haloed[:, :, row_start : row_start + height, col_start : col_start + width]
            )
    return jnp.concatenate(pieces, axis=-1)


def lateral_patches(signal):
    slow_len = signal.shape[1] // 4
    padded = jnp.pad(signal, ((0, 0), (2, 2), (0, 0), (0, 0), (0, 0)))
    grouped = padded.reshape((signal.shape[0], slow_len + 1, 4) + signal.shape[2:])
    pieces = [grouped[:, 0:slow_len, step] for step in range(4)] + [grouped[:, 1 : slow_len + 1, 0]]
    return jnp.concatenate(pieces, axis=-1)


def lateral_back(gradient):
    slow_len = gradient.shape[1]
    pieces = jnp.split(gradient, 5, axis=-1)
    tail_pad = ((0, 0), (0, 1), (0, 0), (0, 0), (0, 0))
    phases = [
        jnp.pad(pieces[0], tail_pad) + jnp.pad(pieces[4], ((0, 0), (1, 0), (0, 0), (0, 0), (0, 0)))
    ]
    phases = phases + [jnp.pad(pieces[step], tail_pad) for step in range(1, 4)]
    stacked = jnp.stack(phases, axis=2)
    merged = stacked.reshape((gradient.shape[0], 4 * slow_len + 4) + stacked.shape[3:])
    return merged[:, 2 : 2 + 4 * slow_len]


def spatial_halo(signal):
    return with_halo(signal, (("ha", 2), ("wa", 3)), 1)


def layer_forward(slow_in, fast_in, slow_w, fast_w, slow_p, fast_p, mask, counts, shortcut, form):
    slow_cnt, fast_cnt = counts
    sp, fp = time_patches(slow_in), time_patches(fast_in)
    ls, lf = slow_in.shape, fast_in.shape
    za_s = unflatten(matmul(flatten_rows(sp), slow_w[0].reshape(-1, slow_w[0].shape[-1])), ls)
    za_f = unflatten(matmul(flatten_rows(fp), fast_w[0].reshape(-1, fast_w[0].shape[-1])), lf)
    vectors = norm_sums(za_s, mask) + norm_sums(za_f, mask)
    if shortcut is not None:
        vectors = vectors + norm_sums(shortcut, mask)
    sums = all_sums(vectors, form)
    rs, rf = za_s.shape[-1], za_f.shape[-1]
    un_s, sv1s = norm_apply(za_s, slow_p[:, :rs], sums[0:2], slow_cnt)
    un_f, sv1f = norm_apply(za_f, fast_p[:, :rf], sums[2:4], fast_cnt)
    short = None
    if shortcut is not None:
        offset = slow_p.shape[1] - shortcut.shape[-1]
        short = norm_apply(shortcut, slow_p[:, offset:], sums[4:6], slow_cnt)
    ha_s, ha_f = [jax.nn.silu(v).astype(jnp.bfloat16) for v in (un_s, un_f)]
    ps = space_patches(spatial_halo(ha_s), ls[2], ls[3], False)
    pf = space_patches(spatial_halo(ha_f), lf[2], lf[3], False)
    zb_s = unflatten(matmul(flatten_rows(ps), slow_w[1].reshape(-1, slow_w[1].shape[-1])), ls)
    zb_f = unflatten(matmul(flatten_rows(pf), fast_w[1].reshape(-1, fast_w[1].shape[-1])), lf)
    sums = all_sums(norm_sums(zb_s, mask) + norm_sums(zb_f, mask), form)
    es, ef = rs + zb_s.shape[-1], rf + zb_f.shape[-1]
    um_s, sv2s = norm_apply(zb_s, slow_p[:, rs:es], sums[0:2], slow_cnt)
    um_f, sv2f = norm_apply(zb_f, fast_p[:, rf:ef], sums[2:4], fast_cnt)
    hb_s, hb_f = [jax.nn.silu(v).astype(jnp.bfloat16) for v in (um_s, um_f)]
    zc_s = unflatten(matmul(flatten_rows(hb_s), slow_w[2]), ls)
    zc_f = unflatten(matmul(flatten_rows(hb_f), fast_w[2]), lf)
    sums = all_sums(norm_sums(zc_s, mask) + norm_sums(zc_f, mask), form)
    xs, xf = es + zc_s.shape[-1], ef + zc_f.shape[-1]
    out_s, sv3s = norm_apply(zc_s, slow_p[:, es:xs], sums[0:2], slow_cnt)
    out_f, sv3f = norm_apply(zc_f, fast_p[:, ef:xf], sums[2:4], fast_cnt)
    saved_s = (sp, un_s, sv1s, ps, um_s, sv2s, hb_s, sv3s)
    saved_f = (fp, un_f, sv1f, pf, um_f, sv2f, hb_f, sv3f)
    return out_s, out_f, short, saved_s, saved_f


def layer_backward(g_s, g_f, slow_w, fast_w, slow_p, fast_p, saved_s, saved_f, mask, short, form):
    sp, un_s, sv1s, ps, um_s, sv2s, hb_s, sv3s = saved_s
    fp, un_f, sv1f, pf, um_f, sv2f, hb_f, sv3f = saved_f
    ls, lf = g_s.shape, g_f.shape
    rs, rf = un_s.shape[-1], un_f.shape[-1]
    es, ef = rs + um_s.shape[-1], rf + um_f.shape[-1]
    xs, xf = es + g_s.shape[-1], ef + g_f.shape[-1]
    vectors = back_sums(g_s, sv3s, mask) + back_sums(g_f, sv3f, mask)
    if short is not None:
        vectors = vectors + back_sums(g_s, short, mask)[1:]
    sums = all_sums(vectors, form)
    gz_s, par3s = back_apply(g_s, slow_p[:, es:xs], sv3s, sums[0:2], mask)
    gz_f, par3f = back_apply(g_f, fast_p[:, ef:xf], sv3f, sums[2:4], mask)
    short_back = None
    if short is not None:
        short_back = back_apply(g_s, slow_p[:, xs:], short, (sums[0], sums[4]), mask)
    gw3s = outer_product(flatten_rows(hb_s), flatten_rows(gz_s))
    gw3f = outer_product(flatten_rows(hb_f), flatten_rows(gz_f))
    g_s = unflatten(times_transposed(flatten_rows(gz_s), slow_w[2]), ls) * silu_slope(um_s)
    g_f = unflatten(times_transposed(flatten_rows(gz_f), fast_w[2]), lf) * silu_slope(um_f)
    sums = all_sums(back_sums(g_s, sv2s, mask) + back_sums(g_f, sv2f, mask), form)
    gz_s, par2s = back_apply(g_s, slow_p[:, rs:es], sv2s, sums[0:2], mask)
    gz_f, par2f = back_apply(g_f, fast_p[:, rf:ef], sv2f, sums[2:4], mask)
    gw2s = outer_product(flatten_rows(ps), flatten_rows(gz_s)).reshape(slow_w[1].shape)
    gw2f = outer_product(flatten_rows(pf), flatten_rows(gz_f)).reshape(fast_w[1].shape)
    bs = space_patches(spatial_halo(gz_s), ls[2], ls[3], True)
    bf = space_patches(spatial_halo(gz_f), lf[2], lf[3], True)
    flip_s = jnp.transpose(slow_w[1], (0, 1, 3, 2)).reshape(-1, slow_w[1].shape[2])
    flip_f = jnp.transpose(fast_w[1], (0, 1, 3, 2)).reshape(-1, fast_w[1].shape[2])
    g_s = unflatten(matmul(flatten_rows(bs), flip_s), ls) * silu_slope(un_s)
    g_f = unflatten(matmul(flatten_rows(bf), flip_f), lf) * silu_slope(un_f)
    sums = all_sums(back_sums(g_s, sv1s, mask) + back_sums(g_f, sv1f, mask), form)
    gz_s, par1s = back_apply(g_s, slow_p[:, :rs], sv1s, sums[0:2], mask)
    gz_f, par1f = back_apply(g_f, fast_p[:, :rf], sv1f, sums[2:4], mask)
    gw1s = outer_product(flatten_rows(sp), flatten_rows(gz_s)).reshape(slow_w[0].shape)
    gw1f = outer_product(flatten_rows(fp), flatten_rows(gz_f)).reshape(fast_w[0].shape)
    in_s = time_back(
        unflatten(times_transposed(flatten_rows(gz_s), slow_w[0].reshape(-1, rs)), ls)
    )
    in_f = time_back(
        unflatten(times_transposed(flatten_rows(gz_f), fast_w[0].reshape(-1, rf)), lf)
    )
    params_s = jnp.concatenate([par1s, par2s, par3s], axis=1)
    params_f = jnp.concatenate([par1f, par2f, par3f], axis=1)
    return in_s, in_f, (gw1s, gw2s, gw3s), (gw1f, gw2f, gw3f), params_s, params_f, short_back


TILE = ("ha", "wa")


def gather_weights(shards, dims):
    rows = [shard.reshape(-1) for shard in shards]
    flat = jnp.concatenate(rows)
    short = -flat.shape[0] % 4096
    packed = jnp.pad(flat, (0, short)).reshape(-1, 256)
    gathered = lax.all_gather(packed, TILE, axis=0)
    count = gathered.shape[0]
    flat = gathered.reshape(count, -1)
    result = []
    at = 0
    for shard, dim in zip(shards, dims):
        part = flat[:, at : at + shard.size].reshape((count,) + shard.shape)
        at += shard.size
        part = jnp.moveaxis(part, 0, dim)
        full = shard.shape[:dim] + (count * shard.shape[dim],) + shard.shape[dim + 1 :]
        result.append(part.reshape(full))
    return result


def reduce_grads(grads, dims, count, direct):
    parts = []
    shapes = []
    for grad, dim in zip(grads, dims):
        low = grad.astype(jnp.bfloat16)
        depth = low.shape[dim] // count
        split = low.reshape(low.shape[:dim] + (count, depth) + low.shape[dim + 1 :])
        split = jnp.moveaxis(split, dim, 0)
        shapes.append(split.shape[1:])
        parts.append(split.reshape(count, -1))
    flat = jnp.concatenate(parts, axis=1)
    short = -flat.shape[1] % 4096
    packed = jnp.pad(flat, ((0, 0), (0, short))).reshape(count, -1, 256)
    if direct:
        pieces = lax.all_to_all(packed, TILE, 0, 0)
        summed = jnp.sum(pieces.astype(jnp.float32), axis=0).astype(jnp.bfloat16)
    else:
        summed = lax.psum_scatter(packed, TILE, scatter_dimension=0, tiled=False)
    total = jnp.sum(lax.all_gather(summed, "clips", axis=0).astype(jnp.float32), axis=0)
    total = total.reshape(-1)
    result = []
    at = 0
    for shape in shapes:
        size = 1
        for length in shape:
            size *= length
        result.append(total[at : at + size].reshape(shape).astype(jnp.float32))
        at += size
    return result


def on_device(
    slow_input,
    fast_input,
    slow_cotangent,
    fast_cotangent,
    clip_counts,
    lateral_weight,
    slow_reduce_one,
    slow_spatial_one,
    slow_expand_one,
    slow_shortcut_one,
    fast_reduce_one,
    fast_spatial_one,
    fast_expand_one,
    slow_reduce_two,
    slow_spatial_two,
    slow_expand_two,
    fast_reduce_two,
    fast_spatial_two,
    fast_expand_two,
    slow_norms_one,
    fast_norms_one,
    slow_norms_two,
    fast_norms_two,
):
    count = lax.axis_size("ha") * lax.axis_size("wa")
    lateral_full, reduce_one = gather_weights((lateral_weight, slow_reduce_one), (1, 1))
    rest = gather_weights(
        (
            slow_spatial_one,
            slow_expand_one,
            slow_shortcut_one,
            fast_reduce_one,
            fast_spatial_one,
            fast_expand_one,
        ),
        (2, 0, 0, 1, 2, 0),
    )
    two = gather_weights(
        (
            slow_reduce_two,
            slow_spatial_two,
            slow_expand_two,
            fast_reduce_two,
            fast_spatial_two,
            fast_expand_two,
        ),
        (1, 2, 0, 1, 2, 0),
    )
    slow_w1 = (reduce_one, rest[0], rest[1])
    shortcut_w = rest[2]
    fast_w1 = tuple(rest[3:6])
    slow_w2, fast_w2 = tuple(two[:3]), tuple(two[3:])
    capacity = slow_input.shape[0]
    mask = (
        (jnp.arange(capacity, dtype=jnp.int32) < clip_counts[0])
        .astype(jnp.float32)
        .reshape(capacity, 1, 1, 1, 1)
    )
    slow_layout = slow_input.shape
    slow_width = slow_input.shape[-1]
    clips_held = lax.psum(clip_counts[0], "clips").astype(jnp.float32)
    spread = lax.axis_size("ha") * lax.axis_size("wa")
    slow_cnt = clips_held * (slow_layout[1] * slow_layout[2] * slow_layout[3] * spread)
    fast_layout = fast_input.shape
    fast_cnt = clips_held * (fast_layout[1] * fast_layout[2] * fast_layout[3] * spread)
    counts = (slow_cnt, fast_cnt)
    lateral_width = lateral_full.shape[-1]
    patches_lateral = lateral_patches(fast_input)
    united = unflatten(
        matmul(flatten_rows(patches_lateral), lateral_full.reshape(-1, lateral_width)), slow_layout
    )
    joined = jnp.concatenate([slow_input, united.astype(jnp.bfloat16)], axis=-1)
    shortcut = unflatten(matmul(flatten_rows(joined), shortcut_w), slow_layout)
    one_s, one_f, short, saved_s1, saved_f1 = layer_forward(
        joined, fast_input, slow_w1, fast_w1, slow_norms_one, fast_norms_one, mask, counts, shortcut, tiers
    )
    slow_sum_one = one_s + short[0]
    slow_hidden = jax.nn.silu(slow_sum_one)
    fast_sum_one = one_f + fast_input.astype(jnp.float32)
    fast_hidden = jax.nn.silu(fast_sum_one)
    two_s, two_f, _, saved_s2, saved_f2 = layer_forward(
        slow_hidden.astype(jnp.bfloat16),
        fast_hidden.astype(jnp.bfloat16),
        slow_w2,
        fast_w2,
        slow_norms_two,
        fast_norms_two,
        mask,
        counts,
        None,
        outer_first,
    )
    slow_sum_two = two_s + slow_hidden
    fast_sum_two = two_f + fast_hidden
    slow_output = (mask * jax.nn.silu(slow_sum_two)).astype(jnp.bfloat16)
    fast_output = (mask * jax.nn.silu(fast_sum_two)).astype(jnp.bfloat16)
    slow_pre_two = slow_cotangent.astype(jnp.float32) * mask * silu_slope(slow_sum_two)
    fast_pre_two = fast_cotangent.astype(jnp.float32) * mask * silu_slope(fast_sum_two)
    in_s2, in_f2, gws2, gwf2, grad_slow_norms_two, grad_fast_norms_two, _ = layer_backward(
        slow_pre_two,
        fast_pre_two,
        slow_w2,
        fast_w2,
        slow_norms_two,
        fast_norms_two,
        saved_s2,
        saved_f2,
        mask,
        None,
        exchange,
    )
    summed_two = reduce_grads(gws2 + gwf2, (1, 2, 0, 1, 2, 0), count, False)
    slow_pre_one = (in_s2 + slow_pre_two) * silu_slope(slow_sum_one)
    fast_pre_one = (in_f2 + fast_pre_two) * silu_slope(fast_sum_one)
    in_s1, in_f1, gws1, gwf1, params_s1, grad_fast_norms_one, short_back = layer_backward(
        slow_pre_one,
        fast_pre_one,
        slow_w1,
        fast_w1,
        slow_norms_one,
        fast_norms_one,
        saved_s1,
        saved_f1,
        mask,
        short[1],
        permutes,
    )
    shortcut_low, shortcut_params = short_back
    grad_shortcut = outer_product(flatten_rows(joined), flatten_rows(shortcut_low))
    joined_grad = in_s1 + unflatten(
        times_transposed(flatten_rows(shortcut_low), shortcut_w), slow_layout
    )
    grad_slow_input = joined_grad[..., :slow_width]
    united_low = joined_grad[..., slow_width:].astype(jnp.bfloat16)
    grad_lateral = outer_product(flatten_rows(patches_lateral), flatten_rows(united_low)).reshape(
        lateral_full.shape
    )
    lateral_patch_grad = unflatten(
        times_transposed(flatten_rows(united_low), lateral_full.reshape(-1, lateral_width)),
        slow_layout,
    )
    grad_fast_input = in_f1 + fast_pre_one + lateral_back(lateral_patch_grad)
    early = reduce_grads((gws1[1], gws1[2], grad_shortcut), (2, 0, 0), count, False)
    late = reduce_grads((grad_lateral, gws1[0]) + gwf1, (1, 1, 1, 2, 0), count, True)
    summed = (
        late[0],
        late[1],
        early[0],
        early[1],
        early[2],
        late[2],
        late[3],
        late[4],
    ) + tuple(summed_two)
    grad_slow_norms_one = jnp.concatenate([params_s1, shortcut_params], axis=1)
    return (
        slow_output,
        fast_output,
        grad_slow_input,
        grad_fast_input,
        summed[0],
        summed[1],
        summed[2],
        summed[3],
        summed[4],
        summed[5],
        summed[6],
        summed[7],
        summed[8],
        summed[9],
        summed[10],
        summed[11],
        summed[12],
        summed[13],
        grad_slow_norms_one,
        grad_fast_norms_one,
        grad_slow_norms_two,
        grad_fast_norms_two,
    )


def solution(mesh):
    in_specs = (
        P("clips", None, "ha", "wa", None),
        P("clips", None, "ha", "wa", None),
        P("clips", None, "ha", "wa", None),
        P("clips", None, "ha", "wa", None),
        P("clips"),
        P(None, ("ha", "wa"), None),
        P(None, ("ha", "wa"), None),
        P(None, None, ("ha", "wa"), None),
        P(("ha", "wa"), None),
        P(("ha", "wa"), None),
        P(None, ("ha", "wa"), None),
        P(None, None, ("ha", "wa"), None),
        P(("ha", "wa"), None),
        P(None, ("ha", "wa"), None),
        P(None, None, ("ha", "wa"), None),
        P(("ha", "wa"), None),
        P(None, ("ha", "wa"), None),
        P(None, None, ("ha", "wa"), None),
        P(("ha", "wa"), None),
        P(),
        P(),
        P(),
        P(),
    )
    out_specs = (
        P("clips", None, "ha", "wa", None),
        P("clips", None, "ha", "wa", None),
        P("clips", None, "ha", "wa", None),
        P("clips", None, "ha", "wa", None),
        P(None, ("ha", "wa"), None),
        P(None, ("ha", "wa"), None),
        P(None, None, ("ha", "wa"), None),
        P(("ha", "wa"), None),
        P(("ha", "wa"), None),
        P(None, ("ha", "wa"), None),
        P(None, None, ("ha", "wa"), None),
        P(("ha", "wa"), None),
        P(None, ("ha", "wa"), None),
        P(None, None, ("ha", "wa"), None),
        P(("ha", "wa"), None),
        P(None, ("ha", "wa"), None),
        P(None, None, ("ha", "wa"), None),
        P(("ha", "wa"), None),
        P(),
        P(),
        P(),
        P(),
    )
    return jax.shard_map(
        on_device, mesh=mesh, in_specs=in_specs, out_specs=out_specs, check_vma=False
    )
```

```python
import jax
import jax.numpy as jnp
from jax import lax
from jax.experimental import pallas as pl
from jax.experimental.pallas import tpu as pltpu
from jax.sharding import PartitionSpec as P

epsilon = 1e-05
F32 = jnp.float32
BF16 = jnp.bfloat16
TILE = ("ha", "wa")
PHASES = 4
SUB = 8


def dot(left, right):
    return lax.dot_general(left, right, (((1,), (0,)), ((), ())), preferred_element_type=F32)


def dot_tn(left, right):
    return lax.dot_general(left, right, (((0,), (0,)), ((), ())), preferred_element_type=F32)


def dot_nt(left, right):
    return lax.dot_general(left, right, (((1,), (1,)), ((), ())), preferred_element_type=F32)


def run(body, outs, smem=(), vmem=(), hbm=(), scratch=()):
    spec = pl.BlockSpec(memory_space=pltpu.VMEM)
    in_specs = (
        [pl.BlockSpec(memory_space=pltpu.SMEM)] * len(smem)
        + [spec] * len(vmem)
        + [pl.BlockSpec(memory_space=pl.ANY)] * len(hbm)
    )
    return pl.pallas_call(
        body,
        out_shape=[jax.ShapeDtypeStruct(shape, kind) for shape, kind in outs],
        in_specs=in_specs,
        out_specs=[spec] * len(outs),
        scratch_shapes=list(scratch),
        compiler_params=pltpu.CompilerParams(vmem_limit_bytes=32 * 1024 * 1024),
    )(*smem, *vmem, *hbm)


class Loads:
    def __init__(self, source, offset, target, sems):
        self.copies = []
        depth = target.shape[2]
        for step in range(target.shape[0]):
            copy = pltpu.make_async_copy(
                source.at[:, pl.ds(offset + step * depth, depth), :],
                target.at[step],
                sems.at[step],
            )
            copy.start()
            self.copies.append(copy)
        self.target = target

    def get(self, step):
        self.copies[step].wait()
        block = self.target[step]
        return block.reshape(-1, block.shape[-1])


class Geometry:
    def __init__(self, slow_shape, fast_shape):
        self.cap, self.frames, self.height, self.width = slow_shape[:4]
        self.groups = self.cap * self.frames
        self.rows = self.groups * SUB

    def three(self, value):
        return value.reshape(-1, SUB, value.shape[-1])

    def flat(self, value):
        return value.reshape(-1, value.shape[-1])

    def shift(self, value, step):
        lanes = value.shape[-1]
        whole = value.reshape(self.cap, self.frames, SUB, lanes)
        zero = jnp.zeros((self.cap, 1, SUB, lanes), value.dtype)
        if step > 0:
            whole = jnp.concatenate([zero, whole[:, :-1]], axis=1)
        else:
            whole = jnp.concatenate([whole[:, 1:], zero], axis=1)
        return whole.reshape(-1, lanes)


def mask_groups(shape, limit, scale=1):
    return lax.broadcasted_iota(jnp.int32, shape, 0) * scale < limit


def rep(ref, row, low, high):
    return jnp.broadcast_to(ref[row : row + 1, low:high], (SUB, high - low))


def fold(value, slow):
    fast = value[:, slow:]
    lanes = fast.shape[-1]
    part = lanes // PHASES
    if part % 128 == 0:
        total = fast[:, :part]
        for phase in range(1, PHASES):
            total = total + fast[:, phase * part : (phase + 1) * part]
        return jnp.concatenate([value[:, :slow]] + [total] * PHASES, axis=1)
    total = fast
    for phase in range(1, PHASES):
        total = total + pltpu.roll(fast, phase * part, 1)
    return jnp.concatenate([value[:, :slow], total], axis=1)


def lane_counts(inv_ref, lanes, slow):
    lane = lax.broadcasted_iota(jnp.int32, (SUB, lanes), 1)
    return jnp.where(lane < slow, inv_ref[0], inv_ref[1])


def moments(stats, inv_ref, slow, low=0, high=None):
    high = stats.shape[1] if high is None else high
    total, square = rep(stats, 0, low, high), rep(stats, 1, low, high)
    if slow < high - low:
        total, square = fold(total, slow), fold(square, slow)
    inv_n = lane_counts(inv_ref, high - low, slow)
    mean = total * inv_n
    return mean, lax.rsqrt(square * inv_n - mean * mean + epsilon)


def affine(stats, params, inv_ref, slow, low=0, high=None):
    mean, inv = moments(stats, inv_ref, slow, low, high)
    lanes = mean.shape[1]
    scale = (1.0 + rep(params, 0, 0, lanes)) * inv
    return scale, rep(params, 1, 0, lanes) - mean * scale, mean, inv


def back_rows(sums, inv_ref, slow, row, low=0, high=None):
    high = sums.shape[1] if high is None else high
    total = rep(sums, row, low, high)
    if slow < high - low:
        total = fold(total, slow)
    return total * lane_counts(inv_ref, high - low, slow)


def silu(value):
    return value * jax.nn.sigmoid(value)


def slope(value):
    sigma = jax.nn.sigmoid(value)
    return sigma * (1.0 + value * (1.0 - sigma))


def put_stats(ref, first, second, low=0):
    lanes = first.shape[-1]
    ref[0:1, low : low + lanes] = jnp.sum(jnp.sum(first, axis=0), axis=0, keepdims=True)
    ref[1:2, low : low + lanes] = jnp.sum(jnp.sum(second, axis=0), axis=0, keepdims=True)


def put_forward(ref, value, limit, low=0):
    masked = jnp.where(mask_groups(value.shape, limit), value, 0.0)
    put_stats(ref, masked, masked * value, low)


def put_messages(value, full_ref, top_ref, bottom_ref):
    lanes = value.shape[-1]
    pairs = value.reshape(-1, 2, SUB, lanes)
    first, second = pairs[:, 0], pairs[:, 1]
    near = lax.broadcasted_iota(jnp.int32, first.shape, 1) < SUB // 2
    top = jnp.where(near, first, pltpu.roll(second, SUB // 2, 1))
    bottom = jnp.where(near, pltpu.roll(first, SUB // 2, 1), second)
    full_ref[...] = value.reshape(-1, lanes).astype(BF16)
    top_ref[...] = top.reshape(-1, lanes).astype(BF16)
    bottom_ref[...] = bottom.reshape(-1, lanes).astype(BF16)


def unpack_bottom(value):
    both = jnp.stack([pltpu.roll(value, SUB // 2, 1), value], axis=1)
    return both.reshape(-1, SUB, value.shape[-1])


def unpack_top(value):
    both = jnp.stack([value, pltpu.roll(value, SUB // 2, 1)], axis=1)
    return both.reshape(-1, SUB, value.shape[-1])


class Neighbours:
    def __init__(self, own, up, down, side, side_up, side_down, meta, width):
        half = SUB // 2
        row = lax.broadcasted_iota(jnp.int32, own.shape, 1)
        near = row < half
        self.col = row % width
        self.width = width
        ha, wa, last = meta[1], meta[2], meta[3]
        up = unpack_bottom(jnp.where(ha > 0, up, 0.0))
        side_up = unpack_bottom(jnp.where(ha > 0, side_up, 0.0))
        down = unpack_top(jnp.where(ha < last, down, 0.0))
        side_down = unpack_top(jnp.where(ha < last, side_down, 0.0))
        self.rows = {
            0: own,
            -1: pltpu.roll(jnp.where(near, own, up), half, 1),
            1: pltpu.roll(jnp.where(near, down, own), half, 1),
        }
        sides = {
            0: pltpu.roll(side, half, 1),
            -1: jnp.where(near, side, side_up),
            1: jnp.where(near, side_down, side),
        }
        self.left = {key: jnp.where(wa > 0, value, 0.0) for key, value in sides.items()}
        self.right = {key: jnp.where(wa > 0, 0.0, value) for key, value in sides.items()}

    def at(self, row_step, col_step):
        base = self.rows[row_step]
        if col_step < 0:
            return pltpu.roll(
                jnp.where(self.col == self.width - 1, self.left[row_step], base), 1, 1
            )
        if col_step > 0:
            return pltpu.roll(jnp.where(self.col == 0, self.right[row_step], base), SUB - 1, 1)
        return base


def exchange_halo(full, top, bottom):
    high, wide = lax.axis_size("ha"), lax.axis_size("wa")

    def pairs(step, cross):
        result = []
        for row in range(high):
            for col in range(wide):
                other = wide - 1 - col if cross else col
                if 0 <= row + step < high:
                    result.append((row * wide + col, (row + step) * wide + other))
        return result

    return (
        lax.ppermute(bottom, TILE, pairs(1, False)),
        lax.ppermute(top, TILE, pairs(-1, False)),
        lax.ppermute(full, TILE, pairs(0, True)),
        lax.ppermute(bottom, TILE, pairs(1, True)),
        lax.ppermute(top, TILE, pairs(-1, True)),
    )


def butterfly(value, axis, low=None):
    size = lax.axis_size(axis)
    step = 1
    while step < size:
        pairs = [(index, index ^ step) for index in range(size)]
        sent = value if low is None else value.astype(low)
        got = lax.ppermute(sent, axis, pairs)
        value = sent.astype(value.dtype) + got.astype(value.dtype)
        step *= 2
    return value


def all_sum(value):
    for axis in ("wa", "ha", "clips"):
        value = butterfly(value, axis)
    return value


def time_conv(geo, parts, blocks):
    result = None
    for tap in range(3):
        at = 0
        total = None
        for part in parts:
            lanes = part.shape[-1]
            term = dot(part, blocks[tap][at : at + lanes])
            at += lanes
            total = term if total is None else total + term
        if tap != 1:
            total = geo.shift(total, 1 - tap)
        result = total if result is None else result + total
    return result


def fast_conv(geo, value, main, before, after):
    lanes = value.shape[-1] // PHASES
    result = dot(value, main)
    result = result + geo.shift(dot(value[:, -lanes:], before), 1)
    return result + geo.shift(dot(value[:, :lanes], after), -1)


def fast_conv_back(steps, main, before, after):
    lanes = before.shape[0]
    middle = dot_nt(steps[1], main)
    first = middle[:, :lanes] + dot_nt(steps[2], after)
    last = middle[:, -lanes:] + dot_nt(steps[0], before)
    return jnp.concatenate([first, middle[:, lanes:-lanes], last], axis=1)


def lane_block(value, phase, part):
    return pltpu.roll(value, value.shape[-1] - phase * part, 1) if phase else value


def fast_reduce_grad(value, steps, ref):
    lanes = value.shape[-1] // PHASES
    part = steps[1].shape[-1] // PHASES
    main = dot_tn(value, steps[1])
    before = dot_tn(value[:, -lanes:], steps[0])
    after = dot_tn(value[:, :lanes], steps[2])

    def block(row, col):
        return lane_block(main[row * lanes : (row + 1) * lanes], col, part)

    for tap in range(3):
        total = before if tap == 0 else None
        if tap == 2:
            total = lane_block(after, PHASES - 1, part)
        for col in range(PHASES):
            row = col + tap - 1
            if 0 <= row < PHASES:
                total = block(row, col) if total is None else total + block(row, col)
        ref[tap] = total


def gather_pack(parts):
    return lax.all_gather(jnp.concatenate(parts, axis=0), TILE, axis=0)


def columns(shard, lanes):
    depth, total = shard.shape
    return jnp.moveaxis(shard.reshape(depth, total // lanes, lanes), 1, 0).reshape(-1, lanes)


def uncolumns(rows, depth):
    lanes = rows.shape[-1]
    return jnp.moveaxis(rows.reshape(-1, depth, lanes), 0, 1).reshape(depth, -1)


def split_phases(value):
    cap, frames, height, width, lanes = value.shape
    value = value.reshape(cap, frames // PHASES, PHASES, height, width, lanes)
    return jnp.moveaxis(value, 2, 4).reshape(-1, PHASES * lanes)


def join_phases(value, shape):
    cap, frames, height, width, lanes = shape
    value = value.reshape(cap, frames // PHASES, height, width, PHASES, lanes)
    return jnp.moveaxis(value, 4, 2).reshape(shape)


def fast_shard(reduce, spatial, expand):
    lanes = reduce.shape[-1]
    return [reduce.reshape(-1, lanes), spatial.reshape(-1, lanes), expand.reshape(-1, lanes)]


def fast_full(blocks, reduce, spatial, expand):
    count, _, lanes = blocks.shape
    at = 0
    result = []
    for shard, dim in ((reduce, 1), (spatial, 2), (expand, 0)):
        rows = shard.size // lanes
        part = blocks[:, at : at + rows].reshape((count,) + shard.shape)
        at += rows
        part = jnp.moveaxis(part, 0, dim)
        result.append(
            part.reshape(shard.shape[:dim] + (count * shard.shape[dim],) + shard.shape[dim + 1 :])
        )
    taps, space, wide = result
    zero = jnp.zeros_like(taps[0])
    cols = []
    for col in range(PHASES):
        rows = [taps[row - col + 1] if abs(row - col) <= 1 else zero for row in range(PHASES)]
        cols.append(jnp.concatenate(rows, axis=0))
    main = jnp.concatenate(cols, axis=1)
    rest = (PHASES - 1) * lanes
    before = jnp.pad(taps[0], ((0, 0), (0, rest)))
    after = jnp.pad(taps[2], ((0, 0), (rest, 0)))
    eye = jnp.eye(PHASES, dtype=blocks.dtype)
    space = space.reshape((-1,) + space.shape[2:])
    space = jnp.einsum("pq,kio->kpiqo", eye, space).reshape(-1, PHASES * lanes, PHASES * lanes)
    wide = jnp.einsum("pq,io->piqo", eye, wide).reshape(PHASES * lanes, -1)
    return main, before, after, space, wide


def fast_grad_rows(grads, count, lanes):
    reduce, spatial, expand = grads
    part = expand.shape[0]
    reduce = reduce[:, :, :part].astype(BF16)
    spatial = spatial[:, :, :part].astype(BF16)
    pieces = [
        jnp.moveaxis(reduce.reshape(reduce.shape[0], count, -1, part), 1, 0).reshape(count, -1),
        jnp.moveaxis(spatial.reshape(spatial.shape[0], count, -1, part), 1, 0).reshape(count, -1),
        expand.astype(BF16).reshape(count, -1),
    ]
    flat = jnp.concatenate(pieces, axis=1)
    short = -flat.shape[1] % (16 * lanes)
    return jnp.pad(flat, ((0, 0), (0, short))).reshape(count, -1, lanes)


def fast_grad_shards(rows, reduce, spatial, expand):
    flat = rows.reshape(-1)
    result = []
    at = 0
    for shard in (reduce, spatial, expand):
        result.append(flat[at : at + shard.size].reshape(shard.shape))
        at += shard.size
    return result


def reduce_rows(parts):
    packed = jnp.concatenate(parts, axis=1)
    summed = lax.psum_scatter(packed, TILE, scatter_dimension=0, tiled=False)
    return butterfly(summed.astype(F32), "clips", BF16)


def on_device(
    slow_input,
    fast_input,
    slow_cotangent,
    fast_cotangent,
    clip_counts,
    lateral_weight,
    slow_reduce_one,
    slow_spatial_one,
    slow_expand_one,
    slow_shortcut_one,
    fast_reduce_one,
    fast_spatial_one,
    fast_expand_one,
    slow_reduce_two,
    slow_spatial_two,
    slow_expand_two,
    fast_reduce_two,
    fast_spatial_two,
    fast_expand_two,
    slow_norms_one,
    fast_norms_one,
    slow_norms_two,
    fast_norms_two,
):
    geo = Geometry(slow_input.shape, fast_input.shape)
    rows, groups = geo.rows, geo.groups
    half_rows = rows // 2
    count = lax.axis_size("ha") * lax.axis_size("wa")
    slow_wide = slow_input.shape[-1]
    fast_wide = PHASES * fast_input.shape[-1]
    wide = slow_wide + fast_wide
    mid = slow_reduce_one.shape[-1]
    fast_part = fast_reduce_one.shape[-1]
    fast_mid = PHASES * fast_part
    small = mid + fast_mid
    lat = lateral_weight.shape[-1]
    blocks = slow_wide // mid

    depth_one = slow_reduce_one.shape[1]
    depth_two = slow_reduce_two.shape[1]
    depth_mid = slow_spatial_one.shape[2]
    depth_lat = lateral_weight.shape[1]
    near = gather_pack([slow_reduce_one.reshape(-1, mid), slow_spatial_one.reshape(-1, mid)])
    far = gather_pack(
        [
            columns(slow_expand_one, mid),
            columns(slow_shortcut_one, mid),
            slow_reduce_two.reshape(-1, mid),
            slow_spatial_two.reshape(-1, mid),
            columns(slow_expand_two, mid),
        ]
    )
    at_space_one = 3 * depth_one
    at_short = blocks * depth_mid
    at_reduce_two = at_short + blocks * depth_one
    at_space_two = at_reduce_two + 3 * depth_two
    at_expand_two = at_space_two + 9 * depth_mid
    lateral = lax.all_gather(lateral_weight, TILE, axis=1, tiled=True)
    fast_shards_one = (fast_reduce_one, fast_spatial_one, fast_expand_one)
    fast_shards_two = (fast_reduce_two, fast_spatial_two, fast_expand_two)
    fast_rows = fast_shard(*fast_shards_one)
    split_at = sum(part.shape[0] for part in fast_rows)
    fast_blocks = gather_pack(fast_rows + fast_shard(*fast_shards_two))
    fast_one = fast_full(fast_blocks[:, :split_at], *fast_shards_one)
    fast_two = fast_full(fast_blocks[:, split_at:], *fast_shards_two)

    held = clip_counts[0]
    clips = butterfly(jnp.full((1, 128), held, F32), "clips")[0, 0]
    positions = clips * (SUB * geo.frames * count)
    inv_n = jnp.stack([1.0 / positions, 1.0 / (positions * PHASES)])
    ha, wa = lax.axis_index("ha"), lax.axis_index("wa")
    meta = jnp.stack([held * geo.frames, ha, wa, jnp.full_like(ha, lax.axis_size("ha") - 1)])
    scalars = (meta, inv_n)

    def joint(slow_p, fast_p):
        ends = (mid, 2 * mid, 2 * mid + slow_wide)
        fast_ends = (fast_part, 2 * fast_part, 2 * fast_part + fast_wide // PHASES)
        result = []
        at = fast_at = 0
        for end, fast_end in zip(ends, fast_ends):
            fast = jnp.tile(fast_p[:, fast_at:fast_end], (1, PHASES))
            result.append(jnp.concatenate([slow_p[:, at:end], fast], axis=1))
            at, fast_at = end, fast_end
        return result

    params_one = joint(slow_norms_one, fast_norms_one)
    params_two = joint(slow_norms_two, fast_norms_two)
    params_short = slow_norms_one[:, 2 * mid + slow_wide :]

    slow_x = slow_input.reshape(rows, slow_wide)
    fast_x = split_phases(fast_input)
    cot = jnp.concatenate(
        [slow_cotangent.reshape(rows, slow_wide), split_phases(fast_cotangent)], axis=1
    )
    dma = pltpu.SemaphoreType.DMA
    messages = [((rows, small), BF16), ((half_rows, small), BF16), ((half_rows, small), BF16)]
    stats_small = ((2, small), F32)
    stats_wide = ((2, wide), F32)
    stats_both = ((2, wide + slow_wide), F32)
    small_out = ((rows, small), F32)
    wide_out = ((rows, wide), F32)

    def lateral_kernel(x_ref, k_ref, main_ref, before_ref, after_ref, united_ref, fast_ref):
        lanes = x_ref.shape[1] // PHASES
        x = x_ref[...]
        main = dot(x[:, : 3 * lanes], k_ref[2:5].reshape(3 * lanes, lat))
        past = dot(x[:, 2 * lanes :], k_ref[0:2].reshape(2 * lanes, lat))
        united_ref[...] = (main + geo.shift(past, 1)).astype(BF16)
        fast_ref[...] = fast_conv(geo, x, main_ref[...], before_ref[...], after_ref[...])

    united, za_fast = run(
        lateral_kernel,
        [((rows, lat), BF16), ((rows, fast_mid), F32)],
        vmem=(fast_x, lateral, *fast_one[:3]),
    )

    def reduce_one_kernel(
        meta_ref, x_ref, united_ref, fast_ref, g_ref, za_ref, stats_ref, full, top, bottom, w, sems
    ):
        loads = Loads(g_ref, 0, w, sems)
        weights = [loads.get(tap) for tap in range(3)]
        za = time_conv(geo, (x_ref[...], united_ref[...]), weights)
        za = jnp.concatenate([za, fast_ref[...]], axis=1)
        za_ref[...] = za
        za = geo.three(za)
        put_forward(stats_ref, za, meta_ref[0])
        put_messages(za, full, top, bottom)

    za_one, stats, *message = run(
        reduce_one_kernel,
        [small_out, stats_small] + messages,
        smem=(meta,),
        vmem=(slow_x, united, za_fast),
        hbm=(near,),
        scratch=[pltpu.VMEM((3, count, depth_one, mid), BF16), dma((3,))],
    )
    stats_a1 = all_sum(stats)
    halo_one = exchange_halo(*message)

    def space_stage(za, stats_a, halo, params, gathered, offset, fast_w):
        def kernel(
            meta_ref,
            inv_ref,
            za_ref,
            up_ref,
            down_ref,
            side_ref,
            side_up_ref,
            side_down_ref,
            stats_ref,
            params_ref,
            fast_ref,
            g_ref,
            zb_ref,
            hidden_ref,
            out_stats,
            w,
            sems,
        ):
            loads = Loads(g_ref, offset, w, sems)
            scale, shift, _, _ = affine(stats_ref, params_ref, inv_ref, mid)

            def act(ref):
                return silu(geo.three(ref[...].astype(F32)) * scale + shift)

            own = act(za_ref)
            hidden_ref[...] = geo.flat(own).astype(BF16)
            near_by = Neighbours(
                own,
                act(up_ref),
                act(down_ref),
                act(side_ref),
                act(side_up_ref),
                act(side_down_ref),
                meta_ref,
                geo.width,
            )
            slow = fast = None
            for tap in range(9):
                moved = geo.flat(near_by.at(tap // 3 - 1, tap % 3 - 1)).astype(BF16)
                slow_term = dot(moved[:, :mid], loads.get(tap))
                fast_term = dot(moved[:, mid:], fast_ref[tap])
                slow = slow_term if slow is None else slow + slow_term
                fast = fast_term if fast is None else fast + fast_term
            zb = jnp.concatenate([slow, fast], axis=1)
            zb_ref[...] = zb
            put_forward(out_stats, geo.three(zb), meta_ref[0])

        zb, hidden, stats = run(
            kernel,
            [small_out, ((rows, small), BF16), stats_small],
            smem=scalars,
            vmem=(za, *halo, stats_a, params, fast_w),
            hbm=(gathered,),
            scratch=[pltpu.VMEM((9, count, depth_mid, mid), BF16), dma((9,))],
        )
        return zb, hidden, all_sum(stats)

    zb_one, ha_one, stats_b1 = space_stage(
        za_one, stats_a1, halo_one, params_one[1 - 1], near, at_space_one, fast_one[3]
    )

    def expand_body(inv_ref, zb_ref, stats_ref, params_ref, fast_ref, hidden_ref, zc_ref, loads):
        scale, shift, _, _ = affine(stats_ref, params_ref, inv_ref, mid)
        hidden = geo.flat(silu(geo.three(zb_ref[...]) * scale + shift)).astype(BF16)
        hidden_ref[...] = hidden
        zc_ref[:, slow_wide:] = dot(hidden[:, mid:], fast_ref[...])
        for block in range(blocks):
            zc_ref[:, block * mid : (block + 1) * mid] = dot(hidden[:, :mid], loads.get(block))

    def expand_one_kernel(
        meta_ref,
        inv_ref,
        zb_ref,
        stats_ref,
        params_ref,
        fast_ref,
        x_ref,
        united_ref,
        g_ref,
        hidden_ref,
        zc_ref,
        short_ref,
        out_stats,
        w,
        s,
        sems,
        more_sems,
    ):
        loads = Loads(g_ref, 0, w, sems)
        shorts = Loads(g_ref, at_short, s, more_sems)
        expand_body(inv_ref, zb_ref, stats_ref, params_ref, fast_ref, hidden_ref, zc_ref, loads)
        put_forward(out_stats, geo.three(zc_ref[...]), meta_ref[0])
        for block in range(blocks):
            weight = shorts.get(block)
            value = dot(x_ref[...], weight[:slow_wide]) + dot(united_ref[...], weight[slow_wide:])
            short_ref[:, block * mid : (block + 1) * mid] = value
            put_forward(out_stats, geo.three(value), meta_ref[0], wide + block * mid)

    hb_one, zc_one, short, stats = run(
        expand_one_kernel,
        [((rows, small), BF16), wide_out, ((rows, slow_wide), F32), stats_both],
        smem=scalars,
        vmem=(zb_one, stats_b1, params_one[1], fast_one[4], slow_x, united),
        hbm=(far,),
        scratch=[
            pltpu.VMEM((blocks, count, depth_mid, mid), BF16),
            pltpu.VMEM((blocks, count, depth_one, mid), BF16),
            dma((blocks,)),
            dma((blocks,)),
        ],
    )
    stats_c1 = all_sum(stats)

    def reduce_two_kernel(
        meta_ref,
        inv_ref,
        zc_ref,
        short_ref,
        stats_ref,
        params_ref,
        short_params_ref,
        x_ref,
        main_ref,
        before_ref,
        after_ref,
        g_ref,
        sum_ref,
        low_ref,
        za_ref,
        out_stats,
        full,
        top,
        bottom,
        w,
        sems,
    ):
        loads = Loads(g_ref, at_reduce_two, w, sems)
        scale, shift, _, _ = affine(stats_ref, params_ref, inv_ref, slow_wide, 0, wide)
        scale_s, shift_s, _, _ = affine(
            stats_ref, short_params_ref, inv_ref, slow_wide, wide, wide + slow_wide
        )
        normed = geo.three(zc_ref[...]) * scale + shift
        slow = normed[..., :slow_wide] + (geo.three(short_ref[...]) * scale_s + shift_s)
        fast = normed[..., slow_wide:] + geo.three(x_ref[...].astype(F32))
        total = jnp.concatenate([slow, fast], axis=-1)
        sum_ref[...] = geo.flat(total)
        low = geo.flat(silu(total)).astype(BF16)
        low_ref[...] = low
        weights = [loads.get(tap) for tap in range(3)]
        za = time_conv(geo, (low[:, :slow_wide],), weights)
        fast_za = fast_conv(
            geo, low[:, slow_wide:], main_ref[...], before_ref[...], after_ref[...]
        )
        za = jnp.concatenate([za, fast_za], axis=1)
        za_ref[...] = za
        za = geo.three(za)
        put_forward(out_stats, za, meta_ref[0])
        put_messages(za, full, top, bottom)

    reduce_two_scratch = [pltpu.VMEM((3, count, depth_two, mid), BF16), dma((3,))]
    sum_one, low_one, za_two, stats, *message = run(
        reduce_two_kernel,
        [wide_out, ((rows, wide), BF16), small_out, stats_small] + messages,
        smem=scalars,
        vmem=(zc_one, short, stats_c1, params_one[2], params_short, fast_x, *fast_two[:3]),
        hbm=(far,),
        scratch=reduce_two_scratch,
    )
    stats_a2 = all_sum(stats)
    halo_two = exchange_halo(*message)
    zb_two, ha_two, stats_b2 = space_stage(
        za_two, stats_a2, halo_two, params_two[0], far, at_space_two, fast_two[3]
    )

    def expand_two_kernel(
        meta_ref,
        inv_ref,
        zb_ref,
        stats_ref,
        params_ref,
        fast_ref,
        g_ref,
        hidden_ref,
        zc_ref,
        out_stats,
        w,
        sems,
    ):
        loads = Loads(g_ref, at_expand_two, w, sems)
        expand_body(inv_ref, zb_ref, stats_ref, params_ref, fast_ref, hidden_ref, zc_ref, loads)
        put_forward(out_stats, geo.three(zc_ref[...]), meta_ref[0])

    expand_scratch = [pltpu.VMEM((blocks, count, depth_mid, mid), BF16), dma((blocks,))]
    hb_two, zc_two, stats = run(
        expand_two_kernel,
        [((rows, small), BF16), wide_out, stats_wide],
        smem=scalars,
        vmem=(zb_two, stats_b2, params_two[1], fast_two[4]),
        hbm=(far,),
        scratch=expand_scratch,
    )
    stats_c2 = all_sum(stats)

    def head_kernel(
        meta_ref, inv_ref, zc_ref, stats_ref, params_ref, sum_ref, cot_ref, out_ref, g_ref, sums_ref
    ):
        scale, shift, mean, inv = affine(stats_ref, params_ref, inv_ref, slow_wide)
        zc = geo.three(zc_ref[...])
        total = zc * scale + shift + silu(geo.three(sum_ref[...]))
        valid = mask_groups(total.shape, meta_ref[0])
        sigma = jax.nn.sigmoid(total)
        out_ref[...] = geo.flat(jnp.where(valid, total * sigma, 0.0)).astype(BF16)
        slopes = sigma * (1.0 + total * (1.0 - sigma))
        gradient = jnp.where(valid, geo.three(cot_ref[...].astype(F32)) * slopes, 0.0)
        g_ref[...] = geo.flat(gradient)
        put_stats(sums_ref, gradient, gradient * ((zc - mean) * inv))

    outputs, g_two, sums = run(
        head_kernel,
        [((rows, wide), BF16), wide_out, stats_wide],
        smem=scalars,
        vmem=(zc_two, stats_c2, params_two[2], sum_one, cot),
    )
    sums_c2 = all_sum(sums)

    def norm_back(gradient, value, coeffs, sums, valid):
        scale, _, mean, inv = coeffs
        crossed = (value - mean) * inv * sums[1] + sums[0]
        return scale * (gradient - jnp.where(valid, crossed, 0.0))

    def expand_back_body(
        meta_ref,
        inv_ref,
        g_ref,
        zc_ref,
        stats_ref,
        sums_ref,
        params_ref,
        zb_ref,
        stats_b_ref,
        params_b_ref,
        fast_ref,
        gz_ref,
        g_out,
        sums_out,
        full,
        top,
        bottom,
        loads,
    ):
        limit = meta_ref[0]
        coeffs = affine(stats_ref, params_ref, inv_ref, slow_wide, 0, wide)
        both = [back_rows(sums_ref, inv_ref, slow_wide, row, 0, wide) for row in range(2)]
        gradient = geo.three(g_ref[...])
        gz = norm_back(
            gradient, geo.three(zc_ref[...]), coeffs, both, mask_groups(gradient.shape, limit)
        )
        gz = geo.flat(gz).astype(BF16)
        gz_ref[...] = gz
        fast = dot_nt(gz[:, slow_wide:], fast_ref[...])
        slow = None
        for block in range(blocks):
            term = dot_nt(gz[:, block * mid : (block + 1) * mid], loads.get(block))
            slow = term if slow is None else slow + term
        scale, shift, mean, inv = affine(stats_b_ref, params_b_ref, inv_ref, mid)
        zb = geo.three(zb_ref[...])
        back = geo.three(jnp.concatenate([slow, fast], axis=1)) * slope(zb * scale + shift)
        g_out[...] = geo.flat(back)
        masked = jnp.where(mask_groups(back.shape, limit), back, 0.0)
        put_stats(sums_out, masked, masked * ((zb - mean) * inv))
        put_messages(jnp.concatenate([back, zb], axis=-1), full, top, bottom)
        return gradient

    messages_back = [
        ((rows, 2 * small), BF16),
        ((half_rows, 2 * small), BF16),
        ((half_rows, 2 * small), BF16),
    ]

    def expand_back_two_kernel(*refs):
        *refs, g_hbm, gz_ref, g_out, sums_out, full, top, bottom, w, sems = refs
        loads = Loads(g_hbm, at_expand_two, w, sems)
        expand_back_body(*refs, gz_ref, g_out, sums_out, full, top, bottom, loads)

    gz_c2, g_b2, sums, *message = run(
        expand_back_two_kernel,
        [((rows, wide), BF16), small_out, stats_small] + messages_back,
        smem=scalars,
        vmem=(
            g_two,
            zc_two,
            stats_c2,
            sums_c2,
            params_two[2],
            zb_two,
            stats_b2,
            params_two[1],
            fast_two[4],
        ),
        hbm=(far,),
        scratch=expand_scratch,
    )
    sums_b2 = all_sum(sums)
    halo_back_two = exchange_halo(*message)

    fast_grads_out = (
        ((3, fast_wide // PHASES, fast_mid), F32),
        ((9, fast_part, fast_mid), F32),
        ((fast_part, fast_wide // PHASES), F32),
    )

    def expand_grad_body(hb_ref, gz_ref, out_ref, fast_out):
        for block in range(blocks):
            value = dot_tn(hb_ref[:, :mid], gz_ref[:, block * mid : (block + 1) * mid])
            out_ref[:, block * depth_mid : (block + 1) * depth_mid, :] = value.astype(
                BF16
            ).reshape(count, depth_mid, mid)
        fast = dot_tn(hb_ref[:, mid:], gz_ref[:, slow_wide:])
        lanes = fast_wide // PHASES
        total = None
        for phase in range(PHASES):
            part = fast[
                phase * fast_part : (phase + 1) * fast_part, phase * lanes : (phase + 1) * lanes
            ]
            total = part if total is None else total + part
        fast_out[...] = total

    expand_grad_outs = [((count, blocks * depth_mid, mid), BF16), fast_grads_out[2]]
    grad_expand_two, fast_expand_grad_two = run(
        expand_grad_body, expand_grad_outs, vmem=(hb_two, gz_c2)
    )

    def space_back_stage(g, zb, za, halo, stats_b, sums_b, params_b, stats_a, params_a, g_hbm, at, fast_w):
        def kernel(
            meta_ref,
            inv_ref,
            g_ref,
            zb_ref,
            za_ref,
            up_ref,
            down_ref,
            side_ref,
            side_up_ref,
            side_down_ref,
            stats_b_ref,
            sums_b_ref,
            params_b_ref,
            stats_a_ref,
            params_a_ref,
            fast_ref,
            weights_ref,
            taps_ref,
            g_out,
            sums_out,
            w,
            sems,
        ):
            loads = Loads(weights_ref, at, w, sems)
            limit = meta_ref[0]
            coeffs = affine(stats_b_ref, params_b_ref, inv_ref, mid)
            both = [back_rows(sums_b_ref, inv_ref, mid, row) for row in range(2)]

            def back(gradient, value, scale):
                valid = mask_groups(gradient.shape, limit, scale)
                return norm_back(gradient, value, coeffs, both, valid)

            def halo_back(ref, scale):
                value = geo.three(ref[...].astype(F32))
                return back(value[..., :small], value[..., small:], scale)

            near_by = Neighbours(
                back(geo.three(g_ref[...]), geo.three(zb_ref[...]), 1),
                halo_back(up_ref, 2),
                halo_back(down_ref, 2),
                halo_back(side_ref, 1),
                halo_back(side_up_ref, 2),
                halo_back(side_down_ref, 2),
                meta_ref,
                geo.width,
            )
            slow = fast = None
            for tap in range(9):
                moved = geo.flat(near_by.at(1 - tap // 3, 1 - tap % 3)).astype(BF16)
                taps_ref[tap] = moved
                slow_term = dot_nt(moved[:, :mid], loads.get(tap))
                fast_term = dot_nt(moved[:, mid:], fast_ref[tap])
                slow = slow_term if slow is None else slow + slow_term
                fast = fast_term if fast is None else fast + fast_term
            scale, shift, mean, inv = affine(stats_a_ref, params_a_ref, inv_ref, mid)
            za = geo.three(za_ref[...])
            result = geo.three(jnp.concatenate([slow, fast], axis=1)) * slope(za * scale + shift)
            g_out[...] = geo.flat(result)
            masked = jnp.where(mask_groups(result.shape, limit), result, 0.0)
            put_stats(sums_out, masked, masked * ((za - mean) * inv))

        taps, g, sums = run(
            kernel,
            [((9, rows, small), BF16), small_out, stats_small],
            smem=scalars,
            vmem=(
                g,
                zb,
                za,
                *halo,
                stats_b,
                sums_b,
                params_b,
                stats_a,
                params_a,
                fast_w,
            ),
            hbm=(g_hbm,),
            scratch=[pltpu.VMEM((9, count, depth_mid, mid), BF16), dma((9,))],
        )
        return taps, g, all_sum(sums)

    def space_grad_kernel(ha_ref, taps_ref, out_ref, fast_out):
        for tap in range(9):
            value = dot_tn(ha_ref[:, :mid], taps_ref[tap, :, :mid])
            out_ref[:, tap * depth_mid : (tap + 1) * depth_mid, :] = value.astype(BF16).reshape(
                count, depth_mid, mid
            )
            fast = dot_tn(ha_ref[:, mid:], taps_ref[tap, :, mid:])
            total = None
            for phase in range(PHASES):
                part = fast[phase * fast_part : (phase + 1) * fast_part]
                part = lane_block(part, phase, fast_part)
                total = part if total is None else total + part
            fast_out[tap] = total

    space_grad_outs = [((count, 9 * depth_mid, mid), BF16), fast_grads_out[1]]
    taps_two, g_a2, sums_a2 = space_back_stage(
        g_b2,
        zb_two,
        za_two,
        halo_back_two,
        stats_b2,
        sums_b2,
        params_two[1],
        stats_a2,
        params_two[0],
        far,
        at_space_two,
        fast_two[3],
    )
    grad_space_two, fast_space_grad_two = run(
        space_grad_kernel, space_grad_outs, vmem=(ha_two, taps_two)
    )

    def reduce_gz(meta_ref, inv_ref, g_ref, za_ref, stats_ref, sums_ref, params_ref, steps_ref):
        coeffs = affine(stats_ref, params_ref, inv_ref, mid)
        both = [back_rows(sums_ref, inv_ref, mid, row) for row in range(2)]
        gradient = geo.three(g_ref[...])
        gz = norm_back(
            gradient,
            geo.three(za_ref[...]),
            coeffs,
            both,
            mask_groups(gradient.shape, meta_ref[0]),
        )
        gz = geo.flat(gz)
        steps = [geo.shift(gz, -1).astype(BF16), gz.astype(BF16), geo.shift(gz, 1).astype(BF16)]
        for tap in range(3):
            steps_ref[tap] = steps[tap]
        return steps

    def reduce_back_two_kernel(
        meta_ref,
        inv_ref,
        g_ref,
        za_ref,
        stats_ref,
        sums_ref,
        params_ref,
        g_two_ref,
        sum_ref,
        zc_ref,
        short_ref,
        stats_c_ref,
        main_ref,
        before_ref,
        after_ref,
        weights_ref,
        steps_ref,
        g_out,
        sums_out,
        w,
        sems,
    ):
        loads = Loads(weights_ref, at_reduce_two, w, sems)
        steps = reduce_gz(
            meta_ref, inv_ref, g_ref, za_ref, stats_ref, sums_ref, params_ref, steps_ref
        )
        slow = None
        for tap in range(3):
            term = dot_nt(steps[tap][:, :mid], loads.get(tap))
            slow = term if slow is None else slow + term
        fast = fast_conv_back(
            [step[:, mid:] for step in steps], main_ref[...], before_ref[...], after_ref[...]
        )
        back = jnp.concatenate([slow, fast], axis=1) + g_two_ref[...]
        back = geo.three(back * slope(sum_ref[...]))
        g_out[...] = geo.flat(back)
        masked = jnp.where(mask_groups(back.shape, meta_ref[0]), back, 0.0)
        mean, inv = moments(stats_c_ref, inv_ref, slow_wide, 0, wide)
        put_stats(sums_out, masked, masked * ((geo.three(zc_ref[...]) - mean) * inv))
        mean, inv = moments(stats_c_ref, inv_ref, slow_wide, wide, wide + slow_wide)
        masked = masked[..., :slow_wide]
        put_stats(sums_out, masked, masked * ((geo.three(short_ref[...]) - mean) * inv), wide)

    steps_two, g_one, sums = run(
        reduce_back_two_kernel,
        [((3, rows, small), BF16), wide_out, stats_both],
        smem=scalars,
        vmem=(
            g_a2,
            za_two,
            stats_a2,
            sums_a2,
            params_two[0],
            g_two,
            sum_one,
            zc_one,
            short,
            stats_c1,
            *fast_two[:3],
        ),
        hbm=(far,),
        scratch=reduce_two_scratch,
    )
    sums_c1 = all_sum(sums)

    def reduce_grad_two_kernel(low_ref, steps_ref, out_ref, fast_out):
        for tap in range(3):
            value = dot_tn(low_ref[:, :slow_wide], steps_ref[tap, :, :mid])
            out_ref[:, tap * depth_two : (tap + 1) * depth_two, :] = value.astype(BF16).reshape(
                count, depth_two, mid
            )
        fast_reduce_grad(
            low_ref[:, slow_wide:], [steps_ref[tap, :, mid:] for tap in range(3)], fast_out
        )

    grad_reduce_two, fast_reduce_grad_two = run(
        reduce_grad_two_kernel,
        [((count, 3 * depth_two, mid), BF16), fast_grads_out[0]],
        vmem=(low_one, steps_two),
    )
    fast_rows_two = fast_grad_rows(
        (fast_reduce_grad_two, fast_space_grad_two, fast_expand_grad_two), count, mid
    )
    total_two = reduce_rows([grad_reduce_two, grad_space_two, grad_expand_two, fast_rows_two])

    def make_expand_back_one():
        def kernel(*refs):
            body = refs[:11]
            short_ref, short_params_ref, g_hbm = refs[11:14]
            gz_ref, g_out, sums_out, full, top, bottom, gs_ref, w, sems = refs[14:]
            loads = Loads(g_hbm, 0, w, sems)
            gradient = expand_back_body(
                *body, gz_ref, g_out, sums_out, full, top, bottom, loads
            )
            meta_ref, inv_ref, stats_ref, sums_ref = body[0], body[1], body[4], body[5]
            low, high = wide, wide + slow_wide
            coeffs = affine(stats_ref, short_params_ref, inv_ref, slow_wide, low, high)
            both = [
                back_rows(sums_ref, inv_ref, slow_wide, 0, 0, slow_wide),
                back_rows(sums_ref, inv_ref, slow_wide, 1, low, high),
            ]
            gradient = gradient[..., :slow_wide]
            valid = mask_groups(gradient.shape, meta_ref[0])
            gs = norm_back(gradient, geo.three(short_ref[...]), coeffs, both, valid)
            gs_ref[...] = geo.flat(gs).astype(BF16)

        return kernel

    gz_c1, g_b1, sums, top_full, top_top, top_bottom, gz_short = run(
        make_expand_back_one(),
        [((rows, wide), BF16), small_out, stats_small]
        + messages_back
        + [((rows, slow_wide), BF16)],
        smem=scalars,
        vmem=(
            g_one,
            zc_one,
            stats_c1,
            sums_c1,
            params_one[2],
            zb_one,
            stats_b1,
            params_one[1],
            fast_one[4],
            short,
            params_short,
        ),
        hbm=(far,),
        scratch=expand_scratch,
    )
    sums_b1 = all_sum(sums)
    halo_back_one = exchange_halo(top_full, top_top, top_bottom)
    grad_expand_one, fast_expand_grad_one = run(
        expand_grad_body, expand_grad_outs, vmem=(hb_one, gz_c1)
    )
    joined_lanes = slow_wide + lat

    def short_back_kernel(x_ref, united_ref, gs_ref, g_hbm, grad_ref, back_ref, w, sems):
        loads = Loads(g_hbm, at_short, w, sems)
        for block in range(blocks):
            gs = gs_ref[:, block * mid : (block + 1) * mid]
            value = jnp.concatenate([dot_tn(x_ref[...], gs), dot_tn(united_ref[...], gs)], axis=0)
            grad_ref[:, block * depth_one : (block + 1) * depth_one, :] = value.astype(
                BF16
            ).reshape(count, depth_one, mid)
            term = dot_nt(gs, loads.get(block))
            back_ref[...] = term if block == 0 else back_ref[...] + term

    grad_short, short_back = run(
        short_back_kernel,
        [((count, blocks * depth_one, mid), BF16), ((rows, joined_lanes), F32)],
        vmem=(slow_x, united, gz_short),
        hbm=(far,),
        scratch=[pltpu.VMEM((blocks, count, depth_one, mid), BF16), dma((blocks,))],
    )
    total_mid = reduce_rows([grad_short, grad_expand_one])

    taps_one, g_a1, sums_a1 = space_back_stage(
        g_b1,
        zb_one,
        za_one,
        halo_back_one,
        stats_b1,
        sums_b1,
        params_one[1],
        stats_a1,
        params_one[0],
        near,
        at_space_one,
        fast_one[3],
    )
    grad_space_one, fast_space_grad_one = run(
        space_grad_kernel, space_grad_outs, vmem=(ha_one, taps_one)
    )

    def last_kernel(
        meta_ref,
        inv_ref,
        g_ref,
        za_ref,
        stats_ref,
        sums_ref,
        params_ref,
        g_one_ref,
        short_ref,
        lateral_ref,
        main_ref,
        before_ref,
        after_ref,
        weights_ref,
        steps_ref,
        slow_ref,
        fast_ref,
        united_ref,
        w,
        sems,
    ):
        loads = Loads(weights_ref, 0, w, sems)
        steps = reduce_gz(
            meta_ref, inv_ref, g_ref, za_ref, stats_ref, sums_ref, params_ref, steps_ref
        )
        joined = short_ref[...]
        for tap in range(3):
            joined = joined + dot_nt(steps[tap][:, :mid], loads.get(tap))
        slow_ref[...] = joined[:, :slow_wide]
        tail = joined[:, slow_wide:]
        now, past = tail.astype(BF16), geo.shift(tail, -1).astype(BF16)
        united_ref[0] = now
        united_ref[1] = past
        lanes = fast_wide // PHASES
        fast = fast_conv_back(
            [step[:, mid:] for step in steps], main_ref[...], before_ref[...], after_ref[...]
        )
        fast = fast + g_one_ref[:, slow_wide:]
        front = dot_nt(now, lateral_ref[2:5].reshape(3 * lanes, lat))
        back = dot_nt(past, lateral_ref[0:2].reshape(2 * lanes, lat))
        fast_ref[:, : 2 * lanes] = fast[:, : 2 * lanes] + front[:, : 2 * lanes]
        fast_ref[:, 2 * lanes : 3 * lanes] = (
            fast[:, 2 * lanes : 3 * lanes] + front[:, 2 * lanes :] + back[:, :lanes]
        )
        fast_ref[:, 3 * lanes :] = fast[:, 3 * lanes :] + back[:, lanes:]

    steps_one, grad_slow, grad_fast, united_low = run(
        last_kernel,
        [
            ((3, rows, small), BF16),
            ((rows, slow_wide), F32),
            ((rows, fast_wide), F32),
            ((2, rows, lat), BF16),
        ],
        smem=scalars,
        vmem=(
            g_a1,
            za_one,
            stats_a1,
            sums_a1,
            params_one[0],
            g_one,
            short_back,
            lateral,
            *fast_one[:3],
        ),
        hbm=(near,),
        scratch=[pltpu.VMEM((3, count, depth_one, mid), BF16), dma((3,))],
    )

    def last_grad_kernel(
        x_ref, united_ref, fast_x_ref, steps_ref, low_ref, out_ref, lat_ref, fast_out
    ):
        lanes = fast_wide // PHASES
        for tap in range(3):
            step = steps_ref[tap, :, :mid]
            value = jnp.concatenate(
                [dot_tn(x_ref[...], step), dot_tn(united_ref[...], step)], axis=0
            )
            out_ref[:, tap * depth_one : (tap + 1) * depth_one, :] = value.astype(BF16).reshape(
                count, depth_one, mid
            )
        past = dot_tn(fast_x_ref[:, 2 * lanes :], low_ref[1])
        now = dot_tn(fast_x_ref[:, : 3 * lanes], low_ref[0])
        both = jnp.concatenate([past, now], axis=0).astype(BF16)
        for tap in range(5):
            lat_ref[:, tap * depth_lat : (tap + 1) * depth_lat, :] = both[
                tap * lanes : (tap + 1) * lanes
            ].reshape(count, depth_lat, lat)
        fast_reduce_grad(
            fast_x_ref[...], [steps_ref[tap, :, mid:] for tap in range(3)], fast_out
        )

    grad_reduce_one, grad_lat, fast_reduce_grad_one = run(
        last_grad_kernel,
        [
            ((count, 3 * depth_one, mid), BF16),
            ((count, 5 * depth_lat, lat), BF16),
            fast_grads_out[0],
        ],
        vmem=(slow_x, united, fast_x, steps_one, united_low),
    )
    fast_rows_one = fast_grad_rows(
        (fast_reduce_grad_one, fast_space_grad_one, fast_expand_grad_one), count, mid
    )
    total_one = reduce_rows([grad_reduce_one, grad_lat, grad_space_one, fast_rows_one])

    at = 3 * depth_two
    grad_slow_reduce_two = total_two[:at].reshape(slow_reduce_two.shape)
    grad_slow_spatial_two = total_two[at : at + 9 * depth_mid].reshape(slow_spatial_two.shape)
    at += 9 * depth_mid
    grad_slow_expand_two = uncolumns(total_two[at : at + blocks * depth_mid], depth_mid)
    at += blocks * depth_mid
    fast_two_grads = fast_grad_shards(total_two[at:], *fast_shards_two)
    at = blocks * depth_one
    grad_slow_shortcut = uncolumns(total_mid[:at], depth_one)
    grad_slow_expand_one = uncolumns(total_mid[at:], depth_mid)
    at = 3 * depth_one
    grad_slow_reduce_one = total_one[:at].reshape(slow_reduce_one.shape)
    grad_lateral = total_one[at : at + 5 * depth_lat].reshape(lateral_weight.shape)
    at += 5 * depth_lat
    grad_slow_spatial_one = total_one[at : at + 9 * depth_mid].reshape(slow_spatial_one.shape)
    at += 9 * depth_mid
    fast_one_grads = fast_grad_shards(total_one[at:], *fast_shards_one)

    def norm_grads(first, second, third):
        slow = [first[:, :mid], second[:, :mid], third[:, :slow_wide]]
        fast = [first[:, mid:], second[:, mid:], third[:, slow_wide:wide]]
        fast = [jnp.sum(part.reshape(2, PHASES, -1), axis=1) for part in fast]
        return slow, fast

    slow_one_p, fast_one_p = norm_grads(sums_a1, sums_b1, sums_c1)
    slow_two_p, fast_two_p = norm_grads(sums_a2, sums_b2, sums_c2)
    grad_slow_norms_one = jnp.concatenate(slow_one_p + [sums_c1[:, wide:]], axis=1)[::-1]
    grad_slow_norms_two = jnp.concatenate(slow_two_p, axis=1)[::-1]
    grad_fast_norms_one = jnp.concatenate(fast_one_p, axis=1)[::-1]
    grad_fast_norms_two = jnp.concatenate(fast_two_p, axis=1)[::-1]
    return (
        outputs[:, :slow_wide].reshape(slow_input.shape),
        join_phases(outputs[:, slow_wide:], fast_input.shape),
        grad_slow.reshape(slow_input.shape),
        join_phases(grad_fast, fast_input.shape),
        grad_lateral,
        grad_slow_reduce_one,
        grad_slow_spatial_one,
        grad_slow_expand_one,
        grad_slow_shortcut,
        *fast_one_grads,
        grad_slow_reduce_two,
        grad_slow_spatial_two,
        grad_slow_expand_two,
        *fast_two_grads,
        grad_slow_norms_one,
        grad_fast_norms_one,
        grad_slow_norms_two,
        grad_fast_norms_two,
    )


def solution(mesh):
    in_specs = (
        P("clips", None, "ha", "wa", None),
        P("clips", None, "ha", "wa", None),
        P("clips", None, "ha", "wa", None),
        P("clips", None, "ha", "wa", None),
        P("clips"),
        P(None, ("ha", "wa"), None),
        P(None, ("ha", "wa"), None),
        P(None, None, ("ha", "wa"), None),
        P(("ha", "wa"), None),
        P(("ha", "wa"), None),
        P(None, ("ha", "wa"), None),
        P(None, None, ("ha", "wa"), None),
        P(("ha", "wa"), None),
        P(None, ("ha", "wa"), None),
        P(None, None, ("ha", "wa"), None),
        P(("ha", "wa"), None),
        P(None, ("ha", "wa"), None),
        P(None, None, ("ha", "wa"), None),
        P(("ha", "wa"), None),
        P(),
        P(),
        P(),
        P(),
    )
    out_specs = (
        P("clips", None, "ha", "wa", None),
        P("clips", None, "ha", "wa", None),
        P("clips", None, "ha", "wa", None),
        P("clips", None, "ha", "wa", None),
        P(None, ("ha", "wa"), None),
        P(None, ("ha", "wa"), None),
        P(None, None, ("ha", "wa"), None),
        P(("ha", "wa"), None),
        P(("ha", "wa"), None),
        P(None, ("ha", "wa"), None),
        P(None, None, ("ha", "wa"), None),
        P(("ha", "wa"), None),
        P(None, ("ha", "wa"), None),
        P(None, None, ("ha", "wa"), None),
        P(("ha", "wa"), None),
        P(None, ("ha", "wa"), None),
        P(None, None, ("ha", "wa"), None),
        P(("ha", "wa"), None),
        P(),
        P(),
        P(),
        P(),
    )
    return jax.shard_map(
        on_device, mesh=mesh, in_specs=in_specs, out_specs=out_specs, check_vma=False
    )
```

```python
import jax
import jax.numpy as jnp
from jax import lax
from jax.experimental import pallas as pl
from jax.experimental.pallas import tpu as pltpu
from jax.sharding import PartitionSpec as P

epsilon = 1e-05
F32 = jnp.float32
BF16 = jnp.bfloat16
TILE = ("ha", "wa")
PHASES = 4
SUB = 8


def dot(left, right):
    return lax.dot_general(left, right, (((1,), (0,)), ((), ())), preferred_element_type=F32)


def dot_tn(left, right):
    return lax.dot_general(left, right, (((0,), (0,)), ((), ())), preferred_element_type=F32)


def dot_nt(left, right):
    return lax.dot_general(left, right, (((1,), (1,)), ((), ())), preferred_element_type=F32)


class Loads:
    def __init__(self, source, offset, target, sems, first):
        self.copies = []
        depth = target.shape[2]
        for step in range(target.shape[0]):
            copy = pltpu.make_async_copy(
                source.at[:, pl.ds(offset + step * depth, depth), :],
                target.at[step],
                sems.at[first + step],
            )
            copy.start()
            self.copies.append(copy)
        self.target = target

    def get(self, step):
        self.copies[step].wait()
        block = self.target[step]
        return block.reshape(-1, block.shape[-1])


class Store:
    def __init__(self, scratch, target, sem):
        self.scratch, self.sent = scratch, False
        self.copy = pltpu.make_async_copy(scratch, target, sem)

    def send(self):
        self.copy.start()
        self.sent = True

    def __setitem__(self, index, value):
        self.scratch[index] = value

    def __getitem__(self, index):
        return self.scratch[index]


def run(body, outs, smem=(), vmem=(), saved=(), weights=(), limit=40):
    near = pl.BlockSpec(memory_space=pltpu.VMEM)
    far = pl.BlockSpec(memory_space=pltpu.HBM)
    sources = []
    for array, *_ in weights:
        if not any(array is other for other in sources):
            sources.append(array)
    stored = [kept for _, _, kept in outs]
    scratch = [pltpu.VMEM(array.shape, array.dtype) for array in saved]
    for array, _, steps, depth in weights:
        scratch.append(pltpu.VMEM((steps, array.shape[0], depth, array.shape[2]), array.dtype))
    scratch += [pltpu.VMEM(shape, kind) for shape, kind, kept in outs if kept]
    sems = len(saved) + sum(steps for _, _, steps, _ in weights) + sum(stored)
    scratch.append(pltpu.SemaphoreType.DMA((max(sems, 1),)))

    def kernel(*refs):
        refs = list(refs)
        sem = refs.pop()

        def take(number):
            taken = refs[:number]
            del refs[:number]
            return taken

        smem_refs, vmem_refs, saved_refs = take(len(smem)), take(len(vmem)), take(len(saved))
        source_refs, out_refs = take(len(sources)), take(len(outs))
        saved_scratch, weight_scratch = take(len(saved)), take(len(weights))
        copies = []
        for at, (source, target) in enumerate(zip(saved_refs, saved_scratch)):
            copy = pltpu.make_async_copy(source, target, sem.at[at])
            copy.start()
            copies.append(copy)
        at = len(saved)
        loads = []
        for (array, offset, steps, _), target in zip(weights, weight_scratch):
            place = [array is other for other in sources].index(True)
            loads.append(Loads(source_refs[place], offset, target, sem, at))
            at += steps
        results = []
        stores = []
        for ref, kept in zip(out_refs, stored):
            if kept:
                stores.append(Store(refs[len(stores)], ref, sem.at[at]))
                at += 1
                results.append(stores[-1])
            else:
                results.append(ref)
        for copy in copies:
            copy.wait()
        body(*smem_refs, *vmem_refs, *saved_scratch, *loads, *results)
        for store in stores:
            if not store.sent:
                store.send()
        for store in stores:
            store.copy.wait()

    return pl.pallas_call(
        kernel,
        out_shape=[jax.ShapeDtypeStruct(shape, kind) for shape, kind, _ in outs],
        in_specs=[pl.BlockSpec(memory_space=pltpu.SMEM)] * len(smem)
        + [near] * len(vmem)
        + [far] * (len(saved) + len(sources)),
        out_specs=[far if kept else near for kept in stored],
        scratch_shapes=scratch,
        compiler_params=pltpu.CompilerParams(vmem_limit_bytes=limit * 1024 * 1024),
    )(*smem, *vmem, *saved, *sources)


class Geometry:
    def __init__(self, slow_shape, fast_shape):
        self.cap, self.frames, self.height, self.width = slow_shape[:4]
        self.groups = self.cap * self.frames
        self.rows = self.groups * SUB

    def three(self, value):
        return value.reshape(-1, SUB, value.shape[-1])

    def flat(self, value):
        return value.reshape(-1, value.shape[-1])

    def shift(self, value, step):
        lanes = value.shape[-1]
        whole = value.reshape(self.cap, self.frames, SUB, lanes)
        zero = jnp.zeros((self.cap, 1, SUB, lanes), value.dtype)
        if step > 0:
            whole = jnp.concatenate([zero, whole[:, :-1]], axis=1)
        else:
            whole = jnp.concatenate([whole[:, 1:], zero], axis=1)
        return whole.reshape(-1, lanes)


def mask_groups(shape, limit, scale=1):
    return lax.broadcasted_iota(jnp.int32, shape, 0) * scale < limit


def rep(ref, row, low, high):
    return jnp.broadcast_to(ref[row : row + 1, low:high], (SUB, high - low))


def fold(value, slow):
    fast = value[:, slow:]
    lanes = fast.shape[-1]
    part = lanes // PHASES
    if part % 128 == 0:
        total = fast[:, :part]
        for phase in range(1, PHASES):
            total = total + fast[:, phase * part : (phase + 1) * part]
        return jnp.concatenate([value[:, :slow]] + [total] * PHASES, axis=1)
    total = fast
    for phase in range(1, PHASES):
        total = total + pltpu.roll(fast, phase * part, 1)
    return jnp.concatenate([value[:, :slow], total], axis=1)


def lane_counts(inv_ref, lanes, slow):
    lane = lax.broadcasted_iota(jnp.int32, (SUB, lanes), 1)
    return jnp.where(lane < slow, inv_ref[0], inv_ref[1])


def moments(stats, inv_ref, slow, low=0, high=None):
    high = stats.shape[1] if high is None else high
    total, square = rep(stats, 0, low, high), rep(stats, 1, low, high)
    if slow < high - low:
        total, square = fold(total, slow), fold(square, slow)
    inv_n = lane_counts(inv_ref, high - low, slow)
    mean = total * inv_n
    return mean, lax.rsqrt(square * inv_n - mean * mean + epsilon)


def affine(stats, params, inv_ref, slow, low=0, high=None):
    mean, inv = moments(stats, inv_ref, slow, low, high)
    lanes = mean.shape[1]
    scale = (1.0 + rep(params, 0, 0, lanes)) * inv
    return scale, rep(params, 1, 0, lanes) - mean * scale, mean, inv


def back_rows(sums, inv_ref, slow, row, low=0, high=None):
    high = sums.shape[1] if high is None else high
    total = rep(sums, row, low, high)
    if slow < high - low:
        total = fold(total, slow)
    return total * lane_counts(inv_ref, high - low, slow)


def silu(value):
    return value * jax.nn.sigmoid(value)


def slope(value):
    sigma = jax.nn.sigmoid(value)
    return sigma * (1.0 + value * (1.0 - sigma))


def put_stats(ref, first, second, low=0):
    lanes = first.shape[-1]
    ref[0:1, low : low + lanes] = jnp.sum(jnp.sum(first, axis=0), axis=0, keepdims=True)
    ref[1:2, low : low + lanes] = jnp.sum(jnp.sum(second, axis=0), axis=0, keepdims=True)


def put_back(ref, gradient, normal, low=0):
    put_stats(ref, gradient * normal, gradient, low)


def put_forward(ref, value, limit, low=0):
    masked = jnp.where(mask_groups(value.shape, limit), value, 0.0)
    put_stats(ref, masked, masked * value, low)


def put_message(value, ref):
    lanes = value.shape[-1]
    pairs = value.reshape(-1, 2, SUB, lanes)
    first, second = pairs[:, 0], pairs[:, 1]
    near = lax.broadcasted_iota(jnp.int32, first.shape, 1) < SUB // 2
    top = jnp.where(near, first, pltpu.roll(second, SUB // 2, 1))
    bottom = jnp.where(near, pltpu.roll(first, SUB // 2, 1), second)
    parts = [part.reshape(-1, lanes).astype(BF16) for part in (value, top, bottom)]
    at = 0
    for part in parts:
        ref[at : at + part.shape[0]] = part
        at += part.shape[0]


def unpack_bottom(value):
    both = jnp.stack([pltpu.roll(value, SUB // 2, 1), value], axis=1)
    return both.reshape(-1, SUB, value.shape[-1])


def unpack_top(value):
    both = jnp.stack([value, pltpu.roll(value, SUB // 2, 1)], axis=1)
    return both.reshape(-1, SUB, value.shape[-1])


class Neighbours:
    def __init__(self, own, up, down, side, side_up, side_down, meta, width):
        half = SUB // 2
        row = lax.broadcasted_iota(jnp.int32, own.shape, 1)
        near = row < half
        self.col = row % width
        self.width = width
        ha, wa, last = meta[1], meta[2], meta[3]
        up = unpack_bottom(jnp.where(ha > 0, up, 0.0))
        side_up = unpack_bottom(jnp.where(ha > 0, side_up, 0.0))
        down = unpack_top(jnp.where(ha < last, down, 0.0))
        side_down = unpack_top(jnp.where(ha < last, side_down, 0.0))
        self.rows = {
            0: own,
            -1: pltpu.roll(jnp.where(near, own, up), half, 1),
            1: pltpu.roll(jnp.where(near, down, own), half, 1),
        }
        sides = {
            0: pltpu.roll(side, half, 1),
            -1: jnp.where(near, side, side_up),
            1: jnp.where(near, side_down, side),
        }
        self.left = {key: jnp.where(wa > 0, value, 0.0) for key, value in sides.items()}
        self.right = {key: jnp.where(wa > 0, 0.0, value) for key, value in sides.items()}

    def at(self, row_step, col_step):
        base = self.rows[row_step]
        if col_step < 0:
            return pltpu.roll(
                jnp.where(self.col == self.width - 1, self.left[row_step], base), 1, 1
            )
        if col_step > 0:
            return pltpu.roll(jnp.where(self.col == 0, self.right[row_step], base), SUB - 1, 1)
        return base


def xor_pairs(size, step):
    return [(index, index ^ step) for index in range(size)]


def direct_sum(value, axis):
    size = lax.axis_size(axis)
    step = 1
    while step < size:
        if size // step >= 4:
            one, two, three = [
                lax.ppermute(value, axis, xor_pairs(size, step * times)) for times in (1, 2, 3)
            ]
            value = (value + two) + (one + three)
            step *= 4
        else:
            value = value + lax.ppermute(value, axis, xor_pairs(size, step))
            step *= 2
    return value


def all_sum(value):
    for axis in ("wa", "ha", "clips"):
        value = direct_sum(value, axis)
    return value


def sum_with_halo(stats, message, rows):
    wide, high = lax.axis_size("wa"), lax.axis_size("ha")
    side = lax.ppermute(message, "wa", xor_pairs(wide, 1))
    stats = direct_sum(stats, "wa")
    half = rows // 2
    tops = jnp.concatenate([message[rows : rows + half], side[rows : rows + half]], axis=0)
    bottoms = jnp.concatenate([message[rows + half :], side[rows + half :]], axis=0)
    up = lax.ppermute(bottoms, "ha", [(row, row + 1) for row in range(high - 1)])
    down = lax.ppermute(tops, "ha", [(row + 1, row) for row in range(high - 1)])
    stats = direct_sum(stats, "ha")
    stats, up, down = lax.optimization_barrier((stats, up, down))
    return direct_sum(stats, "clips"), (side, up, down)


def time_conv(geo, parts, blocks):
    result = None
    for tap in range(3):
        at = 0
        total = None
        for part in parts:
            lanes = part.shape[-1]
            term = dot(part, blocks[tap][at : at + lanes])
            at += lanes
            total = term if total is None else total + term
        if tap != 1:
            total = geo.shift(total, 1 - tap)
        result = total if result is None else result + total
    return result


def fast_conv(geo, value, main, before, after):
    lanes = value.shape[-1] // PHASES
    result = dot(value, main)
    result = result + geo.shift(dot(value[:, -lanes:], before), 1)
    return result + geo.shift(dot(value[:, :lanes], after), -1)


def fast_conv_back(steps, main, before, after):
    lanes = before.shape[0]
    middle = dot_nt(steps[1], main)
    first = middle[:, :lanes] + dot_nt(steps[2], after)
    last = middle[:, -lanes:] + dot_nt(steps[0], before)
    return jnp.concatenate([first, middle[:, lanes:-lanes], last], axis=1)


def lane_block(value, phase, part):
    return pltpu.roll(value, value.shape[-1] - phase * part, 1) if phase else value


def fast_reduce_grad(value, steps):
    lanes = value.shape[-1] // PHASES
    part = steps[1].shape[-1] // PHASES
    main = dot_tn(value, steps[1])
    before = dot_tn(value[:, -lanes:], steps[0])
    after = dot_tn(value[:, :lanes], steps[2])

    def block(row, col):
        return lane_block(main[row * lanes : (row + 1) * lanes], col, part)

    result = []
    for tap in range(3):
        total = before if tap == 0 else None
        if tap == 2:
            total = lane_block(after, PHASES - 1, part)
        for col in range(PHASES):
            row = col + tap - 1
            if 0 <= row < PHASES:
                total = block(row, col) if total is None else total + block(row, col)
        result.append(total)
    return result


def gather_pack(parts):
    return lax.all_gather(jnp.concatenate(parts, axis=0), TILE, axis=0)


def columns(shard, lanes):
    depth, total = shard.shape
    return jnp.moveaxis(shard.reshape(depth, total // lanes, lanes), 1, 0).reshape(-1, lanes)


def uncolumns(rows, depth):
    lanes = rows.shape[-1]
    return jnp.moveaxis(rows.reshape(-1, depth, lanes), 0, 1).reshape(depth, -1)


def split_phases(value):
    cap, frames, height, width, lanes = value.shape
    value = value.reshape(cap, frames // PHASES, PHASES, height, width, lanes)
    return jnp.moveaxis(value, 2, 4).reshape(-1, PHASES * lanes)


def join_phases(value, shape):
    cap, frames, height, width, lanes = shape
    value = value.reshape(cap, frames // PHASES, height, width, PHASES, lanes)
    return jnp.moveaxis(value, 4, 2).reshape(shape)


def fast_gather(shards_one, shards_two):
    rows = []
    lanes = shards_one[2].shape[-1]
    kinds = [jnp.stack(pair) for pair in zip(shards_one, shards_two)]
    for kind in kinds:
        flat = kind.reshape(-1, kind.shape[-1])
        rows.append(jnp.pad(flat, ((0, 0), (0, lanes - flat.shape[-1]))))
    packed = gather_pack(rows)
    result = []
    at = 0
    for kind in kinds:
        depth, width = kind.shape[-2:]
        number = kind.size // width
        part = packed[:, at : at + number, :width].reshape(packed.shape[0], -1, depth, width)
        at += number
        result.append(jnp.moveaxis(part, 0, 1).reshape(part.shape[1], -1, width))
    return result


def prepare_kernel(taps_ref, space_ref, wide_ref, *outs):
    part = taps_ref.shape[-1]
    for layer in range(2):
        main, before, after, space, wide = outs[5 * layer : 5 * layer + 5]
        taps = [taps_ref[3 * layer + tap] for tap in range(3)]
        zero = jnp.zeros_like(taps[0])
        lanes = taps[0].shape[0]
        for row in range(PHASES):
            blocks = [
                taps[row - col + 1] if abs(row - col) <= 1 else zero for col in range(PHASES)
            ]
            main[row * lanes : (row + 1) * lanes, :] = jnp.concatenate(blocks, axis=1)
        before[...] = jnp.concatenate([taps[0]] + [zero] * (PHASES - 1), axis=1)
        after[...] = jnp.concatenate([zero] * (PHASES - 1) + [taps[2]], axis=1)
        for tap in range(9):
            block = space_ref[9 * layer + tap]
            none = jnp.zeros_like(block)
            for row in range(PHASES):
                blocks = [block if row == col else none for col in range(PHASES)]
                space[tap, row * part : (row + 1) * part, :] = jnp.concatenate(blocks, axis=1)
        block = wide_ref[layer]
        none = jnp.zeros_like(block)
        for row in range(PHASES):
            blocks = [block if row == col else none for col in range(PHASES)]
            wide[row * part : (row + 1) * part, :] = jnp.concatenate(blocks, axis=1)


def scatter_rows(packed):
    count, rows, lanes = packed.shape
    clips = lax.axis_size("clips")
    short = -rows % clips
    if short:
        packed = jnp.pad(packed, ((0, 0), (0, short), (0, 0)))
    packed = packed.reshape(count * clips, -1, lanes)
    return lax.psum_scatter(packed, TILE + ("clips",), scatter_dimension=0, tiled=False)


def join_rows(part):
    whole = lax.all_gather(part, "clips", axis=0)
    return whole.reshape(-1, part.shape[-1]).astype(F32)


def on_device(
    slow_input,
    fast_input,
    slow_cotangent,
    fast_cotangent,
    clip_counts,
    lateral_weight,
    slow_reduce_one,
    slow_spatial_one,
    slow_expand_one,
    slow_shortcut_one,
    fast_reduce_one,
    fast_spatial_one,
    fast_expand_one,
    slow_reduce_two,
    slow_spatial_two,
    slow_expand_two,
    fast_reduce_two,
    fast_spatial_two,
    fast_expand_two,
    slow_norms_one,
    fast_norms_one,
    slow_norms_two,
    fast_norms_two,
):
    geo = Geometry(slow_input.shape, fast_input.shape)
    rows, groups = geo.rows, geo.groups
    half_rows = rows // 2
    count = lax.axis_size("ha") * lax.axis_size("wa")
    slow_wide = slow_input.shape[-1]
    fast_wide = PHASES * fast_input.shape[-1]
    wide = slow_wide + fast_wide
    mid = slow_reduce_one.shape[-1]
    fast_part = fast_reduce_one.shape[-1]
    fast_mid = PHASES * fast_part
    small = mid + fast_mid
    lat = lateral_weight.shape[-1]
    blocks = slow_wide // mid

    depth_one = slow_reduce_one.shape[1]
    depth_two = slow_reduce_two.shape[1]
    depth_mid = slow_spatial_one.shape[2]
    depth_lat = lateral_weight.shape[1]
    near = gather_pack([slow_reduce_one.reshape(-1, mid), slow_spatial_one.reshape(-1, mid)])
    far = gather_pack(
        [
            columns(slow_expand_one, mid),
            columns(slow_shortcut_one, mid),
            slow_reduce_two.reshape(-1, mid),
            slow_spatial_two.reshape(-1, mid),
            columns(slow_expand_two, mid),
        ]
    )
    at_space_one = 3 * depth_one
    at_short = blocks * depth_mid
    at_reduce_two = at_short + blocks * depth_one
    at_space_two = at_reduce_two + 3 * depth_two
    at_expand_two = at_space_two + 9 * depth_mid
    lateral = lax.all_gather(lateral_weight, TILE, axis=1, tiled=True)
    fast_shards_one = (fast_reduce_one, fast_spatial_one, fast_expand_one)
    fast_shards_two = (fast_reduce_two, fast_spatial_two, fast_expand_two)
    compact = fast_gather(fast_shards_one, fast_shards_two)
    structured = [
        ((fast_wide, fast_mid), BF16, True),
        ((fast_wide // PHASES, fast_mid), BF16, True),
        ((fast_wide // PHASES, fast_mid), BF16, True),
        ((9, fast_mid, fast_mid), BF16, True),
        ((fast_mid, fast_wide), BF16, True),
    ]
    prepared = run(prepare_kernel, structured * 2, vmem=compact)
    fast_one, fast_two = prepared[:5], prepared[5:]

    held = clip_counts[0]
    clips = direct_sum(jnp.full((1, 128), held, F32), "clips")[0, 0]
    positions = clips * (SUB * geo.frames * count)
    inv_n = jnp.stack([1.0 / positions, 1.0 / (positions * PHASES)])
    ha, wa = lax.axis_index("ha"), lax.axis_index("wa")
    meta = jnp.stack([held * geo.frames, ha, wa, jnp.full_like(ha, lax.axis_size("ha") - 1)])
    scalars = (meta, inv_n)

    def joint(slow_p, fast_p):
        ends = (mid, 2 * mid, 2 * mid + slow_wide)
        fast_ends = (fast_part, 2 * fast_part, 2 * fast_part + fast_wide // PHASES)
        result = []
        at = fast_at = 0
        for end, fast_end in zip(ends, fast_ends):
            fast = jnp.tile(fast_p[:, fast_at:fast_end], (1, PHASES))
            result.append(jnp.concatenate([slow_p[:, at:end], fast], axis=1))
            at, fast_at = end, fast_end
        return result

    params_one = joint(slow_norms_one, fast_norms_one)
    params_two = joint(slow_norms_two, fast_norms_two)
    params_short = slow_norms_one[:, 2 * mid + slow_wide :]

    slow_x = slow_input.reshape(rows, slow_wide)
    fast_x = split_phases(fast_input)
    cot = jnp.concatenate(
        [slow_cotangent.reshape(rows, slow_wide), split_phases(fast_cotangent)], axis=1
    )
    message_out = ((2 * rows, small), BF16, False)
    stats_small = ((2, small), F32, False)
    stats_wide = ((2, wide), F32, False)
    stats_both = ((2, wide + slow_wide), F32, False)
    small_out = ((rows, small), F32, True)
    wide_out = ((rows, wide), F32, True)

    def lateral_kernel(x_ref, k_ref, main_ref, before_ref, after_ref, united_ref, fast_ref):
        lanes = x_ref.shape[1] // PHASES
        x = x_ref[...]
        main = dot(x[:, : 3 * lanes], k_ref[2:5].reshape(3 * lanes, lat))
        past = dot(x[:, 2 * lanes :], k_ref[0:2].reshape(2 * lanes, lat))
        united_ref[...] = (main + geo.shift(past, 1)).astype(BF16)
        fast_ref[...] = fast_conv(geo, x, main_ref[...], before_ref[...], after_ref[...])

    united, za_fast = run(
        lateral_kernel,
        [((rows, lat), BF16, True), ((rows, fast_mid), F32, True)],
        saved=(fast_x, lateral, *fast_one[:3]),
    )

    def reduce_one_kernel(
        meta_ref, x_ref, united_ref, fast_ref, loads, za_ref, stats_ref, message_ref
    ):
        weights = [loads.get(tap) for tap in range(3)]
        za = time_conv(geo, (x_ref[...], united_ref[...]), weights)
        za = jnp.concatenate([za, fast_ref[...]], axis=1)
        za_ref[...] = za
        za_ref.send()
        za = geo.three(za)
        put_forward(stats_ref, za, meta_ref[0])
        put_message(za, message_ref)

    za_one, stats, message = run(
        reduce_one_kernel,
        [small_out, stats_small, message_out],
        smem=(meta,),
        saved=(slow_x, united, za_fast),
        weights=((near, 0, 3, depth_one),),
    )
    stats_a1, halo_one = sum_with_halo(stats, message, rows)

    def space_stage(za, stats_a, halo, params, gathered, offset, fast_w):
        def kernel(
            meta_ref,
            inv_ref,
            side_ref,
            up_ref,
            down_ref,
            stats_ref,
            za_ref,
            params_ref,
            fast_ref,
            loads,
            zb_ref,
            hidden_ref,
            out_stats,
        ):
            scale, shift, _, _ = affine(stats_ref, params_ref, inv_ref, mid)

            def act(value):
                return silu(geo.three(value.astype(F32)) * scale + shift)

            own = act(za_ref[...])
            hidden_ref[...] = geo.flat(own).astype(BF16)
            near_by = Neighbours(
                own,
                act(up_ref[:half_rows]),
                act(down_ref[:half_rows]),
                act(side_ref[:rows]),
                act(up_ref[half_rows:]),
                act(down_ref[half_rows:]),
                meta_ref,
                geo.width,
            )
            slow = fast = None
            for tap in range(9):
                moved = geo.flat(near_by.at(tap // 3 - 1, tap % 3 - 1)).astype(BF16)
                slow_term = dot(moved[:, :mid], loads.get(tap))
                fast_term = dot(moved[:, mid:], fast_ref[tap])
                slow = slow_term if slow is None else slow + slow_term
                fast = fast_term if fast is None else fast + fast_term
            zb = jnp.concatenate([slow, fast], axis=1)
            zb_ref[...] = zb
            zb_ref.send()
            put_forward(out_stats, geo.three(zb), meta_ref[0])

        zb, hidden, stats = run(
            kernel,
            [small_out, ((rows, small), BF16, True), stats_small],
            smem=scalars,
            vmem=(*halo, stats_a),
            saved=(za, params, fast_w),
            weights=((gathered, offset, 9, depth_mid),),
        )
        return zb, hidden, all_sum(stats)

    zb_one, ha_one, stats_b1 = space_stage(
        za_one, stats_a1, halo_one, params_one[0], near, at_space_one, fast_one[3]
    )

    def expand_body(inv_ref, stats_ref, zb_ref, params_ref, fast_ref, hidden_ref, zc_ref, loads):
        scale, shift, _, _ = affine(stats_ref, params_ref, inv_ref, mid)
        hidden = geo.flat(silu(geo.three(zb_ref[...]) * scale + shift)).astype(BF16)
        hidden_ref[...] = hidden
        hidden_ref.send()
        zc_ref[:, slow_wide:] = dot(hidden[:, mid:], fast_ref[...])
        for block in range(blocks):
            zc_ref[:, block * mid : (block + 1) * mid] = dot(hidden[:, :mid], loads.get(block))
        zc_ref.send()

    def expand_one_kernel(
        meta_ref,
        inv_ref,
        stats_ref,
        zb_ref,
        params_ref,
        fast_ref,
        x_ref,
        united_ref,
        loads,
        shorts,
        hidden_ref,
        zc_ref,
        short_ref,
        out_stats,
    ):
        expand_body(inv_ref, stats_ref, zb_ref, params_ref, fast_ref, hidden_ref, zc_ref, loads)
        put_forward(out_stats, geo.three(zc_ref[...]), meta_ref[0])
        for block in range(blocks):
            weight = shorts.get(block)
            value = dot(x_ref[...], weight[:slow_wide]) + dot(united_ref[...], weight[slow_wide:])
            short_ref[:, block * mid : (block + 1) * mid] = value
            put_forward(out_stats, geo.three(value), meta_ref[0], wide + block * mid)
        short_ref.send()

    hb_one, zc_one, short, stats = run(
        expand_one_kernel,
        [((rows, small), BF16, True), wide_out, ((rows, slow_wide), F32, True), stats_both],
        smem=scalars,
        vmem=(stats_b1,),
        saved=(zb_one, params_one[1], fast_one[4], slow_x, united),
        weights=((far, 0, blocks, depth_mid), (far, at_short, blocks, depth_one)),
    )
    stats_c1 = all_sum(stats)

    def reduce_two_kernel(
        meta_ref,
        inv_ref,
        stats_ref,
        zc_ref,
        short_ref,
        params_ref,
        short_params_ref,
        x_ref,
        main_ref,
        before_ref,
        after_ref,
        loads,
        sum_ref,
        low_ref,
        za_ref,
        out_stats,
        message_ref,
    ):
        scale, shift, _, _ = affine(stats_ref, params_ref, inv_ref, slow_wide, 0, wide)
        scale_s, shift_s, _, _ = affine(
            stats_ref, short_params_ref, inv_ref, slow_wide, wide, wide + slow_wide
        )
        normed = geo.three(zc_ref[...]) * scale + shift
        slow = normed[..., :slow_wide] + (geo.three(short_ref[...]) * scale_s + shift_s)
        fast = normed[..., slow_wide:] + geo.three(x_ref[...].astype(F32))
        total = jnp.concatenate([slow, fast], axis=-1)
        sum_ref[...] = geo.flat(total)
        sum_ref.send()
        low = geo.flat(silu(total)).astype(BF16)
        low_ref[...] = low
        low_ref.send()
        weights = [loads.get(tap) for tap in range(3)]
        za = time_conv(geo, (low[:, :slow_wide],), weights)
        fast_za = fast_conv(
            geo, low[:, slow_wide:], main_ref[...], before_ref[...], after_ref[...]
        )
        za = jnp.concatenate([za, fast_za], axis=1)
        za_ref[...] = za
        za_ref.send()
        za = geo.three(za)
        put_forward(out_stats, za, meta_ref[0])
        put_message(za, message_ref)

    sum_one, low_one, za_two, stats, message = run(
        reduce_two_kernel,
        [wide_out, ((rows, wide), BF16, True), small_out, stats_small, message_out],
        smem=scalars,
        vmem=(stats_c1,),
        saved=(zc_one, short, params_one[2], params_short, fast_x, *fast_two[:3]),
        weights=((far, at_reduce_two, 3, depth_two),),
    )
    stats_a2, halo_two = sum_with_halo(stats, message, rows)
    zb_two, ha_two, stats_b2 = space_stage(
        za_two, stats_a2, halo_two, params_two[0], far, at_space_two, fast_two[3]
    )

    def expand_two_kernel(
        meta_ref,
        inv_ref,
        stats_ref,
        zb_ref,
        params_ref,
        fast_ref,
        loads,
        hidden_ref,
        zc_ref,
        out_stats,
    ):
        expand_body(inv_ref, stats_ref, zb_ref, params_ref, fast_ref, hidden_ref, zc_ref, loads)
        put_forward(out_stats, geo.three(zc_ref[...]), meta_ref[0])

    hb_two, zc_two, stats = run(
        expand_two_kernel,
        [((rows, small), BF16, True), wide_out, stats_wide],
        smem=scalars,
        vmem=(stats_b2,),
        saved=(zb_two, params_two[1], fast_two[4]),
        weights=((far, at_expand_two, blocks, depth_mid),),
    )
    stats_c2 = all_sum(stats)

    def head_kernel(
        meta_ref, inv_ref, stats_ref, zc_ref, params_ref, sum_ref, cot_ref, out_ref, g_ref, sums_ref
    ):
        scale, shift, mean, inv = affine(stats_ref, params_ref, inv_ref, slow_wide)
        zc = geo.three(zc_ref[...])
        total = zc * scale + shift + silu(geo.three(sum_ref[...]))
        valid = mask_groups(total.shape, meta_ref[0])
        sigma = jax.nn.sigmoid(total)
        out_ref[...] = geo.flat(jnp.where(valid, total * sigma, 0.0)).astype(BF16)
        slopes = sigma * (1.0 + total * (1.0 - sigma))
        gradient = jnp.where(valid, geo.three(cot_ref[...].astype(F32)) * slopes, 0.0)
        out_ref.send()
        g_ref[...] = geo.flat(gradient)
        g_ref.send()
        put_back(sums_ref, gradient, (zc - mean) * inv)

    outputs, g_two, sums = run(
        head_kernel,
        [((rows, wide), BF16, True), wide_out, stats_wide],
        smem=scalars,
        vmem=(stats_c2,),
        saved=(zc_two, params_two[2], sum_one, cot),
    )
    sums_c2 = all_sum(sums)

    def norm_back(gradient, value, coeffs, sums, valid):
        scale, _, mean, inv = coeffs
        crossed = (value - mean) * inv * sums[0] + sums[1]
        return scale * (gradient - jnp.where(valid, crossed, 0.0))

    def expand_back_body(
        meta_ref,
        inv_ref,
        stats_ref,
        sums_ref,
        stats_b_ref,
        g_ref,
        zc_ref,
        params_ref,
        zb_ref,
        params_b_ref,
        fast_ref,
        loads,
        gz_ref,
        g_out,
        sums_out,
        message_ref,
    ):
        limit = meta_ref[0]
        coeffs = affine(stats_ref, params_ref, inv_ref, slow_wide, 0, wide)
        both = [back_rows(sums_ref, inv_ref, slow_wide, row, 0, wide) for row in range(2)]
        gradient = geo.three(g_ref[...])
        gz = norm_back(
            gradient, geo.three(zc_ref[...]), coeffs, both, mask_groups(gradient.shape, limit)
        )
        gz = geo.flat(gz).astype(BF16)
        gz_ref[...] = gz
        gz_ref.send()
        fast = dot_nt(gz[:, slow_wide:], fast_ref[...])
        slow = None
        for block in range(blocks):
            term = dot_nt(gz[:, block * mid : (block + 1) * mid], loads.get(block))
            slow = term if slow is None else slow + term
        scale, shift, mean, inv = affine(stats_b_ref, params_b_ref, inv_ref, mid)
        zb = geo.three(zb_ref[...])
        back = geo.three(jnp.concatenate([slow, fast], axis=1)) * slope(zb * scale + shift)
        g_out[...] = geo.flat(back)
        g_out.send()
        masked = jnp.where(mask_groups(back.shape, limit), back, 0.0)
        put_back(sums_out, masked, (zb - mean) * inv)
        put_message(jnp.concatenate([back, zb], axis=-1), message_ref)
        return gradient

    message_back = ((2 * rows, 2 * small), BF16, False)
    gz_c2, g_b2, sums, message = run(
        expand_back_body,
        [((rows, wide), BF16, True), small_out, stats_small, message_back],
        smem=scalars,
        vmem=(stats_c2, sums_c2, stats_b2),
        saved=(g_two, zc_two, params_two[2], zb_two, params_two[1], fast_two[4]),
        weights=((far, at_expand_two, blocks, depth_mid),),
    )
    sums_b2, halo_back_two = sum_with_halo(sums, message, rows)

    lanes_fast = fast_wide // PHASES
    fast_rows_count = fast_reduce_one.shape[1] + 2 * SUB

    def expand_grad(hb_ref, gz_ref, out_ref, at):
        for block in range(blocks):
            value = dot_tn(hb_ref[:, :mid], gz_ref[:, block * mid : (block + 1) * mid])
            low = at + block * depth_mid
            out_ref[:, low : low + depth_mid, :] = value.astype(BF16).reshape(
                count, depth_mid, mid
            )

    def fast_expand_grad(hb_ref, gz_ref):
        fast = dot_tn(hb_ref[:, mid:], gz_ref[:, slow_wide:])
        total = None
        for phase in range(PHASES):
            part = fast[
                phase * fast_part : (phase + 1) * fast_part,
                phase * lanes_fast : (phase + 1) * lanes_fast,
            ]
            total = part if total is None else total + part
        return total

    def space_grad(ha_ref, taps_ref, out_ref, at):
        fast_grads = []
        for tap in range(9):
            value = dot_tn(ha_ref[:, :mid], taps_ref[tap, :, :mid])
            low = at + tap * depth_mid
            out_ref[:, low : low + depth_mid, :] = value.astype(BF16).reshape(
                count, depth_mid, mid
            )
            fast = dot_tn(ha_ref[:, mid:], taps_ref[tap, :, mid:])
            total = None
            for phase in range(PHASES):
                part = lane_block(
                    fast[phase * fast_part : (phase + 1) * fast_part], phase, fast_part
                )
                total = part if total is None else total + part
            fast_grads.append(total)
        return fast_grads

    def put_fast(reduce, space, expand, out_ref, at):
        lane = lax.broadcasted_iota(jnp.int32, reduce[0].shape, 1)

        def beside(parts):
            keep = lane[: parts[0].shape[0]]
            total = None
            for place, part in enumerate(parts):
                part = jnp.where(keep < fast_part, part, 0.0)
                part = pltpu.roll(part, place * fast_part, 1) if place else part
                total = part if total is None else total + part
            return total

        depth = reduce[0].shape[0] // count
        taps = beside(reduce).astype(BF16).reshape(count, depth, lanes_fast)
        out_ref[:, at : at + depth, :] = jnp.concatenate([taps, jnp.zeros_like(taps)], axis=-1)

        def spread(value):
            tiles = value.reshape(count // 2, SUB, lanes_fast)
            return jnp.stack([tiles, pltpu.roll(tiles, SUB // 2, 1)], axis=1).reshape(
                count, SUB, lanes_fast
            )

        first = jnp.concatenate([spread(beside(space[0:4])), spread(beside(space[4:8]))], axis=-1)
        second = jnp.concatenate([spread(beside(space[8:9])), spread(expand)], axis=-1)
        both = jnp.concatenate([first, second], axis=1).astype(BF16)
        out_ref[:, at + depth : at + depth + 2 * SUB, :] = both

    def space_back_stage(g, zb, za, halo, stats_b, sums_b, params_b, stats_a, params_a, g_hbm, at, fast_w):
        def kernel(
            meta_ref,
            inv_ref,
            side_ref,
            up_ref,
            down_ref,
            stats_b_ref,
            sums_b_ref,
            stats_a_ref,
            g_ref,
            zb_ref,
            za_ref,
            params_b_ref,
            params_a_ref,
            fast_ref,
            loads,
            taps_ref,
            g_out,
            sums_out,
        ):
            limit = meta_ref[0]
            coeffs = affine(stats_b_ref, params_b_ref, inv_ref, mid)
            both = [back_rows(sums_b_ref, inv_ref, mid, row) for row in range(2)]

            def back(gradient, value, scale):
                valid = mask_groups(gradient.shape, limit, scale)
                return norm_back(gradient, value, coeffs, both, valid)

            def halo_back(value, scale):
                value = geo.three(value.astype(F32))
                return back(value[..., :small], value[..., small:], scale)

            near_by = Neighbours(
                back(geo.three(g_ref[...]), geo.three(zb_ref[...]), 1),
                halo_back(up_ref[:half_rows], 2),
                halo_back(down_ref[:half_rows], 2),
                halo_back(side_ref[:rows], 1),
                halo_back(up_ref[half_rows:], 2),
                halo_back(down_ref[half_rows:], 2),
                meta_ref,
                geo.width,
            )
            slow = fast = None
            for tap in range(9):
                moved = geo.flat(near_by.at(1 - tap // 3, 1 - tap % 3)).astype(BF16)
                taps_ref[tap] = moved
                if tap == 8:
                    taps_ref.send()
                slow_term = dot_nt(moved[:, :mid], loads.get(tap))
                fast_term = dot_nt(moved[:, mid:], fast_ref[tap])
                slow = slow_term if slow is None else slow + slow_term
                fast = fast_term if fast is None else fast + fast_term
            scale, shift, mean, inv = affine(stats_a_ref, params_a_ref, inv_ref, mid)
            za = geo.three(za_ref[...])
            result = geo.three(jnp.concatenate([slow, fast], axis=1)) * slope(za * scale + shift)
            g_out[...] = geo.flat(result)
            g_out.send()
            masked = jnp.where(mask_groups(result.shape, limit), result, 0.0)
            put_back(sums_out, masked, (za - mean) * inv)

        taps, g, sums = run(
            kernel,
            [((9, rows, small), BF16, True), small_out, stats_small],
            smem=scalars,
            vmem=(*halo, stats_b, sums_b, stats_a),
            saved=(g, zb, za, params_b, params_a, fast_w),
            weights=((g_hbm, at, 9, depth_mid),),
        )
        return taps, g, all_sum(sums)

    taps_two, g_a2, sums_a2 = space_back_stage(
        g_b2,
        zb_two,
        za_two,
        halo_back_two,
        stats_b2,
        sums_b2,
        params_two[1],
        stats_a2,
        params_two[0],
        far,
        at_space_two,
        fast_two[3],
    )
    def reduce_gz(meta_ref, inv_ref, g_ref, za_ref, stats_ref, sums_ref, params_ref, steps_ref):
        coeffs = affine(stats_ref, params_ref, inv_ref, mid)
        both = [back_rows(sums_ref, inv_ref, mid, row) for row in range(2)]
        gradient = geo.three(g_ref[...])
        gz = norm_back(
            gradient,
            geo.three(za_ref[...]),
            coeffs,
            both,
            mask_groups(gradient.shape, meta_ref[0]),
        )
        gz = geo.flat(gz)
        steps = [geo.shift(gz, -1).astype(BF16), gz.astype(BF16), geo.shift(gz, 1).astype(BF16)]
        for tap in range(3):
            steps_ref[tap] = steps[tap]
        if isinstance(steps_ref, Store):
            steps_ref.send()
        return steps

    def reduce_back_two_kernel(
        meta_ref,
        inv_ref,
        stats_ref,
        sums_ref,
        stats_c_ref,
        g_ref,
        za_ref,
        params_ref,
        g_two_ref,
        sum_ref,
        zc_ref,
        short_ref,
        main_ref,
        before_ref,
        after_ref,
        loads,
        steps_ref,
        g_out,
        sums_out,
    ):
        steps = reduce_gz(
            meta_ref, inv_ref, g_ref, za_ref, stats_ref, sums_ref, params_ref, steps_ref
        )
        slow = None
        for tap in range(3):
            term = dot_nt(steps[tap][:, :mid], loads.get(tap))
            slow = term if slow is None else slow + term
        fast = fast_conv_back(
            [step[:, mid:] for step in steps], main_ref[...], before_ref[...], after_ref[...]
        )
        back = jnp.concatenate([slow, fast], axis=1) + g_two_ref[...]
        back = geo.three(back * slope(sum_ref[...]))
        g_out[...] = geo.flat(back)
        g_out.send()
        masked = jnp.where(mask_groups(back.shape, meta_ref[0]), back, 0.0)
        mean, inv = moments(stats_c_ref, inv_ref, slow_wide, 0, wide)
        put_back(sums_out, masked, (geo.three(zc_ref[...]) - mean) * inv)
        mean, inv = moments(stats_c_ref, inv_ref, slow_wide, wide, wide + slow_wide)
        masked = masked[..., :slow_wide]
        put_back(sums_out, masked, (geo.three(short_ref[...]) - mean) * inv, wide)

    steps_two, g_one, sums = run(
        reduce_back_two_kernel,
        [((3, rows, small), BF16, True), wide_out, stats_both],
        smem=scalars,
        vmem=(stats_a2, sums_a2, stats_c1),
        saved=(g_a2, za_two, params_two[0], g_two, sum_one, zc_one, short, *fast_two[:3]),
        weights=((far, at_reduce_two, 3, depth_two),),
    )
    sums_c1 = all_sum(sums)

    def grads_two_kernel(hb_ref, gz_ref, ha_ref, taps_ref, low_ref, steps_ref, out_ref):
        for tap in range(3):
            value = dot_tn(low_ref[:, :slow_wide], steps_ref[tap, :, :mid])
            out_ref[:, tap * depth_two : (tap + 1) * depth_two, :] = value.astype(BF16).reshape(
                count, depth_two, mid
            )
        at = 3 * depth_two
        space = space_grad(ha_ref, taps_ref, out_ref, at)
        at += 9 * depth_mid
        expand_grad(hb_ref, gz_ref, out_ref, at)
        at += blocks * depth_mid
        reduce = fast_reduce_grad(
            low_ref[:, slow_wide:], [steps_ref[tap, :, mid:] for tap in range(3)]
        )
        put_fast(reduce, space, fast_expand_grad(hb_ref, gz_ref), out_ref, at)

    rows_two = 3 * depth_two + (9 + blocks) * depth_mid + fast_rows_count
    (packed_two,) = run(
        grads_two_kernel,
        [((count, rows_two, mid), BF16, True)],
        saved=(hb_two, gz_c2, ha_two, taps_two, low_one, steps_two),
    )
    part_two = scatter_rows(packed_two)

    def expand_back_one_kernel(*refs):
        *body, short_ref, short_params_ref, loads, gz_ref, g_out, sums_out, message, gs_ref = refs
        gradient = expand_back_body(*body, loads, gz_ref, g_out, sums_out, message)
        meta_ref, inv_ref, stats_ref, sums_ref = body[:4]
        low, high = wide, wide + slow_wide
        coeffs = affine(stats_ref, short_params_ref, inv_ref, slow_wide, low, high)
        both = [back_rows(sums_ref, inv_ref, slow_wide, row, low, high) for row in range(2)]
        gradient = gradient[..., :slow_wide]
        valid = mask_groups(gradient.shape, meta_ref[0])
        gs = norm_back(gradient, geo.three(short_ref[...]), coeffs, both, valid)
        gs_ref[...] = geo.flat(gs).astype(BF16)

    gz_c1, g_b1, sums, message, gz_short = run(
        expand_back_one_kernel,
        [((rows, wide), BF16, True), small_out, stats_small, message_back]
        + [((rows, slow_wide), BF16, True)],
        smem=scalars,
        vmem=(stats_c1, sums_c1, stats_b1),
        saved=(g_one, zc_one, params_one[2], zb_one, params_one[1], fast_one[4])
        + (short, params_short),
        weights=((far, 0, blocks, depth_mid),),
    )
    sums_b1, halo_back_one = sum_with_halo(sums, message, rows)
    joined_lanes = slow_wide + lat

    def grads_mid_kernel(x_ref, united_ref, gs_ref, hb_ref, gz_ref, loads, out_ref, back_ref):
        for block in range(blocks):
            gs = gs_ref[:, block * mid : (block + 1) * mid]
            value = jnp.concatenate([dot_tn(x_ref[...], gs), dot_tn(united_ref[...], gs)], axis=0)
            out_ref[:, block * depth_one : (block + 1) * depth_one, :] = value.astype(
                BF16
            ).reshape(count, depth_one, mid)
            term = dot_nt(gs, loads.get(block))
            back_ref[...] = term if block == 0 else back_ref[...] + term
        expand_grad(hb_ref, gz_ref, out_ref, blocks * depth_one)

    packed_mid, short_back = run(
        grads_mid_kernel,
        [((count, blocks * (depth_one + depth_mid), mid), BF16, True)]
        + [((rows, joined_lanes), F32, True)],
        saved=(slow_x, united, gz_short, hb_one, gz_c1),
        weights=((far, at_short, blocks, depth_one),),
    )
    part_mid = scatter_rows(packed_mid)

    taps_one, g_a1, sums_a1 = space_back_stage(
        g_b1,
        zb_one,
        za_one,
        halo_back_one,
        stats_b1,
        sums_b1,
        params_one[1],
        stats_a1,
        params_one[0],
        near,
        at_space_one,
        fast_one[3],
    )
    def last_kernel(
        meta_ref,
        inv_ref,
        stats_ref,
        sums_ref,
        g_ref,
        za_ref,
        params_ref,
        g_one_ref,
        short_ref,
        lateral_ref,
        main_ref,
        before_ref,
        after_ref,
        loads,
        steps_ref,
        slow_ref,
        fast_ref,
        united_ref,
    ):
        steps = reduce_gz(
            meta_ref, inv_ref, g_ref, za_ref, stats_ref, sums_ref, params_ref, steps_ref
        )
        joined = short_ref[...]
        for tap in range(3):
            joined = joined + dot_nt(steps[tap][:, :mid], loads.get(tap))
        slow_ref[...] = joined[:, :slow_wide]
        tail = joined[:, slow_wide:]
        now, past = tail.astype(BF16), geo.shift(tail, -1).astype(BF16)
        united_ref[0] = now
        united_ref[1] = past
        lanes = fast_wide // PHASES
        fast = fast_conv_back(
            [step[:, mid:] for step in steps], main_ref[...], before_ref[...], after_ref[...]
        )
        fast = fast + g_one_ref[:, slow_wide:]
        front = dot_nt(now, lateral_ref[2:5].reshape(3 * lanes, lat))
        back = dot_nt(past, lateral_ref[0:2].reshape(2 * lanes, lat))
        fast_ref[:, : 2 * lanes] = fast[:, : 2 * lanes] + front[:, : 2 * lanes]
        fast_ref[:, 2 * lanes : 3 * lanes] = (
            fast[:, 2 * lanes : 3 * lanes] + front[:, 2 * lanes :] + back[:, :lanes]
        )
        fast_ref[:, 3 * lanes :] = fast[:, 3 * lanes :] + back[:, lanes:]

    steps_one, grad_slow, grad_fast, united_low = run(
        last_kernel,
        [
            ((3, rows, small), BF16, False),
            ((rows, slow_wide), F32, True),
            ((rows, fast_wide), F32, True),
            ((2, rows, lat), BF16, False),
        ],
        smem=scalars,
        vmem=(stats_a1, sums_a1),
        saved=(g_a1, za_one, params_one[0], g_one, short_back, lateral, *fast_one[:3]),
        weights=((near, 0, 3, depth_one),),
    )

    def grads_one_kernel(
        steps_ref,
        low_ref,
        x_ref,
        united_ref,
        fast_x_ref,
        ha_ref,
        taps_ref,
        hb_ref,
        gz_ref,
        out_ref,
    ):
        lanes = fast_wide // PHASES
        for tap in range(3):
            step = steps_ref[tap, :, :mid]
            value = jnp.concatenate(
                [dot_tn(x_ref[...], step), dot_tn(united_ref[...], step)], axis=0
            )
            out_ref[:, tap * depth_one : (tap + 1) * depth_one, :] = value.astype(BF16).reshape(
                count, depth_one, mid
            )
        at = 3 * depth_one
        past = dot_tn(fast_x_ref[:, 2 * lanes :], low_ref[1])
        now = dot_tn(fast_x_ref[:, : 3 * lanes], low_ref[0])
        both = jnp.concatenate([past, now], axis=0).astype(BF16)
        for tap in range(5):
            out_ref[:, at + tap * depth_lat : at + (tap + 1) * depth_lat, :] = both[
                tap * lanes : (tap + 1) * lanes
            ].reshape(count, depth_lat, lat)
        at += 5 * depth_lat
        space = space_grad(ha_ref, taps_ref, out_ref, at)
        at += 9 * depth_mid
        reduce = fast_reduce_grad(
            fast_x_ref[...], [steps_ref[tap, :, mid:] for tap in range(3)]
        )
        put_fast(reduce, space, fast_expand_grad(hb_ref, gz_ref), out_ref, at)

    rows_one = 3 * depth_one + 5 * depth_lat + 9 * depth_mid + fast_rows_count
    (packed_one,) = run(
        grads_one_kernel,
        [((count, rows_one, mid), BF16, True)],
        vmem=(steps_one, united_low),
        saved=(slow_x, united, fast_x, ha_one, taps_one, hb_one, gz_c1),
    )
    part_one = scatter_rows(packed_one)
    total_two, total_mid, total_one = [
        join_rows(part) for part in (part_two, part_mid, part_one)
    ]

    def fast_shards_of(block, reduce, space, expand):
        depth, lanes = reduce.shape[1:]
        taps = jnp.moveaxis(block[:depth, : 3 * lanes].reshape(depth, 3, lanes), 1, 0)
        few = space.shape[2]
        first = block[depth : depth + few].reshape(few, SUB, lanes)
        second = block[depth + SUB : depth + SUB + few]
        spatial = jnp.concatenate([first, second[:, None, :lanes]], axis=1)
        spatial = jnp.moveaxis(spatial, 1, 0).reshape(space.shape)
        return taps, spatial, second[:, expand.shape[1] :]

    at = 3 * depth_two
    grad_slow_reduce_two = total_two[:at].reshape(slow_reduce_two.shape)
    grad_slow_spatial_two = total_two[at : at + 9 * depth_mid].reshape(slow_spatial_two.shape)
    at += 9 * depth_mid
    grad_slow_expand_two = uncolumns(total_two[at : at + blocks * depth_mid], depth_mid)
    at += blocks * depth_mid
    fast_two_grads = fast_shards_of(total_two[at:], *fast_shards_two)
    at = blocks * depth_one
    grad_slow_shortcut = uncolumns(total_mid[:at], depth_one)
    grad_slow_expand_one = uncolumns(total_mid[at:], depth_mid)
    at = 3 * depth_one
    grad_slow_reduce_one = total_one[:at].reshape(slow_reduce_one.shape)
    grad_lateral = total_one[at : at + 5 * depth_lat].reshape(lateral_weight.shape)
    at += 5 * depth_lat
    grad_slow_spatial_one = total_one[at : at + 9 * depth_mid].reshape(slow_spatial_one.shape)
    at += 9 * depth_mid
    fast_one_grads = fast_shards_of(total_one[at:], *fast_shards_one)

    def norm_grads(first, second, third):
        slow = [first[:, :mid], second[:, :mid], third[:, :slow_wide]]
        fast = [first[:, mid:], second[:, mid:], third[:, slow_wide:wide]]
        fast = [jnp.sum(part.reshape(2, PHASES, -1), axis=1) for part in fast]
        return slow, fast

    slow_one_p, fast_one_p = norm_grads(sums_a1, sums_b1, sums_c1)
    slow_two_p, fast_two_p = norm_grads(sums_a2, sums_b2, sums_c2)
    grad_slow_norms_one = jnp.concatenate(slow_one_p + [sums_c1[:, wide:]], axis=1)
    grad_slow_norms_two = jnp.concatenate(slow_two_p, axis=1)
    grad_fast_norms_one = jnp.concatenate(fast_one_p, axis=1)
    grad_fast_norms_two = jnp.concatenate(fast_two_p, axis=1)
    return (
        outputs[:, :slow_wide].reshape(slow_input.shape),
        join_phases(outputs[:, slow_wide:], fast_input.shape),
        grad_slow.reshape(slow_input.shape),
        join_phases(grad_fast, fast_input.shape),
        grad_lateral,
        grad_slow_reduce_one,
        grad_slow_spatial_one,
        grad_slow_expand_one,
        grad_slow_shortcut,
        *fast_one_grads,
        grad_slow_reduce_two,
        grad_slow_spatial_two,
        grad_slow_expand_two,
        *fast_two_grads,
        grad_slow_norms_one,
        grad_fast_norms_one,
        grad_slow_norms_two,
        grad_fast_norms_two,
    )


def solution(mesh):
    in_specs = (
        P("clips", None, "ha", "wa", None),
        P("clips", None, "ha", "wa", None),
        P("clips", None, "ha", "wa", None),
        P("clips", None, "ha", "wa", None),
        P("clips"),
        P(None, ("ha", "wa"), None),
        P(None, ("ha", "wa"), None),
        P(None, None, ("ha", "wa"), None),
        P(("ha", "wa"), None),
        P(("ha", "wa"), None),
        P(None, ("ha", "wa"), None),
        P(None, None, ("ha", "wa"), None),
        P(("ha", "wa"), None),
        P(None, ("ha", "wa"), None),
        P(None, None, ("ha", "wa"), None),
        P(("ha", "wa"), None),
        P(None, ("ha", "wa"), None),
        P(None, None, ("ha", "wa"), None),
        P(("ha", "wa"), None),
        P(),
        P(),
        P(),
        P(),
    )
    out_specs = (
        P("clips", None, "ha", "wa", None),
        P("clips", None, "ha", "wa", None),
        P("clips", None, "ha", "wa", None),
        P("clips", None, "ha", "wa", None),
        P(None, ("ha", "wa"), None),
        P(None, ("ha", "wa"), None),
        P(None, None, ("ha", "wa"), None),
        P(("ha", "wa"), None),
        P(("ha", "wa"), None),
        P(None, ("ha", "wa"), None),
        P(None, None, ("ha", "wa"), None),
        P(("ha", "wa"), None),
        P(None, ("ha", "wa"), None),
        P(None, None, ("ha", "wa"), None),
        P(("ha", "wa"), None),
        P(None, ("ha", "wa"), None),
        P(None, None, ("ha", "wa"), None),
        P(("ha", "wa"), None),
        P(),
        P(),
        P(),
        P(),
    )
    return jax.shard_map(
        on_device, mesh=mesh, in_specs=in_specs, out_specs=out_specs, check_vma=False
    )
```

```python
import jax
import jax.numpy as jnp
from jax import lax
from jax.experimental import pallas as pl
from jax.experimental.pallas import tpu as pltpu
from jax.sharding import PartitionSpec as P

epsilon = 1e-05
F32 = jnp.float32
BF16 = jnp.bfloat16
TILE = ("ha", "wa")
PHASES = 4
SUB = 8


def dot(left, right):
    return lax.dot_general(left, right, (((1,), (0,)), ((), ())), preferred_element_type=F32)


def dot_tn(left, right):
    return lax.dot_general(left, right, (((0,), (0,)), ((), ())), preferred_element_type=F32)


def dot_nt(left, right):
    return lax.dot_general(left, right, (((1,), (1,)), ((), ())), preferred_element_type=F32)


class Loads:
    def __init__(self, source, offset, target, sems, first):
        self.copies = []
        depth = target.shape[2]
        for step in range(target.shape[0]):
            copy = pltpu.make_async_copy(
                source.at[:, pl.ds(offset + step * depth, depth), :],
                target.at[step],
                sems.at[first + step],
            )
            copy.start()
            self.copies.append(copy)
        self.target = target

    def get(self, step):
        self.copies[step].wait()
        block = self.target[step]
        return block.reshape(-1, block.shape[-1])


class Store:
    def __init__(self, scratch, target, sem):
        self.scratch, self.shape, self.sent = scratch, scratch.shape, False
        self.copy = pltpu.make_async_copy(scratch, target, sem)

    def send(self):
        self.copy.start()
        self.sent = True

    def __setitem__(self, index, value):
        self.scratch[index] = value

    def __getitem__(self, index):
        return self.scratch[index]


def run(body, outs, smem=(), parts=(), vmem=(), saved=(), weights=(), scratch=(), limit=56):
    near = pl.BlockSpec(memory_space=pltpu.VMEM)
    far = pl.BlockSpec(memory_space=pltpu.HBM)
    sources = []
    for array, *_ in weights:
        if not any(array is other for other in sources):
            sources.append(array)
    outs = list(outs) + [(part.shape[1:], part.dtype, "hbm") for part in parts]
    held = [pltpu.VMEM(array.shape, array.dtype) for array in saved]
    for array, _, steps, depth in weights:
        held.append(pltpu.VMEM((steps, array.shape[0], depth, array.shape[2]), array.dtype))
    for shape, dtype, kind in outs:
        if kind == "hbm":
            held.append(pltpu.VMEM(shape, dtype))
        elif kind == "spread":
            held.append(pltpu.VMEM(shape[1:], dtype))
    sems = len(saved) + sum(steps for _, _, steps, _ in weights) + len(outs)
    held.append(pltpu.SemaphoreType.DMA((sems,)))

    def kernel(*refs):
        refs = list(refs)

        def take(number):
            taken = refs[:number]
            del refs[:number]
            return taken

        smem_refs, part_refs, vmem_refs = take(len(smem)), take(len(parts)), take(len(vmem))
        saved_refs, source_refs, out_refs = take(len(saved)), take(len(sources)), take(len(outs))
        saved_scratch, weight_scratch = take(len(saved)), take(len(weights))
        out_scratch = take(sum(kind in ("hbm", "spread") for _, _, kind in outs))
        sem, more = refs[0], refs[1:]
        copies = []
        for at, (source, target) in enumerate(zip(saved_refs, saved_scratch)):
            copy = pltpu.make_async_copy(source, target, sem.at[at])
            copy.start()
            copies.append(copy)
        at = len(saved)
        loads = []
        for (array, offset, steps, _), target in zip(weights, weight_scratch):
            place = [array is other for other in sources].index(True)
            loads.append(Loads(source_refs[place], offset, target, sem, at))
            at += steps
        results, stores, spreads = [], [], []
        for ref, (_, _, kind) in zip(out_refs, outs):
            if kind == "hbm":
                stores.append(Store(out_scratch.pop(0), ref, sem.at[at]))
                at += 1
                results.append(stores[-1])
            elif kind == "spread":
                spreads.append((out_scratch.pop(0), ref))
                results.append(spreads[-1][0])
            else:
                results.append(ref)
        sums = results[len(results) - len(parts) :]
        results = results[: len(results) - len(parts)]
        for part, total in zip(part_refs, sums):
            total[...] = jnp.sum(part[...], axis=0)
            total.send()
        for copy in copies:
            copy.wait()
        totals = [total.scratch for total in sums]
        body(*smem_refs, *totals, *vmem_refs, *saved_scratch, *loads, *results, *more)
        for store in stores:
            if not store.sent:
                store.send()
        for value, ref in spreads:
            ref[...] = jnp.broadcast_to(value[...][None], ref.shape)
        for store in stores:
            store.copy.wait()

    return pl.pallas_call(
        kernel,
        out_shape=[jax.ShapeDtypeStruct(shape, dtype) for shape, dtype, _ in outs],
        in_specs=[pl.BlockSpec(memory_space=pltpu.SMEM)] * len(smem)
        + [near] * (len(parts) + len(vmem))
        + [far] * (len(saved) + len(sources)),
        out_specs=[far if kind in ("hbm", "raw") else near for _, _, kind in outs],
        scratch_shapes=held + list(scratch),
        compiler_params=pltpu.CompilerParams(vmem_limit_bytes=limit * 1024 * 1024),
    )(*smem, *parts, *vmem, *saved, *sources)


class Geometry:
    def __init__(self, slow_shape, fast_shape):
        self.cap, self.frames, self.height, self.width = slow_shape[:4]
        self.groups = self.cap * self.frames
        self.rows = self.groups * SUB

    def three(self, value):
        return value.reshape(-1, SUB, value.shape[-1])

    def flat(self, value):
        return value.reshape(-1, value.shape[-1])

    def shift(self, value, step):
        lanes = value.shape[-1]
        whole = value.reshape(self.cap, self.frames, SUB, lanes)
        zero = jnp.zeros((self.cap, 1, SUB, lanes), value.dtype)
        if step > 0:
            whole = jnp.concatenate([zero, whole[:, :-1]], axis=1)
        else:
            whole = jnp.concatenate([whole[:, 1:], zero], axis=1)
        return whole.reshape(-1, lanes)


def mask_groups(shape, limit, scale=1):
    return lax.broadcasted_iota(jnp.int32, shape, 0) * scale < limit


def rep(ref, row, low, high):
    return jnp.broadcast_to(ref[row : row + 1, low:high], (SUB, high - low))


def fold(value, slow):
    fast = value[:, slow:]
    lanes = fast.shape[-1]
    part = lanes // PHASES
    if part % 128 == 0:
        total = fast[:, :part]
        for phase in range(1, PHASES):
            total = total + fast[:, phase * part : (phase + 1) * part]
        return jnp.concatenate([value[:, :slow]] + [total] * PHASES, axis=1)
    total = fast
    for phase in range(1, PHASES):
        total = total + pltpu.roll(fast, phase * part, 1)
    return jnp.concatenate([value[:, :slow], total], axis=1)


def lane_counts(inv_ref, lanes, slow):
    lane = lax.broadcasted_iota(jnp.int32, (SUB, lanes), 1)
    return jnp.where(lane < slow, inv_ref[0], inv_ref[1])


def moments(stats, inv_ref, slow, low=0, high=None):
    high = stats.shape[1] if high is None else high
    total, square = rep(stats, 0, low, high), rep(stats, 1, low, high)
    if slow < high - low:
        total, square = fold(total, slow), fold(square, slow)
    inv_n = lane_counts(inv_ref, high - low, slow)
    mean = total * inv_n
    return mean, lax.rsqrt(square * inv_n - mean * mean + epsilon)


def affine(stats, params, inv_ref, slow, low=0, high=None):
    mean, inv = moments(stats, inv_ref, slow, low, high)
    lanes = mean.shape[1]
    scale = (1.0 + rep(params, 0, 0, lanes)) * inv
    return scale, rep(params, 1, 0, lanes) - mean * scale, mean, inv


def back_rows(sums, inv_ref, slow, row, low=0, high=None):
    high = sums.shape[1] if high is None else high
    total = rep(sums, row, low, high)
    if slow < high - low:
        total = fold(total, slow)
    return total * lane_counts(inv_ref, high - low, slow)


def silu(value):
    return value * jax.nn.sigmoid(value)


def slope(value):
    sigma = jax.nn.sigmoid(value)
    return sigma * (1.0 + value * (1.0 - sigma))


def put_stats(ref, first, second, low=0):
    lanes = first.shape[-1]
    ref[0:1, low : low + lanes] = jnp.sum(jnp.sum(first, axis=0), axis=0, keepdims=True)
    ref[1:2, low : low + lanes] = jnp.sum(jnp.sum(second, axis=0), axis=0, keepdims=True)


def put_back(ref, gradient, normal, low=0):
    put_stats(ref, gradient * normal, gradient, low)


def put_forward(ref, value, limit, low=0):
    masked = jnp.where(mask_groups(value.shape, limit), value, 0.0)
    put_stats(ref, masked, masked * value, low)


def put_message(value, ref):
    lanes = value.shape[-1]
    pairs = value.reshape(-1, 2, SUB, lanes)
    first, second = pairs[:, 0], pairs[:, 1]
    near = lax.broadcasted_iota(jnp.int32, first.shape, 1) < SUB // 2
    top = jnp.where(near, first, pltpu.roll(second, SUB // 2, 1))
    bottom = jnp.where(near, pltpu.roll(first, SUB // 2, 1), second)
    parts = [part.reshape(-1, lanes).astype(BF16) for part in (value, top, bottom)]
    at = 0
    for part in parts:
        ref[at : at + part.shape[0]] = part
        at += part.shape[0]


def unpack_bottom(value):
    both = jnp.stack([pltpu.roll(value, SUB // 2, 1), value], axis=1)
    return both.reshape(-1, SUB, value.shape[-1])


def unpack_top(value):
    both = jnp.stack([value, pltpu.roll(value, SUB // 2, 1)], axis=1)
    return both.reshape(-1, SUB, value.shape[-1])


class Neighbours:
    def __init__(self, own, up, down, side, side_up, side_down, meta, width):
        half = SUB // 2
        row = lax.broadcasted_iota(jnp.int32, own.shape, 1)
        near = row < half
        self.col = row % width
        self.width = width
        ha, wa, last = meta[1], meta[2], meta[3]
        up = unpack_bottom(jnp.where(ha > 0, up, 0.0))
        side_up = unpack_bottom(jnp.where(ha > 0, side_up, 0.0))
        down = unpack_top(jnp.where(ha < last, down, 0.0))
        side_down = unpack_top(jnp.where(ha < last, side_down, 0.0))
        self.rows = {
            0: own,
            -1: pltpu.roll(jnp.where(near, own, up), half, 1),
            1: pltpu.roll(jnp.where(near, down, own), half, 1),
        }
        sides = {
            0: pltpu.roll(side, half, 1),
            -1: jnp.where(near, side, side_up),
            1: jnp.where(near, side_down, side),
        }
        self.left = {key: jnp.where(wa > 0, value, 0.0) for key, value in sides.items()}
        self.right = {key: jnp.where(wa > 0, 0.0, value) for key, value in sides.items()}

    def at(self, row_step, col_step):
        base = self.rows[row_step]
        if col_step < 0:
            return pltpu.roll(
                jnp.where(self.col == self.width - 1, self.left[row_step], base), 1, 1
            )
        if col_step > 0:
            return pltpu.roll(jnp.where(self.col == 0, self.right[row_step], base), SUB - 1, 1)
        return base


def xor_pairs(size, step):
    return [(index, index ^ step) for index in range(size)]


def direct_sum(value, axis):
    size = lax.axis_size(axis)
    step = 1
    while step < size:
        if size // step >= 4:
            one, two, three = [
                lax.ppermute(value, axis, xor_pairs(size, step * times)) for times in (1, 2, 3)
            ]
            value = (value + two) + (one + three)
            step *= 4
        else:
            value = value + lax.ppermute(value, axis, xor_pairs(size, step))
            step *= 2
    return value


AXES = ("clips", "ha", "wa")
MOST = 32


def spread_count():
    count = lax.axis_size("ha") * lax.axis_size("wa")
    whole = count * lax.axis_size("clips")
    return whole if whole <= MOST else count


def exchange(copies):
    if copies.shape[0] == lax.axis_size("clips") * lax.axis_size("ha") * lax.axis_size("wa"):
        return lax.all_to_all(copies, AXES, 0, 0)
    return lax.all_to_all(direct_sum(copies, "clips"), TILE, 0, 0)


def exchange_halo(message, rows):
    wide, high = lax.axis_size("wa"), lax.axis_size("ha")
    side = lax.ppermute(message, "wa", xor_pairs(wide, 1))
    half = rows // 2
    tops = jnp.concatenate([message[rows : rows + half], side[rows : rows + half]], axis=0)
    bottoms = jnp.concatenate([message[rows + half :], side[rows + half :]], axis=0)
    up = lax.ppermute(bottoms, "ha", [(row, row + 1) for row in range(high - 1)])
    down = lax.ppermute(tops, "ha", [(row + 1, row) for row in range(high - 1)])
    return side, up, down


def time_conv(geo, parts, blocks):
    result = None
    for tap in range(3):
        at = 0
        total = None
        for part in parts:
            lanes = part.shape[-1]
            term = dot(part, blocks[tap][at : at + lanes])
            at += lanes
            total = term if total is None else total + term
        if tap != 1:
            total = geo.shift(total, 1 - tap)
        result = total if result is None else result + total
    return result


def fast_conv(geo, value, main, before, after):
    lanes = value.shape[-1] // PHASES
    result = dot(value, main)
    result = result + geo.shift(dot(value[:, -lanes:], before), 1)
    return result + geo.shift(dot(value[:, :lanes], after), -1)


def fast_conv_back(steps, main, before, after):
    lanes = before.shape[0]
    middle = dot_nt(steps[1], main)
    first = middle[:, :lanes] + dot_nt(steps[2], after)
    last = middle[:, -lanes:] + dot_nt(steps[0], before)
    return jnp.concatenate([first, middle[:, lanes:-lanes], last], axis=1)


def lane_block(value, phase, part):
    return pltpu.roll(value, value.shape[-1] - phase * part, 1) if phase else value


def fast_reduce_grad(value, steps):
    lanes = value.shape[-1] // PHASES
    part = steps[1].shape[-1] // PHASES
    main = dot_tn(value, steps[1])
    before = dot_tn(value[:, -lanes:], steps[0])
    after = dot_tn(value[:, :lanes], steps[2])

    def block(row, col):
        return lane_block(main[row * lanes : (row + 1) * lanes], col, part)

    result = []
    for tap in range(3):
        total = before if tap == 0 else None
        if tap == 2:
            total = lane_block(after, PHASES - 1, part)
        for col in range(PHASES):
            row = col + tap - 1
            if 0 <= row < PHASES:
                total = block(row, col) if total is None else total + block(row, col)
        result.append(total)
    return result


def gather_pack(parts):
    return lax.all_gather(jnp.concatenate(parts, axis=0), TILE, axis=0)


def columns(shard, lanes):
    depth, total = shard.shape
    return jnp.moveaxis(shard.reshape(depth, total // lanes, lanes), 1, 0).reshape(-1, lanes)


def split_phases(value):
    cap, frames, height, width, lanes = value.shape
    value = value.reshape(cap, frames // PHASES, PHASES, height, width, lanes)
    return jnp.moveaxis(value, 2, 4).reshape(-1, PHASES * lanes)


def join_phases(value, shape):
    cap, frames, height, width, lanes = shape
    value = value.reshape(cap, frames // PHASES, height, width, PHASES, lanes)
    return jnp.moveaxis(value, 4, 2).reshape(shape)


def early_gather(shards_one, shards_two, lateral):
    rows = []
    lanes = shards_one[2].shape[-1]
    kinds = [jnp.stack(pair) for pair in zip(shards_one, shards_two)]
    kinds.append(jnp.stack([lateral[..., :lanes], lateral[..., lanes:]]))
    for kind in kinds:
        flat = kind.reshape(-1, kind.shape[-1])
        rows.append(jnp.pad(flat, ((0, 0), (0, lanes - flat.shape[-1]))))
    packed = gather_pack(rows)
    result = []
    at = 0
    for kind in kinds:
        depth, width = kind.shape[-2:]
        number = kind.size // width
        part = packed[:, at : at + number, :width].reshape(packed.shape[0], -1, depth, width)
        at += number
        result.append(jnp.moveaxis(part, 0, 1).reshape(part.shape[1], -1, width))
    return result


def prepare_kernel(taps_ref, space_ref, wide_ref, lateral_ref, *refs):
    slow_one, fast_one, slow_two, fast_two, *outs = refs
    part = taps_ref.shape[-1]
    lateral, *joint = outs[10:]
    number = lateral.shape[0]
    for tap in range(number):
        lateral[tap] = jnp.concatenate([lateral_ref[tap], lateral_ref[number + tap]], axis=1)
    for layer, (slow, fast) in enumerate(((slow_one, fast_one), (slow_two, fast_two))):
        at = fast_at = 0
        for ref in joint[3 * layer : 3 * layer + 3]:
            fast_lanes = part if ref.shape[1] < slow.shape[1] // 2 else wide_ref.shape[-1]
            lanes = ref.shape[1] - PHASES * fast_lanes
            values = [slow[:, at : at + lanes]]
            values += [fast[:, fast_at : fast_at + fast_lanes]] * PHASES
            ref[...] = jnp.concatenate(values, axis=1)
            at, fast_at = at + lanes, fast_at + fast_lanes
    joint[6][...] = slow_one[:, slow_one.shape[1] - joint[6].shape[1] :]
    for layer in range(2):
        main, before, after, space, wide = outs[5 * layer : 5 * layer + 5]
        taps = [taps_ref[3 * layer + tap] for tap in range(3)]
        zero = jnp.zeros_like(taps[0])
        lanes = taps[0].shape[0]
        for row in range(PHASES):
            blocks = [
                taps[row - col + 1] if abs(row - col) <= 1 else zero for col in range(PHASES)
            ]
            main[row * lanes : (row + 1) * lanes, :] = jnp.concatenate(blocks, axis=1)
        before[...] = jnp.concatenate([taps[0]] + [zero] * (PHASES - 1), axis=1)
        after[...] = jnp.concatenate([zero] * (PHASES - 1) + [taps[2]], axis=1)
        for tap in range(9):
            block = space_ref[9 * layer + tap]
            none = jnp.zeros_like(block)
            for row in range(PHASES):
                blocks = [block if row == col else none for col in range(PHASES)]
                space[tap, row * part : (row + 1) * part, :] = jnp.concatenate(blocks, axis=1)
        block = wide_ref[layer]
        none = jnp.zeros_like(block)
        for row in range(PHASES):
            blocks = [block if row == col else none for col in range(PHASES)]
            wide[row * part : (row + 1) * part, :] = jnp.concatenate(blocks, axis=1)


def clip_partners():
    return range(1, lax.axis_size("clips")) if lax.axis_size("clips") <= 4 else ()


def to_partners(pieces, axis):
    size = lax.axis_size(axis)
    return [
        lax.ppermute(piece, axis, xor_pairs(size, step + 1)) for step, piece in enumerate(pieces)
    ]


def sum_over_clips(rows_sum):
    size = lax.axis_size("clips")
    if size > 4:
        return [lax.psum(rows_sum, "clips").astype(F32)]
    me = lax.axis_index("clips")
    depth = rows_sum.shape[0] // size
    pieces = [
        lax.dynamic_slice_in_dim(rows_sum, (me ^ step) * depth, depth, axis=0)
        for step in range(size)
    ]
    got = to_partners(pieces[1:], "clips")
    return share_with_clips(pieces[0], got)


def share_with_clips(own, got):
    total = own.astype(F32)
    for piece in got:
        total = total + piece.astype(F32)
    total = total.astype(BF16)
    return [total] + to_partners([total] * len(got), "clips")


def on_device(
    slow_input,
    fast_input,
    slow_cotangent,
    fast_cotangent,
    clip_counts,
    lateral_weight,
    slow_reduce_one,
    slow_spatial_one,
    slow_expand_one,
    slow_shortcut_one,
    fast_reduce_one,
    fast_spatial_one,
    fast_expand_one,
    slow_reduce_two,
    slow_spatial_two,
    slow_expand_two,
    fast_reduce_two,
    fast_spatial_two,
    fast_expand_two,
    slow_norms_one,
    fast_norms_one,
    slow_norms_two,
    fast_norms_two,
):
    geo = Geometry(slow_input.shape, fast_input.shape)
    rows, groups = geo.rows, geo.groups
    half_rows = rows // 2
    count = lax.axis_size("ha") * lax.axis_size("wa")
    spread = spread_count()
    slow_wide = slow_input.shape[-1]
    fast_wide = PHASES * fast_input.shape[-1]
    wide = slow_wide + fast_wide
    mid = slow_reduce_one.shape[-1]
    fast_part = fast_reduce_one.shape[-1]
    fast_mid = PHASES * fast_part
    small = mid + fast_mid
    lat = lateral_weight.shape[-1]
    blocks = slow_wide // mid

    depth_one = slow_reduce_one.shape[1]
    depth_two = slow_reduce_two.shape[1]
    depth_mid = slow_spatial_one.shape[2]
    depth_lat = lateral_weight.shape[1]
    near = gather_pack([slow_reduce_one.reshape(-1, mid), slow_spatial_one.reshape(-1, mid)])
    far = gather_pack(
        [
            columns(slow_expand_one, mid),
            columns(slow_shortcut_one, mid),
            slow_reduce_two.reshape(-1, mid),
        ]
    )
    last = gather_pack([slow_spatial_two.reshape(-1, mid), columns(slow_expand_two, mid)])
    at_space_one = 3 * depth_one
    at_short = blocks * depth_mid
    at_reduce_two = at_short + blocks * depth_one
    at_space_two = 0
    at_expand_two = 9 * depth_mid
    fast_shards_one = (fast_reduce_one, fast_spatial_one, fast_expand_one)
    fast_shards_two = (fast_reduce_two, fast_spatial_two, fast_expand_two)
    compact = early_gather(fast_shards_one, fast_shards_two, lateral_weight)
    structured = [
        ((fast_wide, fast_mid), BF16, "hbm"),
        ((fast_wide // PHASES, fast_mid), BF16, "hbm"),
        ((fast_wide // PHASES, fast_mid), BF16, "hbm"),
        ((9, fast_mid, fast_mid), BF16, "hbm"),
        ((fast_mid, fast_wide), BF16, "hbm"),
    ]
    joint_outs = [((2, lanes), F32, "hbm") for lanes in (small, small, wide)]
    prepared = run(
        prepare_kernel,
        structured * 2
        + [((lateral_weight.shape[0], fast_wide // PHASES, lat), BF16, "hbm")]
        + joint_outs * 2
        + [((2, slow_wide), F32, "hbm")],
        vmem=(*compact, slow_norms_one, fast_norms_one, slow_norms_two, fast_norms_two),
    )
    fast_one, fast_two, lateral = prepared[:5], prepared[5:10], prepared[10]
    params_one, params_two, params_short = prepared[11:14], prepared[14:17], prepared[17]

    held = clip_counts[0]
    clips = direct_sum(jnp.full((1, 128), held, F32), "clips")[0, 0]
    positions = clips * (SUB * geo.frames * count)
    inv_n = jnp.stack([1.0 / positions, 1.0 / (positions * PHASES)])
    ha, wa = lax.axis_index("ha"), lax.axis_index("wa")
    last_ha = jnp.full_like(ha, lax.axis_size("ha") - 1)
    meta = jnp.stack([held * geo.frames, ha, wa, last_ha, lax.axis_index("clips")])
    scalars = (meta, inv_n)

    slow_x = slow_input.reshape(rows, slow_wide)
    fast_x = split_phases(fast_input)
    cot = jnp.concatenate(
        [slow_cotangent.reshape(rows, slow_wide), split_phases(fast_cotangent)], axis=1
    )
    message_out = ((2 * rows, small), BF16, "hbm")
    stats_small = ((spread, 2, small), F32, "spread")
    stats_wide = ((spread, 2, wide), F32, "spread")
    stats_both = ((spread, 2, wide + slow_wide), F32, "spread")
    small_out = ((rows, small), F32, "hbm")
    wide_out = ((rows, wide), F32, "hbm")

    def lateral_kernel(x_ref, k_ref, main_ref, before_ref, after_ref, united_ref, fast_ref):
        lanes = x_ref.shape[1] // PHASES
        x = x_ref[...]
        main = dot(x[:, : 3 * lanes], k_ref[2:5].reshape(3 * lanes, lat))
        past = dot(x[:, 2 * lanes :], k_ref[0:2].reshape(2 * lanes, lat))
        united_ref[...] = (main + geo.shift(past, 1)).astype(BF16)
        fast_ref[...] = fast_conv(geo, x, main_ref[...], before_ref[...], after_ref[...])

    united, za_fast = run(
        lateral_kernel,
        [((rows, lat), BF16, "hbm"), ((rows, fast_mid), F32, "hbm")],
        saved=(fast_x, lateral, *fast_one[:3]),
    )

    def reduce_one_kernel(
        meta_ref, x_ref, united_ref, fast_ref, loads, za_ref, stats_ref, message_ref
    ):
        weights = [loads.get(tap) for tap in range(3)]
        za = time_conv(geo, (x_ref[...], united_ref[...]), weights)
        za = jnp.concatenate([za, fast_ref[...]], axis=1)
        za_ref[...] = za
        za_ref.send()
        za = geo.three(za)
        put_forward(stats_ref, za, meta_ref[0])
        put_message(za, message_ref)

    za_one, stats, message = run(
        reduce_one_kernel,
        [small_out, stats_small, message_out],
        smem=(meta,),
        saved=(slow_x, united, za_fast),
        weights=((near, 0, 3, depth_one),),
    )
    parts_a1 = exchange(stats)
    halo_one = exchange_halo(message, rows)

    def space_stage(za, parts_a, halo, params, gathered, offset, fast_w):
        def kernel(
            meta_ref,
            inv_ref,
            stats_ref,
            side_ref,
            up_ref,
            down_ref,
            za_ref,
            params_ref,
            fast_ref,
            loads,
            zb_ref,
            hidden_ref,
            out_stats,
        ):
            scale, shift, _, _ = affine(stats_ref, params_ref, inv_ref, mid)

            def act(value):
                return silu(geo.three(value.astype(F32)) * scale + shift)

            own = act(za_ref[...])
            hidden_ref[...] = geo.flat(own).astype(BF16)
            near_by = Neighbours(
                own,
                act(up_ref[:half_rows]),
                act(down_ref[:half_rows]),
                act(side_ref[:rows]),
                act(up_ref[half_rows:]),
                act(down_ref[half_rows:]),
                meta_ref,
                geo.width,
            )
            slow = fast = None
            for tap in range(9):
                moved = geo.flat(near_by.at(tap // 3 - 1, tap % 3 - 1)).astype(BF16)
                slow_term = dot(moved[:, :mid], loads.get(tap))
                fast_term = dot(moved[:, mid:], fast_ref[tap])
                slow = slow_term if slow is None else slow + slow_term
                fast = fast_term if fast is None else fast + fast_term
            zb = jnp.concatenate([slow, fast], axis=1)
            zb_ref[...] = zb
            zb_ref.send()
            put_forward(out_stats, geo.three(zb), meta_ref[0])

        zb, hidden, stats, stats_a = run(
            kernel,
            [small_out, ((rows, small), BF16, "hbm"), stats_small],
            smem=scalars,
            parts=(parts_a,),
            saved=(*halo, za, params, fast_w),
            weights=((gathered, offset, 9, depth_mid),),
        )
        return zb, hidden, exchange(stats), stats_a

    zb_one, ha_one, parts_b1, stats_a1 = space_stage(
        za_one, parts_a1, halo_one, params_one[0], near, at_space_one, fast_one[3]
    )

    def expand_body(inv_ref, stats_ref, zb_ref, params_ref, fast_ref, hidden_ref, zc_ref, loads):
        scale, shift, _, _ = affine(stats_ref, params_ref, inv_ref, mid)
        hidden = geo.flat(silu(geo.three(zb_ref[...]) * scale + shift)).astype(BF16)
        hidden_ref[...] = hidden
        hidden_ref.send()
        zc_ref[:, slow_wide:] = dot(hidden[:, mid:], fast_ref[...])
        for block in range(blocks):
            zc_ref[:, block * mid : (block + 1) * mid] = dot(hidden[:, :mid], loads.get(block))
        zc_ref.send()

    def expand_one_kernel(
        meta_ref,
        inv_ref,
        stats_ref,
        zb_ref,
        params_ref,
        fast_ref,
        x_ref,
        united_ref,
        loads,
        shorts,
        hidden_ref,
        zc_ref,
        short_ref,
        out_stats,
    ):
        expand_body(inv_ref, stats_ref, zb_ref, params_ref, fast_ref, hidden_ref, zc_ref, loads)
        put_forward(out_stats, geo.three(zc_ref[...]), meta_ref[0])
        for block in range(blocks):
            weight = shorts.get(block)
            value = dot(x_ref[...], weight[:slow_wide]) + dot(united_ref[...], weight[slow_wide:])
            short_ref[:, block * mid : (block + 1) * mid] = value
            put_forward(out_stats, geo.three(value), meta_ref[0], wide + block * mid)
        short_ref.send()

    hb_one, zc_one, short, stats, stats_b1 = run(
        expand_one_kernel,
        [((rows, small), BF16, "hbm"), wide_out, ((rows, slow_wide), F32, "hbm"), stats_both],
        smem=scalars,
        parts=(parts_b1,),
        saved=(zb_one, params_one[1], fast_one[4], slow_x, united),
        weights=((far, 0, blocks, depth_mid), (far, at_short, blocks, depth_one)),
    )
    parts_c1 = exchange(stats)

    def reduce_two_kernel(
        meta_ref,
        inv_ref,
        stats_ref,
        zc_ref,
        short_ref,
        params_ref,
        short_params_ref,
        x_ref,
        main_ref,
        before_ref,
        after_ref,
        loads,
        sum_ref,
        low_ref,
        za_ref,
        out_stats,
        message_ref,
    ):
        scale, shift, _, _ = affine(stats_ref, params_ref, inv_ref, slow_wide, 0, wide)
        scale_s, shift_s, _, _ = affine(
            stats_ref, short_params_ref, inv_ref, slow_wide, wide, wide + slow_wide
        )
        normed = geo.three(zc_ref[...]) * scale + shift
        slow = normed[..., :slow_wide] + (geo.three(short_ref[...]) * scale_s + shift_s)
        fast = normed[..., slow_wide:] + geo.three(x_ref[...].astype(F32))
        total = jnp.concatenate([slow, fast], axis=-1)
        sum_ref[...] = geo.flat(total)
        sum_ref.send()
        low = geo.flat(silu(total)).astype(BF16)
        low_ref[...] = low
        low_ref.send()
        weights = [loads.get(tap) for tap in range(3)]
        za = time_conv(geo, (low[:, :slow_wide],), weights)
        fast_za = fast_conv(
            geo, low[:, slow_wide:], main_ref[...], before_ref[...], after_ref[...]
        )
        za = jnp.concatenate([za, fast_za], axis=1)
        za_ref[...] = za
        za_ref.send()
        za = geo.three(za)
        put_forward(out_stats, za, meta_ref[0])
        put_message(za, message_ref)

    sum_one, low_one, za_two, stats, message, stats_c1 = run(
        reduce_two_kernel,
        [wide_out, ((rows, wide), BF16, "hbm"), small_out, stats_small, message_out],
        smem=scalars,
        parts=(parts_c1,),
        saved=(zc_one, short, params_one[2], params_short, fast_x, *fast_two[:3]),
        weights=((far, at_reduce_two, 3, depth_two),),
    )
    parts_a2 = exchange(stats)
    halo_two = exchange_halo(message, rows)
    zb_two, ha_two, parts_b2, stats_a2 = space_stage(
        za_two, parts_a2, halo_two, params_two[0], last, at_space_two, fast_two[3]
    )

    def expand_two_kernel(
        meta_ref,
        inv_ref,
        stats_ref,
        zb_ref,
        params_ref,
        fast_ref,
        loads,
        hidden_ref,
        zc_ref,
        out_stats,
    ):
        expand_body(inv_ref, stats_ref, zb_ref, params_ref, fast_ref, hidden_ref, zc_ref, loads)
        put_forward(out_stats, geo.three(zc_ref[...]), meta_ref[0])

    hb_two, zc_two, stats, stats_b2 = run(
        expand_two_kernel,
        [((rows, small), BF16, "hbm"), wide_out, stats_wide],
        smem=scalars,
        parts=(parts_b2,),
        saved=(zb_two, params_two[1], fast_two[4]),
        weights=((last, at_expand_two, blocks, depth_mid),),
    )
    parts_c2 = exchange(stats)

    def head_kernel(
        meta_ref, inv_ref, stats_ref, zc_ref, params_ref, sum_ref, cot_ref, out_ref, g_ref, sums_ref
    ):
        scale, shift, mean, inv = affine(stats_ref, params_ref, inv_ref, slow_wide)
        zc = geo.three(zc_ref[...])
        total = zc * scale + shift + silu(geo.three(sum_ref[...]))
        valid = mask_groups(total.shape, meta_ref[0])
        sigma = jax.nn.sigmoid(total)
        out_ref[...] = geo.flat(jnp.where(valid, total * sigma, 0.0)).astype(BF16)
        slopes = sigma * (1.0 + total * (1.0 - sigma))
        gradient = jnp.where(valid, geo.three(cot_ref[...].astype(F32)) * slopes, 0.0)
        out_ref.send()
        g_ref[...] = geo.flat(gradient)
        g_ref.send()
        put_back(sums_ref, gradient, (zc - mean) * inv)

    outputs, g_two, sums, stats_c2 = run(
        head_kernel,
        [((rows, wide), BF16, "hbm"), wide_out, stats_wide],
        smem=scalars,
        parts=(parts_c2,),
        saved=(zc_two, params_two[2], sum_one, cot),
    )
    parts_c2 = exchange(sums)

    def norm_back(gradient, value, coeffs, sums, valid):
        scale, _, mean, inv = coeffs
        crossed = (value - mean) * inv * sums[0] + sums[1]
        return scale * (gradient - jnp.where(valid, crossed, 0.0))

    def expand_back_body(
        meta_ref,
        inv_ref,
        sums_ref,
        stats_ref,
        stats_b_ref,
        g_ref,
        zc_ref,
        params_ref,
        zb_ref,
        params_b_ref,
        fast_ref,
        loads,
        gz_ref,
        g_out,
        sums_out,
        message_ref,
    ):
        limit = meta_ref[0]
        coeffs = affine(stats_ref, params_ref, inv_ref, slow_wide, 0, wide)
        both = [back_rows(sums_ref, inv_ref, slow_wide, row, 0, wide) for row in range(2)]
        gradient = geo.three(g_ref[...])
        gz = norm_back(
            gradient, geo.three(zc_ref[...]), coeffs, both, mask_groups(gradient.shape, limit)
        )
        gz = geo.flat(gz).astype(BF16)
        gz_ref[...] = gz
        gz_ref.send()
        fast = dot_nt(gz[:, slow_wide:], fast_ref[...])
        slow = None
        for block in range(blocks):
            term = dot_nt(gz[:, block * mid : (block + 1) * mid], loads.get(block))
            slow = term if slow is None else slow + term
        scale, shift, mean, inv = affine(stats_b_ref, params_b_ref, inv_ref, mid)
        zb = geo.three(zb_ref[...])
        back = geo.three(jnp.concatenate([slow, fast], axis=1)) * slope(zb * scale + shift)
        g_out[...] = geo.flat(back)
        g_out.send()
        masked = jnp.where(mask_groups(back.shape, limit), back, 0.0)
        put_back(sums_out, masked, (zb - mean) * inv)
        put_message(jnp.concatenate([back, zb], axis=-1), message_ref)
        return gradient

    message_back = ((2 * rows, 2 * small), BF16, "hbm")
    gz_c2, g_b2, sums, message, sums_c2 = run(
        expand_back_body,
        [((rows, wide), BF16, "hbm"), small_out, stats_small, message_back],
        smem=scalars,
        parts=(parts_c2,),
        saved=(stats_c2, stats_b2, g_two, zc_two, params_two[2], zb_two, params_two[1], fast_two[4]),
        weights=((last, at_expand_two, blocks, depth_mid),),
    )
    parts_b2 = exchange(sums)
    halo_back_two = exchange_halo(message, rows)

    lanes_fast = fast_wide // PHASES
    fast_rows_count = fast_reduce_one.shape[1] + 2 * SUB

    def expand_grad(hb_ref, gz_ref, out_ref, at):
        for block in range(blocks):
            value = dot_tn(hb_ref[:, :mid], gz_ref[:, block * mid : (block + 1) * mid])
            low = at + block * depth_mid
            out_ref[:, low : low + depth_mid, :] = value.astype(BF16).reshape(
                count, depth_mid, mid
            )

    def fast_expand_grad(hb_ref, gz_ref):
        fast = dot_tn(hb_ref[:, mid:], gz_ref[:, slow_wide:])
        total = None
        for phase in range(PHASES):
            part = fast[
                phase * fast_part : (phase + 1) * fast_part,
                phase * lanes_fast : (phase + 1) * lanes_fast,
            ]
            total = part if total is None else total + part
        return total

    def space_grad(ha_ref, taps_ref, out_ref, at):
        fast_grads = []
        for tap in range(9):
            value = dot_tn(ha_ref[:, :mid], taps_ref[tap, :, :mid])
            low = at + tap * depth_mid
            out_ref[:, low : low + depth_mid, :] = value.astype(BF16).reshape(
                count, depth_mid, mid
            )
            fast = dot_tn(ha_ref[:, mid:], taps_ref[tap, :, mid:])
            total = None
            for phase in range(PHASES):
                part = lane_block(
                    fast[phase * fast_part : (phase + 1) * fast_part], phase, fast_part
                )
                total = part if total is None else total + part
            fast_grads.append(total)
        return fast_grads

    def put_fast(reduce, space, expand, out_ref, at):
        lane = lax.broadcasted_iota(jnp.int32, reduce[0].shape, 1)

        def beside(parts):
            keep = lane[: parts[0].shape[0]]
            total = None
            for place, part in enumerate(parts):
                part = jnp.where(keep < fast_part, part, 0.0)
                part = pltpu.roll(part, place * fast_part, 1) if place else part
                total = part if total is None else total + part
            return total

        depth = reduce[0].shape[0] // count
        taps = beside(reduce).astype(BF16).reshape(count, depth, lanes_fast)
        out_ref[:, at : at + depth, :] = jnp.concatenate([taps, jnp.zeros_like(taps)], axis=-1)

        def spread(value):
            tiles = value.reshape(count // 2, SUB, lanes_fast)
            return jnp.stack([tiles, pltpu.roll(tiles, SUB // 2, 1)], axis=1).reshape(
                count, SUB, lanes_fast
            )

        first = jnp.concatenate([spread(beside(space[0:4])), spread(beside(space[4:8]))], axis=-1)
        second = jnp.concatenate([spread(beside(space[8:9])), spread(expand)], axis=-1)
        both = jnp.concatenate([first, second], axis=1).astype(BF16)
        out_ref[:, at + depth : at + depth + 2 * SUB, :] = both

    def space_back_stage(
        g, zb, za, halo, stats_b, parts_b, params_b, stats_a, params_a, g_hbm, at, fast_w
    ):
        def kernel(
            meta_ref,
            inv_ref,
            sums_b_ref,
            side_ref,
            up_ref,
            down_ref,
            stats_b_ref,
            stats_a_ref,
            g_ref,
            zb_ref,
            za_ref,
            params_b_ref,
            params_a_ref,
            fast_ref,
            loads,
            taps_ref,
            g_out,
            sums_out,
        ):
            limit = meta_ref[0]
            coeffs = affine(stats_b_ref, params_b_ref, inv_ref, mid)
            both = [back_rows(sums_b_ref, inv_ref, mid, row) for row in range(2)]

            def back(gradient, value, scale):
                valid = mask_groups(gradient.shape, limit, scale)
                return norm_back(gradient, value, coeffs, both, valid)

            def halo_back(value, scale):
                value = geo.three(value.astype(F32))
                return back(value[..., :small], value[..., small:], scale)

            near_by = Neighbours(
                back(geo.three(g_ref[...]), geo.three(zb_ref[...]), 1),
                halo_back(up_ref[:half_rows], 2),
                halo_back(down_ref[:half_rows], 2),
                halo_back(side_ref[:rows], 1),
                halo_back(up_ref[half_rows:], 2),
                halo_back(down_ref[half_rows:], 2),
                meta_ref,
                geo.width,
            )
            slow = fast = None
            for tap in range(9):
                moved = geo.flat(near_by.at(1 - tap // 3, 1 - tap % 3)).astype(BF16)
                taps_ref[tap] = moved
                if tap == 8:
                    taps_ref.send()
                slow_term = dot_nt(moved[:, :mid], loads.get(tap))
                fast_term = dot_nt(moved[:, mid:], fast_ref[tap])
                slow = slow_term if slow is None else slow + slow_term
                fast = fast_term if fast is None else fast + fast_term
            scale, shift, mean, inv = affine(stats_a_ref, params_a_ref, inv_ref, mid)
            za = geo.three(za_ref[...])
            result = geo.three(jnp.concatenate([slow, fast], axis=1)) * slope(za * scale + shift)
            g_out[...] = geo.flat(result)
            g_out.send()
            masked = jnp.where(mask_groups(result.shape, limit), result, 0.0)
            put_back(sums_out, masked, (za - mean) * inv)

        taps, g, sums, sums_b = run(
            kernel,
            [((9, rows, small), BF16, "hbm"), small_out, stats_small],
            smem=scalars,
            parts=(parts_b,),
            saved=(*halo, stats_b, stats_a, g, zb, za, params_b, params_a, fast_w),
            weights=((g_hbm, at, 9, depth_mid),),
        )
        return taps, g, exchange(sums), sums_b

    taps_two, g_a2, parts_a2, sums_b2 = space_back_stage(
        g_b2,
        zb_two,
        za_two,
        halo_back_two,
        stats_b2,
        parts_b2,
        params_two[1],
        stats_a2,
        params_two[0],
        last,
        at_space_two,
        fast_two[3],
    )
    def reduce_gz(meta_ref, inv_ref, g_ref, za_ref, stats_ref, sums_ref, params_ref, steps_ref):
        coeffs = affine(stats_ref, params_ref, inv_ref, mid)
        both = [back_rows(sums_ref, inv_ref, mid, row) for row in range(2)]
        gradient = geo.three(g_ref[...])
        gz = norm_back(
            gradient,
            geo.three(za_ref[...]),
            coeffs,
            both,
            mask_groups(gradient.shape, meta_ref[0]),
        )
        gz = geo.flat(gz)
        steps = [geo.shift(gz, -1).astype(BF16), gz.astype(BF16), geo.shift(gz, 1).astype(BF16)]
        for tap in range(3):
            steps_ref[tap] = steps[tap]
        if isinstance(steps_ref, Store):
            steps_ref.send()
        return steps

    def reduce_back_two_kernel(
        meta_ref,
        inv_ref,
        sums_ref,
        stats_ref,
        stats_c_ref,
        g_ref,
        za_ref,
        params_ref,
        g_two_ref,
        sum_ref,
        zc_ref,
        short_ref,
        main_ref,
        before_ref,
        after_ref,
        loads,
        steps_ref,
        g_out,
        sums_out,
    ):
        steps = reduce_gz(
            meta_ref, inv_ref, g_ref, za_ref, stats_ref, sums_ref, params_ref, steps_ref
        )
        slow = None
        for tap in range(3):
            term = dot_nt(steps[tap][:, :mid], loads.get(tap))
            slow = term if slow is None else slow + term
        fast = fast_conv_back(
            [step[:, mid:] for step in steps], main_ref[...], before_ref[...], after_ref[...]
        )
        back = jnp.concatenate([slow, fast], axis=1) + g_two_ref[...]
        back = geo.three(back * slope(sum_ref[...]))
        g_out[...] = geo.flat(back)
        g_out.send()
        masked = jnp.where(mask_groups(back.shape, meta_ref[0]), back, 0.0)
        mean, inv = moments(stats_c_ref, inv_ref, slow_wide, 0, wide)
        put_back(sums_out, masked, (geo.three(zc_ref[...]) - mean) * inv)
        mean, inv = moments(stats_c_ref, inv_ref, slow_wide, wide, wide + slow_wide)
        masked = masked[..., :slow_wide]
        put_back(sums_out, masked, (geo.three(short_ref[...]) - mean) * inv, wide)

    steps_two, g_one, sums, sums_a2 = run(
        reduce_back_two_kernel,
        [((3, rows, small), BF16, "hbm"), wide_out, stats_both],
        smem=scalars,
        parts=(parts_a2,),
        saved=(stats_a2, stats_c1, g_a2, za_two, params_two[0], g_two, sum_one, zc_one, short, *fast_two[:3]),
        weights=((far, at_reduce_two, 3, depth_two),),
    )
    parts_c1 = exchange(sums)

    def grads_two_kernel(hb_ref, gz_ref, ha_ref, taps_ref, low_ref, steps_ref, out_ref):
        for tap in range(3):
            value = dot_tn(low_ref[:, :slow_wide], steps_ref[tap, :, :mid])
            out_ref[:, tap * depth_two : (tap + 1) * depth_two, :] = value.astype(BF16).reshape(
                count, depth_two, mid
            )
        at = 3 * depth_two
        space = space_grad(ha_ref, taps_ref, out_ref, at)
        at += 9 * depth_mid
        expand_grad(hb_ref, gz_ref, out_ref, at)
        at += blocks * depth_mid
        reduce = fast_reduce_grad(
            low_ref[:, slow_wide:], [steps_ref[tap, :, mid:] for tap in range(3)]
        )
        put_fast(reduce, space, fast_expand_grad(hb_ref, gz_ref), out_ref, at)

    rows_two = 3 * depth_two + (9 + blocks) * depth_mid + fast_rows_count
    (packed_two,) = run(
        grads_two_kernel,
        [((count, rows_two, mid), BF16, "hbm")],
        saved=(hb_two, gz_c2, ha_two, taps_two, low_one, steps_two),
    )
    sum_two = lax.psum_scatter(packed_two, TILE, scatter_dimension=0, tiled=False)
    parts_two = sum_over_clips(sum_two)

    def expand_back_one_kernel(*refs):
        *body, short_ref, short_params_ref, loads, gz_ref, g_out, sums_out, message, gs_ref = refs
        gradient = expand_back_body(*body, loads, gz_ref, g_out, sums_out, message)
        meta_ref, inv_ref, sums_ref, stats_ref = body[:4]
        low, high = wide, wide + slow_wide
        coeffs = affine(stats_ref, short_params_ref, inv_ref, slow_wide, low, high)
        both = [back_rows(sums_ref, inv_ref, slow_wide, row, low, high) for row in range(2)]
        gradient = gradient[..., :slow_wide]
        valid = mask_groups(gradient.shape, meta_ref[0])
        gs = norm_back(gradient, geo.three(short_ref[...]), coeffs, both, valid)
        gs_ref[...] = geo.flat(gs).astype(BF16)

    gz_c1, g_b1, sums, message, gz_short, sums_c1 = run(
        expand_back_one_kernel,
        [((rows, wide), BF16, "hbm"), small_out, stats_small, message_back]
        + [((rows, slow_wide), BF16, "hbm")],
        smem=scalars,
        parts=(parts_c1,),
        saved=(stats_c1, stats_b1, g_one, zc_one, params_one[2], zb_one, params_one[1], fast_one[4])
        + (short, params_short),
        weights=((far, 0, blocks, depth_mid),),
    )
    parts_b1 = exchange(sums)
    halo_back_one = exchange_halo(message, rows)
    joined_lanes = slow_wide + lat

    def grads_mid_kernel(x_ref, united_ref, gs_ref, hb_ref, gz_ref, loads, out_ref, back_ref):
        for block in range(blocks):
            gs = gs_ref[:, block * mid : (block + 1) * mid]
            value = jnp.concatenate([dot_tn(x_ref[...], gs), dot_tn(united_ref[...], gs)], axis=0)
            out_ref[:, block * depth_one : (block + 1) * depth_one, :] = value.astype(
                BF16
            ).reshape(count, depth_one, mid)
            term = dot_nt(gs, loads.get(block))
            back_ref[...] = term if block == 0 else back_ref[...] + term
        expand_grad(hb_ref, gz_ref, out_ref, blocks * depth_one)

    packed_mid, short_back = run(
        grads_mid_kernel,
        [((count, blocks * (depth_one + depth_mid), mid), BF16, "hbm")]
        + [((rows, joined_lanes), F32, "hbm")],
        saved=(slow_x, united, gz_short, hb_one, gz_c1),
        weights=((far, at_short, blocks, depth_one),),
    )
    sum_mid = lax.psum_scatter(packed_mid, TILE, scatter_dimension=0, tiled=False)
    parts_mid = sum_over_clips(sum_mid)

    taps_one, g_a1, parts_a1, sums_b1 = space_back_stage(
        g_b1,
        zb_one,
        za_one,
        halo_back_one,
        stats_b1,
        parts_b1,
        params_one[1],
        stats_a1,
        params_one[0],
        near,
        at_space_one,
        fast_one[3],
    )
    def last_kernel(
        meta_ref,
        inv_ref,
        sums_ref,
        stats_ref,
        g_ref,
        za_ref,
        params_ref,
        g_one_ref,
        short_ref,
        lateral_ref,
        main_ref,
        before_ref,
        after_ref,
        loads,
        steps_ref,
        slow_ref,
        fast_ref,
        united_ref,
    ):
        steps = reduce_gz(
            meta_ref, inv_ref, g_ref, za_ref, stats_ref, sums_ref, params_ref, steps_ref
        )
        joined = short_ref[...]
        for tap in range(3):
            joined = joined + dot_nt(steps[tap][:, :mid], loads.get(tap))
        slow_ref[...] = joined[:, :slow_wide]
        tail = joined[:, slow_wide:]
        now, past = tail.astype(BF16), geo.shift(tail, -1).astype(BF16)
        united_ref[0] = now
        united_ref[1] = past
        lanes = fast_wide // PHASES
        fast = fast_conv_back(
            [step[:, mid:] for step in steps], main_ref[...], before_ref[...], after_ref[...]
        )
        fast = fast + g_one_ref[:, slow_wide:]
        front = dot_nt(now, lateral_ref[2:5].reshape(3 * lanes, lat))
        back = dot_nt(past, lateral_ref[0:2].reshape(2 * lanes, lat))
        fast_ref[:, : 2 * lanes] = fast[:, : 2 * lanes] + front[:, : 2 * lanes]
        fast_ref[:, 2 * lanes : 3 * lanes] = (
            fast[:, 2 * lanes : 3 * lanes] + front[:, 2 * lanes :] + back[:, :lanes]
        )
        fast_ref[:, 3 * lanes :] = fast[:, 3 * lanes :] + back[:, lanes:]

    steps_one, grad_slow, grad_fast, united_low, sums_a1 = run(
        last_kernel,
        [
            ((3, rows, small), BF16, "hbm"),
            ((rows, slow_wide), F32, "hbm"),
            ((rows, fast_wide), F32, "hbm"),
            ((2, rows, lat), BF16, "hbm"),
        ],
        smem=scalars,
        parts=(parts_a1,),
        saved=(stats_a1, g_a1, za_one, params_one[0], g_one, short_back, lateral, *fast_one[:3]),
        weights=((near, 0, 3, depth_one),),
    )

    def grads_one_kernel(
        meta_ref,
        steps_ref,
        low_ref,
        x_ref,
        united_ref,
        fast_x_ref,
        ha_ref,
        taps_ref,
        hb_ref,
        gz_ref,
        own_ref,
        send_ref,
        out_ref,
        sems,
    ):
        lanes = fast_wide // PHASES
        for tap in range(3):
            step = steps_ref[tap, :, :mid]
            value = jnp.concatenate(
                [dot_tn(x_ref[...], step), dot_tn(united_ref[...], step)], axis=0
            )
            out_ref[:, tap * depth_one : (tap + 1) * depth_one, :] = value.astype(BF16).reshape(
                count, depth_one, mid
            )
        at = 3 * depth_one
        past = dot_tn(fast_x_ref[:, 2 * lanes :], low_ref[1])
        now = dot_tn(fast_x_ref[:, : 3 * lanes], low_ref[0])
        both = jnp.concatenate([past, now], axis=0).astype(BF16)
        for tap in range(5):
            out_ref[:, at + tap * depth_lat : at + (tap + 1) * depth_lat, :] = both[
                tap * lanes : (tap + 1) * lanes
            ].reshape(count, depth_lat, lat)
        at += 5 * depth_lat
        space = space_grad(ha_ref, taps_ref, out_ref, at)
        at += 9 * depth_mid
        reduce = fast_reduce_grad(
            fast_x_ref[...], [steps_ref[tap, :, mid:] for tap in range(3)]
        )
        put_fast(reduce, space, fast_expand_grad(hb_ref, gz_ref), out_ref, at)

        put_blocks(out_ref, own_ref, send_ref, meta_ref[1], meta_ref[2], sems)

    def put_blocks(blocks_ref, own_ref, send_ref, ha, wa, sems):
        for block in range(count):
            place, col = ha ^ (block // 2), block % 2
            source, sem = blocks_ref.at[block], sems.at[block]

            @pl.when(wa == col)
            def _():
                pltpu.make_async_copy(source, own_ref.at[place], sem).start()

            @pl.when(wa != col)
            def _():
                pltpu.make_async_copy(source, send_ref.at[place], sem).start()

        for block in range(count):
            pltpu.make_async_copy(blocks_ref.at[block], own_ref.at[0], sems.at[block]).wait()

    high = count // 2
    rows_one = 3 * depth_one + 5 * depth_lat + 9 * depth_mid + fast_rows_count
    rows_late = rows_one + -rows_one % (16 * lax.axis_size("clips"))
    blocks_out = ((high, rows_late, mid), BF16, "raw")
    own_blocks, send_blocks = run(
        grads_one_kernel,
        [blocks_out, blocks_out],
        smem=(meta,),
        saved=(steps_one, united_low, slow_x, united, fast_x, ha_one, taps_one, hb_one, gz_c1),
        scratch=(
            pltpu.VMEM((count, rows_late, mid), BF16),
            pltpu.SemaphoreType.DMA((count,)),
        ),
    )
    side_blocks = lax.ppermute(send_blocks, "wa", xor_pairs(2, 1))

    def chip_kernel(own_ref, side_ref, *out_refs):
        for place in range(high):
            total = own_ref[place].astype(F32) + side_ref[place].astype(F32)
            out_refs[place][...] = total.astype(BF16)
            out_refs[place].send()

    late_out = ((rows_late, mid), BF16, "hbm")
    chip_sums = run(chip_kernel, [late_out] * high, saved=(own_blocks, side_blocks))
    late = [chip_sums[0]] + to_partners(chip_sums[1:], "ha")
    clip_size = lax.axis_size("clips")
    if clip_size <= 4:
        depth = rows_late // clip_size

        def quarter_kernel(meta_ref, *refs):
            ins, outs, total_ref = refs[:high], refs[high:-1], refs[-1]
            total = ins[0][...].astype(F32)
            for ref in ins[1:]:
                total = total + ref[...].astype(F32)
            total_ref[...] = total.astype(BF16)
            for step in range(clip_size):
                start = pl.multiple_of((meta_ref[4] ^ step) * depth, 16)
                outs[step][...] = total_ref[pl.ds(start, depth), :]
                outs[step].send()

        quarters = run(
            quarter_kernel,
            [((depth, mid), BF16, "hbm")] * clip_size,
            smem=(meta,),
            saved=late,
            scratch=(pltpu.VMEM((rows_late, mid), BF16),),
        )
        parts_one = share_with_clips(quarters[0], to_partners(quarters[1:], "clips"))
    else:
        parts_one = sum_over_clips(sum(part.astype(F32) for part in late).astype(BF16))

    def finish(parts, shapes):
        depth = parts[0].shape[0]
        rows_all = depth * len(parts)

        def kernel(meta_ref, *refs):
            ins, outs, total_ref = refs[: len(parts)], refs[len(parts) : -1], refs[-1]
            for step, ref in enumerate(ins):
                place = (meta_ref[4] ^ step) if len(parts) > 1 else 0
                start = pl.multiple_of(place * depth, 16)
                total_ref[pl.ds(start, depth), :] = ref[...].astype(F32)
            at = 0
            for out in outs:
                shape = out.scratch.shape
                if len(shape) == 2 and shape[1] > mid:
                    for block in range(shape[1] // mid):
                        out[:, block * mid : (block + 1) * mid] = total_ref[at : at + shape[0], :]
                        at += shape[0]
                else:
                    number = 1
                    for length in shape[:-1]:
                        number *= length
                    out[...] = total_ref[at : at + number, :].reshape(shape)
                    at += number
                out.send()

        return run(
            kernel,
            [(shape, F32, "hbm") for shape in shapes],
            smem=(meta,),
            saved=parts,
            scratch=(pltpu.VMEM((rows_all, mid), F32),),
        )

    def fast_shards_of(block, reduce, space, expand):
        depth, lanes = reduce.shape[1:]
        taps = jnp.moveaxis(block[:depth, : 3 * lanes].reshape(depth, 3, lanes), 1, 0)
        few = space.shape[2]
        first = block[depth : depth + few].reshape(few, SUB, lanes)
        second = block[depth + SUB : depth + SUB + few]
        spatial = jnp.concatenate([first, second[:, None, :lanes]], axis=1)
        spatial = jnp.moveaxis(spatial, 1, 0).reshape(space.shape)
        return taps, spatial, second[:, expand.shape[1] :]

    fast_block = (fast_rows_count, mid)
    grad_slow_reduce_two, grad_slow_spatial_two, grad_slow_expand_two, block = finish(
        parts_two,
        [slow_reduce_two.shape, slow_spatial_two.shape, slow_expand_two.shape, fast_block],
    )
    fast_two_grads = fast_shards_of(block, *fast_shards_two)
    grad_slow_shortcut, grad_slow_expand_one = finish(
        parts_mid, [slow_shortcut_one.shape, slow_expand_one.shape]
    )
    grad_slow_reduce_one, grad_lateral, grad_slow_spatial_one, block = finish(
        parts_one,
        [slow_reduce_one.shape, lateral_weight.shape, slow_spatial_one.shape, fast_block],
    )
    fast_one_grads = fast_shards_of(block, *fast_shards_one)

    def norm_grads(first, second, third):
        slow = [first[:, :mid], second[:, :mid], third[:, :slow_wide]]
        fast = [first[:, mid:], second[:, mid:], third[:, slow_wide:wide]]
        fast = [jnp.sum(part.reshape(2, PHASES, -1), axis=1) for part in fast]
        return slow, fast

    slow_one_p, fast_one_p = norm_grads(sums_a1, sums_b1, sums_c1)
    slow_two_p, fast_two_p = norm_grads(sums_a2, sums_b2, sums_c2)
    grad_slow_norms_one = jnp.concatenate(slow_one_p + [sums_c1[:, wide:]], axis=1)
    grad_slow_norms_two = jnp.concatenate(slow_two_p, axis=1)
    grad_fast_norms_one = jnp.concatenate(fast_one_p, axis=1)
    grad_fast_norms_two = jnp.concatenate(fast_two_p, axis=1)
    return (
        outputs[:, :slow_wide].reshape(slow_input.shape),
        join_phases(outputs[:, slow_wide:], fast_input.shape),
        grad_slow.reshape(slow_input.shape),
        join_phases(grad_fast, fast_input.shape),
        grad_lateral,
        grad_slow_reduce_one,
        grad_slow_spatial_one,
        grad_slow_expand_one,
        grad_slow_shortcut,
        *fast_one_grads,
        grad_slow_reduce_two,
        grad_slow_spatial_two,
        grad_slow_expand_two,
        *fast_two_grads,
        grad_slow_norms_one,
        grad_fast_norms_one,
        grad_slow_norms_two,
        grad_fast_norms_two,
    )


def solution(mesh):
    in_specs = (
        P("clips", None, "ha", "wa", None),
        P("clips", None, "ha", "wa", None),
        P("clips", None, "ha", "wa", None),
        P("clips", None, "ha", "wa", None),
        P("clips"),
        P(None, ("ha", "wa"), None),
        P(None, ("ha", "wa"), None),
        P(None, None, ("ha", "wa"), None),
        P(("ha", "wa"), None),
        P(("ha", "wa"), None),
        P(None, ("ha", "wa"), None),
        P(None, None, ("ha", "wa"), None),
        P(("ha", "wa"), None),
        P(None, ("ha", "wa"), None),
        P(None, None, ("ha", "wa"), None),
        P(("ha", "wa"), None),
        P(None, ("ha", "wa"), None),
        P(None, None, ("ha", "wa"), None),
        P(("ha", "wa"), None),
        P(),
        P(),
        P(),
        P(),
    )
    out_specs = (
        P("clips", None, "ha", "wa", None),
        P("clips", None, "ha", "wa", None),
        P("clips", None, "ha", "wa", None),
        P("clips", None, "ha", "wa", None),
        P(None, ("ha", "wa"), None),
        P(None, ("ha", "wa"), None),
        P(None, None, ("ha", "wa"), None),
        P(("ha", "wa"), None),
        P(("ha", "wa"), None),
        P(None, ("ha", "wa"), None),
        P(None, None, ("ha", "wa"), None),
        P(("ha", "wa"), None),
        P(None, ("ha", "wa"), None),
        P(None, None, ("ha", "wa"), None),
        P(("ha", "wa"), None),
        P(None, ("ha", "wa"), None),
        P(None, None, ("ha", "wa"), None),
        P(("ha", "wa"), None),
        P(),
        P(),
        P(),
        P(),
    )
    return jax.shard_map(
        on_device, mesh=mesh, in_specs=in_specs, out_specs=out_specs, check_vma=False
    )
```

```python
import jax
import jax.numpy as jnp
from jax import lax
from jax.experimental import pallas as pl
from jax.experimental.pallas import tpu as pltpu
from jax.sharding import PartitionSpec as P

epsilon = 1e-05
F32 = jnp.float32
BF16 = jnp.bfloat16
TILE = ("ha", "wa")
PHASES = 4
SUB = 8


def dot(left, right):
    return lax.dot_general(left, right, (((1,), (0,)), ((), ())), preferred_element_type=F32)


def dot_tn(left, right):
    return lax.dot_general(left, right, (((0,), (0,)), ((), ())), preferred_element_type=F32)


def dot_nt(left, right):
    return lax.dot_general(left, right, (((1,), (1,)), ((), ())), preferred_element_type=F32)


class Loads:
    def __init__(self, source, offset, target, sems, first):
        self.copies = []
        depth = target.shape[2]
        for step in range(target.shape[0]):
            copy = pltpu.make_async_copy(
                source.at[:, pl.ds(offset + step * depth, depth), :],
                target.at[step],
                sems.at[first + step],
            )
            copy.start()
            self.copies.append(copy)
        self.target = target

    def get(self, step):
        self.copies[step].wait()
        block = self.target[step]
        return block.reshape(-1, block.shape[-1])


class Saved:
    def __init__(self, source, scratch, sem):
        self.scratch, self.shape = scratch, scratch.shape
        self.copy = pltpu.make_async_copy(source, scratch, sem)
        self.copy.start()
        self.ready = False

    def wait(self):
        if not self.ready:
            self.copy.wait()
            self.ready = True

    def __getitem__(self, index):
        self.wait()
        return self.scratch[index]


class Store:
    def __init__(self, scratch, target, sem):
        self.scratch, self.shape, self.sent = scratch, scratch.shape, False
        self.copy = pltpu.make_async_copy(scratch, target, sem)

    def send(self):
        self.copy.start()
        self.sent = True

    def __setitem__(self, index, value):
        self.scratch[index] = value

    def __getitem__(self, index):
        return self.scratch[index]


def run(body, outs, smem=(), parts=(), vmem=(), saved=(), weights=(), scratch=(), limit=56):
    near = pl.BlockSpec(memory_space=pltpu.VMEM)
    far = pl.BlockSpec(memory_space=pltpu.HBM)
    sources = []
    for array, *_ in weights:
        if not any(array is other for other in sources):
            sources.append(array)
    outs = list(outs) + [(part.shape[1:], part.dtype, "hbm") for part in parts]
    held = [pltpu.VMEM(array.shape, array.dtype) for array in saved]
    for array, _, steps, depth in weights:
        held.append(pltpu.VMEM((steps, array.shape[0], depth, array.shape[2]), array.dtype))
    for shape, dtype, kind in outs:
        if kind == "hbm":
            held.append(pltpu.VMEM(shape, dtype))
        elif kind == "spread":
            held.append(pltpu.VMEM(shape[1:], dtype))
    sems = len(saved) + sum(steps for _, _, steps, _ in weights) + len(outs)
    held.append(pltpu.SemaphoreType.DMA((sems,)))

    def kernel(*refs):
        refs = list(refs)

        def take(number):
            taken = refs[:number]
            del refs[:number]
            return taken

        smem_refs, part_refs, vmem_refs = take(len(smem)), take(len(parts)), take(len(vmem))
        saved_refs, source_refs, out_refs = take(len(saved)), take(len(sources)), take(len(outs))
        saved_scratch, weight_scratch = take(len(saved)), take(len(weights))
        out_scratch = take(sum(kind in ("hbm", "spread") for _, _, kind in outs))
        sem, more = refs[0], refs[1:]
        copies = [
            Saved(source, target, sem.at[at])
            for at, (source, target) in enumerate(zip(saved_refs, saved_scratch))
        ]
        at = len(saved)
        loads = []
        for (array, offset, steps, _), target in zip(weights, weight_scratch):
            place = [array is other for other in sources].index(True)
            loads.append(Loads(source_refs[place], offset, target, sem, at))
            at += steps
        results, stores, spreads = [], [], []
        for ref, (_, _, kind) in zip(out_refs, outs):
            if kind == "hbm":
                stores.append(Store(out_scratch.pop(0), ref, sem.at[at]))
                at += 1
                results.append(stores[-1])
            elif kind == "spread":
                spreads.append((out_scratch.pop(0), ref))
                results.append(spreads[-1][0])
            else:
                results.append(ref)
        sums = results[len(results) - len(parts) :]
        results = results[: len(results) - len(parts)]
        for part, total in zip(part_refs, sums):
            total[...] = jnp.sum(part[...], axis=0)
            total.send()
        totals = [total.scratch for total in sums]
        body(*smem_refs, *totals, *vmem_refs, *copies, *loads, *results, *more)
        for copy in copies:
            copy.wait()
        for store in stores:
            if not store.sent:
                store.send()
        for value, ref in spreads:
            ref[...] = jnp.broadcast_to(value[...][None], ref.shape)
        for store in stores:
            store.copy.wait()

    return pl.pallas_call(
        kernel,
        out_shape=[jax.ShapeDtypeStruct(shape, dtype) for shape, dtype, _ in outs],
        in_specs=[pl.BlockSpec(memory_space=pltpu.SMEM)] * len(smem)
        + [near] * (len(parts) + len(vmem))
        + [far] * (len(saved) + len(sources)),
        out_specs=[far if kind in ("hbm", "raw") else near for _, _, kind in outs],
        scratch_shapes=held + list(scratch),
        compiler_params=pltpu.CompilerParams(vmem_limit_bytes=limit * 1024 * 1024),
        cost_estimate=pl.CostEstimate(
            flops=2_000_000_000, bytes_accessed=16_000_000, transcendentals=0
        ),
    )(*smem, *parts, *vmem, *saved, *sources)


class Geometry:
    def __init__(self, slow_shape, fast_shape):
        self.cap, self.frames, self.height, self.width = slow_shape[:4]
        self.groups = self.cap * self.frames
        self.rows = self.groups * SUB

    def three(self, value):
        return value.reshape(-1, SUB, value.shape[-1])

    def flat(self, value):
        return value.reshape(-1, value.shape[-1])

    def shift(self, value, step):
        lanes = value.shape[-1]
        whole = value.reshape(self.cap, self.frames, SUB, lanes)
        zero = jnp.zeros((self.cap, 1, SUB, lanes), value.dtype)
        if step > 0:
            whole = jnp.concatenate([zero, whole[:, :-1]], axis=1)
        else:
            whole = jnp.concatenate([whole[:, 1:], zero], axis=1)
        return whole.reshape(-1, lanes)


def mask_groups(shape, limit, scale=1):
    return lax.broadcasted_iota(jnp.int32, shape, 0) * scale < limit


def rep(ref, row, low, high):
    return jnp.broadcast_to(ref[row : row + 1, low:high], (SUB, high - low))


def fold(value, slow):
    fast = value[:, slow:]
    lanes = fast.shape[-1]
    part = lanes // PHASES
    if part % 128 == 0:
        total = fast[:, :part]
        for phase in range(1, PHASES):
            total = total + fast[:, phase * part : (phase + 1) * part]
        return jnp.concatenate([value[:, :slow]] + [total] * PHASES, axis=1)
    total = fast
    for phase in range(1, PHASES):
        total = total + pltpu.roll(fast, phase * part, 1)
    return jnp.concatenate([value[:, :slow], total], axis=1)


def lane_counts(inv_ref, lanes, slow):
    lane = lax.broadcasted_iota(jnp.int32, (SUB, lanes), 1)
    return jnp.where(lane < slow, inv_ref[0], inv_ref[1])


def moments(stats, inv_ref, slow, low=0, high=None):
    high = stats.shape[1] if high is None else high
    total, square = rep(stats, 0, low, high), rep(stats, 1, low, high)
    if slow < high - low:
        total, square = fold(total, slow), fold(square, slow)
    inv_n = lane_counts(inv_ref, high - low, slow)
    mean = total * inv_n
    return mean, lax.rsqrt(square * inv_n - mean * mean + epsilon)


def affine(stats, params, inv_ref, slow, low=0, high=None):
    mean, inv = moments(stats, inv_ref, slow, low, high)
    lanes = mean.shape[1]
    scale = (1.0 + rep(params, 0, 0, lanes)) * inv
    return scale, rep(params, 1, 0, lanes) - mean * scale, mean, inv


def back_rows(sums, inv_ref, slow, row, low=0, high=None):
    high = sums.shape[1] if high is None else high
    total = rep(sums, row, low, high)
    if slow < high - low:
        total = fold(total, slow)
    return total * lane_counts(inv_ref, high - low, slow)


def silu(value):
    return value * jax.nn.sigmoid(value)


def slope(value):
    sigma = jax.nn.sigmoid(value)
    return sigma * (1.0 + value * (1.0 - sigma))


def put_stats(ref, first, second, low=0):
    lanes = first.shape[-1]
    ref[0:1, low : low + lanes] = jnp.sum(jnp.sum(first, axis=0), axis=0, keepdims=True)
    ref[1:2, low : low + lanes] = jnp.sum(jnp.sum(second, axis=0), axis=0, keepdims=True)


def put_back(ref, gradient, normal, low=0):
    put_stats(ref, gradient * normal, gradient, low)


def put_forward(ref, value, limit, low=0):
    masked = jnp.where(mask_groups(value.shape, limit), value, 0.0)
    put_stats(ref, masked, masked * value, low)


def put_message(value, ref):
    lanes = value.shape[-1]
    pairs = value.reshape(-1, 2, SUB, lanes)
    first, second = pairs[:, 0], pairs[:, 1]
    near = lax.broadcasted_iota(jnp.int32, first.shape, 1) < SUB // 2
    top = jnp.where(near, first, pltpu.roll(second, SUB // 2, 1))
    bottom = jnp.where(near, pltpu.roll(first, SUB // 2, 1), second)
    parts = [part.reshape(-1, lanes).astype(BF16) for part in (value, top, bottom)]
    at = 0
    for part in parts:
        ref[at : at + part.shape[0]] = part
        at += part.shape[0]
    ref.send()


def unpack_bottom(value):
    both = jnp.stack([pltpu.roll(value, SUB // 2, 1), value], axis=1)
    return both.reshape(-1, SUB, value.shape[-1])


def unpack_top(value):
    both = jnp.stack([value, pltpu.roll(value, SUB // 2, 1)], axis=1)
    return both.reshape(-1, SUB, value.shape[-1])


class Neighbours:
    def __init__(self, own, up, down, side, side_up, side_down, meta, width):
        half = SUB // 2
        row = lax.broadcasted_iota(jnp.int32, own.shape, 1)
        near = row < half
        self.col = row % width
        self.width = width
        ha, wa, last = meta[1], meta[2], meta[3]
        up = unpack_bottom(jnp.where(ha > 0, up, 0.0))
        side_up = unpack_bottom(jnp.where(ha > 0, side_up, 0.0))
        down = unpack_top(jnp.where(ha < last, down, 0.0))
        side_down = unpack_top(jnp.where(ha < last, side_down, 0.0))
        self.rows = {
            0: own,
            -1: pltpu.roll(jnp.where(near, own, up), half, 1),
            1: pltpu.roll(jnp.where(near, down, own), half, 1),
        }
        sides = {
            0: pltpu.roll(side, half, 1),
            -1: jnp.where(near, side, side_up),
            1: jnp.where(near, side_down, side),
        }
        self.left = {key: jnp.where(wa > 0, value, 0.0) for key, value in sides.items()}
        self.right = {key: jnp.where(wa > 0, 0.0, value) for key, value in sides.items()}

    def at(self, row_step, col_step):
        base = self.rows[row_step]
        if col_step < 0:
            return pltpu.roll(
                jnp.where(self.col == self.width - 1, self.left[row_step], base), 1, 1
            )
        if col_step > 0:
            return pltpu.roll(jnp.where(self.col == 0, self.right[row_step], base), SUB - 1, 1)
        return base


def xor_pairs(size, step):
    return [(index, index ^ step) for index in range(size)]


def direct_sum(value, axis):
    size = lax.axis_size(axis)
    step = 1
    while step < size:
        if size // step >= 4:
            one, two, three = [
                lax.ppermute(value, axis, xor_pairs(size, step * times)) for times in (1, 2, 3)
            ]
            value = (value + two) + (one + three)
            step *= 4
        else:
            value = value + lax.ppermute(value, axis, xor_pairs(size, step))
            step *= 2
    return value


AXES = ("clips", "ha", "wa")
MOST = 32


def spread_count():
    count = lax.axis_size("ha") * lax.axis_size("wa")
    whole = count * lax.axis_size("clips")
    return whole if whole <= MOST else count


def exchange(copies):
    if copies.shape[0] == lax.axis_size("clips") * lax.axis_size("ha") * lax.axis_size("wa"):
        return lax.all_to_all(copies, AXES, 0, 0)
    return lax.all_to_all(direct_sum(copies, "clips"), TILE, 0, 0)


def exchange_widest(sums):
    count = lax.axis_size("ha") * lax.axis_size("wa")
    sums = direct_sum(sums, "clips")
    return lax.all_to_all(jnp.broadcast_to(sums[None], (count,) + sums.shape), TILE, 0, 0)


def exchange_halo(message, rows):
    wide, high = lax.axis_size("wa"), lax.axis_size("ha")
    side = lax.ppermute(message, "wa", xor_pairs(wide, 1))
    half = rows // 2
    tops = jnp.concatenate([message[rows : rows + half], side[rows : rows + half]], axis=0)
    bottoms = jnp.concatenate([message[rows + half :], side[rows + half :]], axis=0)
    up = lax.ppermute(bottoms, "ha", [(row, row + 1) for row in range(high - 1)])
    down = lax.ppermute(tops, "ha", [(row + 1, row) for row in range(high - 1)])
    return side, up, down


def time_conv(geo, parts, blocks):
    result = None
    for tap in range(3):
        at = 0
        total = None
        for part in parts:
            lanes = part.shape[-1]
            term = dot(part, blocks[tap][at : at + lanes])
            at += lanes
            total = term if total is None else total + term
        if tap != 1:
            total = geo.shift(total, 1 - tap)
        result = total if result is None else result + total
    return result


def fast_conv(geo, value, main, before, after):
    lanes = value.shape[-1] // PHASES
    result = dot(value, main)
    result = result + geo.shift(dot(value[:, -lanes:], before), 1)
    return result + geo.shift(dot(value[:, :lanes], after), -1)


def fast_conv_back(steps, main, before, after):
    lanes = before.shape[0]
    middle = dot_nt(steps[1], main)
    first = middle[:, :lanes] + dot_nt(steps[2], after)
    last = middle[:, -lanes:] + dot_nt(steps[0], before)
    return jnp.concatenate([first, middle[:, lanes:-lanes], last], axis=1)


def lane_block(value, phase, part):
    return pltpu.roll(value, value.shape[-1] - phase * part, 1) if phase else value


def fast_reduce_grad(value, steps):
    lanes = value.shape[-1] // PHASES
    part = steps[1].shape[-1] // PHASES
    main = dot_tn(value, steps[1])
    before = dot_tn(value[:, -lanes:], steps[0])
    after = dot_tn(value[:, :lanes], steps[2])

    def block(row, col):
        return lane_block(main[row * lanes : (row + 1) * lanes], col, part)

    result = []
    for tap in range(3):
        total = before if tap == 0 else None
        if tap == 2:
            total = lane_block(after, PHASES - 1, part)
        for col in range(PHASES):
            row = col + tap - 1
            if 0 <= row < PHASES:
                total = block(row, col) if total is None else total + block(row, col)
        result.append(total)
    return result


def gather_pack(parts):
    return lax.all_gather(jnp.concatenate(parts, axis=0), TILE, axis=0)


def columns(shard, lanes):
    depth, total = shard.shape
    return jnp.moveaxis(shard.reshape(depth, total // lanes, lanes), 1, 0).reshape(-1, lanes)


def split_phases(value):
    cap, frames, height, width, lanes = value.shape
    value = value.reshape(cap, frames // PHASES, PHASES, height, width, lanes)
    return jnp.moveaxis(value, 2, 4).reshape(-1, PHASES * lanes)


def join_phases(value, shape):
    cap, frames, height, width, lanes = shape
    value = value.reshape(cap, frames // PHASES, height, width, PHASES, lanes)
    return jnp.moveaxis(value, 4, 2).reshape(shape)


def early_gather(shards_one, shards_two, lateral):
    rows = []
    lanes = shards_one[2].shape[-1]
    kinds = [jnp.stack(pair) for pair in zip(shards_one, shards_two)]
    kinds.append(jnp.stack([lateral[..., :lanes], lateral[..., lanes:]]))
    for kind in kinds:
        flat = kind.reshape(-1, kind.shape[-1])
        rows.append(jnp.pad(flat, ((0, 0), (0, lanes - flat.shape[-1]))))
    packed = gather_pack(rows)
    result = []
    at = 0
    for kind in kinds:
        depth, width = kind.shape[-2:]
        number = kind.size // width
        part = packed[:, at : at + number, :width].reshape(packed.shape[0], -1, depth, width)
        at += number
        result.append(jnp.moveaxis(part, 0, 1).reshape(part.shape[1], -1, width))
    return result


def prepare_kernel(taps_ref, space_ref, wide_ref, lateral_ref, *refs):
    slow_one, fast_one, slow_two, fast_two, *outs = refs
    part = taps_ref.shape[-1]
    lateral, *joint = outs[10:]
    number = lateral.shape[0]
    for tap in range(number):
        lateral[tap] = jnp.concatenate([lateral_ref[tap], lateral_ref[number + tap]], axis=1)
    for layer, (slow, fast) in enumerate(((slow_one, fast_one), (slow_two, fast_two))):
        at = fast_at = 0
        for ref in joint[3 * layer : 3 * layer + 3]:
            fast_lanes = part if ref.shape[1] < slow.shape[1] // 2 else wide_ref.shape[-1]
            lanes = ref.shape[1] - PHASES * fast_lanes
            values = [slow[:, at : at + lanes]]
            values += [fast[:, fast_at : fast_at + fast_lanes]] * PHASES
            ref[...] = jnp.concatenate(values, axis=1)
            at, fast_at = at + lanes, fast_at + fast_lanes
    joint[6][...] = slow_one[:, slow_one.shape[1] - joint[6].shape[1] :]
    for layer in range(2):
        main, before, after, space, wide = outs[5 * layer : 5 * layer + 5]
        taps = [taps_ref[3 * layer + tap] for tap in range(3)]
        zero = jnp.zeros_like(taps[0])
        lanes = taps[0].shape[0]
        for row in range(PHASES):
            blocks = [
                taps[row - col + 1] if abs(row - col) <= 1 else zero for col in range(PHASES)
            ]
            main[row * lanes : (row + 1) * lanes, :] = jnp.concatenate(blocks, axis=1)
        before[...] = jnp.concatenate([taps[0]] + [zero] * (PHASES - 1), axis=1)
        after[...] = jnp.concatenate([zero] * (PHASES - 1) + [taps[2]], axis=1)
        for tap in range(9):
            block = space_ref[9 * layer + tap]
            none = jnp.zeros_like(block)
            for row in range(PHASES):
                blocks = [block if row == col else none for col in range(PHASES)]
                space[tap, row * part : (row + 1) * part, :] = jnp.concatenate(blocks, axis=1)
        block = wide_ref[layer]
        none = jnp.zeros_like(block)
        for row in range(PHASES):
            blocks = [block if row == col else none for col in range(PHASES)]
            wide[row * part : (row + 1) * part, :] = jnp.concatenate(blocks, axis=1)


def to_partners(pieces, axis):
    size = lax.axis_size(axis)
    return [
        lax.ppermute(piece, axis, xor_pairs(size, step + 1)) for step, piece in enumerate(pieces)
    ]


def share_with_clips(own, got):
    total = own.astype(F32)
    for piece in got:
        total = total + piece.astype(F32)
    total = total.astype(BF16)
    return [total] + to_partners([total] * len(got), "clips")


def sum_over_clips(meta, groups):
    size = lax.axis_size("clips")
    if size > 4:
        added = [sum(part.astype(F32) for part in group).astype(BF16) for group in groups]
        return [lax.psum(jnp.concatenate(added), "clips")]
    lanes = groups[0][0].shape[1]
    depths = [group[0].shape[0] // size for group in groups]
    number = sum(len(group) for group in groups)

    def kernel(meta_ref, *refs):
        ins, outs, total_ref = list(refs[:number]), refs[number:-1], refs[-1]
        places = []
        at = 0
        for group, depth in zip(groups, depths):
            mine, ins = ins[: len(group)], ins[len(group) :]
            total = mine[0][...]
            if len(mine) > 1:
                total = total.astype(F32)
                for ref in mine[1:]:
                    total = total + ref[...].astype(F32)
                total = total.astype(BF16)
            total_ref[at : at + depth * size, :] = total
            places.append(at)
            at += depth * size
        for step, out in enumerate(outs):
            low = 0
            for place, depth in zip(places, depths):
                start = pl.multiple_of(place + (meta_ref[4] ^ step) * depth, 16)
                out[low : low + depth, :] = total_ref[pl.ds(start, depth), :]
                low += depth
            out.send()

    quarters = run(
        kernel,
        [((sum(depths), lanes), BF16, "hbm")] * size,
        smem=(meta,),
        saved=[part for group in groups for part in group],
        scratch=(pltpu.VMEM((sum(depths) * size, lanes), BF16),),
    )
    return share_with_clips(quarters[0], to_partners(quarters[1:], "clips"))


def on_device(
    slow_input,
    fast_input,
    slow_cotangent,
    fast_cotangent,
    clip_counts,
    lateral_weight,
    slow_reduce_one,
    slow_spatial_one,
    slow_expand_one,
    slow_shortcut_one,
    fast_reduce_one,
    fast_spatial_one,
    fast_expand_one,
    slow_reduce_two,
    slow_spatial_two,
    slow_expand_two,
    fast_reduce_two,
    fast_spatial_two,
    fast_expand_two,
    slow_norms_one,
    fast_norms_one,
    slow_norms_two,
    fast_norms_two,
):
    geo = Geometry(slow_input.shape, fast_input.shape)
    rows, groups = geo.rows, geo.groups
    half_rows = rows // 2
    count = lax.axis_size("ha") * lax.axis_size("wa")
    spread = spread_count()
    slow_wide = slow_input.shape[-1]
    fast_wide = PHASES * fast_input.shape[-1]
    wide = slow_wide + fast_wide
    mid = slow_reduce_one.shape[-1]
    fast_part = fast_reduce_one.shape[-1]
    fast_mid = PHASES * fast_part
    small = mid + fast_mid
    lat = lateral_weight.shape[-1]
    blocks = slow_wide // mid

    depth_one = slow_reduce_one.shape[1]
    depth_two = slow_reduce_two.shape[1]
    depth_mid = slow_spatial_one.shape[2]
    depth_lat = lateral_weight.shape[1]
    near = gather_pack([slow_reduce_one.reshape(-1, mid), slow_spatial_one.reshape(-1, mid)])
    far = gather_pack(
        [
            columns(slow_expand_one, mid),
            columns(slow_shortcut_one, mid),
            slow_reduce_two.reshape(-1, mid),
        ]
    )
    last = gather_pack([slow_spatial_two.reshape(-1, mid), columns(slow_expand_two, mid)])
    at_space_one = 3 * depth_one
    at_short = blocks * depth_mid
    at_reduce_two = at_short + blocks * depth_one
    at_space_two = 0
    at_expand_two = 9 * depth_mid
    fast_shards_one = (fast_reduce_one, fast_spatial_one, fast_expand_one)
    fast_shards_two = (fast_reduce_two, fast_spatial_two, fast_expand_two)
    compact = early_gather(fast_shards_one, fast_shards_two, lateral_weight)
    structured = [
        ((fast_wide, fast_mid), BF16, "hbm"),
        ((fast_wide // PHASES, fast_mid), BF16, "hbm"),
        ((fast_wide // PHASES, fast_mid), BF16, "hbm"),
        ((9, fast_mid, fast_mid), BF16, "hbm"),
        ((fast_mid, fast_wide), BF16, "hbm"),
    ]
    joint_outs = [((2, lanes), F32, "hbm") for lanes in (small, small, wide)]
    prepared = run(
        prepare_kernel,
        structured * 2
        + [((lateral_weight.shape[0], fast_wide // PHASES, lat), BF16, "hbm")]
        + joint_outs * 2
        + [((2, slow_wide), F32, "hbm")],
        vmem=(*compact, slow_norms_one, fast_norms_one, slow_norms_two, fast_norms_two),
    )
    fast_one, fast_two, lateral = prepared[:5], prepared[5:10], prepared[10]
    params_one, params_two, params_short = prepared[11:14], prepared[14:17], prepared[17]

    held = clip_counts[0]
    clips = direct_sum(jnp.full((1, 128), held, F32), "clips")[0, 0]
    positions = clips * (SUB * geo.frames * count)
    inv_n = jnp.stack([1.0 / positions, 1.0 / (positions * PHASES)])
    ha, wa = lax.axis_index("ha"), lax.axis_index("wa")
    last_ha = jnp.full_like(ha, lax.axis_size("ha") - 1)
    meta = jnp.stack([held * geo.frames, ha, wa, last_ha, lax.axis_index("clips")])
    scalars = (meta, inv_n)

    slow_x = slow_input.reshape(rows, slow_wide)
    fast_x = split_phases(fast_input)
    cot = jnp.concatenate(
        [slow_cotangent.reshape(rows, slow_wide), split_phases(fast_cotangent)], axis=1
    )
    message_out = ((2 * rows, small), BF16, "hbm")
    stats_small = ((spread, 2, small), F32, "spread")
    stats_wide = ((spread, 2, wide), F32, "spread")
    stats_both = ((2, wide + slow_wide), F32, "vmem")
    small_out = ((rows, small), F32, "hbm")
    wide_out = ((rows, wide), F32, "hbm")

    def lateral_kernel(x_ref, k_ref, main_ref, before_ref, after_ref, united_ref, fast_ref):
        lanes = x_ref.shape[1] // PHASES
        x = x_ref[...]
        main = dot(x[:, : 3 * lanes], k_ref[2:5].reshape(3 * lanes, lat))
        past = dot(x[:, 2 * lanes :], k_ref[0:2].reshape(2 * lanes, lat))
        united_ref[...] = (main + geo.shift(past, 1)).astype(BF16)
        fast_ref[...] = fast_conv(geo, x, main_ref[...], before_ref[...], after_ref[...])

    united, za_fast = run(
        lateral_kernel,
        [((rows, lat), BF16, "hbm"), ((rows, fast_mid), F32, "hbm")],
        saved=(fast_x, lateral, *fast_one[:3]),
    )

    def reduce_one_kernel(
        meta_ref, x_ref, united_ref, fast_ref, loads, za_ref, stats_ref, message_ref
    ):
        weights = [loads.get(tap) for tap in range(3)]
        za = time_conv(geo, (x_ref[...], united_ref[...]), weights)
        za = jnp.concatenate([za, fast_ref[...]], axis=1)
        za_ref[...] = za
        za_ref.send()
        za = geo.three(za)
        put_message(za, message_ref)
        put_forward(stats_ref, za, meta_ref[0])

    za_one, stats, message = run(
        reduce_one_kernel,
        [small_out, stats_small, message_out],
        smem=(meta,),
        saved=(slow_x, united, za_fast),
        weights=((near, 0, 3, depth_one),),
    )
    parts_a1 = exchange(stats)
    halo_one = exchange_halo(message, rows)

    def space_stage(za, parts_a, halo, params, gathered, offset, fast_w):
        def kernel(
            meta_ref,
            inv_ref,
            stats_ref,
            side_ref,
            up_ref,
            down_ref,
            za_ref,
            params_ref,
            fast_ref,
            loads,
            zb_ref,
            hidden_ref,
            out_stats,
        ):
            scale, shift, _, _ = affine(stats_ref, params_ref, inv_ref, mid)

            def act(value):
                return silu(geo.three(value.astype(F32)) * scale + shift)

            own = act(za_ref[...])
            hidden_ref[...] = geo.flat(own).astype(BF16)
            hidden_ref.send()
            near_by = Neighbours(
                own,
                act(up_ref[:half_rows]),
                act(down_ref[:half_rows]),
                act(side_ref[:rows]),
                act(up_ref[half_rows:]),
                act(down_ref[half_rows:]),
                meta_ref,
                geo.width,
            )
            slow = fast = None
            for tap in range(9):
                moved = geo.flat(near_by.at(tap // 3 - 1, tap % 3 - 1)).astype(BF16)
                slow_term = dot(moved[:, :mid], loads.get(tap))
                fast_term = dot(moved[:, mid:], fast_ref[tap])
                slow = slow_term if slow is None else slow + slow_term
                fast = fast_term if fast is None else fast + fast_term
            zb = jnp.concatenate([slow, fast], axis=1)
            zb_ref[...] = zb
            zb_ref.send()
            put_forward(out_stats, geo.three(zb), meta_ref[0])

        zb, hidden, stats, stats_a = run(
            kernel,
            [small_out, ((rows, small), BF16, "hbm"), stats_small],
            smem=scalars,
            parts=(parts_a,),
            saved=(*halo, za, params, fast_w),
            weights=((gathered, offset, 9, depth_mid),),
        )
        return zb, hidden, exchange(stats), stats_a

    zb_one, ha_one, parts_b1, stats_a1 = space_stage(
        za_one, parts_a1, halo_one, params_one[0], near, at_space_one, fast_one[3]
    )

    def expand_body(inv_ref, stats_ref, zb_ref, params_ref, fast_ref, hidden_ref, zc_ref, loads):
        scale, shift, _, _ = affine(stats_ref, params_ref, inv_ref, mid)
        hidden = geo.flat(silu(geo.three(zb_ref[...]) * scale + shift)).astype(BF16)
        hidden_ref[...] = hidden
        hidden_ref.send()
        zc_ref[:, slow_wide:] = dot(hidden[:, mid:], fast_ref[...])
        for block in range(blocks):
            zc_ref[:, block * mid : (block + 1) * mid] = dot(hidden[:, :mid], loads.get(block))
        zc_ref.send()

    def expand_one_kernel(
        meta_ref,
        inv_ref,
        stats_ref,
        zb_ref,
        params_ref,
        fast_ref,
        x_ref,
        united_ref,
        loads,
        shorts,
        hidden_ref,
        zc_ref,
        short_ref,
        out_stats,
    ):
        expand_body(inv_ref, stats_ref, zb_ref, params_ref, fast_ref, hidden_ref, zc_ref, loads)
        put_forward(out_stats, geo.three(zc_ref[...]), meta_ref[0])
        for block in range(blocks):
            weight = shorts.get(block)
            value = dot(x_ref[...], weight[:slow_wide]) + dot(united_ref[...], weight[slow_wide:])
            short_ref[:, block * mid : (block + 1) * mid] = value
            put_forward(out_stats, geo.three(value), meta_ref[0], wide + block * mid)
        short_ref.send()

    hb_one, zc_one, short, stats, stats_b1 = run(
        expand_one_kernel,
        [((rows, small), BF16, "hbm"), wide_out, ((rows, slow_wide), F32, "hbm"), stats_both],
        smem=scalars,
        parts=(parts_b1,),
        saved=(zb_one, params_one[1], fast_one[4], slow_x, united),
        weights=((far, 0, blocks, depth_mid), (far, at_short, blocks, depth_one)),
    )
    parts_c1 = exchange_widest(stats)

    def reduce_two_kernel(
        meta_ref,
        inv_ref,
        stats_ref,
        zc_ref,
        short_ref,
        params_ref,
        short_params_ref,
        x_ref,
        main_ref,
        before_ref,
        after_ref,
        loads,
        sum_ref,
        low_ref,
        za_ref,
        out_stats,
        message_ref,
    ):
        scale, shift, _, _ = affine(stats_ref, params_ref, inv_ref, slow_wide, 0, wide)
        scale_s, shift_s, _, _ = affine(
            stats_ref, short_params_ref, inv_ref, slow_wide, wide, wide + slow_wide
        )
        normed = geo.three(zc_ref[...]) * scale + shift
        slow = normed[..., :slow_wide] + (geo.three(short_ref[...]) * scale_s + shift_s)
        fast = normed[..., slow_wide:] + geo.three(x_ref[...].astype(F32))
        total = jnp.concatenate([slow, fast], axis=-1)
        sum_ref[...] = geo.flat(total)
        sum_ref.send()
        low = geo.flat(silu(total)).astype(BF16)
        low_ref[...] = low
        low_ref.send()
        weights = [loads.get(tap) for tap in range(3)]
        za = time_conv(geo, (low[:, :slow_wide],), weights)
        fast_za = fast_conv(
            geo, low[:, slow_wide:], main_ref[...], before_ref[...], after_ref[...]
        )
        za = jnp.concatenate([za, fast_za], axis=1)
        za_ref[...] = za
        za_ref.send()
        za = geo.three(za)
        put_message(za, message_ref)
        put_forward(out_stats, za, meta_ref[0])

    sum_one, low_one, za_two, stats, message, stats_c1 = run(
        reduce_two_kernel,
        [wide_out, ((rows, wide), BF16, "hbm"), small_out, stats_small, message_out],
        smem=scalars,
        parts=(parts_c1,),
        saved=(zc_one, short, params_one[2], params_short, fast_x, *fast_two[:3]),
        weights=((far, at_reduce_two, 3, depth_two),),
    )
    parts_a2 = exchange(stats)
    halo_two = exchange_halo(message, rows)
    zb_two, ha_two, parts_b2, stats_a2 = space_stage(
        za_two, parts_a2, halo_two, params_two[0], last, at_space_two, fast_two[3]
    )

    def expand_two_kernel(
        meta_ref,
        inv_ref,
        stats_ref,
        zb_ref,
        params_ref,
        fast_ref,
        loads,
        hidden_ref,
        zc_ref,
        out_stats,
    ):
        expand_body(inv_ref, stats_ref, zb_ref, params_ref, fast_ref, hidden_ref, zc_ref, loads)
        put_forward(out_stats, geo.three(zc_ref[...]), meta_ref[0])

    hb_two, zc_two, stats, stats_b2 = run(
        expand_two_kernel,
        [((rows, small), BF16, "hbm"), wide_out, stats_wide],
        smem=scalars,
        parts=(parts_b2,),
        saved=(zb_two, params_two[1], fast_two[4]),
        weights=((last, at_expand_two, blocks, depth_mid),),
    )
    parts_c2 = exchange(stats)

    def head_kernel(
        meta_ref, inv_ref, stats_ref, zc_ref, params_ref, sum_ref, cot_ref, out_ref, g_ref, sums_ref
    ):
        scale, shift, mean, inv = affine(stats_ref, params_ref, inv_ref, slow_wide)
        zc = geo.three(zc_ref[...])
        total = zc * scale + shift + silu(geo.three(sum_ref[...]))
        valid = mask_groups(total.shape, meta_ref[0])
        sigma = jax.nn.sigmoid(total)
        out_ref[...] = geo.flat(jnp.where(valid, total * sigma, 0.0)).astype(BF16)
        slopes = sigma * (1.0 + total * (1.0 - sigma))
        gradient = jnp.where(valid, geo.three(cot_ref[...].astype(F32)) * slopes, 0.0)
        out_ref.send()
        g_ref[...] = geo.flat(gradient)
        g_ref.send()
        put_back(sums_ref, gradient, (zc - mean) * inv)

    outputs, g_two, sums, stats_c2 = run(
        head_kernel,
        [((rows, wide), BF16, "hbm"), wide_out, stats_wide],
        smem=scalars,
        parts=(parts_c2,),
        saved=(zc_two, params_two[2], sum_one, cot),
    )
    parts_c2 = exchange(sums)

    def norm_back(gradient, value, coeffs, sums, valid):
        scale, _, mean, inv = coeffs
        crossed = (value - mean) * inv * sums[0] + sums[1]
        return scale * (gradient - jnp.where(valid, crossed, 0.0))

    def expand_back_body(
        meta_ref,
        inv_ref,
        sums_ref,
        stats_ref,
        stats_b_ref,
        g_ref,
        zc_ref,
        params_ref,
        zb_ref,
        params_b_ref,
        fast_ref,
        loads,
        gz_ref,
        g_out,
        sums_out,
        message_ref,
    ):
        limit = meta_ref[0]
        coeffs = affine(stats_ref, params_ref, inv_ref, slow_wide, 0, wide)
        both = [back_rows(sums_ref, inv_ref, slow_wide, row, 0, wide) for row in range(2)]
        gradient = geo.three(g_ref[...])
        gz = norm_back(
            gradient, geo.three(zc_ref[...]), coeffs, both, mask_groups(gradient.shape, limit)
        )
        gz = geo.flat(gz).astype(BF16)
        gz_ref[...] = gz
        gz_ref.send()
        fast = dot_nt(gz[:, slow_wide:], fast_ref[...])
        slow = None
        for block in range(blocks):
            term = dot_nt(gz[:, block * mid : (block + 1) * mid], loads.get(block))
            slow = term if slow is None else slow + term
        scale, shift, mean, inv = affine(stats_b_ref, params_b_ref, inv_ref, mid)
        zb = geo.three(zb_ref[...])
        back = geo.three(jnp.concatenate([slow, fast], axis=1)) * slope(zb * scale + shift)
        g_out[...] = geo.flat(back)
        g_out.send()
        put_message(jnp.concatenate([back, zb], axis=-1), message_ref)
        masked = jnp.where(mask_groups(back.shape, limit), back, 0.0)
        put_back(sums_out, masked, (zb - mean) * inv)
        return gradient

    message_back = ((2 * rows, 2 * small), BF16, "hbm")
    gz_c2, g_b2, sums, message, sums_c2 = run(
        expand_back_body,
        [((rows, wide), BF16, "hbm"), small_out, stats_small, message_back],
        smem=scalars,
        parts=(parts_c2,),
        saved=(stats_c2, stats_b2, g_two, zc_two, params_two[2], zb_two, params_two[1], fast_two[4]),
        weights=((last, at_expand_two, blocks, depth_mid),),
    )
    parts_b2 = exchange(sums)
    halo_back_two = exchange_halo(message, rows)

    lanes_fast = fast_wide // PHASES
    fast_rows_count = fast_reduce_one.shape[1] + 2 * SUB

    def expand_grad(hb_ref, gz_ref, out_ref, at):
        for block in range(blocks):
            value = dot_tn(hb_ref[:, :mid], gz_ref[:, block * mid : (block + 1) * mid])
            low = at + block * depth_mid
            out_ref[:, low : low + depth_mid, :] = value.astype(BF16).reshape(
                count, depth_mid, mid
            )

    def fast_expand_grad(hb_ref, gz_ref):
        fast = dot_tn(hb_ref[:, mid:], gz_ref[:, slow_wide:])
        total = None
        for phase in range(PHASES):
            part = fast[
                phase * fast_part : (phase + 1) * fast_part,
                phase * lanes_fast : (phase + 1) * lanes_fast,
            ]
            total = part if total is None else total + part
        return total

    def space_grad(ha_ref, taps_ref, out_ref, at):
        fast_grads = []
        for tap in range(9):
            value = dot_tn(ha_ref[:, :mid], taps_ref[tap, :, :mid])
            low = at + tap * depth_mid
            out_ref[:, low : low + depth_mid, :] = value.astype(BF16).reshape(
                count, depth_mid, mid
            )
            fast = dot_tn(ha_ref[:, mid:], taps_ref[tap, :, mid:])
            total = None
            for phase in range(PHASES):
                part = lane_block(
                    fast[phase * fast_part : (phase + 1) * fast_part], phase, fast_part
                )
                total = part if total is None else total + part
            fast_grads.append(total)
        return fast_grads

    def put_fast(reduce, space, expand, out_ref, at):
        lane = lax.broadcasted_iota(jnp.int32, reduce[0].shape, 1)

        def beside(parts):
            keep = lane[: parts[0].shape[0]]
            total = None
            for place, part in enumerate(parts):
                part = jnp.where(keep < fast_part, part, 0.0)
                part = pltpu.roll(part, place * fast_part, 1) if place else part
                total = part if total is None else total + part
            return total

        depth = reduce[0].shape[0] // count
        taps = beside(reduce).astype(BF16).reshape(count, depth, lanes_fast)
        out_ref[:, at : at + depth, :] = jnp.concatenate([taps, jnp.zeros_like(taps)], axis=-1)

        def spread(value):
            tiles = value.reshape(count // 2, SUB, lanes_fast)
            return jnp.stack([tiles, pltpu.roll(tiles, SUB // 2, 1)], axis=1).reshape(
                count, SUB, lanes_fast
            )

        first = jnp.concatenate([spread(beside(space[0:4])), spread(beside(space[4:8]))], axis=-1)
        second = jnp.concatenate([spread(beside(space[8:9])), spread(expand)], axis=-1)
        both = jnp.concatenate([first, second], axis=1).astype(BF16)
        out_ref[:, at + depth : at + depth + 2 * SUB, :] = both

    def space_back_stage(
        g, zb, za, halo, stats_b, parts_b, params_b, stats_a, params_a, g_hbm, at, fast_w
    ):
        def kernel(
            meta_ref,
            inv_ref,
            sums_b_ref,
            side_ref,
            up_ref,
            down_ref,
            stats_b_ref,
            stats_a_ref,
            g_ref,
            zb_ref,
            za_ref,
            params_b_ref,
            params_a_ref,
            fast_ref,
            loads,
            taps_ref,
            g_out,
            sums_out,
        ):
            limit = meta_ref[0]
            coeffs = affine(stats_b_ref, params_b_ref, inv_ref, mid)
            both = [back_rows(sums_b_ref, inv_ref, mid, row) for row in range(2)]

            def back(gradient, value, scale):
                valid = mask_groups(gradient.shape, limit, scale)
                return norm_back(gradient, value, coeffs, both, valid)

            def halo_back(value, scale):
                value = geo.three(value.astype(F32))
                return back(value[..., :small], value[..., small:], scale)

            near_by = Neighbours(
                back(geo.three(g_ref[...]), geo.three(zb_ref[...]), 1),
                halo_back(up_ref[:half_rows], 2),
                halo_back(down_ref[:half_rows], 2),
                halo_back(side_ref[:rows], 1),
                halo_back(up_ref[half_rows:], 2),
                halo_back(down_ref[half_rows:], 2),
                meta_ref,
                geo.width,
            )
            slow = fast = None
            for tap in range(9):
                moved = geo.flat(near_by.at(1 - tap // 3, 1 - tap % 3)).astype(BF16)
                taps_ref[tap] = moved
                if tap == 8:
                    taps_ref.send()
                slow_term = dot_nt(moved[:, :mid], loads.get(tap))
                fast_term = dot_nt(moved[:, mid:], fast_ref[tap])
                slow = slow_term if slow is None else slow + slow_term
                fast = fast_term if fast is None else fast + fast_term
            scale, shift, mean, inv = affine(stats_a_ref, params_a_ref, inv_ref, mid)
            za = geo.three(za_ref[...])
            result = geo.three(jnp.concatenate([slow, fast], axis=1)) * slope(za * scale + shift)
            g_out[...] = geo.flat(result)
            g_out.send()
            masked = jnp.where(mask_groups(result.shape, limit), result, 0.0)
            put_back(sums_out, masked, (za - mean) * inv)

        taps, g, sums, sums_b = run(
            kernel,
            [((9, rows, small), BF16, "hbm"), small_out, stats_small],
            smem=scalars,
            parts=(parts_b,),
            saved=(*halo, stats_b, stats_a, g, zb, za, params_b, params_a, fast_w),
            weights=((g_hbm, at, 9, depth_mid),),
        )
        return taps, g, exchange(sums), sums_b

    taps_two, g_a2, parts_a2, sums_b2 = space_back_stage(
        g_b2,
        zb_two,
        za_two,
        halo_back_two,
        stats_b2,
        parts_b2,
        params_two[1],
        stats_a2,
        params_two[0],
        last,
        at_space_two,
        fast_two[3],
    )
    def reduce_gz(meta_ref, inv_ref, g_ref, za_ref, stats_ref, sums_ref, params_ref, steps_ref):
        coeffs = affine(stats_ref, params_ref, inv_ref, mid)
        both = [back_rows(sums_ref, inv_ref, mid, row) for row in range(2)]
        gradient = geo.three(g_ref[...])
        gz = norm_back(
            gradient,
            geo.three(za_ref[...]),
            coeffs,
            both,
            mask_groups(gradient.shape, meta_ref[0]),
        )
        gz = geo.flat(gz)
        steps = [geo.shift(gz, -1).astype(BF16), gz.astype(BF16), geo.shift(gz, 1).astype(BF16)]
        for tap in range(3):
            steps_ref[tap] = steps[tap]
        if isinstance(steps_ref, Store):
            steps_ref.send()
        return steps

    def reduce_back_two_kernel(
        meta_ref,
        inv_ref,
        sums_ref,
        stats_ref,
        stats_c_ref,
        g_ref,
        za_ref,
        params_ref,
        g_two_ref,
        sum_ref,
        zc_ref,
        short_ref,
        main_ref,
        before_ref,
        after_ref,
        loads,
        steps_ref,
        g_out,
        sums_out,
    ):
        steps = reduce_gz(
            meta_ref, inv_ref, g_ref, za_ref, stats_ref, sums_ref, params_ref, steps_ref
        )
        slow = None
        for tap in range(3):
            term = dot_nt(steps[tap][:, :mid], loads.get(tap))
            slow = term if slow is None else slow + term
        fast = fast_conv_back(
            [step[:, mid:] for step in steps], main_ref[...], before_ref[...], after_ref[...]
        )
        back = jnp.concatenate([slow, fast], axis=1) + g_two_ref[...]
        back = geo.three(back * slope(sum_ref[...]))
        g_out[...] = geo.flat(back)
        g_out.send()
        masked = jnp.where(mask_groups(back.shape, meta_ref[0]), back, 0.0)
        mean, inv = moments(stats_c_ref, inv_ref, slow_wide, 0, wide)
        put_back(sums_out, masked, (geo.three(zc_ref[...]) - mean) * inv)
        mean, inv = moments(stats_c_ref, inv_ref, slow_wide, wide, wide + slow_wide)
        masked = masked[..., :slow_wide]
        put_back(sums_out, masked, (geo.three(short_ref[...]) - mean) * inv, wide)

    steps_two, g_one, sums, sums_a2 = run(
        reduce_back_two_kernel,
        [((3, rows, small), BF16, "hbm"), wide_out, stats_both],
        smem=scalars,
        parts=(parts_a2,),
        saved=(stats_a2, stats_c1, g_a2, za_two, params_two[0], g_two, sum_one, zc_one, short, *fast_two[:3]),
        weights=((far, at_reduce_two, 3, depth_two),),
    )
    parts_c1 = exchange_widest(sums)

    def grads_two_kernel(hb_ref, gz_ref, ha_ref, taps_ref, low_ref, steps_ref, out_ref):
        for tap in range(3):
            value = dot_tn(low_ref[:, :slow_wide], steps_ref[tap, :, :mid])
            out_ref[:, tap * depth_two : (tap + 1) * depth_two, :] = value.astype(BF16).reshape(
                count, depth_two, mid
            )
        at = 3 * depth_two
        space = space_grad(ha_ref, taps_ref, out_ref, at)
        at += 9 * depth_mid
        expand_grad(hb_ref, gz_ref, out_ref, at)
        at += blocks * depth_mid
        reduce = fast_reduce_grad(
            low_ref[:, slow_wide:], [steps_ref[tap, :, mid:] for tap in range(3)]
        )
        put_fast(reduce, space, fast_expand_grad(hb_ref, gz_ref), out_ref, at)

    rows_two = 3 * depth_two + (9 + blocks) * depth_mid + fast_rows_count
    (packed_two,) = run(
        grads_two_kernel,
        [((count, rows_two, mid), BF16, "hbm")],
        saved=(hb_two, gz_c2, ha_two, taps_two, low_one, steps_two),
    )
    sum_two = lax.psum_scatter(packed_two, TILE, scatter_dimension=0, tiled=False)

    def expand_back_one_kernel(*refs):
        *body, short_ref, short_params_ref, loads, gz_ref, g_out, sums_out, message, gs_ref = refs
        gradient = expand_back_body(*body, loads, gz_ref, g_out, sums_out, message)
        meta_ref, inv_ref, sums_ref, stats_ref = body[:4]
        low, high = wide, wide + slow_wide
        coeffs = affine(stats_ref, short_params_ref, inv_ref, slow_wide, low, high)
        both = [back_rows(sums_ref, inv_ref, slow_wide, row, low, high) for row in range(2)]
        gradient = gradient[..., :slow_wide]
        valid = mask_groups(gradient.shape, meta_ref[0])
        gs = norm_back(gradient, geo.three(short_ref[...]), coeffs, both, valid)
        gs_ref[...] = geo.flat(gs).astype(BF16)

    gz_c1, g_b1, sums, message, gz_short, sums_c1 = run(
        expand_back_one_kernel,
        [((rows, wide), BF16, "hbm"), small_out, stats_small, message_back]
        + [((rows, slow_wide), BF16, "hbm")],
        smem=scalars,
        parts=(parts_c1,),
        saved=(stats_c1, stats_b1, g_one, zc_one, params_one[2], zb_one, params_one[1], fast_one[4])
        + (short, params_short),
        weights=((far, 0, blocks, depth_mid),),
    )
    parts_b1 = exchange(sums)
    halo_back_one = exchange_halo(message, rows)
    joined_lanes = slow_wide + lat

    def grads_mid_kernel(x_ref, united_ref, gs_ref, hb_ref, gz_ref, loads, out_ref, back_ref):
        for block in range(blocks):
            gs = gs_ref[:, block * mid : (block + 1) * mid]
            value = jnp.concatenate([dot_tn(x_ref[...], gs), dot_tn(united_ref[...], gs)], axis=0)
            out_ref[:, block * depth_one : (block + 1) * depth_one, :] = value.astype(
                BF16
            ).reshape(count, depth_one, mid)
            term = dot_nt(gs, loads.get(block))
            back_ref[...] = term if block == 0 else back_ref[...] + term
        expand_grad(hb_ref, gz_ref, out_ref, blocks * depth_one)

    packed_mid, short_back = run(
        grads_mid_kernel,
        [((count, blocks * (depth_one + depth_mid), mid), BF16, "hbm")]
        + [((rows, joined_lanes), F32, "hbm")],
        saved=(slow_x, united, gz_short, hb_one, gz_c1),
        weights=((far, at_short, blocks, depth_one),),
    )
    sum_mid = lax.psum_scatter(packed_mid, TILE, scatter_dimension=0, tiled=False)

    taps_one, g_a1, parts_a1, sums_b1 = space_back_stage(
        g_b1,
        zb_one,
        za_one,
        halo_back_one,
        stats_b1,
        parts_b1,
        params_one[1],
        stats_a1,
        params_one[0],
        near,
        at_space_one,
        fast_one[3],
    )
    def last_kernel(
        meta_ref,
        inv_ref,
        sums_ref,
        stats_ref,
        g_ref,
        za_ref,
        params_ref,
        g_one_ref,
        short_ref,
        lateral_ref,
        main_ref,
        before_ref,
        after_ref,
        loads,
        steps_ref,
        slow_ref,
        fast_ref,
        united_ref,
    ):
        steps = reduce_gz(
            meta_ref, inv_ref, g_ref, za_ref, stats_ref, sums_ref, params_ref, steps_ref
        )
        joined = short_ref[...]
        for tap in range(3):
            joined = joined + dot_nt(steps[tap][:, :mid], loads.get(tap))
        slow_ref[...] = joined[:, :slow_wide]
        tail = joined[:, slow_wide:]
        now, past = tail.astype(BF16), geo.shift(tail, -1).astype(BF16)
        united_ref[0] = now
        united_ref[1] = past
        lanes = fast_wide // PHASES
        fast = fast_conv_back(
            [step[:, mid:] for step in steps], main_ref[...], before_ref[...], after_ref[...]
        )
        fast = fast + g_one_ref[:, slow_wide:]
        front = dot_nt(now, lateral_ref[2:5].reshape(3 * lanes, lat))
        back = dot_nt(past, lateral_ref[0:2].reshape(2 * lanes, lat))
        fast_ref[:, : 2 * lanes] = fast[:, : 2 * lanes] + front[:, : 2 * lanes]
        fast_ref[:, 2 * lanes : 3 * lanes] = (
            fast[:, 2 * lanes : 3 * lanes] + front[:, 2 * lanes :] + back[:, :lanes]
        )
        fast_ref[:, 3 * lanes :] = fast[:, 3 * lanes :] + back[:, lanes:]

    steps_one, grad_slow, grad_fast, united_low, sums_a1 = run(
        last_kernel,
        [
            ((3, rows, small), BF16, "hbm"),
            ((rows, slow_wide), F32, "hbm"),
            ((rows, fast_wide), F32, "hbm"),
            ((2, rows, lat), BF16, "hbm"),
        ],
        smem=scalars,
        parts=(parts_a1,),
        saved=(stats_a1, g_a1, za_one, params_one[0], g_one, short_back, lateral, *fast_one[:3]),
        weights=((near, 0, 3, depth_one),),
    )

    def grads_one_kernel(
        meta_ref,
        steps_ref,
        low_ref,
        x_ref,
        united_ref,
        fast_x_ref,
        ha_ref,
        taps_ref,
        hb_ref,
        gz_ref,
        own_ref,
        send_ref,
        out_ref,
        sems,
    ):
        lanes = fast_wide // PHASES
        for tap in range(3):
            step = steps_ref[tap, :, :mid]
            value = jnp.concatenate(
                [dot_tn(x_ref[...], step), dot_tn(united_ref[...], step)], axis=0
            )
            out_ref[:, tap * depth_one : (tap + 1) * depth_one, :] = value.astype(BF16).reshape(
                count, depth_one, mid
            )
        at = 3 * depth_one
        past = dot_tn(fast_x_ref[:, 2 * lanes :], low_ref[1])
        now = dot_tn(fast_x_ref[:, : 3 * lanes], low_ref[0])
        both = jnp.concatenate([past, now], axis=0).astype(BF16)
        for tap in range(5):
            out_ref[:, at + tap * depth_lat : at + (tap + 1) * depth_lat, :] = both[
                tap * lanes : (tap + 1) * lanes
            ].reshape(count, depth_lat, lat)
        at += 5 * depth_lat
        space = space_grad(ha_ref, taps_ref, out_ref, at)
        at += 9 * depth_mid
        reduce = fast_reduce_grad(
            fast_x_ref[...], [steps_ref[tap, :, mid:] for tap in range(3)]
        )
        put_fast(reduce, space, fast_expand_grad(hb_ref, gz_ref), out_ref, at)

        put_blocks(out_ref, own_ref, send_ref, meta_ref[1], meta_ref[2], sems)

    def put_blocks(blocks_ref, own_ref, send_ref, ha, wa, sems):
        for block in range(count):
            place, col = ha ^ (block // 2), block % 2
            source, sem = blocks_ref.at[block], sems.at[block]

            @pl.when(wa == col)
            def _():
                pltpu.make_async_copy(source, own_ref.at[place], sem).start()

            @pl.when(wa != col)
            def _():
                pltpu.make_async_copy(source, send_ref.at[place], sem).start()

        for block in range(count):
            pltpu.make_async_copy(blocks_ref.at[block], own_ref.at[0], sems.at[block]).wait()

    high = count // 2
    rows_one = 3 * depth_one + 5 * depth_lat + 9 * depth_mid + fast_rows_count
    rows_late = rows_one + -rows_one % (16 * lax.axis_size("clips"))
    blocks_out = ((high, rows_late, mid), BF16, "raw")
    own_blocks, send_blocks = run(
        grads_one_kernel,
        [blocks_out, blocks_out],
        smem=(meta,),
        saved=(steps_one, united_low, slow_x, united, fast_x, ha_one, taps_one, hb_one, gz_c1),
        scratch=(
            pltpu.VMEM((count, rows_late, mid), BF16),
            pltpu.SemaphoreType.DMA((count,)),
        ),
    )
    side_blocks = lax.ppermute(send_blocks, "wa", xor_pairs(2, 1))

    def chip_kernel(own_ref, side_ref, *out_refs):
        for place in range(high):
            total = own_ref[place].astype(F32) + side_ref[place].astype(F32)
            out_refs[place][...] = total.astype(BF16)
            out_refs[place].send()

    late_out = ((rows_late, mid), BF16, "hbm")
    chip_sums = run(chip_kernel, [late_out] * high, saved=(own_blocks, side_blocks))
    sum_two, sum_mid, chip_sums = lax.optimization_barrier((sum_two, sum_mid, chip_sums))
    late = [chip_sums[0]] + to_partners(chip_sums[1:], "ha")
    parts_early = sum_over_clips(meta, [[sum_two], [sum_mid]])
    parts_late = sum_over_clips(meta, [late])

    def finish(parts, groups):
        size = len(parts)
        outs_all = []
        for _, shapes in groups:
            for shape in shapes:
                outs_all += list(shape) if isinstance(shape[0], tuple) else [shape]

        def kernel(meta_ref, *refs):
            ins, outs, total_ref = refs[:size], list(refs[size:-1]), refs[-1]
            low = base = 0
            for rows_group, shapes in groups:
                depth = rows_group // size
                for step, ref in enumerate(ins):
                    place = (meta_ref[4] ^ step) if size > 1 else 0
                    start = pl.multiple_of(base + place * depth, 16)
                    total_ref[pl.ds(start, depth), :] = ref[low : low + depth, :].astype(F32)
                at = base
                for shape in shapes:
                    if isinstance(shape[0], tuple):
                        reduce, space, expand = outs.pop(0), outs.pop(0), outs.pop(0)
                        rows_tap, lanes = reduce.shape[1:]
                        for tap in range(3):
                            reduce[tap] = total_ref[
                                at : at + rows_tap, tap * lanes : (tap + 1) * lanes
                            ]
                        few = space.shape[2]
                        for tap in range(9):
                            row = at + rows_tap + tap // SUB * SUB
                            lane = tap % SUB * lanes
                            space[tap // 3, tap % 3] = total_ref[
                                row : row + few, lane : lane + lanes
                            ]
                        row = at + rows_tap + SUB
                        expand[...] = total_ref[row : row + few, expand.shape[1] :]
                        for out in (reduce, space, expand):
                            out.send()
                        continue
                    out = outs.pop(0)
                    if len(shape) == 2 and shape[1] > mid:
                        for block in range(shape[1] // mid):
                            out[:, block * mid : (block + 1) * mid] = total_ref[
                                at : at + shape[0], :
                            ]
                            at += shape[0]
                    else:
                        number = 1
                        for length in shape[:-1]:
                            number *= length
                        out[...] = total_ref[at : at + number, :].reshape(shape)
                        at += number
                    out.send()
                low += depth
                base += rows_group

        return run(
            kernel,
            [(shape, F32, "hbm") for shape in outs_all],
            smem=(meta,),
            saved=parts,
            scratch=(pltpu.VMEM((sum(rows_group for rows_group, _ in groups), mid), F32),),
        )

    shapes_one = tuple(shard.shape for shard in fast_shards_one)
    shapes_two = tuple(shard.shape for shard in fast_shards_two)
    (
        grad_slow_reduce_two,
        grad_slow_spatial_two,
        grad_slow_expand_two,
        *rest,
    ) = finish(
        parts_early,
        [
            (
                rows_two,
                [slow_reduce_two.shape, slow_spatial_two.shape, slow_expand_two.shape, shapes_two],
            ),
            (packed_mid.shape[1], [slow_shortcut_one.shape, slow_expand_one.shape]),
        ],
    )
    fast_two_grads, (grad_slow_shortcut, grad_slow_expand_one) = rest[:3], rest[3:]
    grad_slow_reduce_one, grad_lateral, grad_slow_spatial_one, *fast_one_grads = finish(
        parts_late,
        [
            (
                rows_late,
                [slow_reduce_one.shape, lateral_weight.shape, slow_spatial_one.shape, shapes_one],
            )
        ],
    )

    def norm_grads(first, second, third):
        slow = [first[:, :mid], second[:, :mid], third[:, :slow_wide]]
        fast = [first[:, mid:], second[:, mid:], third[:, slow_wide:wide]]
        fast = [jnp.sum(part.reshape(2, PHASES, -1), axis=1) for part in fast]
        return slow, fast

    slow_one_p, fast_one_p = norm_grads(sums_a1, sums_b1, sums_c1)
    slow_two_p, fast_two_p = norm_grads(sums_a2, sums_b2, sums_c2)
    grad_slow_norms_one = jnp.concatenate(slow_one_p + [sums_c1[:, wide:]], axis=1)
    grad_slow_norms_two = jnp.concatenate(slow_two_p, axis=1)
    grad_fast_norms_one = jnp.concatenate(fast_one_p, axis=1)
    grad_fast_norms_two = jnp.concatenate(fast_two_p, axis=1)
    return (
        outputs[:, :slow_wide].reshape(slow_input.shape),
        join_phases(outputs[:, slow_wide:], fast_input.shape),
        grad_slow.reshape(slow_input.shape),
        join_phases(grad_fast, fast_input.shape),
        grad_lateral,
        grad_slow_reduce_one,
        grad_slow_spatial_one,
        grad_slow_expand_one,
        grad_slow_shortcut,
        *fast_one_grads,
        grad_slow_reduce_two,
        grad_slow_spatial_two,
        grad_slow_expand_two,
        *fast_two_grads,
        grad_slow_norms_one,
        grad_fast_norms_one,
        grad_slow_norms_two,
        grad_fast_norms_two,
    )


def solution(mesh):
    in_specs = (
        P("clips", None, "ha", "wa", None),
        P("clips", None, "ha", "wa", None),
        P("clips", None, "ha", "wa", None),
        P("clips", None, "ha", "wa", None),
        P("clips"),
        P(None, ("ha", "wa"), None),
        P(None, ("ha", "wa"), None),
        P(None, None, ("ha", "wa"), None),
        P(("ha", "wa"), None),
        P(("ha", "wa"), None),
        P(None, ("ha", "wa"), None),
        P(None, None, ("ha", "wa"), None),
        P(("ha", "wa"), None),
        P(None, ("ha", "wa"), None),
        P(None, None, ("ha", "wa"), None),
        P(("ha", "wa"), None),
        P(None, ("ha", "wa"), None),
        P(None, None, ("ha", "wa"), None),
        P(("ha", "wa"), None),
        P(),
        P(),
        P(),
        P(),
    )
    out_specs = (
        P("clips", None, "ha", "wa", None),
        P("clips", None, "ha", "wa", None),
        P("clips", None, "ha", "wa", None),
        P("clips", None, "ha", "wa", None),
        P(None, ("ha", "wa"), None),
        P(None, ("ha", "wa"), None),
        P(None, None, ("ha", "wa"), None),
        P(("ha", "wa"), None),
        P(("ha", "wa"), None),
        P(None, ("ha", "wa"), None),
        P(None, None, ("ha", "wa"), None),
        P(("ha", "wa"), None),
        P(None, ("ha", "wa"), None),
        P(None, None, ("ha", "wa"), None),
        P(("ha", "wa"), None),
        P(None, ("ha", "wa"), None),
        P(None, None, ("ha", "wa"), None),
        P(("ha", "wa"), None),
        P(),
        P(),
        P(),
        P(),
    )
    return jax.shard_map(
        on_device, mesh=mesh, in_specs=in_specs, out_specs=out_specs, check_vma=False
    )
```

```python
import jax
import jax.numpy as jnp
from jax import lax
from jax.experimental import pallas as pl
from jax.experimental.pallas import tpu as pltpu
from jax.sharding import PartitionSpec as P

epsilon = 1e-05
F32 = jnp.float32
BF16 = jnp.bfloat16
TILE = ("ha", "wa")
PHASES = 4
SUB = 8


def dot(left, right):
    return lax.dot_general(left, right, (((1,), (0,)), ((), ())), preferred_element_type=F32)


def dot_tn(left, right):
    return lax.dot_general(left, right, (((0,), (0,)), ((), ())), preferred_element_type=F32)


def dot_nt(left, right):
    return lax.dot_general(left, right, (((1,), (1,)), ((), ())), preferred_element_type=F32)


class Loads:
    def __init__(self, source, offset, target, sems, first):
        self.copies = []
        depth = target.shape[2]
        for step in range(target.shape[0]):
            copy = pltpu.make_async_copy(
                source.at[:, pl.ds(offset + step * depth, depth), :],
                target.at[step],
                sems.at[first + step],
            )
            copy.start()
            self.copies.append(copy)
        self.target = target

    def get(self, step):
        self.copies[step].wait()
        block = self.target[step]
        return block.reshape(-1, block.shape[-1])


class Saved:
    def __init__(self, source, scratch, sem):
        self.scratch, self.shape = scratch, scratch.shape
        self.copy = pltpu.make_async_copy(source, scratch, sem)
        self.copy.start()
        self.ready = False

    def wait(self):
        if not self.ready:
            self.copy.wait()
            self.ready = True

    def __getitem__(self, index):
        self.wait()
        return self.scratch[index]


class Store:
    def __init__(self, scratch, target, sem):
        self.scratch, self.shape, self.sent = scratch, scratch.shape, False
        self.copy = pltpu.make_async_copy(scratch, target, sem)

    def send(self):
        self.copy.start()
        self.sent = True

    def __setitem__(self, index, value):
        self.scratch[index] = value

    def __getitem__(self, index):
        return self.scratch[index]


def run(body, outs, smem=(), parts=(), vmem=(), saved=(), weights=(), scratch=(), limit=54):
    near = pl.BlockSpec(memory_space=pltpu.VMEM)
    far = pl.BlockSpec(memory_space=pltpu.HBM)
    sources = []
    for array, *_ in weights:
        if not any(array is other for other in sources):
            sources.append(array)
    outs = list(outs) + [(part.shape[1:], part.dtype, "hbm") for part in parts]
    flat = []
    for shape, dtype, kind in outs:
        flat += [(shape, dtype, "raw"), (shape, dtype, "vmem")] if kind == "both" else [(shape, dtype, kind)]
    held = [pltpu.VMEM(array.shape, array.dtype) for array in saved]
    for array, _, steps, depth in weights:
        held.append(pltpu.VMEM((steps, array.shape[0], depth, array.shape[2]), array.dtype))
    for shape, dtype, kind in outs:
        if kind == "hbm":
            held.append(pltpu.VMEM(shape, dtype))
        elif kind == "spread":
            held.append(pltpu.VMEM(shape[1:], dtype))
    sems = len(saved) + sum(steps for _, _, steps, _ in weights) + len(outs)
    held.append(pltpu.SemaphoreType.DMA((sems,)))

    def kernel(*refs):
        refs = list(refs)

        def take(number):
            taken = refs[:number]
            del refs[:number]
            return taken

        smem_refs, part_refs, vmem_refs = take(len(smem)), take(len(parts)), take(len(vmem))
        saved_refs, source_refs, out_refs = take(len(saved)), take(len(sources)), take(len(flat))
        saved_scratch, weight_scratch = take(len(saved)), take(len(weights))
        out_scratch = take(sum(kind in ("hbm", "spread") for _, _, kind in outs))
        sem, more = refs[0], refs[1:]
        copies = [
            Saved(source, target, sem.at[at])
            for at, (source, target) in enumerate(zip(saved_refs, saved_scratch))
        ]
        at = len(saved)
        loads = []
        for (array, offset, steps, _), target in zip(weights, weight_scratch):
            place = [array is other for other in sources].index(True)
            loads.append(Loads(source_refs[place], offset, target, sem, at))
            at += steps
        results, stores, spreads = [], [], []
        for _, _, kind in outs:
            ref = out_refs.pop(0)
            if kind == "both":
                stores.append(Store(out_refs.pop(0), ref, sem.at[at]))
                at += 1
                results.append(stores[-1])
            elif kind == "hbm":
                stores.append(Store(out_scratch.pop(0), ref, sem.at[at]))
                at += 1
                results.append(stores[-1])
            elif kind == "spread":
                spreads.append((out_scratch.pop(0), ref))
                results.append(spreads[-1][0])
            else:
                results.append(ref)
        sums = results[len(results) - len(parts) :]
        results = results[: len(results) - len(parts)]
        for part, total in zip(part_refs, sums):
            total[...] = jnp.sum(part[...], axis=0)
            total.send()
        totals = [total.scratch for total in sums]
        body(*smem_refs, *totals, *vmem_refs, *copies, *loads, *results, *more)
        for copy in copies:
            copy.wait()
        for store in stores:
            if not store.sent:
                store.send()
        for value, ref in spreads:
            ref[...] = jnp.broadcast_to(value[...][None], ref.shape)
        for store in stores:
            store.copy.wait()

    return pl.pallas_call(
        kernel,
        out_shape=[jax.ShapeDtypeStruct(shape, dtype) for shape, dtype, _ in flat],
        in_specs=[pl.BlockSpec(memory_space=pltpu.SMEM)] * len(smem)
        + [near] * (len(parts) + len(vmem))
        + [far] * (len(saved) + len(sources)),
        out_specs=[far if kind in ("hbm", "raw") else near for _, _, kind in flat],
        scratch_shapes=held + list(scratch),
        compiler_params=pltpu.CompilerParams(vmem_limit_bytes=limit * 1024 * 1024),
        cost_estimate=pl.CostEstimate(
            flops=2_000_000_000, bytes_accessed=16_000_000, transcendentals=0
        ),
    )(*smem, *parts, *vmem, *saved, *sources)


class Geometry:
    def __init__(self, slow_shape, fast_shape):
        self.cap, self.frames, self.height, self.width = slow_shape[:4]
        self.groups = self.cap * self.frames
        self.rows = self.groups * SUB

    def three(self, value):
        return value.reshape(-1, SUB, value.shape[-1])

    def flat(self, value):
        return value.reshape(-1, value.shape[-1])

    def shift(self, value, step):
        lanes = value.shape[-1]
        whole = value.reshape(self.cap, self.frames, SUB, lanes)
        zero = jnp.zeros((self.cap, 1, SUB, lanes), value.dtype)
        if step > 0:
            whole = jnp.concatenate([zero, whole[:, :-1]], axis=1)
        else:
            whole = jnp.concatenate([whole[:, 1:], zero], axis=1)
        return whole.reshape(-1, lanes)


def mask_groups(shape, limit, scale=1):
    return lax.broadcasted_iota(jnp.int32, shape, 0) * scale < limit


def rep(ref, row, low, high):
    return jnp.broadcast_to(ref[row : row + 1, low:high], (SUB, high - low))


def fold(value, slow):
    fast = value[:, slow:]
    lanes = fast.shape[-1]
    part = lanes // PHASES
    if part % 128 == 0:
        total = fast[:, :part]
        for phase in range(1, PHASES):
            total = total + fast[:, phase * part : (phase + 1) * part]
        return jnp.concatenate([value[:, :slow]] + [total] * PHASES, axis=1)
    total = fast
    for phase in range(1, PHASES):
        total = total + pltpu.roll(fast, phase * part, 1)
    return jnp.concatenate([value[:, :slow], total], axis=1)


def lane_counts(inv_ref, lanes, slow):
    lane = lax.broadcasted_iota(jnp.int32, (SUB, lanes), 1)
    return jnp.where(lane < slow, inv_ref[0], inv_ref[1])


def moments(stats, inv_ref, slow, low=0, high=None):
    high = stats.shape[1] if high is None else high
    total, square = rep(stats, 0, low, high), rep(stats, 1, low, high)
    if slow < high - low:
        total, square = fold(total, slow), fold(square, slow)
    inv_n = lane_counts(inv_ref, high - low, slow)
    mean = total * inv_n
    return mean, lax.rsqrt(square * inv_n - mean * mean + epsilon)


def affine(stats, params, inv_ref, slow, low=0, high=None):
    mean, inv = moments(stats, inv_ref, slow, low, high)
    lanes = mean.shape[1]
    scale = (1.0 + rep(params, 0, 0, lanes)) * inv
    return scale, rep(params, 1, 0, lanes) - mean * scale, mean, inv


def back_rows(sums, inv_ref, slow, row, low=0, high=None):
    high = sums.shape[1] if high is None else high
    total = rep(sums, row, low, high)
    if slow < high - low:
        total = fold(total, slow)
    return total * lane_counts(inv_ref, high - low, slow)


def silu(value):
    return value * jax.nn.sigmoid(value)


def slope(value):
    sigma = jax.nn.sigmoid(value)
    return sigma * (1.0 + value * (1.0 - sigma))


def put_stats(ref, first, second, low=0):
    lanes = first.shape[-1]
    ref[0:1, low : low + lanes] = jnp.sum(jnp.sum(first, axis=0), axis=0, keepdims=True)
    ref[1:2, low : low + lanes] = jnp.sum(jnp.sum(second, axis=0), axis=0, keepdims=True)


def put_back(ref, gradient, normal, low=0):
    put_stats(ref, gradient * normal, gradient, low)


def put_forward(ref, value, limit, low=0):
    masked = jnp.where(mask_groups(value.shape, limit), value, 0.0)
    put_stats(ref, masked, masked * value, low)


EDGE = 32


def edge_place(wa, width):
    return jnp.where(wa > 0, 0, width - 1)


def put_message(value, ref, meta_ref, width):
    lanes = value.shape[-1]
    pairs = value.reshape(-1, 2, SUB, lanes)
    first, second = pairs[:, 0], pairs[:, 1]
    near = lax.broadcasted_iota(jnp.int32, first.shape, 1) < SUB // 2
    top = jnp.where(near, first, pltpu.roll(second, SUB // 2, 1))
    bottom = jnp.where(near, pltpu.roll(first, SUB // 2, 1), second)
    flat = value.reshape(-1, lanes).astype(BF16)
    shape = (2 * EDGE, flat.shape[0])
    row, col = [lax.broadcasted_iota(jnp.int32, shape, dim) for dim in range(2)]
    low = row >= EDGE
    source = (row - jnp.where(low, EDGE, 0)) * SUB + jnp.where(low, SUB // 2, 0)
    chosen = (col == source + edge_place(meta_ref[2], width)).astype(F32).astype(BF16)
    edges = dot(chosen, flat)
    at = 0
    for part in (top, bottom, edges):
        part = part.reshape(-1, lanes).astype(BF16)
        ref[at : at + part.shape[0]] = part
        at += part.shape[0]
    ref.send()


def unpack_bottom(value):
    both = jnp.stack([pltpu.roll(value, SUB // 2, 1), value], axis=1)
    return both.reshape(-1, SUB, value.shape[-1])


def unpack_top(value):
    both = jnp.stack([value, pltpu.roll(value, SUB // 2, 1)], axis=1)
    return both.reshape(-1, SUB, value.shape[-1])


class Neighbours:
    def __init__(self, own, up, down, edges, meta, width):
        half = SUB // 2
        near = lax.broadcasted_iota(jnp.int32, own.shape, 1) < half
        self.col = lax.broadcasted_iota(jnp.int32, own.shape, 1) % width
        self.width, self.shape = width, own.shape
        ha, wa, last = meta[1], meta[2], meta[3]
        up = unpack_bottom(jnp.where(ha > 0, up, 0.0))
        down = unpack_top(jnp.where(ha < last, down, 0.0))
        self.rows = {
            0: own,
            -1: pltpu.roll(jnp.where(near, own, up), half, 1),
            1: pltpu.roll(jnp.where(near, down, own), half, 1),
        }
        beyond = lax.broadcasted_iota(jnp.int32, edges.shape, 0)
        inside = ((ha > 0) | (beyond >= EDGE)) & ((ha < last) | (beyond < 3 * EDGE))
        self.edges = jnp.where(inside, edges, 0.0).astype(BF16)
        shape = (own.shape[0] * SUB, edges.shape[0])
        place, self.source = [lax.broadcasted_iota(jnp.int32, shape, dim) for dim in range(2)]
        self.group = place // SUB
        self.row = place // half % 2
        self.touches = place % width == edge_place(wa, width)
        self.sides = {}

    def side(self, row_step):
        if row_step not in self.sides:
            wanted = (self.row + row_step + 1) * EDGE + self.group
            chosen = ((self.source == wanted) & self.touches).astype(F32).astype(BF16)
            self.sides[row_step] = dot(chosen, self.edges).reshape(self.shape)
        return self.sides[row_step]

    def at(self, row_step, col_step):
        base = self.rows[row_step]
        if col_step < 0:
            return jnp.where(self.col == 0, self.side(row_step), pltpu.roll(base, 1, 1))
        if col_step > 0:
            away = self.col == self.width - 1
            return jnp.where(away, self.side(row_step), pltpu.roll(base, SUB - 1, 1))
        return base


def xor_pairs(size, step):
    return [(index, index ^ step) for index in range(size)]


def direct_sum(value, axis):
    size = lax.axis_size(axis)
    step = 1
    while step < size:
        if size // step >= 4:
            one, two, three = [
                lax.ppermute(value, axis, xor_pairs(size, step * times)) for times in (1, 2, 3)
            ]
            value = (value + two) + (one + three)
            step *= 4
        else:
            value = value + lax.ppermute(value, axis, xor_pairs(size, step))
            step *= 2
    return value


AXES = ("clips", "ha", "wa")
MOST = 32


def spread_count():
    count = lax.axis_size("ha") * lax.axis_size("wa")
    whole = count * lax.axis_size("clips")
    return whole if whole <= MOST else count


def exchange(copies):
    if copies.shape[0] == lax.axis_size("clips") * lax.axis_size("ha") * lax.axis_size("wa"):
        return lax.all_to_all(copies, AXES, 0, 0)
    return lax.all_to_all(direct_sum(copies, "clips"), TILE, 0, 0)


def exchange_widest(sums):
    count = lax.axis_size("ha") * lax.axis_size("wa")
    sums = direct_sum(sums, "clips")
    return lax.all_to_all(jnp.broadcast_to(sums[None], (count,) + sums.shape), TILE, 0, 0)


def exchange_halo(message, rows):
    wide, high = lax.axis_size("wa"), lax.axis_size("ha")
    half = rows // 2
    side = lax.ppermute(message[rows:], "wa", xor_pairs(wide, 1))
    tops = jnp.concatenate([message[:half], side[:EDGE]], axis=0)
    bottoms = jnp.concatenate([message[half:rows], side[EDGE:]], axis=0)
    up = lax.ppermute(bottoms, "ha", [(row, row + 1) for row in range(high - 1)])
    down = lax.ppermute(tops, "ha", [(row + 1, row) for row in range(high - 1)])
    return side, up, down


def time_conv(geo, parts, blocks):
    result = None
    for tap in range(3):
        at = 0
        total = None
        for part in parts:
            lanes = part.shape[-1]
            term = dot(part, blocks[tap][at : at + lanes])
            at += lanes
            total = term if total is None else total + term
        if tap != 1:
            total = geo.shift(total, 1 - tap)
        result = total if result is None else result + total
    return result


def fast_conv(geo, value, main, before, after):
    lanes = value.shape[-1] // PHASES
    result = dot(value, main)
    result = result + geo.shift(dot(value[:, -lanes:], before), 1)
    return result + geo.shift(dot(value[:, :lanes], after), -1)


def fast_conv_back(steps, main, before, after):
    lanes = before.shape[0]
    middle = dot_nt(steps[1], main)
    first = middle[:, :lanes] + dot_nt(steps[2], after)
    last = middle[:, -lanes:] + dot_nt(steps[0], before)
    return jnp.concatenate([first, middle[:, lanes:-lanes], last], axis=1)


def lane_block(value, phase, part):
    return pltpu.roll(value, value.shape[-1] - phase * part, 1) if phase else value


def fast_reduce_grad(value, steps):
    lanes = value.shape[-1] // PHASES
    part = steps[1].shape[-1] // PHASES
    main = dot_tn(value, steps[1])
    before = dot_tn(value[:, -lanes:], steps[0])
    after = dot_tn(value[:, :lanes], steps[2])

    def block(row, col):
        return lane_block(main[row * lanes : (row + 1) * lanes], col, part)

    result = []
    for tap in range(3):
        total = before if tap == 0 else None
        if tap == 2:
            total = lane_block(after, PHASES - 1, part)
        for col in range(PHASES):
            row = col + tap - 1
            if 0 <= row < PHASES:
                total = block(row, col) if total is None else total + block(row, col)
        result.append(total)
    return result


def gather_pack(parts):
    return lax.all_gather(jnp.concatenate(parts, axis=0), TILE, axis=0)


def columns(shard, lanes):
    depth, total = shard.shape
    return jnp.moveaxis(shard.reshape(depth, total // lanes, lanes), 1, 0).reshape(-1, lanes)


def split_phases(value):
    cap, frames, height, width, lanes = value.shape
    value = value.reshape(cap, frames // PHASES, PHASES, height, width, lanes)
    return jnp.moveaxis(value, 2, 4).reshape(-1, PHASES * lanes)


def join_phases(value, shape):
    cap, frames, height, width, lanes = shape
    value = value.reshape(cap, frames // PHASES, height, width, PHASES, lanes)
    return jnp.moveaxis(value, 4, 2).reshape(shape)


def early_gather(shards_one, shards_two, lateral):
    rows = []
    lanes = shards_one[2].shape[-1]
    kinds = [jnp.stack(pair) for pair in zip(shards_one, shards_two)]
    kinds.append(jnp.stack([lateral[..., :lanes], lateral[..., lanes:]]))
    for kind in kinds:
        flat = kind.reshape(-1, kind.shape[-1])
        rows.append(jnp.pad(flat, ((0, 0), (0, lanes - flat.shape[-1]))))
    packed = gather_pack(rows)
    result = []
    at = 0
    for kind in kinds:
        depth, width = kind.shape[-2:]
        number = kind.size // width
        part = packed[:, at : at + number, :width].reshape(packed.shape[0], -1, depth, width)
        at += number
        result.append(jnp.moveaxis(part, 0, 1).reshape(part.shape[1], -1, width))
    return result


def prepare_kernel(taps_ref, space_ref, wide_ref, lateral_ref, *refs):
    slow_one, fast_one, slow_two, fast_two, *outs = refs
    part = taps_ref.shape[-1]
    lateral, *joint = outs[10:]
    number = lateral.shape[0]
    for tap in range(number):
        lateral[tap] = jnp.concatenate([lateral_ref[tap], lateral_ref[number + tap]], axis=1)
    for layer, (slow, fast) in enumerate(((slow_one, fast_one), (slow_two, fast_two))):
        at = fast_at = 0
        for ref in joint[3 * layer : 3 * layer + 3]:
            fast_lanes = part if ref.shape[1] < slow.shape[1] // 2 else wide_ref.shape[-1]
            lanes = ref.shape[1] - PHASES * fast_lanes
            values = [slow[:, at : at + lanes]]
            values += [fast[:, fast_at : fast_at + fast_lanes]] * PHASES
            ref[...] = jnp.concatenate(values, axis=1)
            at, fast_at = at + lanes, fast_at + fast_lanes
    joint[6][...] = slow_one[:, slow_one.shape[1] - joint[6].shape[1] :]
    for layer in range(2):
        main, before, after, space, wide = outs[5 * layer : 5 * layer + 5]
        taps = [taps_ref[3 * layer + tap] for tap in range(3)]
        zero = jnp.zeros_like(taps[0])
        lanes = taps[0].shape[0]
        for row in range(PHASES):
            blocks = [
                taps[row - col + 1] if abs(row - col) <= 1 else zero for col in range(PHASES)
            ]
            main[row * lanes : (row + 1) * lanes, :] = jnp.concatenate(blocks, axis=1)
        before[...] = jnp.concatenate([taps[0]] + [zero] * (PHASES - 1), axis=1)
        after[...] = jnp.concatenate([zero] * (PHASES - 1) + [taps[2]], axis=1)
        for tap in range(9):
            block = space_ref[9 * layer + tap]
            none = jnp.zeros_like(block)
            for row in range(PHASES):
                blocks = [block if row == col else none for col in range(PHASES)]
                space[tap, row * part : (row + 1) * part, :] = jnp.concatenate(blocks, axis=1)
        block = wide_ref[layer]
        none = jnp.zeros_like(block)
        for row in range(PHASES):
            blocks = [block if row == col else none for col in range(PHASES)]
            wide[row * part : (row + 1) * part, :] = jnp.concatenate(blocks, axis=1)


def to_partners(pieces, axis):
    size = lax.axis_size(axis)
    return [
        lax.ppermute(piece, axis, xor_pairs(size, step + 1)) for step, piece in enumerate(pieces)
    ]


def share_with_clips(own, got):
    total = own.astype(F32)
    for piece in got:
        total = total + piece.astype(F32)
    total = total.astype(BF16)
    return [total] + to_partners([total] * len(got), "clips")


def sum_over_clips(meta, groups):
    size = lax.axis_size("clips")
    if size > 4:
        added = [sum(part.astype(F32) for part in group).astype(BF16) for group in groups]
        return [lax.psum(jnp.concatenate(added), "clips")]
    lanes = groups[0][0].shape[1]
    depths = [group[0].shape[0] // size for group in groups]
    number = sum(len(group) for group in groups)

    def kernel(meta_ref, *refs):
        ins, outs, total_ref = list(refs[:number]), refs[number:-1], refs[-1]
        places = []
        at = 0
        for group, depth in zip(groups, depths):
            mine, ins = ins[: len(group)], ins[len(group) :]
            total = mine[0][...]
            if len(mine) > 1:
                total = total.astype(F32)
                for ref in mine[1:]:
                    total = total + ref[...].astype(F32)
                total = total.astype(BF16)
            total_ref[at : at + depth * size, :] = total
            places.append(at)
            at += depth * size
        for step, out in enumerate(outs):
            low = 0
            for place, depth in zip(places, depths):
                start = pl.multiple_of(place + (meta_ref[4] ^ step) * depth, 16)
                out[low : low + depth, :] = total_ref[pl.ds(start, depth), :]
                low += depth
            out.send()

    quarters = run(
        kernel,
        [((sum(depths), lanes), BF16, "hbm")] * size,
        smem=(meta,),
        saved=[part for group in groups for part in group],
        scratch=(pltpu.VMEM((sum(depths) * size, lanes), BF16),),
    )
    return share_with_clips(quarters[0], to_partners(quarters[1:], "clips"))


def on_device(
    slow_input,
    fast_input,
    slow_cotangent,
    fast_cotangent,
    clip_counts,
    lateral_weight,
    slow_reduce_one,
    slow_spatial_one,
    slow_expand_one,
    slow_shortcut_one,
    fast_reduce_one,
    fast_spatial_one,
    fast_expand_one,
    slow_reduce_two,
    slow_spatial_two,
    slow_expand_two,
    fast_reduce_two,
    fast_spatial_two,
    fast_expand_two,
    slow_norms_one,
    fast_norms_one,
    slow_norms_two,
    fast_norms_two,
):
    geo = Geometry(slow_input.shape, fast_input.shape)
    rows, groups = geo.rows, geo.groups
    half_rows = rows // 2
    count = lax.axis_size("ha") * lax.axis_size("wa")
    spread = spread_count()
    slow_wide = slow_input.shape[-1]
    fast_wide = PHASES * fast_input.shape[-1]
    wide = slow_wide + fast_wide
    mid = slow_reduce_one.shape[-1]
    fast_part = fast_reduce_one.shape[-1]
    fast_mid = PHASES * fast_part
    small = mid + fast_mid
    lat = lateral_weight.shape[-1]
    blocks = slow_wide // mid

    depth_one = slow_reduce_one.shape[1]
    depth_two = slow_reduce_two.shape[1]
    depth_mid = slow_spatial_one.shape[2]
    depth_lat = lateral_weight.shape[1]
    near = gather_pack([slow_reduce_one.reshape(-1, mid), slow_spatial_one.reshape(-1, mid)])
    far = gather_pack(
        [
            columns(slow_expand_one, mid),
            columns(slow_shortcut_one, mid),
            slow_reduce_two.reshape(-1, mid),
        ]
    )
    last = gather_pack([slow_spatial_two.reshape(-1, mid), columns(slow_expand_two, mid)])
    at_space_one = 3 * depth_one
    at_short = blocks * depth_mid
    at_reduce_two = at_short + blocks * depth_one
    at_space_two = 0
    at_expand_two = 9 * depth_mid
    fast_shards_one = (fast_reduce_one, fast_spatial_one, fast_expand_one)
    fast_shards_two = (fast_reduce_two, fast_spatial_two, fast_expand_two)
    compact = early_gather(fast_shards_one, fast_shards_two, lateral_weight)
    structured = [
        ((fast_wide, fast_mid), BF16, "hbm"),
        ((fast_wide // PHASES, fast_mid), BF16, "hbm"),
        ((fast_wide // PHASES, fast_mid), BF16, "hbm"),
        ((9, fast_mid, fast_mid), BF16, "hbm"),
        ((fast_mid, fast_wide), BF16, "hbm"),
    ]
    joint_outs = [((2, lanes), F32, "hbm") for lanes in (small, small, wide)]
    prepared = run(
        prepare_kernel,
        structured * 2
        + [((lateral_weight.shape[0], fast_wide // PHASES, lat), BF16, "hbm")]
        + joint_outs * 2
        + [((2, slow_wide), F32, "hbm")],
        vmem=(*compact, slow_norms_one, fast_norms_one, slow_norms_two, fast_norms_two),
    )
    fast_one, fast_two, lateral = prepared[:5], prepared[5:10], prepared[10]
    params_one, params_two, params_short = prepared[11:14], prepared[14:17], prepared[17]

    held = clip_counts[0]
    clips = direct_sum(jnp.full((1, 128), held, F32), "clips")[0, 0]
    positions = clips * (SUB * geo.frames * count)
    inv_n = jnp.stack([1.0 / positions, 1.0 / (positions * PHASES)])
    ha, wa = lax.axis_index("ha"), lax.axis_index("wa")
    last_ha = jnp.full_like(ha, lax.axis_size("ha") - 1)
    meta = jnp.stack([held * geo.frames, ha, wa, last_ha, lax.axis_index("clips")])
    scalars = (meta, inv_n)

    slow_x = slow_input.reshape(rows, slow_wide)
    fast_x = split_phases(fast_input)
    cot = jnp.concatenate(
        [slow_cotangent.reshape(rows, slow_wide), split_phases(fast_cotangent)], axis=1
    )
    message_out = ((rows + 2 * EDGE, small), BF16, "hbm")
    stats_small = ((spread, 2, small), F32, "spread")
    stats_wide = ((spread, 2, wide), F32, "spread")
    stats_both = ((2, wide + slow_wide), F32, "vmem")
    small_out = ((rows, small), F32, "hbm")
    wide_out = ((rows, wide), F32, "hbm")
    small_both = ((rows, small), F32, "both")
    small_next = ((rows, small), F32, "vmem")
    wide_both = ((rows, wide), F32, "both")

    def lateral_kernel(x_ref, k_ref, main_ref, before_ref, after_ref, united_ref, fast_ref):
        lanes = x_ref.shape[1] // PHASES
        x = x_ref[...]
        main = dot(x[:, : 3 * lanes], k_ref[2:5].reshape(3 * lanes, lat))
        past = dot(x[:, 2 * lanes :], k_ref[0:2].reshape(2 * lanes, lat))
        united_ref[...] = (main + geo.shift(past, 1)).astype(BF16)
        fast_ref[...] = fast_conv(geo, x, main_ref[...], before_ref[...], after_ref[...])

    united, za_fast = run(
        lateral_kernel,
        [((rows, lat), BF16, "hbm"), ((rows, fast_mid), F32, "hbm")],
        saved=(fast_x, lateral, *fast_one[:3]),
    )

    def reduce_one_kernel(
        meta_ref, x_ref, united_ref, fast_ref, loads, za_ref, stats_ref, message_ref
    ):
        weights = [loads.get(tap) for tap in range(3)]
        za = time_conv(geo, (x_ref[...], united_ref[...]), weights)
        za = jnp.concatenate([za, fast_ref[...]], axis=1)
        za_ref[...] = za
        za_ref.send()
        za = geo.three(za)
        put_message(za, message_ref, meta_ref, geo.width)
        put_forward(stats_ref, za, meta_ref[0])

    za_one, za_next, stats, message = run(
        reduce_one_kernel,
        [small_both, stats_small, message_out],
        smem=(meta,),
        saved=(slow_x, united, za_fast),
        weights=((near, 0, 3, depth_one),),
    )
    parts_a1 = exchange(stats)
    halo_one = exchange_halo(message, rows)

    def space_stage(za, parts_a, halo, params, gathered, offset, fast_w):
        def kernel(
            meta_ref,
            inv_ref,
            stats_ref,
            za_ref,
            side_ref,
            up_ref,
            down_ref,
            params_ref,
            fast_ref,
            loads,
            zb_ref,
            hidden_ref,
            out_stats,
        ):
            scale, shift, _, _ = affine(stats_ref, params_ref, inv_ref, mid)

            def act(value):
                return silu(geo.three(value.astype(F32)) * scale + shift)

            own = act(za_ref[...])
            edges = jnp.concatenate(
                [up_ref[half_rows:], side_ref[...], down_ref[half_rows:]], axis=0
            )
            hidden_ref[...] = geo.flat(own).astype(BF16)
            hidden_ref.send()
            near_by = Neighbours(
                own,
                act(up_ref[:half_rows]),
                act(down_ref[:half_rows]),
                geo.flat(act(edges)),
                meta_ref,
                geo.width,
            )
            slow = fast = None
            for tap in range(9):
                moved = geo.flat(near_by.at(tap // 3 - 1, tap % 3 - 1)).astype(BF16)
                slow_term = dot(moved[:, :mid], loads.get(tap))
                fast_term = dot(moved[:, mid:], fast_ref[tap])
                slow = slow_term if slow is None else slow + slow_term
                fast = fast_term if fast is None else fast + fast_term
            zb = jnp.concatenate([slow, fast], axis=1)
            zb_ref[...] = zb
            zb_ref.send()
            put_forward(out_stats, geo.three(zb), meta_ref[0])

        zb, zb_next, hidden, stats, stats_a = run(
            kernel,
            [small_both, ((rows, small), BF16, "hbm"), stats_small],
            smem=scalars,
            parts=(parts_a,),
            vmem=(za,),
            saved=(*halo, params, fast_w),
            weights=((gathered, offset, 9, depth_mid),),
        )
        return zb, zb_next, hidden, exchange(stats), stats_a

    zb_one, zb_next, ha_one, parts_b1, stats_a1 = space_stage(
        za_next, parts_a1, halo_one, params_one[0], near, at_space_one, fast_one[3]
    )

    def expand_body(inv_ref, stats_ref, zb_ref, params_ref, fast_ref, hidden_ref, zc_ref, loads):
        scale, shift, _, _ = affine(stats_ref, params_ref, inv_ref, mid)
        hidden = geo.flat(silu(geo.three(zb_ref[...]) * scale + shift)).astype(BF16)
        hidden_ref[...] = hidden
        hidden_ref.send()
        zc_ref[:, slow_wide:] = dot(hidden[:, mid:], fast_ref[...])
        for block in range(blocks):
            zc_ref[:, block * mid : (block + 1) * mid] = dot(hidden[:, :mid], loads.get(block))
        zc_ref.send()

    def expand_one_kernel(
        meta_ref,
        inv_ref,
        stats_ref,
        zb_ref,
        params_ref,
        fast_ref,
        x_ref,
        united_ref,
        loads,
        shorts,
        hidden_ref,
        zc_ref,
        short_ref,
        out_stats,
    ):
        expand_body(inv_ref, stats_ref, zb_ref, params_ref, fast_ref, hidden_ref, zc_ref, loads)
        put_forward(out_stats, geo.three(zc_ref[...]), meta_ref[0])
        for block in range(blocks):
            weight = shorts.get(block)
            value = dot(x_ref[...], weight[:slow_wide]) + dot(united_ref[...], weight[slow_wide:])
            short_ref[:, block * mid : (block + 1) * mid] = value
            put_forward(out_stats, geo.three(value), meta_ref[0], wide + block * mid)
        short_ref.send()

    hb_one, zc_one, zc_next, short, short_next, stats, stats_b1 = run(
        expand_one_kernel,
        [((rows, small), BF16, "hbm"), wide_both, ((rows, slow_wide), F32, "both"), stats_both],
        smem=scalars,
        parts=(parts_b1,),
        vmem=(zb_next,),
        saved=(params_one[1], fast_one[4], slow_x, united),
        weights=((far, 0, blocks, depth_mid), (far, at_short, blocks, depth_one)),
    )
    parts_c1 = exchange_widest(stats)

    def reduce_two_kernel(
        meta_ref,
        inv_ref,
        stats_ref,
        zc_ref,
        short_ref,
        params_ref,
        short_params_ref,
        x_ref,
        main_ref,
        before_ref,
        after_ref,
        loads,
        sum_ref,
        low_ref,
        za_ref,
        out_stats,
        message_ref,
    ):
        scale, shift, _, _ = affine(stats_ref, params_ref, inv_ref, slow_wide, 0, wide)
        scale_s, shift_s, _, _ = affine(
            stats_ref, short_params_ref, inv_ref, slow_wide, wide, wide + slow_wide
        )
        normed = geo.three(zc_ref[...]) * scale + shift
        slow = normed[..., :slow_wide] + (geo.three(short_ref[...]) * scale_s + shift_s)
        fast = normed[..., slow_wide:] + geo.three(x_ref[...].astype(F32))
        total = jnp.concatenate([slow, fast], axis=-1)
        sum_ref[...] = geo.flat(total)
        sum_ref.send()
        low = geo.flat(silu(total)).astype(BF16)
        low_ref[...] = low
        low_ref.send()
        weights = [loads.get(tap) for tap in range(3)]
        za = time_conv(geo, (low[:, :slow_wide],), weights)
        fast_za = fast_conv(
            geo, low[:, slow_wide:], main_ref[...], before_ref[...], after_ref[...]
        )
        za = jnp.concatenate([za, fast_za], axis=1)
        za_ref[...] = za
        za_ref.send()
        za = geo.three(za)
        put_message(za, message_ref, meta_ref, geo.width)
        put_forward(out_stats, za, meta_ref[0])

    sum_one, low_one, za_two, za_next, stats, message, stats_c1 = run(
        reduce_two_kernel,
        [wide_out, ((rows, wide), BF16, "hbm"), small_both, stats_small, message_out],
        smem=scalars,
        parts=(parts_c1,),
        vmem=(zc_next, short_next),
        saved=(params_one[2], params_short, fast_x, *fast_two[:3]),
        weights=((far, at_reduce_two, 3, depth_two),),
    )
    parts_a2 = exchange(stats)
    halo_two = exchange_halo(message, rows)
    zb_two, zb_next, ha_two, parts_b2, stats_a2 = space_stage(
        za_next, parts_a2, halo_two, params_two[0], last, at_space_two, fast_two[3]
    )

    def expand_two_kernel(
        meta_ref,
        inv_ref,
        stats_ref,
        zb_ref,
        params_ref,
        fast_ref,
        loads,
        hidden_ref,
        zc_ref,
        out_stats,
    ):
        expand_body(inv_ref, stats_ref, zb_ref, params_ref, fast_ref, hidden_ref, zc_ref, loads)
        put_forward(out_stats, geo.three(zc_ref[...]), meta_ref[0])

    hb_two, zc_two, zc_next, stats, stats_b2 = run(
        expand_two_kernel,
        [((rows, small), BF16, "hbm"), wide_both, stats_wide],
        smem=scalars,
        parts=(parts_b2,),
        vmem=(zb_next,),
        saved=(params_two[1], fast_two[4]),
        weights=((last, at_expand_two, blocks, depth_mid),),
    )
    parts_c2 = exchange(stats)

    def head_kernel(
        meta_ref, inv_ref, stats_ref, zc_ref, params_ref, sum_ref, cot_ref, out_ref, g_ref, sums_ref
    ):
        scale, shift, mean, inv = affine(stats_ref, params_ref, inv_ref, slow_wide)
        zc = geo.three(zc_ref[...])
        total = zc * scale + shift + silu(geo.three(sum_ref[...]))
        valid = mask_groups(total.shape, meta_ref[0])
        sigma = jax.nn.sigmoid(total)
        out_ref[...] = geo.flat(jnp.where(valid, total * sigma, 0.0)).astype(BF16)
        slopes = sigma * (1.0 + total * (1.0 - sigma))
        gradient = jnp.where(valid, geo.three(cot_ref[...].astype(F32)) * slopes, 0.0)
        out_ref.send()
        g_ref[...] = geo.flat(gradient)
        g_ref.send()
        put_back(sums_ref, gradient, (zc - mean) * inv)

    outputs, g_two, g_next, sums, stats_c2 = run(
        head_kernel,
        [((rows, wide), BF16, "hbm"), wide_both, stats_wide],
        smem=scalars,
        parts=(parts_c2,),
        vmem=(zc_next,),
        saved=(params_two[2], sum_one, cot),
    )
    parts_c2 = exchange(sums)

    def norm_back(gradient, value, coeffs, sums, valid):
        scale, _, mean, inv = coeffs
        crossed = (value - mean) * inv * sums[0] + sums[1]
        return scale * (gradient - jnp.where(valid, crossed, 0.0))

    def expand_back_body(
        meta_ref,
        inv_ref,
        sums_ref,
        g_ref,
        stats_ref,
        stats_b_ref,
        zc_ref,
        params_ref,
        zb_ref,
        params_b_ref,
        fast_ref,
        loads,
        gz_ref,
        g_out,
        sums_out,
        message_ref,
    ):
        limit = meta_ref[0]
        coeffs = affine(stats_ref, params_ref, inv_ref, slow_wide, 0, wide)
        both = [back_rows(sums_ref, inv_ref, slow_wide, row, 0, wide) for row in range(2)]
        gradient = geo.three(g_ref[...])
        gz = norm_back(
            gradient, geo.three(zc_ref[...]), coeffs, both, mask_groups(gradient.shape, limit)
        )
        gz = geo.flat(gz).astype(BF16)
        gz_ref[...] = gz
        gz_ref.send()
        fast = dot_nt(gz[:, slow_wide:], fast_ref[...])
        slow = None
        for block in range(blocks):
            term = dot_nt(gz[:, block * mid : (block + 1) * mid], loads.get(block))
            slow = term if slow is None else slow + term
        scale, shift, mean, inv = affine(stats_b_ref, params_b_ref, inv_ref, mid)
        zb = geo.three(zb_ref[...])
        back = geo.three(jnp.concatenate([slow, fast], axis=1)) * slope(zb * scale + shift)
        g_out[...] = geo.flat(back)
        put_message(
            jnp.concatenate([back, zb], axis=-1), message_ref, meta_ref, geo.width
        )
        masked = jnp.where(mask_groups(back.shape, limit), back, 0.0)
        put_back(sums_out, masked, (zb - mean) * inv)
        return gradient

    message_back = ((rows + 2 * EDGE, 2 * small), BF16, "hbm")
    gz_c2, g_b2, sums, message, sums_c2 = run(
        expand_back_body,
        [((rows, wide), BF16, "hbm"), small_next, stats_small, message_back],
        smem=scalars,
        parts=(parts_c2,),
        vmem=(g_next,),
        saved=(stats_c2, stats_b2, zc_two, params_two[2], zb_two, params_two[1], fast_two[4]),
        weights=((last, at_expand_two, blocks, depth_mid),),
    )
    parts_b2 = exchange(sums)
    halo_back_two = exchange_halo(message, rows)
    align = 16 * lax.axis_size("clips")

    def aligned(number):
        return number + -number % align


    lanes_fast = fast_wide // PHASES
    fast_rows_count = fast_reduce_one.shape[1] + 2 * SUB

    def expand_grad(hb_ref, gz_ref, out_ref, at):
        for block in range(blocks):
            value = dot_tn(hb_ref[:, :mid], gz_ref[:, block * mid : (block + 1) * mid])
            low = at + block * depth_mid
            out_ref[:, low : low + depth_mid, :] = value.astype(BF16).reshape(
                count, depth_mid, mid
            )

    def fast_expand_grad(hb_ref, gz_ref):
        fast = dot_tn(hb_ref[:, mid:], gz_ref[:, slow_wide:])
        total = None
        for phase in range(PHASES):
            part = fast[
                phase * fast_part : (phase + 1) * fast_part,
                phase * lanes_fast : (phase + 1) * lanes_fast,
            ]
            total = part if total is None else total + part
        return total

    def space_grad(ha_ref, taps_ref, out_ref, at):
        fast_grads = []
        for tap in range(9):
            value = dot_tn(ha_ref[:, :mid], taps_ref[tap, :, :mid])
            low = at + tap * depth_mid
            out_ref[:, low : low + depth_mid, :] = value.astype(BF16).reshape(
                count, depth_mid, mid
            )
            fast = dot_tn(ha_ref[:, mid:], taps_ref[tap, :, mid:])
            total = None
            for phase in range(PHASES):
                part = lane_block(
                    fast[phase * fast_part : (phase + 1) * fast_part], phase, fast_part
                )
                total = part if total is None else total + part
            fast_grads.append(total)
        return fast_grads

    def put_fast(reduce, space, expand, out_ref, at):
        lane = lax.broadcasted_iota(jnp.int32, reduce[0].shape, 1)

        def beside(parts):
            keep = lane[: parts[0].shape[0]]
            total = None
            for place, part in enumerate(parts):
                part = jnp.where(keep < fast_part, part, 0.0)
                part = pltpu.roll(part, place * fast_part, 1) if place else part
                total = part if total is None else total + part
            return total

        depth = reduce[0].shape[0] // count
        taps = beside(reduce).astype(BF16).reshape(count, depth, lanes_fast)
        out_ref[:, at : at + depth, :] = jnp.concatenate([taps, jnp.zeros_like(taps)], axis=-1)

        def spread(value):
            tiles = value.reshape(count // 2, SUB, lanes_fast)
            return jnp.stack([tiles, pltpu.roll(tiles, SUB // 2, 1)], axis=1).reshape(
                count, SUB, lanes_fast
            )

        first = jnp.concatenate([spread(beside(space[0:4])), spread(beside(space[4:8]))], axis=-1)
        second = jnp.concatenate([spread(beside(space[8:9])), spread(expand)], axis=-1)
        both = jnp.concatenate([first, second], axis=1).astype(BF16)
        out_ref[:, at + depth : at + depth + 2 * SUB, :] = both

    def space_back_stage(
        g, zb, za, halo, stats_b, parts_b, params_b, stats_a, params_a, g_hbm, at, fast_w
    ):
        def kernel(
            meta_ref,
            inv_ref,
            sums_b_ref,
            g_ref,
            side_ref,
            up_ref,
            down_ref,
            stats_b_ref,
            stats_a_ref,
            zb_ref,
            za_ref,
            params_b_ref,
            params_a_ref,
            fast_ref,
            loads,
            taps_ref,
            g_out,
            sums_out,
        ):
            limit = meta_ref[0]
            coeffs = affine(stats_b_ref, params_b_ref, inv_ref, mid)
            both = [back_rows(sums_b_ref, inv_ref, mid, row) for row in range(2)]

            def back(gradient, value, valid):
                return norm_back(gradient, value, coeffs, both, valid)

            def halo_back(value, scale):
                value = geo.three(value.astype(F32))
                valid = mask_groups(value[..., :small].shape, limit, scale)
                return back(value[..., :small], value[..., small:], valid)

            def edge_back(value):
                value = geo.three(value.astype(F32))
                shape = value[..., :small].shape
                group = lax.broadcasted_iota(jnp.int32, shape, 0) * SUB % EDGE
                group = group + lax.broadcasted_iota(jnp.int32, shape, 1)
                return geo.flat(back(value[..., :small], value[..., small:], group < limit))

            own, zb = geo.three(g_ref[...]), geo.three(zb_ref[...])
            edges = jnp.concatenate(
                [up_ref[half_rows:], side_ref[...], down_ref[half_rows:]], axis=0
            )

            near_by = Neighbours(
                back(own, zb, mask_groups(own.shape, limit)),
                halo_back(up_ref[:half_rows], 2),
                halo_back(down_ref[:half_rows], 2),
                edge_back(edges),
                meta_ref,
                geo.width,
            )
            slow = fast = None
            for tap in range(9):
                moved = geo.flat(near_by.at(1 - tap // 3, 1 - tap % 3)).astype(BF16)
                taps_ref[tap] = moved
                if tap == 8:
                    taps_ref.send()
                slow_term = dot_nt(moved[:, :mid], loads.get(tap))
                fast_term = dot_nt(moved[:, mid:], fast_ref[tap])
                slow = slow_term if slow is None else slow + slow_term
                fast = fast_term if fast is None else fast + fast_term
            scale, shift, mean, inv = affine(stats_a_ref, params_a_ref, inv_ref, mid)
            za = geo.three(za_ref[...])
            result = geo.three(jnp.concatenate([slow, fast], axis=1)) * slope(za * scale + shift)
            g_out[...] = geo.flat(result)
            masked = jnp.where(mask_groups(result.shape, limit), result, 0.0)
            put_back(sums_out, masked, (za - mean) * inv)

        taps, g, sums, sums_b = run(
            kernel,
            [((9, rows, small), BF16, "hbm"), small_next, stats_small],
            smem=scalars,
            parts=(parts_b,),
            vmem=(g,),
            saved=(*halo, stats_b, stats_a, zb, za, params_b, params_a, fast_w),
            weights=((g_hbm, at, 9, depth_mid),),
        )
        return taps, g, exchange(sums), sums_b

    taps_two, g_a2, parts_a2, sums_b2 = space_back_stage(
        g_b2,
        zb_two,
        za_two,
        halo_back_two,
        stats_b2,
        parts_b2,
        params_two[1],
        stats_a2,
        params_two[0],
        last,
        at_space_two,
        fast_two[3],
    )
    def grads_two_kernel(hb_ref, gz_ref, ha_ref, taps_ref, out_ref, fast_out):
        space = space_grad(ha_ref, taps_ref, out_ref, 0)
        expand_grad(hb_ref, gz_ref, out_ref, 9 * depth_mid)
        out_ref.send()
        for tap in range(9):
            fast_out[tap] = space[tap]
        fast_out[9] = fast_expand_grad(hb_ref, gz_ref)

    rows_space = aligned((9 + blocks) * depth_mid)
    packed_space, fast_space_two = run(
        grads_two_kernel,
        [((count, rows_space, mid), BF16, "hbm"), ((10, fast_part, lanes_fast), F32, "hbm")],
        saved=(hb_two, gz_c2, ha_two, taps_two),
    )
    sum_space = lax.psum_scatter(packed_space, TILE, scatter_dimension=0, tiled=False)

    def reduce_gz(meta_ref, inv_ref, g_ref, za_ref, stats_ref, sums_ref, params_ref, steps_ref):
        coeffs = affine(stats_ref, params_ref, inv_ref, mid)
        both = [back_rows(sums_ref, inv_ref, mid, row) for row in range(2)]
        gradient = geo.three(g_ref[...])
        gz = norm_back(
            gradient,
            geo.three(za_ref[...]),
            coeffs,
            both,
            mask_groups(gradient.shape, meta_ref[0]),
        )
        gz = geo.flat(gz)
        steps = [geo.shift(gz, -1).astype(BF16), gz.astype(BF16), geo.shift(gz, 1).astype(BF16)]
        for tap in range(3):
            steps_ref[tap] = steps[tap]
        if isinstance(steps_ref, Store):
            steps_ref.send()
        return steps

    def reduce_back_two_kernel(
        meta_ref,
        inv_ref,
        sums_ref,
        g_ref,
        stats_ref,
        stats_c_ref,
        za_ref,
        params_ref,
        g_two_ref,
        sum_ref,
        zc_ref,
        short_ref,
        main_ref,
        before_ref,
        after_ref,
        loads,
        steps_ref,
        g_out,
        sums_out,
    ):
        steps = reduce_gz(
            meta_ref, inv_ref, g_ref, za_ref, stats_ref, sums_ref, params_ref, steps_ref
        )
        slow = None
        for tap in range(3):
            term = dot_nt(steps[tap][:, :mid], loads.get(tap))
            slow = term if slow is None else slow + term
        fast = fast_conv_back(
            [step[:, mid:] for step in steps], main_ref[...], before_ref[...], after_ref[...]
        )
        back = jnp.concatenate([slow, fast], axis=1) + g_two_ref[...]
        back = geo.three(back * slope(sum_ref[...]))
        g_out[...] = geo.flat(back)
        g_out.send()
        masked = jnp.where(mask_groups(back.shape, meta_ref[0]), back, 0.0)
        mean, inv = moments(stats_c_ref, inv_ref, slow_wide, 0, wide)
        put_back(sums_out, masked, (geo.three(zc_ref[...]) - mean) * inv)
        mean, inv = moments(stats_c_ref, inv_ref, slow_wide, wide, wide + slow_wide)
        masked = masked[..., :slow_wide]
        put_back(sums_out, masked, (geo.three(short_ref[...]) - mean) * inv, wide)

    steps_two, g_one, g_next, sums, sums_a2 = run(
        reduce_back_two_kernel,
        [((3, rows, small), BF16, "hbm"), wide_both, stats_both],
        smem=scalars,
        parts=(parts_a2,),
        vmem=(g_a2,),
        saved=(stats_a2, stats_c1, za_two, params_two[0], g_two, sum_one, zc_one, short, *fast_two[:3]),
        weights=((far, at_reduce_two, 3, depth_two),),
    )
    parts_c1 = exchange_widest(sums)

    def expand_back_one_kernel(*refs):
        *body, short_ref, short_params_ref, loads, gz_ref, g_out, sums_out, message, gs_ref = refs
        gradient = expand_back_body(*body, loads, gz_ref, g_out, sums_out, message)
        meta_ref, inv_ref, sums_ref, _, stats_ref = body[:5]
        low, high = wide, wide + slow_wide
        coeffs = affine(stats_ref, short_params_ref, inv_ref, slow_wide, low, high)
        both = [back_rows(sums_ref, inv_ref, slow_wide, row, low, high) for row in range(2)]
        gradient = gradient[..., :slow_wide]
        valid = mask_groups(gradient.shape, meta_ref[0])
        gs = norm_back(gradient, geo.three(short_ref[...]), coeffs, both, valid)
        gs_ref[...] = geo.flat(gs).astype(BF16)

    gz_c1, g_b1, sums, message, gz_short, sums_c1 = run(
        expand_back_one_kernel,
        [((rows, wide), BF16, "hbm"), small_next, stats_small, message_back]
        + [((rows, slow_wide), BF16, "hbm")],
        smem=scalars,
        parts=(parts_c1,),
        vmem=(g_next,),
        saved=(stats_c1, stats_b1, zc_one, params_one[2], zb_one, params_one[1], fast_one[4])
        + (short, params_short),
        weights=((far, 0, blocks, depth_mid),),
    )
    parts_b1 = exchange(sums)
    halo_back_one = exchange_halo(message, rows)
    joined_lanes = slow_wide + lat

    def grads_mid_kernel(
        x_ref,
        united_ref,
        gs_ref,
        hb_ref,
        gz_ref,
        low_ref,
        steps_ref,
        fast_ref,
        loads,
        out_ref,
        back_ref,
    ):
        for tap in range(3):
            value = dot_tn(low_ref[:, :slow_wide], steps_ref[tap, :, :mid])
            out_ref[:, tap * depth_two : (tap + 1) * depth_two, :] = value.astype(BF16).reshape(
                count, depth_two, mid
            )
        at = 3 * depth_two
        reduce = fast_reduce_grad(
            low_ref[:, slow_wide:], [steps_ref[tap, :, mid:] for tap in range(3)]
        )
        put_fast(reduce, [fast_ref[tap] for tap in range(9)], fast_ref[9], out_ref, at)
        at += fast_rows_count
        expand_grad(hb_ref, gz_ref, out_ref, at + blocks * depth_one)
        for block in range(blocks):
            gs = gs_ref[:, block * mid : (block + 1) * mid]
            value = jnp.concatenate([dot_tn(x_ref[...], gs), dot_tn(united_ref[...], gs)], axis=0)
            low = at + block * depth_one
            out_ref[:, low : low + depth_one, :] = value.astype(BF16).reshape(
                count, depth_one, mid
            )
        out_ref.send()
        for block in range(blocks):
            gs = gs_ref[:, block * mid : (block + 1) * mid]
            term = dot_nt(gs, loads.get(block))
            back_ref[...] = term if block == 0 else back_ref[...] + term

    rows_mid = aligned(3 * depth_two + fast_rows_count + blocks * (depth_one + depth_mid))
    packed_mid, short_back = run(
        grads_mid_kernel,
        [((count, rows_mid, mid), BF16, "hbm"), ((rows, joined_lanes), F32, "hbm")],
        saved=(slow_x, united, gz_short, hb_one, gz_c1, low_one, steps_two, fast_space_two),
        weights=((far, at_short, blocks, depth_one),),
    )
    sum_mid = lax.psum_scatter(packed_mid, TILE, scatter_dimension=0, tiled=False)

    taps_one, g_a1, parts_a1, sums_b1 = space_back_stage(
        g_b1,
        zb_one,
        za_one,
        halo_back_one,
        stats_b1,
        parts_b1,
        params_one[1],
        stats_a1,
        params_one[0],
        near,
        at_space_one,
        fast_one[3],
    )
    def last_kernel(
        meta_ref,
        inv_ref,
        sums_ref,
        g_ref,
        stats_ref,
        za_ref,
        params_ref,
        g_one_ref,
        short_ref,
        lateral_ref,
        main_ref,
        before_ref,
        after_ref,
        loads,
        steps_ref,
        slow_ref,
        fast_ref,
        united_ref,
    ):
        steps = reduce_gz(
            meta_ref, inv_ref, g_ref, za_ref, stats_ref, sums_ref, params_ref, steps_ref
        )
        joined = short_ref[...]
        for tap in range(3):
            joined = joined + dot_nt(steps[tap][:, :mid], loads.get(tap))
        slow_ref[...] = joined[:, :slow_wide]
        tail = joined[:, slow_wide:]
        now, past = tail.astype(BF16), geo.shift(tail, -1).astype(BF16)
        united_ref[0] = now
        united_ref[1] = past
        lanes = fast_wide // PHASES
        fast = fast_conv_back(
            [step[:, mid:] for step in steps], main_ref[...], before_ref[...], after_ref[...]
        )
        fast = fast + g_one_ref[:, slow_wide:]
        front = dot_nt(now, lateral_ref[2:5].reshape(3 * lanes, lat))
        back = dot_nt(past, lateral_ref[0:2].reshape(2 * lanes, lat))
        fast_ref[:, : 2 * lanes] = fast[:, : 2 * lanes] + front[:, : 2 * lanes]
        fast_ref[:, 2 * lanes : 3 * lanes] = (
            fast[:, 2 * lanes : 3 * lanes] + front[:, 2 * lanes :] + back[:, :lanes]
        )
        fast_ref[:, 3 * lanes :] = fast[:, 3 * lanes :] + back[:, lanes:]

    steps_one, grad_slow, grad_fast, united_low, sums_a1 = run(
        last_kernel,
        [
            ((3, rows, small), BF16, "hbm"),
            ((rows, slow_wide), F32, "hbm"),
            ((rows, fast_wide), F32, "hbm"),
            ((2, rows, lat), BF16, "hbm"),
        ],
        smem=scalars,
        parts=(parts_a1,),
        vmem=(g_a1,),
        saved=(stats_a1, za_one, params_one[0], g_one, short_back, lateral, *fast_one[:3]),
        weights=((near, 0, 3, depth_one),),
    )

    def grads_one_kernel(
        meta_ref,
        steps_ref,
        low_ref,
        x_ref,
        united_ref,
        fast_x_ref,
        ha_ref,
        taps_ref,
        hb_ref,
        gz_ref,
        own_ref,
        send_ref,
        out_ref,
        sems,
    ):
        lanes = fast_wide // PHASES
        for tap in range(3):
            step = steps_ref[tap, :, :mid]
            value = jnp.concatenate(
                [dot_tn(x_ref[...], step), dot_tn(united_ref[...], step)], axis=0
            )
            out_ref[:, tap * depth_one : (tap + 1) * depth_one, :] = value.astype(BF16).reshape(
                count, depth_one, mid
            )
        at = 3 * depth_one
        past = dot_tn(fast_x_ref[:, 2 * lanes :], low_ref[1])
        now = dot_tn(fast_x_ref[:, : 3 * lanes], low_ref[0])
        both = jnp.concatenate([past, now], axis=0).astype(BF16)
        for tap in range(5):
            out_ref[:, at + tap * depth_lat : at + (tap + 1) * depth_lat, :] = both[
                tap * lanes : (tap + 1) * lanes
            ].reshape(count, depth_lat, lat)
        at += 5 * depth_lat
        space = space_grad(ha_ref, taps_ref, out_ref, at)
        at += 9 * depth_mid
        reduce = fast_reduce_grad(
            fast_x_ref[...], [steps_ref[tap, :, mid:] for tap in range(3)]
        )
        put_fast(reduce, space, fast_expand_grad(hb_ref, gz_ref), out_ref, at)

        put_blocks(out_ref, own_ref, send_ref, meta_ref[1], meta_ref[2], sems)

    def put_blocks(blocks_ref, own_ref, send_ref, ha, wa, sems):
        for block in range(count):
            place, col = ha ^ (block // 2), block % 2
            source, sem = blocks_ref.at[block], sems.at[block]

            @pl.when(wa == col)
            def _():
                pltpu.make_async_copy(source, own_ref.at[place], sem).start()

            @pl.when(wa != col)
            def _():
                pltpu.make_async_copy(source, send_ref.at[place], sem).start()

        for block in range(count):
            pltpu.make_async_copy(blocks_ref.at[block], own_ref.at[0], sems.at[block]).wait()

    high = count // 2
    rows_one = 3 * depth_one + 5 * depth_lat + 9 * depth_mid + fast_rows_count
    rows_late = aligned(rows_one)
    blocks_out = ((high, rows_late, mid), BF16, "raw")
    own_blocks, send_blocks = run(
        grads_one_kernel,
        [blocks_out, blocks_out],
        smem=(meta,),
        saved=(steps_one, united_low, slow_x, united, fast_x, ha_one, taps_one, hb_one, gz_c1),
        scratch=(
            pltpu.VMEM((count, rows_late, mid), BF16),
            pltpu.SemaphoreType.DMA((count,)),
        ),
    )
    side_blocks = lax.ppermute(send_blocks, "wa", xor_pairs(2, 1))

    def chip_kernel(own_ref, side_ref, *out_refs):
        for place in range(high):
            total = own_ref[place].astype(F32) + side_ref[place].astype(F32)
            out_refs[place][...] = total.astype(BF16)
            out_refs[place].send()

    late_out = ((rows_late, mid), BF16, "hbm")
    chip_sums = run(chip_kernel, [late_out] * high, saved=(own_blocks, side_blocks))
    late = [chip_sums[0]] + to_partners(chip_sums[1:], "ha")
    parts_early = sum_over_clips(meta, [[sum_space], [sum_mid]])
    parts_late = sum_over_clips(meta, [late])

    def finish(parts, groups):
        size = len(parts)
        outs_all = []
        for _, shapes in groups:
            for shape in shapes:
                outs_all += list(shape) if isinstance(shape[0], tuple) else [shape]

        def kernel(meta_ref, *refs):
            ins, outs, total_ref = refs[:size], list(refs[size:-1]), refs[-1]
            low = base = 0
            for rows_group, shapes in groups:
                depth = rows_group // size
                for step, ref in enumerate(ins):
                    place = (meta_ref[4] ^ step) if size > 1 else 0
                    start = pl.multiple_of(base + place * depth, 16)
                    total_ref[pl.ds(start, depth), :] = ref[low : low + depth, :].astype(F32)
                at = base
                for shape in shapes:
                    if isinstance(shape[0], tuple):
                        reduce, space, expand = outs.pop(0), outs.pop(0), outs.pop(0)
                        rows_tap, lanes = reduce.shape[1:]
                        for tap in range(3):
                            reduce[tap] = total_ref[
                                at : at + rows_tap, tap * lanes : (tap + 1) * lanes
                            ]
                        few = space.shape[2]
                        for tap in range(9):
                            row = at + rows_tap + tap // SUB * SUB
                            lane = tap % SUB * lanes
                            space[tap // 3, tap % 3] = total_ref[
                                row : row + few, lane : lane + lanes
                            ]
                        row = at + rows_tap + SUB
                        expand[...] = total_ref[row : row + few, expand.shape[1] :]
                        for out in (reduce, space, expand):
                            out.send()
                        at += rows_tap + 2 * SUB
                        continue
                    out = outs.pop(0)
                    if len(shape) == 2 and shape[1] > mid:
                        for block in range(shape[1] // mid):
                            out[:, block * mid : (block + 1) * mid] = total_ref[
                                at : at + shape[0], :
                            ]
                            at += shape[0]
                    else:
                        number = 1
                        for length in shape[:-1]:
                            number *= length
                        out[...] = total_ref[at : at + number, :].reshape(shape)
                        at += number
                    out.send()
                low += depth
                base += rows_group

        return run(
            kernel,
            [(shape, F32, "hbm") for shape in outs_all],
            smem=(meta,),
            saved=parts,
            scratch=(pltpu.VMEM((sum(rows_group for rows_group, _ in groups), mid), F32),),
        )

    shapes_one = tuple(shard.shape for shard in fast_shards_one)
    shapes_two = tuple(shard.shape for shard in fast_shards_two)
    grad_slow_spatial_two, grad_slow_expand_two, grad_slow_reduce_two, *rest = finish(
        parts_early,
        [
            (rows_space, [slow_spatial_two.shape, slow_expand_two.shape]),
            (
                rows_mid,
                [slow_reduce_two.shape, shapes_two, slow_shortcut_one.shape, slow_expand_one.shape],
            ),
        ],
    )
    fast_two_grads, (grad_slow_shortcut, grad_slow_expand_one) = rest[:3], rest[3:]
    grad_slow_reduce_one, grad_lateral, grad_slow_spatial_one, *fast_one_grads = finish(
        parts_late,
        [
            (
                rows_late,
                [slow_reduce_one.shape, lateral_weight.shape, slow_spatial_one.shape, shapes_one],
            )
        ],
    )

    def norm_grads(first, second, third):
        slow = [first[:, :mid], second[:, :mid], third[:, :slow_wide]]
        fast = [first[:, mid:], second[:, mid:], third[:, slow_wide:wide]]
        fast = [jnp.sum(part.reshape(2, PHASES, -1), axis=1) for part in fast]
        return slow, fast

    slow_one_p, fast_one_p = norm_grads(sums_a1, sums_b1, sums_c1)
    slow_two_p, fast_two_p = norm_grads(sums_a2, sums_b2, sums_c2)
    grad_slow_norms_one = jnp.concatenate(slow_one_p + [sums_c1[:, wide:]], axis=1)
    grad_slow_norms_two = jnp.concatenate(slow_two_p, axis=1)
    grad_fast_norms_one = jnp.concatenate(fast_one_p, axis=1)
    grad_fast_norms_two = jnp.concatenate(fast_two_p, axis=1)
    return (
        outputs[:, :slow_wide].reshape(slow_input.shape),
        join_phases(outputs[:, slow_wide:], fast_input.shape),
        grad_slow.reshape(slow_input.shape),
        join_phases(grad_fast, fast_input.shape),
        grad_lateral,
        grad_slow_reduce_one,
        grad_slow_spatial_one,
        grad_slow_expand_one,
        grad_slow_shortcut,
        *fast_one_grads,
        grad_slow_reduce_two,
        grad_slow_spatial_two,
        grad_slow_expand_two,
        *fast_two_grads,
        grad_slow_norms_one,
        grad_fast_norms_one,
        grad_slow_norms_two,
        grad_fast_norms_two,
    )


def solution(mesh):
    in_specs = (
        P("clips", None, "ha", "wa", None),
        P("clips", None, "ha", "wa", None),
        P("clips", None, "ha", "wa", None),
        P("clips", None, "ha", "wa", None),
        P("clips"),
        P(None, ("ha", "wa"), None),
        P(None, ("ha", "wa"), None),
        P(None, None, ("ha", "wa"), None),
        P(("ha", "wa"), None),
        P(("ha", "wa"), None),
        P(None, ("ha", "wa"), None),
        P(None, None, ("ha", "wa"), None),
        P(("ha", "wa"), None),
        P(None, ("ha", "wa"), None),
        P(None, None, ("ha", "wa"), None),
        P(("ha", "wa"), None),
        P(None, ("ha", "wa"), None),
        P(None, None, ("ha", "wa"), None),
        P(("ha", "wa"), None),
        P(),
        P(),
        P(),
        P(),
    )
    out_specs = (
        P("clips", None, "ha", "wa", None),
        P("clips", None, "ha", "wa", None),
        P("clips", None, "ha", "wa", None),
        P("clips", None, "ha", "wa", None),
        P(None, ("ha", "wa"), None),
        P(None, ("ha", "wa"), None),
        P(None, None, ("ha", "wa"), None),
        P(("ha", "wa"), None),
        P(("ha", "wa"), None),
        P(None, ("ha", "wa"), None),
        P(None, None, ("ha", "wa"), None),
        P(("ha", "wa"), None),
        P(None, ("ha", "wa"), None),
        P(None, None, ("ha", "wa"), None),
        P(("ha", "wa"), None),
        P(None, ("ha", "wa"), None),
        P(None, None, ("ha", "wa"), None),
        P(("ha", "wa"), None),
        P(),
        P(),
        P(),
        P(),
    )
    return jax.shard_map(
        on_device, mesh=mesh, in_specs=in_specs, out_specs=out_specs, check_vma=False
    )
```

```python
import jax
import jax.numpy as jnp
from jax import lax
from jax.experimental import pallas as pl
from jax.experimental.pallas import tpu as pltpu
from jax.sharding import PartitionSpec as P

epsilon = 1e-05
F32 = jnp.float32
BF16 = jnp.bfloat16
TILE = ("ha", "wa")
PHASES = 4
SUB = 8


def dot(left, right):
    return lax.dot_general(left, right, (((1,), (0,)), ((), ())), preferred_element_type=F32)


def dot_tn(left, right):
    return lax.dot_general(left, right, (((0,), (0,)), ((), ())), preferred_element_type=F32)


def dot_nt(left, right):
    return lax.dot_general(left, right, (((1,), (1,)), ((), ())), preferred_element_type=F32)


class Loads:
    def __init__(self, source, offset, target, sems, first):
        self.copies = []
        depth = target.shape[2]
        for step in range(target.shape[0]):
            copy = pltpu.make_async_copy(
                source.at[:, pl.ds(offset + step * depth, depth), :],
                target.at[step],
                sems.at[first + step],
            )
            copy.start()
            self.copies.append(copy)
        self.target = target

    def get(self, step):
        self.copies[step].wait()
        block = self.target[step]
        return block.reshape(-1, block.shape[-1])


class Saved:
    def __init__(self, source, scratch, sem):
        self.scratch, self.shape = scratch, scratch.shape
        self.copy = pltpu.make_async_copy(source, scratch, sem)
        self.copy.start()
        self.ready = False

    def wait(self):
        if not self.ready:
            self.copy.wait()
            self.ready = True

    def __getitem__(self, index):
        self.wait()
        return self.scratch[index]


SEGMENTS = 8


class Store:
    def __init__(self, scratch, target, sems):
        self.scratch, self.target, self.shape = scratch, target, scratch.shape
        self.sems, self.copies = sems, []

    def send(self):
        self.copies.append(pltpu.make_async_copy(self.scratch, self.target, self.sems[0]))
        self.copies[-1].start()

    def send_rows(self, low, high):
        rows = pl.ds(low, high - low)
        source, target = self.scratch.at[:, rows, :], self.target.at[:, rows, :]
        self.copies.append(pltpu.make_async_copy(source, target, self.sems[len(self.copies)]))
        self.copies[-1].start()

    def __setitem__(self, index, value):
        self.scratch[index] = value

    def __getitem__(self, index):
        return self.scratch[index]


def run(body, outs, smem=(), parts=(), vmem=(), saved=(), weights=(), scratch=(), limit=54):
    near = pl.BlockSpec(memory_space=pltpu.VMEM)
    far = pl.BlockSpec(memory_space=pltpu.HBM)
    sources = []
    for array, *_ in weights:
        if not any(array is other for other in sources):
            sources.append(array)
    outs = list(outs) + [(part.shape[1:], part.dtype, "hbm") for part in parts]
    flat = []
    for shape, dtype, kind in outs:
        flat += [(shape, dtype, "raw"), (shape, dtype, "vmem")] if kind == "both" else [(shape, dtype, kind)]
    held = [pltpu.VMEM(array.shape, array.dtype) for array in saved]
    for array, _, steps, depth in weights:
        held.append(pltpu.VMEM((steps, array.shape[0], depth, array.shape[2]), array.dtype))
    for shape, dtype, kind in outs:
        if kind in ("hbm", "rows"):
            held.append(pltpu.VMEM(shape, dtype))
        elif kind == "spread":
            held.append(pltpu.VMEM(shape[1:], dtype))
    sems = len(saved) + sum(steps for _, _, steps, _ in weights) + len(outs)
    sems += SEGMENTS * sum(kind == "rows" for _, _, kind in outs)
    held.append(pltpu.SemaphoreType.DMA((sems,)))

    def kernel(*refs):
        refs = list(refs)

        def take(number):
            taken = refs[:number]
            del refs[:number]
            return taken

        smem_refs, part_refs, vmem_refs = take(len(smem)), take(len(parts)), take(len(vmem))
        saved_refs, source_refs, out_refs = take(len(saved)), take(len(sources)), take(len(flat))
        saved_scratch, weight_scratch = take(len(saved)), take(len(weights))
        out_scratch = take(sum(kind in ("hbm", "rows", "spread") for _, _, kind in outs))
        sem, more = refs[0], refs[1:]
        copies = [
            Saved(source, target, sem.at[at])
            for at, (source, target) in enumerate(zip(saved_refs, saved_scratch))
        ]
        at = len(saved)
        loads = []
        for (array, offset, steps, _), target in zip(weights, weight_scratch):
            place = [array is other for other in sources].index(True)
            loads.append(Loads(source_refs[place], offset, target, sem, at))
            at += steps
        results, stores, spreads = [], [], []
        for _, _, kind in outs:
            ref = out_refs.pop(0)
            if kind == "both":
                stores.append(Store(out_refs.pop(0), ref, [sem.at[at]]))
                at += 1
                results.append(stores[-1])
            elif kind in ("hbm", "rows"):
                number = SEGMENTS if kind == "rows" else 1
                stores.append(
                    Store(out_scratch.pop(0), ref, [sem.at[at + part] for part in range(number)])
                )
                at += number
                results.append(stores[-1])
            elif kind == "spread":
                spreads.append((out_scratch.pop(0), ref))
                results.append(spreads[-1][0])
            else:
                results.append(ref)
        sums = results[len(results) - len(parts) :]
        results = results[: len(results) - len(parts)]
        for part, total in zip(part_refs, sums):
            total[...] = jnp.sum(part[...], axis=0)
            total.send()
        totals = [total.scratch for total in sums]
        body(*smem_refs, *totals, *vmem_refs, *copies, *loads, *results, *more)
        for copy in copies:
            copy.wait()
        for store in stores:
            if not store.copies:
                store.send()
        for value, ref in spreads:
            ref[...] = jnp.broadcast_to(value[...][None], ref.shape)
        for store in stores:
            for copy in store.copies:
                copy.wait()

    return pl.pallas_call(
        kernel,
        out_shape=[jax.ShapeDtypeStruct(shape, dtype) for shape, dtype, _ in flat],
        in_specs=[pl.BlockSpec(memory_space=pltpu.SMEM)] * len(smem)
        + [near] * (len(parts) + len(vmem))
        + [far] * (len(saved) + len(sources)),
        out_specs=[far if kind in ("hbm", "rows", "raw") else near for _, _, kind in flat],
        scratch_shapes=held + list(scratch),
        compiler_params=pltpu.CompilerParams(vmem_limit_bytes=limit * 1024 * 1024),
        cost_estimate=pl.CostEstimate(
            flops=2_000_000_000, bytes_accessed=16_000_000, transcendentals=0
        ),
    )(*smem, *parts, *vmem, *saved, *sources)


class Geometry:
    def __init__(self, slow_shape, fast_shape):
        self.cap, self.frames, self.height, self.width = slow_shape[:4]
        self.groups = self.cap * self.frames
        self.rows = self.groups * SUB

    def three(self, value):
        return value.reshape(-1, SUB, value.shape[-1])

    def flat(self, value):
        return value.reshape(-1, value.shape[-1])

    def shift(self, value, step):
        lanes = value.shape[-1]
        whole = value.reshape(self.cap, self.frames, SUB, lanes)
        zero = jnp.zeros((self.cap, 1, SUB, lanes), value.dtype)
        if step > 0:
            whole = jnp.concatenate([zero, whole[:, :-1]], axis=1)
        else:
            whole = jnp.concatenate([whole[:, 1:], zero], axis=1)
        return whole.reshape(-1, lanes)


def mask_groups(shape, limit, scale=1):
    return lax.broadcasted_iota(jnp.int32, shape, 0) * scale < limit


def rep(ref, row, low, high):
    return jnp.broadcast_to(ref[row : row + 1, low:high], (SUB, high - low))


def fold(value, slow):
    fast = value[:, slow:]
    lanes = fast.shape[-1]
    part = lanes // PHASES
    if part % 128 == 0:
        total = fast[:, :part]
        for phase in range(1, PHASES):
            total = total + fast[:, phase * part : (phase + 1) * part]
        return jnp.concatenate([value[:, :slow]] + [total] * PHASES, axis=1)
    total = fast
    for phase in range(1, PHASES):
        total = total + pltpu.roll(fast, phase * part, 1)
    return jnp.concatenate([value[:, :slow], total], axis=1)


def lane_counts(inv_ref, lanes, slow):
    lane = lax.broadcasted_iota(jnp.int32, (SUB, lanes), 1)
    return jnp.where(lane < slow, inv_ref[0], inv_ref[1])


def moments(stats, inv_ref, slow, low=0, high=None):
    high = stats.shape[1] if high is None else high
    total, square = rep(stats, 0, low, high), rep(stats, 1, low, high)
    if slow < high - low:
        total, square = fold(total, slow), fold(square, slow)
    inv_n = lane_counts(inv_ref, high - low, slow)
    mean = total * inv_n
    return mean, lax.rsqrt(square * inv_n - mean * mean + epsilon)


def affine(stats, params, inv_ref, slow, low=0, high=None):
    mean, inv = moments(stats, inv_ref, slow, low, high)
    lanes = mean.shape[1]
    scale = (1.0 + rep(params, 0, 0, lanes)) * inv
    return scale, rep(params, 1, 0, lanes) - mean * scale, mean, inv


def back_rows(sums, inv_ref, slow, row, low=0, high=None):
    high = sums.shape[1] if high is None else high
    total = rep(sums, row, low, high)
    if slow < high - low:
        total = fold(total, slow)
    return total * lane_counts(inv_ref, high - low, slow)


def silu(value):
    return value * jax.nn.sigmoid(value)


def slope(value):
    sigma = jax.nn.sigmoid(value)
    return sigma * (1.0 + value * (1.0 - sigma))


def put_stats(ref, first, second, low=0):
    lanes = first.shape[-1]
    ref[0:1, low : low + lanes] = jnp.sum(jnp.sum(first, axis=0), axis=0, keepdims=True)
    ref[1:2, low : low + lanes] = jnp.sum(jnp.sum(second, axis=0), axis=0, keepdims=True)


def put_back(ref, gradient, normal, low=0):
    put_stats(ref, gradient * normal, gradient, low)


def put_forward(ref, value, limit, low=0):
    masked = jnp.where(mask_groups(value.shape, limit), value, 0.0)
    put_stats(ref, masked, masked * value, low)


EDGE = 32


def edge_place(wa, width):
    return jnp.where(wa > 0, 0, width - 1)


def put_message(value, ref, meta_ref, width):
    lanes = value.shape[-1]
    pairs = value.reshape(-1, 2, SUB, lanes)
    first, second = pairs[:, 0], pairs[:, 1]
    near = lax.broadcasted_iota(jnp.int32, first.shape, 1) < SUB // 2
    top = jnp.where(near, first, pltpu.roll(second, SUB // 2, 1))
    bottom = jnp.where(near, pltpu.roll(first, SUB // 2, 1), second)
    flat = value.reshape(-1, lanes).astype(BF16)
    shape = (2 * EDGE, flat.shape[0])
    row, col = [lax.broadcasted_iota(jnp.int32, shape, dim) for dim in range(2)]
    low = row >= EDGE
    source = (row - jnp.where(low, EDGE, 0)) * SUB + jnp.where(low, SUB // 2, 0)
    chosen = (col == source + edge_place(meta_ref[2], width)).astype(F32).astype(BF16)
    edges = dot(chosen, flat)
    at = 0
    for part in (top, bottom, edges):
        part = part.reshape(-1, lanes).astype(BF16)
        ref[at : at + part.shape[0]] = part
        at += part.shape[0]
    ref.send()


def unpack_bottom(value):
    both = jnp.stack([pltpu.roll(value, SUB // 2, 1), value], axis=1)
    return both.reshape(-1, SUB, value.shape[-1])


def unpack_top(value):
    both = jnp.stack([value, pltpu.roll(value, SUB // 2, 1)], axis=1)
    return both.reshape(-1, SUB, value.shape[-1])


class Neighbours:
    def __init__(self, own, up, down, edges, meta, width):
        half = SUB // 2
        near = lax.broadcasted_iota(jnp.int32, own.shape, 1) < half
        self.col = lax.broadcasted_iota(jnp.int32, own.shape, 1) % width
        self.width, self.shape = width, own.shape
        ha, wa, last = meta[1], meta[2], meta[3]
        up = unpack_bottom(jnp.where(ha > 0, up, 0.0))
        down = unpack_top(jnp.where(ha < last, down, 0.0))
        self.rows = {
            0: own,
            -1: pltpu.roll(jnp.where(near, own, up), half, 1),
            1: pltpu.roll(jnp.where(near, down, own), half, 1),
        }
        beyond = lax.broadcasted_iota(jnp.int32, edges.shape, 0)
        inside = ((ha > 0) | (beyond >= EDGE)) & ((ha < last) | (beyond < 3 * EDGE))
        self.edges = jnp.where(inside, edges, 0.0).astype(BF16)
        shape = (own.shape[0] * SUB, edges.shape[0])
        place, self.source = [lax.broadcasted_iota(jnp.int32, shape, dim) for dim in range(2)]
        self.group = place // SUB
        self.row = place // half % 2
        self.touches = place % width == edge_place(wa, width)
        self.sides = {}

    def side(self, row_step):
        if row_step not in self.sides:
            wanted = (self.row + row_step + 1) * EDGE + self.group
            chosen = ((self.source == wanted) & self.touches).astype(F32).astype(BF16)
            self.sides[row_step] = dot(chosen, self.edges).reshape(self.shape)
        return self.sides[row_step]

    def at(self, row_step, col_step):
        base = self.rows[row_step]
        if col_step < 0:
            return jnp.where(self.col == 0, self.side(row_step), pltpu.roll(base, 1, 1))
        if col_step > 0:
            away = self.col == self.width - 1
            return jnp.where(away, self.side(row_step), pltpu.roll(base, SUB - 1, 1))
        return base


def xor_pairs(size, step):
    return [(index, index ^ step) for index in range(size)]


def direct_sum(value, axis):
    size = lax.axis_size(axis)
    step = 1
    while step < size:
        if size // step >= 4:
            one, two, three = [
                lax.ppermute(value, axis, xor_pairs(size, step * times)) for times in (1, 2, 3)
            ]
            value = (value + two) + (one + three)
            step *= 4
        else:
            value = value + lax.ppermute(value, axis, xor_pairs(size, step))
            step *= 2
    return value


AXES = ("clips", "ha", "wa")
MOST = 32


def spread_count():
    count = lax.axis_size("ha") * lax.axis_size("wa")
    whole = count * lax.axis_size("clips")
    return whole if whole <= MOST else count


def exchange(copies):
    if copies.shape[0] == lax.axis_size("clips") * lax.axis_size("ha") * lax.axis_size("wa"):
        return lax.all_to_all(copies, AXES, 0, 0)
    return lax.all_to_all(direct_sum(copies, "clips"), TILE, 0, 0)


def exchange_widest(sums):
    count = lax.axis_size("ha") * lax.axis_size("wa")
    sums = direct_sum(sums, "clips")
    return lax.all_to_all(jnp.broadcast_to(sums[None], (count,) + sums.shape), TILE, 0, 0)


def exchange_halo(message, rows):
    wide, high = lax.axis_size("wa"), lax.axis_size("ha")
    half = rows // 2
    side = lax.ppermute(message[rows:], "wa", xor_pairs(wide, 1))
    tops = jnp.concatenate([message[:half], side[:EDGE]], axis=0)
    bottoms = jnp.concatenate([message[half:rows], side[EDGE:]], axis=0)
    up = lax.ppermute(bottoms, "ha", [(row, row + 1) for row in range(high - 1)])
    down = lax.ppermute(tops, "ha", [(row + 1, row) for row in range(high - 1)])
    return side, up, down


def time_conv(geo, parts, blocks):
    result = None
    for tap in range(3):
        at = 0
        total = None
        for part in parts:
            lanes = part.shape[-1]
            term = dot(part, blocks[tap][at : at + lanes])
            at += lanes
            total = term if total is None else total + term
        if tap != 1:
            total = geo.shift(total, 1 - tap)
        result = total if result is None else result + total
    return result


def fast_conv(geo, value, main, before, after):
    lanes = value.shape[-1] // PHASES
    result = dot(value, main)
    result = result + geo.shift(dot(value[:, -lanes:], before), 1)
    return result + geo.shift(dot(value[:, :lanes], after), -1)


def fast_conv_back(steps, main, before, after):
    lanes = before.shape[0]
    middle = dot_nt(steps[1], main)
    first = middle[:, :lanes] + dot_nt(steps[2], after)
    last = middle[:, -lanes:] + dot_nt(steps[0], before)
    return jnp.concatenate([first, middle[:, lanes:-lanes], last], axis=1)


def lane_block(value, phase, part):
    return pltpu.roll(value, value.shape[-1] - phase * part, 1) if phase else value


def fast_reduce_grad(value, steps):
    lanes = value.shape[-1] // PHASES
    part = steps[1].shape[-1] // PHASES
    main = dot_tn(value, steps[1])
    before = dot_tn(value[:, -lanes:], steps[0])
    after = dot_tn(value[:, :lanes], steps[2])

    def block(row, col):
        return lane_block(main[row * lanes : (row + 1) * lanes], col, part)

    result = []
    for tap in range(3):
        total = before if tap == 0 else None
        if tap == 2:
            total = lane_block(after, PHASES - 1, part)
        for col in range(PHASES):
            row = col + tap - 1
            if 0 <= row < PHASES:
                total = block(row, col) if total is None else total + block(row, col)
        result.append(total)
    return result


def gather_pack(parts):
    return lax.all_gather(jnp.concatenate(parts, axis=0), TILE, axis=0)


def columns(shard, lanes):
    depth, total = shard.shape
    return jnp.moveaxis(shard.reshape(depth, total // lanes, lanes), 1, 0).reshape(-1, lanes)


def split_phases(value):
    cap, frames, height, width, lanes = value.shape
    value = value.reshape(cap, frames // PHASES, PHASES, height, width, lanes)
    return jnp.moveaxis(value, 2, 4).reshape(-1, PHASES * lanes)


def join_phases(value, shape):
    cap, frames, height, width, lanes = shape
    value = value.reshape(cap, frames // PHASES, height, width, PHASES, lanes)
    return jnp.moveaxis(value, 4, 2).reshape(shape)


def early_gather(shards_one, shards_two, lateral):
    rows = []
    lanes = shards_one[2].shape[-1]
    kinds = [jnp.stack(pair) for pair in zip(shards_one, shards_two)]
    kinds.append(jnp.stack([lateral[..., :lanes], lateral[..., lanes:]]))
    for kind in kinds:
        flat = kind.reshape(-1, kind.shape[-1])
        rows.append(jnp.pad(flat, ((0, 0), (0, lanes - flat.shape[-1]))))
    packed = gather_pack(rows)
    result = []
    at = 0
    for kind in kinds:
        depth, width = kind.shape[-2:]
        number = kind.size // width
        part = packed[:, at : at + number, :width].reshape(packed.shape[0], -1, depth, width)
        at += number
        result.append(jnp.moveaxis(part, 0, 1).reshape(part.shape[1], -1, width))
    return result


def prepare_kernel(taps_ref, space_ref, wide_ref, lateral_ref, *refs):
    slow_one, fast_one, slow_two, fast_two, *outs = refs
    part = taps_ref.shape[-1]
    lateral, *joint = outs[10:]
    number = lateral.shape[0]
    for tap in range(number):
        lateral[tap] = jnp.concatenate([lateral_ref[tap], lateral_ref[number + tap]], axis=1)
    for layer, (slow, fast) in enumerate(((slow_one, fast_one), (slow_two, fast_two))):
        at = fast_at = 0
        for ref in joint[3 * layer : 3 * layer + 3]:
            fast_lanes = part if ref.shape[1] < slow.shape[1] // 2 else wide_ref.shape[-1]
            lanes = ref.shape[1] - PHASES * fast_lanes
            values = [slow[:, at : at + lanes]]
            values += [fast[:, fast_at : fast_at + fast_lanes]] * PHASES
            ref[...] = jnp.concatenate(values, axis=1)
            at, fast_at = at + lanes, fast_at + fast_lanes
    joint[6][...] = slow_one[:, slow_one.shape[1] - joint[6].shape[1] :]
    for layer in range(2):
        main, before, after, space, wide = outs[5 * layer : 5 * layer + 5]
        taps = [taps_ref[3 * layer + tap] for tap in range(3)]
        zero = jnp.zeros_like(taps[0])
        lanes = taps[0].shape[0]
        for row in range(PHASES):
            blocks = [
                taps[row - col + 1] if abs(row - col) <= 1 else zero for col in range(PHASES)
            ]
            main[row * lanes : (row + 1) * lanes, :] = jnp.concatenate(blocks, axis=1)
        before[...] = jnp.concatenate([taps[0]] + [zero] * (PHASES - 1), axis=1)
        after[...] = jnp.concatenate([zero] * (PHASES - 1) + [taps[2]], axis=1)
        for tap in range(9):
            block = space_ref[9 * layer + tap]
            none = jnp.zeros_like(block)
            for row in range(PHASES):
                blocks = [block if row == col else none for col in range(PHASES)]
                space[tap, row * part : (row + 1) * part, :] = jnp.concatenate(blocks, axis=1)
        block = wide_ref[layer]
        none = jnp.zeros_like(block)
        for row in range(PHASES):
            blocks = [block if row == col else none for col in range(PHASES)]
            wide[row * part : (row + 1) * part, :] = jnp.concatenate(blocks, axis=1)


def to_partners(pieces, axis):
    size = lax.axis_size(axis)
    return [
        lax.ppermute(piece, axis, xor_pairs(size, step + 1)) for step, piece in enumerate(pieces)
    ]


def clip_total(own, got):
    if not got:
        return lax.psum(own, "clips") if lax.axis_size("clips") > 1 else own
    total = own.astype(F32)
    for piece in got:
        total = total + piece.astype(F32)
    return total.astype(BF16)


def clip_quarters(meta, groups):
    size = lax.axis_size("clips")
    if size > 4:
        added = [sum(part.astype(F32) for part in group).astype(BF16) for group in groups]
        return [jnp.concatenate(added)]
    lanes = groups[0][0].shape[1]
    depths = [group[0].shape[0] // size for group in groups]
    number = sum(len(group) for group in groups)

    def kernel(meta_ref, *refs):
        ins, outs, total_ref = list(refs[:number]), refs[number:-1], refs[-1]
        places = []
        at = 0
        for group, depth in zip(groups, depths):
            mine, ins = ins[: len(group)], ins[len(group) :]
            total = mine[0][...]
            if len(mine) > 1:
                total = total.astype(F32)
                for ref in mine[1:]:
                    total = total + ref[...].astype(F32)
                total = total.astype(BF16)
            total_ref[at : at + depth * size, :] = total
            places.append(at)
            at += depth * size
        for step, out in enumerate(outs):
            low = 0
            for place, depth in zip(places, depths):
                start = pl.multiple_of(place + (meta_ref[4] ^ step) * depth, 16)
                out[low : low + depth, :] = total_ref[pl.ds(start, depth), :]
                low += depth
            out.send()

    return run(
        kernel,
        [((sum(depths), lanes), BF16, "hbm")] * size,
        smem=(meta,),
        saved=[part for group in groups for part in group],
        scratch=(pltpu.VMEM((sum(depths) * size, lanes), BF16),),
    )


def on_device(
    slow_input,
    fast_input,
    slow_cotangent,
    fast_cotangent,
    clip_counts,
    lateral_weight,
    slow_reduce_one,
    slow_spatial_one,
    slow_expand_one,
    slow_shortcut_one,
    fast_reduce_one,
    fast_spatial_one,
    fast_expand_one,
    slow_reduce_two,
    slow_spatial_two,
    slow_expand_two,
    fast_reduce_two,
    fast_spatial_two,
    fast_expand_two,
    slow_norms_one,
    fast_norms_one,
    slow_norms_two,
    fast_norms_two,
):
    geo = Geometry(slow_input.shape, fast_input.shape)
    rows, groups = geo.rows, geo.groups
    half_rows = rows // 2
    count = lax.axis_size("ha") * lax.axis_size("wa")
    spread = spread_count()
    slow_wide = slow_input.shape[-1]
    fast_wide = PHASES * fast_input.shape[-1]
    wide = slow_wide + fast_wide
    mid = slow_reduce_one.shape[-1]
    fast_part = fast_reduce_one.shape[-1]
    fast_mid = PHASES * fast_part
    small = mid + fast_mid
    lat = lateral_weight.shape[-1]
    blocks = slow_wide // mid

    depth_one = slow_reduce_one.shape[1]
    depth_two = slow_reduce_two.shape[1]
    depth_mid = slow_spatial_one.shape[2]
    depth_lat = lateral_weight.shape[1]
    near = gather_pack([slow_reduce_one.reshape(-1, mid), slow_spatial_one.reshape(-1, mid)])
    far = gather_pack(
        [
            columns(slow_expand_one, mid),
            columns(slow_shortcut_one, mid),
            slow_reduce_two.reshape(-1, mid),
        ]
    )
    last = gather_pack([slow_spatial_two.reshape(-1, mid), columns(slow_expand_two, mid)])
    at_space_one = 3 * depth_one
    at_short = blocks * depth_mid
    at_reduce_two = at_short + blocks * depth_one
    at_space_two = 0
    at_expand_two = 9 * depth_mid
    fast_shards_one = (fast_reduce_one, fast_spatial_one, fast_expand_one)
    fast_shards_two = (fast_reduce_two, fast_spatial_two, fast_expand_two)
    compact = early_gather(fast_shards_one, fast_shards_two, lateral_weight)
    structured = [
        ((fast_wide, fast_mid), BF16, "hbm"),
        ((fast_wide // PHASES, fast_mid), BF16, "hbm"),
        ((fast_wide // PHASES, fast_mid), BF16, "hbm"),
        ((9, fast_mid, fast_mid), BF16, "hbm"),
        ((fast_mid, fast_wide), BF16, "hbm"),
    ]
    joint_outs = [((2, lanes), F32, "hbm") for lanes in (small, small, wide)]
    prepared = run(
        prepare_kernel,
        structured * 2
        + [((lateral_weight.shape[0], fast_wide // PHASES, lat), BF16, "hbm")]
        + joint_outs * 2
        + [((2, slow_wide), F32, "hbm")],
        vmem=(*compact, slow_norms_one, fast_norms_one, slow_norms_two, fast_norms_two),
    )
    fast_one, fast_two, lateral = prepared[:5], prepared[5:10], prepared[10]
    params_one, params_two, params_short = prepared[11:14], prepared[14:17], prepared[17]

    held = clip_counts[0]
    clips = direct_sum(jnp.full((1, 128), held, F32), "clips")[0, 0]
    positions = clips * (SUB * geo.frames * count)
    inv_n = jnp.stack([1.0 / positions, 1.0 / (positions * PHASES)])
    ha, wa = lax.axis_index("ha"), lax.axis_index("wa")
    last_ha = jnp.full_like(ha, lax.axis_size("ha") - 1)
    meta = jnp.stack([held * geo.frames, ha, wa, last_ha, lax.axis_index("clips")])
    scalars = (meta, inv_n)

    slow_x = slow_input.reshape(rows, slow_wide)
    fast_x = split_phases(fast_input)
    cot = jnp.concatenate(
        [slow_cotangent.reshape(rows, slow_wide), split_phases(fast_cotangent)], axis=1
    )
    message_out = ((rows + 2 * EDGE, small), BF16, "hbm")
    stats_small = ((spread, 2, small), F32, "spread")
    stats_wide = ((spread, 2, wide), F32, "spread")
    stats_both = ((2, wide + slow_wide), F32, "vmem")
    small_out = ((rows, small), F32, "hbm")
    wide_out = ((rows, wide), F32, "hbm")
    small_both = ((rows, small), F32, "both")
    small_next = ((rows, small), F32, "vmem")
    wide_next = ((rows, wide), F32, "vmem")
    wide_low = ((rows, wide), BF16, "hbm")

    def lateral_kernel(x_ref, k_ref, main_ref, before_ref, after_ref, united_ref, fast_ref):
        lanes = x_ref.shape[1] // PHASES
        x = x_ref[...]
        main = dot(x[:, : 3 * lanes], k_ref[2:5].reshape(3 * lanes, lat))
        past = dot(x[:, 2 * lanes :], k_ref[0:2].reshape(2 * lanes, lat))
        united_ref[...] = (main + geo.shift(past, 1)).astype(BF16)
        fast_ref[...] = fast_conv(geo, x, main_ref[...], before_ref[...], after_ref[...])

    united, za_fast = run(
        lateral_kernel,
        [((rows, lat), BF16, "hbm"), ((rows, fast_mid), F32, "hbm")],
        saved=(fast_x, lateral, *fast_one[:3]),
    )

    def reduce_one_kernel(
        meta_ref, x_ref, united_ref, fast_ref, loads, za_ref, stats_ref, message_ref
    ):
        weights = [loads.get(tap) for tap in range(3)]
        za = time_conv(geo, (x_ref[...], united_ref[...]), weights)
        za = jnp.concatenate([za, fast_ref[...]], axis=1)
        za_ref[...] = za
        za_ref.send()
        za = geo.three(za)
        put_message(za, message_ref, meta_ref, geo.width)
        put_forward(stats_ref, za, meta_ref[0])

    za_one, za_next, stats, message = run(
        reduce_one_kernel,
        [small_both, stats_small, message_out],
        smem=(meta,),
        saved=(slow_x, united, za_fast),
        weights=((near, 0, 3, depth_one),),
    )
    parts_a1 = exchange(stats)
    halo_one = exchange_halo(message, rows)

    def space_stage(za, parts_a, halo, params, gathered, offset, fast_w):
        def kernel(
            meta_ref,
            inv_ref,
            stats_ref,
            za_ref,
            side_ref,
            up_ref,
            down_ref,
            params_ref,
            fast_ref,
            loads,
            zb_ref,
            hidden_ref,
            out_stats,
        ):
            scale, shift, _, _ = affine(stats_ref, params_ref, inv_ref, mid)

            def act(value):
                return silu(geo.three(value.astype(F32)) * scale + shift)

            own = act(za_ref[...])
            edges = jnp.concatenate(
                [up_ref[half_rows:], side_ref[...], down_ref[half_rows:]], axis=0
            )
            hidden_ref[...] = geo.flat(own).astype(BF16)
            hidden_ref.send()
            near_by = Neighbours(
                own,
                act(up_ref[:half_rows]),
                act(down_ref[:half_rows]),
                geo.flat(act(edges)),
                meta_ref,
                geo.width,
            )
            slow = fast = None
            for tap in range(9):
                moved = geo.flat(near_by.at(tap // 3 - 1, tap % 3 - 1)).astype(BF16)
                slow_term = dot(moved[:, :mid], loads.get(tap))
                fast_term = dot(moved[:, mid:], fast_ref[tap])
                slow = slow_term if slow is None else slow + slow_term
                fast = fast_term if fast is None else fast + fast_term
            zb = jnp.concatenate([slow, fast], axis=1)
            zb_ref[...] = zb
            zb_ref.send()
            put_forward(out_stats, geo.three(zb), meta_ref[0])

        zb, zb_next, hidden, stats, stats_a = run(
            kernel,
            [small_both, ((rows, small), BF16, "hbm"), stats_small],
            smem=scalars,
            parts=(parts_a,),
            vmem=(za,),
            saved=(*halo, params, fast_w),
            weights=((gathered, offset, 9, depth_mid),),
        )
        return zb, zb_next, hidden, exchange(stats), stats_a

    zb_one, zb_next, ha_one, parts_b1, stats_a1 = space_stage(
        za_next, parts_a1, halo_one, params_one[0], near, at_space_one, fast_one[3]
    )

    def expand_body(
        inv_ref, stats_ref, zb_ref, params_ref, fast_ref, hidden_ref, low_ref, zc_ref, loads
    ):
        scale, shift, _, _ = affine(stats_ref, params_ref, inv_ref, mid)
        hidden = geo.flat(silu(geo.three(zb_ref[...]) * scale + shift)).astype(BF16)
        hidden_ref[...] = hidden
        hidden_ref.send()
        zc_ref[:, slow_wide:] = dot(hidden[:, mid:], fast_ref[...])
        for block in range(blocks):
            zc_ref[:, block * mid : (block + 1) * mid] = dot(hidden[:, :mid], loads.get(block))
        low_ref[...] = zc_ref[...].astype(BF16)
        low_ref.send()

    def expand_one_kernel(
        meta_ref,
        inv_ref,
        stats_ref,
        zb_ref,
        params_ref,
        fast_ref,
        x_ref,
        united_ref,
        loads,
        shorts,
        hidden_ref,
        low_ref,
        zc_ref,
        short_low_ref,
        short_ref,
        out_stats,
    ):
        expand_body(
            inv_ref, stats_ref, zb_ref, params_ref, fast_ref, hidden_ref, low_ref, zc_ref, loads
        )
        put_forward(out_stats, geo.three(zc_ref[...]), meta_ref[0])
        for block in range(blocks):
            weight = shorts.get(block)
            value = dot(x_ref[...], weight[:slow_wide]) + dot(united_ref[...], weight[slow_wide:])
            short_ref[:, block * mid : (block + 1) * mid] = value
            put_forward(out_stats, geo.three(value), meta_ref[0], wide + block * mid)
        short_low_ref[...] = short_ref[...].astype(BF16)
        short_low_ref.send()

    hb_one, zc_one, zc_next, short, short_next, stats, stats_b1 = run(
        expand_one_kernel,
        [
            ((rows, small), BF16, "hbm"),
            wide_low,
            wide_next,
            ((rows, slow_wide), BF16, "hbm"),
            ((rows, slow_wide), F32, "vmem"),
            stats_both,
        ],
        smem=scalars,
        parts=(parts_b1,),
        vmem=(zb_next,),
        saved=(params_one[1], fast_one[4], slow_x, united),
        weights=((far, 0, blocks, depth_mid), (far, at_short, blocks, depth_one)),
    )
    parts_c1 = exchange_widest(stats)

    def reduce_two_kernel(
        meta_ref,
        inv_ref,
        stats_ref,
        zc_ref,
        short_ref,
        params_ref,
        short_params_ref,
        x_ref,
        main_ref,
        before_ref,
        after_ref,
        loads,
        sum_ref,
        low_ref,
        za_ref,
        out_stats,
        message_ref,
    ):
        scale, shift, _, _ = affine(stats_ref, params_ref, inv_ref, slow_wide, 0, wide)
        scale_s, shift_s, _, _ = affine(
            stats_ref, short_params_ref, inv_ref, slow_wide, wide, wide + slow_wide
        )
        normed = geo.three(zc_ref[...]) * scale + shift
        slow = normed[..., :slow_wide] + (geo.three(short_ref[...]) * scale_s + shift_s)
        fast = normed[..., slow_wide:] + geo.three(x_ref[...].astype(F32))
        total = jnp.concatenate([slow, fast], axis=-1)
        sum_ref[...] = geo.flat(total).astype(BF16)
        sum_ref.send()
        low = geo.flat(silu(total)).astype(BF16)
        low_ref[...] = low
        low_ref.send()
        weights = [loads.get(tap) for tap in range(3)]
        za = time_conv(geo, (low[:, :slow_wide],), weights)
        fast_za = fast_conv(
            geo, low[:, slow_wide:], main_ref[...], before_ref[...], after_ref[...]
        )
        za = jnp.concatenate([za, fast_za], axis=1)
        za_ref[...] = za
        za_ref.send()
        za = geo.three(za)
        put_message(za, message_ref, meta_ref, geo.width)
        put_forward(out_stats, za, meta_ref[0])

    sum_one, low_one, za_two, za_next, stats, message, stats_c1 = run(
        reduce_two_kernel,
        [wide_low, wide_low, small_both, stats_small, message_out],
        smem=scalars,
        parts=(parts_c1,),
        vmem=(zc_next, short_next),
        saved=(params_one[2], params_short, fast_x, *fast_two[:3]),
        weights=((far, at_reduce_two, 3, depth_two),),
    )
    parts_a2 = exchange(stats)
    halo_two = exchange_halo(message, rows)
    zb_two, zb_next, ha_two, parts_b2, stats_a2 = space_stage(
        za_next, parts_a2, halo_two, params_two[0], last, at_space_two, fast_two[3]
    )

    def expand_two_kernel(
        meta_ref,
        inv_ref,
        stats_ref,
        zb_ref,
        params_ref,
        fast_ref,
        loads,
        hidden_ref,
        low_ref,
        zc_ref,
        out_stats,
    ):
        expand_body(
            inv_ref, stats_ref, zb_ref, params_ref, fast_ref, hidden_ref, low_ref, zc_ref, loads
        )
        put_forward(out_stats, geo.three(zc_ref[...]), meta_ref[0])

    hb_two, zc_two, zc_next, stats, stats_b2 = run(
        expand_two_kernel,
        [((rows, small), BF16, "hbm"), wide_low, wide_next, stats_wide],
        smem=scalars,
        parts=(parts_b2,),
        vmem=(zb_next,),
        saved=(params_two[1], fast_two[4]),
        weights=((last, at_expand_two, blocks, depth_mid),),
    )
    parts_c2 = exchange(stats)

    def head_kernel(
        meta_ref,
        inv_ref,
        stats_ref,
        zc_ref,
        params_ref,
        sum_ref,
        cot_ref,
        out_ref,
        low_ref,
        g_ref,
        sums_ref,
    ):
        scale, shift, mean, inv = affine(stats_ref, params_ref, inv_ref, slow_wide)
        zc = geo.three(zc_ref[...])
        total = zc * scale + shift + silu(geo.three(sum_ref[...].astype(F32)))
        valid = mask_groups(total.shape, meta_ref[0])
        sigma = jax.nn.sigmoid(total)
        out_ref[...] = geo.flat(jnp.where(valid, total * sigma, 0.0)).astype(BF16)
        slopes = sigma * (1.0 + total * (1.0 - sigma))
        gradient = jnp.where(valid, geo.three(cot_ref[...].astype(F32)) * slopes, 0.0)
        out_ref.send()
        g_ref[...] = geo.flat(gradient)
        low_ref[...] = geo.flat(gradient).astype(BF16)
        low_ref.send()
        put_back(sums_ref, gradient, (zc - mean) * inv)

    outputs, g_two, g_next, sums, stats_c2 = run(
        head_kernel,
        [((rows, wide), BF16, "hbm"), wide_low, wide_next, stats_wide],
        smem=scalars,
        parts=(parts_c2,),
        vmem=(zc_next,),
        saved=(params_two[2], sum_one, cot),
    )
    parts_c2 = exchange(sums)

    def norm_back(gradient, value, coeffs, sums, valid):
        scale, _, mean, inv = coeffs
        crossed = (value - mean) * inv * sums[0] + sums[1]
        return scale * (gradient - jnp.where(valid, crossed, 0.0))

    def expand_back_body(
        meta_ref,
        inv_ref,
        sums_ref,
        g_ref,
        stats_ref,
        stats_b_ref,
        zc_ref,
        params_ref,
        zb_ref,
        params_b_ref,
        fast_ref,
        loads,
        gz_ref,
        g_out,
        sums_out,
        message_ref,
    ):
        limit = meta_ref[0]
        coeffs = affine(stats_ref, params_ref, inv_ref, slow_wide, 0, wide)
        both = [back_rows(sums_ref, inv_ref, slow_wide, row, 0, wide) for row in range(2)]
        gradient = geo.three(g_ref[...])
        gz = norm_back(
            gradient,
            geo.three(zc_ref[...].astype(F32)),
            coeffs,
            both,
            mask_groups(gradient.shape, limit),
        )
        gz = geo.flat(gz).astype(BF16)
        gz_ref[...] = gz
        gz_ref.send()
        fast = dot_nt(gz[:, slow_wide:], fast_ref[...])
        slow = None
        for block in range(blocks):
            term = dot_nt(gz[:, block * mid : (block + 1) * mid], loads.get(block))
            slow = term if slow is None else slow + term
        scale, shift, mean, inv = affine(stats_b_ref, params_b_ref, inv_ref, mid)
        zb = geo.three(zb_ref[...])
        back = geo.three(jnp.concatenate([slow, fast], axis=1)) * slope(zb * scale + shift)
        g_out[...] = geo.flat(back)
        put_message(
            jnp.concatenate([back, zb], axis=-1), message_ref, meta_ref, geo.width
        )
        masked = jnp.where(mask_groups(back.shape, limit), back, 0.0)
        put_back(sums_out, masked, (zb - mean) * inv)
        return gradient

    message_back = ((rows + 2 * EDGE, 2 * small), BF16, "hbm")
    gz_c2, g_b2, sums, message, sums_c2 = run(
        expand_back_body,
        [((rows, wide), BF16, "hbm"), small_next, stats_small, message_back],
        smem=scalars,
        parts=(parts_c2,),
        vmem=(g_next,),
        saved=(stats_c2, stats_b2, zc_two, params_two[2], zb_two, params_two[1], fast_two[4]),
        weights=((last, at_expand_two, blocks, depth_mid),),
    )
    parts_b2 = exchange(sums)
    halo_back_two = exchange_halo(message, rows)
    align = 16 * lax.axis_size("clips")

    def aligned(number):
        return number + -number % align


    lanes_fast = fast_wide // PHASES
    fast_rows_count = fast_reduce_one.shape[1] + 2 * SUB

    def expand_grad(hb_ref, gz_ref, out_ref, at):
        for block in range(blocks):
            value = dot_tn(hb_ref[:, :mid], gz_ref[:, block * mid : (block + 1) * mid])
            low = at + block * depth_mid
            out_ref[:, low : low + depth_mid, :] = value.astype(BF16).reshape(
                count, depth_mid, mid
            )
        if isinstance(out_ref, Store):
            out_ref.send_rows(at, at + blocks * depth_mid)

    def fast_expand_grad(hb_ref, gz_ref):
        fast = dot_tn(hb_ref[:, mid:], gz_ref[:, slow_wide:])
        total = None
        for phase in range(PHASES):
            part = fast[
                phase * fast_part : (phase + 1) * fast_part,
                phase * lanes_fast : (phase + 1) * lanes_fast,
            ]
            total = part if total is None else total + part
        return total

    def space_grad(ha_ref, taps_ref, out_ref, at):
        fast_grads = []
        for tap in range(9):
            value = dot_tn(ha_ref[:, :mid], taps_ref[tap, :, :mid])
            low = at + tap * depth_mid
            out_ref[:, low : low + depth_mid, :] = value.astype(BF16).reshape(
                count, depth_mid, mid
            )
            fast = dot_tn(ha_ref[:, mid:], taps_ref[tap, :, mid:])
            total = None
            for phase in range(PHASES):
                part = lane_block(
                    fast[phase * fast_part : (phase + 1) * fast_part], phase, fast_part
                )
                total = part if total is None else total + part
            fast_grads.append(total)
        if isinstance(out_ref, Store):
            out_ref.send_rows(at, at + 9 * depth_mid)
        return fast_grads

    def put_fast(reduce, space, expand, out_ref, at):
        lane = lax.broadcasted_iota(jnp.int32, reduce[0].shape, 1)

        def beside(parts):
            keep = lane[: parts[0].shape[0]]
            total = None
            for place, part in enumerate(parts):
                part = jnp.where(keep < fast_part, part, 0.0)
                part = pltpu.roll(part, place * fast_part, 1) if place else part
                total = part if total is None else total + part
            return total

        depth = reduce[0].shape[0] // count
        taps = beside(reduce).astype(BF16).reshape(count, depth, lanes_fast)
        out_ref[:, at : at + depth, :] = jnp.concatenate([taps, jnp.zeros_like(taps)], axis=-1)

        def spread(value):
            tiles = value.reshape(count // 2, SUB, lanes_fast)
            return jnp.stack([tiles, pltpu.roll(tiles, SUB // 2, 1)], axis=1).reshape(
                count, SUB, lanes_fast
            )

        first = jnp.concatenate([spread(beside(space[0:4])), spread(beside(space[4:8]))], axis=-1)
        second = jnp.concatenate([spread(beside(space[8:9])), spread(expand)], axis=-1)
        both = jnp.concatenate([first, second], axis=1).astype(BF16)
        out_ref[:, at + depth : at + depth + 2 * SUB, :] = both
        if isinstance(out_ref, Store):
            out_ref.send_rows(at, at + depth + 2 * SUB)

    def space_back_stage(
        g, zb, za, halo, stats_b, parts_b, params_b, stats_a, params_a, g_hbm, at, fast_w
    ):
        def kernel(
            meta_ref,
            inv_ref,
            sums_b_ref,
            g_ref,
            side_ref,
            up_ref,
            down_ref,
            stats_b_ref,
            stats_a_ref,
            zb_ref,
            za_ref,
            params_b_ref,
            params_a_ref,
            fast_ref,
            loads,
            taps_ref,
            g_out,
            sums_out,
        ):
            limit = meta_ref[0]
            coeffs = affine(stats_b_ref, params_b_ref, inv_ref, mid)
            both = [back_rows(sums_b_ref, inv_ref, mid, row) for row in range(2)]

            def back(gradient, value, valid):
                return norm_back(gradient, value, coeffs, both, valid)

            def halo_back(value, scale):
                value = geo.three(value.astype(F32))
                valid = mask_groups(value[..., :small].shape, limit, scale)
                return back(value[..., :small], value[..., small:], valid)

            def edge_back(value):
                value = geo.three(value.astype(F32))
                shape = value[..., :small].shape
                group = lax.broadcasted_iota(jnp.int32, shape, 0) * SUB % EDGE
                group = group + lax.broadcasted_iota(jnp.int32, shape, 1)
                return geo.flat(back(value[..., :small], value[..., small:], group < limit))

            own, zb = geo.three(g_ref[...]), geo.three(zb_ref[...])
            edges = jnp.concatenate(
                [up_ref[half_rows:], side_ref[...], down_ref[half_rows:]], axis=0
            )

            near_by = Neighbours(
                back(own, zb, mask_groups(own.shape, limit)),
                halo_back(up_ref[:half_rows], 2),
                halo_back(down_ref[:half_rows], 2),
                edge_back(edges),
                meta_ref,
                geo.width,
            )
            slow = fast = None
            for tap in range(9):
                moved = geo.flat(near_by.at(1 - tap // 3, 1 - tap % 3)).astype(BF16)
                taps_ref[tap] = moved
                if tap == 8:
                    taps_ref.send()
                slow_term = dot_nt(moved[:, :mid], loads.get(tap))
                fast_term = dot_nt(moved[:, mid:], fast_ref[tap])
                slow = slow_term if slow is None else slow + slow_term
                fast = fast_term if fast is None else fast + fast_term
            scale, shift, mean, inv = affine(stats_a_ref, params_a_ref, inv_ref, mid)
            za = geo.three(za_ref[...])
            result = geo.three(jnp.concatenate([slow, fast], axis=1)) * slope(za * scale + shift)
            g_out[...] = geo.flat(result)
            masked = jnp.where(mask_groups(result.shape, limit), result, 0.0)
            put_back(sums_out, masked, (za - mean) * inv)

        taps, g, sums, sums_b = run(
            kernel,
            [((9, rows, small), BF16, "hbm"), small_next, stats_small],
            smem=scalars,
            parts=(parts_b,),
            vmem=(g,),
            saved=(*halo, stats_b, stats_a, zb, za, params_b, params_a, fast_w),
            weights=((g_hbm, at, 9, depth_mid),),
        )
        return taps, g, exchange(sums), sums_b

    taps_two, g_a2, parts_a2, sums_b2 = space_back_stage(
        g_b2,
        zb_two,
        za_two,
        halo_back_two,
        stats_b2,
        parts_b2,
        params_two[1],
        stats_a2,
        params_two[0],
        last,
        at_space_two,
        fast_two[3],
    )
    def grads_two_kernel(hb_ref, gz_ref, ha_ref, taps_ref, out_ref, fast_out):
        space = space_grad(ha_ref, taps_ref, out_ref, 0)
        expand_grad(hb_ref, gz_ref, out_ref, 9 * depth_mid)
        for tap in range(9):
            fast_out[tap] = space[tap]
        fast_out[9] = fast_expand_grad(hb_ref, gz_ref)

    rows_space = aligned((9 + blocks) * depth_mid)
    packed_space, fast_space_two = run(
        grads_two_kernel,
        [((count, rows_space, mid), BF16, "rows"), ((10, fast_part, lanes_fast), F32, "hbm")],
        saved=(hb_two, gz_c2, ha_two, taps_two),
    )
    sum_space = lax.psum_scatter(packed_space, TILE, scatter_dimension=0, tiled=False)

    def reduce_gz(meta_ref, inv_ref, g_ref, za_ref, stats_ref, sums_ref, params_ref, steps_ref):
        coeffs = affine(stats_ref, params_ref, inv_ref, mid)
        both = [back_rows(sums_ref, inv_ref, mid, row) for row in range(2)]
        gradient = geo.three(g_ref[...])
        gz = norm_back(
            gradient,
            geo.three(za_ref[...]),
            coeffs,
            both,
            mask_groups(gradient.shape, meta_ref[0]),
        )
        gz = geo.flat(gz)
        steps = [geo.shift(gz, -1).astype(BF16), gz.astype(BF16), geo.shift(gz, 1).astype(BF16)]
        for tap in range(3):
            steps_ref[tap] = steps[tap]
        if isinstance(steps_ref, Store):
            steps_ref.send()
        return steps

    def reduce_back_two_kernel(
        meta_ref,
        inv_ref,
        sums_ref,
        g_ref,
        stats_ref,
        stats_c_ref,
        za_ref,
        params_ref,
        g_two_ref,
        sum_ref,
        zc_ref,
        short_ref,
        main_ref,
        before_ref,
        after_ref,
        loads,
        steps_ref,
        fast_out,
        g_out,
        sums_out,
    ):
        steps = reduce_gz(
            meta_ref, inv_ref, g_ref, za_ref, stats_ref, sums_ref, params_ref, steps_ref
        )
        slow = None
        for tap in range(3):
            term = dot_nt(steps[tap][:, :mid], loads.get(tap))
            slow = term if slow is None else slow + term
        fast = fast_conv_back(
            [step[:, mid:] for step in steps], main_ref[...], before_ref[...], after_ref[...]
        )
        back = jnp.concatenate([slow, fast], axis=1) + g_two_ref[...].astype(F32)
        back = back * slope(sum_ref[...].astype(F32))
        g_out[...] = back
        fast_out[...] = back[:, slow_wide:]
        fast_out.send()
        back = geo.three(back)
        masked = jnp.where(mask_groups(back.shape, meta_ref[0]), back, 0.0)
        mean, inv = moments(stats_c_ref, inv_ref, slow_wide, 0, wide)
        put_back(sums_out, masked, (geo.three(zc_ref[...].astype(F32)) - mean) * inv)
        mean, inv = moments(stats_c_ref, inv_ref, slow_wide, wide, wide + slow_wide)
        masked = masked[..., :slow_wide]
        put_back(sums_out, masked, (geo.three(short_ref[...].astype(F32)) - mean) * inv, wide)

    steps_two, g_one, g_next, sums, sums_a2 = run(
        reduce_back_two_kernel,
        [
            ((3, rows, small), BF16, "hbm"),
            ((rows, fast_wide), F32, "hbm"),
            wide_next,
            stats_both,
        ],
        smem=scalars,
        parts=(parts_a2,),
        vmem=(g_a2,),
        saved=(stats_a2, stats_c1, za_two, params_two[0], g_two, sum_one, zc_one, short, *fast_two[:3]),
        weights=((far, at_reduce_two, 3, depth_two),),
    )
    parts_c1 = exchange_widest(sums)

    def expand_back_one_kernel(*refs):
        *body, short_ref, short_params_ref, loads, gz_ref, g_out, sums_out, message, gs_ref = refs
        gradient = expand_back_body(*body, loads, gz_ref, g_out, sums_out, message)
        meta_ref, inv_ref, sums_ref, _, stats_ref = body[:5]
        low, high = wide, wide + slow_wide
        coeffs = affine(stats_ref, short_params_ref, inv_ref, slow_wide, low, high)
        both = [back_rows(sums_ref, inv_ref, slow_wide, row, low, high) for row in range(2)]
        gradient = gradient[..., :slow_wide]
        valid = mask_groups(gradient.shape, meta_ref[0])
        gs = norm_back(gradient, geo.three(short_ref[...].astype(F32)), coeffs, both, valid)
        gs_ref[...] = geo.flat(gs).astype(BF16)

    gz_c1, g_b1, sums, message, gz_short, sums_c1 = run(
        expand_back_one_kernel,
        [((rows, wide), BF16, "hbm"), small_next, stats_small, message_back]
        + [((rows, slow_wide), BF16, "hbm")],
        smem=scalars,
        parts=(parts_c1,),
        vmem=(g_next,),
        saved=(stats_c1, stats_b1, zc_one, params_one[2], zb_one, params_one[1], fast_one[4])
        + (short, params_short),
        weights=((far, 0, blocks, depth_mid),),
    )
    parts_b1 = exchange(sums)
    halo_back_one = exchange_halo(message, rows)
    joined_lanes = slow_wide + lat

    def grads_mid_kernel(
        x_ref,
        united_ref,
        gs_ref,
        hb_ref,
        gz_ref,
        low_ref,
        steps_ref,
        fast_ref,
        loads,
        out_ref,
        back_ref,
    ):
        for tap in range(3):
            value = dot_tn(low_ref[:, :slow_wide], steps_ref[tap, :, :mid])
            out_ref[:, tap * depth_two : (tap + 1) * depth_two, :] = value.astype(BF16).reshape(
                count, depth_two, mid
            )
        at = 3 * depth_two
        out_ref.send_rows(0, at)
        reduce = fast_reduce_grad(
            low_ref[:, slow_wide:], [steps_ref[tap, :, mid:] for tap in range(3)]
        )
        put_fast(reduce, [fast_ref[tap] for tap in range(9)], fast_ref[9], out_ref, at)
        at += fast_rows_count
        expand_grad(hb_ref, gz_ref, out_ref, at + blocks * depth_one)
        for block in range(blocks):
            gs = gs_ref[:, block * mid : (block + 1) * mid]
            value = jnp.concatenate([dot_tn(x_ref[...], gs), dot_tn(united_ref[...], gs)], axis=0)
            low = at + block * depth_one
            out_ref[:, low : low + depth_one, :] = value.astype(BF16).reshape(
                count, depth_one, mid
            )
            out_ref.send_rows(low, low + depth_one)
        for block in range(blocks):
            gs = gs_ref[:, block * mid : (block + 1) * mid]
            term = dot_nt(gs, loads.get(block))
            back_ref[...] = term if block == 0 else back_ref[...] + term

    rows_mid = aligned(3 * depth_two + fast_rows_count + blocks * (depth_one + depth_mid))
    packed_mid, short_back = run(
        grads_mid_kernel,
        [((count, rows_mid, mid), BF16, "rows"), ((rows, joined_lanes), F32, "hbm")],
        saved=(slow_x, united, gz_short, hb_one, gz_c1, low_one, steps_two, fast_space_two),
        weights=((far, at_short, blocks, depth_one),),
    )
    sum_mid = lax.psum_scatter(packed_mid, TILE, scatter_dimension=0, tiled=False)

    taps_one, g_a1, parts_a1, sums_b1 = space_back_stage(
        g_b1,
        zb_one,
        za_one,
        halo_back_one,
        stats_b1,
        parts_b1,
        params_one[1],
        stats_a1,
        params_one[0],
        near,
        at_space_one,
        fast_one[3],
    )
    def last_kernel(
        meta_ref,
        inv_ref,
        sums_ref,
        g_ref,
        stats_ref,
        za_ref,
        params_ref,
        g_one_ref,
        short_ref,
        lateral_ref,
        main_ref,
        before_ref,
        after_ref,
        loads,
        steps_ref,
        slow_ref,
        fast_ref,
        united_ref,
    ):
        steps = reduce_gz(
            meta_ref, inv_ref, g_ref, za_ref, stats_ref, sums_ref, params_ref, steps_ref
        )
        joined = short_ref[...]
        for tap in range(3):
            joined = joined + dot_nt(steps[tap][:, :mid], loads.get(tap))
        slow_ref[...] = joined[:, :slow_wide]
        tail = joined[:, slow_wide:]
        now, past = tail.astype(BF16), geo.shift(tail, -1).astype(BF16)
        united_ref[0] = now
        united_ref[1] = past
        lanes = fast_wide // PHASES
        fast = fast_conv_back(
            [step[:, mid:] for step in steps], main_ref[...], before_ref[...], after_ref[...]
        )
        fast = fast + g_one_ref[...]
        front = dot_nt(now, lateral_ref[2:5].reshape(3 * lanes, lat))
        back = dot_nt(past, lateral_ref[0:2].reshape(2 * lanes, lat))
        fast_ref[:, : 2 * lanes] = fast[:, : 2 * lanes] + front[:, : 2 * lanes]
        fast_ref[:, 2 * lanes : 3 * lanes] = (
            fast[:, 2 * lanes : 3 * lanes] + front[:, 2 * lanes :] + back[:, :lanes]
        )
        fast_ref[:, 3 * lanes :] = fast[:, 3 * lanes :] + back[:, lanes:]

    steps_one, grad_slow, grad_fast, united_low, sums_a1 = run(
        last_kernel,
        [
            ((3, rows, small), BF16, "hbm"),
            ((rows, slow_wide), F32, "hbm"),
            ((rows, fast_wide), F32, "hbm"),
            ((2, rows, lat), BF16, "hbm"),
        ],
        smem=scalars,
        parts=(parts_a1,),
        vmem=(g_a1,),
        saved=(stats_a1, za_one, params_one[0], g_one, short_back, lateral, *fast_one[:3]),
        weights=((near, 0, 3, depth_one),),
    )

    def grads_one_kernel(
        meta_ref,
        steps_ref,
        low_ref,
        x_ref,
        united_ref,
        fast_x_ref,
        ha_ref,
        taps_ref,
        hb_ref,
        gz_ref,
        own_ref,
        send_ref,
        out_ref,
        sems,
    ):
        lanes = fast_wide // PHASES
        for tap in range(3):
            step = steps_ref[tap, :, :mid]
            value = jnp.concatenate(
                [dot_tn(x_ref[...], step), dot_tn(united_ref[...], step)], axis=0
            )
            out_ref[:, tap * depth_one : (tap + 1) * depth_one, :] = value.astype(BF16).reshape(
                count, depth_one, mid
            )
        at = 3 * depth_one
        past = dot_tn(fast_x_ref[:, 2 * lanes :], low_ref[1])
        now = dot_tn(fast_x_ref[:, : 3 * lanes], low_ref[0])
        both = jnp.concatenate([past, now], axis=0).astype(BF16)
        for tap in range(5):
            out_ref[:, at + tap * depth_lat : at + (tap + 1) * depth_lat, :] = both[
                tap * lanes : (tap + 1) * lanes
            ].reshape(count, depth_lat, lat)
        at += 5 * depth_lat
        space = space_grad(ha_ref, taps_ref, out_ref, at)
        at += 9 * depth_mid
        reduce = fast_reduce_grad(
            fast_x_ref[...], [steps_ref[tap, :, mid:] for tap in range(3)]
        )
        put_fast(reduce, space, fast_expand_grad(hb_ref, gz_ref), out_ref, at)

        put_blocks(out_ref, own_ref, send_ref, meta_ref[1], meta_ref[2], sems)

    def put_blocks(blocks_ref, own_ref, send_ref, ha, wa, sems):
        for block in range(count):
            place, col = ha ^ (block // 2), block % 2
            source, sem = blocks_ref.at[block], sems.at[block]

            @pl.when(wa == col)
            def _():
                pltpu.make_async_copy(source, own_ref.at[place], sem).start()

            @pl.when(wa != col)
            def _():
                pltpu.make_async_copy(source, send_ref.at[place], sem).start()

        for block in range(count):
            pltpu.make_async_copy(blocks_ref.at[block], own_ref.at[0], sems.at[block]).wait()

    high = count // 2
    rows_one = 3 * depth_one + 5 * depth_lat + 9 * depth_mid + fast_rows_count
    rows_late = aligned(rows_one)
    blocks_out = ((high, rows_late, mid), BF16, "raw")
    own_blocks, send_blocks = run(
        grads_one_kernel,
        [blocks_out, blocks_out],
        smem=(meta,),
        saved=(steps_one, united_low, slow_x, united, fast_x, ha_one, taps_one, hb_one, gz_c1),
        scratch=(
            pltpu.VMEM((count, rows_late, mid), BF16),
            pltpu.SemaphoreType.DMA((count,)),
        ),
    )
    side_blocks = lax.ppermute(send_blocks, "wa", xor_pairs(2, 1))

    def chip_kernel(own_ref, side_ref, *out_refs):
        for place in range(high):
            total = own_ref[place].astype(F32) + side_ref[place].astype(F32)
            out_refs[place][...] = total.astype(BF16)
            out_refs[place].send()

    late_out = ((rows_late, mid), BF16, "hbm")
    quarters_early = clip_quarters(meta, [[sum_space], [sum_mid]])
    own_blocks, side_blocks, quarters_early = lax.optimization_barrier(
        (own_blocks, side_blocks, quarters_early)
    )
    got_early = to_partners(quarters_early[1:], "clips")
    chip_sums = run(chip_kernel, [late_out] * high, saved=(own_blocks, side_blocks))
    late = [chip_sums[0]] + to_partners(chip_sums[1:], "ha")
    total_early = clip_total(quarters_early[0], got_early)
    late, total_early = lax.optimization_barrier((late, total_early))
    parts_early = [total_early] + to_partners([total_early] * len(got_early), "clips")
    quarters_late = clip_quarters(meta, [late])
    got_late = to_partners(quarters_late[1:], "clips")
    total_late = clip_total(quarters_late[0], got_late)
    parts_late = [total_late] + to_partners([total_late] * len(got_late), "clips")

    def finish(parts, groups):
        size = len(parts)
        outs_all = []
        for _, shapes in groups:
            for shape in shapes:
                outs_all += list(shape) if isinstance(shape[0], tuple) else [shape]

        def kernel(meta_ref, *refs):
            ins, outs, total_ref = refs[:size], list(refs[size:-1]), refs[-1]
            low = base = 0
            for rows_group, shapes in groups:
                depth = rows_group // size
                for step, ref in enumerate(ins):
                    place = (meta_ref[4] ^ step) if size > 1 else 0
                    start = pl.multiple_of(base + place * depth, 16)
                    total_ref[pl.ds(start, depth), :] = ref[low : low + depth, :].astype(F32)
                at = base
                for shape in shapes:
                    if isinstance(shape[0], tuple):
                        reduce, space, expand = outs.pop(0), outs.pop(0), outs.pop(0)
                        rows_tap, lanes = reduce.shape[1:]
                        for tap in range(3):
                            reduce[tap] = total_ref[
                                at : at + rows_tap, tap * lanes : (tap + 1) * lanes
                            ]
                        few = space.shape[2]
                        for tap in range(9):
                            row = at + rows_tap + tap // SUB * SUB
                            lane = tap % SUB * lanes
                            space[tap // 3, tap % 3] = total_ref[
                                row : row + few, lane : lane + lanes
                            ]
                        row = at + rows_tap + SUB
                        expand[...] = total_ref[row : row + few, expand.shape[1] :]
                        for out in (reduce, space, expand):
                            out.send()
                        at += rows_tap + 2 * SUB
                        continue
                    out = outs.pop(0)
                    if len(shape) == 2 and shape[1] > mid:
                        for block in range(shape[1] // mid):
                            out[:, block * mid : (block + 1) * mid] = total_ref[
                                at : at + shape[0], :
                            ]
                            at += shape[0]
                    else:
                        number = 1
                        for length in shape[:-1]:
                            number *= length
                        out[...] = total_ref[at : at + number, :].reshape(shape)
                        at += number
                    out.send()
                low += depth
                base += rows_group

        return run(
            kernel,
            [(shape, F32, "hbm") for shape in outs_all],
            smem=(meta,),
            saved=parts,
            scratch=(pltpu.VMEM((sum(rows_group for rows_group, _ in groups), mid), F32),),
        )

    shapes_one = tuple(shard.shape for shard in fast_shards_one)
    shapes_two = tuple(shard.shape for shard in fast_shards_two)
    grad_slow_spatial_two, grad_slow_expand_two, grad_slow_reduce_two, *rest = finish(
        parts_early,
        [
            (rows_space, [slow_spatial_two.shape, slow_expand_two.shape]),
            (
                rows_mid,
                [slow_reduce_two.shape, shapes_two, slow_shortcut_one.shape, slow_expand_one.shape],
            ),
        ],
    )
    fast_two_grads, (grad_slow_shortcut, grad_slow_expand_one) = rest[:3], rest[3:]
    grad_slow_reduce_one, grad_lateral, grad_slow_spatial_one, *fast_one_grads = finish(
        parts_late,
        [
            (
                rows_late,
                [slow_reduce_one.shape, lateral_weight.shape, slow_spatial_one.shape, shapes_one],
            )
        ],
    )

    def norm_grads(first, second, third):
        slow = [first[:, :mid], second[:, :mid], third[:, :slow_wide]]
        fast = [first[:, mid:], second[:, mid:], third[:, slow_wide:wide]]
        fast = [jnp.sum(part.reshape(2, PHASES, -1), axis=1) for part in fast]
        return slow, fast

    slow_one_p, fast_one_p = norm_grads(sums_a1, sums_b1, sums_c1)
    slow_two_p, fast_two_p = norm_grads(sums_a2, sums_b2, sums_c2)
    grad_slow_norms_one = jnp.concatenate(slow_one_p + [sums_c1[:, wide:]], axis=1)
    grad_slow_norms_two = jnp.concatenate(slow_two_p, axis=1)
    grad_fast_norms_one = jnp.concatenate(fast_one_p, axis=1)
    grad_fast_norms_two = jnp.concatenate(fast_two_p, axis=1)
    return (
        outputs[:, :slow_wide].reshape(slow_input.shape),
        join_phases(outputs[:, slow_wide:], fast_input.shape),
        grad_slow.reshape(slow_input.shape),
        join_phases(grad_fast, fast_input.shape),
        grad_lateral,
        grad_slow_reduce_one,
        grad_slow_spatial_one,
        grad_slow_expand_one,
        grad_slow_shortcut,
        *fast_one_grads,
        grad_slow_reduce_two,
        grad_slow_spatial_two,
        grad_slow_expand_two,
        *fast_two_grads,
        grad_slow_norms_one,
        grad_fast_norms_one,
        grad_slow_norms_two,
        grad_fast_norms_two,
    )


def solution(mesh):
    in_specs = (
        P("clips", None, "ha", "wa", None),
        P("clips", None, "ha", "wa", None),
        P("clips", None, "ha", "wa", None),
        P("clips", None, "ha", "wa", None),
        P("clips"),
        P(None, ("ha", "wa"), None),
        P(None, ("ha", "wa"), None),
        P(None, None, ("ha", "wa"), None),
        P(("ha", "wa"), None),
        P(("ha", "wa"), None),
        P(None, ("ha", "wa"), None),
        P(None, None, ("ha", "wa"), None),
        P(("ha", "wa"), None),
        P(None, ("ha", "wa"), None),
        P(None, None, ("ha", "wa"), None),
        P(("ha", "wa"), None),
        P(None, ("ha", "wa"), None),
        P(None, None, ("ha", "wa"), None),
        P(("ha", "wa"), None),
        P(),
        P(),
        P(),
        P(),
    )
    out_specs = (
        P("clips", None, "ha", "wa", None),
        P("clips", None, "ha", "wa", None),
        P("clips", None, "ha", "wa", None),
        P("clips", None, "ha", "wa", None),
        P(None, ("ha", "wa"), None),
        P(None, ("ha", "wa"), None),
        P(None, None, ("ha", "wa"), None),
        P(("ha", "wa"), None),
        P(("ha", "wa"), None),
        P(None, ("ha", "wa"), None),
        P(None, None, ("ha", "wa"), None),
        P(("ha", "wa"), None),
        P(None, ("ha", "wa"), None),
        P(None, None, ("ha", "wa"), None),
        P(("ha", "wa"), None),
        P(None, ("ha", "wa"), None),
        P(None, None, ("ha", "wa"), None),
        P(("ha", "wa"), None),
        P(),
        P(),
        P(),
        P(),
    )
    return jax.shard_map(
        on_device, mesh=mesh, in_specs=in_specs, out_specs=out_specs, check_vma=False
    )
```

```python
import jax
import jax.numpy as jnp
from jax import lax
from jax.experimental import pallas as pl
from jax.experimental.pallas import tpu as pltpu
from jax.sharding import PartitionSpec as P

epsilon = 1e-05
F32 = jnp.float32
BF16 = jnp.bfloat16
TILE = ("ha", "wa")
PHASES = 4
SUB = 8


def dot(left, right):
    return lax.dot_general(left, right, (((1,), (0,)), ((), ())), preferred_element_type=F32)


def dot_tn(left, right):
    return lax.dot_general(left, right, (((0,), (0,)), ((), ())), preferred_element_type=F32)


def dot_nt(left, right):
    return lax.dot_general(left, right, (((1,), (1,)), ((), ())), preferred_element_type=F32)


class Loads:
    def __init__(self, source, offset, target, sems, first):
        self.copies = []
        depth = target.shape[2]
        for step in range(target.shape[0]):
            copy = pltpu.make_async_copy(
                source.at[:, pl.ds(offset + step * depth, depth), :],
                target.at[step],
                sems.at[first + step],
            )
            copy.start()
            self.copies.append(copy)
        self.target = target

    def get(self, step):
        self.copies[step].wait()
        block = self.target[step]
        return block.reshape(-1, block.shape[-1])


class Saved:
    def __init__(self, source, scratch, sem):
        self.scratch, self.shape = scratch, scratch.shape
        self.copy = pltpu.make_async_copy(source, scratch, sem)
        self.copy.start()
        self.ready = False

    def wait(self):
        if not self.ready:
            self.copy.wait()
            self.ready = True

    def __getitem__(self, index):
        self.wait()
        return self.scratch[index]


SEGMENTS = 8


class Store:
    def __init__(self, scratch, target, sems):
        self.scratch, self.target, self.shape = scratch, target, scratch.shape
        self.sems, self.copies = sems, []

    def send(self):
        self.copies.append(pltpu.make_async_copy(self.scratch, self.target, self.sems[0]))
        self.copies[-1].start()

    def send_rows(self, low, high):
        rows = pl.ds(low, high - low)
        source, target = self.scratch.at[:, rows, :], self.target.at[:, rows, :]
        self.copies.append(pltpu.make_async_copy(source, target, self.sems[len(self.copies)]))
        self.copies[-1].start()

    def __setitem__(self, index, value):
        self.scratch[index] = value

    def __getitem__(self, index):
        return self.scratch[index]


def run(body, outs, smem=(), parts=(), vmem=(), saved=(), weights=(), scratch=(), limit=54):
    near = pl.BlockSpec(memory_space=pltpu.VMEM)
    far = pl.BlockSpec(memory_space=pltpu.HBM)
    sources = []
    for array, *_ in weights:
        if not any(array is other for other in sources):
            sources.append(array)
    outs = list(outs) + [(part.shape[1:], part.dtype, "hbm") for part in parts]
    flat = []
    for shape, dtype, kind in outs:
        flat += [(shape, dtype, "raw"), (shape, dtype, "vmem")] if kind == "both" else [(shape, dtype, kind)]
    held = [pltpu.VMEM(array.shape, array.dtype) for array in saved]
    for array, _, steps, depth in weights:
        held.append(pltpu.VMEM((steps, array.shape[0], depth, array.shape[2]), array.dtype))
    for shape, dtype, kind in outs:
        if kind in ("hbm", "rows"):
            held.append(pltpu.VMEM(shape, dtype))
        elif kind == "spread":
            held.append(pltpu.VMEM(shape[1:], dtype))
    sems = len(saved) + sum(steps for _, _, steps, _ in weights) + len(outs)
    sems += SEGMENTS * sum(kind == "rows" for _, _, kind in outs)
    held.append(pltpu.SemaphoreType.DMA((sems,)))

    def kernel(*refs):
        refs = list(refs)

        def take(number):
            taken = refs[:number]
            del refs[:number]
            return taken

        smem_refs, part_refs, vmem_refs = take(len(smem)), take(len(parts)), take(len(vmem))
        saved_refs, source_refs, out_refs = take(len(saved)), take(len(sources)), take(len(flat))
        saved_scratch, weight_scratch = take(len(saved)), take(len(weights))
        out_scratch = take(sum(kind in ("hbm", "rows", "spread") for _, _, kind in outs))
        sem, more = refs[0], refs[1:]
        copies = [
            Saved(source, target, sem.at[at])
            for at, (source, target) in enumerate(zip(saved_refs, saved_scratch))
        ]
        at = len(saved)
        loads = []
        for (array, offset, steps, _), target in zip(weights, weight_scratch):
            place = [array is other for other in sources].index(True)
            loads.append(Loads(source_refs[place], offset, target, sem, at))
            at += steps
        results, stores, spreads = [], [], []
        for _, _, kind in outs:
            ref = out_refs.pop(0)
            if kind == "both":
                stores.append(Store(out_refs.pop(0), ref, [sem.at[at]]))
                at += 1
                results.append(stores[-1])
            elif kind in ("hbm", "rows"):
                number = SEGMENTS if kind == "rows" else 1
                stores.append(
                    Store(out_scratch.pop(0), ref, [sem.at[at + part] for part in range(number)])
                )
                at += number
                results.append(stores[-1])
            elif kind == "spread":
                spreads.append((out_scratch.pop(0), ref))
                results.append(spreads[-1][0])
            else:
                results.append(ref)
        sums = results[len(results) - len(parts) :]
        results = results[: len(results) - len(parts)]
        for part, total in zip(part_refs, sums):
            total[...] = jnp.sum(part[...], axis=0)
            total.send()
        totals = [total.scratch for total in sums]
        body(*smem_refs, *totals, *vmem_refs, *copies, *loads, *results, *more)
        for copy in copies:
            copy.wait()
        for store in stores:
            if not store.copies:
                store.send()
        for value, ref in spreads:
            ref[...] = jnp.broadcast_to(value[...][None], ref.shape)
        for store in stores:
            for copy in store.copies:
                copy.wait()

    return pl.pallas_call(
        kernel,
        out_shape=[jax.ShapeDtypeStruct(shape, dtype) for shape, dtype, _ in flat],
        in_specs=[pl.BlockSpec(memory_space=pltpu.SMEM)] * len(smem)
        + [near] * (len(parts) + len(vmem))
        + [far] * (len(saved) + len(sources)),
        out_specs=[far if kind in ("hbm", "rows", "raw") else near for _, _, kind in flat],
        scratch_shapes=held + list(scratch),
        compiler_params=pltpu.CompilerParams(vmem_limit_bytes=limit * 1024 * 1024),
        cost_estimate=pl.CostEstimate(
            flops=2_000_000_000, bytes_accessed=16_000_000, transcendentals=0
        ),
    )(*smem, *parts, *vmem, *saved, *sources)


class Geometry:
    def __init__(self, slow_shape, fast_shape):
        self.cap, self.frames, self.height, self.width = slow_shape[:4]
        self.groups = self.cap * self.frames
        self.rows = self.groups * SUB

    def three(self, value):
        return value.reshape(-1, SUB, value.shape[-1])

    def flat(self, value):
        return value.reshape(-1, value.shape[-1])

    def shift(self, value, step):
        lanes = value.shape[-1]
        whole = value.reshape(self.cap, self.frames, SUB, lanes)
        zero = jnp.zeros((self.cap, 1, SUB, lanes), value.dtype)
        if step > 0:
            whole = jnp.concatenate([zero, whole[:, :-1]], axis=1)
        else:
            whole = jnp.concatenate([whole[:, 1:], zero], axis=1)
        return whole.reshape(-1, lanes)


def mask_groups(shape, limit, scale=1):
    return lax.broadcasted_iota(jnp.int32, shape, 0) * scale < limit


def rep(ref, row, low, high):
    return jnp.broadcast_to(ref[row : row + 1, low:high], (SUB, high - low))


def fold(value, slow):
    fast = value[:, slow:]
    lanes = fast.shape[-1]
    part = lanes // PHASES
    if part % 128 == 0:
        total = fast[:, :part]
        for phase in range(1, PHASES):
            total = total + fast[:, phase * part : (phase + 1) * part]
        return jnp.concatenate([value[:, :slow]] + [total] * PHASES, axis=1)
    total = fast
    for phase in range(1, PHASES):
        total = total + pltpu.roll(fast, phase * part, 1)
    return jnp.concatenate([value[:, :slow], total], axis=1)


def lane_counts(inv_ref, lanes, slow):
    lane = lax.broadcasted_iota(jnp.int32, (SUB, lanes), 1)
    return jnp.where(lane < slow, inv_ref[0], inv_ref[1])


def moments(stats, inv_ref, slow, low=0, high=None):
    high = stats.shape[1] if high is None else high
    total, square = rep(stats, 0, low, high), rep(stats, 1, low, high)
    if slow < high - low:
        total, square = fold(total, slow), fold(square, slow)
    inv_n = lane_counts(inv_ref, high - low, slow)
    mean = total * inv_n
    return mean, lax.rsqrt(square * inv_n - mean * mean + epsilon)


def affine(stats, params, inv_ref, slow, low=0, high=None):
    mean, inv = moments(stats, inv_ref, slow, low, high)
    lanes = mean.shape[1]
    scale = (1.0 + rep(params, 0, 0, lanes)) * inv
    return scale, rep(params, 1, 0, lanes) - mean * scale, mean, inv


def back_rows(sums, inv_ref, slow, row, low=0, high=None):
    high = sums.shape[1] if high is None else high
    total = rep(sums, row, low, high)
    if slow < high - low:
        total = fold(total, slow)
    return total * lane_counts(inv_ref, high - low, slow)


def silu(value):
    return value * jax.nn.sigmoid(value)


def slope(value):
    sigma = jax.nn.sigmoid(value)
    return sigma * (1.0 + value * (1.0 - sigma))


def put_stats(ref, first, second, low=0):
    lanes = first.shape[-1]
    ref[0:1, low : low + lanes] = jnp.sum(jnp.sum(first, axis=0), axis=0, keepdims=True)
    ref[1:2, low : low + lanes] = jnp.sum(jnp.sum(second, axis=0), axis=0, keepdims=True)


def put_back(ref, gradient, normal, low=0):
    put_stats(ref, gradient * normal, gradient, low)


def put_forward(ref, value, limit, low=0):
    masked = jnp.where(mask_groups(value.shape, limit), value, 0.0)
    put_stats(ref, masked, masked * value, low)


EDGE = 32


def edge_place(wa, width):
    return jnp.where(wa > 0, 0, width - 1)


def put_message(value, ref, edge_ref, meta_ref, width):
    lanes = value.shape[-1]
    pairs = value.reshape(-1, 2, SUB, lanes)
    first, second = pairs[:, 0], pairs[:, 1]
    near = lax.broadcasted_iota(jnp.int32, first.shape, 1) < SUB // 2
    top = jnp.where(near, first, pltpu.roll(second, SUB // 2, 1))
    bottom = jnp.where(near, pltpu.roll(first, SUB // 2, 1), second)
    flat = value.reshape(-1, lanes).astype(BF16)
    shape = (2 * EDGE, flat.shape[0])
    row, col = [lax.broadcasted_iota(jnp.int32, shape, dim) for dim in range(2)]
    low = row >= EDGE
    source = (row - jnp.where(low, EDGE, 0)) * SUB + jnp.where(low, SUB // 2, 0)
    chosen = (col == source + edge_place(meta_ref[2], width)).astype(F32).astype(BF16)
    edges = dot(chosen, flat)
    edge_ref[...] = edges.astype(BF16)
    edge_ref.send()
    top, bottom = [part.reshape(-1, lanes).astype(BF16) for part in (top, bottom)]
    ref[: top.shape[0]] = top
    ref[top.shape[0] :] = bottom
    ref.send()


def unpack_bottom(value):
    both = jnp.stack([pltpu.roll(value, SUB // 2, 1), value], axis=1)
    return both.reshape(-1, SUB, value.shape[-1])


def unpack_top(value):
    both = jnp.stack([value, pltpu.roll(value, SUB // 2, 1)], axis=1)
    return both.reshape(-1, SUB, value.shape[-1])


class Neighbours:
    def __init__(self, own, up, down, edges, meta, width):
        half = SUB // 2
        near = lax.broadcasted_iota(jnp.int32, own.shape, 1) < half
        self.col = lax.broadcasted_iota(jnp.int32, own.shape, 1) % width
        self.width, self.shape = width, own.shape
        ha, wa, last = meta[1], meta[2], meta[3]
        up = unpack_bottom(jnp.where(ha > 0, up, 0.0))
        down = unpack_top(jnp.where(ha < last, down, 0.0))
        self.rows = {
            0: own,
            -1: pltpu.roll(jnp.where(near, own, up), half, 1),
            1: pltpu.roll(jnp.where(near, down, own), half, 1),
        }
        beyond = lax.broadcasted_iota(jnp.int32, edges.shape, 0)
        inside = ((ha > 0) | (beyond >= EDGE)) & ((ha < last) | (beyond < 3 * EDGE))
        self.edges = jnp.where(inside, edges, 0.0).astype(BF16)
        shape = (own.shape[0] * SUB, edges.shape[0])
        place, self.source = [lax.broadcasted_iota(jnp.int32, shape, dim) for dim in range(2)]
        self.group = place // SUB
        self.row = place // half % 2
        self.touches = place % width == edge_place(wa, width)
        self.sides = {}

    def side(self, row_step):
        if row_step not in self.sides:
            wanted = (self.row + row_step + 1) * EDGE + self.group
            chosen = ((self.source == wanted) & self.touches).astype(F32).astype(BF16)
            self.sides[row_step] = dot(chosen, self.edges).reshape(self.shape)
        return self.sides[row_step]

    def at(self, row_step, col_step):
        base = self.rows[row_step]
        if col_step < 0:
            return jnp.where(self.col == 0, self.side(row_step), pltpu.roll(base, 1, 1))
        if col_step > 0:
            away = self.col == self.width - 1
            return jnp.where(away, self.side(row_step), pltpu.roll(base, SUB - 1, 1))
        return base


def xor_pairs(size, step):
    return [(index, index ^ step) for index in range(size)]


def direct_sum(value, axis):
    size = lax.axis_size(axis)
    step = 1
    while step < size:
        if size // step >= 4:
            one, two, three = [
                lax.ppermute(value, axis, xor_pairs(size, step * times)) for times in (1, 2, 3)
            ]
            value = (value + two) + (one + three)
            step *= 4
        else:
            value = value + lax.ppermute(value, axis, xor_pairs(size, step))
            step *= 2
    return value


AXES = ("clips", "ha", "wa")
MOST = 32


def spread_count():
    count = lax.axis_size("ha") * lax.axis_size("wa")
    whole = count * lax.axis_size("clips")
    return whole if whole <= MOST else count


def exchange(copies):
    if copies.shape[0] == lax.axis_size("clips") * lax.axis_size("ha") * lax.axis_size("wa"):
        return lax.all_to_all(copies, AXES, 0, 0)
    return lax.all_to_all(direct_sum(copies, "clips"), TILE, 0, 0)


def exchange_widest(sums):
    count = lax.axis_size("ha") * lax.axis_size("wa")
    sums = direct_sum(sums, "clips")
    return lax.all_to_all(jnp.broadcast_to(sums[None], (count,) + sums.shape), TILE, 0, 0)


def exchange_halo(message, edges):
    wide, high = lax.axis_size("wa"), lax.axis_size("ha")
    half = message.shape[0] // 2
    side = lax.ppermute(edges, "wa", xor_pairs(wide, 1))
    tops = jnp.concatenate([message[:half], side[:EDGE]], axis=0)
    bottoms = jnp.concatenate([message[half:], side[EDGE:]], axis=0)
    up = lax.ppermute(bottoms, "ha", [(row, row + 1) for row in range(high - 1)])
    down = lax.ppermute(tops, "ha", [(row + 1, row) for row in range(high - 1)])
    return side, up, down


def time_conv(geo, parts, blocks):
    result = None
    for tap in range(3):
        at = 0
        total = None
        for part in parts:
            lanes = part.shape[-1]
            term = dot(part, blocks[tap][at : at + lanes])
            at += lanes
            total = term if total is None else total + term
        if tap != 1:
            total = geo.shift(total, 1 - tap)
        result = total if result is None else result + total
    return result


def fast_conv(geo, value, main, before, after):
    lanes = value.shape[-1] // PHASES
    result = dot(value, main)
    result = result + geo.shift(dot(value[:, -lanes:], before), 1)
    return result + geo.shift(dot(value[:, :lanes], after), -1)


def fast_conv_back(steps, main, before, after):
    lanes = before.shape[0]
    middle = dot_nt(steps[1], main)
    first = middle[:, :lanes] + dot_nt(steps[2], after)
    last = middle[:, -lanes:] + dot_nt(steps[0], before)
    return jnp.concatenate([first, middle[:, lanes:-lanes], last], axis=1)


def lane_block(value, phase, part):
    return pltpu.roll(value, value.shape[-1] - phase * part, 1) if phase else value


def fast_reduce_grad(value, steps):
    lanes = value.shape[-1] // PHASES
    part = steps[1].shape[-1] // PHASES
    main = dot_tn(value, steps[1])
    before = dot_tn(value[:, -lanes:], steps[0])
    after = dot_tn(value[:, :lanes], steps[2])

    def block(row, col):
        return lane_block(main[row * lanes : (row + 1) * lanes], col, part)

    result = []
    for tap in range(3):
        total = before if tap == 0 else None
        if tap == 2:
            total = lane_block(after, PHASES - 1, part)
        for col in range(PHASES):
            row = col + tap - 1
            if 0 <= row < PHASES:
                total = block(row, col) if total is None else total + block(row, col)
        result.append(total)
    return result


def gather_pack(parts):
    return lax.all_gather(jnp.concatenate(parts, axis=0), TILE, axis=0)


def columns(shard, lanes):
    depth, total = shard.shape
    return jnp.moveaxis(shard.reshape(depth, total // lanes, lanes), 1, 0).reshape(-1, lanes)


def split_phases(value):
    cap, frames, height, width, lanes = value.shape
    value = value.reshape(cap, frames // PHASES, PHASES, height, width, lanes)
    return jnp.moveaxis(value, 2, 4).reshape(-1, PHASES * lanes)


def join_phases(value, shape):
    cap, frames, height, width, lanes = shape
    value = value.reshape(cap, frames // PHASES, height, width, PHASES, lanes)
    return jnp.moveaxis(value, 4, 2).reshape(shape)


def early_gather(shards_one, shards_two, lateral):
    rows = []
    lanes = shards_one[2].shape[-1]
    kinds = [jnp.stack(pair) for pair in zip(shards_one, shards_two)]
    kinds.append(jnp.stack([lateral[..., :lanes], lateral[..., lanes:]]))
    for kind in kinds:
        flat = kind.reshape(-1, kind.shape[-1])
        rows.append(jnp.pad(flat, ((0, 0), (0, lanes - flat.shape[-1]))))
    packed = gather_pack(rows)
    result = []
    at = 0
    for kind in kinds:
        depth, width = kind.shape[-2:]
        number = kind.size // width
        part = packed[:, at : at + number, :width].reshape(packed.shape[0], -1, depth, width)
        at += number
        result.append(jnp.moveaxis(part, 0, 1).reshape(part.shape[1], -1, width))
    return result


def prepare_kernel(taps_ref, space_ref, wide_ref, lateral_ref, *refs):
    slow_one, fast_one, slow_two, fast_two, *outs = refs
    part = taps_ref.shape[-1]
    lateral, *joint = outs[10:]
    number = lateral.shape[0]
    for tap in range(number):
        lateral[tap] = jnp.concatenate([lateral_ref[tap], lateral_ref[number + tap]], axis=1)
    for layer, (slow, fast) in enumerate(((slow_one, fast_one), (slow_two, fast_two))):
        at = fast_at = 0
        for ref in joint[3 * layer : 3 * layer + 3]:
            fast_lanes = part if ref.shape[1] < slow.shape[1] // 2 else wide_ref.shape[-1]
            lanes = ref.shape[1] - PHASES * fast_lanes
            values = [slow[:, at : at + lanes]]
            values += [fast[:, fast_at : fast_at + fast_lanes]] * PHASES
            ref[...] = jnp.concatenate(values, axis=1)
            at, fast_at = at + lanes, fast_at + fast_lanes
    joint[6][...] = slow_one[:, slow_one.shape[1] - joint[6].shape[1] :]
    for layer in range(2):
        main, before, after, space, wide = outs[5 * layer : 5 * layer + 5]
        taps = [taps_ref[3 * layer + tap] for tap in range(3)]
        zero = jnp.zeros_like(taps[0])
        lanes = taps[0].shape[0]
        for row in range(PHASES):
            blocks = [
                taps[row - col + 1] if abs(row - col) <= 1 else zero for col in range(PHASES)
            ]
            main[row * lanes : (row + 1) * lanes, :] = jnp.concatenate(blocks, axis=1)
        before[...] = jnp.concatenate([taps[0]] + [zero] * (PHASES - 1), axis=1)
        after[...] = jnp.concatenate([zero] * (PHASES - 1) + [taps[2]], axis=1)
        for tap in range(9):
            block = space_ref[9 * layer + tap]
            none = jnp.zeros_like(block)
            for row in range(PHASES):
                blocks = [block if row == col else none for col in range(PHASES)]
                space[tap, row * part : (row + 1) * part, :] = jnp.concatenate(blocks, axis=1)
        block = wide_ref[layer]
        none = jnp.zeros_like(block)
        for row in range(PHASES):
            blocks = [block if row == col else none for col in range(PHASES)]
            wide[row * part : (row + 1) * part, :] = jnp.concatenate(blocks, axis=1)


def to_partners(pieces, axis):
    size = lax.axis_size(axis)
    return [
        lax.ppermute(piece, axis, xor_pairs(size, step + 1)) for step, piece in enumerate(pieces)
    ]


def clip_parts(meta, groups, number):
    lanes = groups[0][0].shape[1]
    lengths = [group[0].shape[0] for group in groups]
    depth = sum(lengths) // number
    total_ins = sum(len(group) for group in groups)

    def kernel(meta_ref, *refs):
        ins, outs, total_ref = list(refs[:total_ins]), refs[total_ins:-1], refs[-1]
        at = 0
        for group, length in zip(groups, lengths):
            mine, ins = ins[: len(group)], ins[len(group) :]
            total = mine[0][...]
            if len(mine) > 1:
                total = total.astype(F32)
                for ref in mine[1:]:
                    total = total + ref[...].astype(F32)
                total = total.astype(BF16)
            total_ref[at : at + length, :] = total
            at += length
        index = meta_ref[4] if number != 2 else meta_ref[4] % 2
        for step, out in enumerate(outs):
            start = pl.multiple_of((index ^ step) * depth, 16)
            out[...] = total_ref[pl.ds(start, depth), :]
            out.send()

    return run(
        kernel,
        [((depth, lanes), BF16, "hbm")] * number,
        smem=(meta,),
        saved=[part for group in groups for part in group],
        scratch=(pltpu.VMEM((sum(lengths), lanes), BF16),),
    )


def add_low(first, *others):
    total = first.astype(F32)
    for other in others:
        total = total + other.astype(F32)
    return total.astype(BF16)


def halves_sum(keep, send):
    across = lax.axis_index("clips") // 2
    half = add_low(keep, lax.ppermute(send, "clips", xor_pairs(4, 1)))
    depth = half.shape[0] // 2
    mine = lax.dynamic_slice_in_dim(half, across * depth, depth, axis=0)
    other = lax.dynamic_slice_in_dim(half, (1 - across) * depth, depth, axis=0)
    total = add_low(mine, lax.ppermute(other, "clips", xor_pairs(4, 2)))
    return total


def halves_share(total):
    beyond = lax.ppermute(total, "clips", xor_pairs(4, 2))
    beside = lax.ppermute(total, "clips", xor_pairs(4, 1))
    return [total, beside, beyond, lax.ppermute(beyond, "clips", xor_pairs(4, 1))]


def on_device(
    slow_input,
    fast_input,
    slow_cotangent,
    fast_cotangent,
    clip_counts,
    lateral_weight,
    slow_reduce_one,
    slow_spatial_one,
    slow_expand_one,
    slow_shortcut_one,
    fast_reduce_one,
    fast_spatial_one,
    fast_expand_one,
    slow_reduce_two,
    slow_spatial_two,
    slow_expand_two,
    fast_reduce_two,
    fast_spatial_two,
    fast_expand_two,
    slow_norms_one,
    fast_norms_one,
    slow_norms_two,
    fast_norms_two,
):
    geo = Geometry(slow_input.shape, fast_input.shape)
    rows, groups = geo.rows, geo.groups
    half_rows = rows // 2
    count = lax.axis_size("ha") * lax.axis_size("wa")
    spread = spread_count()
    slow_wide = slow_input.shape[-1]
    fast_wide = PHASES * fast_input.shape[-1]
    wide = slow_wide + fast_wide
    mid = slow_reduce_one.shape[-1]
    fast_part = fast_reduce_one.shape[-1]
    fast_mid = PHASES * fast_part
    small = mid + fast_mid
    lat = lateral_weight.shape[-1]
    blocks = slow_wide // mid

    depth_one = slow_reduce_one.shape[1]
    depth_two = slow_reduce_two.shape[1]
    depth_mid = slow_spatial_one.shape[2]
    depth_lat = lateral_weight.shape[1]
    near = gather_pack([slow_reduce_one.reshape(-1, mid), slow_spatial_one.reshape(-1, mid)])
    far = gather_pack(
        [
            columns(slow_expand_one, mid),
            columns(slow_shortcut_one, mid),
            slow_reduce_two.reshape(-1, mid),
        ]
    )
    last = gather_pack([slow_spatial_two.reshape(-1, mid), columns(slow_expand_two, mid)])
    at_space_one = 3 * depth_one
    at_short = blocks * depth_mid
    at_reduce_two = at_short + blocks * depth_one
    at_space_two = 0
    at_expand_two = 9 * depth_mid
    fast_shards_one = (fast_reduce_one, fast_spatial_one, fast_expand_one)
    fast_shards_two = (fast_reduce_two, fast_spatial_two, fast_expand_two)
    compact = early_gather(fast_shards_one, fast_shards_two, lateral_weight)
    structured = [
        ((fast_wide, fast_mid), BF16, "hbm"),
        ((fast_wide // PHASES, fast_mid), BF16, "hbm"),
        ((fast_wide // PHASES, fast_mid), BF16, "hbm"),
        ((9, fast_mid, fast_mid), BF16, "hbm"),
        ((fast_mid, fast_wide), BF16, "hbm"),
    ]
    joint_outs = [((2, lanes), F32, "hbm") for lanes in (small, small, wide)]
    prepared = run(
        prepare_kernel,
        structured * 2
        + [((lateral_weight.shape[0], fast_wide // PHASES, lat), BF16, "hbm")]
        + joint_outs * 2
        + [((2, slow_wide), F32, "hbm")],
        vmem=(*compact, slow_norms_one, fast_norms_one, slow_norms_two, fast_norms_two),
    )
    fast_one, fast_two, lateral = prepared[:5], prepared[5:10], prepared[10]
    params_one, params_two, params_short = prepared[11:14], prepared[14:17], prepared[17]

    held = clip_counts[0]
    clips = direct_sum(jnp.full((1, 128), held, F32), "clips")[0, 0]
    positions = clips * (SUB * geo.frames * count)
    inv_n = jnp.stack([1.0 / positions, 1.0 / (positions * PHASES)])
    ha, wa = lax.axis_index("ha"), lax.axis_index("wa")
    last_ha = jnp.full_like(ha, lax.axis_size("ha") - 1)
    meta = jnp.stack([held * geo.frames, ha, wa, last_ha, lax.axis_index("clips")])
    scalars = (meta, inv_n)

    slow_x = slow_input.reshape(rows, slow_wide)
    fast_x = split_phases(fast_input)
    cot = jnp.concatenate(
        [slow_cotangent.reshape(rows, slow_wide), split_phases(fast_cotangent)], axis=1
    )
    message_out = [((rows, small), BF16, "hbm"), ((2 * EDGE, small), BF16, "hbm")]
    stats_small = ((spread, 2, small), F32, "spread")
    stats_wide = ((spread, 2, wide), F32, "spread")
    stats_both = ((2, wide + slow_wide), F32, "vmem")
    small_out = ((rows, small), F32, "hbm")
    wide_out = ((rows, wide), F32, "hbm")
    small_both = ((rows, small), F32, "both")
    small_next = ((rows, small), F32, "vmem")
    wide_next = ((rows, wide), F32, "vmem")
    wide_low = ((rows, wide), BF16, "hbm")

    def lateral_kernel(x_ref, k_ref, main_ref, before_ref, after_ref, united_ref, fast_ref):
        lanes = x_ref.shape[1] // PHASES
        x = x_ref[...]
        main = dot(x[:, : 3 * lanes], k_ref[2:5].reshape(3 * lanes, lat))
        past = dot(x[:, 2 * lanes :], k_ref[0:2].reshape(2 * lanes, lat))
        united_ref[...] = (main + geo.shift(past, 1)).astype(BF16)
        fast_ref[...] = fast_conv(geo, x, main_ref[...], before_ref[...], after_ref[...])

    united, za_fast = run(
        lateral_kernel,
        [((rows, lat), BF16, "hbm"), ((rows, fast_mid), F32, "hbm")],
        saved=(fast_x, lateral, *fast_one[:3]),
    )

    def reduce_one_kernel(
        meta_ref, x_ref, united_ref, fast_ref, loads, za_ref, stats_ref, message_ref, edge_ref
    ):
        weights = [loads.get(tap) for tap in range(3)]
        za = time_conv(geo, (x_ref[...], united_ref[...]), weights)
        za = jnp.concatenate([za, fast_ref[...]], axis=1)
        za_ref[...] = za
        za_ref.send()
        za = geo.three(za)
        put_message(za, message_ref, edge_ref, meta_ref, geo.width)
        put_forward(stats_ref, za, meta_ref[0])

    za_one, za_next, stats, message, edges = run(
        reduce_one_kernel,
        [small_both, stats_small, *message_out],
        smem=(meta,),
        saved=(slow_x, united, za_fast),
        weights=((near, 0, 3, depth_one),),
    )
    parts_a1 = exchange(stats)
    halo_one = exchange_halo(message, edges)

    def space_stage(za, parts_a, halo, params, gathered, offset, fast_w):
        def kernel(
            meta_ref,
            inv_ref,
            stats_ref,
            za_ref,
            side_ref,
            up_ref,
            down_ref,
            params_ref,
            fast_ref,
            loads,
            zb_ref,
            hidden_ref,
            out_stats,
        ):
            scale, shift, _, _ = affine(stats_ref, params_ref, inv_ref, mid)

            def act(value):
                return silu(geo.three(value.astype(F32)) * scale + shift)

            own = act(za_ref[...])
            edges = jnp.concatenate(
                [up_ref[half_rows:], side_ref[...], down_ref[half_rows:]], axis=0
            )
            hidden_ref[...] = geo.flat(own).astype(BF16)
            hidden_ref.send()
            near_by = Neighbours(
                own,
                act(up_ref[:half_rows]),
                act(down_ref[:half_rows]),
                geo.flat(act(edges)),
                meta_ref,
                geo.width,
            )
            slow = fast = None
            for tap in range(9):
                moved = geo.flat(near_by.at(tap // 3 - 1, tap % 3 - 1)).astype(BF16)
                slow_term = dot(moved[:, :mid], loads.get(tap))
                fast_term = dot(moved[:, mid:], fast_ref[tap])
                slow = slow_term if slow is None else slow + slow_term
                fast = fast_term if fast is None else fast + fast_term
            zb = jnp.concatenate([slow, fast], axis=1)
            zb_ref[...] = zb
            zb_ref.send()
            put_forward(out_stats, geo.three(zb), meta_ref[0])

        zb, zb_next, hidden, stats, stats_a = run(
            kernel,
            [small_both, ((rows, small), BF16, "hbm"), stats_small],
            smem=scalars,
            parts=(parts_a,),
            vmem=(za,),
            saved=(*halo, params, fast_w),
            weights=((gathered, offset, 9, depth_mid),),
        )
        return zb, zb_next, hidden, exchange(stats), stats_a

    zb_one, zb_next, ha_one, parts_b1, stats_a1 = space_stage(
        za_next, parts_a1, halo_one, params_one[0], near, at_space_one, fast_one[3]
    )

    def expand_body(
        inv_ref, stats_ref, zb_ref, params_ref, fast_ref, hidden_ref, low_ref, zc_ref, loads
    ):
        scale, shift, _, _ = affine(stats_ref, params_ref, inv_ref, mid)
        hidden = geo.flat(silu(geo.three(zb_ref[...]) * scale + shift)).astype(BF16)
        hidden_ref[...] = hidden
        hidden_ref.send()
        zc_ref[:, slow_wide:] = dot(hidden[:, mid:], fast_ref[...])
        for block in range(blocks):
            zc_ref[:, block * mid : (block + 1) * mid] = dot(hidden[:, :mid], loads.get(block))
        low_ref[...] = zc_ref[...].astype(BF16)
        low_ref.send()

    def expand_one_kernel(
        meta_ref,
        inv_ref,
        stats_ref,
        zb_ref,
        params_ref,
        fast_ref,
        x_ref,
        united_ref,
        loads,
        shorts,
        hidden_ref,
        low_ref,
        zc_ref,
        short_low_ref,
        short_ref,
        out_stats,
    ):
        expand_body(
            inv_ref, stats_ref, zb_ref, params_ref, fast_ref, hidden_ref, low_ref, zc_ref, loads
        )
        put_forward(out_stats, geo.three(zc_ref[...]), meta_ref[0])
        for block in range(blocks):
            weight = shorts.get(block)
            value = dot(x_ref[...], weight[:slow_wide]) + dot(united_ref[...], weight[slow_wide:])
            short_ref[:, block * mid : (block + 1) * mid] = value
            put_forward(out_stats, geo.three(value), meta_ref[0], wide + block * mid)
        short_low_ref[...] = short_ref[...].astype(BF16)
        short_low_ref.send()

    hb_one, zc_one, zc_next, short, short_next, stats, stats_b1 = run(
        expand_one_kernel,
        [
            ((rows, small), BF16, "hbm"),
            wide_low,
            wide_next,
            ((rows, slow_wide), BF16, "hbm"),
            ((rows, slow_wide), F32, "vmem"),
            stats_both,
        ],
        smem=scalars,
        parts=(parts_b1,),
        vmem=(zb_next,),
        saved=(params_one[1], fast_one[4], slow_x, united),
        weights=((far, 0, blocks, depth_mid), (far, at_short, blocks, depth_one)),
    )
    parts_c1 = exchange_widest(stats)

    def reduce_two_kernel(
        meta_ref,
        inv_ref,
        stats_ref,
        zc_ref,
        short_ref,
        params_ref,
        short_params_ref,
        x_ref,
        main_ref,
        before_ref,
        after_ref,
        loads,
        sum_ref,
        low_ref,
        za_ref,
        out_stats,
        message_ref,
        edge_ref,
    ):
        scale, shift, _, _ = affine(stats_ref, params_ref, inv_ref, slow_wide, 0, wide)
        scale_s, shift_s, _, _ = affine(
            stats_ref, short_params_ref, inv_ref, slow_wide, wide, wide + slow_wide
        )
        normed = geo.three(zc_ref[...]) * scale + shift
        slow = normed[..., :slow_wide] + (geo.three(short_ref[...]) * scale_s + shift_s)
        fast = normed[..., slow_wide:] + geo.three(x_ref[...].astype(F32))
        total = jnp.concatenate([slow, fast], axis=-1)
        sum_ref[...] = geo.flat(total).astype(BF16)
        sum_ref.send()
        low = geo.flat(silu(total)).astype(BF16)
        low_ref[...] = low
        low_ref.send()
        weights = [loads.get(tap) for tap in range(3)]
        za = time_conv(geo, (low[:, :slow_wide],), weights)
        fast_za = fast_conv(
            geo, low[:, slow_wide:], main_ref[...], before_ref[...], after_ref[...]
        )
        za = jnp.concatenate([za, fast_za], axis=1)
        za_ref[...] = za
        za_ref.send()
        za = geo.three(za)
        put_message(za, message_ref, edge_ref, meta_ref, geo.width)
        put_forward(out_stats, za, meta_ref[0])

    sum_one, low_one, za_two, za_next, stats, message, edges, stats_c1 = run(
        reduce_two_kernel,
        [wide_low, wide_low, small_both, stats_small, *message_out],
        smem=scalars,
        parts=(parts_c1,),
        vmem=(zc_next, short_next),
        saved=(params_one[2], params_short, fast_x, *fast_two[:3]),
        weights=((far, at_reduce_two, 3, depth_two),),
    )
    parts_a2 = exchange(stats)
    halo_two = exchange_halo(message, edges)
    zb_two, zb_next, ha_two, parts_b2, stats_a2 = space_stage(
        za_next, parts_a2, halo_two, params_two[0], last, at_space_two, fast_two[3]
    )

    def expand_two_kernel(
        meta_ref,
        inv_ref,
        stats_ref,
        zb_ref,
        params_ref,
        fast_ref,
        loads,
        hidden_ref,
        low_ref,
        zc_ref,
        out_stats,
    ):
        expand_body(
            inv_ref, stats_ref, zb_ref, params_ref, fast_ref, hidden_ref, low_ref, zc_ref, loads
        )
        put_forward(out_stats, geo.three(zc_ref[...]), meta_ref[0])

    hb_two, zc_two, zc_next, stats, stats_b2 = run(
        expand_two_kernel,
        [((rows, small), BF16, "hbm"), wide_low, wide_next, stats_wide],
        smem=scalars,
        parts=(parts_b2,),
        vmem=(zb_next,),
        saved=(params_two[1], fast_two[4]),
        weights=((last, at_expand_two, blocks, depth_mid),),
    )
    parts_c2 = exchange(stats)

    def head_kernel(
        meta_ref,
        inv_ref,
        stats_ref,
        zc_ref,
        params_ref,
        sum_ref,
        cot_ref,
        out_ref,
        low_ref,
        g_ref,
        sums_ref,
    ):
        scale, shift, mean, inv = affine(stats_ref, params_ref, inv_ref, slow_wide)
        zc = geo.three(zc_ref[...])
        total = zc * scale + shift + silu(geo.three(sum_ref[...].astype(F32)))
        valid = mask_groups(total.shape, meta_ref[0])
        sigma = jax.nn.sigmoid(total)
        out_ref[...] = geo.flat(jnp.where(valid, total * sigma, 0.0)).astype(BF16)
        slopes = sigma * (1.0 + total * (1.0 - sigma))
        gradient = jnp.where(valid, geo.three(cot_ref[...].astype(F32)) * slopes, 0.0)
        out_ref.send()
        g_ref[...] = geo.flat(gradient)
        low_ref[...] = geo.flat(gradient).astype(BF16)
        low_ref.send()
        put_back(sums_ref, gradient, (zc - mean) * inv)

    outputs, g_two, g_next, sums, stats_c2 = run(
        head_kernel,
        [((rows, wide), BF16, "hbm"), wide_low, wide_next, stats_wide],
        smem=scalars,
        parts=(parts_c2,),
        vmem=(zc_next,),
        saved=(params_two[2], sum_one, cot),
    )
    parts_c2 = exchange(sums)

    def norm_back(gradient, value, coeffs, sums, valid):
        scale, _, mean, inv = coeffs
        crossed = (value - mean) * inv * sums[0] + sums[1]
        return scale * (gradient - jnp.where(valid, crossed, 0.0))

    def expand_back_body(
        meta_ref,
        inv_ref,
        sums_ref,
        g_ref,
        stats_ref,
        stats_b_ref,
        zc_ref,
        params_ref,
        zb_ref,
        params_b_ref,
        fast_ref,
        loads,
        gz_ref,
        g_out,
        sums_out,
        message_ref,
        edge_ref,
    ):
        limit = meta_ref[0]
        coeffs = affine(stats_ref, params_ref, inv_ref, slow_wide, 0, wide)
        both = [back_rows(sums_ref, inv_ref, slow_wide, row, 0, wide) for row in range(2)]
        gradient = geo.three(g_ref[...])
        gz = norm_back(
            gradient,
            geo.three(zc_ref[...].astype(F32)),
            coeffs,
            both,
            mask_groups(gradient.shape, limit),
        )
        gz = geo.flat(gz).astype(BF16)
        gz_ref[...] = gz
        gz_ref.send()
        fast = dot_nt(gz[:, slow_wide:], fast_ref[...])
        slow = None
        for block in range(blocks):
            term = dot_nt(gz[:, block * mid : (block + 1) * mid], loads.get(block))
            slow = term if slow is None else slow + term
        scale, shift, mean, inv = affine(stats_b_ref, params_b_ref, inv_ref, mid)
        zb = geo.three(zb_ref[...])
        back = geo.three(jnp.concatenate([slow, fast], axis=1)) * slope(zb * scale + shift)
        g_out[...] = geo.flat(back)
        put_message(
            jnp.concatenate([back, zb], axis=-1), message_ref, edge_ref, meta_ref, geo.width
        )
        masked = jnp.where(mask_groups(back.shape, limit), back, 0.0)
        put_back(sums_out, masked, (zb - mean) * inv)
        return gradient

    message_back = [((rows, 2 * small), BF16, "hbm"), ((2 * EDGE, 2 * small), BF16, "hbm")]
    gz_c2, g_b2, sums, message, edges, sums_c2 = run(
        expand_back_body,
        [((rows, wide), BF16, "hbm"), small_next, stats_small, *message_back],
        smem=scalars,
        parts=(parts_c2,),
        vmem=(g_next,),
        saved=(stats_c2, stats_b2, zc_two, params_two[2], zb_two, params_two[1], fast_two[4]),
        weights=((last, at_expand_two, blocks, depth_mid),),
    )
    parts_b2 = exchange(sums)
    halo_back_two = exchange_halo(message, edges)
    align = 16 * lax.axis_size("clips")

    def aligned(number):
        return number + -number % align


    lanes_fast = fast_wide // PHASES
    fast_rows_count = fast_reduce_one.shape[1] + 2 * SUB

    def expand_grad(hb_ref, gz_ref, out_ref, at):
        for block in range(blocks):
            value = dot_tn(hb_ref[:, :mid], gz_ref[:, block * mid : (block + 1) * mid])
            low = at + block * depth_mid
            out_ref[:, low : low + depth_mid, :] = value.astype(BF16).reshape(
                count, depth_mid, mid
            )
        if isinstance(out_ref, Store):
            out_ref.send_rows(at, at + blocks * depth_mid)

    def fast_expand_grad(hb_ref, gz_ref):
        fast = dot_tn(hb_ref[:, mid:], gz_ref[:, slow_wide:])
        total = None
        for phase in range(PHASES):
            part = fast[
                phase * fast_part : (phase + 1) * fast_part,
                phase * lanes_fast : (phase + 1) * lanes_fast,
            ]
            total = part if total is None else total + part
        return total

    def space_grad(ha_ref, taps_ref, out_ref, at):
        fast_grads = []
        for tap in range(9):
            value = dot_tn(ha_ref[:, :mid], taps_ref[tap, :, :mid])
            low = at + tap * depth_mid
            out_ref[:, low : low + depth_mid, :] = value.astype(BF16).reshape(
                count, depth_mid, mid
            )
            fast = dot_tn(ha_ref[:, mid:], taps_ref[tap, :, mid:])
            total = None
            for phase in range(PHASES):
                part = lane_block(
                    fast[phase * fast_part : (phase + 1) * fast_part], phase, fast_part
                )
                total = part if total is None else total + part
            fast_grads.append(total)
        if isinstance(out_ref, Store):
            out_ref.send_rows(at, at + 9 * depth_mid)
        return fast_grads

    def put_fast(reduce, space, expand, out_ref, at):
        lane = lax.broadcasted_iota(jnp.int32, reduce[0].shape, 1)

        def beside(parts):
            keep = lane[: parts[0].shape[0]]
            total = None
            for place, part in enumerate(parts):
                part = jnp.where(keep < fast_part, part, 0.0)
                part = pltpu.roll(part, place * fast_part, 1) if place else part
                total = part if total is None else total + part
            return total

        depth = reduce[0].shape[0] // count
        taps = beside(reduce).astype(BF16).reshape(count, depth, lanes_fast)
        out_ref[:, at : at + depth, :] = jnp.concatenate([taps, jnp.zeros_like(taps)], axis=-1)

        def spread(value):
            tiles = value.reshape(count // 2, SUB, lanes_fast)
            return jnp.stack([tiles, pltpu.roll(tiles, SUB // 2, 1)], axis=1).reshape(
                count, SUB, lanes_fast
            )

        first = jnp.concatenate([spread(beside(space[0:4])), spread(beside(space[4:8]))], axis=-1)
        second = jnp.concatenate([spread(beside(space[8:9])), spread(expand)], axis=-1)
        both = jnp.concatenate([first, second], axis=1).astype(BF16)
        out_ref[:, at + depth : at + depth + 2 * SUB, :] = both
        if isinstance(out_ref, Store):
            out_ref.send_rows(at, at + depth + 2 * SUB)

    def space_back_stage(
        g, zb, za, halo, stats_b, parts_b, params_b, stats_a, params_a, g_hbm, at, fast_w
    ):
        def kernel(
            meta_ref,
            inv_ref,
            sums_b_ref,
            g_ref,
            side_ref,
            up_ref,
            down_ref,
            stats_b_ref,
            stats_a_ref,
            zb_ref,
            za_ref,
            params_b_ref,
            params_a_ref,
            fast_ref,
            loads,
            taps_ref,
            g_out,
            sums_out,
        ):
            limit = meta_ref[0]
            coeffs = affine(stats_b_ref, params_b_ref, inv_ref, mid)
            both = [back_rows(sums_b_ref, inv_ref, mid, row) for row in range(2)]

            def back(gradient, value, valid):
                return norm_back(gradient, value, coeffs, both, valid)

            def halo_back(value, scale):
                value = geo.three(value.astype(F32))
                valid = mask_groups(value[..., :small].shape, limit, scale)
                return back(value[..., :small], value[..., small:], valid)

            def edge_back(value):
                value = geo.three(value.astype(F32))
                shape = value[..., :small].shape
                group = lax.broadcasted_iota(jnp.int32, shape, 0) * SUB % EDGE
                group = group + lax.broadcasted_iota(jnp.int32, shape, 1)
                return geo.flat(back(value[..., :small], value[..., small:], group < limit))

            own, zb = geo.three(g_ref[...]), geo.three(zb_ref[...])
            edges = jnp.concatenate(
                [up_ref[half_rows:], side_ref[...], down_ref[half_rows:]], axis=0
            )

            near_by = Neighbours(
                back(own, zb, mask_groups(own.shape, limit)),
                halo_back(up_ref[:half_rows], 2),
                halo_back(down_ref[:half_rows], 2),
                edge_back(edges),
                meta_ref,
                geo.width,
            )
            slow = fast = None
            for tap in range(9):
                moved = geo.flat(near_by.at(1 - tap // 3, 1 - tap % 3)).astype(BF16)
                taps_ref[tap] = moved
                if tap == 8:
                    taps_ref.send()
                slow_term = dot_nt(moved[:, :mid], loads.get(tap))
                fast_term = dot_nt(moved[:, mid:], fast_ref[tap])
                slow = slow_term if slow is None else slow + slow_term
                fast = fast_term if fast is None else fast + fast_term
            scale, shift, mean, inv = affine(stats_a_ref, params_a_ref, inv_ref, mid)
            za = geo.three(za_ref[...])
            result = geo.three(jnp.concatenate([slow, fast], axis=1)) * slope(za * scale + shift)
            g_out[...] = geo.flat(result)
            masked = jnp.where(mask_groups(result.shape, limit), result, 0.0)
            put_back(sums_out, masked, (za - mean) * inv)

        taps, g, sums, sums_b = run(
            kernel,
            [((9, rows, small), BF16, "hbm"), small_next, stats_small],
            smem=scalars,
            parts=(parts_b,),
            vmem=(g,),
            saved=(*halo, stats_b, stats_a, zb, za, params_b, params_a, fast_w),
            weights=((g_hbm, at, 9, depth_mid),),
        )
        return taps, g, exchange(sums), sums_b

    taps_two, g_a2, parts_a2, sums_b2 = space_back_stage(
        g_b2,
        zb_two,
        za_two,
        halo_back_two,
        stats_b2,
        parts_b2,
        params_two[1],
        stats_a2,
        params_two[0],
        last,
        at_space_two,
        fast_two[3],
    )
    def grads_two_kernel(hb_ref, gz_ref, ha_ref, taps_ref, out_ref, fast_out):
        space = space_grad(ha_ref, taps_ref, out_ref, 0)
        expand_grad(hb_ref, gz_ref, out_ref, 9 * depth_mid)
        for tap in range(9):
            fast_out[tap] = space[tap]
        fast_out[9] = fast_expand_grad(hb_ref, gz_ref)

    rows_space = aligned((9 + blocks) * depth_mid)
    packed_space, fast_space_two = run(
        grads_two_kernel,
        [((count, rows_space, mid), BF16, "rows"), ((10, fast_part, lanes_fast), F32, "hbm")],
        saved=(hb_two, gz_c2, ha_two, taps_two),
    )
    sum_space = lax.psum_scatter(packed_space, TILE, scatter_dimension=0, tiled=False)

    def reduce_gz(meta_ref, inv_ref, g_ref, za_ref, stats_ref, sums_ref, params_ref, steps_ref):
        coeffs = affine(stats_ref, params_ref, inv_ref, mid)
        both = [back_rows(sums_ref, inv_ref, mid, row) for row in range(2)]
        gradient = geo.three(g_ref[...])
        gz = norm_back(
            gradient,
            geo.three(za_ref[...]),
            coeffs,
            both,
            mask_groups(gradient.shape, meta_ref[0]),
        )
        gz = geo.flat(gz)
        steps = [geo.shift(gz, -1).astype(BF16), gz.astype(BF16), geo.shift(gz, 1).astype(BF16)]
        for tap in range(3):
            steps_ref[tap] = steps[tap]
        if isinstance(steps_ref, Store):
            steps_ref.send()
        return steps

    def reduce_back_two_kernel(
        meta_ref,
        inv_ref,
        sums_ref,
        g_ref,
        stats_ref,
        stats_c_ref,
        za_ref,
        params_ref,
        g_two_ref,
        sum_ref,
        zc_ref,
        short_ref,
        main_ref,
        before_ref,
        after_ref,
        loads,
        steps_ref,
        fast_out,
        g_out,
        sums_out,
    ):
        steps = reduce_gz(
            meta_ref, inv_ref, g_ref, za_ref, stats_ref, sums_ref, params_ref, steps_ref
        )
        slow = None
        for tap in range(3):
            term = dot_nt(steps[tap][:, :mid], loads.get(tap))
            slow = term if slow is None else slow + term
        fast = fast_conv_back(
            [step[:, mid:] for step in steps], main_ref[...], before_ref[...], after_ref[...]
        )
        back = jnp.concatenate([slow, fast], axis=1) + g_two_ref[...].astype(F32)
        back = back * slope(sum_ref[...].astype(F32))
        g_out[...] = back
        fast_out[...] = back[:, slow_wide:]
        fast_out.send()
        back = geo.three(back)
        masked = jnp.where(mask_groups(back.shape, meta_ref[0]), back, 0.0)
        mean, inv = moments(stats_c_ref, inv_ref, slow_wide, 0, wide)
        put_back(sums_out, masked, (geo.three(zc_ref[...].astype(F32)) - mean) * inv)
        mean, inv = moments(stats_c_ref, inv_ref, slow_wide, wide, wide + slow_wide)
        masked = masked[..., :slow_wide]
        put_back(sums_out, masked, (geo.three(short_ref[...].astype(F32)) - mean) * inv, wide)

    steps_two, g_one, g_next, sums, sums_a2 = run(
        reduce_back_two_kernel,
        [
            ((3, rows, small), BF16, "hbm"),
            ((rows, fast_wide), F32, "hbm"),
            wide_next,
            stats_both,
        ],
        smem=scalars,
        parts=(parts_a2,),
        vmem=(g_a2,),
        saved=(stats_a2, stats_c1, za_two, params_two[0], g_two, sum_one, zc_one, short, *fast_two[:3]),
        weights=((far, at_reduce_two, 3, depth_two),),
    )
    parts_c1 = exchange_widest(sums)

    def expand_back_one_kernel(*refs):
        *body, short_ref, short_params_ref, loads, gz_ref, g_out, sums_out, message, edge, gs_ref = (
            refs
        )
        gradient = expand_back_body(*body, loads, gz_ref, g_out, sums_out, message, edge)
        meta_ref, inv_ref, sums_ref, _, stats_ref = body[:5]
        low, high = wide, wide + slow_wide
        coeffs = affine(stats_ref, short_params_ref, inv_ref, slow_wide, low, high)
        both = [back_rows(sums_ref, inv_ref, slow_wide, row, low, high) for row in range(2)]
        gradient = gradient[..., :slow_wide]
        valid = mask_groups(gradient.shape, meta_ref[0])
        gs = norm_back(gradient, geo.three(short_ref[...].astype(F32)), coeffs, both, valid)
        gs_ref[...] = geo.flat(gs).astype(BF16)

    gz_c1, g_b1, sums, message, edges, gz_short, sums_c1 = run(
        expand_back_one_kernel,
        [((rows, wide), BF16, "hbm"), small_next, stats_small, *message_back]
        + [((rows, slow_wide), BF16, "hbm")],
        smem=scalars,
        parts=(parts_c1,),
        vmem=(g_next,),
        saved=(stats_c1, stats_b1, zc_one, params_one[2], zb_one, params_one[1], fast_one[4])
        + (short, params_short),
        weights=((far, 0, blocks, depth_mid),),
    )
    parts_b1 = exchange(sums)
    halo_back_one = exchange_halo(message, edges)
    joined_lanes = slow_wide + lat

    def grads_mid_kernel(
        x_ref,
        united_ref,
        gs_ref,
        hb_ref,
        gz_ref,
        low_ref,
        steps_ref,
        fast_ref,
        loads,
        out_ref,
        back_ref,
    ):
        for tap in range(3):
            value = dot_tn(low_ref[:, :slow_wide], steps_ref[tap, :, :mid])
            out_ref[:, tap * depth_two : (tap + 1) * depth_two, :] = value.astype(BF16).reshape(
                count, depth_two, mid
            )
        at = 3 * depth_two
        out_ref.send_rows(0, at)
        reduce = fast_reduce_grad(
            low_ref[:, slow_wide:], [steps_ref[tap, :, mid:] for tap in range(3)]
        )
        put_fast(reduce, [fast_ref[tap] for tap in range(9)], fast_ref[9], out_ref, at)
        at += fast_rows_count
        expand_grad(hb_ref, gz_ref, out_ref, at + blocks * depth_one)
        for block in range(blocks):
            gs = gs_ref[:, block * mid : (block + 1) * mid]
            value = jnp.concatenate([dot_tn(x_ref[...], gs), dot_tn(united_ref[...], gs)], axis=0)
            low = at + block * depth_one
            out_ref[:, low : low + depth_one, :] = value.astype(BF16).reshape(
                count, depth_one, mid
            )
            out_ref.send_rows(low, low + depth_one)
        for block in range(blocks):
            gs = gs_ref[:, block * mid : (block + 1) * mid]
            term = dot_nt(gs, loads.get(block))
            back_ref[...] = term if block == 0 else back_ref[...] + term

    rows_mid = aligned(3 * depth_two + fast_rows_count + blocks * (depth_one + depth_mid))
    packed_mid, short_back = run(
        grads_mid_kernel,
        [((count, rows_mid, mid), BF16, "rows"), ((rows, joined_lanes), F32, "hbm")],
        saved=(slow_x, united, gz_short, hb_one, gz_c1, low_one, steps_two, fast_space_two),
        weights=((far, at_short, blocks, depth_one),),
    )
    sum_mid = lax.psum_scatter(packed_mid, TILE, scatter_dimension=0, tiled=False)

    taps_one, g_a1, parts_a1, sums_b1 = space_back_stage(
        g_b1,
        zb_one,
        za_one,
        halo_back_one,
        stats_b1,
        parts_b1,
        params_one[1],
        stats_a1,
        params_one[0],
        near,
        at_space_one,
        fast_one[3],
    )
    def last_kernel(
        meta_ref,
        inv_ref,
        sums_ref,
        g_ref,
        stats_ref,
        za_ref,
        params_ref,
        g_one_ref,
        short_ref,
        lateral_ref,
        main_ref,
        before_ref,
        after_ref,
        loads,
        steps_ref,
        slow_ref,
        fast_ref,
        united_ref,
    ):
        steps = reduce_gz(
            meta_ref, inv_ref, g_ref, za_ref, stats_ref, sums_ref, params_ref, steps_ref
        )
        joined = short_ref[...]
        for tap in range(3):
            joined = joined + dot_nt(steps[tap][:, :mid], loads.get(tap))
        slow_ref[...] = joined[:, :slow_wide]
        tail = joined[:, slow_wide:]
        now, past = tail.astype(BF16), geo.shift(tail, -1).astype(BF16)
        united_ref[0] = now
        united_ref[1] = past
        lanes = fast_wide // PHASES
        fast = fast_conv_back(
            [step[:, mid:] for step in steps], main_ref[...], before_ref[...], after_ref[...]
        )
        fast = fast + g_one_ref[...]
        front = dot_nt(now, lateral_ref[2:5].reshape(3 * lanes, lat))
        back = dot_nt(past, lateral_ref[0:2].reshape(2 * lanes, lat))
        fast_ref[:, : 2 * lanes] = fast[:, : 2 * lanes] + front[:, : 2 * lanes]
        fast_ref[:, 2 * lanes : 3 * lanes] = (
            fast[:, 2 * lanes : 3 * lanes] + front[:, 2 * lanes :] + back[:, :lanes]
        )
        fast_ref[:, 3 * lanes :] = fast[:, 3 * lanes :] + back[:, lanes:]

    steps_one, grad_slow, grad_fast, united_low, sums_a1 = run(
        last_kernel,
        [
            ((3, rows, small), BF16, "hbm"),
            ((rows, slow_wide), F32, "hbm"),
            ((rows, fast_wide), F32, "hbm"),
            ((2, rows, lat), BF16, "hbm"),
        ],
        smem=scalars,
        parts=(parts_a1,),
        vmem=(g_a1,),
        saved=(stats_a1, za_one, params_one[0], g_one, short_back, lateral, *fast_one[:3]),
        weights=((near, 0, 3, depth_one),),
    )

    def grads_one_kernel(
        meta_ref,
        steps_ref,
        low_ref,
        x_ref,
        united_ref,
        fast_x_ref,
        ha_ref,
        taps_ref,
        hb_ref,
        gz_ref,
        own_ref,
        send_ref,
        out_ref,
        sems,
    ):
        lanes = fast_wide // PHASES
        for tap in range(3):
            step = steps_ref[tap, :, :mid]
            value = jnp.concatenate(
                [dot_tn(x_ref[...], step), dot_tn(united_ref[...], step)], axis=0
            )
            out_ref[:, tap * depth_one : (tap + 1) * depth_one, :] = value.astype(BF16).reshape(
                count, depth_one, mid
            )
        at = 3 * depth_one
        place = (own_ref, send_ref, meta_ref[1], meta_ref[2], sems)
        put_blocks(out_ref, 0, at, *place, 0)
        past = dot_tn(fast_x_ref[:, 2 * lanes :], low_ref[1])
        now = dot_tn(fast_x_ref[:, : 3 * lanes], low_ref[0])
        both = jnp.concatenate([past, now], axis=0).astype(BF16)
        for tap in range(5):
            out_ref[:, at + tap * depth_lat : at + (tap + 1) * depth_lat, :] = both[
                tap * lanes : (tap + 1) * lanes
            ].reshape(count, depth_lat, lat)
        at += 5 * depth_lat
        space = space_grad(ha_ref, taps_ref, out_ref, at)
        at += 9 * depth_mid
        reduce = fast_reduce_grad(
            fast_x_ref[...], [steps_ref[tap, :, mid:] for tap in range(3)]
        )
        put_fast(reduce, space, fast_expand_grad(hb_ref, gz_ref), out_ref, at)

        put_blocks(out_ref, 3 * depth_one, rows_late, *place, 1)
        for low, top, turn in ((0, 3 * depth_one, 0), (3 * depth_one, rows_late, 1)):
            rows_part = pl.ds(low, top - low)
            for block in range(count):
                source, target = out_ref.at[block, rows_part, :], own_ref.at[0, rows_part, :]
                pltpu.make_async_copy(source, target, sems.at[turn, block]).wait()

    def put_blocks(blocks_ref, low, top, own_ref, send_ref, ha, wa, sems, turn):
        rows_part = pl.ds(low, top - low)
        for block in range(count):
            place, col = ha ^ (block // 2), block % 2
            source, sem = blocks_ref.at[block, rows_part, :], sems.at[turn, block]

            @pl.when(wa == col)
            def _():
                pltpu.make_async_copy(source, own_ref.at[place, rows_part, :], sem).start()

            @pl.when(wa != col)
            def _():
                pltpu.make_async_copy(source, send_ref.at[place, rows_part, :], sem).start()

    high = count // 2
    rows_one = 3 * depth_one + 5 * depth_lat + 9 * depth_mid + fast_rows_count
    rows_late = aligned(rows_one)
    blocks_out = ((high, rows_late, mid), BF16, "raw")
    own_blocks, send_blocks = run(
        grads_one_kernel,
        [blocks_out, blocks_out],
        smem=(meta,),
        saved=(steps_one, united_low, slow_x, united, fast_x, ha_one, taps_one, hb_one, gz_c1),
        scratch=(
            pltpu.VMEM((count, rows_late, mid), BF16),
            pltpu.SemaphoreType.DMA((2, count)),
        ),
    )
    side_blocks = lax.ppermute(send_blocks, "wa", xor_pairs(2, 1))

    def chip_kernel(own_ref, side_ref, *out_refs):
        for place in range(high):
            total = own_ref[place].astype(F32) + side_ref[place].astype(F32)
            out_refs[place][...] = total.astype(BF16)
            out_refs[place].send()

    late_out = ((rows_late, mid), BF16, "hbm")
    four = lax.axis_size("clips") == 4
    halves = clip_parts(meta, [[sum_space], [sum_mid]], 2 if four else 1)
    own_blocks, side_blocks, halves = lax.optimization_barrier((own_blocks, side_blocks, halves))
    total_early = halves_sum(*halves) if four else lax.psum(halves[0], "clips")
    chip_sums = run(chip_kernel, [late_out] * high, saved=(own_blocks, side_blocks))
    late = [chip_sums[0]] + to_partners(chip_sums[1:], "ha")
    parts_early = halves_share(total_early) if four else [total_early]
    late, _ = lax.optimization_barrier((late, total_early))
    quarters = clip_parts(meta, [late], 4 if four else 1)
    if four:
        total_late = add_low(quarters[0], *to_partners(quarters[1:], "clips"))
        parts_late = [total_late] + to_partners([total_late] * 3, "clips")
    else:
        parts_late = [lax.psum(quarters[0], "clips")]

    def finish(parts, groups, by_halves):
        size = len(parts)
        outs_all = []
        for _, shapes in groups:
            for shape in shapes:
                outs_all += list(shape) if isinstance(shape[0], tuple) else [shape]

        def kernel(meta_ref, *refs):
            ins, outs, total_ref = refs[:size], list(refs[size:-1]), refs[-1]
            depth = sum(rows_group for rows_group, _ in groups) // size
            base = 0
            for step, ref in enumerate(ins):
                clip = meta_ref[4] ^ step
                place = clip % 2 * 2 + clip // 2 if by_halves else clip
                start = pl.multiple_of(place * depth, 16) if size > 1 else 0
                total_ref[pl.ds(start, depth), :] = ref[...].astype(F32)
            for rows_group, shapes in groups:
                at = base
                for shape in shapes:
                    if isinstance(shape[0], tuple):
                        reduce, space, expand = outs.pop(0), outs.pop(0), outs.pop(0)
                        rows_tap, lanes = reduce.shape[1:]
                        for tap in range(3):
                            reduce[tap] = total_ref[
                                at : at + rows_tap, tap * lanes : (tap + 1) * lanes
                            ]
                        few = space.shape[2]
                        for tap in range(9):
                            row = at + rows_tap + tap // SUB * SUB
                            lane = tap % SUB * lanes
                            space[tap // 3, tap % 3] = total_ref[
                                row : row + few, lane : lane + lanes
                            ]
                        row = at + rows_tap + SUB
                        expand[...] = total_ref[row : row + few, expand.shape[1] :]
                        for out in (reduce, space, expand):
                            out.send()
                        at += rows_tap + 2 * SUB
                        continue
                    out = outs.pop(0)
                    if len(shape) == 2 and shape[1] > mid:
                        for block in range(shape[1] // mid):
                            out[:, block * mid : (block + 1) * mid] = total_ref[
                                at : at + shape[0], :
                            ]
                            at += shape[0]
                    else:
                        number = 1
                        for length in shape[:-1]:
                            number *= length
                        out[...] = total_ref[at : at + number, :].reshape(shape)
                        at += number
                    out.send()
                base += rows_group

        return run(
            kernel,
            [(shape, F32, "hbm") for shape in outs_all],
            smem=(meta,),
            saved=parts,
            scratch=(pltpu.VMEM((sum(rows_group for rows_group, _ in groups), mid), F32),),
        )

    shapes_one = tuple(shard.shape for shard in fast_shards_one)
    shapes_two = tuple(shard.shape for shard in fast_shards_two)
    grad_slow_spatial_two, grad_slow_expand_two, grad_slow_reduce_two, *rest = finish(
        parts_early,
        [
            (rows_space, [slow_spatial_two.shape, slow_expand_two.shape]),
            (
                rows_mid,
                [slow_reduce_two.shape, shapes_two, slow_shortcut_one.shape, slow_expand_one.shape],
            ),
        ],
        True,
    )
    fast_two_grads, (grad_slow_shortcut, grad_slow_expand_one) = rest[:3], rest[3:]
    grad_slow_reduce_one, grad_lateral, grad_slow_spatial_one, *fast_one_grads = finish(
        parts_late,
        [
            (
                rows_late,
                [slow_reduce_one.shape, lateral_weight.shape, slow_spatial_one.shape, shapes_one],
            )
        ],
        False,
    )

    def norm_grads(first, second, third):
        slow = [first[:, :mid], second[:, :mid], third[:, :slow_wide]]
        fast = [first[:, mid:], second[:, mid:], third[:, slow_wide:wide]]
        fast = [jnp.sum(part.reshape(2, PHASES, -1), axis=1) for part in fast]
        return slow, fast

    slow_one_p, fast_one_p = norm_grads(sums_a1, sums_b1, sums_c1)
    slow_two_p, fast_two_p = norm_grads(sums_a2, sums_b2, sums_c2)
    grad_slow_norms_one = jnp.concatenate(slow_one_p + [sums_c1[:, wide:]], axis=1)
    grad_slow_norms_two = jnp.concatenate(slow_two_p, axis=1)
    grad_fast_norms_one = jnp.concatenate(fast_one_p, axis=1)
    grad_fast_norms_two = jnp.concatenate(fast_two_p, axis=1)
    return (
        outputs[:, :slow_wide].reshape(slow_input.shape),
        join_phases(outputs[:, slow_wide:], fast_input.shape),
        grad_slow.reshape(slow_input.shape),
        join_phases(grad_fast, fast_input.shape),
        grad_lateral,
        grad_slow_reduce_one,
        grad_slow_spatial_one,
        grad_slow_expand_one,
        grad_slow_shortcut,
        *fast_one_grads,
        grad_slow_reduce_two,
        grad_slow_spatial_two,
        grad_slow_expand_two,
        *fast_two_grads,
        grad_slow_norms_one,
        grad_fast_norms_one,
        grad_slow_norms_two,
        grad_fast_norms_two,
    )


def solution(mesh):
    in_specs = (
        P("clips", None, "ha", "wa", None),
        P("clips", None, "ha", "wa", None),
        P("clips", None, "ha", "wa", None),
        P("clips", None, "ha", "wa", None),
        P("clips"),
        P(None, ("ha", "wa"), None),
        P(None, ("ha", "wa"), None),
        P(None, None, ("ha", "wa"), None),
        P(("ha", "wa"), None),
        P(("ha", "wa"), None),
        P(None, ("ha", "wa"), None),
        P(None, None, ("ha", "wa"), None),
        P(("ha", "wa"), None),
        P(None, ("ha", "wa"), None),
        P(None, None, ("ha", "wa"), None),
        P(("ha", "wa"), None),
        P(None, ("ha", "wa"), None),
        P(None, None, ("ha", "wa"), None),
        P(("ha", "wa"), None),
        P(),
        P(),
        P(),
        P(),
    )
    out_specs = (
        P("clips", None, "ha", "wa", None),
        P("clips", None, "ha", "wa", None),
        P("clips", None, "ha", "wa", None),
        P("clips", None, "ha", "wa", None),
        P(None, ("ha", "wa"), None),
        P(None, ("ha", "wa"), None),
        P(None, None, ("ha", "wa"), None),
        P(("ha", "wa"), None),
        P(("ha", "wa"), None),
        P(None, ("ha", "wa"), None),
        P(None, None, ("ha", "wa"), None),
        P(("ha", "wa"), None),
        P(None, ("ha", "wa"), None),
        P(None, None, ("ha", "wa"), None),
        P(("ha", "wa"), None),
        P(None, ("ha", "wa"), None),
        P(None, None, ("ha", "wa"), None),
        P(("ha", "wa"), None),
        P(),
        P(),
        P(),
        P(),
    )
    return jax.shard_map(
        on_device, mesh=mesh, in_specs=in_specs, out_specs=out_specs, check_vma=False
    )
```

```python
import jax
import jax.numpy as jnp
from jax import lax
from jax.experimental import pallas as pl
from jax.experimental.pallas import tpu as pltpu
from jax.sharding import PartitionSpec as P

epsilon = 1e-05
F32 = jnp.float32
BF16 = jnp.bfloat16
TILE = ("ha", "wa")
PHASES = 4
SUB = 8


def dot(left, right):
    return lax.dot_general(left, right, (((1,), (0,)), ((), ())), preferred_element_type=F32)


def dot_tn(left, right):
    return lax.dot_general(left, right, (((0,), (0,)), ((), ())), preferred_element_type=F32)


def dot_nt(left, right):
    return lax.dot_general(left, right, (((1,), (1,)), ((), ())), preferred_element_type=F32)


class Loads:
    def __init__(self, source, offset, target, sems, first):
        self.copies = []
        depth = target.shape[2]
        for step in range(target.shape[0]):
            copy = pltpu.make_async_copy(
                source.at[:, pl.ds(offset + step * depth, depth), :],
                target.at[step],
                sems.at[first + step],
            )
            copy.start()
            self.copies.append(copy)
        self.target = target

    def get(self, step):
        self.copies[step].wait()
        block = self.target[step]
        return block.reshape(-1, block.shape[-1])


class Saved:
    def __init__(self, source, scratch, sem):
        self.scratch, self.shape = scratch, scratch.shape
        self.copy = pltpu.make_async_copy(source, scratch, sem)
        self.copy.start()
        self.ready = False

    def wait(self):
        if not self.ready:
            self.copy.wait()
            self.ready = True

    def __getitem__(self, index):
        self.wait()
        return self.scratch[index]


SEGMENTS = 8


class Store:
    def __init__(self, scratch, target, sems):
        self.scratch, self.target, self.shape = scratch, target, scratch.shape
        self.sems, self.copies = sems, []

    def send(self):
        self.copies.append(pltpu.make_async_copy(self.scratch, self.target, self.sems[0]))
        self.copies[-1].start()

    def send_rows(self, low, high):
        rows = pl.ds(low, high - low)
        source, target = self.scratch.at[:, rows, :], self.target.at[:, rows, :]
        self.copies.append(pltpu.make_async_copy(source, target, self.sems[len(self.copies)]))
        self.copies[-1].start()

    def __setitem__(self, index, value):
        self.scratch[index] = value

    def __getitem__(self, index):
        return self.scratch[index]


CLOSE = 200 * 1024


def run(body, outs, smem=(), parts=(), vmem=(), saved=(), weights=(), scratch=(), limit=53):
    near = pl.BlockSpec(memory_space=pltpu.VMEM)
    far = pl.BlockSpec(memory_space=pltpu.HBM)
    sources = []
    for array, *_ in weights:
        if not any(array is other for other in sources):
            sources.append(array)
    outs = list(outs) + [(part.shape[1:], part.dtype, "hbm") for part in parts]
    flat = []
    for shape, dtype, kind in outs:
        flat += [(shape, dtype, "raw"), (shape, dtype, "vmem")] if kind == "both" else [(shape, dtype, kind)]
    close = [array.size * array.dtype.itemsize <= CLOSE for array in saved]
    held = [pltpu.VMEM(array.shape, array.dtype) for array, here in zip(saved, close) if not here]
    for array, _, steps, depth in weights:
        held.append(pltpu.VMEM((steps, array.shape[0], depth, array.shape[2]), array.dtype))
    for shape, dtype, kind in outs:
        if kind in ("hbm", "rows"):
            held.append(pltpu.VMEM(shape, dtype))
        elif kind == "spread":
            held.append(pltpu.VMEM(shape[1:], dtype))
    sems = len(saved) + sum(steps for _, _, steps, _ in weights) + len(outs)
    sems += SEGMENTS * sum(kind == "rows" for _, _, kind in outs)
    held.append(pltpu.SemaphoreType.DMA((sems,)))

    def kernel(*refs):
        refs = list(refs)

        def take(number):
            taken = refs[:number]
            del refs[:number]
            return taken

        smem_refs, part_refs, vmem_refs = take(len(smem)), take(len(parts)), take(len(vmem))
        saved_refs, source_refs, out_refs = take(len(saved)), take(len(sources)), take(len(flat))
        saved_scratch, weight_scratch = take(len(saved) - sum(close)), take(len(weights))
        out_scratch = take(sum(kind in ("hbm", "rows", "spread") for _, _, kind in outs))
        sem, more = refs[0], refs[1:]
        arrays, copies = [], []
        for source, here in zip(saved_refs, close):
            if not here:
                copies.append(Saved(source, saved_scratch[len(copies)], sem.at[len(copies)]))
            arrays.append(source if here else copies[-1])
        at = len(saved)
        loads = []
        for (array, offset, steps, _), target in zip(weights, weight_scratch):
            place = [array is other for other in sources].index(True)
            loads.append(Loads(source_refs[place], offset, target, sem, at))
            at += steps
        results, stores, spreads = [], [], []
        for _, _, kind in outs:
            ref = out_refs.pop(0)
            if kind == "both":
                stores.append(Store(out_refs.pop(0), ref, [sem.at[at]]))
                at += 1
                results.append(stores[-1])
            elif kind in ("hbm", "rows"):
                number = SEGMENTS if kind == "rows" else 1
                stores.append(
                    Store(out_scratch.pop(0), ref, [sem.at[at + part] for part in range(number)])
                )
                at += number
                results.append(stores[-1])
            elif kind == "spread":
                spreads.append((out_scratch.pop(0), ref))
                results.append(spreads[-1][0])
            else:
                results.append(ref)
        sums = results[len(results) - len(parts) :]
        results = results[: len(results) - len(parts)]
        for part, total in zip(part_refs, sums):
            total[...] = jnp.sum(part[...], axis=0)
            total.send()
        totals = [total.scratch for total in sums]
        body(*smem_refs, *totals, *vmem_refs, *arrays, *loads, *results, *more)
        for copy in copies:
            copy.wait()
        for store in stores:
            if not store.copies:
                store.send()
        for value, ref in spreads:
            ref[...] = jnp.broadcast_to(value[...][None], ref.shape)
        for store in stores:
            for copy in store.copies:
                copy.wait()

    return pl.pallas_call(
        kernel,
        out_shape=[jax.ShapeDtypeStruct(shape, dtype) for shape, dtype, _ in flat],
        in_specs=[pl.BlockSpec(memory_space=pltpu.SMEM)] * len(smem)
        + [near] * (len(parts) + len(vmem))
        + [near if here else far for here in close]
        + [far] * len(sources),
        out_specs=[far if kind in ("hbm", "rows", "raw") else near for _, _, kind in flat],
        scratch_shapes=held + list(scratch),
        compiler_params=pltpu.CompilerParams(vmem_limit_bytes=limit * 1024 * 1024),
        cost_estimate=pl.CostEstimate(
            flops=2_000_000_000, bytes_accessed=16_000_000, transcendentals=0
        ),
    )(*smem, *parts, *vmem, *saved, *sources)


class Geometry:
    def __init__(self, slow_shape, fast_shape):
        self.cap, self.frames, self.height, self.width = slow_shape[:4]
        self.groups = self.cap * self.frames
        self.rows = self.groups * SUB

    def three(self, value):
        return value.reshape(-1, SUB, value.shape[-1])

    def flat(self, value):
        return value.reshape(-1, value.shape[-1])

    def shift(self, value, step):
        lanes = value.shape[-1]
        whole = value.reshape(self.cap, self.frames, SUB, lanes)
        zero = jnp.zeros((self.cap, 1, SUB, lanes), value.dtype)
        if step > 0:
            whole = jnp.concatenate([zero, whole[:, :-1]], axis=1)
        else:
            whole = jnp.concatenate([whole[:, 1:], zero], axis=1)
        return whole.reshape(-1, lanes)


def mask_groups(shape, limit, scale=1):
    return lax.broadcasted_iota(jnp.int32, shape, 0) * scale < limit


def rep(ref, row, low, high):
    return jnp.broadcast_to(ref[row : row + 1, low:high], (SUB, high - low))


def fold(value, slow):
    fast = value[:, slow:]
    lanes = fast.shape[-1]
    part = lanes // PHASES
    if part % 128 == 0:
        total = fast[:, :part]
        for phase in range(1, PHASES):
            total = total + fast[:, phase * part : (phase + 1) * part]
        return jnp.concatenate([value[:, :slow]] + [total] * PHASES, axis=1)
    total = fast
    for phase in range(1, PHASES):
        total = total + pltpu.roll(fast, phase * part, 1)
    return jnp.concatenate([value[:, :slow], total], axis=1)


def lane_counts(inv_ref, lanes, slow):
    lane = lax.broadcasted_iota(jnp.int32, (SUB, lanes), 1)
    return jnp.where(lane < slow, inv_ref[0], inv_ref[1])


def moments(stats, inv_ref, slow, low=0, high=None):
    high = stats.shape[1] if high is None else high
    total, square = rep(stats, 0, low, high), rep(stats, 1, low, high)
    if slow < high - low:
        total, square = fold(total, slow), fold(square, slow)
    inv_n = lane_counts(inv_ref, high - low, slow)
    mean = total * inv_n
    return mean, lax.rsqrt(square * inv_n - mean * mean + epsilon)


def affine(stats, params, inv_ref, slow, low=0, high=None):
    mean, inv = moments(stats, inv_ref, slow, low, high)
    lanes = mean.shape[1]
    scale = (1.0 + rep(params, 0, 0, lanes)) * inv
    return scale, rep(params, 1, 0, lanes) - mean * scale, mean, inv


def back_rows(sums, inv_ref, slow, row, low=0, high=None):
    high = sums.shape[1] if high is None else high
    total = rep(sums, row, low, high)
    if slow < high - low:
        total = fold(total, slow)
    return total * lane_counts(inv_ref, high - low, slow)


def silu(value):
    return value * jax.nn.sigmoid(value)


def slope(value):
    sigma = jax.nn.sigmoid(value)
    return sigma * (1.0 + value * (1.0 - sigma))


def put_stats(ref, first, second, low=0):
    lanes = first.shape[-1]
    ref[0:1, low : low + lanes] = jnp.sum(jnp.sum(first, axis=0), axis=0, keepdims=True)
    ref[1:2, low : low + lanes] = jnp.sum(jnp.sum(second, axis=0), axis=0, keepdims=True)


def put_back(ref, gradient, normal, low=0):
    put_stats(ref, gradient * normal, gradient, low)


def put_forward(ref, value, limit, low=0):
    masked = jnp.where(mask_groups(value.shape, limit), value, 0.0)
    put_stats(ref, masked, masked * value, low)


EDGE = 32


def edge_place(wa, width):
    return jnp.where(wa > 0, 0, width - 1)


def put_message(value, ref, edge_ref, meta_ref, width):
    lanes = value.shape[-1]
    pairs = value.reshape(-1, 2, SUB, lanes)
    first, second = pairs[:, 0], pairs[:, 1]
    near = lax.broadcasted_iota(jnp.int32, first.shape, 1) < SUB // 2
    top = jnp.where(near, first, pltpu.roll(second, SUB // 2, 1))
    bottom = jnp.where(near, pltpu.roll(first, SUB // 2, 1), second)
    flat = value.reshape(-1, lanes).astype(BF16)
    shape = (2 * EDGE, flat.shape[0])
    row, col = [lax.broadcasted_iota(jnp.int32, shape, dim) for dim in range(2)]
    low = row >= EDGE
    source = (row - jnp.where(low, EDGE, 0)) * SUB + jnp.where(low, SUB // 2, 0)
    chosen = (col == source + edge_place(meta_ref[2], width)).astype(F32).astype(BF16)
    edges = dot(chosen, flat)
    edge_ref[...] = edges.astype(BF16)
    edge_ref.send()
    top, bottom = [part.reshape(-1, lanes).astype(BF16) for part in (top, bottom)]
    ref[: top.shape[0]] = top
    ref[top.shape[0] :] = bottom
    ref.send()


def unpack_bottom(value):
    both = jnp.stack([pltpu.roll(value, SUB // 2, 1), value], axis=1)
    return both.reshape(-1, SUB, value.shape[-1])


def unpack_top(value):
    both = jnp.stack([value, pltpu.roll(value, SUB // 2, 1)], axis=1)
    return both.reshape(-1, SUB, value.shape[-1])


class Neighbours:
    def __init__(self, own, up, down, edges, meta, width):
        half = SUB // 2
        near = lax.broadcasted_iota(jnp.int32, own.shape, 1) < half
        self.col = lax.broadcasted_iota(jnp.int32, own.shape, 1) % width
        self.width, self.shape = width, own.shape
        ha, wa, last = meta[1], meta[2], meta[3]
        up = unpack_bottom(jnp.where(ha > 0, up, 0.0))
        down = unpack_top(jnp.where(ha < last, down, 0.0))
        self.rows = {
            0: own,
            -1: pltpu.roll(jnp.where(near, own, up), half, 1),
            1: pltpu.roll(jnp.where(near, down, own), half, 1),
        }
        beyond = lax.broadcasted_iota(jnp.int32, edges.shape, 0)
        inside = ((ha > 0) | (beyond >= EDGE)) & ((ha < last) | (beyond < 3 * EDGE))
        self.edges = jnp.where(inside, edges, 0.0).astype(BF16)
        shape = (own.shape[0] * SUB, edges.shape[0])
        place, self.source = [lax.broadcasted_iota(jnp.int32, shape, dim) for dim in range(2)]
        self.group = place // SUB
        self.row = place // half % 2
        self.touches = place % width == edge_place(wa, width)
        self.sides = {}

    def side(self, row_step):
        if row_step not in self.sides:
            wanted = (self.row + row_step + 1) * EDGE + self.group
            chosen = ((self.source == wanted) & self.touches).astype(F32).astype(BF16)
            self.sides[row_step] = dot(chosen, self.edges).reshape(self.shape)
        return self.sides[row_step]

    def at(self, row_step, col_step):
        base = self.rows[row_step]
        if col_step < 0:
            return jnp.where(self.col == 0, self.side(row_step), pltpu.roll(base, 1, 1))
        if col_step > 0:
            away = self.col == self.width - 1
            return jnp.where(away, self.side(row_step), pltpu.roll(base, SUB - 1, 1))
        return base


def xor_pairs(size, step):
    return [(index, index ^ step) for index in range(size)]


def direct_sum(value, axis):
    size = lax.axis_size(axis)
    step = 1
    while step < size:
        if size // step >= 4:
            one, two, three = [
                lax.ppermute(value, axis, xor_pairs(size, step * times)) for times in (1, 2, 3)
            ]
            value = (value + two) + (one + three)
            step *= 4
        else:
            value = value + lax.ppermute(value, axis, xor_pairs(size, step))
            step *= 2
    return value


AXES = ("clips", "ha", "wa")
MOST = 32


def spread_count():
    count = lax.axis_size("ha") * lax.axis_size("wa")
    whole = count * lax.axis_size("clips")
    return whole if whole <= MOST else count


def exchange(copies):
    if copies.shape[0] == lax.axis_size("clips") * lax.axis_size("ha") * lax.axis_size("wa"):
        return lax.all_to_all(copies, AXES, 0, 0)
    return lax.all_to_all(direct_sum(copies, "clips"), TILE, 0, 0)


def exchange_widest(sums):
    count = lax.axis_size("ha") * lax.axis_size("wa")
    sums = direct_sum(sums, "clips")
    return lax.all_to_all(jnp.broadcast_to(sums[None], (count,) + sums.shape), TILE, 0, 0)


def exchange_halo(message, edges):
    wide, high = lax.axis_size("wa"), lax.axis_size("ha")
    half = message.shape[0] // 2
    side = lax.ppermute(edges, "wa", xor_pairs(wide, 1))
    tops = jnp.concatenate([message[:half], side[:EDGE]], axis=0)
    bottoms = jnp.concatenate([message[half:], side[EDGE:]], axis=0)
    up = lax.ppermute(bottoms, "ha", [(row, row + 1) for row in range(high - 1)])
    down = lax.ppermute(tops, "ha", [(row + 1, row) for row in range(high - 1)])
    return side, up, down


def time_conv(geo, parts, blocks):
    result = None
    for tap in range(3):
        at = 0
        total = None
        for part in parts:
            lanes = part.shape[-1]
            term = dot(part, blocks[tap][at : at + lanes])
            at += lanes
            total = term if total is None else total + term
        if tap != 1:
            total = geo.shift(total, 1 - tap)
        result = total if result is None else result + total
    return result


def fast_conv(geo, value, main, before, after):
    lanes = value.shape[-1] // PHASES
    result = dot(value, main)
    result = result + geo.shift(dot(value[:, -lanes:], before), 1)
    return result + geo.shift(dot(value[:, :lanes], after), -1)


def fast_conv_back(steps, main, before, after):
    lanes = before.shape[0]
    middle = dot_nt(steps[1], main)
    first = middle[:, :lanes] + dot_nt(steps[2], after)
    last = middle[:, -lanes:] + dot_nt(steps[0], before)
    return jnp.concatenate([first, middle[:, lanes:-lanes], last], axis=1)


def lane_block(value, phase, part):
    return pltpu.roll(value, value.shape[-1] - phase * part, 1) if phase else value


def fast_reduce_grad(value, steps):
    lanes = value.shape[-1] // PHASES
    part = steps[1].shape[-1] // PHASES
    main = dot_tn(value, steps[1])
    before = dot_tn(value[:, -lanes:], steps[0])
    after = dot_tn(value[:, :lanes], steps[2])

    def block(row, col):
        return lane_block(main[row * lanes : (row + 1) * lanes], col, part)

    result = []
    for tap in range(3):
        total = before if tap == 0 else None
        if tap == 2:
            total = lane_block(after, PHASES - 1, part)
        for col in range(PHASES):
            row = col + tap - 1
            if 0 <= row < PHASES:
                total = block(row, col) if total is None else total + block(row, col)
        result.append(total)
    return result


def gather_pack(parts):
    return lax.all_gather(jnp.concatenate(parts, axis=0), TILE, axis=0)


def columns(shard, lanes):
    depth, total = shard.shape
    return jnp.moveaxis(shard.reshape(depth, total // lanes, lanes), 1, 0).reshape(-1, lanes)


def split_phases(value):
    cap, frames, height, width, lanes = value.shape
    value = value.reshape(cap, frames // PHASES, PHASES, height, width, lanes)
    return jnp.moveaxis(value, 2, 4).reshape(-1, PHASES * lanes)


def join_phases(value, shape):
    cap, frames, height, width, lanes = shape
    value = value.reshape(cap, frames // PHASES, height, width, PHASES, lanes)
    return jnp.moveaxis(value, 4, 2).reshape(shape)


def early_gather(shards_one, shards_two, lateral):
    rows = []
    lanes = shards_one[2].shape[-1]
    kinds = [jnp.stack(pair) for pair in zip(shards_one, shards_two)]
    kinds.append(jnp.stack([lateral[..., :lanes], lateral[..., lanes:]]))
    for kind in kinds:
        flat = kind.reshape(-1, kind.shape[-1])
        rows.append(jnp.pad(flat, ((0, 0), (0, lanes - flat.shape[-1]))))
    packed = gather_pack(rows)
    result = []
    at = 0
    for kind in kinds:
        depth, width = kind.shape[-2:]
        number = kind.size // width
        part = packed[:, at : at + number, :width].reshape(packed.shape[0], -1, depth, width)
        at += number
        result.append(jnp.moveaxis(part, 0, 1).reshape(part.shape[1], -1, width))
    return result


def prepare_kernel(taps_ref, space_ref, wide_ref, lateral_ref, *refs):
    slow_one, fast_one, slow_two, fast_two, *outs = refs
    part = taps_ref.shape[-1]
    lateral, *joint = outs[10:]
    number = lateral.shape[0]
    for tap in range(number):
        lateral[tap] = jnp.concatenate([lateral_ref[tap], lateral_ref[number + tap]], axis=1)
    for layer, (slow, fast) in enumerate(((slow_one, fast_one), (slow_two, fast_two))):
        at = fast_at = 0
        for ref in joint[3 * layer : 3 * layer + 3]:
            fast_lanes = part if ref.shape[1] < slow.shape[1] // 2 else wide_ref.shape[-1]
            lanes = ref.shape[1] - PHASES * fast_lanes
            values = [slow[:, at : at + lanes]]
            values += [fast[:, fast_at : fast_at + fast_lanes]] * PHASES
            ref[...] = jnp.concatenate(values, axis=1)
            at, fast_at = at + lanes, fast_at + fast_lanes
    joint[6][...] = slow_one[:, slow_one.shape[1] - joint[6].shape[1] :]
    for layer in range(2):
        main, before, after, space, wide = outs[5 * layer : 5 * layer + 5]
        taps = [taps_ref[3 * layer + tap] for tap in range(3)]
        zero = jnp.zeros_like(taps[0])
        lanes = taps[0].shape[0]
        for row in range(PHASES):
            blocks = [
                taps[row - col + 1] if abs(row - col) <= 1 else zero for col in range(PHASES)
            ]
            main[row * lanes : (row + 1) * lanes, :] = jnp.concatenate(blocks, axis=1)
        before[...] = jnp.concatenate([taps[0]] + [zero] * (PHASES - 1), axis=1)
        after[...] = jnp.concatenate([zero] * (PHASES - 1) + [taps[2]], axis=1)
        for tap in range(9):
            block = space_ref[9 * layer + tap]
            none = jnp.zeros_like(block)
            for row in range(PHASES):
                blocks = [block if row == col else none for col in range(PHASES)]
                space[tap, row * part : (row + 1) * part, :] = jnp.concatenate(blocks, axis=1)
        block = wide_ref[layer]
        none = jnp.zeros_like(block)
        for row in range(PHASES):
            blocks = [block if row == col else none for col in range(PHASES)]
            wide[row * part : (row + 1) * part, :] = jnp.concatenate(blocks, axis=1)


def to_partners(pieces, axis):
    size = lax.axis_size(axis)
    return [
        lax.ppermute(piece, axis, xor_pairs(size, step + 1)) for step, piece in enumerate(pieces)
    ]


def clip_parts(meta, groups, number):
    lanes = groups[0][0].shape[1]
    lengths = [group[0].shape[0] for group in groups]
    depth = sum(lengths) // number
    total_ins = sum(len(group) for group in groups)

    def kernel(meta_ref, *refs):
        ins, outs, total_ref = list(refs[:total_ins]), refs[total_ins:-1], refs[-1]
        at = 0
        for group, length in zip(groups, lengths):
            mine, ins = ins[: len(group)], ins[len(group) :]
            total = mine[0][...]
            if len(mine) > 1:
                total = total.astype(F32)
                for ref in mine[1:]:
                    total = total + ref[...].astype(F32)
                total = total.astype(BF16)
            total_ref[at : at + length, :] = total
            at += length
        index = meta_ref[4] if number != 2 else meta_ref[4] % 2
        for step, out in enumerate(outs):
            start = pl.multiple_of((index ^ step) * depth, 16)
            out[...] = total_ref[pl.ds(start, depth), :]
            out.send()

    return run(
        kernel,
        [((depth, lanes), BF16, "hbm")] * number,
        smem=(meta,),
        saved=[part for group in groups for part in group],
        scratch=(pltpu.VMEM((sum(lengths), lanes), BF16),),
    )


def add_low(first, *others):
    total = first.astype(F32)
    for other in others:
        total = total + other.astype(F32)
    return total.astype(BF16)


def halves_first(keep, send):
    return add_low(keep, lax.ppermute(send, "clips", xor_pairs(4, 1)))


def halves_second(half):
    across = lax.axis_index("clips") // 2
    depth = half.shape[0] // 2
    mine = lax.dynamic_slice_in_dim(half, across * depth, depth, axis=0)
    other = lax.dynamic_slice_in_dim(half, (1 - across) * depth, depth, axis=0)
    return add_low(mine, lax.ppermute(other, "clips", xor_pairs(4, 2)))


def halves_share(total):
    beyond = lax.ppermute(total, "clips", xor_pairs(4, 2))
    beside = lax.ppermute(total, "clips", xor_pairs(4, 1))
    return [total, beside, beyond, lax.ppermute(beyond, "clips", xor_pairs(4, 1))]


def on_device(
    slow_input,
    fast_input,
    slow_cotangent,
    fast_cotangent,
    clip_counts,
    lateral_weight,
    slow_reduce_one,
    slow_spatial_one,
    slow_expand_one,
    slow_shortcut_one,
    fast_reduce_one,
    fast_spatial_one,
    fast_expand_one,
    slow_reduce_two,
    slow_spatial_two,
    slow_expand_two,
    fast_reduce_two,
    fast_spatial_two,
    fast_expand_two,
    slow_norms_one,
    fast_norms_one,
    slow_norms_two,
    fast_norms_two,
):
    geo = Geometry(slow_input.shape, fast_input.shape)
    rows, groups = geo.rows, geo.groups
    half_rows = rows // 2
    count = lax.axis_size("ha") * lax.axis_size("wa")
    spread = spread_count()
    slow_wide = slow_input.shape[-1]
    fast_wide = PHASES * fast_input.shape[-1]
    wide = slow_wide + fast_wide
    mid = slow_reduce_one.shape[-1]
    fast_part = fast_reduce_one.shape[-1]
    fast_mid = PHASES * fast_part
    small = mid + fast_mid
    lat = lateral_weight.shape[-1]
    blocks = slow_wide // mid

    depth_one = slow_reduce_one.shape[1]
    depth_two = slow_reduce_two.shape[1]
    depth_mid = slow_spatial_one.shape[2]
    depth_lat = lateral_weight.shape[1]
    near = gather_pack([slow_reduce_one.reshape(-1, mid), slow_spatial_one.reshape(-1, mid)])
    far = gather_pack(
        [
            columns(slow_expand_one, mid),
            columns(slow_shortcut_one, mid),
            slow_reduce_two.reshape(-1, mid),
        ]
    )
    last = gather_pack([slow_spatial_two.reshape(-1, mid), columns(slow_expand_two, mid)])
    at_space_one = 3 * depth_one
    at_short = blocks * depth_mid
    at_reduce_two = at_short + blocks * depth_one
    at_space_two = 0
    at_expand_two = 9 * depth_mid
    fast_shards_one = (fast_reduce_one, fast_spatial_one, fast_expand_one)
    fast_shards_two = (fast_reduce_two, fast_spatial_two, fast_expand_two)
    compact = early_gather(fast_shards_one, fast_shards_two, lateral_weight)
    structured = [
        ((fast_wide, fast_mid), BF16, "hbm"),
        ((fast_wide // PHASES, fast_mid), BF16, "hbm"),
        ((fast_wide // PHASES, fast_mid), BF16, "hbm"),
        ((9, fast_mid, fast_mid), BF16, "hbm"),
        ((fast_mid, fast_wide), BF16, "hbm"),
    ]
    joint_outs = [((2, lanes), F32, "hbm") for lanes in (small, small, wide)]
    prepared = run(
        prepare_kernel,
        structured * 2
        + [((lateral_weight.shape[0], fast_wide // PHASES, lat), BF16, "hbm")]
        + joint_outs * 2
        + [((2, slow_wide), F32, "hbm")],
        vmem=(*compact, slow_norms_one, fast_norms_one, slow_norms_two, fast_norms_two),
    )
    fast_one, fast_two, lateral = prepared[:5], prepared[5:10], prepared[10]
    params_one, params_two, params_short = prepared[11:14], prepared[14:17], prepared[17]

    held = clip_counts[0]
    clips = direct_sum(jnp.full((1, 128), held, F32), "clips")[0, 0]
    positions = clips * (SUB * geo.frames * count)
    inv_n = jnp.stack([1.0 / positions, 1.0 / (positions * PHASES)])
    ha, wa = lax.axis_index("ha"), lax.axis_index("wa")
    last_ha = jnp.full_like(ha, lax.axis_size("ha") - 1)
    meta = jnp.stack([held * geo.frames, ha, wa, last_ha, lax.axis_index("clips")])
    scalars = (meta, inv_n)

    slow_x = slow_input.reshape(rows, slow_wide)
    fast_x = split_phases(fast_input)
    cot = jnp.concatenate(
        [slow_cotangent.reshape(rows, slow_wide), split_phases(fast_cotangent)], axis=1
    )
    message_out = [((rows, small), BF16, "hbm"), ((2 * EDGE, small), BF16, "hbm")]
    stats_small = ((spread, 2, small), F32, "spread")
    stats_wide = ((spread, 2, wide), F32, "spread")
    stats_both = ((2, wide + slow_wide), F32, "vmem")
    small_out = ((rows, small), F32, "hbm")
    wide_out = ((rows, wide), F32, "hbm")
    small_both = ((rows, small), F32, "both")
    small_next = ((rows, small), F32, "vmem")
    wide_next = ((rows, wide), F32, "vmem")
    wide_low = ((rows, wide), BF16, "hbm")

    def lateral_kernel(x_ref, k_ref, main_ref, before_ref, after_ref, united_ref, fast_ref):
        lanes = x_ref.shape[1] // PHASES
        x = x_ref[...]
        main = dot(x[:, : 3 * lanes], k_ref[2:5].reshape(3 * lanes, lat))
        past = dot(x[:, 2 * lanes :], k_ref[0:2].reshape(2 * lanes, lat))
        united_ref[...] = (main + geo.shift(past, 1)).astype(BF16)
        fast_ref[...] = fast_conv(geo, x, main_ref[...], before_ref[...], after_ref[...])

    united, za_fast = run(
        lateral_kernel,
        [((rows, lat), BF16, "hbm"), ((rows, fast_mid), F32, "hbm")],
        saved=(fast_x, lateral, *fast_one[:3]),
    )

    def reduce_one_kernel(
        meta_ref, x_ref, united_ref, fast_ref, loads, za_ref, stats_ref, message_ref, edge_ref
    ):
        weights = [loads.get(tap) for tap in range(3)]
        za = time_conv(geo, (x_ref[...], united_ref[...]), weights)
        za = jnp.concatenate([za, fast_ref[...]], axis=1)
        za_ref[...] = za
        za_ref.send()
        za = geo.three(za)
        put_message(za, message_ref, edge_ref, meta_ref, geo.width)
        put_forward(stats_ref, za, meta_ref[0])

    za_one, za_next, stats, message, edges = run(
        reduce_one_kernel,
        [small_both, stats_small, *message_out],
        smem=(meta,),
        saved=(slow_x, united, za_fast),
        weights=((near, 0, 3, depth_one),),
    )
    parts_a1 = exchange(stats)
    halo_one = exchange_halo(message, edges)

    def space_stage(za, parts_a, halo, params, gathered, offset, fast_w):
        def kernel(
            meta_ref,
            inv_ref,
            stats_ref,
            za_ref,
            side_ref,
            up_ref,
            down_ref,
            params_ref,
            fast_ref,
            loads,
            zb_ref,
            hidden_ref,
            out_stats,
        ):
            scale, shift, _, _ = affine(stats_ref, params_ref, inv_ref, mid)

            def act(value):
                return silu(geo.three(value.astype(F32)) * scale + shift)

            own = act(za_ref[...])
            edges = jnp.concatenate(
                [up_ref[half_rows:], side_ref[...], down_ref[half_rows:]], axis=0
            )
            hidden_ref[...] = geo.flat(own).astype(BF16)
            hidden_ref.send()
            near_by = Neighbours(
                own,
                act(up_ref[:half_rows]),
                act(down_ref[:half_rows]),
                geo.flat(act(edges)),
                meta_ref,
                geo.width,
            )
            slow = fast = None
            for tap in range(9):
                moved = geo.flat(near_by.at(tap // 3 - 1, tap % 3 - 1)).astype(BF16)
                slow_term = dot(moved[:, :mid], loads.get(tap))
                fast_term = dot(moved[:, mid:], fast_ref[tap])
                slow = slow_term if slow is None else slow + slow_term
                fast = fast_term if fast is None else fast + fast_term
            zb = jnp.concatenate([slow, fast], axis=1)
            zb_ref[...] = zb
            zb_ref.send()
            put_forward(out_stats, geo.three(zb), meta_ref[0])

        zb, zb_next, hidden, stats, stats_a = run(
            kernel,
            [small_both, ((rows, small), BF16, "hbm"), stats_small],
            smem=scalars,
            parts=(parts_a,),
            vmem=(za,),
            saved=(*halo, params, fast_w),
            weights=((gathered, offset, 9, depth_mid),),
        )
        return zb, zb_next, hidden, exchange(stats), stats_a

    zb_one, zb_next, ha_one, parts_b1, stats_a1 = space_stage(
        za_next, parts_a1, halo_one, params_one[0], near, at_space_one, fast_one[3]
    )

    def expand_body(
        inv_ref, stats_ref, zb_ref, params_ref, fast_ref, hidden_ref, low_ref, zc_ref, loads
    ):
        scale, shift, _, _ = affine(stats_ref, params_ref, inv_ref, mid)
        hidden = geo.flat(silu(geo.three(zb_ref[...]) * scale + shift)).astype(BF16)
        hidden_ref[...] = hidden
        hidden_ref.send()
        zc_ref[:, slow_wide:] = dot(hidden[:, mid:], fast_ref[...])
        for block in range(blocks):
            zc_ref[:, block * mid : (block + 1) * mid] = dot(hidden[:, :mid], loads.get(block))
        low_ref[...] = zc_ref[...].astype(BF16)
        low_ref.send()

    def expand_one_kernel(
        meta_ref,
        inv_ref,
        stats_ref,
        zb_ref,
        params_ref,
        fast_ref,
        x_ref,
        united_ref,
        loads,
        shorts,
        hidden_ref,
        low_ref,
        zc_ref,
        short_low_ref,
        short_ref,
        out_stats,
    ):
        expand_body(
            inv_ref, stats_ref, zb_ref, params_ref, fast_ref, hidden_ref, low_ref, zc_ref, loads
        )
        put_forward(out_stats, geo.three(zc_ref[...]), meta_ref[0])
        for block in range(blocks):
            weight = shorts.get(block)
            value = dot(x_ref[...], weight[:slow_wide]) + dot(united_ref[...], weight[slow_wide:])
            short_ref[:, block * mid : (block + 1) * mid] = value
            put_forward(out_stats, geo.three(value), meta_ref[0], wide + block * mid)
        short_low_ref[...] = short_ref[...].astype(BF16)
        short_low_ref.send()

    hb_one, zc_one, zc_next, short, short_next, stats, stats_b1 = run(
        expand_one_kernel,
        [
            ((rows, small), BF16, "hbm"),
            wide_low,
            wide_next,
            ((rows, slow_wide), BF16, "hbm"),
            ((rows, slow_wide), F32, "vmem"),
            stats_both,
        ],
        smem=scalars,
        parts=(parts_b1,),
        vmem=(zb_next,),
        saved=(params_one[1], fast_one[4], slow_x, united),
        weights=((far, 0, blocks, depth_mid), (far, at_short, blocks, depth_one)),
    )
    parts_c1 = exchange_widest(stats)

    def reduce_two_kernel(
        meta_ref,
        inv_ref,
        stats_ref,
        zc_ref,
        short_ref,
        params_ref,
        short_params_ref,
        x_ref,
        main_ref,
        before_ref,
        after_ref,
        loads,
        sum_ref,
        low_ref,
        za_ref,
        out_stats,
        message_ref,
        edge_ref,
    ):
        scale, shift, _, _ = affine(stats_ref, params_ref, inv_ref, slow_wide, 0, wide)
        scale_s, shift_s, _, _ = affine(
            stats_ref, short_params_ref, inv_ref, slow_wide, wide, wide + slow_wide
        )
        normed = geo.three(zc_ref[...]) * scale + shift
        slow = normed[..., :slow_wide] + (geo.three(short_ref[...]) * scale_s + shift_s)
        fast = normed[..., slow_wide:] + geo.three(x_ref[...].astype(F32))
        total = jnp.concatenate([slow, fast], axis=-1)
        sum_ref[...] = geo.flat(total).astype(BF16)
        sum_ref.send()
        low = geo.flat(silu(total)).astype(BF16)
        low_ref[...] = low
        low_ref.send()
        weights = [loads.get(tap) for tap in range(3)]
        za = time_conv(geo, (low[:, :slow_wide],), weights)
        fast_za = fast_conv(
            geo, low[:, slow_wide:], main_ref[...], before_ref[...], after_ref[...]
        )
        za = jnp.concatenate([za, fast_za], axis=1)
        za_ref[...] = za
        za_ref.send()
        za = geo.three(za)
        put_message(za, message_ref, edge_ref, meta_ref, geo.width)
        put_forward(out_stats, za, meta_ref[0])

    sum_one, low_one, za_two, za_next, stats, message, edges, stats_c1 = run(
        reduce_two_kernel,
        [wide_low, wide_low, small_both, stats_small, *message_out],
        smem=scalars,
        parts=(parts_c1,),
        vmem=(zc_next, short_next),
        saved=(params_one[2], params_short, fast_x, *fast_two[:3]),
        weights=((far, at_reduce_two, 3, depth_two),),
    )
    parts_a2 = exchange(stats)
    halo_two = exchange_halo(message, edges)
    zb_two, zb_next, ha_two, parts_b2, stats_a2 = space_stage(
        za_next, parts_a2, halo_two, params_two[0], last, at_space_two, fast_two[3]
    )

    def expand_two_kernel(
        meta_ref,
        inv_ref,
        stats_ref,
        zb_ref,
        params_ref,
        fast_ref,
        loads,
        hidden_ref,
        low_ref,
        zc_ref,
        out_stats,
    ):
        expand_body(
            inv_ref, stats_ref, zb_ref, params_ref, fast_ref, hidden_ref, low_ref, zc_ref, loads
        )
        put_forward(out_stats, geo.three(zc_ref[...]), meta_ref[0])

    hb_two, zc_two, zc_next, stats, stats_b2 = run(
        expand_two_kernel,
        [((rows, small), BF16, "hbm"), wide_low, wide_next, stats_wide],
        smem=scalars,
        parts=(parts_b2,),
        vmem=(zb_next,),
        saved=(params_two[1], fast_two[4]),
        weights=((last, at_expand_two, blocks, depth_mid),),
    )
    parts_c2 = exchange(stats)

    def head_kernel(
        meta_ref,
        inv_ref,
        stats_ref,
        zc_ref,
        params_ref,
        sum_ref,
        cot_ref,
        out_ref,
        low_ref,
        g_ref,
        sums_ref,
    ):
        scale, shift, mean, inv = affine(stats_ref, params_ref, inv_ref, slow_wide)
        zc = geo.three(zc_ref[...])
        total = zc * scale + shift + silu(geo.three(sum_ref[...].astype(F32)))
        valid = mask_groups(total.shape, meta_ref[0])
        sigma = jax.nn.sigmoid(total)
        out_ref[...] = geo.flat(jnp.where(valid, total * sigma, 0.0)).astype(BF16)
        slopes = sigma * (1.0 + total * (1.0 - sigma))
        gradient = jnp.where(valid, geo.three(cot_ref[...].astype(F32)) * slopes, 0.0)
        out_ref.send()
        g_ref[...] = geo.flat(gradient)
        low_ref[...] = geo.flat(gradient).astype(BF16)
        low_ref.send()
        put_back(sums_ref, gradient, (zc - mean) * inv)

    outputs, g_two, g_next, sums, stats_c2 = run(
        head_kernel,
        [((rows, wide), BF16, "hbm"), wide_low, wide_next, stats_wide],
        smem=scalars,
        parts=(parts_c2,),
        vmem=(zc_next,),
        saved=(params_two[2], sum_one, cot),
    )
    parts_c2 = exchange(sums)

    def norm_back(gradient, value, coeffs, sums, valid):
        scale, _, mean, inv = coeffs
        crossed = (value - mean) * inv * sums[0] + sums[1]
        return scale * (gradient - jnp.where(valid, crossed, 0.0))

    def expand_back_body(
        meta_ref,
        inv_ref,
        sums_ref,
        g_ref,
        stats_ref,
        stats_b_ref,
        zc_ref,
        params_ref,
        zb_ref,
        params_b_ref,
        fast_ref,
        loads,
        gz_ref,
        g_out,
        sums_out,
        message_ref,
        edge_ref,
    ):
        limit = meta_ref[0]
        coeffs = affine(stats_ref, params_ref, inv_ref, slow_wide, 0, wide)
        both = [back_rows(sums_ref, inv_ref, slow_wide, row, 0, wide) for row in range(2)]
        gradient = geo.three(g_ref[...])
        gz = norm_back(
            gradient,
            geo.three(zc_ref[...].astype(F32)),
            coeffs,
            both,
            mask_groups(gradient.shape, limit),
        )
        gz = geo.flat(gz).astype(BF16)
        gz_ref[...] = gz
        gz_ref.send()
        fast = dot_nt(gz[:, slow_wide:], fast_ref[...])
        slow = None
        for block in range(blocks):
            term = dot_nt(gz[:, block * mid : (block + 1) * mid], loads.get(block))
            slow = term if slow is None else slow + term
        scale, shift, mean, inv = affine(stats_b_ref, params_b_ref, inv_ref, mid)
        zb = geo.three(zb_ref[...])
        back = geo.three(jnp.concatenate([slow, fast], axis=1)) * slope(zb * scale + shift)
        g_out[...] = geo.flat(back)
        put_message(
            jnp.concatenate([back, zb], axis=-1), message_ref, edge_ref, meta_ref, geo.width
        )
        masked = jnp.where(mask_groups(back.shape, limit), back, 0.0)
        put_back(sums_out, masked, (zb - mean) * inv)
        return gradient

    message_back = [((rows, 2 * small), BF16, "hbm"), ((2 * EDGE, 2 * small), BF16, "hbm")]
    gz_c2, g_b2, sums, message, edges, sums_c2 = run(
        expand_back_body,
        [((rows, wide), BF16, "hbm"), small_next, stats_small, *message_back],
        smem=scalars,
        parts=(parts_c2,),
        vmem=(g_next,),
        saved=(stats_c2, stats_b2, zc_two, params_two[2], zb_two, params_two[1], fast_two[4]),
        weights=((last, at_expand_two, blocks, depth_mid),),
    )
    parts_b2 = exchange(sums)
    halo_back_two = exchange_halo(message, edges)
    align = 16 * lax.axis_size("clips")

    def aligned(number):
        return number + -number % align


    lanes_fast = fast_wide // PHASES
    fast_rows_count = fast_reduce_one.shape[1] + 2 * SUB

    def expand_grad(hb_ref, gz_ref, out_ref, at):
        for block in range(blocks):
            value = dot_tn(hb_ref[:, :mid], gz_ref[:, block * mid : (block + 1) * mid])
            low = at + block * depth_mid
            out_ref[:, low : low + depth_mid, :] = value.astype(BF16).reshape(
                count, depth_mid, mid
            )
        if isinstance(out_ref, Store):
            out_ref.send_rows(at, at + blocks * depth_mid)

    def fast_expand_grad(hb_ref, gz_ref):
        fast = dot_tn(hb_ref[:, mid:], gz_ref[:, slow_wide:])
        total = None
        for phase in range(PHASES):
            part = fast[
                phase * fast_part : (phase + 1) * fast_part,
                phase * lanes_fast : (phase + 1) * lanes_fast,
            ]
            total = part if total is None else total + part
        return total

    def space_grad(ha_ref, taps_ref, out_ref, at):
        fast_grads = []
        for tap in range(9):
            value = dot_tn(ha_ref[:, :mid], taps_ref[tap, :, :mid])
            low = at + tap * depth_mid
            out_ref[:, low : low + depth_mid, :] = value.astype(BF16).reshape(
                count, depth_mid, mid
            )
            fast = dot_tn(ha_ref[:, mid:], taps_ref[tap, :, mid:])
            total = None
            for phase in range(PHASES):
                part = lane_block(
                    fast[phase * fast_part : (phase + 1) * fast_part], phase, fast_part
                )
                total = part if total is None else total + part
            fast_grads.append(total)
        if isinstance(out_ref, Store):
            out_ref.send_rows(at, at + 9 * depth_mid)
        return fast_grads

    def put_fast(reduce, space, expand, out_ref, at):
        lane = lax.broadcasted_iota(jnp.int32, reduce[0].shape, 1)

        def beside(parts):
            keep = lane[: parts[0].shape[0]]
            total = None
            for place, part in enumerate(parts):
                part = jnp.where(keep < fast_part, part, 0.0)
                part = pltpu.roll(part, place * fast_part, 1) if place else part
                total = part if total is None else total + part
            return total

        depth = reduce[0].shape[0] // count
        taps = beside(reduce).astype(BF16).reshape(count, depth, lanes_fast)
        out_ref[:, at : at + depth, :] = jnp.concatenate([taps, jnp.zeros_like(taps)], axis=-1)

        def spread(value):
            tiles = value.reshape(count // 2, SUB, lanes_fast)
            return jnp.stack([tiles, pltpu.roll(tiles, SUB // 2, 1)], axis=1).reshape(
                count, SUB, lanes_fast
            )

        first = jnp.concatenate([spread(beside(space[0:4])), spread(beside(space[4:8]))], axis=-1)
        second = jnp.concatenate([spread(beside(space[8:9])), spread(expand)], axis=-1)
        both = jnp.concatenate([first, second], axis=1).astype(BF16)
        out_ref[:, at + depth : at + depth + 2 * SUB, :] = both
        if isinstance(out_ref, Store):
            out_ref.send_rows(at, at + depth + 2 * SUB)

    def space_back_stage(
        g, zb, za, halo, stats_b, parts_b, params_b, stats_a, params_a, g_hbm, at, fast_w
    ):
        def kernel(
            meta_ref,
            inv_ref,
            sums_b_ref,
            g_ref,
            side_ref,
            up_ref,
            down_ref,
            stats_b_ref,
            stats_a_ref,
            zb_ref,
            za_ref,
            params_b_ref,
            params_a_ref,
            fast_ref,
            loads,
            taps_ref,
            g_out,
            sums_out,
        ):
            limit = meta_ref[0]
            coeffs = affine(stats_b_ref, params_b_ref, inv_ref, mid)
            both = [back_rows(sums_b_ref, inv_ref, mid, row) for row in range(2)]

            def back(gradient, value, valid):
                return norm_back(gradient, value, coeffs, both, valid)

            def halo_back(value, scale):
                value = geo.three(value.astype(F32))
                valid = mask_groups(value[..., :small].shape, limit, scale)
                return back(value[..., :small], value[..., small:], valid)

            def edge_back(value):
                value = geo.three(value.astype(F32))
                shape = value[..., :small].shape
                group = lax.broadcasted_iota(jnp.int32, shape, 0) * SUB % EDGE
                group = group + lax.broadcasted_iota(jnp.int32, shape, 1)
                return geo.flat(back(value[..., :small], value[..., small:], group < limit))

            own, zb = geo.three(g_ref[...]), geo.three(zb_ref[...])
            edges = jnp.concatenate(
                [up_ref[half_rows:], side_ref[...], down_ref[half_rows:]], axis=0
            )

            near_by = Neighbours(
                back(own, zb, mask_groups(own.shape, limit)),
                halo_back(up_ref[:half_rows], 2),
                halo_back(down_ref[:half_rows], 2),
                edge_back(edges),
                meta_ref,
                geo.width,
            )
            slow = fast = None
            for tap in range(9):
                moved = geo.flat(near_by.at(1 - tap // 3, 1 - tap % 3)).astype(BF16)
                taps_ref[tap] = moved
                if tap == 8:
                    taps_ref.send()
                slow_term = dot_nt(moved[:, :mid], loads.get(tap))
                fast_term = dot_nt(moved[:, mid:], fast_ref[tap])
                slow = slow_term if slow is None else slow + slow_term
                fast = fast_term if fast is None else fast + fast_term
            scale, shift, mean, inv = affine(stats_a_ref, params_a_ref, inv_ref, mid)
            za = geo.three(za_ref[...])
            result = geo.three(jnp.concatenate([slow, fast], axis=1)) * slope(za * scale + shift)
            g_out[...] = geo.flat(result)
            masked = jnp.where(mask_groups(result.shape, limit), result, 0.0)
            put_back(sums_out, masked, (za - mean) * inv)

        taps, g, sums, sums_b = run(
            kernel,
            [((9, rows, small), BF16, "hbm"), small_next, stats_small],
            smem=scalars,
            parts=(parts_b,),
            vmem=(g,),
            saved=(*halo, stats_b, stats_a, zb, za, params_b, params_a, fast_w),
            weights=((g_hbm, at, 9, depth_mid),),
        )
        return taps, g, exchange(sums), sums_b

    taps_two, g_a2, parts_a2, sums_b2 = space_back_stage(
        g_b2,
        zb_two,
        za_two,
        halo_back_two,
        stats_b2,
        parts_b2,
        params_two[1],
        stats_a2,
        params_two[0],
        last,
        at_space_two,
        fast_two[3],
    )
    def grads_two_kernel(hb_ref, gz_ref, ha_ref, taps_ref, out_ref, fast_out):
        space = space_grad(ha_ref, taps_ref, out_ref, 0)
        expand_grad(hb_ref, gz_ref, out_ref, 9 * depth_mid)
        for tap in range(9):
            fast_out[tap] = space[tap]
        fast_out[9] = fast_expand_grad(hb_ref, gz_ref)

    rows_space = aligned((9 + blocks) * depth_mid)
    packed_space, fast_space_two = run(
        grads_two_kernel,
        [((count, rows_space, mid), BF16, "rows"), ((10, fast_part, lanes_fast), F32, "hbm")],
        saved=(hb_two, gz_c2, ha_two, taps_two),
    )
    sum_space = lax.psum_scatter(packed_space, TILE, scatter_dimension=0, tiled=False)

    def reduce_gz(meta_ref, inv_ref, g_ref, za_ref, stats_ref, sums_ref, params_ref, steps_ref):
        coeffs = affine(stats_ref, params_ref, inv_ref, mid)
        both = [back_rows(sums_ref, inv_ref, mid, row) for row in range(2)]
        gradient = geo.three(g_ref[...])
        gz = norm_back(
            gradient,
            geo.three(za_ref[...]),
            coeffs,
            both,
            mask_groups(gradient.shape, meta_ref[0]),
        )
        gz = geo.flat(gz)
        steps = [geo.shift(gz, -1).astype(BF16), gz.astype(BF16), geo.shift(gz, 1).astype(BF16)]
        for tap in range(3):
            steps_ref[tap] = steps[tap]
        if isinstance(steps_ref, Store):
            steps_ref.send()
        return steps

    def reduce_back_two_kernel(
        meta_ref,
        inv_ref,
        sums_ref,
        g_ref,
        stats_ref,
        stats_c_ref,
        za_ref,
        params_ref,
        g_two_ref,
        sum_ref,
        zc_ref,
        short_ref,
        main_ref,
        before_ref,
        after_ref,
        loads,
        steps_ref,
        fast_out,
        g_out,
        sums_out,
    ):
        steps = reduce_gz(
            meta_ref, inv_ref, g_ref, za_ref, stats_ref, sums_ref, params_ref, steps_ref
        )
        slow = None
        for tap in range(3):
            term = dot_nt(steps[tap][:, :mid], loads.get(tap))
            slow = term if slow is None else slow + term
        fast = fast_conv_back(
            [step[:, mid:] for step in steps], main_ref[...], before_ref[...], after_ref[...]
        )
        back = jnp.concatenate([slow, fast], axis=1) + g_two_ref[...].astype(F32)
        back = back * slope(sum_ref[...].astype(F32))
        g_out[...] = back
        fast_out[...] = back[:, slow_wide:]
        fast_out.send()
        back = geo.three(back)
        masked = jnp.where(mask_groups(back.shape, meta_ref[0]), back, 0.0)
        mean, inv = moments(stats_c_ref, inv_ref, slow_wide, 0, wide)
        put_back(sums_out, masked, (geo.three(zc_ref[...].astype(F32)) - mean) * inv)
        mean, inv = moments(stats_c_ref, inv_ref, slow_wide, wide, wide + slow_wide)
        masked = masked[..., :slow_wide]
        put_back(sums_out, masked, (geo.three(short_ref[...].astype(F32)) - mean) * inv, wide)

    steps_two, g_one, g_next, sums, sums_a2 = run(
        reduce_back_two_kernel,
        [
            ((3, rows, small), BF16, "hbm"),
            ((rows, fast_wide), F32, "hbm"),
            wide_next,
            stats_both,
        ],
        smem=scalars,
        parts=(parts_a2,),
        vmem=(g_a2,),
        saved=(stats_a2, stats_c1, za_two, params_two[0], g_two, sum_one, zc_one, short, *fast_two[:3]),
        weights=((far, at_reduce_two, 3, depth_two),),
    )
    parts_c1 = exchange_widest(sums)

    def expand_back_one_kernel(*refs):
        *body, short_ref, short_params_ref, loads, gz_ref, g_out, sums_out, message, edge, gs_ref = (
            refs
        )
        gradient = expand_back_body(*body, loads, gz_ref, g_out, sums_out, message, edge)
        meta_ref, inv_ref, sums_ref, _, stats_ref = body[:5]
        low, high = wide, wide + slow_wide
        coeffs = affine(stats_ref, short_params_ref, inv_ref, slow_wide, low, high)
        both = [back_rows(sums_ref, inv_ref, slow_wide, row, low, high) for row in range(2)]
        gradient = gradient[..., :slow_wide]
        valid = mask_groups(gradient.shape, meta_ref[0])
        gs = norm_back(gradient, geo.three(short_ref[...].astype(F32)), coeffs, both, valid)
        gs_ref[...] = geo.flat(gs).astype(BF16)

    gz_c1, g_b1, sums, message, edges, gz_short, sums_c1 = run(
        expand_back_one_kernel,
        [((rows, wide), BF16, "hbm"), small_next, stats_small, *message_back]
        + [((rows, slow_wide), BF16, "hbm")],
        smem=scalars,
        parts=(parts_c1,),
        vmem=(g_next,),
        saved=(stats_c1, stats_b1, zc_one, params_one[2], zb_one, params_one[1], fast_one[4])
        + (short, params_short),
        weights=((far, 0, blocks, depth_mid),),
    )
    parts_b1 = exchange(sums)
    halo_back_one = exchange_halo(message, edges)
    joined_lanes = slow_wide + lat

    def grads_mid_kernel(
        x_ref,
        united_ref,
        gs_ref,
        hb_ref,
        gz_ref,
        low_ref,
        steps_ref,
        fast_ref,
        loads,
        out_ref,
        back_ref,
    ):
        for tap in range(3):
            value = dot_tn(low_ref[:, :slow_wide], steps_ref[tap, :, :mid])
            out_ref[:, tap * depth_two : (tap + 1) * depth_two, :] = value.astype(BF16).reshape(
                count, depth_two, mid
            )
        at = 3 * depth_two
        out_ref.send_rows(0, at)
        reduce = fast_reduce_grad(
            low_ref[:, slow_wide:], [steps_ref[tap, :, mid:] for tap in range(3)]
        )
        put_fast(reduce, [fast_ref[tap] for tap in range(9)], fast_ref[9], out_ref, at)
        at += fast_rows_count
        expand_grad(hb_ref, gz_ref, out_ref, at + blocks * depth_one)
        for block in range(blocks):
            gs = gs_ref[:, block * mid : (block + 1) * mid]
            value = jnp.concatenate([dot_tn(x_ref[...], gs), dot_tn(united_ref[...], gs)], axis=0)
            low = at + block * depth_one
            out_ref[:, low : low + depth_one, :] = value.astype(BF16).reshape(
                count, depth_one, mid
            )
            out_ref.send_rows(low, low + depth_one)
        for block in range(blocks):
            gs = gs_ref[:, block * mid : (block + 1) * mid]
            term = dot_nt(gs, loads.get(block))
            back_ref[...] = term if block == 0 else back_ref[...] + term

    rows_mid = aligned(3 * depth_two + fast_rows_count + blocks * (depth_one + depth_mid))
    packed_mid, short_back = run(
        grads_mid_kernel,
        [((count, rows_mid, mid), BF16, "rows"), ((rows, joined_lanes), F32, "hbm")],
        saved=(slow_x, united, gz_short, hb_one, gz_c1, low_one, steps_two, fast_space_two),
        weights=((far, at_short, blocks, depth_one),),
    )
    sum_mid = lax.psum_scatter(packed_mid, TILE, scatter_dimension=0, tiled=False)

    taps_one, g_a1, parts_a1, sums_b1 = space_back_stage(
        g_b1,
        zb_one,
        za_one,
        halo_back_one,
        stats_b1,
        parts_b1,
        params_one[1],
        stats_a1,
        params_one[0],
        near,
        at_space_one,
        fast_one[3],
    )
    def last_kernel(
        meta_ref,
        inv_ref,
        sums_ref,
        g_ref,
        stats_ref,
        za_ref,
        params_ref,
        g_one_ref,
        short_ref,
        lateral_ref,
        main_ref,
        before_ref,
        after_ref,
        loads,
        steps_ref,
        slow_ref,
        fast_ref,
        united_ref,
    ):
        steps = reduce_gz(
            meta_ref, inv_ref, g_ref, za_ref, stats_ref, sums_ref, params_ref, steps_ref
        )
        joined = short_ref[...]
        for tap in range(3):
            joined = joined + dot_nt(steps[tap][:, :mid], loads.get(tap))
        slow_ref[...] = joined[:, :slow_wide]
        tail = joined[:, slow_wide:]
        now, past = tail.astype(BF16), geo.shift(tail, -1).astype(BF16)
        united_ref[0] = now
        united_ref[1] = past
        lanes = fast_wide // PHASES
        fast = fast_conv_back(
            [step[:, mid:] for step in steps], main_ref[...], before_ref[...], after_ref[...]
        )
        fast = fast + g_one_ref[...]
        front = dot_nt(now, lateral_ref[2:5].reshape(3 * lanes, lat))
        back = dot_nt(past, lateral_ref[0:2].reshape(2 * lanes, lat))
        fast_ref[:, : 2 * lanes] = fast[:, : 2 * lanes] + front[:, : 2 * lanes]
        fast_ref[:, 2 * lanes : 3 * lanes] = (
            fast[:, 2 * lanes : 3 * lanes] + front[:, 2 * lanes :] + back[:, :lanes]
        )
        fast_ref[:, 3 * lanes :] = fast[:, 3 * lanes :] + back[:, lanes:]

    steps_one, grad_slow, grad_fast, united_low, sums_a1 = run(
        last_kernel,
        [
            ((3, rows, small), BF16, "hbm"),
            ((rows, slow_wide), F32, "hbm"),
            ((rows, fast_wide), F32, "hbm"),
            ((2, rows, lat), BF16, "hbm"),
        ],
        smem=scalars,
        parts=(parts_a1,),
        vmem=(g_a1,),
        saved=(stats_a1, za_one, params_one[0], g_one, short_back, lateral, *fast_one[:3]),
        weights=((near, 0, 3, depth_one),),
    )

    def grads_one_kernel(
        meta_ref,
        steps_ref,
        low_ref,
        x_ref,
        united_ref,
        fast_x_ref,
        ha_ref,
        taps_ref,
        hb_ref,
        gz_ref,
        own_ref,
        send_ref,
        out_ref,
        sems,
    ):
        lanes = fast_wide // PHASES
        for tap in range(3):
            step = steps_ref[tap, :, :mid]
            value = jnp.concatenate(
                [dot_tn(x_ref[...], step), dot_tn(united_ref[...], step)], axis=0
            )
            out_ref[:, tap * depth_one : (tap + 1) * depth_one, :] = value.astype(BF16).reshape(
                count, depth_one, mid
            )
        at = 3 * depth_one
        place = (own_ref, send_ref, meta_ref[1], meta_ref[2], sems)
        put_blocks(out_ref, 0, at, *place, 0)
        past = dot_tn(fast_x_ref[:, 2 * lanes :], low_ref[1])
        now = dot_tn(fast_x_ref[:, : 3 * lanes], low_ref[0])
        both = jnp.concatenate([past, now], axis=0).astype(BF16)
        for tap in range(5):
            out_ref[:, at + tap * depth_lat : at + (tap + 1) * depth_lat, :] = both[
                tap * lanes : (tap + 1) * lanes
            ].reshape(count, depth_lat, lat)
        at += 5 * depth_lat
        space = space_grad(ha_ref, taps_ref, out_ref, at)
        at += 9 * depth_mid
        reduce = fast_reduce_grad(
            fast_x_ref[...], [steps_ref[tap, :, mid:] for tap in range(3)]
        )
        put_fast(reduce, space, fast_expand_grad(hb_ref, gz_ref), out_ref, at)

        put_blocks(out_ref, 3 * depth_one, rows_late, *place, 1)
        for low, top, turn in ((0, 3 * depth_one, 0), (3 * depth_one, rows_late, 1)):
            rows_part = pl.ds(low, top - low)
            for block in range(count):
                source, target = out_ref.at[block, rows_part, :], own_ref.at[0, rows_part, :]
                pltpu.make_async_copy(source, target, sems.at[turn, block]).wait()

    def put_blocks(blocks_ref, low, top, own_ref, send_ref, ha, wa, sems, turn):
        rows_part = pl.ds(low, top - low)
        for block in range(count):
            place, col = ha ^ (block // 2), block % 2
            source, sem = blocks_ref.at[block, rows_part, :], sems.at[turn, block]

            @pl.when(wa == col)
            def _():
                pltpu.make_async_copy(source, own_ref.at[place, rows_part, :], sem).start()

            @pl.when(wa != col)
            def _():
                pltpu.make_async_copy(source, send_ref.at[place, rows_part, :], sem).start()

    high = count // 2
    rows_one = 3 * depth_one + 5 * depth_lat + 9 * depth_mid + fast_rows_count
    rows_late = aligned(rows_one)
    blocks_out = ((high, rows_late, mid), BF16, "raw")
    own_blocks, send_blocks = run(
        grads_one_kernel,
        [blocks_out, blocks_out],
        smem=(meta,),
        saved=(steps_one, united_low, slow_x, united, fast_x, ha_one, taps_one, hb_one, gz_c1),
        scratch=(
            pltpu.VMEM((count, rows_late, mid), BF16),
            pltpu.SemaphoreType.DMA((2, count)),
        ),
    )
    side_blocks = lax.ppermute(send_blocks, "wa", xor_pairs(2, 1))

    def chip_kernel(own_ref, side_ref, *out_refs):
        for place in range(high):
            total = own_ref[place].astype(F32) + side_ref[place].astype(F32)
            out_refs[place][...] = total.astype(BF16)
            out_refs[place].send()

    late_out = ((rows_late, mid), BF16, "hbm")
    chip_sums = run(chip_kernel, [late_out] * high, saved=(own_blocks, side_blocks))
    late = [chip_sums[0]] + to_partners(chip_sums[1:], "ha")
    four = lax.axis_size("clips") == 4
    sum_space, sum_mid, _ = lax.optimization_barrier((sum_space, sum_mid, chip_sums[0]))
    halves = clip_parts(meta, [[sum_space], [sum_mid]], 2 if four else 1)
    if four:
        half = halves_first(*halves)
        late, half = lax.optimization_barrier((late, half))
        total_early = halves_second(half)
        parts_early = halves_share(total_early)
    else:
        parts_early = [lax.psum(halves[0], "clips")]
    quarters = clip_parts(meta, [late], 4 if four else 1)
    if four:
        total_late = add_low(quarters[0], *to_partners(quarters[1:], "clips"))
        parts_late = [total_late] + to_partners([total_late] * 3, "clips")
    else:
        parts_late = [lax.psum(quarters[0], "clips")]

    def finish(*jobs):
        outs_all = []
        for _, groups, _ in jobs:
            for _, shapes in groups:
                for shape in shapes:
                    outs_all += list(shape) if isinstance(shape[0], tuple) else [shape]
        number = sum(len(parts) for parts, _, _ in jobs)
        deepest = max(sum(rows_group for rows_group, _ in groups) for _, groups, _ in jobs)

        def kernel(meta_ref, *refs):
            ins, outs, total_ref = list(refs[:number]), list(refs[number:-1]), refs[-1]
            for parts, groups, by_halves in jobs:
                mine, ins = ins[: len(parts)], ins[len(parts) :]
                one_job(meta_ref, mine, outs, total_ref, groups, by_halves)

        def one_job(meta_ref, ins, outs, total_ref, groups, by_halves):
            size = len(ins)
            depth = sum(rows_group for rows_group, _ in groups) // size
            base = 0
            for step, ref in enumerate(ins):
                clip = meta_ref[4] ^ step
                place = clip % 2 * 2 + clip // 2 if by_halves else clip
                start = pl.multiple_of(place * depth, 16) if size > 1 else 0
                total_ref[pl.ds(start, depth), :] = ref[...].astype(F32)
            for rows_group, shapes in groups:
                at = base
                for shape in shapes:
                    if isinstance(shape[0], tuple):
                        reduce, space, expand = outs.pop(0), outs.pop(0), outs.pop(0)
                        rows_tap, lanes = reduce.shape[1:]
                        for tap in range(3):
                            reduce[tap] = total_ref[
                                at : at + rows_tap, tap * lanes : (tap + 1) * lanes
                            ]
                        few = space.shape[2]
                        for tap in range(9):
                            row = at + rows_tap + tap // SUB * SUB
                            lane = tap % SUB * lanes
                            space[tap // 3, tap % 3] = total_ref[
                                row : row + few, lane : lane + lanes
                            ]
                        row = at + rows_tap + SUB
                        expand[...] = total_ref[row : row + few, expand.shape[1] :]
                        for out in (reduce, space, expand):
                            out.send()
                        at += rows_tap + 2 * SUB
                        continue
                    out = outs.pop(0)
                    if len(shape) == 2 and shape[1] > mid:
                        for block in range(shape[1] // mid):
                            out[:, block * mid : (block + 1) * mid] = total_ref[
                                at : at + shape[0], :
                            ]
                            at += shape[0]
                    else:
                        number = 1
                        for length in shape[:-1]:
                            number *= length
                        out[...] = total_ref[at : at + number, :].reshape(shape)
                        at += number
                    out.send()
                base += rows_group

        return run(
            kernel,
            [(shape, F32, "hbm") for shape in outs_all],
            smem=(meta,),
            saved=[part for parts, _, _ in jobs for part in parts],
            scratch=(pltpu.VMEM((deepest, mid), F32),),
        )

    shapes_one = tuple(shard.shape for shard in fast_shards_one)
    shapes_two = tuple(shard.shape for shard in fast_shards_two)
    groups_early = [
        (rows_space, [slow_spatial_two.shape, slow_expand_two.shape]),
        (
            rows_mid,
            [slow_reduce_two.shape, shapes_two, slow_shortcut_one.shape, slow_expand_one.shape],
        ),
    ]
    groups_late = [
        (
            rows_late,
            [slow_reduce_one.shape, lateral_weight.shape, slow_spatial_one.shape, shapes_one],
        )
    ]
    finished = finish((parts_early, groups_early, True), (parts_late, groups_late, False))
    grad_slow_spatial_two, grad_slow_expand_two, grad_slow_reduce_two = finished[:3]
    fast_two_grads, (grad_slow_shortcut, grad_slow_expand_one) = finished[3:6], finished[6:8]
    grad_slow_reduce_one, grad_lateral, grad_slow_spatial_one, *fast_one_grads = finished[8:]

    def norm_grads(first, second, third):
        slow = [first[:, :mid], second[:, :mid], third[:, :slow_wide]]
        fast = [first[:, mid:], second[:, mid:], third[:, slow_wide:wide]]
        fast = [jnp.sum(part.reshape(2, PHASES, -1), axis=1) for part in fast]
        return slow, fast

    slow_one_p, fast_one_p = norm_grads(sums_a1, sums_b1, sums_c1)
    slow_two_p, fast_two_p = norm_grads(sums_a2, sums_b2, sums_c2)
    grad_slow_norms_one = jnp.concatenate(slow_one_p + [sums_c1[:, wide:]], axis=1)
    grad_slow_norms_two = jnp.concatenate(slow_two_p, axis=1)
    grad_fast_norms_one = jnp.concatenate(fast_one_p, axis=1)
    grad_fast_norms_two = jnp.concatenate(fast_two_p, axis=1)
    return (
        outputs[:, :slow_wide].reshape(slow_input.shape),
        join_phases(outputs[:, slow_wide:], fast_input.shape),
        grad_slow.reshape(slow_input.shape),
        join_phases(grad_fast, fast_input.shape),
        grad_lateral,
        grad_slow_reduce_one,
        grad_slow_spatial_one,
        grad_slow_expand_one,
        grad_slow_shortcut,
        *fast_one_grads,
        grad_slow_reduce_two,
        grad_slow_spatial_two,
        grad_slow_expand_two,
        *fast_two_grads,
        grad_slow_norms_one,
        grad_fast_norms_one,
        grad_slow_norms_two,
        grad_fast_norms_two,
    )


def solution(mesh):
    in_specs = (
        P("clips", None, "ha", "wa", None),
        P("clips", None, "ha", "wa", None),
        P("clips", None, "ha", "wa", None),
        P("clips", None, "ha", "wa", None),
        P("clips"),
        P(None, ("ha", "wa"), None),
        P(None, ("ha", "wa"), None),
        P(None, None, ("ha", "wa"), None),
        P(("ha", "wa"), None),
        P(("ha", "wa"), None),
        P(None, ("ha", "wa"), None),
        P(None, None, ("ha", "wa"), None),
        P(("ha", "wa"), None),
        P(None, ("ha", "wa"), None),
        P(None, None, ("ha", "wa"), None),
        P(("ha", "wa"), None),
        P(None, ("ha", "wa"), None),
        P(None, None, ("ha", "wa"), None),
        P(("ha", "wa"), None),
        P(),
        P(),
        P(),
        P(),
    )
    out_specs = (
        P("clips", None, "ha", "wa", None),
        P("clips", None, "ha", "wa", None),
        P("clips", None, "ha", "wa", None),
        P("clips", None, "ha", "wa", None),
        P(None, ("ha", "wa"), None),
        P(None, ("ha", "wa"), None),
        P(None, None, ("ha", "wa"), None),
        P(("ha", "wa"), None),
        P(("ha", "wa"), None),
        P(None, ("ha", "wa"), None),
        P(None, None, ("ha", "wa"), None),
        P(("ha", "wa"), None),
        P(None, ("ha", "wa"), None),
        P(None, None, ("ha", "wa"), None),
        P(("ha", "wa"), None),
        P(None, ("ha", "wa"), None),
        P(None, None, ("ha", "wa"), None),
        P(("ha", "wa"), None),
        P(),
        P(),
        P(),
        P(),
    )
    return jax.shard_map(
        on_device, mesh=mesh, in_specs=in_specs, out_specs=out_specs, check_vma=False
    )
```

```python
import jax
import jax.numpy as jnp
from jax import lax
from jax.experimental import pallas as pl
from jax.experimental.pallas import tpu as pltpu
from jax.sharding import PartitionSpec as P

epsilon = 1e-05
F32 = jnp.float32
BF16 = jnp.bfloat16
TILE = ("ha", "wa")
PHASES = 4
SUB = 8


def dot(left, right):
    return lax.dot_general(left, right, (((1,), (0,)), ((), ())), preferred_element_type=F32)


def dot_tn(left, right):
    return lax.dot_general(left, right, (((0,), (0,)), ((), ())), preferred_element_type=F32)


def dot_nt(left, right):
    return lax.dot_general(left, right, (((1,), (1,)), ((), ())), preferred_element_type=F32)


class Keep:
    def __init__(self, ref):
        self.scratch, self.shape = ref, ref.shape

    def send(self):
        pass

    def __setitem__(self, index, value):
        self.scratch[index] = value

    def __getitem__(self, index):
        return self.scratch[index]


class Loads:
    def __init__(self, source, offset, target, sems, first):
        self.copies = []
        depth = target.shape[2]
        for step in range(target.shape[0]):
            copy = pltpu.make_async_copy(
                source.at[:, pl.ds(offset + step * depth, depth), :],
                target.at[step],
                sems.at[first + step],
            )
            copy.start()
            self.copies.append(copy)
        self.target = target

    def get(self, step):
        self.copies[step].wait()
        block = self.target[step]
        return block.reshape(-1, block.shape[-1])


class Saved:
    def __init__(self, source, scratch, sem):
        self.scratch, self.shape = scratch, scratch.shape
        self.copy = pltpu.make_async_copy(source, scratch, sem)
        self.copy.start()
        self.ready = False

    def wait(self):
        if not self.ready:
            self.copy.wait()
            self.ready = True

    def __getitem__(self, index):
        self.wait()
        return self.scratch[index]


SEGMENTS = 8


class Store:
    def __init__(self, scratch, target, sems):
        self.scratch, self.target, self.shape = scratch, target, scratch.shape
        self.sems, self.copies = sems, []

    def send(self):
        self.copies.append(pltpu.make_async_copy(self.scratch, self.target, self.sems[0]))
        self.copies[-1].start()

    def send_rows(self, low, high):
        rows = pl.ds(low, high - low)
        source, target = self.scratch.at[:, rows, :], self.target.at[:, rows, :]
        self.copies.append(pltpu.make_async_copy(source, target, self.sems[len(self.copies)]))
        self.copies[-1].start()

    def __setitem__(self, index, value):
        self.scratch[index] = value

    def __getitem__(self, index):
        return self.scratch[index]


CLOSE = 320 * 1024


def run(body, outs, smem=(), parts=(), vmem=(), saved=(), weights=(), scratch=(), limit=53):
    near = pl.BlockSpec(memory_space=pltpu.VMEM)
    far = pl.BlockSpec(memory_space=pltpu.HBM)
    sources = []
    for array, *_ in weights:
        if not any(array is other for other in sources):
            sources.append(array)
    outs = list(outs) + [(part.shape[1:], part.dtype, "hbm") for part in parts]
    flat = []
    twice = []
    for at, (shape, dtype, kind) in enumerate(outs):
        size = jnp.dtype(dtype).itemsize
        for length in shape:
            size *= length
        twice.append(kind == "both" and size <= CLOSE)
        if kind in ("hbm", "both") and size <= CLOSE:
            outs[at] = (shape, dtype, "vmem")
    for shape, dtype, kind in outs:
        flat += [(shape, dtype, "raw"), (shape, dtype, "vmem")] if kind == "both" else [(shape, dtype, kind)]
    close = [array.size * array.dtype.itemsize <= CLOSE for array in saved]
    held = [pltpu.VMEM(array.shape, array.dtype) for array, here in zip(saved, close) if not here]
    for array, _, steps, depth in weights:
        held.append(pltpu.VMEM((steps, array.shape[0], depth, array.shape[2]), array.dtype))
    for shape, dtype, kind in outs:
        if kind in ("hbm", "rows"):
            held.append(pltpu.VMEM(shape, dtype))
        elif kind == "spread":
            held.append(pltpu.VMEM(shape[1:], dtype))
    sems = len(saved) + sum(steps for _, _, steps, _ in weights) + len(outs)
    sems += SEGMENTS * sum(kind == "rows" for _, _, kind in outs)
    held.append(pltpu.SemaphoreType.DMA((sems,)))

    def kernel(*refs):
        refs = list(refs)

        def take(number):
            taken = refs[:number]
            del refs[:number]
            return taken

        smem_refs, part_refs, vmem_refs = take(len(smem)), take(len(parts)), take(len(vmem))
        saved_refs, source_refs, out_refs = take(len(saved)), take(len(sources)), take(len(flat))
        saved_scratch, weight_scratch = take(len(saved) - sum(close)), take(len(weights))
        out_scratch = take(sum(kind in ("hbm", "rows", "spread") for _, _, kind in outs))
        sem, more = refs[0], refs[1:]
        arrays, copies = [], []
        for source, here in zip(saved_refs, close):
            if not here:
                copies.append(Saved(source, saved_scratch[len(copies)], sem.at[len(copies)]))
            arrays.append(source if here else copies[-1])
        at = len(saved)
        loads = []
        for (array, offset, steps, _), target in zip(weights, weight_scratch):
            place = [array is other for other in sources].index(True)
            loads.append(Loads(source_refs[place], offset, target, sem, at))
            at += steps
        results, stores, spreads = [], [], []
        for _, _, kind in outs:
            ref = out_refs.pop(0)
            if kind == "both":
                stores.append(Store(out_refs.pop(0), ref, [sem.at[at]]))
                at += 1
                results.append(stores[-1])
            elif kind in ("hbm", "rows"):
                number = SEGMENTS if kind == "rows" else 1
                stores.append(
                    Store(out_scratch.pop(0), ref, [sem.at[at + part] for part in range(number)])
                )
                at += number
                results.append(stores[-1])
            elif kind == "spread":
                spreads.append((out_scratch.pop(0), ref))
                results.append(spreads[-1][0])
            elif kind == "vmem":
                results.append(Keep(ref))
            else:
                results.append(ref)
        sums = results[len(results) - len(parts) :]
        results = results[: len(results) - len(parts)]
        for part, total in zip(part_refs, sums):
            total[...] = jnp.sum(part[...], axis=0)
            total.send()
        totals = [total.scratch for total in sums]
        body(*smem_refs, *totals, *vmem_refs, *arrays, *loads, *results, *more)
        for copy in copies:
            copy.wait()
        for store in stores:
            if not store.copies:
                store.send()
        for value, ref in spreads:
            ref[...] = jnp.broadcast_to(value[...][None], ref.shape)
        for store in stores:
            for copy in store.copies:
                copy.wait()

    results = pl.pallas_call(
        kernel,
        out_shape=[jax.ShapeDtypeStruct(shape, dtype) for shape, dtype, _ in flat],
        in_specs=[pl.BlockSpec(memory_space=pltpu.SMEM)] * len(smem)
        + [near] * (len(parts) + len(vmem))
        + [near if here else far for here in close]
        + [far] * len(sources),
        out_specs=[far if kind in ("hbm", "rows", "raw") else near for _, _, kind in flat],
        scratch_shapes=held + list(scratch),
        compiler_params=pltpu.CompilerParams(vmem_limit_bytes=limit * 1024 * 1024),
        cost_estimate=pl.CostEstimate(
            flops=2_000_000_000, bytes_accessed=16_000_000, transcendentals=0
        ),
    )(*smem, *parts, *vmem, *saved, *sources)
    returned = []
    for (_, _, kind), double in zip(outs, twice):
        taken, results = results[: 2 if kind == "both" else 1], results[2 if kind == "both" else 1 :]
        returned += list(taken) * (2 if double else 1)
    return returned


class Geometry:
    def __init__(self, slow_shape, fast_shape):
        self.cap, self.frames, self.height, self.width = slow_shape[:4]
        self.groups = self.cap * self.frames
        self.rows = self.groups * SUB

    def three(self, value):
        return value.reshape(-1, SUB, value.shape[-1])

    def flat(self, value):
        return value.reshape(-1, value.shape[-1])

    def shift(self, value, step):
        lanes = value.shape[-1]
        whole = value.reshape(self.cap, self.frames, SUB, lanes)
        zero = jnp.zeros((self.cap, 1, SUB, lanes), value.dtype)
        if step > 0:
            whole = jnp.concatenate([zero, whole[:, :-1]], axis=1)
        else:
            whole = jnp.concatenate([whole[:, 1:], zero], axis=1)
        return whole.reshape(-1, lanes)


def mask_groups(shape, limit, scale=1):
    return lax.broadcasted_iota(jnp.int32, shape, 0) * scale < limit


def rep(ref, row, low, high):
    return jnp.broadcast_to(ref[row : row + 1, low:high], (SUB, high - low))


def fold(value, slow):
    fast = value[:, slow:]
    lanes = fast.shape[-1]
    part = lanes // PHASES
    if part % 128 == 0:
        total = fast[:, :part]
        for phase in range(1, PHASES):
            total = total + fast[:, phase * part : (phase + 1) * part]
        return jnp.concatenate([value[:, :slow]] + [total] * PHASES, axis=1)
    total = fast
    for phase in range(1, PHASES):
        total = total + pltpu.roll(fast, phase * part, 1)
    return jnp.concatenate([value[:, :slow], total], axis=1)


def lane_counts(inv_ref, lanes, slow):
    lane = lax.broadcasted_iota(jnp.int32, (SUB, lanes), 1)
    return jnp.where(lane < slow, inv_ref[0], inv_ref[1])


def moments(stats, inv_ref, slow, low=0, high=None):
    high = stats.shape[1] if high is None else high
    total, square = rep(stats, 0, low, high), rep(stats, 1, low, high)
    if slow < high - low:
        total, square = fold(total, slow), fold(square, slow)
    inv_n = lane_counts(inv_ref, high - low, slow)
    mean = total * inv_n
    return mean, lax.rsqrt(square * inv_n - mean * mean + epsilon)


def affine(stats, params, inv_ref, slow, low=0, high=None):
    mean, inv = moments(stats, inv_ref, slow, low, high)
    lanes = mean.shape[1]
    scale = (1.0 + rep(params, 0, 0, lanes)) * inv
    return scale, rep(params, 1, 0, lanes) - mean * scale, mean, inv


def back_rows(sums, inv_ref, slow, row, low=0, high=None):
    high = sums.shape[1] if high is None else high
    total = rep(sums, row, low, high)
    if slow < high - low:
        total = fold(total, slow)
    return total * lane_counts(inv_ref, high - low, slow)


def silu(value):
    return value * jax.nn.sigmoid(value)


def slope(value):
    sigma = jax.nn.sigmoid(value)
    return sigma * (1.0 + value * (1.0 - sigma))


def put_stats(ref, first, second, low=0):
    lanes = first.shape[-1]
    ref[0:1, low : low + lanes] = jnp.sum(jnp.sum(first, axis=0), axis=0, keepdims=True)
    ref[1:2, low : low + lanes] = jnp.sum(jnp.sum(second, axis=0), axis=0, keepdims=True)


def put_back(ref, gradient, normal, low=0):
    put_stats(ref, gradient * normal, gradient, low)


def put_forward(ref, value, limit, low=0):
    masked = jnp.where(mask_groups(value.shape, limit), value, 0.0)
    put_stats(ref, masked, masked * value, low)


EDGE = 32


def edge_place(wa, width):
    return jnp.where(wa > 0, 0, width - 1)


def put_message(value, ref, edge_ref, meta_ref, width):
    lanes = value.shape[-1]
    pairs = value.reshape(-1, 2, SUB, lanes)
    first, second = pairs[:, 0], pairs[:, 1]
    near = lax.broadcasted_iota(jnp.int32, first.shape, 1) < SUB // 2
    top = jnp.where(near, first, pltpu.roll(second, SUB // 2, 1))
    bottom = jnp.where(near, pltpu.roll(first, SUB // 2, 1), second)
    flat = value.reshape(-1, lanes).astype(BF16)
    shape = (2 * EDGE, flat.shape[0])
    row, col = [lax.broadcasted_iota(jnp.int32, shape, dim) for dim in range(2)]
    low = row >= EDGE
    source = (row - jnp.where(low, EDGE, 0)) * SUB + jnp.where(low, SUB // 2, 0)
    chosen = (col == source + edge_place(meta_ref[2], width)).astype(F32).astype(BF16)
    edges = dot(chosen, flat)
    edge_ref[...] = edges.astype(BF16)
    edge_ref.send()
    top, bottom = [part.reshape(-1, lanes).astype(BF16) for part in (top, bottom)]
    ref[: top.shape[0]] = top
    ref[top.shape[0] :] = bottom
    ref.send()


def unpack_bottom(value):
    both = jnp.stack([pltpu.roll(value, SUB // 2, 1), value], axis=1)
    return both.reshape(-1, SUB, value.shape[-1])


def unpack_top(value):
    both = jnp.stack([value, pltpu.roll(value, SUB // 2, 1)], axis=1)
    return both.reshape(-1, SUB, value.shape[-1])


class Neighbours:
    def __init__(self, own, up, down, edges, meta, width):
        half = SUB // 2
        near = lax.broadcasted_iota(jnp.int32, own.shape, 1) < half
        self.col = lax.broadcasted_iota(jnp.int32, own.shape, 1) % width
        self.width, self.shape = width, own.shape
        ha, wa, last = meta[1], meta[2], meta[3]
        up = unpack_bottom(jnp.where(ha > 0, up, 0.0))
        down = unpack_top(jnp.where(ha < last, down, 0.0))
        self.rows = {
            0: own,
            -1: pltpu.roll(jnp.where(near, own, up), half, 1),
            1: pltpu.roll(jnp.where(near, down, own), half, 1),
        }
        beyond = lax.broadcasted_iota(jnp.int32, edges.shape, 0)
        inside = ((ha > 0) | (beyond >= EDGE)) & ((ha < last) | (beyond < 3 * EDGE))
        self.edges = jnp.where(inside, edges, 0.0).astype(BF16)
        shape = (own.shape[0] * SUB, edges.shape[0])
        place, self.source = [lax.broadcasted_iota(jnp.int32, shape, dim) for dim in range(2)]
        self.group = place // SUB
        self.row = place // half % 2
        self.touches = place % width == edge_place(wa, width)
        self.sides = {}

    def side(self, row_step):
        if row_step not in self.sides:
            wanted = (self.row + row_step + 1) * EDGE + self.group
            chosen = ((self.source == wanted) & self.touches).astype(F32).astype(BF16)
            self.sides[row_step] = dot(chosen, self.edges).reshape(self.shape)
        return self.sides[row_step]

    def at(self, row_step, col_step):
        base = self.rows[row_step]
        if col_step < 0:
            return jnp.where(self.col == 0, self.side(row_step), pltpu.roll(base, 1, 1))
        if col_step > 0:
            away = self.col == self.width - 1
            return jnp.where(away, self.side(row_step), pltpu.roll(base, SUB - 1, 1))
        return base


def xor_pairs(size, step):
    return [(index, index ^ step) for index in range(size)]


def direct_sum(value, axis):
    size = lax.axis_size(axis)
    step = 1
    while step < size:
        if size // step >= 4:
            one, two, three = [
                lax.ppermute(value, axis, xor_pairs(size, step * times)) for times in (1, 2, 3)
            ]
            value = (value + two) + (one + three)
            step *= 4
        else:
            value = value + lax.ppermute(value, axis, xor_pairs(size, step))
            step *= 2
    return value


AXES = ("clips", "ha", "wa")
MOST = 32


def spread_count():
    count = lax.axis_size("ha") * lax.axis_size("wa")
    whole = count * lax.axis_size("clips")
    return whole if whole <= MOST else count


def exchange(copies):
    if copies.shape[0] == lax.axis_size("clips") * lax.axis_size("ha") * lax.axis_size("wa"):
        return lax.all_to_all(copies, AXES, 0, 0)
    return lax.all_to_all(direct_sum(copies, "clips"), TILE, 0, 0)


def exchange_widest(sums):
    count = lax.axis_size("ha") * lax.axis_size("wa")
    sums = direct_sum(sums, "clips")
    return lax.all_to_all(jnp.broadcast_to(sums[None], (count,) + sums.shape), TILE, 0, 0)


def exchange_halo(message, edges):
    wide, high = lax.axis_size("wa"), lax.axis_size("ha")
    half = message.shape[0] // 2
    side = lax.ppermute(edges, "wa", xor_pairs(wide, 1))
    tops = jnp.concatenate([message[:half], side[:EDGE]], axis=0)
    bottoms = jnp.concatenate([message[half:], side[EDGE:]], axis=0)
    up = lax.ppermute(bottoms, "ha", [(row, row + 1) for row in range(high - 1)])
    down = lax.ppermute(tops, "ha", [(row + 1, row) for row in range(high - 1)])
    return side, up, down


def time_conv(geo, parts, blocks):
    result = None
    for tap in range(3):
        at = 0
        total = None
        for part in parts:
            lanes = part.shape[-1]
            term = dot(part, blocks[tap][at : at + lanes])
            at += lanes
            total = term if total is None else total + term
        if tap != 1:
            total = geo.shift(total, 1 - tap)
        result = total if result is None else result + total
    return result


def fast_conv(geo, value, main, before, after):
    lanes = value.shape[-1] // PHASES
    result = dot(value, main)
    result = result + geo.shift(dot(value[:, -lanes:], before), 1)
    return result + geo.shift(dot(value[:, :lanes], after), -1)


def fast_conv_back(steps, main, before, after):
    lanes = before.shape[0]
    middle = dot_nt(steps[1], main)
    first = middle[:, :lanes] + dot_nt(steps[2], after)
    last = middle[:, -lanes:] + dot_nt(steps[0], before)
    return jnp.concatenate([first, middle[:, lanes:-lanes], last], axis=1)


def lane_block(value, phase, part):
    return pltpu.roll(value, value.shape[-1] - phase * part, 1) if phase else value


def fast_reduce_grad(value, steps):
    lanes = value.shape[-1] // PHASES
    part = steps[1].shape[-1] // PHASES
    main = dot_tn(value, steps[1])
    before = dot_tn(value[:, -lanes:], steps[0])
    after = dot_tn(value[:, :lanes], steps[2])

    def block(row, col):
        return lane_block(main[row * lanes : (row + 1) * lanes], col, part)

    result = []
    for tap in range(3):
        total = before if tap == 0 else None
        if tap == 2:
            total = lane_block(after, PHASES - 1, part)
        for col in range(PHASES):
            row = col + tap - 1
            if 0 <= row < PHASES:
                total = block(row, col) if total is None else total + block(row, col)
        result.append(total)
    return result


def gather_pack(parts):
    return lax.all_gather(jnp.concatenate(parts, axis=0), TILE, axis=0)


def columns(shard, lanes):
    depth, total = shard.shape
    return jnp.moveaxis(shard.reshape(depth, total // lanes, lanes), 1, 0).reshape(-1, lanes)


def split_phases(value):
    cap, frames, height, width, lanes = value.shape
    value = value.reshape(cap, frames // PHASES, PHASES, height, width, lanes)
    return jnp.moveaxis(value, 2, 4).reshape(-1, PHASES * lanes)


def join_phases(value, shape):
    cap, frames, height, width, lanes = shape
    value = value.reshape(cap, frames // PHASES, height, width, PHASES, lanes)
    return jnp.moveaxis(value, 4, 2).reshape(shape)


def early_gather(shards_one, shards_two, lateral):
    rows = []
    lanes = shards_one[2].shape[-1]
    kinds = [jnp.stack(pair) for pair in zip(shards_one, shards_two)]
    kinds.append(jnp.stack([lateral[..., :lanes], lateral[..., lanes:]]))
    for kind in kinds:
        flat = kind.reshape(-1, kind.shape[-1])
        rows.append(jnp.pad(flat, ((0, 0), (0, lanes - flat.shape[-1]))))
    packed = gather_pack(rows)
    result = []
    at = 0
    for kind in kinds:
        depth, width = kind.shape[-2:]
        number = kind.size // width
        part = packed[:, at : at + number, :width].reshape(packed.shape[0], -1, depth, width)
        at += number
        result.append(jnp.moveaxis(part, 0, 1).reshape(part.shape[1], -1, width))
    return result


def prepare_kernel(taps_ref, space_ref, wide_ref, lateral_ref, *refs):
    slow_one, fast_one, slow_two, fast_two, *outs = refs
    part = taps_ref.shape[-1]
    lateral, *joint = outs[10:]
    number = lateral.shape[0]
    for tap in range(number):
        lateral[tap] = jnp.concatenate([lateral_ref[tap], lateral_ref[number + tap]], axis=1)
    for layer, (slow, fast) in enumerate(((slow_one, fast_one), (slow_two, fast_two))):
        at = fast_at = 0
        for ref in joint[3 * layer : 3 * layer + 3]:
            fast_lanes = part if ref.shape[1] < slow.shape[1] // 2 else wide_ref.shape[-1]
            lanes = ref.shape[1] - PHASES * fast_lanes
            values = [slow[:, at : at + lanes]]
            values += [fast[:, fast_at : fast_at + fast_lanes]] * PHASES
            ref[...] = jnp.concatenate(values, axis=1)
            at, fast_at = at + lanes, fast_at + fast_lanes
    joint[6][...] = slow_one[:, slow_one.shape[1] - joint[6].shape[1] :]
    for layer in range(2):
        main, before, after, space, wide = outs[5 * layer : 5 * layer + 5]
        taps = [taps_ref[3 * layer + tap] for tap in range(3)]
        zero = jnp.zeros_like(taps[0])
        lanes = taps[0].shape[0]
        for row in range(PHASES):
            blocks = [
                taps[row - col + 1] if abs(row - col) <= 1 else zero for col in range(PHASES)
            ]
            main[row * lanes : (row + 1) * lanes, :] = jnp.concatenate(blocks, axis=1)
        before[...] = jnp.concatenate([taps[0]] + [zero] * (PHASES - 1), axis=1)
        after[...] = jnp.concatenate([zero] * (PHASES - 1) + [taps[2]], axis=1)
        for tap in range(9):
            block = space_ref[9 * layer + tap]
            none = jnp.zeros_like(block)
            for row in range(PHASES):
                blocks = [block if row == col else none for col in range(PHASES)]
                space[tap, row * part : (row + 1) * part, :] = jnp.concatenate(blocks, axis=1)
        block = wide_ref[layer]
        none = jnp.zeros_like(block)
        for row in range(PHASES):
            blocks = [block if row == col else none for col in range(PHASES)]
            wide[row * part : (row + 1) * part, :] = jnp.concatenate(blocks, axis=1)


def to_partners(pieces, axis):
    size = lax.axis_size(axis)
    return [
        lax.ppermute(piece, axis, xor_pairs(size, step + 1)) for step, piece in enumerate(pieces)
    ]


def clip_parts(meta, groups, number):
    lanes = groups[0][0].shape[1]
    lengths = [group[0].shape[0] for group in groups]
    depth = sum(lengths) // number
    total_ins = sum(len(group) for group in groups)

    def kernel(meta_ref, *refs):
        ins, outs, total_ref = list(refs[:total_ins]), refs[total_ins:-1], refs[-1]
        at = 0
        for group, length in zip(groups, lengths):
            mine, ins = ins[: len(group)], ins[len(group) :]
            total = mine[0][...]
            if len(mine) > 1:
                total = total.astype(F32)
                for ref in mine[1:]:
                    total = total + ref[...].astype(F32)
                total = total.astype(BF16)
            total_ref[at : at + length, :] = total
            at += length
        index = meta_ref[4] if number != 2 else meta_ref[4] % 2
        for step, out in enumerate(outs):
            start = pl.multiple_of((index ^ step) * depth, 16)
            out[...] = total_ref[pl.ds(start, depth), :]
            out.send()

    return run(
        kernel,
        [((depth, lanes), BF16, "hbm")] * number,
        smem=(meta,),
        saved=[part for group in groups for part in group],
        scratch=(pltpu.VMEM((sum(lengths), lanes), BF16),),
    )


def add_low(first, *others):
    total = first.astype(F32)
    for other in others:
        total = total + other.astype(F32)
    return total.astype(BF16)


def halves_first(keep, send):
    return add_low(keep, lax.ppermute(send, "clips", xor_pairs(4, 1)))


def halves_second(half):
    across = lax.axis_index("clips") // 2
    depth = half.shape[0] // 2
    mine = lax.dynamic_slice_in_dim(half, across * depth, depth, axis=0)
    other = lax.dynamic_slice_in_dim(half, (1 - across) * depth, depth, axis=0)
    return add_low(mine, lax.ppermute(other, "clips", xor_pairs(4, 2)))


def halves_share(total):
    beyond = lax.ppermute(total, "clips", xor_pairs(4, 2))
    beside = lax.ppermute(total, "clips", xor_pairs(4, 1))
    return [total, beside, beyond, lax.ppermute(beyond, "clips", xor_pairs(4, 1))]


def on_device(
    slow_input,
    fast_input,
    slow_cotangent,
    fast_cotangent,
    clip_counts,
    lateral_weight,
    slow_reduce_one,
    slow_spatial_one,
    slow_expand_one,
    slow_shortcut_one,
    fast_reduce_one,
    fast_spatial_one,
    fast_expand_one,
    slow_reduce_two,
    slow_spatial_two,
    slow_expand_two,
    fast_reduce_two,
    fast_spatial_two,
    fast_expand_two,
    slow_norms_one,
    fast_norms_one,
    slow_norms_two,
    fast_norms_two,
):
    geo = Geometry(slow_input.shape, fast_input.shape)
    rows, groups = geo.rows, geo.groups
    half_rows = rows // 2
    count = lax.axis_size("ha") * lax.axis_size("wa")
    spread = spread_count()
    slow_wide = slow_input.shape[-1]
    fast_wide = PHASES * fast_input.shape[-1]
    wide = slow_wide + fast_wide
    mid = slow_reduce_one.shape[-1]
    fast_part = fast_reduce_one.shape[-1]
    fast_mid = PHASES * fast_part
    small = mid + fast_mid
    lat = lateral_weight.shape[-1]
    blocks = slow_wide // mid

    depth_one = slow_reduce_one.shape[1]
    depth_two = slow_reduce_two.shape[1]
    depth_mid = slow_spatial_one.shape[2]
    depth_lat = lateral_weight.shape[1]
    near = gather_pack([slow_reduce_one.reshape(-1, mid), slow_spatial_one.reshape(-1, mid)])
    far = gather_pack(
        [
            columns(slow_expand_one, mid),
            columns(slow_shortcut_one, mid),
            slow_reduce_two.reshape(-1, mid),
        ]
    )
    last = gather_pack([slow_spatial_two.reshape(-1, mid), columns(slow_expand_two, mid)])
    at_space_one = 3 * depth_one
    at_short = blocks * depth_mid
    at_reduce_two = at_short + blocks * depth_one
    at_space_two = 0
    at_expand_two = 9 * depth_mid
    fast_shards_one = (fast_reduce_one, fast_spatial_one, fast_expand_one)
    fast_shards_two = (fast_reduce_two, fast_spatial_two, fast_expand_two)
    compact = early_gather(fast_shards_one, fast_shards_two, lateral_weight)
    structured = [
        ((fast_wide, fast_mid), BF16, "hbm"),
        ((fast_wide // PHASES, fast_mid), BF16, "hbm"),
        ((fast_wide // PHASES, fast_mid), BF16, "hbm"),
        ((9, fast_mid, fast_mid), BF16, "hbm"),
        ((fast_mid, fast_wide), BF16, "hbm"),
    ]
    joint_outs = [((2, lanes), F32, "hbm") for lanes in (small, small, wide)]
    prepared = run(
        prepare_kernel,
        structured * 2
        + [((lateral_weight.shape[0], fast_wide // PHASES, lat), BF16, "hbm")]
        + joint_outs * 2
        + [((2, slow_wide), F32, "hbm")],
        vmem=(*compact, slow_norms_one, fast_norms_one, slow_norms_two, fast_norms_two),
    )
    fast_one, fast_two, lateral = prepared[:5], prepared[5:10], prepared[10]
    params_one, params_two, params_short = prepared[11:14], prepared[14:17], prepared[17]

    held = clip_counts[0]
    clips = direct_sum(jnp.full((1, 128), held, F32), "clips")[0, 0]
    positions = clips * (SUB * geo.frames * count)
    inv_n = jnp.stack([1.0 / positions, 1.0 / (positions * PHASES)])
    ha, wa = lax.axis_index("ha"), lax.axis_index("wa")
    last_ha = jnp.full_like(ha, lax.axis_size("ha") - 1)
    meta = jnp.stack([held * geo.frames, ha, wa, last_ha, lax.axis_index("clips")])
    scalars = (meta, inv_n)

    slow_x = slow_input.reshape(rows, slow_wide)
    fast_x = split_phases(fast_input)
    cot = jnp.concatenate(
        [slow_cotangent.reshape(rows, slow_wide), split_phases(fast_cotangent)], axis=1
    )
    message_out = [((rows, small), BF16, "hbm"), ((2 * EDGE, small), BF16, "hbm")]
    stats_small = ((spread, 2, small), F32, "spread")
    stats_wide = ((spread, 2, wide), F32, "spread")
    stats_both = ((2, wide + slow_wide), F32, "vmem")
    small_out = ((rows, small), F32, "hbm")
    wide_out = ((rows, wide), F32, "hbm")
    small_both = ((rows, small), F32, "both")
    small_next = ((rows, small), F32, "vmem")
    wide_low = ((rows, wide), BF16, "hbm")

    def lateral_kernel(x_ref, k_ref, main_ref, before_ref, after_ref, united_ref, fast_ref):
        lanes = x_ref.shape[1] // PHASES
        x = x_ref[...]
        main = dot(x[:, : 3 * lanes], k_ref[2:5].reshape(3 * lanes, lat))
        past = dot(x[:, 2 * lanes :], k_ref[0:2].reshape(2 * lanes, lat))
        united_ref[...] = (main + geo.shift(past, 1)).astype(BF16)
        fast_ref[...] = fast_conv(geo, x, main_ref[...], before_ref[...], after_ref[...])

    united, za_fast = run(
        lateral_kernel,
        [((rows, lat), BF16, "hbm"), ((rows, fast_mid), F32, "hbm")],
        saved=(fast_x, lateral, *fast_one[:3]),
    )

    def reduce_one_kernel(
        meta_ref, x_ref, united_ref, fast_ref, loads, za_ref, stats_ref, message_ref, edge_ref
    ):
        weights = [loads.get(tap) for tap in range(3)]
        za = time_conv(geo, (x_ref[...], united_ref[...]), weights)
        za = jnp.concatenate([za, fast_ref[...]], axis=1)
        za_ref[...] = za
        za_ref.send()
        za = geo.three(za)
        put_message(za, message_ref, edge_ref, meta_ref, geo.width)
        put_forward(stats_ref, za, meta_ref[0])

    za_one, za_next, stats, message, edges = run(
        reduce_one_kernel,
        [small_both, stats_small, *message_out],
        smem=(meta,),
        saved=(slow_x, united, za_fast),
        weights=((near, 0, 3, depth_one),),
    )
    parts_a1 = exchange(stats)
    halo_one = exchange_halo(message, edges)

    def space_stage(za, parts_a, halo, params, gathered, offset, fast_w):
        def kernel(
            meta_ref,
            inv_ref,
            stats_ref,
            za_ref,
            side_ref,
            up_ref,
            down_ref,
            params_ref,
            fast_ref,
            loads,
            zb_ref,
            hidden_ref,
            out_stats,
        ):
            scale, shift, _, _ = affine(stats_ref, params_ref, inv_ref, mid)

            def act(value):
                return silu(geo.three(value.astype(F32)) * scale + shift)

            own = act(za_ref[...])
            edges = jnp.concatenate(
                [up_ref[half_rows:], side_ref[...], down_ref[half_rows:]], axis=0
            )
            hidden_ref[...] = geo.flat(own).astype(BF16)
            hidden_ref.send()
            near_by = Neighbours(
                own,
                act(up_ref[:half_rows]),
                act(down_ref[:half_rows]),
                geo.flat(act(edges)),
                meta_ref,
                geo.width,
            )
            slow = fast = None
            for tap in range(9):
                moved = geo.flat(near_by.at(tap // 3 - 1, tap % 3 - 1)).astype(BF16)
                slow_term = dot(moved[:, :mid], loads.get(tap))
                fast_term = dot(moved[:, mid:], fast_ref[tap])
                slow = slow_term if slow is None else slow + slow_term
                fast = fast_term if fast is None else fast + fast_term
            zb = jnp.concatenate([slow, fast], axis=1)
            zb_ref[...] = zb
            zb_ref.send()
            put_forward(out_stats, geo.three(zb), meta_ref[0])

        zb, zb_next, hidden, stats, stats_a = run(
            kernel,
            [small_both, ((rows, small), BF16, "hbm"), stats_small],
            smem=scalars,
            parts=(parts_a,),
            vmem=(za,),
            saved=(*halo, params, fast_w),
            weights=((gathered, offset, 9, depth_mid),),
        )
        return zb, zb_next, hidden, exchange(stats), stats_a

    zb_one, zb_next, ha_one, parts_b1, stats_a1 = space_stage(
        za_next, parts_a1, halo_one, params_one[0], near, at_space_one, fast_one[3]
    )

    def expand_body(
        inv_ref, stats_ref, zb_ref, params_ref, fast_ref, hidden_ref, low_ref, zc_ref, loads
    ):
        scale, shift, _, _ = affine(stats_ref, params_ref, inv_ref, mid)
        hidden = geo.flat(silu(geo.three(zb_ref[...]) * scale + shift)).astype(BF16)
        hidden_ref[...] = hidden
        hidden_ref.send()
        zc_ref[:, slow_wide:] = dot(hidden[:, mid:], fast_ref[...])
        for block in range(blocks):
            zc_ref[:, block * mid : (block + 1) * mid] = dot(hidden[:, :mid], loads.get(block))
        low_ref[...] = zc_ref[...].astype(BF16)
        low_ref.send()

    def expand_one_kernel(
        meta_ref,
        inv_ref,
        stats_ref,
        zb_ref,
        params_ref,
        fast_ref,
        x_ref,
        united_ref,
        loads,
        shorts,
        hidden_ref,
        low_ref,
        short_low_ref,
        out_stats,
        zc_ref,
        short_ref,
    ):
        expand_body(
            inv_ref, stats_ref, zb_ref, params_ref, fast_ref, hidden_ref, low_ref, zc_ref, loads
        )
        put_forward(out_stats, geo.three(zc_ref[...]), meta_ref[0])
        for block in range(blocks):
            weight = shorts.get(block)
            value = dot(x_ref[...], weight[:slow_wide]) + dot(united_ref[...], weight[slow_wide:])
            short_ref[:, block * mid : (block + 1) * mid] = value
            put_forward(out_stats, geo.three(value), meta_ref[0], wide + block * mid)
        short_low_ref[...] = short_ref[...].astype(BF16)
        short_low_ref.send()

    hb_one, zc_one, short, stats, stats_b1 = run(
        expand_one_kernel,
        [
            ((rows, small), BF16, "hbm"),
            wide_low,
            ((rows, slow_wide), BF16, "hbm"),
            stats_both,
        ],
        scratch=(pltpu.VMEM((rows, wide), F32), pltpu.VMEM((rows, slow_wide), F32)),
        smem=scalars,
        parts=(parts_b1,),
        vmem=(zb_next,),
        saved=(params_one[1], fast_one[4], slow_x, united),
        weights=((far, 0, blocks, depth_mid), (far, at_short, blocks, depth_one)),
    )
    parts_c1 = exchange_widest(stats)

    def reduce_two_kernel(
        meta_ref,
        inv_ref,
        stats_ref,
        zc_ref,
        short_ref,
        params_ref,
        short_params_ref,
        x_ref,
        main_ref,
        before_ref,
        after_ref,
        loads,
        sum_ref,
        low_ref,
        za_ref,
        out_stats,
        message_ref,
        edge_ref,
    ):
        scale, shift, _, _ = affine(stats_ref, params_ref, inv_ref, slow_wide, 0, wide)
        scale_s, shift_s, _, _ = affine(
            stats_ref, short_params_ref, inv_ref, slow_wide, wide, wide + slow_wide
        )
        normed = geo.three(zc_ref[...].astype(F32)) * scale + shift
        slow = normed[..., :slow_wide] + (
            geo.three(short_ref[...].astype(F32)) * scale_s + shift_s
        )
        fast = normed[..., slow_wide:] + geo.three(x_ref[...].astype(F32))
        total = jnp.concatenate([slow, fast], axis=-1)
        sum_ref[...] = geo.flat(total).astype(BF16)
        sum_ref.send()
        low = geo.flat(silu(total)).astype(BF16)
        low_ref[...] = low
        low_ref.send()
        weights = [loads.get(tap) for tap in range(3)]
        za = time_conv(geo, (low[:, :slow_wide],), weights)
        fast_za = fast_conv(
            geo, low[:, slow_wide:], main_ref[...], before_ref[...], after_ref[...]
        )
        za = jnp.concatenate([za, fast_za], axis=1)
        za_ref[...] = za
        za_ref.send()
        za = geo.three(za)
        put_message(za, message_ref, edge_ref, meta_ref, geo.width)
        put_forward(out_stats, za, meta_ref[0])

    sum_one, low_one, za_two, za_next, stats, message, edges, stats_c1 = run(
        reduce_two_kernel,
        [wide_low, wide_low, small_both, stats_small, *message_out],
        smem=scalars,
        parts=(parts_c1,),
        saved=(zc_one, short, params_one[2], params_short, fast_x, *fast_two[:3]),
        weights=((far, at_reduce_two, 3, depth_two),),
    )
    parts_a2 = exchange(stats)
    halo_two = exchange_halo(message, edges)
    zb_two, zb_next, ha_two, parts_b2, stats_a2 = space_stage(
        za_next, parts_a2, halo_two, params_two[0], last, at_space_two, fast_two[3]
    )

    def expand_two_kernel(
        meta_ref,
        inv_ref,
        stats_ref,
        zb_ref,
        params_ref,
        fast_ref,
        loads,
        hidden_ref,
        low_ref,
        out_stats,
        zc_ref,
    ):
        expand_body(
            inv_ref, stats_ref, zb_ref, params_ref, fast_ref, hidden_ref, low_ref, zc_ref, loads
        )
        put_forward(out_stats, geo.three(zc_ref[...]), meta_ref[0])

    hb_two, zc_two, stats, stats_b2 = run(
        expand_two_kernel,
        [((rows, small), BF16, "hbm"), wide_low, stats_wide],
        scratch=(pltpu.VMEM((rows, wide), F32),),
        smem=scalars,
        parts=(parts_b2,),
        vmem=(zb_next,),
        saved=(params_two[1], fast_two[4]),
        weights=((last, at_expand_two, blocks, depth_mid),),
    )
    parts_c2 = exchange(stats)

    def head_kernel(
        meta_ref,
        inv_ref,
        stats_ref,
        zc_ref,
        params_ref,
        sum_ref,
        cot_ref,
        out_ref,
        low_ref,
        sums_ref,
    ):
        scale, shift, mean, inv = affine(stats_ref, params_ref, inv_ref, slow_wide)
        zc = geo.three(zc_ref[...].astype(F32))
        total = zc * scale + shift + silu(geo.three(sum_ref[...].astype(F32)))
        valid = mask_groups(total.shape, meta_ref[0])
        sigma = jax.nn.sigmoid(total)
        out_ref[...] = geo.flat(jnp.where(valid, total * sigma, 0.0)).astype(BF16)
        slopes = sigma * (1.0 + total * (1.0 - sigma))
        gradient = jnp.where(valid, geo.three(cot_ref[...].astype(F32)) * slopes, 0.0)
        out_ref.send()
        low_ref[...] = geo.flat(gradient).astype(BF16)
        low_ref.send()
        put_back(sums_ref, gradient, (zc - mean) * inv)

    outputs, g_two, sums, stats_c2 = run(
        head_kernel,
        [((rows, wide), BF16, "hbm"), wide_low, stats_wide],
        smem=scalars,
        parts=(parts_c2,),
        saved=(zc_two, params_two[2], sum_one, cot),
    )
    parts_c2 = exchange(sums)

    def norm_back(gradient, value, coeffs, sums, valid):
        scale, _, mean, inv = coeffs
        crossed = (value - mean) * inv * sums[0] + sums[1]
        return scale * (gradient - jnp.where(valid, crossed, 0.0))

    def expand_back_body(
        meta_ref,
        inv_ref,
        sums_ref,
        g_ref,
        stats_ref,
        stats_b_ref,
        zc_ref,
        params_ref,
        zb_ref,
        params_b_ref,
        fast_ref,
        loads,
        gz_ref,
        g_out,
        sums_out,
        message_ref,
        edge_ref,
    ):
        limit = meta_ref[0]
        coeffs = affine(stats_ref, params_ref, inv_ref, slow_wide, 0, wide)
        both = [back_rows(sums_ref, inv_ref, slow_wide, row, 0, wide) for row in range(2)]
        gradient = geo.three(g_ref[...].astype(F32))
        gz = norm_back(
            gradient,
            geo.three(zc_ref[...].astype(F32)),
            coeffs,
            both,
            mask_groups(gradient.shape, limit),
        )
        gz = geo.flat(gz).astype(BF16)
        gz_ref[...] = gz
        gz_ref.send()
        fast = dot_nt(gz[:, slow_wide:], fast_ref[...])
        slow = None
        for block in range(blocks):
            term = dot_nt(gz[:, block * mid : (block + 1) * mid], loads.get(block))
            slow = term if slow is None else slow + term
        scale, shift, mean, inv = affine(stats_b_ref, params_b_ref, inv_ref, mid)
        zb = geo.three(zb_ref[...])
        back = geo.three(jnp.concatenate([slow, fast], axis=1)) * slope(zb * scale + shift)
        g_out[...] = geo.flat(back)
        put_message(
            jnp.concatenate([back, zb], axis=-1), message_ref, edge_ref, meta_ref, geo.width
        )
        masked = jnp.where(mask_groups(back.shape, limit), back, 0.0)
        put_back(sums_out, masked, (zb - mean) * inv)
        return gradient

    message_back = [((rows, 2 * small), BF16, "hbm"), ((2 * EDGE, 2 * small), BF16, "hbm")]
    gz_c2, g_b2, sums, message, edges, sums_c2 = run(
        expand_back_body,
        [((rows, wide), BF16, "hbm"), small_next, stats_small, *message_back],
        smem=scalars,
        parts=(parts_c2,),
        saved=(g_two, stats_c2, stats_b2, zc_two, params_two[2], zb_two, params_two[1], fast_two[4]),
        weights=((last, at_expand_two, blocks, depth_mid),),
    )
    parts_b2 = exchange(sums)
    halo_back_two = exchange_halo(message, edges)
    align = 16 * lax.axis_size("clips")

    def aligned(number):
        return number + -number % align


    lanes_fast = fast_wide // PHASES
    fast_rows_count = fast_reduce_one.shape[1] + 2 * SUB

    def expand_grad(hb_ref, gz_ref, out_ref, at):
        for block in range(blocks):
            value = dot_tn(hb_ref[:, :mid], gz_ref[:, block * mid : (block + 1) * mid])
            low = at + block * depth_mid
            out_ref[:, low : low + depth_mid, :] = value.astype(BF16).reshape(
                count, depth_mid, mid
            )
        if isinstance(out_ref, Store):
            out_ref.send_rows(at, at + blocks * depth_mid)

    def fast_expand_grad(hb_ref, gz_ref):
        fast = dot_tn(hb_ref[:, mid:], gz_ref[:, slow_wide:])
        total = None
        for phase in range(PHASES):
            part = fast[
                phase * fast_part : (phase + 1) * fast_part,
                phase * lanes_fast : (phase + 1) * lanes_fast,
            ]
            total = part if total is None else total + part
        return total

    def space_grad(ha_ref, taps_ref, out_ref, at):
        fast_grads = []
        for tap in range(9):
            value = dot_tn(ha_ref[:, :mid], taps_ref[tap, :, :mid])
            low = at + tap * depth_mid
            out_ref[:, low : low + depth_mid, :] = value.astype(BF16).reshape(
                count, depth_mid, mid
            )
            fast = dot_tn(ha_ref[:, mid:], taps_ref[tap, :, mid:])
            total = None
            for phase in range(PHASES):
                part = lane_block(
                    fast[phase * fast_part : (phase + 1) * fast_part], phase, fast_part
                )
                total = part if total is None else total + part
            fast_grads.append(total)
        if isinstance(out_ref, Store):
            out_ref.send_rows(at, at + 9 * depth_mid)
        return fast_grads

    def put_fast(reduce, space, expand, out_ref, at):
        lane = lax.broadcasted_iota(jnp.int32, reduce[0].shape, 1)

        def beside(parts):
            keep = lane[: parts[0].shape[0]]
            total = None
            for place, part in enumerate(parts):
                part = jnp.where(keep < fast_part, part, 0.0)
                part = pltpu.roll(part, place * fast_part, 1) if place else part
                total = part if total is None else total + part
            return total

        depth = reduce[0].shape[0] // count
        taps = beside(reduce).astype(BF16).reshape(count, depth, lanes_fast)
        out_ref[:, at : at + depth, :] = jnp.concatenate([taps, jnp.zeros_like(taps)], axis=-1)

        def spread(value):
            tiles = value.reshape(count // 2, SUB, lanes_fast)
            return jnp.stack([tiles, pltpu.roll(tiles, SUB // 2, 1)], axis=1).reshape(
                count, SUB, lanes_fast
            )

        first = jnp.concatenate([spread(beside(space[0:4])), spread(beside(space[4:8]))], axis=-1)
        second = jnp.concatenate([spread(beside(space[8:9])), spread(expand)], axis=-1)
        both = jnp.concatenate([first, second], axis=1).astype(BF16)
        out_ref[:, at + depth : at + depth + 2 * SUB, :] = both
        if isinstance(out_ref, Store):
            out_ref.send_rows(at, at + depth + 2 * SUB)

    def space_back_stage(
        g, zb, za, halo, stats_b, parts_b, params_b, stats_a, params_a, g_hbm, at, fast_w
    ):
        def kernel(
            meta_ref,
            inv_ref,
            sums_b_ref,
            g_ref,
            side_ref,
            up_ref,
            down_ref,
            stats_b_ref,
            stats_a_ref,
            zb_ref,
            za_ref,
            params_b_ref,
            params_a_ref,
            fast_ref,
            loads,
            taps_ref,
            g_out,
            sums_out,
        ):
            limit = meta_ref[0]
            coeffs = affine(stats_b_ref, params_b_ref, inv_ref, mid)
            both = [back_rows(sums_b_ref, inv_ref, mid, row) for row in range(2)]

            def back(gradient, value, valid):
                return norm_back(gradient, value, coeffs, both, valid)

            def halo_back(value, scale):
                value = geo.three(value.astype(F32))
                valid = mask_groups(value[..., :small].shape, limit, scale)
                return back(value[..., :small], value[..., small:], valid)

            def edge_back(value):
                value = geo.three(value.astype(F32))
                shape = value[..., :small].shape
                group = lax.broadcasted_iota(jnp.int32, shape, 0) * SUB % EDGE
                group = group + lax.broadcasted_iota(jnp.int32, shape, 1)
                return geo.flat(back(value[..., :small], value[..., small:], group < limit))

            own, zb = geo.three(g_ref[...]), geo.three(zb_ref[...])
            edges = jnp.concatenate(
                [up_ref[half_rows:], side_ref[...], down_ref[half_rows:]], axis=0
            )

            near_by = Neighbours(
                back(own, zb, mask_groups(own.shape, limit)),
                halo_back(up_ref[:half_rows], 2),
                halo_back(down_ref[:half_rows], 2),
                edge_back(edges),
                meta_ref,
                geo.width,
            )
            slow = fast = None
            for tap in range(9):
                moved = geo.flat(near_by.at(1 - tap // 3, 1 - tap % 3)).astype(BF16)
                taps_ref[tap] = moved
                if tap == 8:
                    taps_ref.send()
                slow_term = dot_nt(moved[:, :mid], loads.get(tap))
                fast_term = dot_nt(moved[:, mid:], fast_ref[tap])
                slow = slow_term if slow is None else slow + slow_term
                fast = fast_term if fast is None else fast + fast_term
            scale, shift, mean, inv = affine(stats_a_ref, params_a_ref, inv_ref, mid)
            za = geo.three(za_ref[...])
            result = geo.three(jnp.concatenate([slow, fast], axis=1)) * slope(za * scale + shift)
            g_out[...] = geo.flat(result)
            masked = jnp.where(mask_groups(result.shape, limit), result, 0.0)
            put_back(sums_out, masked, (za - mean) * inv)

        taps, g, sums, sums_b = run(
            kernel,
            [((9, rows, small), BF16, "hbm"), small_next, stats_small],
            smem=scalars,
            parts=(parts_b,),
            vmem=(g,),
            saved=(*halo, stats_b, stats_a, zb, za, params_b, params_a, fast_w),
            weights=((g_hbm, at, 9, depth_mid),),
        )
        return taps, g, exchange(sums), sums_b

    taps_two, g_a2, parts_a2, sums_b2 = space_back_stage(
        g_b2,
        zb_two,
        za_two,
        halo_back_two,
        stats_b2,
        parts_b2,
        params_two[1],
        stats_a2,
        params_two[0],
        last,
        at_space_two,
        fast_two[3],
    )
    def grads_two_kernel(hb_ref, gz_ref, ha_ref, taps_ref, out_ref, fast_out):
        space = space_grad(ha_ref, taps_ref, out_ref, 0)
        expand_grad(hb_ref, gz_ref, out_ref, 9 * depth_mid)
        for tap in range(9):
            fast_out[tap] = space[tap]
        fast_out[9] = fast_expand_grad(hb_ref, gz_ref)

    rows_space = aligned((9 + blocks) * depth_mid)
    packed_space, fast_space_two = run(
        grads_two_kernel,
        [((count, rows_space, mid), BF16, "rows"), ((10, fast_part, lanes_fast), F32, "hbm")],
        saved=(hb_two, gz_c2, ha_two, taps_two),
    )
    sum_space = lax.psum_scatter(packed_space, TILE, scatter_dimension=0, tiled=False)

    def reduce_gz(meta_ref, inv_ref, g_ref, za_ref, stats_ref, sums_ref, params_ref, steps_ref):
        coeffs = affine(stats_ref, params_ref, inv_ref, mid)
        both = [back_rows(sums_ref, inv_ref, mid, row) for row in range(2)]
        gradient = geo.three(g_ref[...])
        gz = norm_back(
            gradient,
            geo.three(za_ref[...]),
            coeffs,
            both,
            mask_groups(gradient.shape, meta_ref[0]),
        )
        gz = geo.flat(gz)
        steps = [geo.shift(gz, -1).astype(BF16), gz.astype(BF16), geo.shift(gz, 1).astype(BF16)]
        for tap in range(3):
            steps_ref[tap] = steps[tap]
        steps_ref.send()
        return steps

    def reduce_back_two_kernel(
        meta_ref,
        inv_ref,
        sums_ref,
        g_ref,
        stats_ref,
        stats_c_ref,
        za_ref,
        params_ref,
        g_two_ref,
        sum_ref,
        zc_ref,
        short_ref,
        main_ref,
        before_ref,
        after_ref,
        loads,
        steps_ref,
        fast_out,
        g_out,
        sums_out,
    ):
        steps = reduce_gz(
            meta_ref, inv_ref, g_ref, za_ref, stats_ref, sums_ref, params_ref, steps_ref
        )
        slow = None
        for tap in range(3):
            term = dot_nt(steps[tap][:, :mid], loads.get(tap))
            slow = term if slow is None else slow + term
        fast = fast_conv_back(
            [step[:, mid:] for step in steps], main_ref[...], before_ref[...], after_ref[...]
        )
        back = jnp.concatenate([slow, fast], axis=1) + g_two_ref[...].astype(F32)
        back = back * slope(sum_ref[...].astype(F32))
        g_out[...] = back.astype(BF16)
        g_out.send()
        fast_out[...] = back[:, slow_wide:]
        fast_out.send()
        back = geo.three(back)
        masked = jnp.where(mask_groups(back.shape, meta_ref[0]), back, 0.0)
        mean, inv = moments(stats_c_ref, inv_ref, slow_wide, 0, wide)
        put_back(sums_out, masked, (geo.three(zc_ref[...].astype(F32)) - mean) * inv)
        mean, inv = moments(stats_c_ref, inv_ref, slow_wide, wide, wide + slow_wide)
        masked = masked[..., :slow_wide]
        put_back(sums_out, masked, (geo.three(short_ref[...].astype(F32)) - mean) * inv, wide)

    steps_two, g_one_fast, g_one, sums, sums_a2 = run(
        reduce_back_two_kernel,
        [
            ((3, rows, small), BF16, "hbm"),
            ((rows, fast_wide), F32, "hbm"),
            wide_low,
            stats_both,
        ],
        smem=scalars,
        parts=(parts_a2,),
        vmem=(g_a2,),
        saved=(stats_a2, stats_c1, za_two, params_two[0], g_two, sum_one, zc_one, short, *fast_two[:3]),
        weights=((far, at_reduce_two, 3, depth_two),),
    )
    parts_c1 = exchange_widest(sums)

    def expand_back_one_kernel(*refs):
        *body, short_ref, short_params_ref, loads, gz_ref, g_out, sums_out, message, edge, gs_ref = (
            refs
        )
        gradient = expand_back_body(*body, loads, gz_ref, g_out, sums_out, message, edge)
        meta_ref, inv_ref, sums_ref, _, stats_ref = body[:5]
        low, high = wide, wide + slow_wide
        coeffs = affine(stats_ref, short_params_ref, inv_ref, slow_wide, low, high)
        both = [back_rows(sums_ref, inv_ref, slow_wide, row, low, high) for row in range(2)]
        gradient = gradient[..., :slow_wide]
        valid = mask_groups(gradient.shape, meta_ref[0])
        gs = norm_back(gradient, geo.three(short_ref[...].astype(F32)), coeffs, both, valid)
        gs_ref[...] = geo.flat(gs).astype(BF16)

    gz_c1, g_b1, sums, message, edges, gz_short, sums_c1 = run(
        expand_back_one_kernel,
        [((rows, wide), BF16, "hbm"), small_next, stats_small, *message_back]
        + [((rows, slow_wide), BF16, "hbm")],
        smem=scalars,
        parts=(parts_c1,),
        saved=(g_one, stats_c1, stats_b1, zc_one, params_one[2], zb_one, params_one[1], fast_one[4])
        + (short, params_short),
        weights=((far, 0, blocks, depth_mid),),
    )
    parts_b1 = exchange(sums)
    halo_back_one = exchange_halo(message, edges)
    joined_lanes = slow_wide + lat

    def grads_mid_kernel(
        x_ref,
        united_ref,
        gs_ref,
        hb_ref,
        gz_ref,
        low_ref,
        steps_ref,
        fast_ref,
        loads,
        out_ref,
        back_ref,
    ):
        for tap in range(3):
            value = dot_tn(low_ref[:, :slow_wide], steps_ref[tap, :, :mid])
            out_ref[:, tap * depth_two : (tap + 1) * depth_two, :] = value.astype(BF16).reshape(
                count, depth_two, mid
            )
        at = 3 * depth_two
        out_ref.send_rows(0, at)
        reduce = fast_reduce_grad(
            low_ref[:, slow_wide:], [steps_ref[tap, :, mid:] for tap in range(3)]
        )
        put_fast(reduce, [fast_ref[tap] for tap in range(9)], fast_ref[9], out_ref, at)
        at += fast_rows_count
        expand_grad(hb_ref, gz_ref, out_ref, at + blocks * depth_one)
        for block in range(blocks):
            gs = gs_ref[:, block * mid : (block + 1) * mid]
            value = jnp.concatenate([dot_tn(x_ref[...], gs), dot_tn(united_ref[...], gs)], axis=0)
            low = at + block * depth_one
            out_ref[:, low : low + depth_one, :] = value.astype(BF16).reshape(
                count, depth_one, mid
            )
            out_ref.send_rows(low, low + depth_one)
        for block in range(blocks):
            gs = gs_ref[:, block * mid : (block + 1) * mid]
            term = dot_nt(gs, loads.get(block))
            back_ref[...] = term if block == 0 else back_ref[...] + term

    rows_mid = aligned(3 * depth_two + fast_rows_count + blocks * (depth_one + depth_mid))
    packed_mid, short_back = run(
        grads_mid_kernel,
        [((count, rows_mid, mid), BF16, "rows"), ((rows, joined_lanes), F32, "hbm")],
        saved=(slow_x, united, gz_short, hb_one, gz_c1, low_one, steps_two, fast_space_two),
        weights=((far, at_short, blocks, depth_one),),
    )
    sum_mid = lax.psum_scatter(packed_mid, TILE, scatter_dimension=0, tiled=False)

    taps_one, g_a1, parts_a1, sums_b1 = space_back_stage(
        g_b1,
        zb_one,
        za_one,
        halo_back_one,
        stats_b1,
        parts_b1,
        params_one[1],
        stats_a1,
        params_one[0],
        near,
        at_space_one,
        fast_one[3],
    )
    def last_kernel(
        meta_ref,
        inv_ref,
        sums_ref,
        g_ref,
        stats_ref,
        za_ref,
        params_ref,
        g_one_ref,
        short_ref,
        lateral_ref,
        main_ref,
        before_ref,
        after_ref,
        loads,
        steps_ref,
        slow_ref,
        fast_ref,
        united_ref,
    ):
        steps = reduce_gz(
            meta_ref, inv_ref, g_ref, za_ref, stats_ref, sums_ref, params_ref, steps_ref
        )
        joined = short_ref[...]
        for tap in range(3):
            joined = joined + dot_nt(steps[tap][:, :mid], loads.get(tap))
        slow_ref[...] = joined[:, :slow_wide]
        tail = joined[:, slow_wide:]
        now, past = tail.astype(BF16), geo.shift(tail, -1).astype(BF16)
        united_ref[0] = now
        united_ref[1] = past
        lanes = fast_wide // PHASES
        fast = fast_conv_back(
            [step[:, mid:] for step in steps], main_ref[...], before_ref[...], after_ref[...]
        )
        fast = fast + g_one_ref[...]
        front = dot_nt(now, lateral_ref[2:5].reshape(3 * lanes, lat))
        back = dot_nt(past, lateral_ref[0:2].reshape(2 * lanes, lat))
        fast_ref[:, : 2 * lanes] = fast[:, : 2 * lanes] + front[:, : 2 * lanes]
        fast_ref[:, 2 * lanes : 3 * lanes] = (
            fast[:, 2 * lanes : 3 * lanes] + front[:, 2 * lanes :] + back[:, :lanes]
        )
        fast_ref[:, 3 * lanes :] = fast[:, 3 * lanes :] + back[:, lanes:]

    steps_one, grad_slow, grad_fast, united_low, sums_a1 = run(
        last_kernel,
        [
            ((3, rows, small), BF16, "hbm"),
            ((rows, slow_wide), F32, "hbm"),
            ((rows, fast_wide), F32, "hbm"),
            ((2, rows, lat), BF16, "hbm"),
        ],
        smem=scalars,
        parts=(parts_a1,),
        vmem=(g_a1,),
        saved=(stats_a1, za_one, params_one[0], g_one_fast, short_back, lateral, *fast_one[:3]),
        weights=((near, 0, 3, depth_one),),
    )

    def grads_one_kernel(
        meta_ref,
        steps_ref,
        low_ref,
        x_ref,
        united_ref,
        fast_x_ref,
        ha_ref,
        taps_ref,
        hb_ref,
        gz_ref,
        own_ref,
        send_ref,
        out_ref,
        sems,
    ):
        lanes = fast_wide // PHASES
        for tap in range(3):
            step = steps_ref[tap, :, :mid]
            value = jnp.concatenate(
                [dot_tn(x_ref[...], step), dot_tn(united_ref[...], step)], axis=0
            )
            out_ref[:, tap * depth_one : (tap + 1) * depth_one, :] = value.astype(BF16).reshape(
                count, depth_one, mid
            )
        at = 3 * depth_one
        place = (own_ref, send_ref, meta_ref[1], meta_ref[2], sems)
        put_blocks(out_ref, 0, at, *place, 0)
        past = dot_tn(fast_x_ref[:, 2 * lanes :], low_ref[1])
        now = dot_tn(fast_x_ref[:, : 3 * lanes], low_ref[0])
        both = jnp.concatenate([past, now], axis=0).astype(BF16)
        for tap in range(5):
            out_ref[:, at + tap * depth_lat : at + (tap + 1) * depth_lat, :] = both[
                tap * lanes : (tap + 1) * lanes
            ].reshape(count, depth_lat, lat)
        at += 5 * depth_lat
        space = space_grad(ha_ref, taps_ref, out_ref, at)
        at += 9 * depth_mid
        reduce = fast_reduce_grad(
            fast_x_ref[...], [steps_ref[tap, :, mid:] for tap in range(3)]
        )
        put_fast(reduce, space, fast_expand_grad(hb_ref, gz_ref), out_ref, at)

        put_blocks(out_ref, 3 * depth_one, rows_late, *place, 1)
        for low, top, turn in ((0, 3 * depth_one, 0), (3 * depth_one, rows_late, 1)):
            rows_part = pl.ds(low, top - low)
            for block in range(count):
                source, target = out_ref.at[block, rows_part, :], own_ref.at[0, rows_part, :]
                pltpu.make_async_copy(source, target, sems.at[turn, block]).wait()

    def put_blocks(blocks_ref, low, top, own_ref, send_ref, ha, wa, sems, turn):
        rows_part = pl.ds(low, top - low)
        for block in range(count):
            place, col = ha ^ (block // 2), block % 2
            source, sem = blocks_ref.at[block, rows_part, :], sems.at[turn, block]

            @pl.when(wa == col)
            def _():
                pltpu.make_async_copy(source, own_ref.at[place, rows_part, :], sem).start()

            @pl.when(wa != col)
            def _():
                pltpu.make_async_copy(source, send_ref.at[place, rows_part, :], sem).start()

    high = count // 2
    rows_one = 3 * depth_one + 5 * depth_lat + 9 * depth_mid + fast_rows_count
    rows_late = aligned(rows_one)
    blocks_out = ((high, rows_late, mid), BF16, "raw")
    own_blocks, send_blocks = run(
        grads_one_kernel,
        [blocks_out, blocks_out],
        smem=(meta,),
        saved=(steps_one, united_low, slow_x, united, fast_x, ha_one, taps_one, hb_one, gz_c1),
        scratch=(
            pltpu.VMEM((count, rows_late, mid), BF16),
            pltpu.SemaphoreType.DMA((2, count)),
        ),
    )
    side_blocks = lax.ppermute(send_blocks, "wa", xor_pairs(2, 1))

    def chip_kernel(own_ref, side_ref, *out_refs):
        for place in range(high):
            total = own_ref[place].astype(F32) + side_ref[place].astype(F32)
            out_refs[place][...] = total.astype(BF16)
            out_refs[place].send()

    late_out = ((rows_late, mid), BF16, "hbm")
    chip_sums = run(chip_kernel, [late_out] * high, saved=(own_blocks, side_blocks))
    late = [chip_sums[0]] + to_partners(chip_sums[1:], "ha")
    four = lax.axis_size("clips") == 4
    sum_space, sum_mid, _ = lax.optimization_barrier((sum_space, sum_mid, chip_sums[0]))
    halves = clip_parts(meta, [[sum_space], [sum_mid]], 2 if four else 1)
    if four:
        half = halves_first(*halves)
        total_early = halves_second(half)
        late, _ = lax.optimization_barrier((late, total_early))
        parts_early = halves_share(total_early)
    else:
        parts_early = [lax.psum(halves[0], "clips")]
    quarters = clip_parts(meta, [late], 4 if four else 1)
    if four:
        total_late = add_low(quarters[0], *to_partners(quarters[1:], "clips"))
        parts_late = [total_late] + to_partners([total_late] * 3, "clips")
    else:
        parts_late = [lax.psum(quarters[0], "clips")]

    def finish(*jobs):
        outs_all = []
        for _, groups, _ in jobs:
            for _, shapes in groups:
                for shape in shapes:
                    outs_all += list(shape) if isinstance(shape[0], tuple) else [shape]
        number = sum(len(parts) for parts, _, _ in jobs)
        deepest = max(sum(rows_group for rows_group, _ in groups) for _, groups, _ in jobs)

        def kernel(meta_ref, *refs):
            ins, outs, total_ref = list(refs[:number]), list(refs[number:-1]), refs[-1]
            for parts, groups, by_halves in jobs:
                mine, ins = ins[: len(parts)], ins[len(parts) :]
                one_job(meta_ref, mine, outs, total_ref, groups, by_halves)

        def one_job(meta_ref, ins, outs, total_ref, groups, by_halves):
            size = len(ins)
            depth = sum(rows_group for rows_group, _ in groups) // size
            base = 0
            for step, ref in enumerate(ins):
                clip = meta_ref[4] ^ step
                place = clip % 2 * 2 + clip // 2 if by_halves else clip
                start = pl.multiple_of(place * depth, 16) if size > 1 else 0
                total_ref[pl.ds(start, depth), :] = ref[...].astype(F32)
            for rows_group, shapes in groups:
                at = base
                for shape in shapes:
                    if isinstance(shape[0], tuple):
                        reduce, space, expand = outs.pop(0), outs.pop(0), outs.pop(0)
                        rows_tap, lanes = reduce.shape[1:]
                        for tap in range(3):
                            reduce[tap] = total_ref[
                                at : at + rows_tap, tap * lanes : (tap + 1) * lanes
                            ]
                        few = space.shape[2]
                        for tap in range(9):
                            row = at + rows_tap + tap // SUB * SUB
                            lane = tap % SUB * lanes
                            space[tap // 3, tap % 3] = total_ref[
                                row : row + few, lane : lane + lanes
                            ]
                        row = at + rows_tap + SUB
                        expand[...] = total_ref[row : row + few, expand.shape[1] :]
                        for out in (reduce, space, expand):
                            out.send()
                        at += rows_tap + 2 * SUB
                        continue
                    out = outs.pop(0)
                    if len(shape) == 2 and shape[1] > mid:
                        for block in range(shape[1] // mid):
                            out[:, block * mid : (block + 1) * mid] = total_ref[
                                at : at + shape[0], :
                            ]
                            at += shape[0]
                    else:
                        number = 1
                        for length in shape[:-1]:
                            number *= length
                        out[...] = total_ref[at : at + number, :].reshape(shape)
                        at += number
                    out.send()
                base += rows_group

        return run(
            kernel,
            [(shape, F32, "hbm") for shape in outs_all],
            smem=(meta,),
            saved=[part for parts, _, _ in jobs for part in parts],
            scratch=(pltpu.VMEM((deepest, mid), F32),),
        )

    shapes_one = tuple(shard.shape for shard in fast_shards_one)
    shapes_two = tuple(shard.shape for shard in fast_shards_two)
    groups_early = [
        (rows_space, [slow_spatial_two.shape, slow_expand_two.shape]),
        (
            rows_mid,
            [slow_reduce_two.shape, shapes_two, slow_shortcut_one.shape, slow_expand_one.shape],
        ),
    ]
    groups_late = [
        (
            rows_late,
            [slow_reduce_one.shape, lateral_weight.shape, slow_spatial_one.shape, shapes_one],
        )
    ]
    finished = finish((parts_early, groups_early, True), (parts_late, groups_late, False))
    grad_slow_spatial_two, grad_slow_expand_two, grad_slow_reduce_two = finished[:3]
    fast_two_grads, (grad_slow_shortcut, grad_slow_expand_one) = finished[3:6], finished[6:8]
    grad_slow_reduce_one, grad_lateral, grad_slow_spatial_one, *fast_one_grads = finished[8:]

    def norm_grads(first, second, third):
        slow = [first[:, :mid], second[:, :mid], third[:, :slow_wide]]
        fast = [first[:, mid:], second[:, mid:], third[:, slow_wide:wide]]
        fast = [jnp.sum(part.reshape(2, PHASES, -1), axis=1) for part in fast]
        return slow, fast

    slow_one_p, fast_one_p = norm_grads(sums_a1, sums_b1, sums_c1)
    slow_two_p, fast_two_p = norm_grads(sums_a2, sums_b2, sums_c2)
    grad_slow_norms_one = jnp.concatenate(slow_one_p + [sums_c1[:, wide:]], axis=1)
    grad_slow_norms_two = jnp.concatenate(slow_two_p, axis=1)
    grad_fast_norms_one = jnp.concatenate(fast_one_p, axis=1)
    grad_fast_norms_two = jnp.concatenate(fast_two_p, axis=1)
    return (
        outputs[:, :slow_wide].reshape(slow_input.shape),
        join_phases(outputs[:, slow_wide:], fast_input.shape),
        grad_slow.reshape(slow_input.shape),
        join_phases(grad_fast, fast_input.shape),
        grad_lateral,
        grad_slow_reduce_one,
        grad_slow_spatial_one,
        grad_slow_expand_one,
        grad_slow_shortcut,
        *fast_one_grads,
        grad_slow_reduce_two,
        grad_slow_spatial_two,
        grad_slow_expand_two,
        *fast_two_grads,
        grad_slow_norms_one,
        grad_fast_norms_one,
        grad_slow_norms_two,
        grad_fast_norms_two,
    )


def solution(mesh):
    in_specs = (
        P("clips", None, "ha", "wa", None),
        P("clips", None, "ha", "wa", None),
        P("clips", None, "ha", "wa", None),
        P("clips", None, "ha", "wa", None),
        P("clips"),
        P(None, ("ha", "wa"), None),
        P(None, ("ha", "wa"), None),
        P(None, None, ("ha", "wa"), None),
        P(("ha", "wa"), None),
        P(("ha", "wa"), None),
        P(None, ("ha", "wa"), None),
        P(None, None, ("ha", "wa"), None),
        P(("ha", "wa"), None),
        P(None, ("ha", "wa"), None),
        P(None, None, ("ha", "wa"), None),
        P(("ha", "wa"), None),
        P(None, ("ha", "wa"), None),
        P(None, None, ("ha", "wa"), None),
        P(("ha", "wa"), None),
        P(),
        P(),
        P(),
        P(),
    )
    out_specs = (
        P("clips", None, "ha", "wa", None),
        P("clips", None, "ha", "wa", None),
        P("clips", None, "ha", "wa", None),
        P("clips", None, "ha", "wa", None),
        P(None, ("ha", "wa"), None),
        P(None, ("ha", "wa"), None),
        P(None, None, ("ha", "wa"), None),
        P(("ha", "wa"), None),
        P(("ha", "wa"), None),
        P(None, ("ha", "wa"), None),
        P(None, None, ("ha", "wa"), None),
        P(("ha", "wa"), None),
        P(None, ("ha", "wa"), None),
        P(None, None, ("ha", "wa"), None),
        P(("ha", "wa"), None),
        P(None, ("ha", "wa"), None),
        P(None, None, ("ha", "wa"), None),
        P(("ha", "wa"), None),
        P(),
        P(),
        P(),
        P(),
    )
    return jax.shard_map(
        on_device, mesh=mesh, in_specs=in_specs, out_specs=out_specs, check_vma=False
    )
```

```python
import jax
import jax.numpy as jnp
from jax import lax
from jax.experimental import pallas as pl
from jax.experimental.pallas import tpu as pltpu
from jax.sharding import PartitionSpec as P

epsilon = 1e-05
F32 = jnp.float32
BF16 = jnp.bfloat16
TILE = ("ha", "wa")
PHASES = 4
SUB = 8


def dot(left, right):
    return lax.dot_general(left, right, (((1,), (0,)), ((), ())), preferred_element_type=F32)


def dot_tn(left, right):
    return lax.dot_general(left, right, (((0,), (0,)), ((), ())), preferred_element_type=F32)


def dot_nt(left, right):
    return lax.dot_general(left, right, (((1,), (1,)), ((), ())), preferred_element_type=F32)


class Keep:
    def __init__(self, ref):
        self.scratch, self.shape = ref, ref.shape

    def send(self):
        pass

    def __setitem__(self, index, value):
        self.scratch[index] = value

    def __getitem__(self, index):
        return self.scratch[index]


class Loads:
    def __init__(self, source, offset, target, sems, first):
        self.copies = []
        depth = target.shape[2]
        for step in range(target.shape[0]):
            copy = pltpu.make_async_copy(
                source.at[:, pl.ds(offset + step * depth, depth), :],
                target.at[step],
                sems.at[first + step],
            )
            copy.start()
            self.copies.append(copy)
        self.target = target

    def get(self, step):
        self.copies[step].wait()
        block = self.target[step]
        return block.reshape(-1, block.shape[-1])


class Saved:
    def __init__(self, source, scratch, sem):
        self.scratch, self.shape = scratch, scratch.shape
        self.copy = pltpu.make_async_copy(source, scratch, sem)
        self.copy.start()
        self.ready = False

    def wait(self):
        if not self.ready:
            self.copy.wait()
            self.ready = True

    def __getitem__(self, index):
        self.wait()
        return self.scratch[index]


SEGMENTS = 8


class Store:
    def __init__(self, scratch, target, sems):
        self.scratch, self.target, self.shape = scratch, target, scratch.shape
        self.sems, self.copies = sems, []

    def send(self):
        self.copies.append(pltpu.make_async_copy(self.scratch, self.target, self.sems[0]))
        self.copies[-1].start()

    def send_rows(self, low, high):
        rows = pl.ds(low, high - low)
        source, target = self.scratch.at[:, rows, :], self.target.at[:, rows, :]
        self.copies.append(pltpu.make_async_copy(source, target, self.sems[len(self.copies)]))
        self.copies[-1].start()

    def __setitem__(self, index, value):
        self.scratch[index] = value

    def __getitem__(self, index):
        return self.scratch[index]


CLOSE = 320 * 1024


def run(body, outs, smem=(), parts=(), vmem=(), saved=(), weights=(), scratch=(), limit=53):
    near = pl.BlockSpec(memory_space=pltpu.VMEM)
    far = pl.BlockSpec(memory_space=pltpu.HBM)
    sources = []
    for array, *_ in weights:
        if not any(array is other for other in sources):
            sources.append(array)
    outs = list(outs) + [(part.shape[1:], part.dtype, "hbm") for part in parts]
    flat = []
    twice = []
    for at, (shape, dtype, kind) in enumerate(outs):
        size = jnp.dtype(dtype).itemsize
        for length in shape:
            size *= length
        twice.append(kind == "both" and size <= CLOSE)
        if kind in ("hbm", "both") and size <= CLOSE:
            outs[at] = (shape, dtype, "vmem")
    for shape, dtype, kind in outs:
        flat += [(shape, dtype, "raw"), (shape, dtype, "vmem")] if kind == "both" else [(shape, dtype, kind)]
    close = [array.size * array.dtype.itemsize <= CLOSE for array in saved]
    held = [pltpu.VMEM(array.shape, array.dtype) for array, here in zip(saved, close) if not here]
    for array, _, steps, depth in weights:
        held.append(pltpu.VMEM((steps, array.shape[0], depth, array.shape[2]), array.dtype))
    for shape, dtype, kind in outs:
        if kind in ("hbm", "rows"):
            held.append(pltpu.VMEM(shape, dtype))
        elif kind == "spread":
            held.append(pltpu.VMEM(shape[1:], dtype))
    sems = len(saved) + sum(steps for _, _, steps, _ in weights) + len(outs)
    sems += SEGMENTS * sum(kind == "rows" for _, _, kind in outs)
    held.append(pltpu.SemaphoreType.DMA((sems,)))

    def kernel(*refs):
        refs = list(refs)

        def take(number):
            taken = refs[:number]
            del refs[:number]
            return taken

        smem_refs, part_refs, vmem_refs = take(len(smem)), take(len(parts)), take(len(vmem))
        saved_refs, source_refs, out_refs = take(len(saved)), take(len(sources)), take(len(flat))
        saved_scratch, weight_scratch = take(len(saved) - sum(close)), take(len(weights))
        out_scratch = take(sum(kind in ("hbm", "rows", "spread") for _, _, kind in outs))
        sem, more = refs[0], refs[1:]
        arrays, copies = [], []
        for source, here in zip(saved_refs, close):
            if not here:
                copies.append(Saved(source, saved_scratch[len(copies)], sem.at[len(copies)]))
            arrays.append(source if here else copies[-1])
        at = len(saved)
        loads = []
        for (array, offset, steps, _), target in zip(weights, weight_scratch):
            place = [array is other for other in sources].index(True)
            loads.append(Loads(source_refs[place], offset, target, sem, at))
            at += steps
        results, stores, spreads = [], [], []
        for _, _, kind in outs:
            ref = out_refs.pop(0)
            if kind == "both":
                stores.append(Store(out_refs.pop(0), ref, [sem.at[at]]))
                at += 1
                results.append(stores[-1])
            elif kind in ("hbm", "rows"):
                number = SEGMENTS if kind == "rows" else 1
                stores.append(
                    Store(out_scratch.pop(0), ref, [sem.at[at + part] for part in range(number)])
                )
                at += number
                results.append(stores[-1])
            elif kind == "spread":
                spreads.append((out_scratch.pop(0), ref))
                results.append(spreads[-1][0])
            elif kind == "vmem":
                results.append(Keep(ref))
            else:
                results.append(ref)
        sums = results[len(results) - len(parts) :]
        results = results[: len(results) - len(parts)]
        for part, total in zip(part_refs, sums):
            total[...] = jnp.sum(part[...], axis=0)
            total.send()
        totals = [total.scratch for total in sums]
        body(*smem_refs, *totals, *vmem_refs, *arrays, *loads, *results, *more)
        for copy in copies:
            copy.wait()
        for store in stores:
            if not store.copies:
                store.send()
        for value, ref in spreads:
            ref[...] = jnp.broadcast_to(value[...][None], ref.shape)
        for store in stores:
            for copy in store.copies:
                copy.wait()

    results = pl.pallas_call(
        kernel,
        out_shape=[jax.ShapeDtypeStruct(shape, dtype) for shape, dtype, _ in flat],
        in_specs=[pl.BlockSpec(memory_space=pltpu.SMEM)] * len(smem)
        + [near] * (len(parts) + len(vmem))
        + [near if here else far for here in close]
        + [far] * len(sources),
        out_specs=[far if kind in ("hbm", "rows", "raw") else near for _, _, kind in flat],
        scratch_shapes=held + list(scratch),
        compiler_params=pltpu.CompilerParams(vmem_limit_bytes=limit * 1024 * 1024),
        cost_estimate=pl.CostEstimate(
            flops=2_000_000_000, bytes_accessed=16_000_000, transcendentals=0
        ),
    )(*smem, *parts, *vmem, *saved, *sources)
    returned = []
    for (_, _, kind), double in zip(outs, twice):
        taken, results = results[: 2 if kind == "both" else 1], results[2 if kind == "both" else 1 :]
        returned += list(taken) * (2 if double else 1)
    return returned


class Geometry:
    def __init__(self, slow_shape, fast_shape):
        self.cap, self.frames, self.height, self.width = slow_shape[:4]
        self.groups = self.cap * self.frames
        self.rows = self.groups * SUB

    def three(self, value):
        return value.reshape(-1, SUB, value.shape[-1])

    def flat(self, value):
        return value.reshape(-1, value.shape[-1])

    def shift(self, value, step):
        lanes = value.shape[-1]
        whole = value.reshape(self.cap, self.frames, SUB, lanes)
        zero = jnp.zeros((self.cap, 1, SUB, lanes), value.dtype)
        if step > 0:
            whole = jnp.concatenate([zero, whole[:, :-1]], axis=1)
        else:
            whole = jnp.concatenate([whole[:, 1:], zero], axis=1)
        return whole.reshape(-1, lanes)


def mask_groups(shape, limit, scale=1):
    return lax.broadcasted_iota(jnp.int32, shape, 0) * scale < limit


def rep(ref, row, low, high):
    return jnp.broadcast_to(ref[row : row + 1, low:high], (SUB, high - low))


def fold(value, slow):
    fast = value[:, slow:]
    lanes = fast.shape[-1]
    part = lanes // PHASES
    if part % 128 == 0:
        total = fast[:, :part]
        for phase in range(1, PHASES):
            total = total + fast[:, phase * part : (phase + 1) * part]
        return jnp.concatenate([value[:, :slow]] + [total] * PHASES, axis=1)
    total = fast
    for phase in range(1, PHASES):
        total = total + pltpu.roll(fast, phase * part, 1)
    return jnp.concatenate([value[:, :slow], total], axis=1)


def lane_counts(inv_ref, lanes, slow):
    lane = lax.broadcasted_iota(jnp.int32, (SUB, lanes), 1)
    return jnp.where(lane < slow, inv_ref[0], inv_ref[1])


def moments(stats, inv_ref, slow, low=0, high=None):
    high = stats.shape[1] if high is None else high
    total, square = rep(stats, 0, low, high), rep(stats, 1, low, high)
    if slow < high - low:
        total, square = fold(total, slow), fold(square, slow)
    inv_n = lane_counts(inv_ref, high - low, slow)
    mean = total * inv_n
    return mean, lax.rsqrt(square * inv_n - mean * mean + epsilon)


def affine(stats, params, inv_ref, slow, low=0, high=None):
    mean, inv = moments(stats, inv_ref, slow, low, high)
    lanes = mean.shape[1]
    scale = (1.0 + rep(params, 0, 0, lanes)) * inv
    return scale, rep(params, 1, 0, lanes) - mean * scale, mean, inv


def back_rows(sums, inv_ref, slow, row, low=0, high=None):
    high = sums.shape[1] if high is None else high
    total = rep(sums, row, low, high)
    if slow < high - low:
        total = fold(total, slow)
    return total * lane_counts(inv_ref, high - low, slow)


def silu(value):
    return value * jax.nn.sigmoid(value)


def slope(value):
    sigma = jax.nn.sigmoid(value)
    return sigma * (1.0 + value * (1.0 - sigma))


def put_stats(ref, first, second, low=0):
    lanes = first.shape[-1]
    ref[0:1, low : low + lanes] = jnp.sum(jnp.sum(first, axis=0), axis=0, keepdims=True)
    ref[1:2, low : low + lanes] = jnp.sum(jnp.sum(second, axis=0), axis=0, keepdims=True)


def put_back(ref, gradient, normal, low=0):
    put_stats(ref, gradient * normal, gradient, low)


def put_forward(ref, value, limit, low=0):
    masked = jnp.where(mask_groups(value.shape, limit), value, 0.0)
    put_stats(ref, masked, masked * value, low)


EDGE = 32


def edge_place(wa, width):
    return jnp.where(wa > 0, 0, width - 1)


def put_message(value, ref, edge_ref, meta_ref, width):
    lanes = value.shape[-1]
    pairs = value.reshape(-1, 2, SUB, lanes)
    first, second = pairs[:, 0], pairs[:, 1]
    near = lax.broadcasted_iota(jnp.int32, first.shape, 1) < SUB // 2
    top = jnp.where(near, first, pltpu.roll(second, SUB // 2, 1))
    bottom = jnp.where(near, pltpu.roll(first, SUB // 2, 1), second)
    flat = value.reshape(-1, lanes).astype(BF16)
    shape = (2 * EDGE, flat.shape[0])
    row, col = [lax.broadcasted_iota(jnp.int32, shape, dim) for dim in range(2)]
    low = row >= EDGE
    source = (row - jnp.where(low, EDGE, 0)) * SUB + jnp.where(low, SUB // 2, 0)
    chosen = (col == source + edge_place(meta_ref[2], width)).astype(F32).astype(BF16)
    edges = dot(chosen, flat)
    edge_ref[...] = edges.astype(BF16)
    edge_ref.send()
    top, bottom = [part.reshape(-1, lanes).astype(BF16) for part in (top, bottom)]
    ref[: top.shape[0]] = top
    ref[top.shape[0] :] = bottom
    ref.send()


def unpack_bottom(value):
    both = jnp.stack([pltpu.roll(value, SUB // 2, 1), value], axis=1)
    return both.reshape(-1, SUB, value.shape[-1])


def unpack_top(value):
    both = jnp.stack([value, pltpu.roll(value, SUB // 2, 1)], axis=1)
    return both.reshape(-1, SUB, value.shape[-1])


class Neighbours:
    def __init__(self, own, up, down, edges, meta, width):
        half = SUB // 2
        near = lax.broadcasted_iota(jnp.int32, own.shape, 1) < half
        self.col = lax.broadcasted_iota(jnp.int32, own.shape, 1) % width
        self.width, self.shape = width, own.shape
        ha, wa, last = meta[1], meta[2], meta[3]
        up = unpack_bottom(jnp.where(ha > 0, up, 0.0))
        down = unpack_top(jnp.where(ha < last, down, 0.0))
        self.rows = {
            0: own,
            -1: pltpu.roll(jnp.where(near, own, up), half, 1),
            1: pltpu.roll(jnp.where(near, down, own), half, 1),
        }
        beyond = lax.broadcasted_iota(jnp.int32, edges.shape, 0)
        inside = ((ha > 0) | (beyond >= EDGE)) & ((ha < last) | (beyond < 3 * EDGE))
        self.edges = jnp.where(inside, edges, 0.0).astype(BF16)
        shape = (own.shape[0] * SUB, edges.shape[0])
        place, self.source = [lax.broadcasted_iota(jnp.int32, shape, dim) for dim in range(2)]
        self.group = place // SUB
        self.row = place // half % 2
        self.touches = place % width == edge_place(wa, width)
        self.sides = {}

    def side(self, row_step):
        if row_step not in self.sides:
            wanted = (self.row + row_step + 1) * EDGE + self.group
            chosen = ((self.source == wanted) & self.touches).astype(F32).astype(BF16)
            self.sides[row_step] = dot(chosen, self.edges).reshape(self.shape)
        return self.sides[row_step]

    def at(self, row_step, col_step):
        base = self.rows[row_step]
        if col_step < 0:
            return jnp.where(self.col == 0, self.side(row_step), pltpu.roll(base, 1, 1))
        if col_step > 0:
            away = self.col == self.width - 1
            return jnp.where(away, self.side(row_step), pltpu.roll(base, SUB - 1, 1))
        return base


def xor_pairs(size, step):
    return [(index, index ^ step) for index in range(size)]


def direct_sum(value, axis):
    size = lax.axis_size(axis)
    step = 1
    while step < size:
        if size // step >= 4:
            one, two, three = [
                lax.ppermute(value, axis, xor_pairs(size, step * times)) for times in (1, 2, 3)
            ]
            value = (value + two) + (one + three)
            step *= 4
        else:
            value = value + lax.ppermute(value, axis, xor_pairs(size, step))
            step *= 2
    return value


AXES = ("clips", "ha", "wa")
MOST = 32


def spread_count():
    count = lax.axis_size("ha") * lax.axis_size("wa")
    whole = count * lax.axis_size("clips")
    return whole if whole <= MOST else count


def exchange(copies):
    if copies.shape[0] == lax.axis_size("clips") * lax.axis_size("ha") * lax.axis_size("wa"):
        return lax.all_to_all(copies, AXES, 0, 0)
    return lax.all_to_all(direct_sum(copies, "clips"), TILE, 0, 0)


def exchange_widest(sums):
    count = lax.axis_size("ha") * lax.axis_size("wa")
    sums = direct_sum(sums, "clips")
    return lax.all_to_all(jnp.broadcast_to(sums[None], (count,) + sums.shape), TILE, 0, 0)


def exchange_halo(message, edges):
    wide, high = lax.axis_size("wa"), lax.axis_size("ha")
    half = message.shape[0] // 2
    side = lax.ppermute(edges, "wa", xor_pairs(wide, 1))
    odd = lax.axis_index("ha") % 2 == 1
    tops = jnp.concatenate([message[:half], side[:EDGE]], axis=0)
    bottoms = jnp.concatenate([message[half:], side[EDGE:]], axis=0)
    first = lax.ppermute(jnp.where(odd, tops, bottoms), "ha", xor_pairs(high, 1))
    pairs = [(row, row + 1) for row in range(1, high - 1, 2)]
    pairs = pairs + [(low, row) for row, low in pairs]
    second = lax.ppermute(jnp.where(odd, bottoms, tops), "ha", pairs)
    return side, first, second


def from_above_and_below(first_ref, second_ref, meta_ref):
    first, second = first_ref[...].astype(F32), second_ref[...].astype(F32)
    odd = meta_ref[1] % 2 == 1
    return jnp.where(odd, first, second), jnp.where(odd, second, first)


def time_conv(geo, parts, blocks):
    result = None
    for tap in range(3):
        at = 0
        total = None
        for part in parts:
            lanes = part.shape[-1]
            term = dot(part, blocks[tap][at : at + lanes])
            at += lanes
            total = term if total is None else total + term
        if tap != 1:
            total = geo.shift(total, 1 - tap)
        result = total if result is None else result + total
    return result


def fast_conv(geo, value, main, before, after):
    lanes = value.shape[-1] // PHASES
    result = dot(value, main)
    result = result + geo.shift(dot(value[:, -lanes:], before), 1)
    return result + geo.shift(dot(value[:, :lanes], after), -1)


def fast_conv_back(steps, main, before, after):
    lanes = before.shape[0]
    middle = dot_nt(steps[1], main)
    first = middle[:, :lanes] + dot_nt(steps[2], after)
    last = middle[:, -lanes:] + dot_nt(steps[0], before)
    return jnp.concatenate([first, middle[:, lanes:-lanes], last], axis=1)


def lane_block(value, phase, part):
    return pltpu.roll(value, value.shape[-1] - phase * part, 1) if phase else value


def fast_reduce_grad(value, steps):
    lanes = value.shape[-1] // PHASES
    part = steps[1].shape[-1] // PHASES
    main = dot_tn(value, steps[1])
    before = dot_tn(value[:, -lanes:], steps[0])
    after = dot_tn(value[:, :lanes], steps[2])

    def block(row, col):
        return lane_block(main[row * lanes : (row + 1) * lanes], col, part)

    result = []
    for tap in range(3):
        total = before if tap == 0 else None
        if tap == 2:
            total = lane_block(after, PHASES - 1, part)
        for col in range(PHASES):
            row = col + tap - 1
            if 0 <= row < PHASES:
                total = block(row, col) if total is None else total + block(row, col)
        result.append(total)
    return result


def gather_pack(parts):
    return lax.all_gather(jnp.concatenate(parts, axis=0), TILE, axis=0)


def columns(shard, lanes):
    depth, total = shard.shape
    return jnp.moveaxis(shard.reshape(depth, total // lanes, lanes), 1, 0).reshape(-1, lanes)


def split_phases(value):
    cap, frames, height, width, lanes = value.shape
    value = value.reshape(cap, frames // PHASES, PHASES, height, width, lanes)
    return jnp.moveaxis(value, 2, 4).reshape(-1, PHASES * lanes)


def join_phases(value, shape):
    cap, frames, height, width, lanes = shape
    value = value.reshape(cap, frames // PHASES, height, width, PHASES, lanes)
    return jnp.moveaxis(value, 4, 2).reshape(shape)


def early_gather(shards_one, shards_two, lateral):
    rows = []
    lanes = shards_one[2].shape[-1]
    kinds = [jnp.stack(pair) for pair in zip(shards_one, shards_two)]
    kinds.append(jnp.stack([lateral[..., :lanes], lateral[..., lanes:]]))
    for kind in kinds:
        flat = kind.reshape(-1, kind.shape[-1])
        rows.append(jnp.pad(flat, ((0, 0), (0, lanes - flat.shape[-1]))))
    packed = gather_pack(rows)
    result = []
    at = 0
    for kind in kinds:
        depth, width = kind.shape[-2:]
        number = kind.size // width
        part = packed[:, at : at + number, :width].reshape(packed.shape[0], -1, depth, width)
        at += number
        result.append(jnp.moveaxis(part, 0, 1).reshape(part.shape[1], -1, width))
    return result


def prepare_kernel(taps_ref, space_ref, wide_ref, lateral_ref, *refs):
    slow_one, fast_one, slow_two, fast_two, *outs = refs
    part = taps_ref.shape[-1]
    lateral, *joint = outs[10:]
    number = lateral.shape[0]
    for tap in range(number):
        lateral[tap] = jnp.concatenate([lateral_ref[tap], lateral_ref[number + tap]], axis=1)
    for layer, (slow, fast) in enumerate(((slow_one, fast_one), (slow_two, fast_two))):
        at = fast_at = 0
        for ref in joint[3 * layer : 3 * layer + 3]:
            fast_lanes = part if ref.shape[1] < slow.shape[1] // 2 else wide_ref.shape[-1]
            lanes = ref.shape[1] - PHASES * fast_lanes
            values = [slow[:, at : at + lanes]]
            values += [fast[:, fast_at : fast_at + fast_lanes]] * PHASES
            ref[...] = jnp.concatenate(values, axis=1)
            at, fast_at = at + lanes, fast_at + fast_lanes
    joint[6][...] = slow_one[:, slow_one.shape[1] - joint[6].shape[1] :]
    for layer in range(2):
        main, before, after, space, wide = outs[5 * layer : 5 * layer + 5]
        taps = [taps_ref[3 * layer + tap] for tap in range(3)]
        zero = jnp.zeros_like(taps[0])
        lanes = taps[0].shape[0]
        for row in range(PHASES):
            blocks = [
                taps[row - col + 1] if abs(row - col) <= 1 else zero for col in range(PHASES)
            ]
            main[row * lanes : (row + 1) * lanes, :] = jnp.concatenate(blocks, axis=1)
        before[...] = jnp.concatenate([taps[0]] + [zero] * (PHASES - 1), axis=1)
        after[...] = jnp.concatenate([zero] * (PHASES - 1) + [taps[2]], axis=1)
        for tap in range(9):
            block = space_ref[9 * layer + tap]
            none = jnp.zeros_like(block)
            for row in range(PHASES):
                blocks = [block if row == col else none for col in range(PHASES)]
                space[tap, row * part : (row + 1) * part, :] = jnp.concatenate(blocks, axis=1)
        block = wide_ref[layer]
        none = jnp.zeros_like(block)
        for row in range(PHASES):
            blocks = [block if row == col else none for col in range(PHASES)]
            wide[row * part : (row + 1) * part, :] = jnp.concatenate(blocks, axis=1)


def to_partners(pieces, axis):
    size = lax.axis_size(axis)
    return [
        lax.ppermute(piece, axis, xor_pairs(size, step + 1)) for step, piece in enumerate(pieces)
    ]


def clip_parts(meta, groups, number):
    lanes = groups[0][0].shape[1]
    lengths = [group[0].shape[0] for group in groups]
    depth = sum(lengths) // number
    total_ins = sum(len(group) for group in groups)

    def kernel(meta_ref, *refs):
        ins, outs, total_ref = list(refs[:total_ins]), refs[total_ins:-1], refs[-1]
        at = 0
        for group, length in zip(groups, lengths):
            mine, ins = ins[: len(group)], ins[len(group) :]
            total = mine[0][...]
            if len(mine) > 1:
                total = total.astype(F32)
                for ref in mine[1:]:
                    total = total + ref[...].astype(F32)
                total = total.astype(BF16)
            total_ref[at : at + length, :] = total
            at += length
        for step, out in enumerate(outs):
            start = pl.multiple_of((meta_ref[4] ^ step) * depth, 16) if number > 1 else 0
            out[...] = total_ref[pl.ds(start, depth), :]
            out.send()

    return run(
        kernel,
        [((depth, lanes), BF16, "hbm")] * number,
        smem=(meta,),
        saved=[part for group in groups for part in group],
        scratch=(pltpu.VMEM((sum(lengths), lanes), BF16),),
    )


def add_low(first, *others):
    total = first.astype(F32)
    for other in others:
        total = total + other.astype(F32)
    return total.astype(BF16)


def on_device(
    slow_input,
    fast_input,
    slow_cotangent,
    fast_cotangent,
    clip_counts,
    lateral_weight,
    slow_reduce_one,
    slow_spatial_one,
    slow_expand_one,
    slow_shortcut_one,
    fast_reduce_one,
    fast_spatial_one,
    fast_expand_one,
    slow_reduce_two,
    slow_spatial_two,
    slow_expand_two,
    fast_reduce_two,
    fast_spatial_two,
    fast_expand_two,
    slow_norms_one,
    fast_norms_one,
    slow_norms_two,
    fast_norms_two,
):
    geo = Geometry(slow_input.shape, fast_input.shape)
    rows, groups = geo.rows, geo.groups
    half_rows = rows // 2
    count = lax.axis_size("ha") * lax.axis_size("wa")
    spread = spread_count()
    slow_wide = slow_input.shape[-1]
    fast_wide = PHASES * fast_input.shape[-1]
    wide = slow_wide + fast_wide
    mid = slow_reduce_one.shape[-1]
    fast_part = fast_reduce_one.shape[-1]
    fast_mid = PHASES * fast_part
    small = mid + fast_mid
    lat = lateral_weight.shape[-1]
    blocks = slow_wide // mid

    depth_one = slow_reduce_one.shape[1]
    depth_two = slow_reduce_two.shape[1]
    depth_mid = slow_spatial_one.shape[2]
    depth_lat = lateral_weight.shape[1]
    near = gather_pack([slow_reduce_one.reshape(-1, mid), slow_spatial_one.reshape(-1, mid)])
    far = gather_pack(
        [
            columns(slow_expand_one, mid),
            columns(slow_shortcut_one, mid),
            slow_reduce_two.reshape(-1, mid),
        ]
    )
    last = gather_pack([slow_spatial_two.reshape(-1, mid), columns(slow_expand_two, mid)])
    at_space_one = 3 * depth_one
    at_short = blocks * depth_mid
    at_reduce_two = at_short + blocks * depth_one
    at_space_two = 0
    at_expand_two = 9 * depth_mid
    fast_shards_one = (fast_reduce_one, fast_spatial_one, fast_expand_one)
    fast_shards_two = (fast_reduce_two, fast_spatial_two, fast_expand_two)
    compact = early_gather(fast_shards_one, fast_shards_two, lateral_weight)
    structured = [
        ((fast_wide, fast_mid), BF16, "hbm"),
        ((fast_wide // PHASES, fast_mid), BF16, "hbm"),
        ((fast_wide // PHASES, fast_mid), BF16, "hbm"),
        ((9, fast_mid, fast_mid), BF16, "hbm"),
        ((fast_mid, fast_wide), BF16, "hbm"),
    ]
    joint_outs = [((2, lanes), F32, "hbm") for lanes in (small, small, wide)]
    prepared = run(
        prepare_kernel,
        structured * 2
        + [((lateral_weight.shape[0], fast_wide // PHASES, lat), BF16, "hbm")]
        + joint_outs * 2
        + [((2, slow_wide), F32, "hbm")],
        vmem=(*compact, slow_norms_one, fast_norms_one, slow_norms_two, fast_norms_two),
    )
    fast_one, fast_two, lateral = prepared[:5], prepared[5:10], prepared[10]
    params_one, params_two, params_short = prepared[11:14], prepared[14:17], prepared[17]

    held = clip_counts[0]
    clips = direct_sum(jnp.full((1, 128), held, F32), "clips")[0, 0]
    positions = clips * (SUB * geo.frames * count)
    inv_n = jnp.stack([1.0 / positions, 1.0 / (positions * PHASES)])
    ha, wa = lax.axis_index("ha"), lax.axis_index("wa")
    last_ha = jnp.full_like(ha, lax.axis_size("ha") - 1)
    meta = jnp.stack([held * geo.frames, ha, wa, last_ha, lax.axis_index("clips")])
    scalars = (meta, inv_n)

    slow_x = slow_input.reshape(rows, slow_wide)
    fast_x = split_phases(fast_input)
    cot = jnp.concatenate(
        [slow_cotangent.reshape(rows, slow_wide), split_phases(fast_cotangent)], axis=1
    )
    message_out = [((rows, small), BF16, "hbm"), ((2 * EDGE, small), BF16, "hbm")]
    stats_small = ((spread, 2, small), F32, "spread")
    stats_wide = ((spread, 2, wide), F32, "spread")
    stats_both = ((2, wide + slow_wide), F32, "vmem")
    small_out = ((rows, small), F32, "hbm")
    wide_out = ((rows, wide), F32, "hbm")
    small_both = ((rows, small), F32, "both")
    small_next = ((rows, small), F32, "vmem")
    wide_low = ((rows, wide), BF16, "hbm")

    def lateral_kernel(x_ref, k_ref, main_ref, before_ref, after_ref, united_ref, fast_ref):
        lanes = x_ref.shape[1] // PHASES
        x = x_ref[...]
        main = dot(x[:, : 3 * lanes], k_ref[2:5].reshape(3 * lanes, lat))
        past = dot(x[:, 2 * lanes :], k_ref[0:2].reshape(2 * lanes, lat))
        united_ref[...] = (main + geo.shift(past, 1)).astype(BF16)
        fast_ref[...] = fast_conv(geo, x, main_ref[...], before_ref[...], after_ref[...])

    united, za_fast = run(
        lateral_kernel,
        [((rows, lat), BF16, "hbm"), ((rows, fast_mid), F32, "hbm")],
        saved=(fast_x, lateral, *fast_one[:3]),
    )

    def reduce_one_kernel(
        meta_ref, x_ref, united_ref, fast_ref, loads, za_ref, stats_ref, message_ref, edge_ref
    ):
        weights = [loads.get(tap) for tap in range(3)]
        za = time_conv(geo, (x_ref[...], united_ref[...]), weights)
        za = jnp.concatenate([za, fast_ref[...]], axis=1)
        za_ref[...] = za
        za_ref.send()
        za = geo.three(za)
        put_message(za, message_ref, edge_ref, meta_ref, geo.width)
        put_forward(stats_ref, za, meta_ref[0])

    za_one, za_next, stats, message, edges = run(
        reduce_one_kernel,
        [small_both, stats_small, *message_out],
        smem=(meta,),
        saved=(slow_x, united, za_fast),
        weights=((near, 0, 3, depth_one),),
    )
    parts_a1 = exchange(stats)
    halo_one = exchange_halo(message, edges)

    def space_stage(za, parts_a, halo, params, gathered, offset, fast_w):
        def kernel(
            meta_ref,
            inv_ref,
            stats_ref,
            za_ref,
            side_ref,
            up_ref,
            down_ref,
            params_ref,
            fast_ref,
            loads,
            zb_ref,
            hidden_ref,
            out_stats,
        ):
            scale, shift, _, _ = affine(stats_ref, params_ref, inv_ref, mid)

            def act(value):
                return silu(geo.three(value.astype(F32)) * scale + shift)

            own = act(za_ref[...])
            up, down = from_above_and_below(up_ref, down_ref, meta_ref)
            side = side_ref[...].astype(F32)
            edges = jnp.concatenate([up[half_rows:], side, down[half_rows:]], axis=0)
            hidden_ref[...] = geo.flat(own).astype(BF16)
            hidden_ref.send()
            near_by = Neighbours(
                own,
                act(up[:half_rows]),
                act(down[:half_rows]),
                geo.flat(act(edges)),
                meta_ref,
                geo.width,
            )
            slow = fast = None
            for tap in range(9):
                moved = geo.flat(near_by.at(tap // 3 - 1, tap % 3 - 1)).astype(BF16)
                slow_term = dot(moved[:, :mid], loads.get(tap))
                fast_term = dot(moved[:, mid:], fast_ref[tap])
                slow = slow_term if slow is None else slow + slow_term
                fast = fast_term if fast is None else fast + fast_term
            zb = jnp.concatenate([slow, fast], axis=1)
            zb_ref[...] = zb
            zb_ref.send()
            put_forward(out_stats, geo.three(zb), meta_ref[0])

        zb, zb_next, hidden, stats, stats_a = run(
            kernel,
            [small_both, ((rows, small), BF16, "hbm"), stats_small],
            smem=scalars,
            parts=(parts_a,),
            vmem=(za,),
            saved=(*halo, params, fast_w),
            weights=((gathered, offset, 9, depth_mid),),
        )
        return zb, zb_next, hidden, exchange(stats), stats_a

    zb_one, zb_next, ha_one, parts_b1, stats_a1 = space_stage(
        za_next, parts_a1, halo_one, params_one[0], near, at_space_one, fast_one[3]
    )

    def expand_body(
        inv_ref, stats_ref, zb_ref, params_ref, fast_ref, hidden_ref, low_ref, zc_ref, loads
    ):
        scale, shift, _, _ = affine(stats_ref, params_ref, inv_ref, mid)
        hidden = geo.flat(silu(geo.three(zb_ref[...]) * scale + shift)).astype(BF16)
        hidden_ref[...] = hidden
        hidden_ref.send()
        zc_ref[:, slow_wide:] = dot(hidden[:, mid:], fast_ref[...])
        for block in range(blocks):
            zc_ref[:, block * mid : (block + 1) * mid] = dot(hidden[:, :mid], loads.get(block))
        low_ref[...] = zc_ref[...].astype(BF16)
        low_ref.send()

    def expand_one_kernel(
        meta_ref,
        inv_ref,
        stats_ref,
        zb_ref,
        params_ref,
        fast_ref,
        x_ref,
        united_ref,
        loads,
        shorts,
        hidden_ref,
        low_ref,
        short_low_ref,
        out_stats,
        zc_ref,
        short_ref,
    ):
        expand_body(
            inv_ref, stats_ref, zb_ref, params_ref, fast_ref, hidden_ref, low_ref, zc_ref, loads
        )
        put_forward(out_stats, geo.three(zc_ref[...]), meta_ref[0])
        for block in range(blocks):
            weight = shorts.get(block)
            value = dot(x_ref[...], weight[:slow_wide]) + dot(united_ref[...], weight[slow_wide:])
            short_ref[:, block * mid : (block + 1) * mid] = value
            put_forward(out_stats, geo.three(value), meta_ref[0], wide + block * mid)
        short_low_ref[...] = short_ref[...].astype(BF16)
        short_low_ref.send()

    hb_one, zc_one, short, stats, stats_b1 = run(
        expand_one_kernel,
        [
            ((rows, small), BF16, "hbm"),
            wide_low,
            ((rows, slow_wide), BF16, "hbm"),
            stats_both,
        ],
        scratch=(pltpu.VMEM((rows, wide), F32), pltpu.VMEM((rows, slow_wide), F32)),
        smem=scalars,
        parts=(parts_b1,),
        vmem=(zb_next,),
        saved=(params_one[1], fast_one[4], slow_x, united),
        weights=((far, 0, blocks, depth_mid), (far, at_short, blocks, depth_one)),
    )
    parts_c1 = exchange_widest(stats)

    def reduce_two_kernel(
        meta_ref,
        inv_ref,
        stats_ref,
        zc_ref,
        short_ref,
        params_ref,
        short_params_ref,
        x_ref,
        main_ref,
        before_ref,
        after_ref,
        loads,
        sum_ref,
        low_ref,
        za_ref,
        out_stats,
        message_ref,
        edge_ref,
    ):
        scale, shift, _, _ = affine(stats_ref, params_ref, inv_ref, slow_wide, 0, wide)
        scale_s, shift_s, _, _ = affine(
            stats_ref, short_params_ref, inv_ref, slow_wide, wide, wide + slow_wide
        )
        normed = geo.three(zc_ref[...].astype(F32)) * scale + shift
        slow = normed[..., :slow_wide] + (
            geo.three(short_ref[...].astype(F32)) * scale_s + shift_s
        )
        fast = normed[..., slow_wide:] + geo.three(x_ref[...].astype(F32))
        total = jnp.concatenate([slow, fast], axis=-1)
        sum_ref[...] = geo.flat(total).astype(BF16)
        sum_ref.send()
        low = geo.flat(silu(total)).astype(BF16)
        low_ref[...] = low
        low_ref.send()
        weights = [loads.get(tap) for tap in range(3)]
        za = time_conv(geo, (low[:, :slow_wide],), weights)
        fast_za = fast_conv(
            geo, low[:, slow_wide:], main_ref[...], before_ref[...], after_ref[...]
        )
        za = jnp.concatenate([za, fast_za], axis=1)
        za_ref[...] = za
        za_ref.send()
        za = geo.three(za)
        put_message(za, message_ref, edge_ref, meta_ref, geo.width)
        put_forward(out_stats, za, meta_ref[0])

    sum_one, low_one, za_two, za_next, stats, message, edges, stats_c1 = run(
        reduce_two_kernel,
        [wide_low, wide_low, small_both, stats_small, *message_out],
        smem=scalars,
        parts=(parts_c1,),
        saved=(zc_one, short, params_one[2], params_short, fast_x, *fast_two[:3]),
        weights=((far, at_reduce_two, 3, depth_two),),
    )
    parts_a2 = exchange(stats)
    halo_two = exchange_halo(message, edges)
    zb_two, zb_next, ha_two, parts_b2, stats_a2 = space_stage(
        za_next, parts_a2, halo_two, params_two[0], last, at_space_two, fast_two[3]
    )

    def expand_two_kernel(
        meta_ref,
        inv_ref,
        stats_ref,
        zb_ref,
        params_ref,
        fast_ref,
        loads,
        hidden_ref,
        low_ref,
        out_stats,
        zc_ref,
    ):
        expand_body(
            inv_ref, stats_ref, zb_ref, params_ref, fast_ref, hidden_ref, low_ref, zc_ref, loads
        )
        put_forward(out_stats, geo.three(zc_ref[...]), meta_ref[0])

    hb_two, zc_two, stats, stats_b2 = run(
        expand_two_kernel,
        [((rows, small), BF16, "hbm"), wide_low, stats_wide],
        scratch=(pltpu.VMEM((rows, wide), F32),),
        smem=scalars,
        parts=(parts_b2,),
        vmem=(zb_next,),
        saved=(params_two[1], fast_two[4]),
        weights=((last, at_expand_two, blocks, depth_mid),),
    )
    parts_c2 = exchange(stats)

    def head_kernel(
        meta_ref,
        inv_ref,
        stats_ref,
        zc_ref,
        params_ref,
        sum_ref,
        cot_ref,
        out_ref,
        low_ref,
        sums_ref,
    ):
        scale, shift, mean, inv = affine(stats_ref, params_ref, inv_ref, slow_wide)
        zc = geo.three(zc_ref[...].astype(F32))
        total = zc * scale + shift + silu(geo.three(sum_ref[...].astype(F32)))
        valid = mask_groups(total.shape, meta_ref[0])
        sigma = jax.nn.sigmoid(total)
        out_ref[...] = geo.flat(jnp.where(valid, total * sigma, 0.0)).astype(BF16)
        slopes = sigma * (1.0 + total * (1.0 - sigma))
        gradient = jnp.where(valid, geo.three(cot_ref[...].astype(F32)) * slopes, 0.0)
        out_ref.send()
        low_ref[...] = geo.flat(gradient).astype(BF16)
        low_ref.send()
        put_back(sums_ref, gradient, (zc - mean) * inv)

    outputs, g_two, sums, stats_c2 = run(
        head_kernel,
        [((rows, wide), BF16, "hbm"), wide_low, stats_wide],
        smem=scalars,
        parts=(parts_c2,),
        saved=(zc_two, params_two[2], sum_one, cot),
    )
    parts_c2 = exchange(sums)

    def norm_back(gradient, value, coeffs, sums, valid):
        scale, _, mean, inv = coeffs
        crossed = (value - mean) * inv * sums[0] + sums[1]
        return scale * (gradient - jnp.where(valid, crossed, 0.0))

    def expand_back_body(
        meta_ref,
        inv_ref,
        sums_ref,
        g_ref,
        stats_ref,
        stats_b_ref,
        zc_ref,
        params_ref,
        zb_ref,
        params_b_ref,
        fast_ref,
        loads,
        gz_ref,
        g_out,
        sums_out,
        message_ref,
        edge_ref,
    ):
        limit = meta_ref[0]
        coeffs = affine(stats_ref, params_ref, inv_ref, slow_wide, 0, wide)
        both = [back_rows(sums_ref, inv_ref, slow_wide, row, 0, wide) for row in range(2)]
        gradient = geo.three(g_ref[...].astype(F32))
        gz = norm_back(
            gradient,
            geo.three(zc_ref[...].astype(F32)),
            coeffs,
            both,
            mask_groups(gradient.shape, limit),
        )
        gz = geo.flat(gz).astype(BF16)
        gz_ref[...] = gz
        gz_ref.send()
        fast = dot_nt(gz[:, slow_wide:], fast_ref[...])
        slow = None
        for block in range(blocks):
            term = dot_nt(gz[:, block * mid : (block + 1) * mid], loads.get(block))
            slow = term if slow is None else slow + term
        scale, shift, mean, inv = affine(stats_b_ref, params_b_ref, inv_ref, mid)
        zb = geo.three(zb_ref[...])
        back = geo.three(jnp.concatenate([slow, fast], axis=1)) * slope(zb * scale + shift)
        g_out[...] = geo.flat(back)
        put_message(
            jnp.concatenate([back, zb], axis=-1), message_ref, edge_ref, meta_ref, geo.width
        )
        masked = jnp.where(mask_groups(back.shape, limit), back, 0.0)
        put_back(sums_out, masked, (zb - mean) * inv)
        return gradient

    message_back = [((rows, 2 * small), BF16, "hbm"), ((2 * EDGE, 2 * small), BF16, "hbm")]
    gz_c2, g_b2, sums, message, edges, sums_c2 = run(
        expand_back_body,
        [((rows, wide), BF16, "hbm"), small_next, stats_small, *message_back],
        smem=scalars,
        parts=(parts_c2,),
        saved=(g_two, stats_c2, stats_b2, zc_two, params_two[2], zb_two, params_two[1], fast_two[4]),
        weights=((last, at_expand_two, blocks, depth_mid),),
    )
    parts_b2 = exchange(sums)
    halo_back_two = exchange_halo(message, edges)
    align = 16 * lax.axis_size("clips")

    def aligned(number):
        return number + -number % align


    lanes_fast = fast_wide // PHASES
    fast_rows_count = fast_reduce_one.shape[1] + 2 * SUB

    def expand_grad(hb_ref, gz_ref, out_ref, at):
        for block in range(blocks):
            value = dot_tn(hb_ref[:, :mid], gz_ref[:, block * mid : (block + 1) * mid])
            low = at + block * depth_mid
            out_ref[:, low : low + depth_mid, :] = value.astype(BF16).reshape(
                count, depth_mid, mid
            )
        if isinstance(out_ref, Store):
            out_ref.send_rows(at, at + blocks * depth_mid)

    def fast_expand_grad(hb_ref, gz_ref):
        fast = dot_tn(hb_ref[:, mid:], gz_ref[:, slow_wide:])
        total = None
        for phase in range(PHASES):
            part = fast[
                phase * fast_part : (phase + 1) * fast_part,
                phase * lanes_fast : (phase + 1) * lanes_fast,
            ]
            total = part if total is None else total + part
        return total

    def space_grad(ha_ref, taps_ref, out_ref, at):
        fast_grads = []
        for tap in range(9):
            value = dot_tn(ha_ref[:, :mid], taps_ref[tap, :, :mid])
            low = at + tap * depth_mid
            out_ref[:, low : low + depth_mid, :] = value.astype(BF16).reshape(
                count, depth_mid, mid
            )
            fast = dot_tn(ha_ref[:, mid:], taps_ref[tap, :, mid:])
            total = None
            for phase in range(PHASES):
                part = lane_block(
                    fast[phase * fast_part : (phase + 1) * fast_part], phase, fast_part
                )
                total = part if total is None else total + part
            fast_grads.append(total)
        if isinstance(out_ref, Store):
            out_ref.send_rows(at, at + 9 * depth_mid)
        return fast_grads

    def put_fast(reduce, space, expand, out_ref, at):
        lane = lax.broadcasted_iota(jnp.int32, reduce[0].shape, 1)

        def beside(parts):
            keep = lane[: parts[0].shape[0]]
            total = None
            for place, part in enumerate(parts):
                part = jnp.where(keep < fast_part, part, 0.0)
                part = pltpu.roll(part, place * fast_part, 1) if place else part
                total = part if total is None else total + part
            return total

        depth = reduce[0].shape[0] // count
        taps = beside(reduce).astype(BF16).reshape(count, depth, lanes_fast)
        out_ref[:, at : at + depth, :] = jnp.concatenate([taps, jnp.zeros_like(taps)], axis=-1)

        def spread(value):
            tiles = value.reshape(count // 2, SUB, lanes_fast)
            return jnp.stack([tiles, pltpu.roll(tiles, SUB // 2, 1)], axis=1).reshape(
                count, SUB, lanes_fast
            )

        first = jnp.concatenate([spread(beside(space[0:4])), spread(beside(space[4:8]))], axis=-1)
        second = jnp.concatenate([spread(beside(space[8:9])), spread(expand)], axis=-1)
        both = jnp.concatenate([first, second], axis=1).astype(BF16)
        out_ref[:, at + depth : at + depth + 2 * SUB, :] = both
        if isinstance(out_ref, Store):
            out_ref.send_rows(at, at + depth + 2 * SUB)

    def space_back_stage(
        g, zb, za, halo, stats_b, parts_b, params_b, stats_a, params_a, g_hbm, at, fast_w
    ):
        def kernel(
            meta_ref,
            inv_ref,
            sums_b_ref,
            g_ref,
            side_ref,
            up_ref,
            down_ref,
            stats_b_ref,
            stats_a_ref,
            zb_ref,
            za_ref,
            params_b_ref,
            params_a_ref,
            fast_ref,
            loads,
            taps_ref,
            g_out,
            sums_out,
        ):
            limit = meta_ref[0]
            coeffs = affine(stats_b_ref, params_b_ref, inv_ref, mid)
            both = [back_rows(sums_b_ref, inv_ref, mid, row) for row in range(2)]

            def back(gradient, value, valid):
                return norm_back(gradient, value, coeffs, both, valid)

            def halo_back(value, scale):
                value = geo.three(value.astype(F32))
                valid = mask_groups(value[..., :small].shape, limit, scale)
                return back(value[..., :small], value[..., small:], valid)

            def edge_back(value):
                value = geo.three(value.astype(F32))
                shape = value[..., :small].shape
                group = lax.broadcasted_iota(jnp.int32, shape, 0) * SUB % EDGE
                group = group + lax.broadcasted_iota(jnp.int32, shape, 1)
                return geo.flat(back(value[..., :small], value[..., small:], group < limit))

            own, zb = geo.three(g_ref[...]), geo.three(zb_ref[...])
            up, down = from_above_and_below(up_ref, down_ref, meta_ref)
            side = side_ref[...].astype(F32)
            edges = jnp.concatenate([up[half_rows:], side, down[half_rows:]], axis=0)

            near_by = Neighbours(
                back(own, zb, mask_groups(own.shape, limit)),
                halo_back(up[:half_rows], 2),
                halo_back(down[:half_rows], 2),
                edge_back(edges),
                meta_ref,
                geo.width,
            )
            slow = fast = None
            for tap in range(9):
                moved = geo.flat(near_by.at(1 - tap // 3, 1 - tap % 3)).astype(BF16)
                taps_ref[tap] = moved
                if tap == 8:
                    taps_ref.send()
                slow_term = dot_nt(moved[:, :mid], loads.get(tap))
                fast_term = dot_nt(moved[:, mid:], fast_ref[tap])
                slow = slow_term if slow is None else slow + slow_term
                fast = fast_term if fast is None else fast + fast_term
            scale, shift, mean, inv = affine(stats_a_ref, params_a_ref, inv_ref, mid)
            za = geo.three(za_ref[...])
            result = geo.three(jnp.concatenate([slow, fast], axis=1)) * slope(za * scale + shift)
            g_out[...] = geo.flat(result)
            masked = jnp.where(mask_groups(result.shape, limit), result, 0.0)
            put_back(sums_out, masked, (za - mean) * inv)

        taps, g, sums, sums_b = run(
            kernel,
            [((9, rows, small), BF16, "hbm"), small_next, stats_small],
            smem=scalars,
            parts=(parts_b,),
            vmem=(g,),
            saved=(*halo, stats_b, stats_a, zb, za, params_b, params_a, fast_w),
            weights=((g_hbm, at, 9, depth_mid),),
        )
        return taps, g, exchange(sums), sums_b

    taps_two, g_a2, parts_a2, sums_b2 = space_back_stage(
        g_b2,
        zb_two,
        za_two,
        halo_back_two,
        stats_b2,
        parts_b2,
        params_two[1],
        stats_a2,
        params_two[0],
        last,
        at_space_two,
        fast_two[3],
    )
    def grads_two_kernel(hb_ref, gz_ref, ha_ref, taps_ref, out_ref, fast_out):
        space = space_grad(ha_ref, taps_ref, out_ref, 0)
        expand_grad(hb_ref, gz_ref, out_ref, 9 * depth_mid)
        for tap in range(9):
            fast_out[tap] = space[tap]
        fast_out[9] = fast_expand_grad(hb_ref, gz_ref)

    rows_space = aligned((9 + blocks) * depth_mid)
    packed_space, fast_space_two = run(
        grads_two_kernel,
        [((count, rows_space, mid), BF16, "rows"), ((10, fast_part, lanes_fast), F32, "hbm")],
        saved=(hb_two, gz_c2, ha_two, taps_two),
    )
    sum_space = lax.psum_scatter(packed_space, TILE, scatter_dimension=0, tiled=False)

    def reduce_gz(meta_ref, inv_ref, g_ref, za_ref, stats_ref, sums_ref, params_ref, steps_ref):
        coeffs = affine(stats_ref, params_ref, inv_ref, mid)
        both = [back_rows(sums_ref, inv_ref, mid, row) for row in range(2)]
        gradient = geo.three(g_ref[...])
        gz = norm_back(
            gradient,
            geo.three(za_ref[...]),
            coeffs,
            both,
            mask_groups(gradient.shape, meta_ref[0]),
        )
        gz = geo.flat(gz)
        steps = [geo.shift(gz, -1).astype(BF16), gz.astype(BF16), geo.shift(gz, 1).astype(BF16)]
        for tap in range(3):
            steps_ref[tap] = steps[tap]
        steps_ref.send()
        return steps

    def reduce_back_two_kernel(
        meta_ref,
        inv_ref,
        sums_ref,
        g_ref,
        stats_ref,
        stats_c_ref,
        za_ref,
        params_ref,
        g_two_ref,
        sum_ref,
        zc_ref,
        short_ref,
        main_ref,
        before_ref,
        after_ref,
        loads,
        steps_ref,
        fast_out,
        g_out,
        sums_out,
    ):
        steps = reduce_gz(
            meta_ref, inv_ref, g_ref, za_ref, stats_ref, sums_ref, params_ref, steps_ref
        )
        slow = None
        for tap in range(3):
            term = dot_nt(steps[tap][:, :mid], loads.get(tap))
            slow = term if slow is None else slow + term
        fast = fast_conv_back(
            [step[:, mid:] for step in steps], main_ref[...], before_ref[...], after_ref[...]
        )
        back = jnp.concatenate([slow, fast], axis=1) + g_two_ref[...].astype(F32)
        back = back * slope(sum_ref[...].astype(F32))
        g_out[...] = back.astype(BF16)
        g_out.send()
        fast_out[...] = back[:, slow_wide:]
        fast_out.send()
        back = geo.three(back)
        masked = jnp.where(mask_groups(back.shape, meta_ref[0]), back, 0.0)
        mean, inv = moments(stats_c_ref, inv_ref, slow_wide, 0, wide)
        put_back(sums_out, masked, (geo.three(zc_ref[...].astype(F32)) - mean) * inv)
        mean, inv = moments(stats_c_ref, inv_ref, slow_wide, wide, wide + slow_wide)
        masked = masked[..., :slow_wide]
        put_back(sums_out, masked, (geo.three(short_ref[...].astype(F32)) - mean) * inv, wide)

    steps_two, g_one_fast, g_one, sums, sums_a2 = run(
        reduce_back_two_kernel,
        [
            ((3, rows, small), BF16, "hbm"),
            ((rows, fast_wide), F32, "hbm"),
            wide_low,
            stats_both,
        ],
        smem=scalars,
        parts=(parts_a2,),
        vmem=(g_a2,),
        saved=(stats_a2, stats_c1, za_two, params_two[0], g_two, sum_one, zc_one, short, *fast_two[:3]),
        weights=((far, at_reduce_two, 3, depth_two),),
    )
    parts_c1 = exchange_widest(sums)

    def expand_back_one_kernel(*refs):
        *body, short_ref, short_params_ref, loads, gz_ref, g_out, sums_out, message, edge, gs_ref = (
            refs
        )
        gradient = expand_back_body(*body, loads, gz_ref, g_out, sums_out, message, edge)
        meta_ref, inv_ref, sums_ref, _, stats_ref = body[:5]
        low, high = wide, wide + slow_wide
        coeffs = affine(stats_ref, short_params_ref, inv_ref, slow_wide, low, high)
        both = [back_rows(sums_ref, inv_ref, slow_wide, row, low, high) for row in range(2)]
        gradient = gradient[..., :slow_wide]
        valid = mask_groups(gradient.shape, meta_ref[0])
        gs = norm_back(gradient, geo.three(short_ref[...].astype(F32)), coeffs, both, valid)
        gs_ref[...] = geo.flat(gs).astype(BF16)

    gz_c1, g_b1, sums, message, edges, gz_short, sums_c1 = run(
        expand_back_one_kernel,
        [((rows, wide), BF16, "hbm"), small_next, stats_small, *message_back]
        + [((rows, slow_wide), BF16, "hbm")],
        smem=scalars,
        parts=(parts_c1,),
        saved=(g_one, stats_c1, stats_b1, zc_one, params_one[2], zb_one, params_one[1], fast_one[4])
        + (short, params_short),
        weights=((far, 0, blocks, depth_mid),),
    )
    parts_b1 = exchange(sums)
    halo_back_one = exchange_halo(message, edges)
    joined_lanes = slow_wide + lat

    def grads_mid_kernel(
        x_ref,
        united_ref,
        gs_ref,
        hb_ref,
        gz_ref,
        low_ref,
        steps_ref,
        fast_ref,
        loads,
        out_ref,
        back_ref,
    ):
        for tap in range(3):
            value = dot_tn(low_ref[:, :slow_wide], steps_ref[tap, :, :mid])
            out_ref[:, tap * depth_two : (tap + 1) * depth_two, :] = value.astype(BF16).reshape(
                count, depth_two, mid
            )
        at = 3 * depth_two
        out_ref.send_rows(0, at)
        reduce = fast_reduce_grad(
            low_ref[:, slow_wide:], [steps_ref[tap, :, mid:] for tap in range(3)]
        )
        put_fast(reduce, [fast_ref[tap] for tap in range(9)], fast_ref[9], out_ref, at)
        at += fast_rows_count
        expand_grad(hb_ref, gz_ref, out_ref, at + blocks * depth_one)
        for block in range(blocks):
            gs = gs_ref[:, block * mid : (block + 1) * mid]
            value = jnp.concatenate([dot_tn(x_ref[...], gs), dot_tn(united_ref[...], gs)], axis=0)
            low = at + block * depth_one
            out_ref[:, low : low + depth_one, :] = value.astype(BF16).reshape(
                count, depth_one, mid
            )
            out_ref.send_rows(low, low + depth_one)
        for block in range(blocks):
            gs = gs_ref[:, block * mid : (block + 1) * mid]
            term = dot_nt(gs, loads.get(block))
            back_ref[...] = term if block == 0 else back_ref[...] + term

    rows_mid = aligned(3 * depth_two + fast_rows_count + blocks * (depth_one + depth_mid))
    packed_mid, short_back = run(
        grads_mid_kernel,
        [((count, rows_mid, mid), BF16, "rows"), ((rows, joined_lanes), F32, "hbm")],
        saved=(slow_x, united, gz_short, hb_one, gz_c1, low_one, steps_two, fast_space_two),
        weights=((far, at_short, blocks, depth_one),),
    )
    sum_mid = lax.psum_scatter(packed_mid, TILE, scatter_dimension=0, tiled=False)

    taps_one, g_a1, parts_a1, sums_b1 = space_back_stage(
        g_b1,
        zb_one,
        za_one,
        halo_back_one,
        stats_b1,
        parts_b1,
        params_one[1],
        stats_a1,
        params_one[0],
        near,
        at_space_one,
        fast_one[3],
    )
    def last_kernel(
        meta_ref,
        inv_ref,
        sums_ref,
        g_ref,
        stats_ref,
        za_ref,
        params_ref,
        g_one_ref,
        short_ref,
        lateral_ref,
        main_ref,
        before_ref,
        after_ref,
        loads,
        steps_ref,
        slow_ref,
        fast_ref,
        united_ref,
    ):
        steps = reduce_gz(
            meta_ref, inv_ref, g_ref, za_ref, stats_ref, sums_ref, params_ref, steps_ref
        )
        joined = short_ref[...]
        for tap in range(3):
            joined = joined + dot_nt(steps[tap][:, :mid], loads.get(tap))
        slow_ref[...] = joined[:, :slow_wide]
        tail = joined[:, slow_wide:]
        now, past = tail.astype(BF16), geo.shift(tail, -1).astype(BF16)
        united_ref[0] = now
        united_ref[1] = past
        lanes = fast_wide // PHASES
        fast = fast_conv_back(
            [step[:, mid:] for step in steps], main_ref[...], before_ref[...], after_ref[...]
        )
        fast = fast + g_one_ref[...]
        front = dot_nt(now, lateral_ref[2:5].reshape(3 * lanes, lat))
        back = dot_nt(past, lateral_ref[0:2].reshape(2 * lanes, lat))
        fast_ref[:, : 2 * lanes] = fast[:, : 2 * lanes] + front[:, : 2 * lanes]
        fast_ref[:, 2 * lanes : 3 * lanes] = (
            fast[:, 2 * lanes : 3 * lanes] + front[:, 2 * lanes :] + back[:, :lanes]
        )
        fast_ref[:, 3 * lanes :] = fast[:, 3 * lanes :] + back[:, lanes:]

    steps_one, grad_slow, grad_fast, united_low, sums_a1 = run(
        last_kernel,
        [
            ((3, rows, small), BF16, "hbm"),
            ((rows, slow_wide), F32, "hbm"),
            ((rows, fast_wide), F32, "hbm"),
            ((2, rows, lat), BF16, "hbm"),
        ],
        smem=scalars,
        parts=(parts_a1,),
        vmem=(g_a1,),
        saved=(stats_a1, za_one, params_one[0], g_one_fast, short_back, lateral, *fast_one[:3]),
        weights=((near, 0, 3, depth_one),),
    )

    def grads_one_kernel(
        meta_ref,
        steps_ref,
        low_ref,
        x_ref,
        united_ref,
        fast_x_ref,
        ha_ref,
        taps_ref,
        hb_ref,
        gz_ref,
        own_ref,
        send_ref,
        out_ref,
        sems,
    ):
        lanes = fast_wide // PHASES
        for tap in range(3):
            step = steps_ref[tap, :, :mid]
            value = jnp.concatenate(
                [dot_tn(x_ref[...], step), dot_tn(united_ref[...], step)], axis=0
            )
            out_ref[:, tap * depth_one : (tap + 1) * depth_one, :] = value.astype(BF16).reshape(
                count, depth_one, mid
            )
        at = 3 * depth_one
        place = (own_ref, send_ref, meta_ref[1], meta_ref[2], sems)
        put_blocks(out_ref, 0, at, *place, 0)
        past = dot_tn(fast_x_ref[:, 2 * lanes :], low_ref[1])
        now = dot_tn(fast_x_ref[:, : 3 * lanes], low_ref[0])
        both = jnp.concatenate([past, now], axis=0).astype(BF16)
        for tap in range(5):
            out_ref[:, at + tap * depth_lat : at + (tap + 1) * depth_lat, :] = both[
                tap * lanes : (tap + 1) * lanes
            ].reshape(count, depth_lat, lat)
        at += 5 * depth_lat
        space = space_grad(ha_ref, taps_ref, out_ref, at)
        at += 9 * depth_mid
        reduce = fast_reduce_grad(
            fast_x_ref[...], [steps_ref[tap, :, mid:] for tap in range(3)]
        )
        put_fast(reduce, space, fast_expand_grad(hb_ref, gz_ref), out_ref, at)

        put_blocks(out_ref, 3 * depth_one, rows_late, *place, 1)
        for low, top, turn in ((0, 3 * depth_one, 0), (3 * depth_one, rows_late, 1)):
            rows_part = pl.ds(low, top - low)
            for block in range(count):
                source, target = out_ref.at[block, rows_part, :], own_ref.at[0, rows_part, :]
                pltpu.make_async_copy(source, target, sems.at[turn, block]).wait()

    def put_blocks(blocks_ref, low, top, own_ref, send_ref, ha, wa, sems, turn):
        rows_part = pl.ds(low, top - low)
        for block in range(count):
            place, col = ha ^ (block // 2), block % 2
            source, sem = blocks_ref.at[block, rows_part, :], sems.at[turn, block]

            @pl.when(wa == col)
            def _():
                pltpu.make_async_copy(source, own_ref.at[place, rows_part, :], sem).start()

            @pl.when(wa != col)
            def _():
                pltpu.make_async_copy(source, send_ref.at[place, rows_part, :], sem).start()

    high = count // 2
    rows_one = 3 * depth_one + 5 * depth_lat + 9 * depth_mid + fast_rows_count
    rows_late = aligned(rows_one)
    blocks_out = ((high, rows_late, mid), BF16, "raw")
    own_blocks, send_blocks = run(
        grads_one_kernel,
        [blocks_out, blocks_out],
        smem=(meta,),
        saved=(steps_one, united_low, slow_x, united, fast_x, ha_one, taps_one, hb_one, gz_c1),
        scratch=(
            pltpu.VMEM((count, rows_late, mid), BF16),
            pltpu.SemaphoreType.DMA((2, count)),
        ),
    )
    side_blocks = lax.ppermute(send_blocks, "wa", xor_pairs(2, 1))

    def chip_kernel(own_ref, side_ref, *out_refs):
        for place in range(high):
            total = own_ref[place].astype(F32) + side_ref[place].astype(F32)
            out_refs[place][...] = total.astype(BF16)
            out_refs[place].send()

    late_out = ((rows_late, mid), BF16, "hbm")
    chip_sums = run(chip_kernel, [late_out] * high, saved=(own_blocks, side_blocks))
    early = jnp.concatenate([sum_space, sum_mid])
    chip_sums, early = lax.optimization_barrier((chip_sums, early))
    late = [chip_sums[0]] + to_partners(chip_sums[1:], "ha")
    four = lax.axis_size("clips") == 4
    parts_early = [lax.psum(early, "clips")]
    quarters = clip_parts(meta, [late], 4 if four else 1)
    if four:
        total_late = add_low(quarters[0], *to_partners(quarters[1:], "clips"))
        parts_late = [total_late] + to_partners([total_late] * 3, "clips")
    else:
        parts_late = [lax.psum(quarters[0], "clips")]

    def finish(*jobs):
        outs_all = []
        for _, groups in jobs:
            for _, shapes in groups:
                for shape in shapes:
                    outs_all += list(shape) if isinstance(shape[0], tuple) else [shape]
        number = sum(len(parts) for parts, _ in jobs)
        deepest = max(sum(rows_group for rows_group, _ in groups) for _, groups in jobs)

        def kernel(meta_ref, *refs):
            ins, outs, total_ref = list(refs[:number]), list(refs[number:-1]), refs[-1]
            for parts, groups in jobs:
                mine, ins = ins[: len(parts)], ins[len(parts) :]
                one_job(meta_ref, mine, outs, total_ref, groups)

        def one_job(meta_ref, ins, outs, total_ref, groups):
            size = len(ins)
            depth = sum(rows_group for rows_group, _ in groups) // size
            base = 0
            for step, ref in enumerate(ins):
                start = pl.multiple_of((meta_ref[4] ^ step) * depth, 16) if size > 1 else 0
                total_ref[pl.ds(start, depth), :] = ref[...].astype(F32)
            for rows_group, shapes in groups:
                at = base
                for shape in shapes:
                    if isinstance(shape[0], tuple):
                        reduce, space, expand = outs.pop(0), outs.pop(0), outs.pop(0)
                        rows_tap, lanes = reduce.shape[1:]
                        for tap in range(3):
                            reduce[tap] = total_ref[
                                at : at + rows_tap, tap * lanes : (tap + 1) * lanes
                            ]
                        few = space.shape[2]
                        for tap in range(9):
                            row = at + rows_tap + tap // SUB * SUB
                            lane = tap % SUB * lanes
                            space[tap // 3, tap % 3] = total_ref[
                                row : row + few, lane : lane + lanes
                            ]
                        row = at + rows_tap + SUB
                        expand[...] = total_ref[row : row + few, expand.shape[1] :]
                        for out in (reduce, space, expand):
                            out.send()
                        at += rows_tap + 2 * SUB
                        continue
                    out = outs.pop(0)
                    if len(shape) == 2 and shape[1] > mid:
                        for block in range(shape[1] // mid):
                            out[:, block * mid : (block + 1) * mid] = total_ref[
                                at : at + shape[0], :
                            ]
                            at += shape[0]
                    else:
                        number = 1
                        for length in shape[:-1]:
                            number *= length
                        out[...] = total_ref[at : at + number, :].reshape(shape)
                        at += number
                    out.send()
                base += rows_group

        return run(
            kernel,
            [(shape, F32, "hbm") for shape in outs_all],
            smem=(meta,),
            saved=[part for parts, _ in jobs for part in parts],
            scratch=(pltpu.VMEM((deepest, mid), F32),),
        )

    shapes_one = tuple(shard.shape for shard in fast_shards_one)
    shapes_two = tuple(shard.shape for shard in fast_shards_two)
    groups_early = [
        (rows_space, [slow_spatial_two.shape, slow_expand_two.shape]),
        (
            rows_mid,
            [slow_reduce_two.shape, shapes_two, slow_shortcut_one.shape, slow_expand_one.shape],
        ),
    ]
    groups_late = [
        (
            rows_late,
            [slow_reduce_one.shape, lateral_weight.shape, slow_spatial_one.shape, shapes_one],
        )
    ]
    finished = finish((parts_early, groups_early), (parts_late, groups_late))
    grad_slow_spatial_two, grad_slow_expand_two, grad_slow_reduce_two = finished[:3]
    fast_two_grads, (grad_slow_shortcut, grad_slow_expand_one) = finished[3:6], finished[6:8]
    grad_slow_reduce_one, grad_lateral, grad_slow_spatial_one, *fast_one_grads = finished[8:]

    def norm_grads(first, second, third):
        slow = [first[:, :mid], second[:, :mid], third[:, :slow_wide]]
        fast = [first[:, mid:], second[:, mid:], third[:, slow_wide:wide]]
        fast = [jnp.sum(part.reshape(2, PHASES, -1), axis=1) for part in fast]
        return slow, fast

    slow_one_p, fast_one_p = norm_grads(sums_a1, sums_b1, sums_c1)
    slow_two_p, fast_two_p = norm_grads(sums_a2, sums_b2, sums_c2)
    grad_slow_norms_one = jnp.concatenate(slow_one_p + [sums_c1[:, wide:]], axis=1)
    grad_slow_norms_two = jnp.concatenate(slow_two_p, axis=1)
    grad_fast_norms_one = jnp.concatenate(fast_one_p, axis=1)
    grad_fast_norms_two = jnp.concatenate(fast_two_p, axis=1)
    return (
        outputs[:, :slow_wide].reshape(slow_input.shape),
        join_phases(outputs[:, slow_wide:], fast_input.shape),
        grad_slow.reshape(slow_input.shape),
        join_phases(grad_fast, fast_input.shape),
        grad_lateral,
        grad_slow_reduce_one,
        grad_slow_spatial_one,
        grad_slow_expand_one,
        grad_slow_shortcut,
        *fast_one_grads,
        grad_slow_reduce_two,
        grad_slow_spatial_two,
        grad_slow_expand_two,
        *fast_two_grads,
        grad_slow_norms_one,
        grad_fast_norms_one,
        grad_slow_norms_two,
        grad_fast_norms_two,
    )


def solution(mesh):
    in_specs = (
        P("clips", None, "ha", "wa", None),
        P("clips", None, "ha", "wa", None),
        P("clips", None, "ha", "wa", None),
        P("clips", None, "ha", "wa", None),
        P("clips"),
        P(None, ("ha", "wa"), None),
        P(None, ("ha", "wa"), None),
        P(None, None, ("ha", "wa"), None),
        P(("ha", "wa"), None),
        P(("ha", "wa"), None),
        P(None, ("ha", "wa"), None),
        P(None, None, ("ha", "wa"), None),
        P(("ha", "wa"), None),
        P(None, ("ha", "wa"), None),
        P(None, None, ("ha", "wa"), None),
        P(("ha", "wa"), None),
        P(None, ("ha", "wa"), None),
        P(None, None, ("ha", "wa"), None),
        P(("ha", "wa"), None),
        P(),
        P(),
        P(),
        P(),
    )
    out_specs = (
        P("clips", None, "ha", "wa", None),
        P("clips", None, "ha", "wa", None),
        P("clips", None, "ha", "wa", None),
        P("clips", None, "ha", "wa", None),
        P(None, ("ha", "wa"), None),
        P(None, ("ha", "wa"), None),
        P(None, None, ("ha", "wa"), None),
        P(("ha", "wa"), None),
        P(("ha", "wa"), None),
        P(None, ("ha", "wa"), None),
        P(None, None, ("ha", "wa"), None),
        P(("ha", "wa"), None),
        P(None, ("ha", "wa"), None),
        P(None, None, ("ha", "wa"), None),
        P(("ha", "wa"), None),
        P(None, ("ha", "wa"), None),
        P(None, None, ("ha", "wa"), None),
        P(("ha", "wa"), None),
        P(),
        P(),
        P(),
        P(),
    )
    return jax.shard_map(
        on_device, mesh=mesh, in_specs=in_specs, out_specs=out_specs, check_vma=False
    )
```

```python
import jax
import jax.numpy as jnp
from jax import lax
from jax.experimental import pallas as pl
from jax.experimental.pallas import tpu as pltpu
from jax.sharding import PartitionSpec as P

epsilon = 1e-05
F32 = jnp.float32
BF16 = jnp.bfloat16
TILE = ("ha", "wa")
PHASES = 4
SUB = 8


def dot(left, right):
    return lax.dot_general(left, right, (((1,), (0,)), ((), ())), preferred_element_type=F32)


def dot_tn(left, right):
    return lax.dot_general(left, right, (((0,), (0,)), ((), ())), preferred_element_type=F32)


def dot_nt(left, right):
    return lax.dot_general(left, right, (((1,), (1,)), ((), ())), preferred_element_type=F32)


class Keep:
    def __init__(self, ref):
        self.scratch, self.shape = ref, ref.shape

    def send(self):
        pass

    def __setitem__(self, index, value):
        self.scratch[index] = value

    def __getitem__(self, index):
        return self.scratch[index]


class Loads:
    def __init__(self, source, offset, target, sems, first):
        self.copies = []
        depth = target.shape[2]
        for step in range(target.shape[0]):
            copy = pltpu.make_async_copy(
                source.at[:, pl.ds(offset + step * depth, depth), :],
                target.at[step],
                sems.at[first + step],
            )
            copy.start()
            self.copies.append(copy)
        self.target = target

    def get(self, step):
        self.copies[step].wait()
        block = self.target[step]
        return block.reshape(-1, block.shape[-1])


class Saved:
    def __init__(self, source, scratch, sem):
        self.scratch, self.shape = scratch, scratch.shape
        self.copy = pltpu.make_async_copy(source, scratch, sem)
        self.copy.start()
        self.ready = False

    def wait(self):
        if not self.ready:
            self.copy.wait()
            self.ready = True

    def __getitem__(self, index):
        self.wait()
        return self.scratch[index]


SEGMENTS = 8


class Store:
    def __init__(self, scratch, target, sems):
        self.scratch, self.target, self.shape = scratch, target, scratch.shape
        self.sems, self.copies = sems, []

    def send(self):
        self.copies.append(pltpu.make_async_copy(self.scratch, self.target, self.sems[0]))
        self.copies[-1].start()

    def send_rows(self, low, high):
        rows = pl.ds(low, high - low)
        source, target = self.scratch.at[:, rows, :], self.target.at[:, rows, :]
        self.copies.append(pltpu.make_async_copy(source, target, self.sems[len(self.copies)]))
        self.copies[-1].start()

    def __setitem__(self, index, value):
        self.scratch[index] = value

    def __getitem__(self, index):
        return self.scratch[index]


CLOSE = 320 * 1024


def run(body, outs, smem=(), parts=(), vmem=(), saved=(), weights=(), scratch=(), limit=53):
    near = pl.BlockSpec(memory_space=pltpu.VMEM)
    far = pl.BlockSpec(memory_space=pltpu.HBM)
    sources = []
    for array, *_ in weights:
        if not any(array is other for other in sources):
            sources.append(array)
    outs = list(outs) + [(part.shape[1:], part.dtype, "hbm") for part in parts]
    flat = []
    twice = []
    for at, (shape, dtype, kind) in enumerate(outs):
        size = jnp.dtype(dtype).itemsize
        for length in shape:
            size *= length
        twice.append(kind == "both" and size <= CLOSE)
        if kind in ("hbm", "both") and size <= CLOSE:
            outs[at] = (shape, dtype, "vmem")
    for shape, dtype, kind in outs:
        flat += [(shape, dtype, "raw"), (shape, dtype, "vmem")] if kind == "both" else [(shape, dtype, kind)]
    close = [array.size * array.dtype.itemsize <= CLOSE for array in saved]
    held = [pltpu.VMEM(array.shape, array.dtype) for array, here in zip(saved, close) if not here]
    for array, _, steps, depth in weights:
        held.append(pltpu.VMEM((steps, array.shape[0], depth, array.shape[2]), array.dtype))
    for shape, dtype, kind in outs:
        if kind in ("hbm", "rows"):
            held.append(pltpu.VMEM(shape, dtype))
        elif kind == "spread":
            held.append(pltpu.VMEM(shape[1:], dtype))
    sems = len(saved) + sum(steps for _, _, steps, _ in weights) + len(outs)
    sems += SEGMENTS * sum(kind == "rows" for _, _, kind in outs)
    held.append(pltpu.SemaphoreType.DMA((sems,)))

    def kernel(*refs):
        refs = list(refs)

        def take(number):
            taken = refs[:number]
            del refs[:number]
            return taken

        smem_refs, part_refs, vmem_refs = take(len(smem)), take(len(parts)), take(len(vmem))
        saved_refs, source_refs, out_refs = take(len(saved)), take(len(sources)), take(len(flat))
        saved_scratch, weight_scratch = take(len(saved) - sum(close)), take(len(weights))
        out_scratch = take(sum(kind in ("hbm", "rows", "spread") for _, _, kind in outs))
        sem, more = refs[0], refs[1:]
        arrays, copies = [], []
        for source, here in zip(saved_refs, close):
            if not here:
                copies.append(Saved(source, saved_scratch[len(copies)], sem.at[len(copies)]))
            arrays.append(source if here else copies[-1])
        at = len(saved)
        loads = []
        for (array, offset, steps, _), target in zip(weights, weight_scratch):
            place = [array is other for other in sources].index(True)
            loads.append(Loads(source_refs[place], offset, target, sem, at))
            at += steps
        results, stores, spreads = [], [], []
        for _, _, kind in outs:
            ref = out_refs.pop(0)
            if kind == "both":
                stores.append(Store(out_refs.pop(0), ref, [sem.at[at]]))
                at += 1
                results.append(stores[-1])
            elif kind in ("hbm", "rows"):
                number = SEGMENTS if kind == "rows" else 1
                stores.append(
                    Store(out_scratch.pop(0), ref, [sem.at[at + part] for part in range(number)])
                )
                at += number
                results.append(stores[-1])
            elif kind == "spread":
                spreads.append((out_scratch.pop(0), ref))
                results.append(spreads[-1][0])
            elif kind == "vmem":
                results.append(Keep(ref))
            else:
                results.append(ref)
        sums = results[len(results) - len(parts) :]
        results = results[: len(results) - len(parts)]
        for part, total in zip(part_refs, sums):
            total[...] = jnp.sum(part[...], axis=0)
            total.send()
        totals = [total.scratch for total in sums]
        body(*smem_refs, *totals, *vmem_refs, *arrays, *loads, *results, *more)
        for copy in copies:
            copy.wait()
        for store in stores:
            if not store.copies:
                store.send()
        for value, ref in spreads:
            ref[...] = jnp.broadcast_to(value[...][None], ref.shape)
        for store in stores:
            for copy in store.copies:
                copy.wait()

    results = pl.pallas_call(
        kernel,
        out_shape=[jax.ShapeDtypeStruct(shape, dtype) for shape, dtype, _ in flat],
        in_specs=[pl.BlockSpec(memory_space=pltpu.SMEM)] * len(smem)
        + [near] * (len(parts) + len(vmem))
        + [near if here else far for here in close]
        + [far] * len(sources),
        out_specs=[far if kind in ("hbm", "rows", "raw") else near for _, _, kind in flat],
        scratch_shapes=held + list(scratch),
        compiler_params=pltpu.CompilerParams(vmem_limit_bytes=limit * 1024 * 1024),
        cost_estimate=pl.CostEstimate(
            flops=2_000_000_000, bytes_accessed=16_000_000, transcendentals=0
        ),
    )(*smem, *parts, *vmem, *saved, *sources)
    returned = []
    for (_, _, kind), double in zip(outs, twice):
        taken, results = results[: 2 if kind == "both" else 1], results[2 if kind == "both" else 1 :]
        returned += list(taken) * (2 if double else 1)
    return returned


class Geometry:
    def __init__(self, slow_shape, fast_shape):
        self.cap, self.frames, self.height, self.width = slow_shape[:4]
        self.groups = self.cap * self.frames
        self.rows = self.groups * SUB

    def three(self, value):
        return value.reshape(-1, SUB, value.shape[-1])

    def flat(self, value):
        return value.reshape(-1, value.shape[-1])

    def shift(self, value, step):
        lanes = value.shape[-1]
        whole = value.reshape(self.cap, self.frames, SUB, lanes)
        zero = jnp.zeros((self.cap, 1, SUB, lanes), value.dtype)
        if step > 0:
            whole = jnp.concatenate([zero, whole[:, :-1]], axis=1)
        else:
            whole = jnp.concatenate([whole[:, 1:], zero], axis=1)
        return whole.reshape(-1, lanes)


def mask_groups(shape, limit, scale=1):
    return lax.broadcasted_iota(jnp.int32, shape, 0) * scale < limit


def rep(ref, row, low, high):
    return jnp.broadcast_to(ref[row : row + 1, low:high], (SUB, high - low))


def fold(value, slow):
    fast = value[:, slow:]
    lanes = fast.shape[-1]
    if lanes * PHASES <= slow:
        return jnp.concatenate([value[:, :slow]] + [fast] * PHASES, axis=1)
    total = fast
    for phase in range(1, PHASES):
        total = total + pltpu.roll(fast, phase * (lanes // PHASES), 1)
    return jnp.concatenate([value[:, :slow], total], axis=1)


def lane_counts(inv_ref, lanes, slow):
    lane = lax.broadcasted_iota(jnp.int32, (SUB, lanes), 1)
    return jnp.where(lane < slow, inv_ref[0], inv_ref[1])


def moments(stats, inv_ref, slow, low=0, high=None):
    high = stats.shape[1] if high is None else high
    total, square = rep(stats, 0, low, high), rep(stats, 1, low, high)
    if slow < high - low:
        total, square = fold(total, slow), fold(square, slow)
    inv_n = lane_counts(inv_ref, total.shape[1], slow)
    mean = total * inv_n
    return mean, lax.rsqrt(square * inv_n - mean * mean + epsilon)


def affine(stats, params, inv_ref, slow, low=0, high=None):
    mean, inv = moments(stats, inv_ref, slow, low, high)
    lanes = mean.shape[1]
    scale = (1.0 + rep(params, 0, 0, lanes)) * inv
    return scale, rep(params, 1, 0, lanes) - mean * scale, mean, inv


def back_rows(sums, inv_ref, slow, row, low=0, high=None):
    high = sums.shape[1] if high is None else high
    total = rep(sums, row, low, high)
    if slow < high - low:
        total = fold(total, slow)
    return total * lane_counts(inv_ref, total.shape[1], slow)


def silu(value):
    return value * jax.nn.sigmoid(value)


def slope(value):
    sigma = jax.nn.sigmoid(value)
    return sigma * (1.0 + value * (1.0 - sigma))


def put_stats(ref, first, second, low=0, slow=None):
    for row, value in enumerate((first, second)):
        total = jnp.sum(jnp.sum(value, axis=0), axis=0, keepdims=True)
        if slow is not None:
            part = (total.shape[1] - slow) // PHASES
            fast = total[:, slow : slow + part]
            for phase in range(1, PHASES):
                fast = fast + total[:, slow + phase * part : slow + (phase + 1) * part]
            total = jnp.concatenate([total[:, :slow], fast], axis=1)
        ref[row : row + 1, low : low + total.shape[1]] = total


def put_back(ref, gradient, normal, low=0, slow=None):
    put_stats(ref, gradient * normal, gradient, low, slow)


def put_forward(ref, value, limit, low=0, slow=None):
    masked = jnp.where(mask_groups(value.shape, limit), value, 0.0)
    put_stats(ref, masked, masked * value, low, slow)


EDGE = 32


def edge_place(wa, width):
    return jnp.where(wa > 0, 0, width - 1)


def put_message(value, ref, edge_ref, meta_ref, width):
    lanes = value.shape[-1]
    pairs = value.reshape(-1, 2, SUB, lanes)
    first, second = pairs[:, 0], pairs[:, 1]
    near = lax.broadcasted_iota(jnp.int32, first.shape, 1) < SUB // 2
    top = jnp.where(near, first, pltpu.roll(second, SUB // 2, 1))
    bottom = jnp.where(near, pltpu.roll(first, SUB // 2, 1), second)
    flat = value.reshape(-1, lanes).astype(BF16)
    shape = (2 * EDGE, flat.shape[0])
    row, col = [lax.broadcasted_iota(jnp.int32, shape, dim) for dim in range(2)]
    low = row >= EDGE
    source = (row - jnp.where(low, EDGE, 0)) * SUB + jnp.where(low, SUB // 2, 0)
    chosen = (col == source + edge_place(meta_ref[2], width)).astype(F32).astype(BF16)
    edges = dot(chosen, flat)
    edge_ref[...] = edges.astype(BF16)
    edge_ref.send()
    top, bottom = [part.reshape(-1, lanes).astype(BF16) for part in (top, bottom)]
    ref[: top.shape[0]] = top
    ref[top.shape[0] :] = bottom
    ref.send()


def unpack_bottom(value):
    both = jnp.stack([pltpu.roll(value, SUB // 2, 1), value], axis=1)
    return both.reshape(-1, SUB, value.shape[-1])


def unpack_top(value):
    both = jnp.stack([value, pltpu.roll(value, SUB // 2, 1)], axis=1)
    return both.reshape(-1, SUB, value.shape[-1])


class Neighbours:
    def __init__(self, own, up, down, edges, meta, width):
        half = SUB // 2
        near = lax.broadcasted_iota(jnp.int32, own.shape, 1) < half
        self.col = lax.broadcasted_iota(jnp.int32, own.shape, 1) % width
        self.width, self.shape = width, own.shape
        ha, wa, last = meta[1], meta[2], meta[3]
        up = unpack_bottom(jnp.where(ha > 0, up, 0.0))
        down = unpack_top(jnp.where(ha < last, down, 0.0))
        self.rows = {
            0: own,
            -1: pltpu.roll(jnp.where(near, own, up), half, 1),
            1: pltpu.roll(jnp.where(near, down, own), half, 1),
        }
        beyond = lax.broadcasted_iota(jnp.int32, edges.shape, 0)
        inside = ((ha > 0) | (beyond >= EDGE)) & ((ha < last) | (beyond < 3 * EDGE))
        self.edges = jnp.where(inside, edges, 0.0).astype(BF16)
        shape = (own.shape[0] * SUB, edges.shape[0])
        place, self.source = [lax.broadcasted_iota(jnp.int32, shape, dim) for dim in range(2)]
        self.group = place // SUB
        self.row = place // half % 2
        self.touches = place % width == edge_place(wa, width)
        self.sides = {}

    def side(self, row_step):
        if row_step not in self.sides:
            wanted = (self.row + row_step + 1) * EDGE + self.group
            chosen = ((self.source == wanted) & self.touches).astype(F32).astype(BF16)
            self.sides[row_step] = dot(chosen, self.edges).reshape(self.shape)
        return self.sides[row_step]

    def at(self, row_step, col_step):
        base = self.rows[row_step]
        if col_step < 0:
            return jnp.where(self.col == 0, self.side(row_step), pltpu.roll(base, 1, 1))
        if col_step > 0:
            away = self.col == self.width - 1
            return jnp.where(away, self.side(row_step), pltpu.roll(base, SUB - 1, 1))
        return base


def xor_pairs(size, step):
    return [(index, index ^ step) for index in range(size)]


def direct_sum(value, axis):
    size = lax.axis_size(axis)
    step = 1
    while step < size:
        if size // step >= 4:
            one, two, three = [
                lax.ppermute(value, axis, xor_pairs(size, step * times)) for times in (1, 2, 3)
            ]
            value = (value + two) + (one + three)
            step *= 4
        else:
            value = value + lax.ppermute(value, axis, xor_pairs(size, step))
            step *= 2
    return value


AXES = ("clips", "ha", "wa")
MOST = 32


def spread_count():
    count = lax.axis_size("ha") * lax.axis_size("wa")
    whole = count * lax.axis_size("clips")
    return whole if whole <= MOST else count


def exchange(copies):
    if copies.shape[0] == lax.axis_size("clips") * lax.axis_size("ha") * lax.axis_size("wa"):
        return lax.all_to_all(copies, AXES, 0, 0)
    return lax.all_to_all(direct_sum(copies, "clips"), TILE, 0, 0)


def exchange_widest(sums):
    count = lax.axis_size("ha") * lax.axis_size("wa")
    sums = direct_sum(sums, "clips")
    return lax.all_to_all(jnp.broadcast_to(sums[None], (count,) + sums.shape), TILE, 0, 0)


def exchange_halo(message, edges):
    wide, high = lax.axis_size("wa"), lax.axis_size("ha")
    half = message.shape[0] // 2
    side = lax.ppermute(edges, "wa", xor_pairs(wide, 1))
    odd = lax.axis_index("ha") % 2 == 1
    tops = jnp.concatenate([message[:half], side[:EDGE]], axis=0)
    bottoms = jnp.concatenate([message[half:], side[EDGE:]], axis=0)
    first = lax.ppermute(jnp.where(odd, tops, bottoms), "ha", xor_pairs(high, 1))
    pairs = [(row, row + 1) for row in range(1, high - 1, 2)]
    pairs = pairs + [(low, row) for row, low in pairs]
    second = lax.ppermute(jnp.where(odd, bottoms, tops), "ha", pairs)
    return side, first, second


def from_above_and_below(first_ref, second_ref, meta_ref):
    first, second = first_ref[...].astype(F32), second_ref[...].astype(F32)
    odd = meta_ref[1] % 2 == 1
    return jnp.where(odd, first, second), jnp.where(odd, second, first)


def time_conv(geo, parts, blocks):
    result = None
    for tap in range(3):
        at = 0
        total = None
        for part in parts:
            lanes = part.shape[-1]
            term = dot(part, blocks[tap][at : at + lanes])
            at += lanes
            total = term if total is None else total + term
        if tap != 1:
            total = geo.shift(total, 1 - tap)
        result = total if result is None else result + total
    return result


def fast_conv(geo, value, main, before, after):
    lanes = value.shape[-1] // PHASES
    result = dot(value, main)
    result = result + geo.shift(dot(value[:, -lanes:], before), 1)
    return result + geo.shift(dot(value[:, :lanes], after), -1)


def fast_conv_back(steps, main, before, after):
    lanes = before.shape[0]
    middle = dot_nt(steps[1], main)
    first = middle[:, :lanes] + dot_nt(steps[2], after)
    last = middle[:, -lanes:] + dot_nt(steps[0], before)
    return jnp.concatenate([first, middle[:, lanes:-lanes], last], axis=1)


def lane_block(value, phase, part):
    return pltpu.roll(value, value.shape[-1] - phase * part, 1) if phase else value


def fast_reduce_grad(value, steps):
    lanes = value.shape[-1] // PHASES
    part = steps[1].shape[-1] // PHASES
    main = dot_tn(value, steps[1])
    before = dot_tn(value[:, -lanes:], steps[0])
    after = dot_tn(value[:, :lanes], steps[2])

    def block(row, col):
        return lane_block(main[row * lanes : (row + 1) * lanes], col, part)

    result = []
    for tap in range(3):
        total = before if tap == 0 else None
        if tap == 2:
            total = lane_block(after, PHASES - 1, part)
        for col in range(PHASES):
            row = col + tap - 1
            if 0 <= row < PHASES:
                total = block(row, col) if total is None else total + block(row, col)
        result.append(total)
    return result


def gather_pack(parts):
    return lax.all_gather(jnp.concatenate(parts, axis=0), TILE, axis=0)


def columns(shard, lanes):
    depth, total = shard.shape
    return jnp.moveaxis(shard.reshape(depth, total // lanes, lanes), 1, 0).reshape(-1, lanes)


def split_phases(value):
    cap, frames, height, width, lanes = value.shape
    value = value.reshape(cap, frames // PHASES, PHASES, height, width, lanes)
    return jnp.moveaxis(value, 2, 4).reshape(-1, PHASES * lanes)


def join_phases(value, shape):
    cap, frames, height, width, lanes = shape
    value = value.reshape(cap, frames // PHASES, height, width, PHASES, lanes)
    return jnp.moveaxis(value, 4, 2).reshape(shape)


def early_gather(shards_one, shards_two, lateral):
    rows = []
    lanes = shards_one[2].shape[-1]
    kinds = [jnp.stack(pair) for pair in zip(shards_one, shards_two)]
    kinds.append(jnp.stack([lateral[..., :lanes], lateral[..., lanes:]]))
    for kind in kinds:
        flat = kind.reshape(-1, kind.shape[-1])
        rows.append(jnp.pad(flat, ((0, 0), (0, lanes - flat.shape[-1]))))
    packed = gather_pack(rows)
    result = []
    at = 0
    for kind in kinds:
        depth, width = kind.shape[-2:]
        number = kind.size // width
        part = packed[:, at : at + number, :width].reshape(packed.shape[0], -1, depth, width)
        at += number
        result.append(jnp.moveaxis(part, 0, 1).reshape(part.shape[1], -1, width))
    return result


def prepare_kernel(taps_ref, space_ref, wide_ref, lateral_ref, *refs):
    slow_one, fast_one, slow_two, fast_two, *outs = refs
    part = taps_ref.shape[-1]
    lateral, *joint = outs[10:]
    number = lateral.shape[0]
    for tap in range(number):
        lateral[tap] = jnp.concatenate([lateral_ref[tap], lateral_ref[number + tap]], axis=1)
    for layer, (slow, fast) in enumerate(((slow_one, fast_one), (slow_two, fast_two))):
        at = fast_at = 0
        for ref in joint[3 * layer : 3 * layer + 3]:
            fast_lanes = part if ref.shape[1] < slow.shape[1] // 2 else wide_ref.shape[-1]
            lanes = ref.shape[1] - PHASES * fast_lanes
            values = [slow[:, at : at + lanes]]
            values += [fast[:, fast_at : fast_at + fast_lanes]] * PHASES
            ref[...] = jnp.concatenate(values, axis=1)
            at, fast_at = at + lanes, fast_at + fast_lanes
    joint[6][...] = slow_one[:, slow_one.shape[1] - joint[6].shape[1] :]
    for layer in range(2):
        main, before, after, space, wide = outs[5 * layer : 5 * layer + 5]
        taps = [taps_ref[3 * layer + tap] for tap in range(3)]
        zero = jnp.zeros_like(taps[0])
        lanes = taps[0].shape[0]
        for row in range(PHASES):
            blocks = [
                taps[row - col + 1] if abs(row - col) <= 1 else zero for col in range(PHASES)
            ]
            main[row * lanes : (row + 1) * lanes, :] = jnp.concatenate(blocks, axis=1)
        before[...] = jnp.concatenate([taps[0]] + [zero] * (PHASES - 1), axis=1)
        after[...] = jnp.concatenate([zero] * (PHASES - 1) + [taps[2]], axis=1)
        for tap in range(9):
            block = space_ref[9 * layer + tap]
            none = jnp.zeros_like(block)
            for row in range(PHASES):
                blocks = [block if row == col else none for col in range(PHASES)]
                space[tap, row * part : (row + 1) * part, :] = jnp.concatenate(blocks, axis=1)
        block = wide_ref[layer]
        none = jnp.zeros_like(block)
        for row in range(PHASES):
            blocks = [block if row == col else none for col in range(PHASES)]
            wide[row * part : (row + 1) * part, :] = jnp.concatenate(blocks, axis=1)


def to_partners(pieces, axis):
    size = lax.axis_size(axis)
    return [
        lax.ppermute(piece, axis, xor_pairs(size, step + 1)) for step, piece in enumerate(pieces)
    ]


def clip_parts(meta, groups, number):
    lanes = groups[0][0].shape[1]
    lengths = [group[0].shape[0] for group in groups]
    depth = sum(lengths) // number
    total_ins = sum(len(group) for group in groups)

    def kernel(meta_ref, *refs):
        ins, outs, total_ref = list(refs[:total_ins]), refs[total_ins:-1], refs[-1]
        at = 0
        for group, length in zip(groups, lengths):
            mine, ins = ins[: len(group)], ins[len(group) :]
            total = mine[0][...]
            if len(mine) > 1:
                total = total.astype(F32)
                for ref in mine[1:]:
                    total = total + ref[...].astype(F32)
                total = total.astype(BF16)
            total_ref[at : at + length, :] = total
            at += length
        for step, out in enumerate(outs):
            start = pl.multiple_of((meta_ref[4] ^ step) * depth, 16) if number > 1 else 0
            out[...] = total_ref[pl.ds(start, depth), :]
            out.send()

    return run(
        kernel,
        [((depth, lanes), BF16, "hbm")] * number,
        smem=(meta,),
        saved=[part for group in groups for part in group],
        scratch=(pltpu.VMEM((sum(lengths), lanes), BF16),),
    )


def add_low(first, *others):
    total = first.astype(F32)
    for other in others:
        total = total + other.astype(F32)
    return total.astype(BF16)


def on_device(
    slow_input,
    fast_input,
    slow_cotangent,
    fast_cotangent,
    clip_counts,
    lateral_weight,
    slow_reduce_one,
    slow_spatial_one,
    slow_expand_one,
    slow_shortcut_one,
    fast_reduce_one,
    fast_spatial_one,
    fast_expand_one,
    slow_reduce_two,
    slow_spatial_two,
    slow_expand_two,
    fast_reduce_two,
    fast_spatial_two,
    fast_expand_two,
    slow_norms_one,
    fast_norms_one,
    slow_norms_two,
    fast_norms_two,
):
    geo = Geometry(slow_input.shape, fast_input.shape)
    rows, groups = geo.rows, geo.groups
    half_rows = rows // 2
    count = lax.axis_size("ha") * lax.axis_size("wa")
    spread = spread_count()
    slow_wide = slow_input.shape[-1]
    fast_wide = PHASES * fast_input.shape[-1]
    wide = slow_wide + fast_wide
    packed = slow_wide + fast_wide // PHASES
    mid = slow_reduce_one.shape[-1]
    fast_part = fast_reduce_one.shape[-1]
    fast_mid = PHASES * fast_part
    small = mid + fast_mid
    lat = lateral_weight.shape[-1]
    blocks = slow_wide // mid

    depth_one = slow_reduce_one.shape[1]
    depth_two = slow_reduce_two.shape[1]
    depth_mid = slow_spatial_one.shape[2]
    depth_lat = lateral_weight.shape[1]
    near = gather_pack([slow_reduce_one.reshape(-1, mid), slow_spatial_one.reshape(-1, mid)])
    far = gather_pack(
        [
            columns(slow_expand_one, mid),
            columns(slow_shortcut_one, mid),
            slow_reduce_two.reshape(-1, mid),
        ]
    )
    last = gather_pack([slow_spatial_two.reshape(-1, mid), columns(slow_expand_two, mid)])
    at_space_one = 3 * depth_one
    at_short = blocks * depth_mid
    at_reduce_two = at_short + blocks * depth_one
    at_space_two = 0
    at_expand_two = 9 * depth_mid
    fast_shards_one = (fast_reduce_one, fast_spatial_one, fast_expand_one)
    fast_shards_two = (fast_reduce_two, fast_spatial_two, fast_expand_two)
    compact = early_gather(fast_shards_one, fast_shards_two, lateral_weight)
    structured = [
        ((fast_wide, fast_mid), BF16, "hbm"),
        ((fast_wide // PHASES, fast_mid), BF16, "hbm"),
        ((fast_wide // PHASES, fast_mid), BF16, "hbm"),
        ((9, fast_mid, fast_mid), BF16, "hbm"),
        ((fast_mid, fast_wide), BF16, "hbm"),
    ]
    joint_outs = [((2, lanes), F32, "hbm") for lanes in (small, small, wide)]
    prepared = run(
        prepare_kernel,
        structured * 2
        + [((lateral_weight.shape[0], fast_wide // PHASES, lat), BF16, "hbm")]
        + joint_outs * 2
        + [((2, slow_wide), F32, "hbm")],
        vmem=(*compact, slow_norms_one, fast_norms_one, slow_norms_two, fast_norms_two),
    )
    fast_one, fast_two, lateral = prepared[:5], prepared[5:10], prepared[10]
    params_one, params_two, params_short = prepared[11:14], prepared[14:17], prepared[17]

    held = clip_counts[0]
    clips = direct_sum(jnp.full((1, 128), held, F32), "clips")[0, 0]
    positions = clips * (SUB * geo.frames * count)
    inv_n = jnp.stack([1.0 / positions, 1.0 / (positions * PHASES)])
    ha, wa = lax.axis_index("ha"), lax.axis_index("wa")
    last_ha = jnp.full_like(ha, lax.axis_size("ha") - 1)
    meta = jnp.stack([held * geo.frames, ha, wa, last_ha, lax.axis_index("clips")])
    scalars = (meta, inv_n)

    slow_x = slow_input.reshape(rows, slow_wide)
    fast_x = split_phases(fast_input)
    cot = jnp.concatenate(
        [slow_cotangent.reshape(rows, slow_wide), split_phases(fast_cotangent)], axis=1
    )
    message_out = [((rows, small), BF16, "hbm"), ((2 * EDGE, small), BF16, "hbm")]
    stats_small = ((spread, 2, small), F32, "spread")
    stats_wide = ((spread, 2, packed), F32, "spread")
    stats_both = ((2, packed + slow_wide), F32, "vmem")
    small_out = ((rows, small), F32, "hbm")
    wide_out = ((rows, wide), F32, "hbm")
    small_both = ((rows, small), F32, "both")
    small_next = ((rows, small), F32, "vmem")
    wide_low = ((rows, wide), BF16, "hbm")

    def lateral_kernel(x_ref, k_ref, main_ref, before_ref, after_ref, united_ref, fast_ref):
        lanes = x_ref.shape[1] // PHASES
        x = x_ref[...]
        main = dot(x[:, : 3 * lanes], k_ref[2:5].reshape(3 * lanes, lat))
        past = dot(x[:, 2 * lanes :], k_ref[0:2].reshape(2 * lanes, lat))
        united_ref[...] = (main + geo.shift(past, 1)).astype(BF16)
        fast_ref[...] = fast_conv(geo, x, main_ref[...], before_ref[...], after_ref[...])

    united, za_fast = run(
        lateral_kernel,
        [((rows, lat), BF16, "hbm"), ((rows, fast_mid), F32, "hbm")],
        saved=(fast_x, lateral, *fast_one[:3]),
    )

    def reduce_one_kernel(
        meta_ref, x_ref, united_ref, fast_ref, loads, za_ref, stats_ref, message_ref, edge_ref
    ):
        weights = [loads.get(tap) for tap in range(3)]
        za = time_conv(geo, (x_ref[...], united_ref[...]), weights)
        za = jnp.concatenate([za, fast_ref[...]], axis=1)
        za_ref[...] = za
        za_ref.send()
        za = geo.three(za)
        put_message(za, message_ref, edge_ref, meta_ref, geo.width)
        put_forward(stats_ref, za, meta_ref[0])

    za_one, za_next, stats, message, edges = run(
        reduce_one_kernel,
        [small_both, stats_small, *message_out],
        smem=(meta,),
        saved=(slow_x, united, za_fast),
        weights=((near, 0, 3, depth_one),),
    )
    parts_a1 = exchange(stats)
    halo_one = exchange_halo(message, edges)

    def space_stage(za, parts_a, halo, params, gathered, offset, fast_w):
        def kernel(
            meta_ref,
            inv_ref,
            stats_ref,
            za_ref,
            side_ref,
            up_ref,
            down_ref,
            params_ref,
            fast_ref,
            loads,
            zb_ref,
            hidden_ref,
            out_stats,
        ):
            scale, shift, _, _ = affine(stats_ref, params_ref, inv_ref, mid)

            def act(value):
                return silu(geo.three(value.astype(F32)) * scale + shift)

            own = act(za_ref[...])
            up, down = from_above_and_below(up_ref, down_ref, meta_ref)
            side = side_ref[...].astype(F32)
            edges = jnp.concatenate([up[half_rows:], side, down[half_rows:]], axis=0)
            hidden_ref[...] = geo.flat(own).astype(BF16)
            hidden_ref.send()
            near_by = Neighbours(
                own,
                act(up[:half_rows]),
                act(down[:half_rows]),
                geo.flat(act(edges)),
                meta_ref,
                geo.width,
            )
            slow = fast = None
            for tap in range(9):
                moved = geo.flat(near_by.at(tap // 3 - 1, tap % 3 - 1)).astype(BF16)
                slow_term = dot(moved[:, :mid], loads.get(tap))
                fast_term = dot(moved[:, mid:], fast_ref[tap])
                slow = slow_term if slow is None else slow + slow_term
                fast = fast_term if fast is None else fast + fast_term
            zb = jnp.concatenate([slow, fast], axis=1)
            zb_ref[...] = zb
            zb_ref.send()
            put_forward(out_stats, geo.three(zb), meta_ref[0])

        zb, zb_next, hidden, stats, stats_a = run(
            kernel,
            [small_both, ((rows, small), BF16, "hbm"), stats_small],
            smem=scalars,
            parts=(parts_a,),
            vmem=(za,),
            saved=(*halo, params, fast_w),
            weights=((gathered, offset, 9, depth_mid),),
        )
        return zb, zb_next, hidden, exchange(stats), stats_a

    zb_one, zb_next, ha_one, parts_b1, stats_a1 = space_stage(
        za_next, parts_a1, halo_one, params_one[0], near, at_space_one, fast_one[3]
    )

    def expand_body(
        inv_ref, stats_ref, zb_ref, params_ref, fast_ref, hidden_ref, low_ref, zc_ref, loads
    ):
        scale, shift, _, _ = affine(stats_ref, params_ref, inv_ref, mid)
        hidden = geo.flat(silu(geo.three(zb_ref[...]) * scale + shift)).astype(BF16)
        hidden_ref[...] = hidden
        hidden_ref.send()
        zc_ref[:, slow_wide:] = dot(hidden[:, mid:], fast_ref[...])
        for block in range(blocks):
            zc_ref[:, block * mid : (block + 1) * mid] = dot(hidden[:, :mid], loads.get(block))
        low_ref[...] = zc_ref[...].astype(BF16)
        low_ref.send()

    def expand_one_kernel(
        meta_ref,
        inv_ref,
        stats_ref,
        zb_ref,
        params_ref,
        fast_ref,
        x_ref,
        united_ref,
        loads,
        shorts,
        hidden_ref,
        low_ref,
        short_low_ref,
        out_stats,
        zc_ref,
        short_ref,
    ):
        expand_body(
            inv_ref, stats_ref, zb_ref, params_ref, fast_ref, hidden_ref, low_ref, zc_ref, loads
        )
        put_forward(out_stats, geo.three(zc_ref[...]), meta_ref[0], 0, slow_wide)
        for block in range(blocks):
            weight = shorts.get(block)
            value = dot(x_ref[...], weight[:slow_wide]) + dot(united_ref[...], weight[slow_wide:])
            short_ref[:, block * mid : (block + 1) * mid] = value
            put_forward(out_stats, geo.three(value), meta_ref[0], packed + block * mid)
        short_low_ref[...] = short_ref[...].astype(BF16)
        short_low_ref.send()

    hb_one, zc_one, short, stats, stats_b1 = run(
        expand_one_kernel,
        [
            ((rows, small), BF16, "hbm"),
            wide_low,
            ((rows, slow_wide), BF16, "hbm"),
            stats_both,
        ],
        scratch=(pltpu.VMEM((rows, wide), F32), pltpu.VMEM((rows, slow_wide), F32)),
        smem=scalars,
        parts=(parts_b1,),
        vmem=(zb_next,),
        saved=(params_one[1], fast_one[4], slow_x, united),
        weights=((far, 0, blocks, depth_mid), (far, at_short, blocks, depth_one)),
    )
    parts_c1 = exchange_widest(stats)

    def reduce_two_kernel(
        meta_ref,
        inv_ref,
        stats_ref,
        zc_ref,
        short_ref,
        params_ref,
        short_params_ref,
        x_ref,
        main_ref,
        before_ref,
        after_ref,
        loads,
        sum_ref,
        low_ref,
        za_ref,
        out_stats,
        message_ref,
        edge_ref,
    ):
        scale, shift, _, _ = affine(stats_ref, params_ref, inv_ref, slow_wide, 0, packed)
        scale_s, shift_s, _, _ = affine(
            stats_ref, short_params_ref, inv_ref, slow_wide, packed, packed + slow_wide
        )
        normed = geo.three(zc_ref[...].astype(F32)) * scale + shift
        slow = normed[..., :slow_wide] + (
            geo.three(short_ref[...].astype(F32)) * scale_s + shift_s
        )
        fast = normed[..., slow_wide:] + geo.three(x_ref[...].astype(F32))
        total = jnp.concatenate([slow, fast], axis=-1)
        sum_ref[...] = geo.flat(total).astype(BF16)
        sum_ref.send()
        low = geo.flat(silu(total)).astype(BF16)
        low_ref[...] = low
        low_ref.send()
        weights = [loads.get(tap) for tap in range(3)]
        za = time_conv(geo, (low[:, :slow_wide],), weights)
        fast_za = fast_conv(
            geo, low[:, slow_wide:], main_ref[...], before_ref[...], after_ref[...]
        )
        za = jnp.concatenate([za, fast_za], axis=1)
        za_ref[...] = za
        za_ref.send()
        za = geo.three(za)
        put_message(za, message_ref, edge_ref, meta_ref, geo.width)
        put_forward(out_stats, za, meta_ref[0])

    sum_one, low_one, za_two, za_next, stats, message, edges, stats_c1 = run(
        reduce_two_kernel,
        [wide_low, wide_low, small_both, stats_small, *message_out],
        smem=scalars,
        parts=(parts_c1,),
        saved=(zc_one, short, params_one[2], params_short, fast_x, *fast_two[:3]),
        weights=((far, at_reduce_two, 3, depth_two),),
    )
    parts_a2 = exchange(stats)
    halo_two = exchange_halo(message, edges)
    zb_two, zb_next, ha_two, parts_b2, stats_a2 = space_stage(
        za_next, parts_a2, halo_two, params_two[0], last, at_space_two, fast_two[3]
    )

    def expand_two_kernel(
        meta_ref,
        inv_ref,
        stats_ref,
        zb_ref,
        params_ref,
        fast_ref,
        loads,
        hidden_ref,
        low_ref,
        out_stats,
        zc_ref,
    ):
        expand_body(
            inv_ref, stats_ref, zb_ref, params_ref, fast_ref, hidden_ref, low_ref, zc_ref, loads
        )
        put_forward(out_stats, geo.three(zc_ref[...]), meta_ref[0], 0, slow_wide)

    hb_two, zc_two, stats, stats_b2 = run(
        expand_two_kernel,
        [((rows, small), BF16, "hbm"), wide_low, stats_wide],
        scratch=(pltpu.VMEM((rows, wide), F32),),
        smem=scalars,
        parts=(parts_b2,),
        vmem=(zb_next,),
        saved=(params_two[1], fast_two[4]),
        weights=((last, at_expand_two, blocks, depth_mid),),
    )
    parts_c2 = exchange(stats)

    def head_kernel(
        meta_ref,
        inv_ref,
        stats_ref,
        zc_ref,
        params_ref,
        sum_ref,
        cot_ref,
        out_ref,
        low_ref,
        sums_ref,
    ):
        scale, shift, mean, inv = affine(stats_ref, params_ref, inv_ref, slow_wide)
        zc = geo.three(zc_ref[...].astype(F32))
        total = zc * scale + shift + silu(geo.three(sum_ref[...].astype(F32)))
        valid = mask_groups(total.shape, meta_ref[0])
        sigma = jax.nn.sigmoid(total)
        out_ref[...] = geo.flat(jnp.where(valid, total * sigma, 0.0)).astype(BF16)
        slopes = sigma * (1.0 + total * (1.0 - sigma))
        gradient = jnp.where(valid, geo.three(cot_ref[...].astype(F32)) * slopes, 0.0)
        out_ref.send()
        low_ref[...] = geo.flat(gradient).astype(BF16)
        low_ref.send()
        put_back(sums_ref, gradient, (zc - mean) * inv, 0, slow_wide)

    outputs, g_two, sums, stats_c2 = run(
        head_kernel,
        [((rows, wide), BF16, "hbm"), wide_low, stats_wide],
        smem=scalars,
        parts=(parts_c2,),
        saved=(zc_two, params_two[2], sum_one, cot),
    )
    parts_c2 = exchange(sums)

    def norm_back(gradient, value, coeffs, sums, valid):
        scale, _, mean, inv = coeffs
        crossed = (value - mean) * inv * sums[0] + sums[1]
        return scale * (gradient - jnp.where(valid, crossed, 0.0))

    def expand_back_body(
        meta_ref,
        inv_ref,
        sums_ref,
        g_ref,
        stats_ref,
        stats_b_ref,
        zc_ref,
        params_ref,
        zb_ref,
        params_b_ref,
        fast_ref,
        loads,
        gz_ref,
        g_out,
        sums_out,
        message_ref,
        edge_ref,
    ):
        limit = meta_ref[0]
        coeffs = affine(stats_ref, params_ref, inv_ref, slow_wide, 0, packed)
        both = [back_rows(sums_ref, inv_ref, slow_wide, row, 0, packed) for row in range(2)]
        gradient = geo.three(g_ref[...].astype(F32))
        gz = norm_back(
            gradient,
            geo.three(zc_ref[...].astype(F32)),
            coeffs,
            both,
            mask_groups(gradient.shape, limit),
        )
        gz = geo.flat(gz).astype(BF16)
        gz_ref[...] = gz
        gz_ref.send()
        fast = dot_nt(gz[:, slow_wide:], fast_ref[...])
        slow = None
        for block in range(blocks):
            term = dot_nt(gz[:, block * mid : (block + 1) * mid], loads.get(block))
            slow = term if slow is None else slow + term
        scale, shift, mean, inv = affine(stats_b_ref, params_b_ref, inv_ref, mid)
        zb = geo.three(zb_ref[...])
        back = geo.three(jnp.concatenate([slow, fast], axis=1)) * slope(zb * scale + shift)
        g_out[...] = geo.flat(back)
        put_message(
            jnp.concatenate([back, zb], axis=-1), message_ref, edge_ref, meta_ref, geo.width
        )
        masked = jnp.where(mask_groups(back.shape, limit), back, 0.0)
        put_back(sums_out, masked, (zb - mean) * inv)
        return gradient

    message_back = [((rows, 2 * small), BF16, "hbm"), ((2 * EDGE, 2 * small), BF16, "hbm")]
    gz_c2, g_b2, sums, message, edges, sums_c2 = run(
        expand_back_body,
        [((rows, wide), BF16, "hbm"), small_next, stats_small, *message_back],
        smem=scalars,
        parts=(parts_c2,),
        saved=(g_two, stats_c2, stats_b2, zc_two, params_two[2], zb_two, params_two[1], fast_two[4]),
        weights=((last, at_expand_two, blocks, depth_mid),),
    )
    parts_b2 = exchange(sums)
    halo_back_two = exchange_halo(message, edges)
    align = 16 * lax.axis_size("clips")

    def aligned(number):
        return number + -number % align


    lanes_fast = fast_wide // PHASES
    fast_rows_count = fast_reduce_one.shape[1] + 2 * SUB

    def expand_grad(hb_ref, gz_ref, out_ref, at):
        for block in range(blocks):
            value = dot_tn(hb_ref[:, :mid], gz_ref[:, block * mid : (block + 1) * mid])
            low = at + block * depth_mid
            out_ref[:, low : low + depth_mid, :] = value.astype(BF16).reshape(
                count, depth_mid, mid
            )
        if isinstance(out_ref, Store):
            out_ref.send_rows(at, at + blocks * depth_mid)

    def fast_expand_grad(hb_ref, gz_ref):
        fast = dot_tn(hb_ref[:, mid:], gz_ref[:, slow_wide:])
        total = None
        for phase in range(PHASES):
            part = fast[
                phase * fast_part : (phase + 1) * fast_part,
                phase * lanes_fast : (phase + 1) * lanes_fast,
            ]
            total = part if total is None else total + part
        return total

    def space_grad(ha_ref, taps_ref, out_ref, at):
        fast_grads = []
        for tap in range(9):
            value = dot_tn(ha_ref[:, :mid], taps_ref[tap, :, :mid])
            low = at + tap * depth_mid
            out_ref[:, low : low + depth_mid, :] = value.astype(BF16).reshape(
                count, depth_mid, mid
            )
            fast = dot_tn(ha_ref[:, mid:], taps_ref[tap, :, mid:])
            total = None
            for phase in range(PHASES):
                part = lane_block(
                    fast[phase * fast_part : (phase + 1) * fast_part], phase, fast_part
                )
                total = part if total is None else total + part
            fast_grads.append(total)
        if isinstance(out_ref, Store):
            out_ref.send_rows(at, at + 9 * depth_mid)
        return fast_grads

    def put_fast(reduce, space, expand, out_ref, at):
        lane = lax.broadcasted_iota(jnp.int32, reduce[0].shape, 1)

        def beside(parts):
            keep = lane[: parts[0].shape[0]]
            total = None
            for place, part in enumerate(parts):
                part = jnp.where(keep < fast_part, part, 0.0)
                part = pltpu.roll(part, place * fast_part, 1) if place else part
                total = part if total is None else total + part
            return total

        depth = reduce[0].shape[0] // count
        taps = beside(reduce).astype(BF16).reshape(count, depth, lanes_fast)
        out_ref[:, at : at + depth, :] = jnp.concatenate([taps, jnp.zeros_like(taps)], axis=-1)

        def spread(value):
            tiles = value.reshape(count // 2, SUB, lanes_fast)
            return jnp.stack([tiles, pltpu.roll(tiles, SUB // 2, 1)], axis=1).reshape(
                count, SUB, lanes_fast
            )

        first = jnp.concatenate([spread(beside(space[0:4])), spread(beside(space[4:8]))], axis=-1)
        second = jnp.concatenate([spread(beside(space[8:9])), spread(expand)], axis=-1)
        both = jnp.concatenate([first, second], axis=1).astype(BF16)
        out_ref[:, at + depth : at + depth + 2 * SUB, :] = both
        if isinstance(out_ref, Store):
            out_ref.send_rows(at, at + depth + 2 * SUB)

    def space_back_stage(
        g, zb, za, halo, stats_b, parts_b, params_b, stats_a, params_a, g_hbm, at, fast_w
    ):
        def kernel(
            meta_ref,
            inv_ref,
            sums_b_ref,
            g_ref,
            side_ref,
            up_ref,
            down_ref,
            stats_b_ref,
            stats_a_ref,
            zb_ref,
            za_ref,
            params_b_ref,
            params_a_ref,
            fast_ref,
            loads,
            taps_ref,
            g_out,
            sums_out,
        ):
            limit = meta_ref[0]
            coeffs = affine(stats_b_ref, params_b_ref, inv_ref, mid)
            both = [back_rows(sums_b_ref, inv_ref, mid, row) for row in range(2)]

            def back(gradient, value, valid):
                return norm_back(gradient, value, coeffs, both, valid)

            def halo_back(value, scale):
                value = geo.three(value.astype(F32))
                valid = mask_groups(value[..., :small].shape, limit, scale)
                return back(value[..., :small], value[..., small:], valid)

            def edge_back(value):
                value = geo.three(value.astype(F32))
                shape = value[..., :small].shape
                group = lax.broadcasted_iota(jnp.int32, shape, 0) * SUB % EDGE
                group = group + lax.broadcasted_iota(jnp.int32, shape, 1)
                return geo.flat(back(value[..., :small], value[..., small:], group < limit))

            own, zb = geo.three(g_ref[...]), geo.three(zb_ref[...])
            up, down = from_above_and_below(up_ref, down_ref, meta_ref)
            side = side_ref[...].astype(F32)
            edges = jnp.concatenate([up[half_rows:], side, down[half_rows:]], axis=0)

            near_by = Neighbours(
                back(own, zb, mask_groups(own.shape, limit)),
                halo_back(up[:half_rows], 2),
                halo_back(down[:half_rows], 2),
                edge_back(edges),
                meta_ref,
                geo.width,
            )
            slow = fast = None
            for tap in range(9):
                moved = geo.flat(near_by.at(1 - tap // 3, 1 - tap % 3)).astype(BF16)
                taps_ref[tap] = moved
                if tap == 8:
                    taps_ref.send()
                slow_term = dot_nt(moved[:, :mid], loads.get(tap))
                fast_term = dot_nt(moved[:, mid:], fast_ref[tap])
                slow = slow_term if slow is None else slow + slow_term
                fast = fast_term if fast is None else fast + fast_term
            scale, shift, mean, inv = affine(stats_a_ref, params_a_ref, inv_ref, mid)
            za = geo.three(za_ref[...])
            result = geo.three(jnp.concatenate([slow, fast], axis=1)) * slope(za * scale + shift)
            g_out[...] = geo.flat(result)
            masked = jnp.where(mask_groups(result.shape, limit), result, 0.0)
            put_back(sums_out, masked, (za - mean) * inv)

        taps, g, sums, sums_b = run(
            kernel,
            [((9, rows, small), BF16, "hbm"), small_next, stats_small],
            smem=scalars,
            parts=(parts_b,),
            vmem=(g,),
            saved=(*halo, stats_b, stats_a, zb, za, params_b, params_a, fast_w),
            weights=((g_hbm, at, 9, depth_mid),),
        )
        return taps, g, exchange(sums), sums_b

    taps_two, g_a2, parts_a2, sums_b2 = space_back_stage(
        g_b2,
        zb_two,
        za_two,
        halo_back_two,
        stats_b2,
        parts_b2,
        params_two[1],
        stats_a2,
        params_two[0],
        last,
        at_space_two,
        fast_two[3],
    )
    def grads_two_kernel(hb_ref, gz_ref, ha_ref, taps_ref, out_ref, fast_out):
        space = space_grad(ha_ref, taps_ref, out_ref, 0)
        expand_grad(hb_ref, gz_ref, out_ref, 9 * depth_mid)
        for tap in range(9):
            fast_out[tap] = space[tap]
        fast_out[9] = fast_expand_grad(hb_ref, gz_ref)

    rows_space = aligned((9 + blocks) * depth_mid)
    packed_space, fast_space_two = run(
        grads_two_kernel,
        [((count, rows_space, mid), BF16, "rows"), ((10, fast_part, lanes_fast), F32, "hbm")],
        saved=(hb_two, gz_c2, ha_two, taps_two),
    )
    sum_space = lax.psum_scatter(packed_space, TILE, scatter_dimension=0, tiled=False)

    def reduce_gz(meta_ref, inv_ref, g_ref, za_ref, stats_ref, sums_ref, params_ref, steps_ref):
        coeffs = affine(stats_ref, params_ref, inv_ref, mid)
        both = [back_rows(sums_ref, inv_ref, mid, row) for row in range(2)]
        gradient = geo.three(g_ref[...])
        gz = norm_back(
            gradient,
            geo.three(za_ref[...]),
            coeffs,
            both,
            mask_groups(gradient.shape, meta_ref[0]),
        )
        gz = geo.flat(gz)
        steps = [geo.shift(gz, -1).astype(BF16), gz.astype(BF16), geo.shift(gz, 1).astype(BF16)]
        for tap in range(3):
            steps_ref[tap] = steps[tap]
        steps_ref.send()
        return steps

    def reduce_back_two_kernel(
        meta_ref,
        inv_ref,
        sums_ref,
        g_ref,
        stats_ref,
        stats_c_ref,
        za_ref,
        params_ref,
        g_two_ref,
        sum_ref,
        zc_ref,
        short_ref,
        main_ref,
        before_ref,
        after_ref,
        loads,
        steps_ref,
        fast_out,
        g_out,
        sums_out,
    ):
        steps = reduce_gz(
            meta_ref, inv_ref, g_ref, za_ref, stats_ref, sums_ref, params_ref, steps_ref
        )
        slow = None
        for tap in range(3):
            term = dot_nt(steps[tap][:, :mid], loads.get(tap))
            slow = term if slow is None else slow + term
        fast = fast_conv_back(
            [step[:, mid:] for step in steps], main_ref[...], before_ref[...], after_ref[...]
        )
        back = jnp.concatenate([slow, fast], axis=1) + g_two_ref[...].astype(F32)
        back = back * slope(sum_ref[...].astype(F32))
        g_out[...] = back.astype(BF16)
        g_out.send()
        fast_out[...] = back[:, slow_wide:]
        fast_out.send()
        back = geo.three(back)
        masked = jnp.where(mask_groups(back.shape, meta_ref[0]), back, 0.0)
        mean, inv = moments(stats_c_ref, inv_ref, slow_wide, 0, packed)
        put_back(
            sums_out, masked, (geo.three(zc_ref[...].astype(F32)) - mean) * inv, 0, slow_wide
        )
        mean, inv = moments(stats_c_ref, inv_ref, slow_wide, packed, packed + slow_wide)
        masked = masked[..., :slow_wide]
        put_back(sums_out, masked, (geo.three(short_ref[...].astype(F32)) - mean) * inv, packed)

    steps_two, g_one_fast, g_one, sums, sums_a2 = run(
        reduce_back_two_kernel,
        [
            ((3, rows, small), BF16, "hbm"),
            ((rows, fast_wide), F32, "hbm"),
            wide_low,
            stats_both,
        ],
        smem=scalars,
        parts=(parts_a2,),
        vmem=(g_a2,),
        saved=(stats_a2, stats_c1, za_two, params_two[0], g_two, sum_one, zc_one, short, *fast_two[:3]),
        weights=((far, at_reduce_two, 3, depth_two),),
    )
    parts_c1 = exchange_widest(sums)

    def expand_back_one_kernel(*refs):
        *body, short_ref, short_params_ref, loads, gz_ref, g_out, sums_out, message, edge, gs_ref = (
            refs
        )
        gradient = expand_back_body(*body, loads, gz_ref, g_out, sums_out, message, edge)
        meta_ref, inv_ref, sums_ref, _, stats_ref = body[:5]
        low, high = packed, packed + slow_wide
        coeffs = affine(stats_ref, short_params_ref, inv_ref, slow_wide, low, high)
        both = [back_rows(sums_ref, inv_ref, slow_wide, row, low, high) for row in range(2)]
        gradient = gradient[..., :slow_wide]
        valid = mask_groups(gradient.shape, meta_ref[0])
        gs = norm_back(gradient, geo.three(short_ref[...].astype(F32)), coeffs, both, valid)
        gs_ref[...] = geo.flat(gs).astype(BF16)

    gz_c1, g_b1, sums, message, edges, gz_short, sums_c1 = run(
        expand_back_one_kernel,
        [((rows, wide), BF16, "hbm"), small_next, stats_small, *message_back]
        + [((rows, slow_wide), BF16, "hbm")],
        smem=scalars,
        parts=(parts_c1,),
        saved=(g_one, stats_c1, stats_b1, zc_one, params_one[2], zb_one, params_one[1], fast_one[4])
        + (short, params_short),
        weights=((far, 0, blocks, depth_mid),),
    )
    parts_b1 = exchange(sums)
    halo_back_one = exchange_halo(message, edges)
    joined_lanes = slow_wide + lat

    def grads_mid_kernel(
        x_ref,
        united_ref,
        gs_ref,
        hb_ref,
        gz_ref,
        low_ref,
        steps_ref,
        fast_ref,
        loads,
        out_ref,
        back_ref,
    ):
        for tap in range(3):
            value = dot_tn(low_ref[:, :slow_wide], steps_ref[tap, :, :mid])
            out_ref[:, tap * depth_two : (tap + 1) * depth_two, :] = value.astype(BF16).reshape(
                count, depth_two, mid
            )
        at = 3 * depth_two
        out_ref.send_rows(0, at)
        reduce = fast_reduce_grad(
            low_ref[:, slow_wide:], [steps_ref[tap, :, mid:] for tap in range(3)]
        )
        put_fast(reduce, [fast_ref[tap] for tap in range(9)], fast_ref[9], out_ref, at)
        at += fast_rows_count
        expand_grad(hb_ref, gz_ref, out_ref, at + blocks * depth_one)
        for block in range(blocks):
            gs = gs_ref[:, block * mid : (block + 1) * mid]
            value = jnp.concatenate([dot_tn(x_ref[...], gs), dot_tn(united_ref[...], gs)], axis=0)
            low = at + block * depth_one
            out_ref[:, low : low + depth_one, :] = value.astype(BF16).reshape(
                count, depth_one, mid
            )
            out_ref.send_rows(low, low + depth_one)
        for block in range(blocks):
            gs = gs_ref[:, block * mid : (block + 1) * mid]
            term = dot_nt(gs, loads.get(block))
            back_ref[...] = term if block == 0 else back_ref[...] + term

    rows_mid = aligned(3 * depth_two + fast_rows_count + blocks * (depth_one + depth_mid))
    packed_mid, short_back = run(
        grads_mid_kernel,
        [((count, rows_mid, mid), BF16, "rows"), ((rows, joined_lanes), F32, "hbm")],
        saved=(slow_x, united, gz_short, hb_one, gz_c1, low_one, steps_two, fast_space_two),
        weights=((far, at_short, blocks, depth_one),),
    )
    sum_mid = lax.psum_scatter(packed_mid, TILE, scatter_dimension=0, tiled=False)

    taps_one, g_a1, parts_a1, sums_b1 = space_back_stage(
        g_b1,
        zb_one,
        za_one,
        halo_back_one,
        stats_b1,
        parts_b1,
        params_one[1],
        stats_a1,
        params_one[0],
        near,
        at_space_one,
        fast_one[3],
    )
    def last_kernel(
        meta_ref,
        inv_ref,
        sums_ref,
        g_ref,
        stats_ref,
        za_ref,
        params_ref,
        g_one_ref,
        short_ref,
        lateral_ref,
        main_ref,
        before_ref,
        after_ref,
        loads,
        steps_ref,
        slow_ref,
        fast_ref,
        united_ref,
    ):
        steps = reduce_gz(
            meta_ref, inv_ref, g_ref, za_ref, stats_ref, sums_ref, params_ref, steps_ref
        )
        joined = short_ref[...]
        for tap in range(3):
            joined = joined + dot_nt(steps[tap][:, :mid], loads.get(tap))
        slow_ref[...] = joined[:, :slow_wide]
        tail = joined[:, slow_wide:]
        now, past = tail.astype(BF16), geo.shift(tail, -1).astype(BF16)
        united_ref[0] = now
        united_ref[1] = past
        lanes = fast_wide // PHASES
        fast = fast_conv_back(
            [step[:, mid:] for step in steps], main_ref[...], before_ref[...], after_ref[...]
        )
        fast = fast + g_one_ref[...]
        front = dot_nt(now, lateral_ref[2:5].reshape(3 * lanes, lat))
        back = dot_nt(past, lateral_ref[0:2].reshape(2 * lanes, lat))
        fast_ref[:, : 2 * lanes] = fast[:, : 2 * lanes] + front[:, : 2 * lanes]
        fast_ref[:, 2 * lanes : 3 * lanes] = (
            fast[:, 2 * lanes : 3 * lanes] + front[:, 2 * lanes :] + back[:, :lanes]
        )
        fast_ref[:, 3 * lanes :] = fast[:, 3 * lanes :] + back[:, lanes:]

    steps_one, grad_slow, grad_fast, united_low, sums_a1 = run(
        last_kernel,
        [
            ((3, rows, small), BF16, "hbm"),
            ((rows, slow_wide), F32, "hbm"),
            ((rows, fast_wide), F32, "hbm"),
            ((2, rows, lat), BF16, "hbm"),
        ],
        smem=scalars,
        parts=(parts_a1,),
        vmem=(g_a1,),
        saved=(stats_a1, za_one, params_one[0], g_one_fast, short_back, lateral, *fast_one[:3]),
        weights=((near, 0, 3, depth_one),),
    )

    def grads_one_kernel(
        meta_ref,
        steps_ref,
        low_ref,
        x_ref,
        united_ref,
        fast_x_ref,
        ha_ref,
        taps_ref,
        hb_ref,
        gz_ref,
        own_ref,
        send_ref,
        out_ref,
        sems,
    ):
        lanes = fast_wide // PHASES
        for tap in range(3):
            step = steps_ref[tap, :, :mid]
            value = jnp.concatenate(
                [dot_tn(x_ref[...], step), dot_tn(united_ref[...], step)], axis=0
            )
            out_ref[:, tap * depth_one : (tap + 1) * depth_one, :] = value.astype(BF16).reshape(
                count, depth_one, mid
            )
        at = 3 * depth_one
        place = (own_ref, send_ref, meta_ref[1], meta_ref[2], sems)
        put_blocks(out_ref, 0, at, *place, 0)
        past = dot_tn(fast_x_ref[:, 2 * lanes :], low_ref[1])
        now = dot_tn(fast_x_ref[:, : 3 * lanes], low_ref[0])
        both = jnp.concatenate([past, now], axis=0).astype(BF16)
        for tap in range(5):
            out_ref[:, at + tap * depth_lat : at + (tap + 1) * depth_lat, :] = both[
                tap * lanes : (tap + 1) * lanes
            ].reshape(count, depth_lat, lat)
        at += 5 * depth_lat
        space = space_grad(ha_ref, taps_ref, out_ref, at)
        at += 9 * depth_mid
        reduce = fast_reduce_grad(
            fast_x_ref[...], [steps_ref[tap, :, mid:] for tap in range(3)]
        )
        put_fast(reduce, space, fast_expand_grad(hb_ref, gz_ref), out_ref, at)

        put_blocks(out_ref, 3 * depth_one, rows_late, *place, 1)
        for low, top, turn in ((0, 3 * depth_one, 0), (3 * depth_one, rows_late, 1)):
            rows_part = pl.ds(low, top - low)
            for block in range(count):
                source, target = out_ref.at[block, rows_part, :], own_ref.at[0, rows_part, :]
                pltpu.make_async_copy(source, target, sems.at[turn, block]).wait()

    def put_blocks(blocks_ref, low, top, own_ref, send_ref, ha, wa, sems, turn):
        rows_part = pl.ds(low, top - low)
        for block in range(count):
            place, col = ha ^ (block // 2), block % 2
            source, sem = blocks_ref.at[block, rows_part, :], sems.at[turn, block]

            @pl.when(wa == col)
            def _():
                pltpu.make_async_copy(source, own_ref.at[place, rows_part, :], sem).start()

            @pl.when(wa != col)
            def _():
                pltpu.make_async_copy(source, send_ref.at[place, rows_part, :], sem).start()

    high = count // 2
    rows_one = 3 * depth_one + 5 * depth_lat + 9 * depth_mid + fast_rows_count
    rows_late = aligned(rows_one)
    blocks_out = ((high, rows_late, mid), BF16, "raw")
    own_blocks, send_blocks = run(
        grads_one_kernel,
        [blocks_out, blocks_out],
        smem=(meta,),
        saved=(steps_one, united_low, slow_x, united, fast_x, ha_one, taps_one, hb_one, gz_c1),
        scratch=(
            pltpu.VMEM((count, rows_late, mid), BF16),
            pltpu.SemaphoreType.DMA((2, count)),
        ),
    )
    side_blocks = lax.ppermute(send_blocks, "wa", xor_pairs(2, 1))

    def chip_kernel(side_ref, own_ref, *out_refs):
        for place in range(high):
            total = own_ref[place].astype(F32) + side_ref[place].astype(F32)
            out_refs[place][...] = total.astype(BF16)
            out_refs[place].send()

    late_out = ((rows_late, mid), BF16, "hbm")
    chip_sums = run(chip_kernel, [late_out] * high, vmem=(side_blocks,), saved=(own_blocks,))
    chip_sums, early = lax.optimization_barrier((chip_sums, (sum_space, sum_mid)))
    late = [chip_sums[0]] + to_partners(chip_sums[1:], "ha")
    four = lax.axis_size("clips") == 4
    early_space, early_mid = lax.psum(early, "clips")
    quarters = clip_parts(meta, [late], 4 if four else 1)
    if four:
        total_late = add_low(quarters[0], *to_partners(quarters[1:], "clips"))
        parts_late = [total_late] + to_partners([total_late] * 3, "clips")
    else:
        parts_late = [lax.psum(quarters[0], "clips")]

    def finish(*jobs):
        outs_all = []
        for _, groups in jobs:
            for _, shapes in groups:
                for shape in shapes:
                    outs_all += list(shape) if isinstance(shape[0], tuple) else [shape]
        number = sum(len(parts) for parts, _ in jobs)
        deepest = max(sum(rows_group for rows_group, _ in groups) for _, groups in jobs)

        def kernel(meta_ref, *refs):
            ins, outs, total_ref = list(refs[:number]), list(refs[number:-1]), refs[-1]
            for parts, groups in jobs:
                mine, ins = ins[: len(parts)], ins[len(parts) :]
                one_job(meta_ref, mine, outs, total_ref, groups)

        def one_job(meta_ref, ins, outs, total_ref, groups):
            size = len(ins)
            depth = sum(rows_group for rows_group, _ in groups) // size
            base = 0
            for step, ref in enumerate(ins):
                start = pl.multiple_of((meta_ref[4] ^ step) * depth, 16) if size > 1 else 0
                total_ref[pl.ds(start, depth), :] = ref[...].astype(F32)
            for rows_group, shapes in groups:
                at = base
                for shape in shapes:
                    if isinstance(shape[0], tuple):
                        reduce, space, expand = outs.pop(0), outs.pop(0), outs.pop(0)
                        rows_tap, lanes = reduce.shape[1:]
                        for tap in range(3):
                            reduce[tap] = total_ref[
                                at : at + rows_tap, tap * lanes : (tap + 1) * lanes
                            ]
                        few = space.shape[2]
                        for tap in range(9):
                            row = at + rows_tap + tap // SUB * SUB
                            lane = tap % SUB * lanes
                            space[tap // 3, tap % 3] = total_ref[
                                row : row + few, lane : lane + lanes
                            ]
                        row = at + rows_tap + SUB
                        expand[...] = total_ref[row : row + few, expand.shape[1] :]
                        for out in (reduce, space, expand):
                            out.send()
                        at += rows_tap + 2 * SUB
                        continue
                    out = outs.pop(0)
                    if len(shape) == 2 and shape[1] > mid:
                        for block in range(shape[1] // mid):
                            out[:, block * mid : (block + 1) * mid] = total_ref[
                                at : at + shape[0], :
                            ]
                            at += shape[0]
                    else:
                        number = 1
                        for length in shape[:-1]:
                            number *= length
                        out[...] = total_ref[at : at + number, :].reshape(shape)
                        at += number
                    out.send()
                base += rows_group

        return run(
            kernel,
            [(shape, F32, "hbm") for shape in outs_all],
            smem=(meta,),
            saved=[part for parts, _ in jobs for part in parts],
            scratch=(pltpu.VMEM((deepest, mid), F32),),
        )

    shapes_one = tuple(shard.shape for shard in fast_shards_one)
    shapes_two = tuple(shard.shape for shard in fast_shards_two)
    groups_space = [(rows_space, [slow_spatial_two.shape, slow_expand_two.shape])]
    groups_mid = [
        (
            rows_mid,
            [slow_reduce_two.shape, shapes_two, slow_shortcut_one.shape, slow_expand_one.shape],
        ),
    ]
    groups_late = [
        (
            rows_late,
            [slow_reduce_one.shape, lateral_weight.shape, slow_spatial_one.shape, shapes_one],
        )
    ]
    finished = finish(
        ([early_space], groups_space), ([early_mid], groups_mid), (parts_late, groups_late)
    )
    grad_slow_spatial_two, grad_slow_expand_two, grad_slow_reduce_two = finished[:3]
    fast_two_grads, (grad_slow_shortcut, grad_slow_expand_one) = finished[3:6], finished[6:8]
    grad_slow_reduce_one, grad_lateral, grad_slow_spatial_one, *fast_one_grads = finished[8:]

    def norm_grads(first, second, third):
        slow = [first[:, :mid], second[:, :mid], third[:, :slow_wide]]
        fast = [first[:, mid:], second[:, mid:]]
        fast = [jnp.sum(part.reshape(2, PHASES, -1), axis=1) for part in fast]
        return slow, fast + [third[:, slow_wide:packed]]

    slow_one_p, fast_one_p = norm_grads(sums_a1, sums_b1, sums_c1)
    slow_two_p, fast_two_p = norm_grads(sums_a2, sums_b2, sums_c2)
    grad_slow_norms_one = jnp.concatenate(slow_one_p + [sums_c1[:, packed:]], axis=1)
    grad_slow_norms_two = jnp.concatenate(slow_two_p, axis=1)
    grad_fast_norms_one = jnp.concatenate(fast_one_p, axis=1)
    grad_fast_norms_two = jnp.concatenate(fast_two_p, axis=1)
    return (
        outputs[:, :slow_wide].reshape(slow_input.shape),
        join_phases(outputs[:, slow_wide:], fast_input.shape),
        grad_slow.reshape(slow_input.shape),
        join_phases(grad_fast, fast_input.shape),
        grad_lateral,
        grad_slow_reduce_one,
        grad_slow_spatial_one,
        grad_slow_expand_one,
        grad_slow_shortcut,
        *fast_one_grads,
        grad_slow_reduce_two,
        grad_slow_spatial_two,
        grad_slow_expand_two,
        *fast_two_grads,
        grad_slow_norms_one,
        grad_fast_norms_one,
        grad_slow_norms_two,
        grad_fast_norms_two,
    )


def solution(mesh):
    in_specs = (
        P("clips", None, "ha", "wa", None),
        P("clips", None, "ha", "wa", None),
        P("clips", None, "ha", "wa", None),
        P("clips", None, "ha", "wa", None),
        P("clips"),
        P(None, ("ha", "wa"), None),
        P(None, ("ha", "wa"), None),
        P(None, None, ("ha", "wa"), None),
        P(("ha", "wa"), None),
        P(("ha", "wa"), None),
        P(None, ("ha", "wa"), None),
        P(None, None, ("ha", "wa"), None),
        P(("ha", "wa"), None),
        P(None, ("ha", "wa"), None),
        P(None, None, ("ha", "wa"), None),
        P(("ha", "wa"), None),
        P(None, ("ha", "wa"), None),
        P(None, None, ("ha", "wa"), None),
        P(("ha", "wa"), None),
        P(),
        P(),
        P(),
        P(),
    )
    out_specs = (
        P("clips", None, "ha", "wa", None),
        P("clips", None, "ha", "wa", None),
        P("clips", None, "ha", "wa", None),
        P("clips", None, "ha", "wa", None),
        P(None, ("ha", "wa"), None),
        P(None, ("ha", "wa"), None),
        P(None, None, ("ha", "wa"), None),
        P(("ha", "wa"), None),
        P(("ha", "wa"), None),
        P(None, ("ha", "wa"), None),
        P(None, None, ("ha", "wa"), None),
        P(("ha", "wa"), None),
        P(None, ("ha", "wa"), None),
        P(None, None, ("ha", "wa"), None),
        P(("ha", "wa"), None),
        P(None, ("ha", "wa"), None),
        P(None, None, ("ha", "wa"), None),
        P(("ha", "wa"), None),
        P(),
        P(),
        P(),
        P(),
    )
    return jax.shard_map(
        on_device, mesh=mesh, in_specs=in_specs, out_specs=out_specs, check_vma=False
    )
```

```python
import jax
import jax.numpy as jnp
from jax import lax
from jax.experimental import pallas as pl
from jax.experimental.pallas import tpu as pltpu
from jax.sharding import PartitionSpec as P

epsilon = 1e-05
F32 = jnp.float32
BF16 = jnp.bfloat16
TILE = ("ha", "wa")
PHASES = 4
SUB = 8


def dot(left, right):
    return lax.dot_general(left, right, (((1,), (0,)), ((), ())), preferred_element_type=F32)


def dot_tn(left, right):
    return lax.dot_general(left, right, (((0,), (0,)), ((), ())), preferred_element_type=F32)


def dot_nt(left, right):
    return lax.dot_general(left, right, (((1,), (1,)), ((), ())), preferred_element_type=F32)


class Keep:
    def __init__(self, ref):
        self.scratch, self.shape = ref, ref.shape

    def send(self):
        pass

    def __setitem__(self, index, value):
        self.scratch[index] = value

    def __getitem__(self, index):
        return self.scratch[index]


class Loads:
    def __init__(self, source, offset, target, sems, first):
        self.copies = []
        depth = target.shape[2]
        for step in range(target.shape[0]):
            copy = pltpu.make_async_copy(
                source.at[:, pl.ds(offset + step * depth, depth), :],
                target.at[step],
                sems.at[first + step],
            )
            copy.start()
            self.copies.append(copy)
        self.target = target

    def get(self, step):
        self.copies[step].wait()
        block = self.target[step]
        return block.reshape(-1, block.shape[-1])


class Saved:
    def __init__(self, source, scratch, sem):
        self.scratch, self.shape = scratch, scratch.shape
        self.copy = pltpu.make_async_copy(source, scratch, sem)
        self.copy.start()
        self.ready = False

    def wait(self):
        if not self.ready:
            self.copy.wait()
            self.ready = True

    def __getitem__(self, index):
        self.wait()
        return self.scratch[index]


SEGMENTS = 8


class Store:
    def __init__(self, scratch, target, sems):
        self.scratch, self.target, self.shape = scratch, target, scratch.shape
        self.sems, self.copies = sems, []

    def send(self):
        self.copies.append(pltpu.make_async_copy(self.scratch, self.target, self.sems[0]))
        self.copies[-1].start()

    def send_rows(self, low, high):
        rows = pl.ds(low, high - low)
        source, target = self.scratch.at[:, rows, :], self.target.at[:, rows, :]
        self.copies.append(pltpu.make_async_copy(source, target, self.sems[len(self.copies)]))
        self.copies[-1].start()

    def __setitem__(self, index, value):
        self.scratch[index] = value

    def __getitem__(self, index):
        return self.scratch[index]


CLOSE = 320 * 1024


def run(body, outs, smem=(), parts=(), vmem=(), saved=(), weights=(), scratch=(), limit=53):
    near = pl.BlockSpec(memory_space=pltpu.VMEM)
    far = pl.BlockSpec(memory_space=pltpu.HBM)
    sources = []
    for array, *_ in weights:
        if not any(array is other for other in sources):
            sources.append(array)
    outs = list(outs) + [(part.shape[1:], part.dtype, "hbm") for part in parts]
    flat = []
    twice = []
    for at, (shape, dtype, kind) in enumerate(outs):
        size = jnp.dtype(dtype).itemsize
        for length in shape:
            size *= length
        twice.append(kind == "both" and size <= CLOSE)
        if kind in ("hbm", "both") and size <= CLOSE:
            outs[at] = (shape, dtype, "vmem")
    for shape, dtype, kind in outs:
        flat += [(shape, dtype, "raw"), (shape, dtype, "vmem")] if kind == "both" else [(shape, dtype, kind)]
    close = [array.size * array.dtype.itemsize <= CLOSE for array in saved]
    held = [pltpu.VMEM(array.shape, array.dtype) for array, here in zip(saved, close) if not here]
    for array, _, steps, depth in weights:
        held.append(pltpu.VMEM((steps, array.shape[0], depth, array.shape[2]), array.dtype))
    for shape, dtype, kind in outs:
        if kind in ("hbm", "rows"):
            held.append(pltpu.VMEM(shape, dtype))
        elif kind == "spread":
            held.append(pltpu.VMEM(shape[1:], dtype))
    sems = len(saved) + sum(steps for _, _, steps, _ in weights) + len(outs)
    sems += SEGMENTS * sum(kind == "rows" for _, _, kind in outs)
    held.append(pltpu.SemaphoreType.DMA((sems,)))

    def kernel(*refs):
        refs = list(refs)

        def take(number):
            taken = refs[:number]
            del refs[:number]
            return taken

        smem_refs, part_refs, vmem_refs = take(len(smem)), take(len(parts)), take(len(vmem))
        saved_refs, source_refs, out_refs = take(len(saved)), take(len(sources)), take(len(flat))
        saved_scratch, weight_scratch = take(len(saved) - sum(close)), take(len(weights))
        out_scratch = take(sum(kind in ("hbm", "rows", "spread") for _, _, kind in outs))
        sem, more = refs[0], refs[1:]
        arrays, copies = [], []
        for source, here in zip(saved_refs, close):
            if not here:
                copies.append(Saved(source, saved_scratch[len(copies)], sem.at[len(copies)]))
            arrays.append(source if here else copies[-1])
        at = len(saved)
        loads = []
        for (array, offset, steps, _), target in zip(weights, weight_scratch):
            place = [array is other for other in sources].index(True)
            loads.append(Loads(source_refs[place], offset, target, sem, at))
            at += steps
        results, stores, spreads = [], [], []
        for _, _, kind in outs:
            ref = out_refs.pop(0)
            if kind == "both":
                stores.append(Store(out_refs.pop(0), ref, [sem.at[at]]))
                at += 1
                results.append(stores[-1])
            elif kind in ("hbm", "rows"):
                number = SEGMENTS if kind == "rows" else 1
                stores.append(
                    Store(out_scratch.pop(0), ref, [sem.at[at + part] for part in range(number)])
                )
                at += number
                results.append(stores[-1])
            elif kind == "spread":
                spreads.append((out_scratch.pop(0), ref))
                results.append(spreads[-1][0])
            elif kind == "vmem":
                results.append(Keep(ref))
            else:
                results.append(ref)
        sums = results[len(results) - len(parts) :]
        results = results[: len(results) - len(parts)]
        for part, total in zip(part_refs, sums):
            total[...] = jnp.sum(part[...], axis=0)
            total.send()
        totals = [total.scratch for total in sums]
        body(*smem_refs, *totals, *vmem_refs, *arrays, *loads, *results, *more)
        for copy in copies:
            copy.wait()
        for store in stores:
            if not store.copies:
                store.send()
        for value, ref in spreads:
            ref[...] = jnp.broadcast_to(value[...][None], ref.shape)
        for store in stores:
            for copy in store.copies:
                copy.wait()

    results = pl.pallas_call(
        kernel,
        out_shape=[jax.ShapeDtypeStruct(shape, dtype) for shape, dtype, _ in flat],
        in_specs=[pl.BlockSpec(memory_space=pltpu.SMEM)] * len(smem)
        + [near] * (len(parts) + len(vmem))
        + [near if here else far for here in close]
        + [far] * len(sources),
        out_specs=[far if kind in ("hbm", "rows", "raw") else near for _, _, kind in flat],
        scratch_shapes=held + list(scratch),
        compiler_params=pltpu.CompilerParams(vmem_limit_bytes=limit * 1024 * 1024),
        cost_estimate=pl.CostEstimate(
            flops=2_000_000_000, bytes_accessed=16_000_000, transcendentals=0
        ),
    )(*smem, *parts, *vmem, *saved, *sources)
    returned = []
    for (_, _, kind), double in zip(outs, twice):
        taken, results = results[: 2 if kind == "both" else 1], results[2 if kind == "both" else 1 :]
        returned += list(taken) * (2 if double else 1)
    return returned


class Geometry:
    def __init__(self, slow_shape, fast_shape):
        self.cap, self.frames, self.height, self.width = slow_shape[:4]
        self.groups = self.cap * self.frames
        self.rows = self.groups * SUB

    def three(self, value):
        return value.reshape(-1, SUB, value.shape[-1])

    def flat(self, value):
        return value.reshape(-1, value.shape[-1])

    def shift(self, value, step):
        lanes = value.shape[-1]
        whole = value.reshape(self.cap, self.frames, SUB, lanes)
        zero = jnp.zeros((self.cap, 1, SUB, lanes), value.dtype)
        if step > 0:
            whole = jnp.concatenate([zero, whole[:, :-1]], axis=1)
        else:
            whole = jnp.concatenate([whole[:, 1:], zero], axis=1)
        return whole.reshape(-1, lanes)


def mask_groups(shape, limit, scale=1):
    return lax.broadcasted_iota(jnp.int32, shape, 0) * scale < limit


def rep(ref, row, low, high):
    return jnp.broadcast_to(ref[row : row + 1, low:high], (SUB, high - low))


def fold(value, slow):
    fast = value[:, slow:]
    lanes = fast.shape[-1]
    if lanes * PHASES <= slow:
        return jnp.concatenate([value[:, :slow]] + [fast] * PHASES, axis=1)
    total = fast
    for phase in range(1, PHASES):
        total = total + pltpu.roll(fast, phase * (lanes // PHASES), 1)
    return jnp.concatenate([value[:, :slow], total], axis=1)


def lane_counts(inv_ref, lanes, slow):
    lane = lax.broadcasted_iota(jnp.int32, (SUB, lanes), 1)
    return jnp.where(lane < slow, inv_ref[0], inv_ref[1])


def moments(stats, inv_ref, slow, low=0, high=None):
    high = stats.shape[1] if high is None else high
    total, square = rep(stats, 0, low, high), rep(stats, 1, low, high)
    if slow < high - low:
        total, square = fold(total, slow), fold(square, slow)
    inv_n = lane_counts(inv_ref, total.shape[1], slow)
    mean = total * inv_n
    return mean, lax.rsqrt(square * inv_n - mean * mean + epsilon)


def affine(stats, params, inv_ref, slow, low=0, high=None):
    mean, inv = moments(stats, inv_ref, slow, low, high)
    lanes = mean.shape[1]
    scale = (1.0 + rep(params, 0, 0, lanes)) * inv
    return scale, rep(params, 1, 0, lanes) - mean * scale, mean, inv


def back_rows(sums, inv_ref, slow, row, low=0, high=None):
    high = sums.shape[1] if high is None else high
    total = rep(sums, row, low, high)
    if slow < high - low:
        total = fold(total, slow)
    return total * lane_counts(inv_ref, total.shape[1], slow)


def silu(value):
    return value * jax.nn.sigmoid(value)


def slope(value):
    sigma = jax.nn.sigmoid(value)
    return sigma * (1.0 + value * (1.0 - sigma))


def put_stats(ref, first, second, low=0, slow=None):
    for row, value in enumerate((first, second)):
        total = jnp.sum(jnp.sum(value, axis=0), axis=0, keepdims=True)
        if slow is not None:
            part = (total.shape[1] - slow) // PHASES
            fast = total[:, slow : slow + part]
            for phase in range(1, PHASES):
                fast = fast + total[:, slow + phase * part : slow + (phase + 1) * part]
            total = jnp.concatenate([total[:, :slow], fast], axis=1)
        ref[row : row + 1, low : low + total.shape[1]] = total


def put_back(ref, gradient, normal, low=0, slow=None):
    put_stats(ref, gradient * normal, gradient, low, slow)


def put_forward(ref, value, limit, low=0, slow=None):
    masked = jnp.where(mask_groups(value.shape, limit), value, 0.0)
    put_stats(ref, masked, masked * value, low, slow)


EDGE = 32


def edge_place(wa, width):
    return jnp.where(wa > 0, 0, width - 1)


def put_message(value, ref, edge_ref, meta_ref, width):
    lanes = value.shape[-1]
    pairs = value.reshape(-1, 2, SUB, lanes)
    first, second = pairs[:, 0], pairs[:, 1]
    near = lax.broadcasted_iota(jnp.int32, first.shape, 1) < SUB // 2
    top = jnp.where(near, first, pltpu.roll(second, SUB // 2, 1))
    bottom = jnp.where(near, pltpu.roll(first, SUB // 2, 1), second)
    flat = value.reshape(-1, lanes).astype(BF16)
    shape = (2 * EDGE, flat.shape[0])
    row, col = [lax.broadcasted_iota(jnp.int32, shape, dim) for dim in range(2)]
    low = row >= EDGE
    source = (row - jnp.where(low, EDGE, 0)) * SUB + jnp.where(low, SUB // 2, 0)
    chosen = (col == source + edge_place(meta_ref[2], width)).astype(F32).astype(BF16)
    edges = dot(chosen, flat)
    edge_ref[...] = edges.astype(BF16)
    edge_ref.send()
    top, bottom = [part.reshape(-1, lanes).astype(BF16) for part in (top, bottom)]
    ref[: top.shape[0]] = top
    ref[top.shape[0] :] = bottom
    ref.send()


def unpack_bottom(value):
    both = jnp.stack([pltpu.roll(value, SUB // 2, 1), value], axis=1)
    return both.reshape(-1, SUB, value.shape[-1])


def unpack_top(value):
    both = jnp.stack([value, pltpu.roll(value, SUB // 2, 1)], axis=1)
    return both.reshape(-1, SUB, value.shape[-1])


class Neighbours:
    def __init__(self, own, up, down, edges, meta, width):
        half = SUB // 2
        near = lax.broadcasted_iota(jnp.int32, own.shape, 1) < half
        self.col = lax.broadcasted_iota(jnp.int32, own.shape, 1) % width
        self.width, self.shape = width, own.shape
        ha, wa, last = meta[1], meta[2], meta[3]
        up = unpack_bottom(jnp.where(ha > 0, up, 0.0))
        down = unpack_top(jnp.where(ha < last, down, 0.0))
        self.rows = {
            0: own,
            -1: pltpu.roll(jnp.where(near, own, up), half, 1),
            1: pltpu.roll(jnp.where(near, down, own), half, 1),
        }
        beyond = lax.broadcasted_iota(jnp.int32, edges.shape, 0)
        inside = ((ha > 0) | (beyond >= EDGE)) & ((ha < last) | (beyond < 3 * EDGE))
        self.edges = jnp.where(inside, edges, 0.0).astype(BF16)
        shape = (own.shape[0] * SUB, edges.shape[0])
        place, self.source = [lax.broadcasted_iota(jnp.int32, shape, dim) for dim in range(2)]
        self.group = place // SUB
        self.row = place // half % 2
        self.touches = place % width == edge_place(wa, width)
        self.sides = {}

    def side(self, row_step):
        if row_step not in self.sides:
            wanted = (self.row + row_step + 1) * EDGE + self.group
            chosen = ((self.source == wanted) & self.touches).astype(F32).astype(BF16)
            self.sides[row_step] = dot(chosen, self.edges).reshape(self.shape)
        return self.sides[row_step]

    def at(self, row_step, col_step):
        base = self.rows[row_step]
        if col_step < 0:
            return jnp.where(self.col == 0, self.side(row_step), pltpu.roll(base, 1, 1))
        if col_step > 0:
            away = self.col == self.width - 1
            return jnp.where(away, self.side(row_step), pltpu.roll(base, SUB - 1, 1))
        return base


def xor_pairs(size, step):
    return [(index, index ^ step) for index in range(size)]


def direct_sum(value, axis):
    size = lax.axis_size(axis)
    step = 1
    while step < size:
        if size // step >= 4:
            one, two, three = [
                lax.ppermute(value, axis, xor_pairs(size, step * times)) for times in (1, 2, 3)
            ]
            value = (value + two) + (one + three)
            step *= 4
        else:
            value = value + lax.ppermute(value, axis, xor_pairs(size, step))
            step *= 2
    return value


AXES = ("clips", "ha", "wa")
MOST = 32


def spread_count():
    count = lax.axis_size("ha") * lax.axis_size("wa")
    whole = count * lax.axis_size("clips")
    return whole if whole <= MOST else count


def exchange(copies):
    if copies.shape[0] == lax.axis_size("clips") * lax.axis_size("ha") * lax.axis_size("wa"):
        return lax.all_to_all(copies, AXES, 0, 0)
    return lax.all_to_all(direct_sum(copies, "clips"), TILE, 0, 0)


def exchange_widest(sums):
    count = lax.axis_size("ha") * lax.axis_size("wa")
    sums = direct_sum(sums, "clips")
    return lax.all_to_all(jnp.broadcast_to(sums[None], (count,) + sums.shape), TILE, 0, 0)


def exchange_halo(message, edges):
    wide, high = lax.axis_size("wa"), lax.axis_size("ha")
    half = message.shape[0] // 2
    side = lax.ppermute(edges, "wa", xor_pairs(wide, 1))
    odd = lax.axis_index("ha") % 2 == 1
    tops = jnp.concatenate([message[:half], side[:EDGE]], axis=0)
    bottoms = jnp.concatenate([message[half:], side[EDGE:]], axis=0)
    first = lax.ppermute(jnp.where(odd, tops, bottoms), "ha", xor_pairs(high, 1))
    pairs = [(row, row + 1) for row in range(1, high - 1, 2)]
    pairs = pairs + [(low, row) for row, low in pairs]
    second = lax.ppermute(jnp.where(odd, bottoms, tops), "ha", pairs)
    return side, first, second


def from_above_and_below(first_ref, second_ref, meta_ref):
    first, second = first_ref[...].astype(F32), second_ref[...].astype(F32)
    odd = meta_ref[1] % 2 == 1
    return jnp.where(odd, first, second), jnp.where(odd, second, first)


def time_conv(geo, parts, blocks):
    result = None
    for tap in range(3):
        at = 0
        total = None
        for part in parts:
            lanes = part.shape[-1]
            term = dot(part, blocks[tap][at : at + lanes])
            at += lanes
            total = term if total is None else total + term
        if tap != 1:
            total = geo.shift(total, 1 - tap)
        result = total if result is None else result + total
    return result


def fast_conv(geo, value, main, before, after):
    lanes = value.shape[-1] // PHASES
    result = dot(value, main)
    result = result + geo.shift(dot(value[:, -lanes:], before), 1)
    return result + geo.shift(dot(value[:, :lanes], after), -1)


def fast_conv_back(steps, main, before, after):
    lanes = before.shape[0]
    middle = dot_nt(steps[1], main)
    first = middle[:, :lanes] + dot_nt(steps[2], after)
    last = middle[:, -lanes:] + dot_nt(steps[0], before)
    return jnp.concatenate([first, middle[:, lanes:-lanes], last], axis=1)


def lane_block(value, phase, part):
    return pltpu.roll(value, value.shape[-1] - phase * part, 1) if phase else value


def fast_reduce_grad(value, steps):
    lanes = value.shape[-1] // PHASES
    part = steps[1].shape[-1] // PHASES
    main = dot_tn(value, steps[1])
    before = dot_tn(value[:, -lanes:], steps[0])
    after = dot_tn(value[:, :lanes], steps[2])

    def block(row, col):
        return lane_block(main[row * lanes : (row + 1) * lanes], col, part)

    result = []
    for tap in range(3):
        total = before if tap == 0 else None
        if tap == 2:
            total = lane_block(after, PHASES - 1, part)
        for col in range(PHASES):
            row = col + tap - 1
            if 0 <= row < PHASES:
                total = block(row, col) if total is None else total + block(row, col)
        result.append(total)
    return result


def gather_pack(parts):
    return lax.all_gather(jnp.concatenate(parts, axis=0), TILE, axis=0)


def columns(shard, lanes):
    depth, total = shard.shape
    return jnp.moveaxis(shard.reshape(depth, total // lanes, lanes), 1, 0).reshape(-1, lanes)


def split_phases(value):
    cap, frames, height, width, lanes = value.shape
    value = value.reshape(cap, frames // PHASES, PHASES, height, width, lanes)
    return jnp.moveaxis(value, 2, 4).reshape(-1, PHASES * lanes)


def join_phases(value, shape):
    cap, frames, height, width, lanes = shape
    value = value.reshape(cap, frames // PHASES, height, width, PHASES, lanes)
    return jnp.moveaxis(value, 4, 2).reshape(shape)


def early_gather(shards_one, shards_two, lateral):
    rows = []
    lanes = shards_one[2].shape[-1]
    kinds = [jnp.stack(pair) for pair in zip(shards_one, shards_two)]
    kinds.append(jnp.stack([lateral[..., :lanes], lateral[..., lanes:]]))
    for kind in kinds:
        flat = kind.reshape(-1, kind.shape[-1])
        rows.append(jnp.pad(flat, ((0, 0), (0, lanes - flat.shape[-1]))))
    packed = gather_pack(rows)
    result = []
    at = 0
    for kind in kinds:
        depth, width = kind.shape[-2:]
        number = kind.size // width
        part = packed[:, at : at + number, :width].reshape(packed.shape[0], -1, depth, width)
        at += number
        result.append(jnp.moveaxis(part, 0, 1).reshape(part.shape[1], -1, width))
    return result


def prepare_kernel(taps_ref, space_ref, wide_ref, lateral_ref, *refs):
    slow_one, fast_one, slow_two, fast_two, *outs = refs
    part = taps_ref.shape[-1]
    lateral, *joint = outs[10:]
    number = lateral.shape[0]
    for tap in range(number):
        lateral[tap] = jnp.concatenate([lateral_ref[tap], lateral_ref[number + tap]], axis=1)
    for layer, (slow, fast) in enumerate(((slow_one, fast_one), (slow_two, fast_two))):
        at = fast_at = 0
        for ref in joint[3 * layer : 3 * layer + 3]:
            fast_lanes = part if ref.shape[1] < slow.shape[1] // 2 else wide_ref.shape[-1]
            lanes = ref.shape[1] - PHASES * fast_lanes
            values = [slow[:, at : at + lanes]]
            values += [fast[:, fast_at : fast_at + fast_lanes]] * PHASES
            ref[...] = jnp.concatenate(values, axis=1)
            at, fast_at = at + lanes, fast_at + fast_lanes
    joint[6][...] = slow_one[:, slow_one.shape[1] - joint[6].shape[1] :]
    for layer in range(2):
        main, before, after, space, wide = outs[5 * layer : 5 * layer + 5]
        taps = [taps_ref[3 * layer + tap] for tap in range(3)]
        zero = jnp.zeros_like(taps[0])
        lanes = taps[0].shape[0]
        for row in range(PHASES):
            blocks = [
                taps[row - col + 1] if abs(row - col) <= 1 else zero for col in range(PHASES)
            ]
            main[row * lanes : (row + 1) * lanes, :] = jnp.concatenate(blocks, axis=1)
        before[...] = jnp.concatenate([taps[0]] + [zero] * (PHASES - 1), axis=1)
        after[...] = jnp.concatenate([zero] * (PHASES - 1) + [taps[2]], axis=1)
        for tap in range(9):
            block = space_ref[9 * layer + tap]
            none = jnp.zeros_like(block)
            for row in range(PHASES):
                blocks = [block if row == col else none for col in range(PHASES)]
                space[tap, row * part : (row + 1) * part, :] = jnp.concatenate(blocks, axis=1)
        block = wide_ref[layer]
        none = jnp.zeros_like(block)
        for row in range(PHASES):
            blocks = [block if row == col else none for col in range(PHASES)]
            wide[row * part : (row + 1) * part, :] = jnp.concatenate(blocks, axis=1)


def to_partners(pieces, axis):
    size = lax.axis_size(axis)
    return [
        lax.ppermute(piece, axis, xor_pairs(size, step + 1)) for step, piece in enumerate(pieces)
    ]


def clip_parts(meta, groups, number):
    lanes = groups[0][0].shape[1]
    lengths = [group[0].shape[0] for group in groups]
    depth = sum(lengths) // number
    total_ins = sum(len(group) for group in groups)

    def kernel(meta_ref, *refs):
        ins, outs, total_ref = list(refs[:total_ins]), refs[total_ins:-1], refs[-1]
        at = 0
        for group, length in zip(groups, lengths):
            mine, ins = ins[: len(group)], ins[len(group) :]
            total = mine[0][...]
            if len(mine) > 1:
                total = total.astype(F32)
                for ref in mine[1:]:
                    total = total + ref[...].astype(F32)
                total = total.astype(BF16)
            total_ref[at : at + length, :] = total
            at += length
        for step, out in enumerate(outs):
            start = pl.multiple_of((meta_ref[4] ^ step) * depth, 16) if number > 1 else 0
            out[...] = total_ref[pl.ds(start, depth), :]
            out.send()

    return run(
        kernel,
        [((depth, lanes), BF16, "hbm")] * number,
        smem=(meta,),
        saved=[part for group in groups for part in group],
        scratch=(pltpu.VMEM((sum(lengths), lanes), BF16),),
    )


def add_low(first, *others):
    total = first.astype(F32)
    for other in others:
        total = total + other.astype(F32)
    return total.astype(BF16)


def on_device(
    slow_input,
    fast_input,
    slow_cotangent,
    fast_cotangent,
    clip_counts,
    lateral_weight,
    slow_reduce_one,
    slow_spatial_one,
    slow_expand_one,
    slow_shortcut_one,
    fast_reduce_one,
    fast_spatial_one,
    fast_expand_one,
    slow_reduce_two,
    slow_spatial_two,
    slow_expand_two,
    fast_reduce_two,
    fast_spatial_two,
    fast_expand_two,
    slow_norms_one,
    fast_norms_one,
    slow_norms_two,
    fast_norms_two,
):
    geo = Geometry(slow_input.shape, fast_input.shape)
    rows, groups = geo.rows, geo.groups
    half_rows = rows // 2
    count = lax.axis_size("ha") * lax.axis_size("wa")
    spread = spread_count()
    slow_wide = slow_input.shape[-1]
    fast_wide = PHASES * fast_input.shape[-1]
    wide = slow_wide + fast_wide
    packed = slow_wide + fast_wide // PHASES
    mid = slow_reduce_one.shape[-1]
    fast_part = fast_reduce_one.shape[-1]
    fast_mid = PHASES * fast_part
    small = mid + fast_mid
    lat = lateral_weight.shape[-1]
    blocks = slow_wide // mid

    depth_one = slow_reduce_one.shape[1]
    depth_two = slow_reduce_two.shape[1]
    depth_mid = slow_spatial_one.shape[2]
    depth_lat = lateral_weight.shape[1]
    near = gather_pack([slow_reduce_one.reshape(-1, mid), slow_spatial_one.reshape(-1, mid)])
    far = gather_pack(
        [
            columns(slow_shortcut_one, mid),
            slow_reduce_two.reshape(-1, mid),
        ]
    )
    last = gather_pack([slow_spatial_two.reshape(-1, mid), columns(slow_expand_two, mid)])
    at_space_one = 3 * depth_one
    at_short = 0
    at_reduce_two = at_short + blocks * depth_one
    at_space_two = 0
    at_expand_two = 9 * depth_mid
    fast_shards_one = (fast_reduce_one, fast_spatial_one, fast_expand_one)
    fast_shards_two = (fast_reduce_two, fast_spatial_two, fast_expand_two)
    expand_one = gather_pack([columns(slow_expand_one, mid)])
    compact = early_gather(fast_shards_one, fast_shards_two, lateral_weight)
    compact, expand_one = lax.optimization_barrier((compact, expand_one))
    structured = [
        ((fast_wide, fast_mid), BF16, "hbm"),
        ((fast_wide // PHASES, fast_mid), BF16, "hbm"),
        ((fast_wide // PHASES, fast_mid), BF16, "hbm"),
        ((9, fast_mid, fast_mid), BF16, "hbm"),
        ((fast_mid, fast_wide), BF16, "hbm"),
    ]
    joint_outs = [((2, lanes), F32, "hbm") for lanes in (small, small, wide)]
    prepared = run(
        prepare_kernel,
        structured * 2
        + [((lateral_weight.shape[0], fast_wide // PHASES, lat), BF16, "hbm")]
        + joint_outs * 2
        + [((2, slow_wide), F32, "hbm")],
        vmem=(*compact, slow_norms_one, fast_norms_one, slow_norms_two, fast_norms_two),
    )
    fast_one, fast_two, lateral = prepared[:5], prepared[5:10], prepared[10]
    params_one, params_two, params_short = prepared[11:14], prepared[14:17], prepared[17]

    held = clip_counts[0]
    clips = direct_sum(jnp.full((1, 128), held, F32), "clips")[0, 0]
    positions = clips * (SUB * geo.frames * count)
    inv_n = jnp.stack([1.0 / positions, 1.0 / (positions * PHASES)])
    ha, wa = lax.axis_index("ha"), lax.axis_index("wa")
    last_ha = jnp.full_like(ha, lax.axis_size("ha") - 1)
    meta = jnp.stack([held * geo.frames, ha, wa, last_ha, lax.axis_index("clips")])
    scalars = (meta, inv_n)

    slow_x = slow_input.reshape(rows, slow_wide)
    fast_x = split_phases(fast_input)
    cot = jnp.concatenate(
        [slow_cotangent.reshape(rows, slow_wide), split_phases(fast_cotangent)], axis=1
    )
    message_out = [((rows, small), BF16, "hbm"), ((2 * EDGE, small), BF16, "hbm")]
    stats_small = ((spread, 2, small), F32, "spread")
    stats_wide = ((spread, 2, packed), F32, "spread")
    stats_both = ((2, packed + slow_wide), F32, "vmem")
    small_out = ((rows, small), F32, "hbm")
    wide_out = ((rows, wide), F32, "hbm")
    small_both = ((rows, small), F32, "both")
    small_next = ((rows, small), F32, "vmem")
    wide_low = ((rows, wide), BF16, "hbm")

    def lateral_kernel(x_ref, k_ref, main_ref, before_ref, after_ref, united_ref, fast_ref):
        lanes = x_ref.shape[1] // PHASES
        x = x_ref[...]
        main = dot(x[:, : 3 * lanes], k_ref[2:5].reshape(3 * lanes, lat))
        past = dot(x[:, 2 * lanes :], k_ref[0:2].reshape(2 * lanes, lat))
        united_ref[...] = (main + geo.shift(past, 1)).astype(BF16)
        fast_ref[...] = fast_conv(geo, x, main_ref[...], before_ref[...], after_ref[...])

    united, za_fast = run(
        lateral_kernel,
        [((rows, lat), BF16, "hbm"), ((rows, fast_mid), F32, "hbm")],
        saved=(fast_x, lateral, *fast_one[:3]),
    )

    def reduce_one_kernel(
        meta_ref, x_ref, united_ref, fast_ref, loads, za_ref, stats_ref, message_ref, edge_ref
    ):
        weights = [loads.get(tap) for tap in range(3)]
        za = time_conv(geo, (x_ref[...], united_ref[...]), weights)
        za = jnp.concatenate([za, fast_ref[...]], axis=1)
        za_ref[...] = za
        za_ref.send()
        za = geo.three(za)
        put_message(za, message_ref, edge_ref, meta_ref, geo.width)
        put_forward(stats_ref, za, meta_ref[0])

    za_one, za_next, stats, message, edges = run(
        reduce_one_kernel,
        [small_both, stats_small, *message_out],
        smem=(meta,),
        saved=(slow_x, united, za_fast),
        weights=((near, 0, 3, depth_one),),
    )
    parts_a1 = exchange(stats)
    halo_one = exchange_halo(message, edges)

    def space_stage(za, parts_a, halo, params, gathered, offset, fast_w):
        def kernel(
            meta_ref,
            inv_ref,
            stats_ref,
            za_ref,
            side_ref,
            up_ref,
            down_ref,
            params_ref,
            fast_ref,
            loads,
            zb_ref,
            hidden_ref,
            out_stats,
        ):
            scale, shift, _, _ = affine(stats_ref, params_ref, inv_ref, mid)

            def act(value):
                return silu(geo.three(value.astype(F32)) * scale + shift)

            own = act(za_ref[...])
            up, down = from_above_and_below(up_ref, down_ref, meta_ref)
            side = side_ref[...].astype(F32)
            edges = jnp.concatenate([up[half_rows:], side, down[half_rows:]], axis=0)
            hidden_ref[...] = geo.flat(own).astype(BF16)
            hidden_ref.send()
            near_by = Neighbours(
                own,
                act(up[:half_rows]),
                act(down[:half_rows]),
                geo.flat(act(edges)),
                meta_ref,
                geo.width,
            )
            slow = fast = None
            for tap in range(9):
                moved = geo.flat(near_by.at(tap // 3 - 1, tap % 3 - 1)).astype(BF16)
                slow_term = dot(moved[:, :mid], loads.get(tap))
                fast_term = dot(moved[:, mid:], fast_ref[tap])
                slow = slow_term if slow is None else slow + slow_term
                fast = fast_term if fast is None else fast + fast_term
            zb = jnp.concatenate([slow, fast], axis=1)
            zb_ref[...] = zb
            zb_ref.send()
            put_forward(out_stats, geo.three(zb), meta_ref[0])

        zb, zb_next, hidden, stats, stats_a = run(
            kernel,
            [small_both, ((rows, small), BF16, "hbm"), stats_small],
            smem=scalars,
            parts=(parts_a,),
            vmem=(za,),
            saved=(*halo, params, fast_w),
            weights=((gathered, offset, 9, depth_mid),),
        )
        return zb, zb_next, hidden, exchange(stats), stats_a

    zb_one, zb_next, ha_one, parts_b1, stats_a1 = space_stage(
        za_next, parts_a1, halo_one, params_one[0], near, at_space_one, fast_one[3]
    )

    def expand_body(
        inv_ref, stats_ref, zb_ref, params_ref, fast_ref, hidden_ref, low_ref, zc_ref, loads
    ):
        scale, shift, _, _ = affine(stats_ref, params_ref, inv_ref, mid)
        hidden = geo.flat(silu(geo.three(zb_ref[...]) * scale + shift)).astype(BF16)
        hidden_ref[...] = hidden
        hidden_ref.send()
        zc_ref[:, slow_wide:] = dot(hidden[:, mid:], fast_ref[...])
        for block in range(blocks):
            zc_ref[:, block * mid : (block + 1) * mid] = dot(hidden[:, :mid], loads.get(block))
        low_ref[...] = zc_ref[...].astype(BF16)
        low_ref.send()

    def expand_one_kernel(
        meta_ref,
        inv_ref,
        stats_ref,
        zb_ref,
        params_ref,
        fast_ref,
        x_ref,
        united_ref,
        loads,
        shorts,
        hidden_ref,
        low_ref,
        short_low_ref,
        out_stats,
        zc_ref,
        short_ref,
    ):
        expand_body(
            inv_ref, stats_ref, zb_ref, params_ref, fast_ref, hidden_ref, low_ref, zc_ref, loads
        )
        put_forward(out_stats, geo.three(zc_ref[...]), meta_ref[0], 0, slow_wide)
        for block in range(blocks):
            weight = shorts.get(block)
            value = dot(x_ref[...], weight[:slow_wide]) + dot(united_ref[...], weight[slow_wide:])
            short_ref[:, block * mid : (block + 1) * mid] = value
            put_forward(out_stats, geo.three(value), meta_ref[0], packed + block * mid)
        short_low_ref[...] = short_ref[...].astype(BF16)
        short_low_ref.send()

    hb_one, zc_one, short, stats, stats_b1 = run(
        expand_one_kernel,
        [
            ((rows, small), BF16, "hbm"),
            wide_low,
            ((rows, slow_wide), BF16, "hbm"),
            stats_both,
        ],
        scratch=(pltpu.VMEM((rows, wide), F32), pltpu.VMEM((rows, slow_wide), F32)),
        smem=scalars,
        parts=(parts_b1,),
        vmem=(zb_next,),
        saved=(params_one[1], fast_one[4], slow_x, united),
        weights=((expand_one, 0, blocks, depth_mid), (far, at_short, blocks, depth_one)),
    )
    parts_c1 = exchange_widest(stats)

    def reduce_two_kernel(
        meta_ref,
        inv_ref,
        stats_ref,
        zc_ref,
        short_ref,
        params_ref,
        short_params_ref,
        x_ref,
        main_ref,
        before_ref,
        after_ref,
        loads,
        sum_ref,
        low_ref,
        za_ref,
        out_stats,
        message_ref,
        edge_ref,
    ):
        scale, shift, _, _ = affine(stats_ref, params_ref, inv_ref, slow_wide, 0, packed)
        scale_s, shift_s, _, _ = affine(
            stats_ref, short_params_ref, inv_ref, slow_wide, packed, packed + slow_wide
        )
        normed = geo.three(zc_ref[...].astype(F32)) * scale + shift
        slow = normed[..., :slow_wide] + (
            geo.three(short_ref[...].astype(F32)) * scale_s + shift_s
        )
        fast = normed[..., slow_wide:] + geo.three(x_ref[...].astype(F32))
        total = jnp.concatenate([slow, fast], axis=-1)
        sum_ref[...] = geo.flat(total).astype(BF16)
        sum_ref.send()
        low = geo.flat(silu(total)).astype(BF16)
        low_ref[...] = low
        low_ref.send()
        weights = [loads.get(tap) for tap in range(3)]
        za = time_conv(geo, (low[:, :slow_wide],), weights)
        fast_za = fast_conv(
            geo, low[:, slow_wide:], main_ref[...], before_ref[...], after_ref[...]
        )
        za = jnp.concatenate([za, fast_za], axis=1)
        za_ref[...] = za
        za_ref.send()
        za = geo.three(za)
        put_message(za, message_ref, edge_ref, meta_ref, geo.width)
        put_forward(out_stats, za, meta_ref[0])

    sum_one, low_one, za_two, za_next, stats, message, edges, stats_c1 = run(
        reduce_two_kernel,
        [wide_low, wide_low, small_both, stats_small, *message_out],
        smem=scalars,
        parts=(parts_c1,),
        saved=(zc_one, short, params_one[2], params_short, fast_x, *fast_two[:3]),
        weights=((far, at_reduce_two, 3, depth_two),),
    )
    parts_a2 = exchange(stats)
    halo_two = exchange_halo(message, edges)
    zb_two, zb_next, ha_two, parts_b2, stats_a2 = space_stage(
        za_next, parts_a2, halo_two, params_two[0], last, at_space_two, fast_two[3]
    )

    def expand_two_kernel(
        meta_ref,
        inv_ref,
        stats_ref,
        zb_ref,
        params_ref,
        fast_ref,
        loads,
        hidden_ref,
        low_ref,
        out_stats,
        zc_ref,
    ):
        expand_body(
            inv_ref, stats_ref, zb_ref, params_ref, fast_ref, hidden_ref, low_ref, zc_ref, loads
        )
        put_forward(out_stats, geo.three(zc_ref[...]), meta_ref[0], 0, slow_wide)

    hb_two, zc_two, stats, stats_b2 = run(
        expand_two_kernel,
        [((rows, small), BF16, "hbm"), wide_low, stats_wide],
        scratch=(pltpu.VMEM((rows, wide), F32),),
        smem=scalars,
        parts=(parts_b2,),
        vmem=(zb_next,),
        saved=(params_two[1], fast_two[4]),
        weights=((last, at_expand_two, blocks, depth_mid),),
    )
    parts_c2 = exchange(stats)

    def head_kernel(
        meta_ref,
        inv_ref,
        stats_ref,
        zc_ref,
        params_ref,
        sum_ref,
        cot_ref,
        out_ref,
        low_ref,
        sums_ref,
    ):
        scale, shift, mean, inv = affine(stats_ref, params_ref, inv_ref, slow_wide)
        zc = geo.three(zc_ref[...].astype(F32))
        total = zc * scale + shift + silu(geo.three(sum_ref[...].astype(F32)))
        valid = mask_groups(total.shape, meta_ref[0])
        sigma = jax.nn.sigmoid(total)
        out_ref[...] = geo.flat(jnp.where(valid, total * sigma, 0.0)).astype(BF16)
        slopes = sigma * (1.0 + total * (1.0 - sigma))
        gradient = jnp.where(valid, geo.three(cot_ref[...].astype(F32)) * slopes, 0.0)
        out_ref.send()
        low_ref[...] = geo.flat(gradient).astype(BF16)
        low_ref.send()
        put_back(sums_ref, gradient, (zc - mean) * inv, 0, slow_wide)

    outputs, g_two, sums, stats_c2 = run(
        head_kernel,
        [((rows, wide), BF16, "hbm"), wide_low, stats_wide],
        smem=scalars,
        parts=(parts_c2,),
        saved=(zc_two, params_two[2], sum_one, cot),
    )
    parts_c2 = exchange(sums)

    def norm_back(gradient, value, coeffs, sums, valid):
        scale, _, mean, inv = coeffs
        crossed = (value - mean) * inv * sums[0] + sums[1]
        return scale * (gradient - jnp.where(valid, crossed, 0.0))

    def expand_back_body(
        meta_ref,
        inv_ref,
        sums_ref,
        g_ref,
        stats_ref,
        stats_b_ref,
        zc_ref,
        params_ref,
        zb_ref,
        params_b_ref,
        fast_ref,
        loads,
        gz_ref,
        g_out,
        sums_out,
        message_ref,
        edge_ref,
    ):
        limit = meta_ref[0]
        coeffs = affine(stats_ref, params_ref, inv_ref, slow_wide, 0, packed)
        both = [back_rows(sums_ref, inv_ref, slow_wide, row, 0, packed) for row in range(2)]
        gradient = geo.three(g_ref[...].astype(F32))
        gz = norm_back(
            gradient,
            geo.three(zc_ref[...].astype(F32)),
            coeffs,
            both,
            mask_groups(gradient.shape, limit),
        )
        gz = geo.flat(gz).astype(BF16)
        gz_ref[...] = gz
        gz_ref.send()
        fast = dot_nt(gz[:, slow_wide:], fast_ref[...])
        slow = None
        for block in range(blocks):
            term = dot_nt(gz[:, block * mid : (block + 1) * mid], loads.get(block))
            slow = term if slow is None else slow + term
        scale, shift, mean, inv = affine(stats_b_ref, params_b_ref, inv_ref, mid)
        zb = geo.three(zb_ref[...])
        back = geo.three(jnp.concatenate([slow, fast], axis=1)) * slope(zb * scale + shift)
        g_out[...] = geo.flat(back)
        put_message(
            jnp.concatenate([back, zb], axis=-1), message_ref, edge_ref, meta_ref, geo.width
        )
        masked = jnp.where(mask_groups(back.shape, limit), back, 0.0)
        put_back(sums_out, masked, (zb - mean) * inv)
        return gradient

    message_back = [((rows, 2 * small), BF16, "hbm"), ((2 * EDGE, 2 * small), BF16, "hbm")]
    gz_c2, g_b2, sums, message, edges, sums_c2 = run(
        expand_back_body,
        [((rows, wide), BF16, "hbm"), small_next, stats_small, *message_back],
        smem=scalars,
        parts=(parts_c2,),
        saved=(g_two, stats_c2, stats_b2, zc_two, params_two[2], zb_two, params_two[1], fast_two[4]),
        weights=((last, at_expand_two, blocks, depth_mid),),
    )
    parts_b2 = exchange(sums)
    halo_back_two = exchange_halo(message, edges)
    align = 16 * lax.axis_size("clips")

    def aligned(number):
        return number + -number % align


    lanes_fast = fast_wide // PHASES
    fast_rows_count = fast_reduce_one.shape[1] + 2 * SUB

    def expand_grad(hb_ref, gz_ref, out_ref, at):
        for block in range(blocks):
            value = dot_tn(hb_ref[:, :mid], gz_ref[:, block * mid : (block + 1) * mid])
            low = at + block * depth_mid
            out_ref[:, low : low + depth_mid, :] = value.astype(BF16).reshape(
                count, depth_mid, mid
            )
        if isinstance(out_ref, Store):
            out_ref.send_rows(at, at + blocks * depth_mid)

    def fast_expand_grad(hb_ref, gz_ref):
        fast = dot_tn(hb_ref[:, mid:], gz_ref[:, slow_wide:])
        total = None
        for phase in range(PHASES):
            part = fast[
                phase * fast_part : (phase + 1) * fast_part,
                phase * lanes_fast : (phase + 1) * lanes_fast,
            ]
            total = part if total is None else total + part
        return total

    def space_grad(ha_ref, taps_ref, out_ref, at):
        fast_grads = []
        for tap in range(9):
            value = dot_tn(ha_ref[:, :mid], taps_ref[tap, :, :mid])
            low = at + tap * depth_mid
            out_ref[:, low : low + depth_mid, :] = value.astype(BF16).reshape(
                count, depth_mid, mid
            )
            fast = dot_tn(ha_ref[:, mid:], taps_ref[tap, :, mid:])
            total = None
            for phase in range(PHASES):
                part = lane_block(
                    fast[phase * fast_part : (phase + 1) * fast_part], phase, fast_part
                )
                total = part if total is None else total + part
            fast_grads.append(total)
        if isinstance(out_ref, Store):
            out_ref.send_rows(at, at + 9 * depth_mid)
        return fast_grads

    def put_fast(reduce, space, expand, out_ref, at):
        lane = lax.broadcasted_iota(jnp.int32, reduce[0].shape, 1)

        def beside(parts):
            keep = lane[: parts[0].shape[0]]
            total = None
            for place, part in enumerate(parts):
                part = jnp.where(keep < fast_part, part, 0.0)
                part = pltpu.roll(part, place * fast_part, 1) if place else part
                total = part if total is None else total + part
            return total

        depth = reduce[0].shape[0] // count
        taps = beside(reduce).astype(BF16).reshape(count, depth, lanes_fast)
        out_ref[:, at : at + depth, :] = jnp.concatenate([taps, jnp.zeros_like(taps)], axis=-1)

        def spread(value):
            tiles = value.reshape(count // 2, SUB, lanes_fast)
            return jnp.stack([tiles, pltpu.roll(tiles, SUB // 2, 1)], axis=1).reshape(
                count, SUB, lanes_fast
            )

        first = jnp.concatenate([spread(beside(space[0:4])), spread(beside(space[4:8]))], axis=-1)
        second = jnp.concatenate([spread(beside(space[8:9])), spread(expand)], axis=-1)
        both = jnp.concatenate([first, second], axis=1).astype(BF16)
        out_ref[:, at + depth : at + depth + 2 * SUB, :] = both
        if isinstance(out_ref, Store):
            out_ref.send_rows(at, at + depth + 2 * SUB)

    def space_back_stage(
        g, zb, za, halo, stats_b, parts_b, params_b, stats_a, params_a, g_hbm, at, fast_w
    ):
        def kernel(
            meta_ref,
            inv_ref,
            sums_b_ref,
            g_ref,
            side_ref,
            up_ref,
            down_ref,
            stats_b_ref,
            stats_a_ref,
            zb_ref,
            za_ref,
            params_b_ref,
            params_a_ref,
            fast_ref,
            loads,
            taps_ref,
            g_out,
            sums_out,
        ):
            limit = meta_ref[0]
            coeffs = affine(stats_b_ref, params_b_ref, inv_ref, mid)
            both = [back_rows(sums_b_ref, inv_ref, mid, row) for row in range(2)]

            def back(gradient, value, valid):
                return norm_back(gradient, value, coeffs, both, valid)

            def halo_back(value, scale):
                value = geo.three(value.astype(F32))
                valid = mask_groups(value[..., :small].shape, limit, scale)
                return back(value[..., :small], value[..., small:], valid)

            def edge_back(value):
                value = geo.three(value.astype(F32))
                shape = value[..., :small].shape
                group = lax.broadcasted_iota(jnp.int32, shape, 0) * SUB % EDGE
                group = group + lax.broadcasted_iota(jnp.int32, shape, 1)
                return geo.flat(back(value[..., :small], value[..., small:], group < limit))

            own, zb = geo.three(g_ref[...]), geo.three(zb_ref[...])
            up, down = from_above_and_below(up_ref, down_ref, meta_ref)
            side = side_ref[...].astype(F32)
            edges = jnp.concatenate([up[half_rows:], side, down[half_rows:]], axis=0)

            near_by = Neighbours(
                back(own, zb, mask_groups(own.shape, limit)),
                halo_back(up[:half_rows], 2),
                halo_back(down[:half_rows], 2),
                edge_back(edges),
                meta_ref,
                geo.width,
            )
            slow = fast = None
            for tap in range(9):
                moved = geo.flat(near_by.at(1 - tap // 3, 1 - tap % 3)).astype(BF16)
                taps_ref[tap] = moved
                if tap == 8:
                    taps_ref.send()
                slow_term = dot_nt(moved[:, :mid], loads.get(tap))
                fast_term = dot_nt(moved[:, mid:], fast_ref[tap])
                slow = slow_term if slow is None else slow + slow_term
                fast = fast_term if fast is None else fast + fast_term
            scale, shift, mean, inv = affine(stats_a_ref, params_a_ref, inv_ref, mid)
            za = geo.three(za_ref[...])
            result = geo.three(jnp.concatenate([slow, fast], axis=1)) * slope(za * scale + shift)
            g_out[...] = geo.flat(result)
            masked = jnp.where(mask_groups(result.shape, limit), result, 0.0)
            put_back(sums_out, masked, (za - mean) * inv)

        taps, g, sums, sums_b = run(
            kernel,
            [((9, rows, small), BF16, "hbm"), small_next, stats_small],
            smem=scalars,
            parts=(parts_b,),
            vmem=(g,),
            saved=(*halo, stats_b, stats_a, zb, za, params_b, params_a, fast_w),
            weights=((g_hbm, at, 9, depth_mid),),
        )
        return taps, g, exchange(sums), sums_b

    taps_two, g_a2, parts_a2, sums_b2 = space_back_stage(
        g_b2,
        zb_two,
        za_two,
        halo_back_two,
        stats_b2,
        parts_b2,
        params_two[1],
        stats_a2,
        params_two[0],
        last,
        at_space_two,
        fast_two[3],
    )
    def grads_two_kernel(hb_ref, gz_ref, ha_ref, taps_ref, out_ref, fast_out):
        space = space_grad(ha_ref, taps_ref, out_ref, 0)
        expand_grad(hb_ref, gz_ref, out_ref, 9 * depth_mid)
        for tap in range(9):
            fast_out[tap] = space[tap]
        fast_out[9] = fast_expand_grad(hb_ref, gz_ref)

    rows_space = aligned((9 + blocks) * depth_mid)
    packed_space, fast_space_two = run(
        grads_two_kernel,
        [((count, rows_space, mid), BF16, "rows"), ((10, fast_part, lanes_fast), F32, "hbm")],
        saved=(hb_two, gz_c2, ha_two, taps_two),
    )
    sum_space = lax.psum_scatter(packed_space, TILE, scatter_dimension=0, tiled=False)

    def reduce_gz(meta_ref, inv_ref, g_ref, za_ref, stats_ref, sums_ref, params_ref, steps_ref):
        coeffs = affine(stats_ref, params_ref, inv_ref, mid)
        both = [back_rows(sums_ref, inv_ref, mid, row) for row in range(2)]
        gradient = geo.three(g_ref[...])
        gz = norm_back(
            gradient,
            geo.three(za_ref[...]),
            coeffs,
            both,
            mask_groups(gradient.shape, meta_ref[0]),
        )
        gz = geo.flat(gz)
        steps = [geo.shift(gz, -1).astype(BF16), gz.astype(BF16), geo.shift(gz, 1).astype(BF16)]
        for tap in range(3):
            steps_ref[tap] = steps[tap]
        steps_ref.send()
        return steps

    def reduce_back_two_kernel(
        meta_ref,
        inv_ref,
        sums_ref,
        g_ref,
        stats_ref,
        stats_c_ref,
        za_ref,
        params_ref,
        g_two_ref,
        sum_ref,
        zc_ref,
        short_ref,
        main_ref,
        before_ref,
        after_ref,
        loads,
        steps_ref,
        fast_out,
        g_out,
        sums_out,
    ):
        steps = reduce_gz(
            meta_ref, inv_ref, g_ref, za_ref, stats_ref, sums_ref, params_ref, steps_ref
        )
        slow = None
        for tap in range(3):
            term = dot_nt(steps[tap][:, :mid], loads.get(tap))
            slow = term if slow is None else slow + term
        fast = fast_conv_back(
            [step[:, mid:] for step in steps], main_ref[...], before_ref[...], after_ref[...]
        )
        back = jnp.concatenate([slow, fast], axis=1) + g_two_ref[...].astype(F32)
        back = back * slope(sum_ref[...].astype(F32))
        g_out[...] = back.astype(BF16)
        g_out.send()
        fast_out[...] = back[:, slow_wide:]
        fast_out.send()
        back = geo.three(back)
        masked = jnp.where(mask_groups(back.shape, meta_ref[0]), back, 0.0)
        mean, inv = moments(stats_c_ref, inv_ref, slow_wide, 0, packed)
        put_back(
            sums_out, masked, (geo.three(zc_ref[...].astype(F32)) - mean) * inv, 0, slow_wide
        )
        mean, inv = moments(stats_c_ref, inv_ref, slow_wide, packed, packed + slow_wide)
        masked = masked[..., :slow_wide]
        put_back(sums_out, masked, (geo.three(short_ref[...].astype(F32)) - mean) * inv, packed)

    steps_two, g_one_fast, g_one, sums, sums_a2 = run(
        reduce_back_two_kernel,
        [
            ((3, rows, small), BF16, "hbm"),
            ((rows, fast_wide), F32, "hbm"),
            wide_low,
            stats_both,
        ],
        smem=scalars,
        parts=(parts_a2,),
        vmem=(g_a2,),
        saved=(stats_a2, stats_c1, za_two, params_two[0], g_two, sum_one, zc_one, short, *fast_two[:3]),
        weights=((far, at_reduce_two, 3, depth_two),),
    )
    parts_c1 = exchange_widest(sums)

    def expand_back_one_kernel(*refs):
        *body, short_ref, short_params_ref, loads, gz_ref, g_out, sums_out, message, edge, gs_ref = (
            refs
        )
        gradient = expand_back_body(*body, loads, gz_ref, g_out, sums_out, message, edge)
        meta_ref, inv_ref, sums_ref, _, stats_ref = body[:5]
        low, high = packed, packed + slow_wide
        coeffs = affine(stats_ref, short_params_ref, inv_ref, slow_wide, low, high)
        both = [back_rows(sums_ref, inv_ref, slow_wide, row, low, high) for row in range(2)]
        gradient = gradient[..., :slow_wide]
        valid = mask_groups(gradient.shape, meta_ref[0])
        gs = norm_back(gradient, geo.three(short_ref[...].astype(F32)), coeffs, both, valid)
        gs_ref[...] = geo.flat(gs).astype(BF16)

    gz_c1, g_b1, sums, message, edges, gz_short, sums_c1 = run(
        expand_back_one_kernel,
        [((rows, wide), BF16, "hbm"), small_next, stats_small, *message_back]
        + [((rows, slow_wide), BF16, "hbm")],
        smem=scalars,
        parts=(parts_c1,),
        saved=(g_one, stats_c1, stats_b1, zc_one, params_one[2], zb_one, params_one[1], fast_one[4])
        + (short, params_short),
        weights=((expand_one, 0, blocks, depth_mid),),
    )
    parts_b1 = exchange(sums)
    halo_back_one = exchange_halo(message, edges)
    joined_lanes = slow_wide + lat

    def grads_mid_kernel(
        x_ref,
        united_ref,
        gs_ref,
        hb_ref,
        gz_ref,
        low_ref,
        steps_ref,
        fast_ref,
        loads,
        out_ref,
        back_ref,
    ):
        for tap in range(3):
            value = dot_tn(low_ref[:, :slow_wide], steps_ref[tap, :, :mid])
            out_ref[:, tap * depth_two : (tap + 1) * depth_two, :] = value.astype(BF16).reshape(
                count, depth_two, mid
            )
        at = 3 * depth_two
        out_ref.send_rows(0, at)
        reduce = fast_reduce_grad(
            low_ref[:, slow_wide:], [steps_ref[tap, :, mid:] for tap in range(3)]
        )
        put_fast(reduce, [fast_ref[tap] for tap in range(9)], fast_ref[9], out_ref, at)
        at += fast_rows_count
        expand_grad(hb_ref, gz_ref, out_ref, at + blocks * depth_one)
        for block in range(blocks):
            gs = gs_ref[:, block * mid : (block + 1) * mid]
            value = jnp.concatenate([dot_tn(x_ref[...], gs), dot_tn(united_ref[...], gs)], axis=0)
            low = at + block * depth_one
            out_ref[:, low : low + depth_one, :] = value.astype(BF16).reshape(
                count, depth_one, mid
            )
            out_ref.send_rows(low, low + depth_one)
        for block in range(blocks):
            gs = gs_ref[:, block * mid : (block + 1) * mid]
            term = dot_nt(gs, loads.get(block))
            back_ref[...] = term if block == 0 else back_ref[...] + term

    rows_mid = aligned(3 * depth_two + fast_rows_count + blocks * (depth_one + depth_mid))
    packed_mid, short_back = run(
        grads_mid_kernel,
        [((count, rows_mid, mid), BF16, "rows"), ((rows, joined_lanes), F32, "hbm")],
        saved=(slow_x, united, gz_short, hb_one, gz_c1, low_one, steps_two, fast_space_two),
        weights=((far, at_short, blocks, depth_one),),
    )
    sum_mid = lax.psum_scatter(packed_mid, TILE, scatter_dimension=0, tiled=False)

    taps_one, g_a1, parts_a1, sums_b1 = space_back_stage(
        g_b1,
        zb_one,
        za_one,
        halo_back_one,
        stats_b1,
        parts_b1,
        params_one[1],
        stats_a1,
        params_one[0],
        near,
        at_space_one,
        fast_one[3],
    )
    def last_kernel(
        meta_ref,
        inv_ref,
        sums_ref,
        g_ref,
        stats_ref,
        za_ref,
        params_ref,
        g_one_ref,
        short_ref,
        lateral_ref,
        main_ref,
        before_ref,
        after_ref,
        loads,
        steps_ref,
        slow_ref,
        fast_ref,
        united_ref,
    ):
        steps = reduce_gz(
            meta_ref, inv_ref, g_ref, za_ref, stats_ref, sums_ref, params_ref, steps_ref
        )
        joined = short_ref[...]
        for tap in range(3):
            joined = joined + dot_nt(steps[tap][:, :mid], loads.get(tap))
        slow_ref[...] = joined[:, :slow_wide]
        tail = joined[:, slow_wide:]
        now, past = tail.astype(BF16), geo.shift(tail, -1).astype(BF16)
        united_ref[0] = now
        united_ref[1] = past
        lanes = fast_wide // PHASES
        fast = fast_conv_back(
            [step[:, mid:] for step in steps], main_ref[...], before_ref[...], after_ref[...]
        )
        fast = fast + g_one_ref[...]
        front = dot_nt(now, lateral_ref[2:5].reshape(3 * lanes, lat))
        back = dot_nt(past, lateral_ref[0:2].reshape(2 * lanes, lat))
        fast_ref[:, : 2 * lanes] = fast[:, : 2 * lanes] + front[:, : 2 * lanes]
        fast_ref[:, 2 * lanes : 3 * lanes] = (
            fast[:, 2 * lanes : 3 * lanes] + front[:, 2 * lanes :] + back[:, :lanes]
        )
        fast_ref[:, 3 * lanes :] = fast[:, 3 * lanes :] + back[:, lanes:]

    steps_one, grad_slow, grad_fast, united_low, sums_a1 = run(
        last_kernel,
        [
            ((3, rows, small), BF16, "hbm"),
            ((rows, slow_wide), F32, "hbm"),
            ((rows, fast_wide), F32, "hbm"),
            ((2, rows, lat), BF16, "hbm"),
        ],
        smem=scalars,
        parts=(parts_a1,),
        vmem=(g_a1,),
        saved=(stats_a1, za_one, params_one[0], g_one_fast, short_back, lateral, *fast_one[:3]),
        weights=((near, 0, 3, depth_one),),
    )

    def grads_one_kernel(
        meta_ref,
        steps_ref,
        low_ref,
        x_ref,
        united_ref,
        fast_x_ref,
        ha_ref,
        taps_ref,
        hb_ref,
        gz_ref,
        own_ref,
        send_ref,
        out_ref,
        sems,
    ):
        lanes = fast_wide // PHASES
        for tap in range(3):
            step = steps_ref[tap, :, :mid]
            value = jnp.concatenate(
                [dot_tn(x_ref[...], step), dot_tn(united_ref[...], step)], axis=0
            )
            out_ref[:, tap * depth_one : (tap + 1) * depth_one, :] = value.astype(BF16).reshape(
                count, depth_one, mid
            )
        at = 3 * depth_one
        place = (own_ref, send_ref, meta_ref[1], meta_ref[2], sems)
        put_blocks(out_ref, 0, at, *place, 0)
        past = dot_tn(fast_x_ref[:, 2 * lanes :], low_ref[1])
        now = dot_tn(fast_x_ref[:, : 3 * lanes], low_ref[0])
        both = jnp.concatenate([past, now], axis=0).astype(BF16)
        for tap in range(5):
            out_ref[:, at + tap * depth_lat : at + (tap + 1) * depth_lat, :] = both[
                tap * lanes : (tap + 1) * lanes
            ].reshape(count, depth_lat, lat)
        at += 5 * depth_lat
        space = space_grad(ha_ref, taps_ref, out_ref, at)
        at += 9 * depth_mid
        reduce = fast_reduce_grad(
            fast_x_ref[...], [steps_ref[tap, :, mid:] for tap in range(3)]
        )
        put_fast(reduce, space, fast_expand_grad(hb_ref, gz_ref), out_ref, at)

        put_blocks(out_ref, 3 * depth_one, rows_late, *place, 1)
        for low, top, turn in ((0, 3 * depth_one, 0), (3 * depth_one, rows_late, 1)):
            rows_part = pl.ds(low, top - low)
            for block in range(count):
                source, target = out_ref.at[block, rows_part, :], own_ref.at[0, rows_part, :]
                pltpu.make_async_copy(source, target, sems.at[turn, block]).wait()

    def put_blocks(blocks_ref, low, top, own_ref, send_ref, ha, wa, sems, turn):
        rows_part = pl.ds(low, top - low)
        for block in range(count):
            place, col = ha ^ (block // 2), block % 2
            source, sem = blocks_ref.at[block, rows_part, :], sems.at[turn, block]

            @pl.when(wa == col)
            def _():
                pltpu.make_async_copy(source, own_ref.at[place, rows_part, :], sem).start()

            @pl.when(wa != col)
            def _():
                pltpu.make_async_copy(source, send_ref.at[place, rows_part, :], sem).start()

    high = count // 2
    rows_one = 3 * depth_one + 5 * depth_lat + 9 * depth_mid + fast_rows_count
    rows_late = aligned(rows_one)
    blocks_out = ((high, rows_late, mid), BF16, "raw")
    own_blocks, send_blocks = run(
        grads_one_kernel,
        [blocks_out, blocks_out],
        smem=(meta,),
        saved=(steps_one, united_low, slow_x, united, fast_x, ha_one, taps_one, hb_one, gz_c1),
        scratch=(
            pltpu.VMEM((count, rows_late, mid), BF16),
            pltpu.SemaphoreType.DMA((2, count)),
        ),
    )
    side_blocks = lax.ppermute(send_blocks, "wa", xor_pairs(2, 1))

    def chip_kernel(side_ref, own_ref, *out_refs):
        for place in range(high):
            total = own_ref[place].astype(F32) + side_ref[place].astype(F32)
            out_refs[place][...] = total.astype(BF16)
            out_refs[place].send()

    late_out = ((rows_late, mid), BF16, "hbm")
    chip_sums = run(chip_kernel, [late_out] * high, vmem=(side_blocks,), saved=(own_blocks,))
    chip_sums, early = lax.optimization_barrier((chip_sums, (sum_space, sum_mid)))
    late = [chip_sums[0]] + to_partners(chip_sums[1:], "ha")
    four = lax.axis_size("clips") == 4
    early_space, early_mid = lax.psum(early, "clips")
    quarters = clip_parts(meta, [late], 4 if four else 1)
    if four:
        total_late = add_low(quarters[0], *to_partners(quarters[1:], "clips"))
        parts_late = [total_late] + to_partners([total_late] * 3, "clips")
    else:
        parts_late = [lax.psum(quarters[0], "clips")]

    def finish(*jobs):
        outs_all = []
        for _, groups in jobs:
            for _, shapes in groups:
                for shape in shapes:
                    outs_all += list(shape) if isinstance(shape[0], tuple) else [shape]
        number = sum(len(parts) for parts, _ in jobs)
        deepest = max(sum(rows_group for rows_group, _ in groups) for _, groups in jobs)

        def kernel(meta_ref, *refs):
            ins, outs, total_ref = list(refs[:number]), list(refs[number:-1]), refs[-1]
            for parts, groups in jobs:
                mine, ins = ins[: len(parts)], ins[len(parts) :]
                one_job(meta_ref, mine, outs, total_ref, groups)

        def one_job(meta_ref, ins, outs, total_ref, groups):
            size = len(ins)
            depth = sum(rows_group for rows_group, _ in groups) // size
            base = 0
            for step, ref in enumerate(ins):
                start = pl.multiple_of((meta_ref[4] ^ step) * depth, 16) if size > 1 else 0
                total_ref[pl.ds(start, depth), :] = ref[...].astype(F32)
            for rows_group, shapes in groups:
                at = base
                for shape in shapes:
                    if isinstance(shape[0], tuple):
                        reduce, space, expand = outs.pop(0), outs.pop(0), outs.pop(0)
                        rows_tap, lanes = reduce.shape[1:]
                        for tap in range(3):
                            reduce[tap] = total_ref[
                                at : at + rows_tap, tap * lanes : (tap + 1) * lanes
                            ]
                        few = space.shape[2]
                        for tap in range(9):
                            row = at + rows_tap + tap // SUB * SUB
                            lane = tap % SUB * lanes
                            space[tap // 3, tap % 3] = total_ref[
                                row : row + few, lane : lane + lanes
                            ]
                        row = at + rows_tap + SUB
                        expand[...] = total_ref[row : row + few, expand.shape[1] :]
                        for out in (reduce, space, expand):
                            out.send()
                        at += rows_tap + 2 * SUB
                        continue
                    out = outs.pop(0)
                    if len(shape) == 2 and shape[1] > mid:
                        for block in range(shape[1] // mid):
                            out[:, block * mid : (block + 1) * mid] = total_ref[
                                at : at + shape[0], :
                            ]
                            at += shape[0]
                    else:
                        number = 1
                        for length in shape[:-1]:
                            number *= length
                        out[...] = total_ref[at : at + number, :].reshape(shape)
                        at += number
                    out.send()
                base += rows_group

        return run(
            kernel,
            [(shape, F32, "hbm") for shape in outs_all],
            smem=(meta,),
            saved=[part for parts, _ in jobs for part in parts],
            scratch=(pltpu.VMEM((deepest, mid), F32),),
        )

    shapes_one = tuple(shard.shape for shard in fast_shards_one)
    shapes_two = tuple(shard.shape for shard in fast_shards_two)
    groups_space = [(rows_space, [slow_spatial_two.shape, slow_expand_two.shape])]
    groups_mid = [
        (
            rows_mid,
            [slow_reduce_two.shape, shapes_two, slow_shortcut_one.shape, slow_expand_one.shape],
        ),
    ]
    groups_late = [
        (
            rows_late,
            [slow_reduce_one.shape, lateral_weight.shape, slow_spatial_one.shape, shapes_one],
        )
    ]
    finished = finish(
        ([early_space], groups_space), ([early_mid], groups_mid), (parts_late, groups_late)
    )
    grad_slow_spatial_two, grad_slow_expand_two, grad_slow_reduce_two = finished[:3]
    fast_two_grads, (grad_slow_shortcut, grad_slow_expand_one) = finished[3:6], finished[6:8]
    grad_slow_reduce_one, grad_lateral, grad_slow_spatial_one, *fast_one_grads = finished[8:]

    def norm_grads(first, second, third):
        slow = [first[:, :mid], second[:, :mid], third[:, :slow_wide]]
        fast = [first[:, mid:], second[:, mid:]]
        fast = [jnp.sum(part.reshape(2, PHASES, -1), axis=1) for part in fast]
        return slow, fast + [third[:, slow_wide:packed]]

    slow_one_p, fast_one_p = norm_grads(sums_a1, sums_b1, sums_c1)
    slow_two_p, fast_two_p = norm_grads(sums_a2, sums_b2, sums_c2)
    grad_slow_norms_one = jnp.concatenate(slow_one_p + [sums_c1[:, packed:]], axis=1)
    grad_slow_norms_two = jnp.concatenate(slow_two_p, axis=1)
    grad_fast_norms_one = jnp.concatenate(fast_one_p, axis=1)
    grad_fast_norms_two = jnp.concatenate(fast_two_p, axis=1)
    return (
        outputs[:, :slow_wide].reshape(slow_input.shape),
        join_phases(outputs[:, slow_wide:], fast_input.shape),
        grad_slow.reshape(slow_input.shape),
        join_phases(grad_fast, fast_input.shape),
        grad_lateral,
        grad_slow_reduce_one,
        grad_slow_spatial_one,
        grad_slow_expand_one,
        grad_slow_shortcut,
        *fast_one_grads,
        grad_slow_reduce_two,
        grad_slow_spatial_two,
        grad_slow_expand_two,
        *fast_two_grads,
        grad_slow_norms_one,
        grad_fast_norms_one,
        grad_slow_norms_two,
        grad_fast_norms_two,
    )


def solution(mesh):
    in_specs = (
        P("clips", None, "ha", "wa", None),
        P("clips", None, "ha", "wa", None),
        P("clips", None, "ha", "wa", None),
        P("clips", None, "ha", "wa", None),
        P("clips"),
        P(None, ("ha", "wa"), None),
        P(None, ("ha", "wa"), None),
        P(None, None, ("ha", "wa"), None),
        P(("ha", "wa"), None),
        P(("ha", "wa"), None),
        P(None, ("ha", "wa"), None),
        P(None, None, ("ha", "wa"), None),
        P(("ha", "wa"), None),
        P(None, ("ha", "wa"), None),
        P(None, None, ("ha", "wa"), None),
        P(("ha", "wa"), None),
        P(None, ("ha", "wa"), None),
        P(None, None, ("ha", "wa"), None),
        P(("ha", "wa"), None),
        P(),
        P(),
        P(),
        P(),
    )
    out_specs = (
        P("clips", None, "ha", "wa", None),
        P("clips", None, "ha", "wa", None),
        P("clips", None, "ha", "wa", None),
        P("clips", None, "ha", "wa", None),
        P(None, ("ha", "wa"), None),
        P(None, ("ha", "wa"), None),
        P(None, None, ("ha", "wa"), None),
        P(("ha", "wa"), None),
        P(("ha", "wa"), None),
        P(None, ("ha", "wa"), None),
        P(None, None, ("ha", "wa"), None),
        P(("ha", "wa"), None),
        P(None, ("ha", "wa"), None),
        P(None, None, ("ha", "wa"), None),
        P(("ha", "wa"), None),
        P(None, ("ha", "wa"), None),
        P(None, None, ("ha", "wa"), None),
        P(("ha", "wa"), None),
        P(),
        P(),
        P(),
        P(),
    )
    return jax.shard_map(
        on_device, mesh=mesh, in_specs=in_specs, out_specs=out_specs, check_vma=False
    )
```
